32 devices in a mesh: gx: 8 (over z, core), gy: 4 (over y, x).
Axes of the slice: x: 2, y: 2, z: 4, core: 2. Of those that a mesh axis runs over, the one named last changes fastest.
Arguments:
- positions: float32 [8, 4, 3, 256], P('gx', 'gy'), may hold values from 0 to 10
- species: int32 [8, 4, 256], P('gx', 'gy'), may hold values from 0 to 5
- neighbours: int32 [8, 4, 256, 12], P('gx', 'gy'), may hold values from 0 to 2303
- counts: int32 [8, 4, 256], P('gx', 'gy'), may hold values from 6 to 12
- species_embed: float32 [6, 128], replicated, may hold values from -6 to 6
- radial: float32 [2, 2, 8, 128], replicated, may hold values from -2 to 2
- mixing: float32 [2, 2, 128, 128], replicated, may hold values from -0.5 to 0.5
- read_hidden: float32 [128, 128], replicated, may hold values from -0.5 to 0.5
- read_out: float32 [128], replicated, may hold values from -0.5 to 0.5
- charge_map: float32 [128, 64], replicated, may hold values from -0.5 to 0.5
- wavevectors: int32 [3, 4096], replicated, may hold values from -8 to 8, as said below
Outputs:
- forces: float32 [8, 4, 3, 256], P('gx', 'gy')
- site_energy: float32 [8, 4, 256], P('gx', 'gy')
The draws below stay inside these ranges and needn't reach their ends.
Inputs may be any that keep to these rules, and one draw needn't show every extreme that they name: `neighbours`: entry (3 a + b) * 256 + t names atom t of the cell offset by (a - 1, b - 1) along gx, gy, periodically. Slots n < counts are used. `wavevectors`: the 4096 triples are distinct, and no triple has its first two components both zero.
All inputs are finite; a program needn't handle non-finite values.
Results may differ from the reference program's by a relative error of at most 0.0017.
Values may be sent and summed in bfloat16 or wider, within the bound.
No kernel may reach another device: no remote copies, remote signals or barrier semaphores. Data moves between devices by JAX's collectives and lax.ppermute only.
A program may use at most 128 MiB of HBM per device.

```python
import math
import jax
import jax.numpy as jnp
from jax import lax

ATOM_DEV = 256
NB = 12
C = 128
CL = 64
K = 4096
NR = 8
NS = 6
LAYERS = 2
N_GX = 8
N_GY = 4


def draw_wavevectors(key, part):
    order = jax.random.permutation(key, jnp.arange(4896, dtype=jnp.int32))[:K]
    pair_index = order // 17
    third = order % 17 - 8
    pair_index = pair_index + (pair_index >= 144).astype(jnp.int32)
    first = pair_index // 17 - 8
    second = pair_index % 17 - 8
    return jnp.stack([first, second, third]).astype(jnp.int32)


def touch_ends(values, key, least, largest):
    spot = [jax.random.randint(jax.random.fold_in(key, axis), (), 0, length) for axis, length in enumerate(values.shape)]
    widest = values.shape.index(max(values.shape))
    neighbour = spot[:widest] + [(spot[widest] + 1) % values.shape[widest]] + spot[widest + 1:]
    return values.at[tuple(spot)].set(least).at[tuple(neighbour)].set(largest)


def levels(stream_key, shape, pieces, smallest, top_value):
    def one(axis_at, parts):
        steps = jax.random.uniform(jax.random.fold_in(jax.random.fold_in(stream_key, 6), axis_at), (parts,), jnp.float32, smallest / len(pieces), top_value / len(pieces))
        return jnp.repeat(jnp.exp(steps), shape[axis_at] // parts).reshape((-1,) + (1,) * (len(shape) - axis_at - 1))

    level = one(*pieces[0])
    for cut in pieces[1:]:
        level = level * one(*cut)
    return level


def normal_values(rng, shape, width, most, kind=jnp.bfloat16):
    entries = jax.random.normal(rng, shape, jnp.float32) * width
    return jnp.minimum(jnp.maximum(entries, -most), most).astype(kind)


def setup_inputs(seed: int = 0) -> dict:
    key_list = jax.random.split(jax.random.key(seed), 12)
    return {
        "positions": jnp.clip(10.0 * jax.random.uniform(key_list[0], (N_GX, N_GY, 3, ATOM_DEV), jnp.float32) ** levels(key_list[0], (N_GX, N_GY, 3, ATOM_DEV), ((0, 8), (1, 4)), -0.2, 0.2), 0.0, 10.0),
        "species": touch_ends(jax.random.randint(key_list[1], (N_GX, N_GY, ATOM_DEV), 0, NS), jax.random.fold_in(key_list[1], 1), 0, NS - 1).astype(jnp.int32),
        "neighbours": touch_ends(jax.random.randint(key_list[2], (N_GX, N_GY, ATOM_DEV, NB), 0, 9 * ATOM_DEV), jax.random.fold_in(key_list[2], 1), 0, (9 * ATOM_DEV) - 1).astype(jnp.int32),
        "counts": touch_ends(jax.random.randint(key_list[3], (N_GX, N_GY, ATOM_DEV), NB // 2, NB + 1), jax.random.fold_in(key_list[3], 1), NB // 2, NB).astype(jnp.int32),
        "species_embed": normal_values(key_list[4], (NS, C), 1.0, 6.0, jnp.float32),
        "radial": normal_values(key_list[5], (LAYERS, 2, NR, C), NR ** -0.5, 2.0, jnp.float32),
        "mixing": normal_values(key_list[6], (LAYERS, 2, C, C), C ** -0.5, 0.5, jnp.float32),
        "read_hidden": normal_values(key_list[7], (C, C), C ** -0.5, 0.5, jnp.float32),
        "read_out": normal_values(key_list[8], (C,), C ** -0.5, 0.5, jnp.float32),
        "charge_map": normal_values(key_list[9], (C, CL), C ** -0.5, 0.5, jnp.float32),
        "wavevectors": draw_wavevectors(jax.random.fold_in(key_list[11], 71), 0),
    }


cell_width = 10.0
box_height = 30.0
cut_radius = 50.0
soften = 0.25
screen = 0.5
smear_width = 0.5
highest = lax.Precision.HIGHEST

def build_frame(extended):
    offsets = (jnp.arange(3, dtype=jnp.float32) - 1.0) * cell_width
    shift_x = jnp.broadcast_to(offsets[:, None], (3, 3))
    shift_y = jnp.broadcast_to(offsets[None, :], (3, 3))
    shifts = jnp.stack([shift_x, shift_y, jnp.zeros((3, 3), jnp.float32)], axis=2)
    coords = extended[:, :, :3, :] + shifts[:, :, :, None]
    src_pos = jnp.moveaxis(coords, 2, 0).reshape(3, -1)
    kind_codes = extended[:, :, 3, :].reshape(-1)
    return (src_pos, kind_codes)

def embed_rows(kind_codes, species_embed):
    lookup = (kind_codes[:, None] == jnp.arange(species_embed.shape[0], dtype=jnp.float32)[None, :]).astype(jnp.float32)
    return jnp.dot(lookup, species_embed, precision=highest)

def interact(h_dst, h_src, own_pos, src_pos, neighbour_ids, slot_counts, radial_pair, mix_pair):
    slots = neighbour_ids.shape[1]
    orders = radial_pair.shape[1]
    relative = src_pos[:, neighbour_ids] - own_pos[:, :, None]
    distance = jnp.sqrt(lax.optimization_barrier(jnp.sum(relative * relative, axis=0)) + soften)
    unit_vec = relative / distance[None]
    frequency = jnp.arange(1, orders + 1, dtype=jnp.float32) * (math.pi / cut_radius)
    arg_scaled = distance[:, :, None] * frequency
    radial_basis = jnp.sin(arg_scaled) / arg_scaled
    live_slots = (jnp.arange(slots)[None, :] < slot_counts[:, None]).astype(jnp.float32)
    weight_zero = jnp.einsum('anr,rc->anc', radial_basis, radial_pair[0], precision=highest) * live_slots[:, :, None]
    weight_one = jnp.einsum('anr,rc->anc', radial_basis, radial_pair[1], precision=highest) * live_slots[:, :, None]
    source = h_src[neighbour_ids]
    norm_factor = 1.0 / math.sqrt(slots)
    msg_zero = lax.optimization_barrier(jnp.sum(weight_zero * source, axis=1)) * norm_factor
    msg_one = jnp.einsum('anc,xan->xac', weight_one * source, unit_vec, precision=highest) * norm_factor
    squares = lax.optimization_barrier(jnp.sum(msg_one * msg_one, axis=0))
    preact = jnp.dot(msg_zero, mix_pair[0], precision=highest) + jnp.dot(squares, mix_pair[1], precision=highest)
    return h_dst + jax.nn.silu(preact)

def first_layer(own_pos, src_pos, initial_src, neighbour_ids, slot_counts, radial, mixing):
    atom_count = own_pos.shape[1]
    return interact(initial_src[4 * atom_count:5 * atom_count], initial_src, own_pos, src_pos, neighbour_ids, slot_counts, radial[0], mixing[0])

def second_section(hidden_src, own_pos, src_pos, neighbour_ids, slot_counts, radial, mixing, read_hidden, read_out, charge_map):
    atom_count = own_pos.shape[1]
    hidden_two = interact(hidden_src[4 * atom_count:5 * atom_count], hidden_src, own_pos, src_pos, neighbour_ids, slot_counts, radial[1], mixing[1])
    energy = jnp.dot(jax.nn.silu(jnp.dot(hidden_two, read_hidden, precision=highest)), read_out, precision=highest)
    charges = jnp.dot(hidden_two, charge_map, precision=highest)
    return (energy, charges)

def wave_terms(wavevectors, grid_x, grid_y):
    lengths = jnp.array([grid_x * cell_width, grid_y * cell_width, box_height], dtype=jnp.float32)
    wave_phys = 2.0 * math.pi * wavevectors.astype(jnp.float32) / lengths[:, None]
    wave_sq = lax.optimization_barrier(jnp.sum(wave_phys * wave_phys, axis=0))
    green_weight = jnp.exp(-smear_width * wave_sq) / (wave_sq + screen * screen)
    return (wave_phys, green_weight)

def phase_pair(global_pos, wave_part):
    angle = global_pos[0][:, None] * wave_part[0][None, :] + global_pos[1][:, None] * wave_part[1][None, :] + global_pos[2][:, None] * wave_part[2][None, :]
    return (jnp.cos(angle), jnp.sin(angle))

def structure_term(charges, global_pos, wave_part):
    cosine, sine_part = phase_pair(global_pos, wave_part)
    dims = (((0,), (0,)), ((), ()))
    real_part = lax.dot_general(cosine, charges, dims, precision=highest)
    imag_part = lax.dot_general(sine_part, charges, dims, precision=highest)
    return jnp.concatenate([real_part, imag_part], axis=1)

def fold_terms(carried, piece_rows, start_row, charges, global_pos, wave_phys):
    potential, lr_grad = carried
    row_count = piece_rows.shape[0]
    lat_width = charges.shape[1]
    wave_part = lax.dynamic_slice_in_dim(wave_phys, jnp.asarray(start_row).astype(jnp.int32), row_count, 1)
    cosine, sine_part = phase_pair(global_pos, wave_part)
    weight_re = piece_rows[:, :lat_width]
    weight_im = piece_rows[:, lat_width:]
    potential = potential + jnp.dot(cosine, weight_re, precision=highest) + jnp.dot(sine_part, weight_im, precision=highest)
    dims = (((1,), (1,)), ((), ()))
    proj_re = lax.dot_general(charges, weight_re, dims, precision=highest)
    proj_im = lax.dot_general(charges, weight_im, dims, precision=highest)
    phase_turn = cosine * proj_im - sine_part * proj_re
    lr_grad = lr_grad + lax.dot_general(wave_part, phase_turn, dims, precision=highest)
    return (potential, lr_grad)

def reference(positions, species, neighbours, counts, species_embed, radial, mixing, read_hidden, read_out, charge_map, wavevectors):
    grid_x = positions.shape[0]
    grid_y = positions.shape[1]
    atom_count = positions.shape[3]
    device_total = grid_x * grid_y
    lat_width = charge_map.shape[1]
    wave_count = wavevectors.shape[1]
    kind_all = species.astype(jnp.float32)[:, :, None, :]

    def neighbour_block(lookup, device):
        row_index = device // grid_y
        col_index = device % grid_y
        row_ids = (row_index + jnp.arange(3) - 1) % grid_x
        col_ids = (col_index + jnp.arange(3) - 1) % grid_y
        return (lookup[row_ids[:, None], col_ids[None, :]], row_index, col_index)

    def layer_one_all(pos_all):
        packed = jnp.concatenate([pos_all, kind_all], axis=2)

        def single(device):
            extended, row_index, col_index = neighbour_block(packed, device)
            src_pos, kind_codes = build_frame(extended)
            initial_src = embed_rows(kind_codes, species_embed)
            return first_layer(pos_all[row_index, col_index], src_pos, initial_src, neighbours[row_index, col_index], counts[row_index, col_index], radial, mixing)
        result = lax.map(jax.checkpoint(single), jnp.arange(device_total))
        return result.reshape(grid_x, grid_y, atom_count, -1)
    hidden_one, pull_one = jax.vjp(layer_one_all, positions)
    hidden_low = lax.optimization_barrier(hidden_one.astype(jnp.bfloat16)).astype(jnp.float32)

    def section_two_all(hidden_all, pos_all):
        packed = jnp.concatenate([pos_all, kind_all], axis=2)

        def single(device):
            extended, row_index, col_index = neighbour_block(packed, device)
            src_pos, kind_codes = build_frame(extended)
            hidden_ext, row_same, col_same = neighbour_block(hidden_all, device)
            hidden_src = hidden_ext.reshape(9 * atom_count, -1)
            return second_section(hidden_src, pos_all[row_index, col_index], src_pos, neighbours[row_index, col_index], counts[row_index, col_index], radial, mixing, read_hidden, read_out, charge_map)
        return lax.map(jax.checkpoint(single), jnp.arange(device_total))
    (energy_sr, charges), pull_two = jax.vjp(section_two_all, hidden_low, positions)
    wave_phys, green_weight = wave_terms(wavevectors, grid_x, grid_y)
    device_ids = jnp.arange(device_total)
    anchor = jnp.stack([(device_ids // grid_y).astype(jnp.float32) * cell_width, (device_ids % grid_y).astype(jnp.float32) * cell_width, jnp.zeros((device_total,), jnp.float32)], axis=1)
    global_all = positions.reshape(device_total, 3, atom_count) + anchor[:, :, None]

    def add_term(running, members):
        return (running + structure_term(members[0], members[1], wave_phys), None)
    structure, unused = lax.scan(add_term, jnp.zeros((wave_count, 2 * lat_width), jnp.float32), (charges, global_all))
    weighted = green_weight[:, None] * structure

    def per_device(members):
        start_state = (jnp.zeros((atom_count, lat_width), jnp.float32), jnp.zeros((3, atom_count), jnp.float32))
        return fold_terms(start_state, weighted, 0, members[0], members[1], wave_phys)
    potential, lr_grad = lax.map(per_device, (charges, global_all))
    lr_scale = 1.0 / math.sqrt(wave_count * lat_width * device_total * atom_count)
    site_energy = energy_sr + lr_scale * lax.optimization_barrier(jnp.sum(charges * potential, axis=2))
    grad_hidden, grad_pos_two = pull_two((jnp.ones_like(energy_sr), 2.0 * lr_scale * potential))
    grad_pos_one = pull_one(grad_hidden)[0]
    forces = -(grad_pos_one + grad_pos_two + 2.0 * lr_scale * lr_grad.reshape(grid_x, grid_y, 3, atom_count))
    return (forces, site_energy.reshape(grid_x, grid_y, atom_count))
```

```python
import functools
import math

import jax
import jax.numpy as jnp
import numpy as np
from jax import lax
from jax.experimental import pallas as pl
from jax.experimental.pallas import tpu as pltpu
from jax.sharding import PartitionSpec as P

cell_width = 10.0
box_height = 30.0
cut_radius = 50.0
soften = 0.25
screen = 0.5
smear_width = 0.5
highest = lax.Precision.HIGHEST
WAVE_REACH = 8


def passed_along(block, axis, distance):
    devices = range(lax.axis_size(axis))
    route = [((i - distance) % len(devices), i) for i in devices]
    return lax.ppermute(block, axis, route)


def with_halo(block, sides, width):
    for axis, dim in sides:
        count = lax.axis_size(axis)
        forward = [(i, i + 1) for i in range(count - 1)]
        forward.append((count - 1, 0))
        backward = [(target, source) for source, target in forward]
        low = lax.ppermute(
            lax.slice_in_dim(block, block.shape[dim] - width, None, axis=dim), axis, forward
        )
        high = lax.ppermute(lax.slice_in_dim(block, 0, width, axis=dim), axis, backward)
        block = jnp.concatenate([low, block, high], axis=dim)
    return block


def build_frame(extended):
    offsets = (jnp.arange(3, dtype=jnp.float32) - 1.0) * cell_width
    shift_x = jnp.broadcast_to(offsets[:, None], (3, 3))
    shift_y = jnp.broadcast_to(offsets[None, :], (3, 3))
    shifts = jnp.stack([shift_x, shift_y, jnp.zeros((3, 3), jnp.float32)], axis=2)
    coords = extended[:, :, :3, :] + shifts[:, :, :, None]
    src_pos = jnp.moveaxis(coords, 2, 0).reshape(3, -1)
    kind_codes = extended[:, :, 3, :].reshape(-1)
    return (src_pos, kind_codes)


def embed_rows(kind_codes, species_embed):
    lookup = (
        kind_codes[:, None] == jnp.arange(species_embed.shape[0], dtype=jnp.float32)[None, :]
    ).astype(jnp.float32)
    return jnp.dot(lookup, species_embed, precision=highest)


def interact(h_dst, h_src, own_pos, src_pos, neighbour_ids, slot_counts, radial_pair, mix_pair):
    slots = neighbour_ids.shape[1]
    orders = radial_pair.shape[1]
    relative = src_pos[:, neighbour_ids] - own_pos[:, :, None]
    distance = jnp.sqrt(jnp.sum(relative * relative, axis=0) + soften)
    unit_vec = relative / distance[None]
    frequency = jnp.arange(1, orders + 1, dtype=jnp.float32) * (math.pi / cut_radius)
    arg_scaled = distance[:, :, None] * frequency
    radial_basis = jnp.sin(arg_scaled) / arg_scaled
    live_slots = (jnp.arange(slots)[None, :] < slot_counts[:, None]).astype(jnp.float32)
    weight_zero = (
        jnp.einsum("anr,rc->anc", radial_basis, radial_pair[0], precision=highest)
        * live_slots[:, :, None]
    )
    weight_one = (
        jnp.einsum("anr,rc->anc", radial_basis, radial_pair[1], precision=highest)
        * live_slots[:, :, None]
    )
    source = h_src[neighbour_ids]
    norm_factor = 1.0 / math.sqrt(slots)
    msg_zero = jnp.sum(weight_zero * source, axis=1) * norm_factor
    msg_one = (
        jnp.einsum("anc,xan->xac", weight_one * source, unit_vec, precision=highest) * norm_factor
    )
    squares = jnp.sum(msg_one * msg_one, axis=0)
    preact = jnp.dot(msg_zero, mix_pair[0], precision=highest) + jnp.dot(
        squares, mix_pair[1], precision=highest
    )
    return h_dst + jax.nn.silu(preact)


def first_layer(own_pos, src_pos, initial_src, neighbour_ids, slot_counts, radial, mixing):
    atom_count = own_pos.shape[1]
    return interact(
        initial_src[4 * atom_count : 5 * atom_count],
        initial_src,
        own_pos,
        src_pos,
        neighbour_ids,
        slot_counts,
        radial[0],
        mixing[0],
    )


def second_section(
    hidden_src,
    own_pos,
    src_pos,
    neighbour_ids,
    slot_counts,
    radial,
    mixing,
    read_hidden,
    read_out,
    charge_map,
):
    atom_count = own_pos.shape[1]
    hidden_two = interact(
        hidden_src[4 * atom_count : 5 * atom_count],
        hidden_src,
        own_pos,
        src_pos,
        neighbour_ids,
        slot_counts,
        radial[1],
        mixing[1],
    )
    energy = jnp.dot(
        jax.nn.silu(jnp.dot(hidden_two, read_hidden, precision=highest)),
        read_out,
        precision=highest,
    )
    charges = jnp.dot(hidden_two, charge_map, precision=highest)
    return (energy, charges)


def recv_from(block, axis, distance):
    count = lax.axis_size(axis)
    return lax.ppermute(block, axis, [((i + distance) % count, i) for i in range(count)])


def whole(space=pltpu.VMEM):
    return pl.BlockSpec(memory_space=space)


def run(kernel, outs, args, scratch=(), smem=0, flops=1_000_000, name=None):
    specs = [whole(pltpu.SMEM)] * smem + [whole()] * (len(args) - smem)
    return pl.pallas_call(
        kernel,
        out_shape=outs,
        in_specs=specs,
        out_specs=jax.tree.map(lambda _: whole(), outs),
        scratch_shapes=list(scratch),
        compiler_params=pltpu.CompilerParams(vmem_limit_bytes=48 * 1024 * 1024),
        cost_estimate=pl.CostEstimate(flops=flops, bytes_accessed=1_000_000, transcendentals=0),
        name=name,
    )(*args)


def split(value):
    high = value.astype(jnp.bfloat16)
    return high, (value - high.astype(jnp.float32)).astype(jnp.bfloat16)


def dot(left, right, contract=((1,), (0,))):
    return lax.dot_general(left, right, (contract, ((), ())), preferred_element_type=jnp.float32)


def pair_tables(parts):
    reach = WAVE_REACH
    pairs = [(0, y) for y in range(1, reach + 1)]
    pairs += [(x, y) for x in range(1, reach + 1) for y in range(-reach, reach + 1)]
    share = -(-len(pairs) // parts)
    padded = -(-share // 8) * 8
    side = 2 * reach + 1
    pair_rows = np.zeros((parts, padded, 8), np.float32)
    wave_rows = np.zeros((parts, 2 * 8 * share + padded, 8), np.float32)
    for part in range(parts):
        for slot, (x, y) in enumerate(pairs[part * share : (part + 1) * share]):
            pair_rows[part, slot, :2] = (x, y)
            rows = [(8 * slot + z - 1, z) for z in range(1, 9)]
            rows += [(8 * share + 8 * slot + z - 1, -z) for z in range(1, 9)]
            rows += [(16 * share + slot, 0)]
            for row, z in rows:
                code = ((x + reach) * side + y + reach) * side + z + reach
                wave_rows[part, row, :5] = (x, y, z, code, 1.0)
    return share, padded, pair_rows, wave_rows


def table_kernel(share, padded, grid, pos_ref, pair_ref, wave_ref, vec_ref, *refs):
    grid_x, grid_y = grid
    blocks, (ca_ref, sa_ref, cb_ref, sb_ref, weight_ref) = refs[:grid_x], refs[grid_x:]
    turn = 2.0 * math.pi
    col = pos_ref[1].astype(jnp.float32) * (1.0 / grid_y)
    kx = pair_ref[:, 0:1]
    ky = pair_ref[:, 1:2]
    kz = (lax.broadcasted_iota(jnp.int32, (8, 1), 0) + 1).astype(jnp.float32)
    for d in range(grid_x):
        row_id = lax.rem(pos_ref[0] + d, grid_x).astype(jnp.float32) * (1.0 / grid_x)
        block = blocks[d]
        lanes = pl.ds(d * block.shape[1], block.shape[1])
        x = block[0:1, :] * (1.0 / (grid_x * cell_width)) + row_id
        y = block[1:2, :] * (1.0 / (grid_y * cell_width)) + col
        z = block[2:3, :] * (1.0 / box_height)
        alpha = kx * x + ky * y
        alpha = (alpha - jnp.round(alpha)) * turn
        beta = kz * z
        beta = (beta - jnp.round(beta)) * turn
        ca_ref[:, lanes] = jnp.cos(alpha)
        sa_ref[:, lanes] = jnp.sin(alpha)
        cb_ref[:, lanes] = jnp.cos(beta)
        sb_ref[:, lanes] = jnp.sin(beta)
    side = 2 * WAVE_REACH + 1
    top = side * side * side - 1
    vec = vec_ref[...].astype(jnp.float32) + WAVE_REACH
    code = (vec[0:1] * side + vec[1:2]) * side + vec[2:3]
    code = jnp.maximum(code, top - code)
    wave = wave_ref[...]
    own = wave[:, 3:4]
    width = code.shape[1]
    seen = jnp.zeros((own.shape[0], 128), jnp.float32)
    for start in range(0, width, 128):
        seen = seen + jnp.where(own == code[:, start : start + 128], 1.0, 0.0)
    count = jnp.sum(seen, axis=1, keepdims=True) * wave[:, 4:5]
    sq = (
        (wave[:, 0:1] * (turn / (grid_x * cell_width))) ** 2
        + (wave[:, 1:2] * (turn / (grid_y * cell_width))) ** 2
        + (wave[:, 2:3] * (turn / box_height)) ** 2
    )
    green = jnp.exp(-smear_width * sq) / (sq + screen * screen) * count
    weight_ref[...] = jnp.broadcast_to(green, weight_ref.shape)


def basis_rows(share, ca, sa, cb, sb):
    cc, ss, sc, cs = [], [], [], []
    for p in range(share):
        c, s = ca[p : p + 1], sa[p : p + 1]
        cc.append(c * cb)
        ss.append(s * sb)
        sc.append(s * cb)
        cs.append(c * sb)
    return cc, ss, sc, cs


def unpack_rows(block):
    half = block.shape[1] // 2
    return jnp.concatenate([block[:, :half], block[:, half:]], axis=0)


def pack_rows(block):
    half = block.shape[0] // 2
    return jnp.concatenate([block[:half], block[half:]], axis=1)


def structure_kernel(share, padded, grid_x, *refs):
    ca_ref, sa_ref, cb_ref, sb_ref = refs[:4]
    blocks, (out_ref,) = refs[4 : 4 + grid_x], refs[4 + grid_x :]
    total = None
    for d in range(grid_x):
        charge = unpack_rows(blocks[d][...].astype(jnp.float32))
        q_high, q_low = split(charge)
        atoms = charge.shape[0]
        lanes = pl.ds(d * atoms, atoms)
        ca, sa, cb, sb = ca_ref[:, lanes], sa_ref[:, lanes], cb_ref[:, lanes], sb_ref[:, lanes]
        cc, ss, sc, cs = basis_rows(share, ca, sa, cb, sb)
        high, low = split(jnp.concatenate(cc + ss + sc + cs + [ca, sa], axis=0))
        wide = charge.shape[1]
        both = dot(high, jnp.concatenate([q_high, q_low], axis=1))
        term = both[:, :wide] + both[:, wide:] + dot(low, q_high)
        total = term if total is None else total + term
    out_ref[...] = pack_rows(total).astype(out_ref.dtype)


def fold_kernel(share, padded, grid, *refs):
    grid_x, grid_y = grid
    ca_ref, sa_ref, cb_ref, sb_ref, weight_ref, pair_ref = refs[:6]
    blocks = refs[6 : 6 + grid_x]
    parts = refs[6 + grid_x : 6 + grid_x + grid_y]
    outs = refs[6 + grid_x + grid_y :]
    turn = 2.0 * math.pi
    packed = parts[0][...].astype(jnp.float32)
    for part in parts[1:]:
        packed = packed + part[...].astype(jnp.float32)
    struct = unpack_rows(packed)
    wide = struct.shape[1]
    span = 8 * share
    cc, ss, sc, cs = (struct[i * span : (i + 1) * span] for i in range(4))
    weight = weight_ref[:, :wide]
    plus, minus, flat = weight[:span], weight[span : 2 * span], weight[2 * span :]
    re_plus, im_plus = plus * (cc - ss), plus * (sc + cs)
    re_minus, im_minus = minus * (cc + ss), minus * (sc - cs)
    rows = jnp.concatenate(
        [
            re_plus + re_minus,
            re_minus - re_plus,
            im_plus + im_minus,
            im_plus - im_minus,
            flat * struct[4 * span : 4 * span + padded],
            flat * struct[4 * span + padded :],
        ],
        axis=0,
    )
    row_high, row_low = split(rows)
    row_three = jnp.concatenate([row_high, row_low, row_high], axis=1)
    turned = rows.T
    t_high, t_low = split(turned)
    t_both = jnp.concatenate([t_high, t_low], axis=0)
    kx = pair_ref[:, 0:1] * (turn / (grid_x * cell_width))
    ky = pair_ref[:, 1:2] * (turn / (grid_y * cell_width))
    kz = (lax.broadcasted_iota(jnp.int32, (8, 1), 0) + 1).astype(jnp.float32) * (turn / box_height)
    for d in range(grid_x):
        charge = unpack_rows(blocks[d][...].astype(jnp.float32))
        q_high, q_low = split(charge)
        atoms = charge.shape[0]
        lanes = pl.ds(d * atoms, atoms)
        ca, sa, cb, sb = ca_ref[:, lanes], sa_ref[:, lanes], cb_ref[:, lanes], sb_ref[:, lanes]
        bcc, bss, bsc, bcs = basis_rows(share, ca, sa, cb, sb)
        high, low = split(jnp.concatenate(bcc + bss + bsc + bcs + [ca, sa], axis=0))
        both = dot(t_both, high)
        pot = both[:wide] + both[wide:] + dot(t_high, low)
        proj = dot(row_three, jnp.concatenate([q_high, q_high, q_low], axis=1), ((1,), (1,)))
        by_x = jnp.zeros((8, atoms), jnp.float32)
        by_y = jnp.zeros((8, atoms), jnp.float32)
        by_z = jnp.zeros((8, atoms), jnp.float32)
        for p in range(share):
            pcc, pss, psc, pcs = (
                proj[i * span + 8 * p : i * span + 8 * p + 8] for i in range(4)
            )
            slope = bcs[p] * pss - bsc[p] * pcc + bcc[p] * psc - bss[p] * pcs
            by_x = by_x + kx[p : p + 1] * slope
            by_y = by_y + ky[p : p + 1] * slope
            by_z = by_z + (bsc[p] * pss - bcs[p] * pcc - bss[p] * psc + bcc[p] * pcs)
        flat_slope = ca * proj[4 * span + padded :] - sa * proj[4 * span : 4 * span + padded]
        grad_x = jnp.sum(by_x, axis=0, keepdims=True) + jnp.sum(kx * flat_slope, axis=0, keepdims=True)
        grad_y = jnp.sum(by_y, axis=0, keepdims=True) + jnp.sum(ky * flat_slope, axis=0, keepdims=True)
        grad_z = jnp.sum(kz * by_z, axis=0, keepdims=True)
        zero = jnp.zeros((5, atoms), jnp.float32)
        outs[d][...] = jnp.concatenate([pot, grad_x, grad_y, grad_z, zero], axis=0)


def long_range(own_rows, charge_block, vectors, lat_width):
    grid_x, grid_y = lax.axis_size("gx"), lax.axis_size("gy")
    atoms = own_rows.shape[1]
    share, padded, pair_np, wave_np = pair_tables(grid_x)
    place = jnp.stack([lax.axis_index("gx"), lax.axis_index("gy")]).astype(jnp.int32)
    pair_rows = lax.dynamic_index_in_dim(jnp.asarray(pair_np), place[0], 0, keepdims=False)
    wave_rows = lax.dynamic_index_in_dim(jnp.asarray(wave_np), place[0], 0, keepdims=False)
    row_blocks = [own_rows] + [recv_from(own_rows, "gx", d) for d in range(1, grid_x)]
    total_atoms = grid_x * atoms
    f32 = jnp.float32
    tables = run(
        functools.partial(table_kernel, share, padded, (grid_x, grid_y)),
        [
            jax.ShapeDtypeStruct((padded, total_atoms), f32),
            jax.ShapeDtypeStruct((padded, total_atoms), f32),
            jax.ShapeDtypeStruct((8, total_atoms), f32),
            jax.ShapeDtypeStruct((8, total_atoms), f32),
            jax.ShapeDtypeStruct((wave_np.shape[1], 128), f32),
        ],
        [place, pair_rows, wave_rows, vectors] + row_blocks,
        smem=1,
        name="tables",
    )
    return tables, pair_rows, share, padded


def long_range_sum(tables, pair_rows, share, padded, charge_block, lat_width, atoms):
    grid_x, grid_y = lax.axis_size("gx"), lax.axis_size("gy")
    f32 = jnp.float32
    phases, weight = list(tables[:4]), tables[4]
    blocks = [charge_block] + [recv_from(charge_block, "gx", d) for d in range(1, grid_x)]
    rows = 32 * share + 2 * padded
    (part,) = run(
        functools.partial(structure_kernel, share, padded, grid_x),
        [jax.ShapeDtypeStruct((rows // 2, 2 * lat_width), f32)],
        phases + blocks,
        name="structure",
    )
    parts = [part] + [recv_from(part, "gy", d) for d in range(1, grid_y)]
    folds = run(
        functools.partial(fold_kernel, share, padded, (grid_x, grid_y)),
        [jax.ShapeDtypeStruct((lat_width + 8, atoms), f32)] * grid_x,
        phases + [weight, pair_rows] + blocks + parts,
        name="fold",
    )
    total = folds[0]
    for d in range(1, grid_x):
        total = total + recv_from(folds[d], "gx", -d)
    return total[:lat_width], total[lat_width : lat_width + 3]


def send_back(cotangent_grid):
    column = cotangent_grid[:, 1]
    for shift_by, column_pick in ((1, 2), (-1, 0)):
        column = column + passed_along(cotangent_grid[:, column_pick], "gy", shift_by)
    running = column[1]
    for shift_by, column_pick in ((1, 2), (-1, 0)):
        running = running + passed_along(column[column_pick], "gx", shift_by)
    return running


def per_device(
    positions,
    species,
    neighbours,
    counts,
    species_embed,
    radial,
    mixing,
    read_hidden,
    read_out,
    charge_map,
    wavevectors,
):
    atom_count = positions.shape[3]
    width = read_hidden.shape[0]
    lat_width = charge_map.shape[1]
    wave_count = wavevectors.shape[1]
    own_pos = positions[0, 0]
    neighbour_ids = neighbours[0, 0]
    slot_counts = counts[0, 0]
    packed = jnp.concatenate([positions, species.astype(jnp.float32)[:, :, None, :]], axis=2)
    packed8 = jnp.concatenate(
        [packed[0, 0], jnp.zeros((4, atom_count), jnp.float32)], axis=0
    )
    extended = with_halo(packed, (("gx", 0), ("gy", 1)), 1)
    src_pos, kind_codes = build_frame(extended)
    initial_src = embed_rows(kind_codes, species_embed)

    def layer_one(own_coords, source_coords):
        return first_layer(
            own_coords, source_coords, initial_src, neighbour_ids, slot_counts, radial, mixing
        )

    hidden_one, pull_one = jax.vjp(layer_one, own_pos, src_pos)
    hidden_low = hidden_one.astype(jnp.bfloat16)
    ghost_hidden = with_halo(hidden_low[None, None], (("gx", 0), ("gy", 1)), 1)
    hidden_src = ghost_hidden.reshape(9 * atom_count, width).astype(jnp.float32)

    def section_two(source_hidden, own_coords, source_coords):
        return second_section(
            source_hidden,
            own_coords,
            source_coords,
            neighbour_ids,
            slot_counts,
            radial,
            mixing,
            read_hidden,
            read_out,
            charge_map,
        )

    (energy_sr, charges), pull_two = jax.vjp(section_two, hidden_src, own_pos, src_pos)
    grid_x = lax.axis_size("gx")
    grid_y = lax.axis_size("gy")
    tables, pair_rows, share, padded = long_range(packed8, None, wavevectors, lat_width)
    potential, lr_grad = long_range_sum(
        tables, pair_rows, share, padded, pack_rows(charges), lat_width, atom_count
    )
    potential = potential.T
    lr_scale = 1.0 / math.sqrt(wave_count * lat_width * atom_count * grid_x * grid_y)
    site_energy = energy_sr + lr_scale * jnp.sum(charges * potential, axis=1)
    grad_hidden, grad_own_two, grad_src_two = pull_two(
        (jnp.ones_like(energy_sr), 2.0 * lr_scale * potential)
    )
    grad_hidden_own = send_back(grad_hidden.reshape(3, 3, atom_count, width))
    grad_own_one, grad_src_one = pull_one(grad_hidden_own)
    grad_src = jnp.moveaxis((grad_src_one + grad_src_two).reshape(3, 3, 3, atom_count), 0, 2)
    grad_back = send_back(grad_src)
    forces = -(grad_own_one + grad_own_two + grad_back + 2.0 * lr_scale * lr_grad)
    return (forces[None, None], site_energy[None, None])


def solution(mesh):
    in_specs = (
        P("gx", "gy", None, None),
        P("gx", "gy", None),
        P("gx", "gy", None, None),
        P("gx", "gy", None),
        P(),
        P(),
        P(),
        P(),
        P(),
        P(),
        P(),
    )
    out_specs = (P("gx", "gy", None, None), P("gx", "gy", None))
    return jax.shard_map(
        per_device, mesh=mesh, in_specs=in_specs, out_specs=out_specs, check_vma=False
    )
```

```python
import functools
import math

import jax
import jax.numpy as jnp
import numpy as np
from jax import lax
from jax.experimental import pallas as pl
from jax.experimental.pallas import tpu as pltpu
from jax.sharding import PartitionSpec as P

cell_width = 10.0
box_height = 30.0
cut_radius = 50.0
soften = 0.25
screen = 0.5
smear_width = 0.5
WAVE_REACH = 8
F32 = jnp.float32
BF16 = jnp.bfloat16
OFFSETS = [(a, b) for a in (-1, 0, 1) for b in (-1, 0, 1)]
CENTRE = 4


def shifted(block, along_x, along_y):
    count_x, count_y = lax.axis_size("gx"), lax.axis_size("gy")
    route = []
    for i in range(count_x):
        for j in range(count_y):
            source = ((i + along_x) % count_x) * count_y + (j + along_y) % count_y
            route.append((source, i * count_y + j))
    return lax.ppermute(block, ("gx", "gy"), route)


def whole(space=pltpu.VMEM):
    return pl.BlockSpec(memory_space=space)


def run(kernel, outs, args, scratch=(), smem=0, flops=1_000_000, name=None):
    specs = [whole(pltpu.SMEM)] * smem + [whole()] * (len(args) - smem)
    return pl.pallas_call(
        kernel,
        out_shape=outs,
        in_specs=specs,
        out_specs=jax.tree.map(lambda _: whole(), outs),
        scratch_shapes=list(scratch),
        compiler_params=pltpu.CompilerParams(vmem_limit_bytes=48 * 1024 * 1024),
        cost_estimate=pl.CostEstimate(flops=flops, bytes_accessed=1_000_000, transcendentals=0),
        name=name,
    )(*args)


def shape(*dims, dtype=F32):
    return jax.ShapeDtypeStruct(dims, dtype)


def split(value):
    high = value.astype(BF16)
    return high, (value - high.astype(F32)).astype(BF16)


def dot(left, right, contract=((1,), (0,))):
    return lax.dot_general(left, right, (contract, ((), ())), preferred_element_type=F32)


def dot3(left, right):
    left_high, left_low = split(left)
    right_high, right_low = split(right)
    return dot(left_high, right_high) + (dot(left_high, right_low) + dot(left_low, right_high))


def stacked_left(value):
    high = value.astype(BF16).astype(F32)
    rows = jnp.concatenate([high, high, value - high, jnp.zeros_like(high)], axis=0)
    return rows.T.astype(BF16)


def stacked_right(value):
    high = value.astype(BF16).astype(F32)
    return jnp.concatenate([high, value - high, high, jnp.zeros_like(high)], axis=0).astype(BF16)


def silu_pair(value):
    gate = 1.0 / (1.0 + jnp.exp(-value))
    return value * gate, gate * (1.0 + value * (1.0 - gate))


def flat_row(block):
    return jnp.concatenate([block[n : n + 1] for n in range(block.shape[0])], axis=1)


def onehot_kinds(kinds, rows):
    levels = lax.broadcasted_iota(jnp.int32, (rows, kinds.shape[1]), 0).astype(F32)
    return jnp.where(kinds == levels, 1.0, 0.0)


def embedding_stack(embed):
    high = embed.astype(BF16).astype(F32)
    rest = embed - high
    middle = rest.astype(BF16).astype(F32)
    rows = jnp.concatenate([high, middle, rest - middle, jnp.zeros_like(high)], axis=0)
    return rows.T.astype(BF16)


def embedded(stack, kinds):
    hot = onehot_kinds(kinds, 8)
    return dot(stack, jnp.concatenate([hot, hot, hot, jnp.zeros_like(hot)], axis=0).astype(BF16))


def messages(edge_rows, radial_ref, layer, slots, atoms, source):
    scalar = stacked_left(radial_ref[layer, 0])
    vector = stacked_left(radial_ref[layer, 1])
    sums = [None] * 4
    for n in range(slots):
        lanes = slice(n * atoms, (n + 1) * atoms)
        feature = source(n)
        for part in range(4):
            weight = dot(vector if part else scalar, stacked_right(edge_rows[part][:, lanes]))
            term = weight * feature
            sums[part] = term if sums[part] is None else sums[part] + term
    norm = 1.0 / math.sqrt(slots)
    return [total * norm for total in sums]


def mixed(sums, mixing_ref, layer):
    squares = sums[1] * sums[1] + sums[2] * sums[2] + sums[3] * sums[3]
    pre = dot3(mixing_ref[layer, 0].T, sums[0]) + dot3(mixing_ref[layer, 1].T, squares)
    return silu_pair(pre)


def edge_parts(basis_ref, unit_ref):
    basis = basis_ref[...]
    unit = unit_ref[...]
    return [basis] + [basis * unit[i : i + 1] for i in range(3)]


def first_kernel(slots, neighbour_ref, count_ref, embed_ref, radial_ref, mixing_ref, *refs):
    frame, (low_ref, basis_ref, slope_ref, unit_ref, sums_ref, gate_ref) = refs[:9], refs[9:]
    atoms = frame[0].shape[1]
    ids = flat_row(neighbour_ref[...])
    halves = []
    for cell, (a, b) in enumerate(OFFSETS):
        block = frame[cell][...]
        if (a, b) != (0, 0):
            block = jnp.concatenate(
                [block[0:1] + a * cell_width, block[1:2] + b * cell_width, block[2:]], axis=0
            )
        halves += [block[:, s : s + 128] for s in range(0, atoms, 128)]
    pieces = []
    for start in range(0, ids.shape[1], 128):
        part = jnp.broadcast_to(ids[:, start : start + 128], (8, 128))
        lane, half = part & 127, part >> 7
        found = jnp.zeros((8, 128), F32)
        for h, rows in enumerate(halves):
            found = jnp.where(half == h, jnp.take_along_axis(rows, lane, axis=1), found)
        pieces.append(found)
    found = jnp.concatenate(pieces, axis=1)
    own = frame[CENTRE][...]
    relative = found - jnp.concatenate([own] * slots, axis=1)
    rel = [relative[i : i + 1] for i in range(3)]
    distance = jnp.sqrt(rel[0] * rel[0] + rel[1] * rel[1] + rel[2] * rel[2] + soften)
    inverse = 1.0 / distance
    orders = radial_ref.shape[2]
    order = (lax.broadcasted_iota(jnp.int32, (orders, 1), 0) + 1).astype(F32)
    phase = (order * (math.pi / cut_radius)) * distance
    wave = jnp.sin(phase) / phase
    count = count_ref[...]
    live = jnp.concatenate([jnp.where(count > n, 1.0, 0.0) for n in range(slots)], axis=1)
    basis_ref[...] = wave * live
    slope_ref[...] = (jnp.cos(phase) - wave) * (inverse * live)
    kinds = found[3:4]
    unit_ref[...] = jnp.concatenate(
        [r * inverse for r in rel] + [inverse, kinds] + [jnp.zeros_like(kinds)] * 3, axis=0
    )
    stack = embedding_stack(embed_ref[...])
    sums = messages(
        edge_parts(basis_ref, unit_ref),
        radial_ref,
        0,
        slots,
        atoms,
        lambda n: embedded(stack, kinds[:, n * atoms : (n + 1) * atoms]),
    )
    step, gate = mixed(sums, mixing_ref, 0)
    low_ref[...] = (embedded(stack, own[3:4]) + step).astype(BF16)
    for part in range(3):
        sums_ref[part] = sums[part + 1]
    gate_ref[...] = gate


def hot_columns(ids, rows):
    place = lax.broadcasted_iota(jnp.int32, (rows, ids.shape[1]), 0)
    return jnp.where(ids == place, 1.0, 0.0).astype(BF16)


def second_kernel(slots, neighbour_ref, basis_ref, unit_ref, radial_ref, mixing_ref, hidden_ref,
                  out_ref, charge_ref, *refs):
    frame, refs = refs[:9], refs[9:]
    feature_ref, sums_ref, gate_ref, low_charge_ref, full_charge_ref, energy_ref, slope_ref = refs[:7]
    (source_ref,) = refs[7:]
    atoms = frame[0].shape[1]
    for cell in range(9):
        source_ref[:, cell * atoms : (cell + 1) * atoms] = frame[cell][...]

    def gathered(n):
        hot = hot_columns(neighbour_ref[n : n + 1, :], 9 * atoms)
        feature = dot(source_ref[...], hot)
        feature_ref[:, n * atoms : (n + 1) * atoms] = feature.astype(BF16)
        return feature

    sums = messages(edge_parts(basis_ref, unit_ref), radial_ref, 1, slots, atoms, gathered)
    step, gate = mixed(sums, mixing_ref, 1)
    hidden = frame[CENTRE][...].astype(F32) + step
    for part in range(3):
        sums_ref[part] = sums[part + 1]
    gate_ref[...] = gate
    charge = dot3(charge_ref[...].T, hidden)
    full_charge_ref[...] = charge
    low_charge_ref[...] = charge.astype(low_charge_ref.dtype)
    value, slope = silu_pair(dot3(hidden_ref[...].T, hidden))
    out = out_ref[...].T
    energy_ref[...] = jnp.sum(value * out, axis=0, keepdims=True)
    slope_ref[...] = dot3(hidden_ref[...], slope * out)


def message_grads(cotangent, gate_ref, sums_ref, mixing_ref, layer, slots):
    pre = cotangent * gate_ref[...]
    norm = 1.0 / math.sqrt(slots)
    scalar = dot3(mixing_ref[layer, 0], pre) * norm
    squares = dot3(mixing_ref[layer, 1], pre) * (2.0 * norm)
    return [scalar] + [squares * sums_ref[i] for i in range(3)]


def radial_left(radial_ref, layer, path):
    high, low = split(radial_ref[layer, path])
    top = jnp.concatenate([high.astype(F32), high.astype(F32)], axis=1)
    end = jnp.concatenate([low.astype(F32), jnp.zeros(low.shape, F32)], axis=1)
    return jnp.concatenate([top, end], axis=0).astype(BF16)


def radial_grad(left, value):
    high, low = split(value)
    both = dot(left, jnp.concatenate([high, low], axis=0))
    half = both.shape[0] // 2
    return both[:half] + both[half:]


def second_back_kernel(slots, scale, grid_x, neighbour_ref, basis_ref, unit_ref, radial_ref,
                       mixing_ref, charge_ref, feature_ref, sums_ref, gate_ref, full_charge_ref,
                       energy_ref, slope_ref, *refs):
    folds, refs = refs[:grid_x], refs[grid_x:]
    site_ref, long_ref, edge_ref, centre_ref = refs[:4]
    ghosts, (term_ref,) = refs[4:12], refs[12:]
    atoms = gate_ref.shape[1]
    total = folds[0][...]
    for fold in folds[1:]:
        total = total + fold[...]
    wide = full_charge_ref.shape[0]
    potential = total[:wide]
    long_ref[...] = total[wide:] * (2.0 * scale)
    site_ref[...] = energy_ref[...] + scale * jnp.sum(
        full_charge_ref[...] * potential, axis=0, keepdims=True
    )
    cotangent = slope_ref[...] + dot3(charge_ref[...], potential * (2.0 * scale))
    grads = message_grads(cotangent, gate_ref, sums_ref, mixing_ref, 1, slots)
    left = [stacked_left(radial_ref[1, path]) for path in range(2)]
    back = [radial_left(radial_ref, 1, path) for path in range(2)]
    parts = edge_parts(basis_ref, unit_ref)
    for n in range(slots):
        lanes = slice(n * atoms, (n + 1) * atoms)
        feature = feature_ref[:, lanes].astype(F32)
        term = None
        for part in range(4):
            path = 1 if part else 0
            edge_ref[8 * part : 8 * part + 8, lanes] = radial_grad(back[path], grads[part] * feature)
            weight = dot(left[path], stacked_right(parts[part][:, lanes])) * grads[part]
            term = weight if term is None else term + weight
        high, low = split(term)
        term_ref[:, lanes] = jnp.concatenate([high, low], axis=0)
    ids = flat_row(neighbour_ref[...])
    features = centre_ref.shape[0]
    for cell in range(9):
        hot = hot_columns(ids - cell * atoms, atoms)
        both = dot(term_ref[...], hot, ((1,), (1,)))
        grad = both[:features] + both[features:]
        if cell == CENTRE:
            centre_ref[...] = grad + cotangent
        else:
            ghosts[cell - (cell > CENTRE)][...] = grad.astype(BF16)


def first_back_kernel(slots, neighbour_ref, basis_ref, slope_ref, unit_ref, embed_ref, radial_ref,
                      mixing_ref, sums_ref, gate_ref, edge_ref, long_ref, centre_ref, *refs):
    ghosts, refs = refs[:8], refs[8:]
    own_ref, outs = refs[0], refs[1:]
    atoms = gate_ref.shape[1]
    cotangent = centre_ref[...]
    for ghost in ghosts:
        cotangent = cotangent + ghost[...].astype(F32)
    grads = message_grads(cotangent, gate_ref, sums_ref, mixing_ref, 0, slots)
    back = [radial_left(radial_ref, 0, path) for path in range(2)]
    stack = embedding_stack(embed_ref[...])
    unit = unit_ref[...]
    kinds = unit[4:5]
    edges = [[] for _ in range(4)]
    for n in range(slots):
        lanes = slice(n * atoms, (n + 1) * atoms)
        feature = embedded(stack, kinds[:, lanes])
        for part in range(4):
            edges[part].append(radial_grad(back[1 if part else 0], grads[part] * feature))
    edges = [
        edge_ref[8 * part : 8 * part + 8] + jnp.concatenate(edges[part], axis=1) for part in range(4)
    ]
    basis = basis_ref[...]
    units = [unit[i : i + 1] for i in range(3)]
    inverse = unit[3:4]
    by_basis = edges[0]
    for i in range(3):
        by_basis = by_basis + edges[i + 1] * units[i]
    by_unit = [jnp.sum(edges[i + 1] * basis, axis=0, keepdims=True) * inverse for i in range(3)]
    by_distance = jnp.sum(by_basis * slope_ref[...], axis=0, keepdims=True)
    for i in range(3):
        by_distance = by_distance - by_unit[i] * units[i]
    moves = [by_unit[i] + by_distance * units[i] for i in range(3)]
    zero = jnp.zeros_like(moves[0])
    move = jnp.concatenate(moves + [zero] * 5, axis=0)
    own = long_ref[...]
    for n in range(slots):
        own = own - move[:, n * atoms : (n + 1) * atoms]
    ids = flat_row(neighbour_ref[...])
    lane_hot = hot_columns(ids & 127, 128)
    half = ids >> 7
    high = move.astype(BF16).astype(F32)
    both = jnp.concatenate([high, move - high], axis=0)
    per_cell = atoms // 128
    rows = jnp.concatenate(
        [jnp.where(half == h, both, 0.0).astype(BF16) for h in range(9 * per_cell)], axis=0
    )
    spread = dot(rows, lane_hot, ((1,), (1,)))
    for cell in range(9):
        found = []
        for h in range(cell * per_cell, (cell + 1) * per_cell):
            found.append(spread[16 * h : 16 * h + 8] + spread[16 * h + 8 : 16 * h + 16])
        grad = jnp.concatenate(found, axis=1)
        if cell == CENTRE:
            own_ref[...] = own + grad
        else:
            outs[cell - (cell > CENTRE)][...] = grad


def pair_tables(parts):
    reach = WAVE_REACH
    pairs = [(0, y) for y in range(1, reach + 1)]
    pairs += [(x, y) for x in range(1, reach + 1) for y in range(-reach, reach + 1)]
    share = -(-len(pairs) // parts)
    padded = -(-share // 8) * 8
    side = 2 * reach + 1
    pair_rows = np.zeros((parts, padded, 8), np.float32)
    wave_rows = np.zeros((parts, 2 * 8 * share + padded, 8), np.float32)
    for part in range(parts):
        for slot, (x, y) in enumerate(pairs[part * share : (part + 1) * share]):
            pair_rows[part, slot, :2] = (x, y)
            rows = [(8 * slot + z - 1, z) for z in range(1, 9)]
            rows += [(8 * share + 8 * slot + z - 1, -z) for z in range(1, 9)]
            rows += [(16 * share + slot, 0)]
            for row, z in rows:
                code = ((x + reach) * side + y + reach) * side + z + reach
                wave_rows[part, row, :5] = (x, y, z, code, 1.0)
    return share, padded, pair_rows, wave_rows


def table_kernel(share, padded, grid, pos_ref, pair_ref, wave_ref, vec_ref, *refs):
    grid_x, grid_y = grid
    blocks, (ca_ref, sa_ref, cb_ref, sb_ref, weight_ref) = refs[:grid_x], refs[grid_x:]
    turn = 2.0 * math.pi
    col = pos_ref[1].astype(jnp.float32) * (1.0 / grid_y)
    kx = pair_ref[:, 0:1]
    ky = pair_ref[:, 1:2]
    kz = (lax.broadcasted_iota(jnp.int32, (8, 1), 0) + 1).astype(jnp.float32)
    for d in range(grid_x):
        row_id = lax.rem(pos_ref[0] + d, grid_x).astype(jnp.float32) * (1.0 / grid_x)
        block = blocks[d]
        lanes = pl.ds(d * block.shape[1], block.shape[1])
        x = block[0:1, :] * (1.0 / (grid_x * cell_width)) + row_id
        y = block[1:2, :] * (1.0 / (grid_y * cell_width)) + col
        z = block[2:3, :] * (1.0 / box_height)
        alpha = kx * x + ky * y
        alpha = (alpha - jnp.round(alpha)) * turn
        beta = kz * z
        beta = (beta - jnp.round(beta)) * turn
        ca_ref[:, lanes] = jnp.cos(alpha)
        sa_ref[:, lanes] = jnp.sin(alpha)
        cb_ref[:, lanes] = jnp.cos(beta)
        sb_ref[:, lanes] = jnp.sin(beta)
    side = 2 * WAVE_REACH + 1
    top = side * side * side - 1
    vec = vec_ref[...].astype(jnp.float32) + WAVE_REACH
    code = (vec[0:1] * side + vec[1:2]) * side + vec[2:3]
    code = jnp.maximum(code, top - code)
    wave = wave_ref[...]
    own = wave[:, 3:4]
    width = code.shape[1]
    seen = jnp.zeros((own.shape[0], 128), jnp.float32)
    for start in range(0, width, 128):
        seen = seen + jnp.where(own == code[:, start : start + 128], 1.0, 0.0)
    count = jnp.sum(seen, axis=1, keepdims=True) * wave[:, 4:5]
    sq = (
        (wave[:, 0:1] * (turn / (grid_x * cell_width))) ** 2
        + (wave[:, 1:2] * (turn / (grid_y * cell_width))) ** 2
        + (wave[:, 2:3] * (turn / box_height)) ** 2
    )
    green = jnp.exp(-smear_width * sq) / (sq + screen * screen) * count
    weight_ref[...] = jnp.broadcast_to(green, weight_ref.shape)


def basis_rows(share, ca, sa, cb, sb):
    cc, ss, sc, cs = [], [], [], []
    for p in range(share):
        c, s = ca[p : p + 1], sa[p : p + 1]
        cc.append(c * cb)
        ss.append(s * sb)
        sc.append(s * cb)
        cs.append(c * sb)
    return cc, ss, sc, cs


def unpack_rows(block):
    half = block.shape[1] // 2
    return jnp.concatenate([block[:, :half], block[:, half:]], axis=0)


def pack_rows(block):
    half = block.shape[0] // 2
    return jnp.concatenate([block[:half], block[half:]], axis=1)


def structure_kernel(share, padded, grid_x, *refs):
    ca_ref, sa_ref, cb_ref, sb_ref = refs[:4]
    blocks, (out_ref,) = refs[4 : 4 + grid_x], refs[4 + grid_x :]
    total = None
    for d in range(grid_x):
        charge = blocks[d][...]
        atoms = charge.shape[1]
        lanes = pl.ds(d * atoms, atoms)
        ca, sa, cb, sb = ca_ref[:, lanes], sa_ref[:, lanes], cb_ref[:, lanes], sb_ref[:, lanes]
        cc, ss, sc, cs = basis_rows(share, ca, sa, cb, sb)
        high, low = split(jnp.concatenate(cc + ss + sc + cs + [ca, sa], axis=0))
        term = dot(high, charge, ((1,), (1,))) + dot(low, charge, ((1,), (1,)))
        total = term if total is None else total + term
    out_ref[...] = pack_rows(total).astype(out_ref.dtype)


def fold_kernel(share, padded, grid, *refs):
    grid_x, grid_y = grid
    ca_ref, sa_ref, cb_ref, sb_ref, weight_ref, pair_ref = refs[:6]
    blocks = refs[6 : 6 + grid_x]
    parts = refs[6 + grid_x : 6 + grid_x + grid_y]
    outs = refs[6 + grid_x + grid_y :]
    turn = 2.0 * math.pi
    packed = parts[0][...].astype(jnp.float32)
    for part in parts[1:]:
        packed = packed + part[...].astype(jnp.float32)
    struct = unpack_rows(packed)
    wide = struct.shape[1]
    span = 8 * share
    cc, ss, sc, cs = (struct[i * span : (i + 1) * span] for i in range(4))
    weight = weight_ref[:, :wide]
    plus, minus, flat = weight[:span], weight[span : 2 * span], weight[2 * span :]
    re_plus, im_plus = plus * (cc - ss), plus * (sc + cs)
    re_minus, im_minus = minus * (cc + ss), minus * (sc - cs)
    rows = jnp.concatenate(
        [
            re_plus + re_minus,
            re_minus - re_plus,
            im_plus + im_minus,
            im_plus - im_minus,
            flat * struct[4 * span : 4 * span + padded],
            flat * struct[4 * span + padded :],
        ],
        axis=0,
    )
    row_high, row_low = split(rows)
    row_pair = jnp.concatenate([row_high, row_low], axis=1)
    turned = rows.T
    t_high, t_low = split(turned)
    t_both = jnp.concatenate([t_high, t_low], axis=0)
    kx = pair_ref[:, 0:1] * (turn / (grid_x * cell_width))
    ky = pair_ref[:, 1:2] * (turn / (grid_y * cell_width))
    kz = (lax.broadcasted_iota(jnp.int32, (8, 1), 0) + 1).astype(jnp.float32) * (turn / box_height)
    for d in range(grid_x):
        charge = blocks[d][...]
        atoms = charge.shape[1]
        lanes = pl.ds(d * atoms, atoms)
        ca, sa, cb, sb = ca_ref[:, lanes], sa_ref[:, lanes], cb_ref[:, lanes], sb_ref[:, lanes]
        bcc, bss, bsc, bcs = basis_rows(share, ca, sa, cb, sb)
        high, low = split(jnp.concatenate(bcc + bss + bsc + bcs + [ca, sa], axis=0))
        both = dot(t_both, high)
        pot = both[:wide] + both[wide:] + dot(t_high, low)
        proj = dot(row_pair, jnp.concatenate([charge, charge], axis=0))
        by_x = jnp.zeros((8, atoms), jnp.float32)
        by_y = jnp.zeros((8, atoms), jnp.float32)
        by_z = jnp.zeros((8, atoms), jnp.float32)
        for p in range(share):
            pcc, pss, psc, pcs = (
                proj[i * span + 8 * p : i * span + 8 * p + 8] for i in range(4)
            )
            slope = bcs[p] * pss - bsc[p] * pcc + bcc[p] * psc - bss[p] * pcs
            by_x = by_x + kx[p : p + 1] * slope
            by_y = by_y + ky[p : p + 1] * slope
            by_z = by_z + (bsc[p] * pss - bcs[p] * pcc - bss[p] * psc + bcc[p] * pcs)
        flat_slope = ca * proj[4 * span + padded :] - sa * proj[4 * span : 4 * span + padded]
        grad_x = jnp.sum(by_x, axis=0, keepdims=True) + jnp.sum(kx * flat_slope, axis=0, keepdims=True)
        grad_y = jnp.sum(by_y, axis=0, keepdims=True) + jnp.sum(ky * flat_slope, axis=0, keepdims=True)
        grad_z = jnp.sum(kz * by_z, axis=0, keepdims=True)
        zero = jnp.zeros((5, atoms), jnp.float32)
        outs[d][...] = jnp.concatenate([pot, grad_x, grad_y, grad_z, zero], axis=0)


def per_device(
    positions,
    species,
    neighbours,
    counts,
    species_embed,
    radial,
    mixing,
    read_hidden,
    read_out,
    charge_map,
    wavevectors,
):
    atoms = positions.shape[3]
    slots = neighbours.shape[3]
    features, lat_width = charge_map.shape
    wave_count = wavevectors.shape[1]
    grid = lax.axis_size("gx"), lax.axis_size("gy")
    grid_x, grid_y = grid
    edges = slots * atoms
    scale = 1.0 / math.sqrt(wave_count * lat_width * atoms * grid_x * grid_y)
    ids = neighbours[0, 0].T
    count = counts[0]
    embed = jnp.pad(species_embed, ((0, 8 - species_embed.shape[0]), (0, 0)))
    kinds = species[0].astype(F32)
    own = jnp.concatenate([positions[0, 0], kinds, jnp.zeros((4, atoms), F32)], axis=0)

    frame = [own if cell == CENTRE else shifted(own, *at) for cell, at in enumerate(OFFSETS)]
    row = {0: own, 1: frame[7], grid_x - 1: frame[1]}
    row = [row[d] if d in row else shifted(own, d, 0) for d in range(grid_x)]

    low, basis, slope, unit, sums_one, gate_one = run(
        functools.partial(first_kernel, slots),
        [
            shape(features, atoms, dtype=BF16),
            shape(8, edges),
            shape(8, edges),
            shape(8, edges),
            shape(3, features, atoms),
            shape(features, atoms),
        ],
        [ids, count, embed, radial, mixing] + frame,
        name="first",
    )
    hidden = [low if cell == CENTRE else shifted(low, *at) for cell, at in enumerate(OFFSETS)]

    share, padded, pair_np, wave_np = pair_tables(grid_x)
    place = jnp.stack([lax.axis_index("gx"), lax.axis_index("gy")]).astype(jnp.int32)
    pair_rows = lax.dynamic_index_in_dim(jnp.asarray(pair_np), place[0], 0, keepdims=False)
    wave_rows = lax.dynamic_index_in_dim(jnp.asarray(wave_np), place[0], 0, keepdims=False)
    span = grid_x * atoms
    *phases, weight = run(
        functools.partial(table_kernel, share, padded, grid),
        [
            shape(padded, span),
            shape(padded, span),
            shape(8, span),
            shape(8, span),
            shape(wave_np.shape[1], 128),
        ],
        [place, pair_rows, wave_rows, wavevectors] + row,
        smem=1,
        name="tables",
    )

    feature, sums_two, gate_two, low_charge, charge, energy, energy_slope = run(
        functools.partial(second_kernel, slots),
        [
            shape(features, edges, dtype=BF16),
            shape(3, features, atoms),
            shape(features, atoms),
            shape(lat_width, atoms, dtype=BF16),
            shape(lat_width, atoms),
            shape(1, atoms),
            shape(features, atoms),
        ],
        [ids, basis, unit, radial, mixing, read_hidden, read_out[None, :], charge_map] + hidden,
        scratch=[pltpu.VMEM((features, 9 * atoms), BF16)],
        name="second",
    )
    charges = [low_charge] + [shifted(low_charge, d, 0) for d in range(1, grid_x)]
    rows = 32 * share + 2 * padded
    (part,) = run(
        functools.partial(structure_kernel, share, padded, grid_x),
        [shape(rows // 2, 2 * lat_width)],
        phases + charges,
        name="structure",
    )
    parts = [part] + [shifted(part, 0, d) for d in range(1, grid_y)]
    folds = run(
        functools.partial(fold_kernel, share, padded, grid),
        [shape(lat_width + 8, atoms)] * grid_x,
        phases + [weight, pair_rows] + charges + parts,
        name="fold",
    )
    folds = [folds[0]] + [shifted(folds[d], -d, 0) for d in range(1, grid_x)]

    site, long, edge, centre, *ghosts = run(
        functools.partial(second_back_kernel, slots, scale, grid_x),
        [shape(1, atoms), shape(8, atoms), shape(32, edges), shape(features, atoms)]
        + [shape(features, atoms, dtype=BF16)] * 8,
        [ids, basis, unit, radial, mixing, charge_map, feature, sums_two, gate_two, charge, energy,
         energy_slope] + folds,
        scratch=[pltpu.VMEM((2 * features, edges), BF16)],
        name="second_back",
    )
    around = [at for at in OFFSETS if at != (0, 0)]
    ghosts = [shifted(ghost, -a, -b) for ghost, (a, b) in zip(ghosts, around)]
    mine, *moves = run(
        functools.partial(first_back_kernel, slots),
        [shape(8, atoms)] * 9,
        [ids, basis, slope, unit, embed, radial, mixing, sums_one, gate_one, edge, long, centre]
        + ghosts,
        name="first_back",
    )
    for move, (a, b) in zip(moves, around):
        mine = mine + shifted(move, -a, -b)
    return (-mine[None, None, :3], site[None])


def solution(mesh):
    in_specs = (
        P("gx", "gy", None, None),
        P("gx", "gy", None),
        P("gx", "gy", None, None),
        P("gx", "gy", None),
        P(),
        P(),
        P(),
        P(),
        P(),
        P(),
        P(),
    )
    out_specs = (P("gx", "gy", None, None), P("gx", "gy", None))
    return jax.shard_map(
        per_device, mesh=mesh, in_specs=in_specs, out_specs=out_specs, check_vma=False
    )
```

```python
import functools
import math

import jax
import jax.numpy as jnp
import numpy as np
from jax import lax
from jax.experimental import pallas as pl
from jax.experimental.pallas import tpu as pltpu
from jax.sharding import PartitionSpec as P

cell_width = 10.0
box_height = 30.0
cut_radius = 50.0
soften = 0.25
screen = 0.5
smear_width = 0.5
WAVE_REACH = 8
F32 = jnp.float32
BF16 = jnp.bfloat16
OFFSETS = [(a, b) for a in (-1, 0, 1) for b in (-1, 0, 1)]
CENTRE = 4


def shifted(block, along_x, along_y):
    count_x, count_y = lax.axis_size("gx"), lax.axis_size("gy")
    route = []
    for i in range(count_x):
        for j in range(count_y):
            source = ((i + along_x) % count_x) * count_y + (j + along_y) % count_y
            route.append((source, i * count_y + j))
    return lax.ppermute(block, ("gx", "gy"), route)


def exchanged(blocks, axis):
    return lax.all_to_all(blocks, axis, 0, 0)


def around(block):
    column = jnp.stack([shifted(block, 0, -1), block, shifted(block, 0, 1)])
    return [shifted(column, -1, 0), column, shifted(column, 1, 0)]


def whole(space=pltpu.VMEM):
    return pl.BlockSpec(memory_space=space)


def run(kernel, outs, args, scratch=(), smem=0, flops=1_000_000, name=None):
    specs = [whole(pltpu.SMEM)] * smem + [whole()] * (len(args) - smem)
    return pl.pallas_call(
        kernel,
        out_shape=outs,
        in_specs=specs,
        out_specs=jax.tree.map(lambda _: whole(), outs),
        scratch_shapes=list(scratch),
        compiler_params=pltpu.CompilerParams(vmem_limit_bytes=48 * 1024 * 1024),
        cost_estimate=pl.CostEstimate(flops=flops, bytes_accessed=1_000_000, transcendentals=0),
        name=name,
    )(*args)


def shape(*dims, dtype=F32):
    return jax.ShapeDtypeStruct(dims, dtype)


def split(value):
    high = value.astype(BF16)
    return high, (value - high.astype(F32)).astype(BF16)


def dot(left, right, contract=((1,), (0,))):
    return lax.dot_general(left, right, (contract, ((), ())), preferred_element_type=F32)


def dot3(left, right):
    left_high, left_low = split(left)
    right_high, right_low = split(right)
    return dot(left_high, right_high) + (dot(left_high, right_low) + dot(left_low, right_high))


def stacked_left(value):
    high = value.astype(BF16).astype(F32)
    rows = jnp.concatenate([high, high, value - high, jnp.zeros_like(high)], axis=0)
    return rows.T.astype(BF16)


def stacked_right(value):
    high = value.astype(BF16).astype(F32)
    return jnp.concatenate([high, value - high, high, jnp.zeros_like(high)], axis=0).astype(BF16)


def silu_pair(value):
    gate = 1.0 / (1.0 + jnp.exp(-value))
    return value * gate, gate * (1.0 + value * (1.0 - gate))


def flat_row(block):
    return jnp.concatenate([block[n : n + 1] for n in range(block.shape[0])], axis=1)


def onehot_kinds(kinds, rows):
    levels = lax.broadcasted_iota(jnp.int32, (rows, kinds.shape[1]), 0).astype(F32)
    return jnp.where(kinds == levels, 1.0, 0.0)


def embedding_stack(embed):
    high = embed.astype(BF16).astype(F32)
    rest = embed - high
    middle = rest.astype(BF16).astype(F32)
    rows = jnp.concatenate([high, middle, rest - middle, jnp.zeros_like(high)], axis=0)
    return rows.T.astype(BF16)


def embedded(stack, kinds):
    hot = onehot_kinds(kinds, 8)
    return dot(stack, jnp.concatenate([hot, hot, hot, jnp.zeros_like(hot)], axis=0).astype(BF16))


def messages(edge_rows, radial_ref, layer, slots, atoms, source):
    scalar = stacked_left(radial_ref[layer, 0])
    vector = stacked_left(radial_ref[layer, 1])
    sums = [None] * 4
    for n in range(slots):
        lanes = slice(n * atoms, (n + 1) * atoms)
        feature = source(n)
        for part in range(4):
            weight = dot(vector if part else scalar, stacked_right(edge_rows[part][:, lanes]))
            term = weight * feature
            sums[part] = term if sums[part] is None else sums[part] + term
    norm = 1.0 / math.sqrt(slots)
    return [total * norm for total in sums]


def mixed(sums, mixing_ref, layer):
    squares = sums[1] * sums[1] + sums[2] * sums[2] + sums[3] * sums[3]
    pre = dot3(mixing_ref[layer, 0].T, sums[0]) + dot3(mixing_ref[layer, 1].T, squares)
    return silu_pair(pre)


def edge_parts(basis_ref, unit_ref):
    basis = basis_ref[...]
    unit = unit_ref[...]
    return [basis] + [basis * unit[i : i + 1] for i in range(3)]


def pack_kernel(position_ref, species_ref, out_ref):
    rows = jnp.concatenate([position_ref[0, 0], species_ref[0].astype(F32)], axis=0)
    block = jnp.concatenate([rows[:, s : s + 128] for s in range(0, rows.shape[1], 128)], axis=0)
    for copy in range(out_ref.shape[0]):
        out_ref[copy] = block


def prep_kernel(grid, neighbour_ref, embed_ref, radial_ref, mixing_ref, hidden_ref, charge_ref,
                wave_ref, vec_ref, id_ref, rows_ref, radial_out, mixing_out, hidden_out, charge_out,
                weight_ref):
    id_ref[...] = neighbour_ref[0, 0].astype(F32).T.astype(jnp.int32)
    kinds = embed_ref.shape[0]
    rows_ref[...] = jnp.concatenate(
        [embed_ref[...], jnp.zeros((8 - kinds, embed_ref.shape[1]), F32)], axis=0
    )
    radial_out[...] = radial_ref[...]
    mixing_out[...] = mixing_ref[...]
    hidden_out[...] = hidden_ref[...]
    charge_out[...] = charge_ref[...]
    green_weights(grid, wave_ref, vec_ref, weight_ref)


def unfold_block(block, atoms):
    parts = atoms // 128
    return jnp.concatenate([block[4 * s : 4 * s + 4] for s in range(parts)], axis=1)


def first_kernel(slots, grid, place_ref, neighbour_ref, count_ref, embed_ref, radial_ref,
                 mixing_ref, all_ref, low_ref, basis_ref, slope_ref, unit_ref, sums_ref, gate_ref):
    atoms = low_ref.shape[1]
    ids = flat_row(neighbour_ref[...])
    halves = []
    for cell, (a, b) in enumerate(OFFSETS):
        block = all_ref[lax.rem(place_ref[0] + (a + grid[0]), grid[0]),
                        lax.rem(place_ref[1] + (b + grid[1]), grid[1])]
        if cell == CENTRE:
            own = unfold_block(block, atoms)
            own = jnp.concatenate([own, jnp.zeros_like(own)], axis=0)
        for s in range(atoms // 128):
            rows = block[4 * s : 4 * s + 4]
            halves.append(
                jnp.concatenate(
                    [rows[0:1] + a * cell_width, rows[1:2] + b * cell_width, rows[2:4], rows],
                    axis=0,
                )
            )
    pieces = []
    for start in range(0, ids.shape[1], 128):
        part = jnp.broadcast_to(ids[:, start : start + 128], (8, 128))
        lane, half = part & 127, part >> 7
        found = jnp.zeros((8, 128), F32)
        for h, rows in enumerate(halves):
            found = jnp.where(half == h, jnp.take_along_axis(rows, lane, axis=1), found)
        pieces.append(found)
    found = jnp.concatenate(pieces, axis=1)
    relative = found - jnp.concatenate([own] * slots, axis=1)
    rel = [relative[i : i + 1] for i in range(3)]
    distance = jnp.sqrt(rel[0] * rel[0] + rel[1] * rel[1] + rel[2] * rel[2] + soften)
    inverse = 1.0 / distance
    orders = radial_ref.shape[2]
    order = (lax.broadcasted_iota(jnp.int32, (orders, 1), 0) + 1).astype(F32)
    phase = (order * (math.pi / cut_radius)) * distance
    wave = jnp.sin(phase) / phase
    count = count_ref[...]
    live = jnp.concatenate([jnp.where(count > n, 1.0, 0.0) for n in range(slots)], axis=1)
    basis_ref[...] = wave * live
    slope_ref[...] = (jnp.cos(phase) - wave) * (inverse * live)
    kinds = found[3:4]
    unit_ref[...] = jnp.concatenate(
        [r * inverse for r in rel] + [inverse, kinds] + [jnp.zeros_like(kinds)] * 3, axis=0
    )
    stack = embedding_stack(embed_ref[...])
    sums = messages(
        edge_parts(basis_ref, unit_ref),
        radial_ref,
        0,
        slots,
        atoms,
        lambda n: embedded(stack, kinds[:, n * atoms : (n + 1) * atoms]),
    )
    step, gate = mixed(sums, mixing_ref, 0)
    low_ref[...] = (embedded(stack, own[3:4]) + step).astype(BF16)
    for part in range(3):
        sums_ref[part] = sums[part + 1]
    gate_ref[...] = gate


def hot_columns(ids, rows):
    place = lax.broadcasted_iota(jnp.int32, (rows, ids.shape[1]), 0)
    return jnp.where(ids == place, 1.0, 0.0).astype(BF16)


def second_kernel(slots, neighbour_ref, basis_ref, unit_ref, radial_ref, mixing_ref, hidden_ref,
                  out_ref, charge_ref, *refs):
    frame, refs = refs[:3], refs[3:]
    feature_ref, sums_ref, gate_ref, low_charge_ref, full_charge_ref, energy_ref, slope_ref = refs[:7]
    (source_ref,) = refs[7:]
    atoms = frame[0].shape[2]
    for cell in range(9):
        source_ref[:, cell * atoms : (cell + 1) * atoms] = frame[cell // 3][cell % 3]

    def gathered(n):
        hot = hot_columns(neighbour_ref[n : n + 1, :], 9 * atoms)
        feature = dot(source_ref[...], hot)
        feature_ref[:, n * atoms : (n + 1) * atoms] = feature.astype(BF16)
        return feature

    sums = messages(edge_parts(basis_ref, unit_ref), radial_ref, 1, slots, atoms, gathered)
    step, gate = mixed(sums, mixing_ref, 1)
    hidden = frame[1][1].astype(F32) + step
    for part in range(3):
        sums_ref[part] = sums[part + 1]
    gate_ref[...] = gate
    charge = dot3(charge_ref[...].T, hidden)
    full_charge_ref[...] = charge
    for copy in range(low_charge_ref.shape[0]):
        low_charge_ref[copy] = charge.astype(low_charge_ref.dtype)
    value, slope = silu_pair(dot3(hidden_ref[...].T, hidden))
    out = out_ref[...].T
    energy_ref[...] = jnp.sum(value * out, axis=0, keepdims=True)
    slope_ref[...] = dot3(hidden_ref[...], slope * out)


def message_grads(cotangent, gate_ref, sums_ref, mixing_ref, layer, slots):
    pre = cotangent * gate_ref[...]
    norm = 1.0 / math.sqrt(slots)
    scalar = dot3(mixing_ref[layer, 0], pre) * norm
    squares = dot3(mixing_ref[layer, 1], pre) * (2.0 * norm)
    return [scalar] + [squares * sums_ref[i] for i in range(3)]


def radial_left(radial_ref, layer, path):
    high, low = split(radial_ref[layer, path])
    top = jnp.concatenate([high.astype(F32), high.astype(F32)], axis=1)
    end = jnp.concatenate([low.astype(F32), jnp.zeros(low.shape, F32)], axis=1)
    return jnp.concatenate([top, end], axis=0).astype(BF16)


def radial_grad(left, value):
    high, low = split(value)
    both = dot(left, jnp.concatenate([high, low], axis=0))
    half = both.shape[0] // 2
    return both[:half] + both[half:]


def second_back_kernel(slots, scale, grid_x, neighbour_ref, basis_ref, unit_ref, radial_ref,
                       mixing_ref, charge_ref, feature_ref, sums_ref, gate_ref, full_charge_ref,
                       energy_ref, slope_ref, fold_ref, site_ref, long_ref, edge_ref, before_ref,
                       middle_ref, after_ref, term_ref):
    ghosts = [before_ref, middle_ref, after_ref]
    atoms = gate_ref.shape[1]
    total = fold_ref[0]
    for part in range(1, grid_x):
        total = total + fold_ref[part]
    wide = full_charge_ref.shape[0]
    potential = total[:wide]
    long_ref[...] = total[wide:] * (2.0 * scale)
    site_ref[...] = energy_ref[...] + scale * jnp.sum(
        full_charge_ref[...] * potential, axis=0, keepdims=True
    )
    cotangent = slope_ref[...] + dot3(charge_ref[...], potential * (2.0 * scale))
    grads = message_grads(cotangent, gate_ref, sums_ref, mixing_ref, 1, slots)
    left = [stacked_left(radial_ref[1, path]) for path in range(2)]
    back = [radial_left(radial_ref, 1, path) for path in range(2)]
    parts = edge_parts(basis_ref, unit_ref)
    for n in range(slots):
        lanes = slice(n * atoms, (n + 1) * atoms)
        feature = feature_ref[:, lanes].astype(F32)
        term = None
        for part in range(4):
            path = 1 if part else 0
            edge_ref[8 * part : 8 * part + 8, lanes] = radial_grad(back[path], grads[part] * feature)
            weight = dot(left[path], stacked_right(parts[part][:, lanes])) * grads[part]
            term = weight if term is None else term + weight
        high, low = split(term)
        term_ref[:, lanes] = jnp.concatenate([high, low], axis=0)
    ids = flat_row(neighbour_ref[...])
    features = middle_ref.shape[1]
    for cell in range(9):
        hot = hot_columns(ids - cell * atoms, atoms)
        both = dot(term_ref[...], hot, ((1,), (1,)))
        grad = both[:features] + both[features:]
        if cell == CENTRE:
            grad = grad + cotangent
        ghosts[cell // 3][cell % 3] = grad.astype(ghosts[cell // 3].dtype)


def first_back_kernel(slots, neighbour_ref, basis_ref, slope_ref, unit_ref, embed_ref, radial_ref,
                      mixing_ref, sums_ref, gate_ref, edge_ref, long_ref, middle_ref, *refs):
    from_x, from_y, outs = refs[:2], refs[2:4], refs[4:]
    atoms = gate_ref.shape[1]
    cotangent = middle_ref[1]
    for block in (from_x[0][1], from_x[1][1], from_y[0][...], from_y[1][...]):
        cotangent = cotangent + block.astype(F32)
    grads = message_grads(cotangent, gate_ref, sums_ref, mixing_ref, 0, slots)
    back = [radial_left(radial_ref, 0, path) for path in range(2)]
    stack = embedding_stack(embed_ref[...])
    unit = unit_ref[...]
    kinds = unit[4:5]
    edges = [[] for _ in range(4)]
    for n in range(slots):
        lanes = slice(n * atoms, (n + 1) * atoms)
        feature = embedded(stack, kinds[:, lanes])
        for part in range(4):
            edges[part].append(radial_grad(back[1 if part else 0], grads[part] * feature))
    edges = [
        edge_ref[8 * part : 8 * part + 8] + jnp.concatenate(edges[part], axis=1) for part in range(4)
    ]
    basis = basis_ref[...]
    units = [unit[i : i + 1] for i in range(3)]
    inverse = unit[3:4]
    by_basis = edges[0]
    for i in range(3):
        by_basis = by_basis + edges[i + 1] * units[i]
    by_unit = [jnp.sum(edges[i + 1] * basis, axis=0, keepdims=True) * inverse for i in range(3)]
    by_distance = jnp.sum(by_basis * slope_ref[...], axis=0, keepdims=True)
    for i in range(3):
        by_distance = by_distance - by_unit[i] * units[i]
    moves = [by_unit[i] + by_distance * units[i] for i in range(3)]
    zero = jnp.zeros_like(moves[0])
    move = jnp.concatenate(moves + [zero] * 5, axis=0)
    own = long_ref[...]
    for n in range(slots):
        own = own - move[:, n * atoms : (n + 1) * atoms]
    ids = flat_row(neighbour_ref[...])
    lane_hot = hot_columns(ids & 127, 128)
    half = ids >> 7
    high = move.astype(BF16).astype(F32)
    both = jnp.concatenate([high, move - high], axis=0)
    per_cell = atoms // 128
    rows = jnp.concatenate(
        [jnp.where(half == h, both, 0.0).astype(BF16) for h in range(9 * per_cell)], axis=0
    )
    spread = dot(rows, lane_hot, ((1,), (1,)))
    for cell in range(9):
        found = []
        for h in range(cell * per_cell, (cell + 1) * per_cell):
            found.append(spread[16 * h : 16 * h + 8] + spread[16 * h + 8 : 16 * h + 16])
        grad = jnp.concatenate(found, axis=1)
        if cell == CENTRE:
            grad = own + grad
        outs[cell // 3][cell % 3] = grad


def pair_tables(parts):
    reach = WAVE_REACH
    pairs = [(0, y) for y in range(1, reach + 1)]
    pairs += [(x, y) for x in range(1, reach + 1) for y in range(-reach, reach + 1)]
    share = -(-len(pairs) // parts)
    padded = -(-share // 8) * 8
    side = 2 * reach + 1
    pair_rows = np.zeros((parts, padded, 8), np.float32)
    wave_rows = np.zeros((parts, 2 * 8 * share + padded, 8), np.float32)
    for part in range(parts):
        for slot, (x, y) in enumerate(pairs[part * share : (part + 1) * share]):
            pair_rows[part, slot, :2] = (x, y)
            rows = [(8 * slot + z - 1, z) for z in range(1, 9)]
            rows += [(8 * share + 8 * slot + z - 1, -z) for z in range(1, 9)]
            rows += [(16 * share + slot, 0)]
            for row, z in rows:
                code = ((x + reach) * side + y + reach) * side + z + reach
                wave_rows[part, row, :5] = (x, y, z, code, 1.0)
    return share, padded, pair_rows, wave_rows


def green_weights(grid, wave_ref, vec_ref, weight_ref):
    grid_x, grid_y = grid
    turn = 2.0 * math.pi
    side = 2 * WAVE_REACH + 1
    top = side * side * side - 1
    vec = vec_ref[...].astype(F32) + WAVE_REACH
    code = (vec[0:1] * side + vec[1:2]) * side + vec[2:3]
    code = jnp.maximum(code, top - code)
    wave = wave_ref[...]
    own = wave[:, 3:4]
    seen = jnp.zeros((own.shape[0], 128), F32)
    for start in range(0, code.shape[1], 128):
        seen = seen + jnp.where(own == code[:, start : start + 128], 1.0, 0.0)
    count = jnp.sum(seen, axis=1, keepdims=True) * wave[:, 4:5]
    sq = (
        (wave[:, 0:1] * (turn / (grid_x * cell_width))) ** 2
        + (wave[:, 1:2] * (turn / (grid_y * cell_width))) ** 2
        + (wave[:, 2:3] * (turn / box_height)) ** 2
    )
    green = jnp.exp(-smear_width * sq) / (sq + screen * screen) * count
    weight_ref[...] = jnp.broadcast_to(green, weight_ref.shape)


def table_kernel(grid, place_ref, pair_ref, all_ref, ca_ref, sa_ref, cb_ref, sb_ref):
    grid_x, grid_y = grid
    turn = 2.0 * math.pi
    col = place_ref[1].astype(F32) * (1.0 / grid_y)
    kx = pair_ref[:, 0:1]
    ky = pair_ref[:, 1:2]
    kz = (lax.broadcasted_iota(jnp.int32, (8, 1), 0) + 1).astype(F32)
    atoms = ca_ref.shape[1] // grid_x
    for d in range(grid_x):
        block = unfold_block(all_ref[d, place_ref[1]], atoms)
        lanes = pl.ds(d * atoms, atoms)
        x = block[0:1] * (1.0 / (grid_x * cell_width)) + d / grid_x
        y = block[1:2] * (1.0 / (grid_y * cell_width)) + col
        z = block[2:3] * (1.0 / box_height)
        alpha = kx * x + ky * y
        alpha = (alpha - jnp.round(alpha)) * turn
        beta = kz * z
        beta = (beta - jnp.round(beta)) * turn
        ca_ref[:, lanes] = jnp.cos(alpha)
        sa_ref[:, lanes] = jnp.sin(alpha)
        cb_ref[:, lanes] = jnp.cos(beta)
        sb_ref[:, lanes] = jnp.sin(beta)


def basis_rows(share, ca, sa, cb, sb):
    cc, ss, sc, cs = [], [], [], []
    for p in range(share):
        c, s = ca[p : p + 1], sa[p : p + 1]
        cc.append(c * cb)
        ss.append(s * sb)
        sc.append(s * cb)
        cs.append(c * sb)
    return cc, ss, sc, cs


def unpack_rows(block):
    half = block.shape[1] // 2
    return jnp.concatenate([block[:, :half], block[:, half:]], axis=0)


def pack_rows(block):
    half = block.shape[0] // 2
    return jnp.concatenate([block[:half], block[half:]], axis=1)


def structure_kernel(share, grid_x, ca_ref, sa_ref, cb_ref, sb_ref, blocks, out_ref):
    total = None
    for d in range(grid_x):
        charge = blocks[d]
        atoms = charge.shape[1]
        lanes = pl.ds(d * atoms, atoms)
        ca, sa, cb, sb = ca_ref[:, lanes], sa_ref[:, lanes], cb_ref[:, lanes], sb_ref[:, lanes]
        cc, ss, sc, cs = basis_rows(share, ca, sa, cb, sb)
        high, low = split(jnp.concatenate(cc + ss + sc + cs + [ca, sa], axis=0))
        term = dot(high, charge, ((1,), (1,))) + dot(low, charge, ((1,), (1,)))
        total = term if total is None else total + term
    packed = pack_rows(total).astype(out_ref.dtype)
    for copy in range(out_ref.shape[0]):
        out_ref[copy] = packed


def fold_kernel(share, padded, grid, ca_ref, sa_ref, cb_ref, sb_ref, weight_ref, pair_ref, blocks,
                parts, outs):
    grid_x, grid_y = grid
    turn = 2.0 * math.pi
    packed = parts[0].astype(F32)
    for part in range(1, grid_y):
        packed = packed + parts[part].astype(F32)
    struct = unpack_rows(packed)
    wide = struct.shape[1]
    span = 8 * share
    cc, ss, sc, cs = (struct[i * span : (i + 1) * span] for i in range(4))
    weight = weight_ref[:, :wide]
    plus, minus, flat = weight[:span], weight[span : 2 * span], weight[2 * span :]
    re_plus, im_plus = plus * (cc - ss), plus * (sc + cs)
    re_minus, im_minus = minus * (cc + ss), minus * (sc - cs)
    rows = jnp.concatenate(
        [
            re_plus + re_minus,
            re_minus - re_plus,
            im_plus + im_minus,
            im_plus - im_minus,
            flat * struct[4 * span : 4 * span + padded],
            flat * struct[4 * span + padded :],
        ],
        axis=0,
    )
    row_high, row_low = split(rows)
    row_pair = jnp.concatenate([row_high, row_low], axis=1)
    turned = rows.T
    t_high, t_low = split(turned)
    t_both = jnp.concatenate([t_high, t_low], axis=0)
    kx = pair_ref[:, 0:1] * (turn / (grid_x * cell_width))
    ky = pair_ref[:, 1:2] * (turn / (grid_y * cell_width))
    kz = (lax.broadcasted_iota(jnp.int32, (8, 1), 0) + 1).astype(jnp.float32) * (turn / box_height)
    for d in range(grid_x):
        charge = blocks[d]
        atoms = charge.shape[1]
        lanes = pl.ds(d * atoms, atoms)
        ca, sa, cb, sb = ca_ref[:, lanes], sa_ref[:, lanes], cb_ref[:, lanes], sb_ref[:, lanes]
        bcc, bss, bsc, bcs = basis_rows(share, ca, sa, cb, sb)
        high, low = split(jnp.concatenate(bcc + bss + bsc + bcs + [ca, sa], axis=0))
        both = dot(t_both, high)
        pot = both[:wide] + both[wide:] + dot(t_high, low)
        proj = dot(row_pair, jnp.concatenate([charge, charge], axis=0))
        by_x = jnp.zeros((8, atoms), jnp.float32)
        by_y = jnp.zeros((8, atoms), jnp.float32)
        by_z = jnp.zeros((8, atoms), jnp.float32)
        for p in range(share):
            pcc, pss, psc, pcs = (
                proj[i * span + 8 * p : i * span + 8 * p + 8] for i in range(4)
            )
            slope = bcs[p] * pss - bsc[p] * pcc + bcc[p] * psc - bss[p] * pcs
            by_x = by_x + kx[p : p + 1] * slope
            by_y = by_y + ky[p : p + 1] * slope
            by_z = by_z + (bsc[p] * pss - bcs[p] * pcc - bss[p] * psc + bcc[p] * pcs)
        flat_slope = ca * proj[4 * span + padded :] - sa * proj[4 * span : 4 * span + padded]
        grad_x = jnp.sum(by_x, axis=0, keepdims=True) + jnp.sum(kx * flat_slope, axis=0, keepdims=True)
        grad_y = jnp.sum(by_y, axis=0, keepdims=True) + jnp.sum(ky * flat_slope, axis=0, keepdims=True)
        grad_z = jnp.sum(kz * by_z, axis=0, keepdims=True)
        zero = jnp.zeros((5, atoms), jnp.float32)
        outs[d] = jnp.concatenate([pot, grad_x, grad_y, grad_z, zero], axis=0)


def per_device(
    positions,
    species,
    neighbours,
    counts,
    species_embed,
    radial,
    mixing,
    read_hidden,
    read_out,
    charge_map,
    wavevectors,
):
    atoms = positions.shape[3]
    slots = neighbours.shape[3]
    features, lat_width = charge_map.shape
    wave_count = wavevectors.shape[1]
    grid = lax.axis_size("gx"), lax.axis_size("gy")
    grid_x, grid_y = grid
    edges = slots * atoms
    scale = 1.0 / math.sqrt(wave_count * lat_width * atoms * grid_x * grid_y)
    place = jnp.stack([lax.axis_index("gx"), lax.axis_index("gy")]).astype(jnp.int32)
    share, padded, pair_np, wave_np = pair_tables(grid_x)
    pair_rows = lax.dynamic_index_in_dim(jnp.asarray(pair_np), place[0], 0, keepdims=False)
    wave_rows = lax.dynamic_index_in_dim(jnp.asarray(wave_np), place[0], 0, keepdims=False)
    cell_rows = 4 * atoms // 128

    (own,) = run(pack_kernel, [shape(grid_y, cell_rows, 128)], [positions, species], name="pack")
    column = exchanged(own, "gy")
    everywhere = exchanged(jnp.broadcast_to(column[None], (grid_x,) + column.shape), "gx")

    ids, embed, radial, mixing, read_hidden, charge_map, weight = run(
        functools.partial(prep_kernel, grid),
        [
            shape(slots, atoms, dtype=jnp.int32),
            shape(8, features),
            shape(*radial.shape),
            shape(*mixing.shape),
            shape(*read_hidden.shape),
            shape(*charge_map.shape),
            shape(wave_np.shape[1], 128),
        ],
        [neighbours, species_embed, radial, mixing, read_hidden, charge_map, wave_rows,
         wavevectors],
        name="prep",
    )
    low, basis, slope, unit, sums_one, gate_one = run(
        functools.partial(first_kernel, slots, grid),
        [
            shape(features, atoms, dtype=BF16),
            shape(8, edges),
            shape(8, edges),
            shape(8, edges),
            shape(3, features, atoms),
            shape(features, atoms),
        ],
        [place, ids, counts[0], embed, radial, mixing, everywhere],
        smem=1,
        name="first",
    )
    hidden = around(low)

    span = grid_x * atoms
    phases = run(
        functools.partial(table_kernel, grid),
        [shape(padded, span), shape(padded, span), shape(8, span), shape(8, span)],
        [place, pair_rows, everywhere],
        smem=1,
        name="tables",
    )
    feature, sums_two, gate_two, low_charge, charge, energy, energy_slope = run(
        functools.partial(second_kernel, slots),
        [
            shape(features, edges, dtype=BF16),
            shape(3, features, atoms),
            shape(features, atoms),
            shape(grid_x, lat_width, atoms, dtype=BF16),
            shape(lat_width, atoms),
            shape(1, atoms),
            shape(features, atoms),
        ],
        [ids, basis, unit, radial, mixing, read_hidden, read_out[None, :], charge_map] + hidden,
        scratch=[pltpu.VMEM((features, 9 * atoms), BF16)],
        name="second",
    )
    charges = exchanged(low_charge, "gx")
    rows = 32 * share + 2 * padded
    (part,) = run(
        functools.partial(structure_kernel, share, grid_x),
        [shape(grid_y, rows // 2, 2 * lat_width)],
        list(phases) + [charges],
        name="structure",
    )
    parts = exchanged(part, "gy")
    (folds,) = run(
        functools.partial(fold_kernel, share, padded, grid),
        [shape(grid_x, lat_width + 8, atoms)],
        list(phases) + [weight, pair_rows, charges, parts],
        name="fold",
    )
    folds = exchanged(folds, "gx")

    site, long, edge, before, middle, after = run(
        functools.partial(second_back_kernel, slots, scale, grid_x),
        [
            shape(1, atoms),
            shape(8, atoms),
            shape(32, edges),
            shape(3, features, atoms, dtype=BF16),
            shape(3, features, atoms),
            shape(3, features, atoms, dtype=BF16),
        ],
        [ids, basis, unit, radial, mixing, charge_map, feature, sums_two, gate_two, charge, energy,
         energy_slope, folds],
        scratch=[pltpu.VMEM((2 * features, edges), BF16)],
        name="second_back",
    )
    from_x = [shifted(after, -1, 0), shifted(before, 1, 0)]
    sides = [
        (middle[b] + from_x[0][b].astype(F32) + from_x[1][b].astype(F32)).astype(BF16)
        for b in (0, 2)
    ]
    from_y = [shifted(sides[1], 0, -1), shifted(sides[0], 0, 1)]
    before, middle, after = run(
        functools.partial(first_back_kernel, slots),
        [shape(3, 8, atoms)] * 3,
        [ids, basis, slope, unit, embed, radial, mixing, sums_one, gate_one, edge, long, middle]
        + from_x + from_y,
        name="first_back",
    )
    total = middle + shifted(after, -1, 0) + shifted(before, 1, 0)
    total = total[1] + shifted(total[2], 0, -1) + shifted(total[0], 0, 1)
    return (-total[None, None, :3], site[None])


def solution(mesh):
    in_specs = (
        P("gx", "gy", None, None),
        P("gx", "gy", None),
        P("gx", "gy", None, None),
        P("gx", "gy", None),
        P(),
        P(),
        P(),
        P(),
        P(),
        P(),
        P(),
    )
    out_specs = (P("gx", "gy", None, None), P("gx", "gy", None))
    return jax.shard_map(
        per_device, mesh=mesh, in_specs=in_specs, out_specs=out_specs, check_vma=False
    )
```

```python
import functools
import math

import jax
import jax.numpy as jnp
import numpy as np
from jax import lax
from jax.experimental import pallas as pl
from jax.experimental.pallas import tpu as pltpu
from jax.sharding import PartitionSpec as P

cell_width = 10.0
box_height = 30.0
cut_radius = 50.0
soften = 0.25
screen = 0.5
smear_width = 0.5
WAVE_REACH = 8
F32 = jnp.float32
BF16 = jnp.bfloat16
OFFSETS = [(a, b) for a in (-1, 0, 1) for b in (-1, 0, 1)]
CENTRE = 4


def shifted(block, along_x, along_y):
    count_x, count_y = lax.axis_size("gx"), lax.axis_size("gy")
    route = []
    for i in range(count_x):
        for j in range(count_y):
            source = ((i + along_x) % count_x) * count_y + (j + along_y) % count_y
            route.append((source, i * count_y + j))
    return lax.ppermute(block, ("gx", "gy"), route)


def around(block):
    column = jnp.stack([shifted(block, 0, -1), block, shifted(block, 0, 1)])
    return [shifted(column, -1, 0), column, shifted(column, 1, 0)]


def whole(space=pltpu.VMEM):
    return pl.BlockSpec(memory_space=space)


def run(kernel, outs, args, scratch=(), smem=0, hbm=0, flops=10_000_000, name=None):
    specs = [whole(pltpu.SMEM)] * smem + [whole(pl.ANY)] * hbm
    specs += [whole()] * (len(args) - smem - hbm)
    return list(
        pl.pallas_call(
            kernel,
            out_shape=outs,
            in_specs=specs,
            out_specs=[whole() for _ in outs],
            scratch_shapes=list(scratch),
            compiler_params=pltpu.CompilerParams(vmem_limit_bytes=32 * 1024 * 1024),
            cost_estimate=pl.CostEstimate(
                flops=flops, bytes_accessed=1_000_000, transcendentals=0
            ),
            name=name,
        )(*args)
    )


def shape(*dims, dtype=F32):
    return jax.ShapeDtypeStruct(dims, dtype)


def split(value):
    high = value.astype(BF16)
    return high, (value - high.astype(F32)).astype(BF16)


def dot(left, right, contract=((1,), (0,))):
    return lax.dot_general(left, right, (contract, ((), ())), preferred_element_type=F32)


def dot3(left, right):
    left_high, left_low = split(left)
    right_high, right_low = split(right)
    return dot(left_high, right_high) + (dot(left_high, right_low) + dot(left_low, right_high))


def dot_split(left, right):
    right_high, right_low = split(right)
    return dot(left[0], right_high) + (dot(left[0], right_low) + dot(left[1], right_high))


def sin_cos(turns):
    quarter = jnp.round(turns * 4.0)
    x = (turns - quarter * 0.25) * (2.0 * math.pi)
    z = x * x
    sine = ((-1.9515295891e-4 * z + 8.3321608736e-3) * z - 1.6666654611e-1) * (z * x) + x
    cosine = (2.443315711809948e-5 * z - 1.388731625493765e-3) * z + 4.166664568298827e-2
    cosine = cosine * (z * z) - 0.5 * z + 1.0
    k = quarter.astype(jnp.int32) & 3
    odd = (k & 1) == 1
    by_sine = jnp.where(odd, cosine, sine)
    by_cosine = jnp.where(odd, sine, cosine)
    return (
        jnp.where(k >= 2, -by_sine, by_sine),
        jnp.where((k == 1) | (k == 2), -by_cosine, by_cosine),
    )


def stacked_left(value):
    high = value.astype(BF16).astype(F32)
    rows = jnp.concatenate([high, high, value - high, jnp.zeros_like(high)], axis=0)
    return rows.T.astype(BF16)


def stacked_right(value):
    high = value.astype(BF16).astype(F32)
    return jnp.concatenate([high, value - high, high, jnp.zeros_like(high)], axis=0).astype(BF16)


def silu_pair(value):
    gate = 1.0 / (1.0 + jnp.exp(-value))
    return value * gate, gate * (1.0 + value * (1.0 - gate))


def onehot_kinds(kinds, rows):
    levels = lax.broadcasted_iota(jnp.int32, (rows, kinds.shape[1]), 0).astype(F32)
    return jnp.where(kinds == levels, 1.0, 0.0)


def embedding_stack(embed):
    high = embed.astype(BF16).astype(F32)
    rest = embed - high
    middle = rest.astype(BF16).astype(F32)
    rows = jnp.concatenate([high, middle, rest - middle, jnp.zeros_like(high)], axis=0)
    return rows.T.astype(BF16)


def embedded(stack, kinds):
    hot = onehot_kinds(kinds, 8)
    return dot(stack, jnp.concatenate([hot, hot, hot, jnp.zeros_like(hot)], axis=0).astype(BF16))


def weights_of(stack_ref, layer, part, rows):
    return dot(stack_ref[layer, 1 if part else 0], stacked_right(rows))


def mixed(sums, high_ref, low_ref, layer):
    squares = sums[1] * sums[1] + sums[2] * sums[2] + sums[3] * sums[3]
    both = jnp.concatenate([sums[0], squares], axis=0)
    return silu_pair(dot_split((high_ref[layer], low_ref[layer]), both))


def edge_parts(basis, unit):
    return [basis] + [basis * unit[i : i + 1] for i in range(3)]


def pack_kernel(position_ref, species_ref, out_ref, place, kind, sems):
    copies = [
        pltpu.make_async_copy(position_ref, place, sems.at[0]),
        pltpu.make_async_copy(species_ref, kind, sems.at[1]),
    ]
    for copy in copies:
        copy.start()
    for copy in copies:
        copy.wait()
    rows = [place[0, i] for i in range(3)] + [kind[0].astype(F32)]
    atoms = rows[0].shape[1]
    out_ref[...] = jnp.concatenate(
        [row[:, s : s + 128] for s in range(0, atoms, 128) for row in rows], axis=0
    )


def radial_left(radial):
    high = radial.astype(BF16).astype(F32)
    low = radial - high
    top = jnp.concatenate([high, high], axis=1)
    end = jnp.concatenate([low, jnp.zeros_like(low)], axis=1)
    return jnp.concatenate([top, end], axis=0).astype(BF16)


def put_split(value, high_ref, low_ref, *at):
    high, low = split(value)
    high_ref[at] = high
    low_ref[at] = low


def prep_kernel(share, padded, grid, norm, place_ref, *refs):
    sources, outs, scratch = refs[:9], refs[9:25], refs[25:]
    id_ref, count_ref, read_ref = outs[:3]
    (embed_out, left_out, back_out, mix_high, mix_low, turn_high, turn_low, hidden_high, hidden_low,
     hidden_turn_high, hidden_turn_low, charge_pair, weight_ref) = outs[3:]
    embed_ref, radial_ref, mixing_ref, hidden_ref, charge_ref, vec_ref, sems = scratch
    targets = [id_ref, count_ref, read_ref, embed_ref, radial_ref, mixing_ref, hidden_ref,
               charge_ref, vec_ref]
    copies = [
        pltpu.make_async_copy(source, target, sems.at[i])
        for i, (source, target) in enumerate(zip(sources, targets))
    ]
    for copy in copies:
        copy.start()
    for copy in copies:
        copy.wait()
    embed = embed_ref[...]
    embed = jnp.concatenate([embed, jnp.zeros((8 - embed.shape[0], embed.shape[1]), F32)], axis=0)
    embed_out[...] = embedding_stack(embed)
    for layer in range(2):
        for path in range(2):
            radial = radial_ref[layer, path] * norm
            left_out[layer, path] = stacked_left(radial)
            back_out[layer, path] = radial_left(radial)
        scalar, vector = mixing_ref[layer, 0], mixing_ref[layer, 1]
        put_split(jnp.concatenate([scalar.T, vector.T], axis=1), mix_high, mix_low, layer)
        put_split(jnp.concatenate([scalar, 2.0 * vector], axis=0), turn_high, turn_low, layer)
    put_split(hidden_ref[...].T, hidden_high, hidden_low, Ellipsis)
    put_split(hidden_ref[...], hidden_turn_high, hidden_turn_low, Ellipsis)
    charge = charge_ref[...]
    high = charge.astype(BF16).astype(F32)
    charge_pair[0] = high.astype(BF16)
    charge_pair[1] = (charge - high).astype(BF16)
    green_weights(share, padded, grid, place_ref, vec_ref, weight_ref)


def unfold_block(block, atoms):
    parts = atoms // 128
    return jnp.concatenate([block[4 * s : 4 * s + 4] for s in range(parts)], axis=1)


def first_kernel(slots, ids_ref, count_ref, embed_ref, left_ref, mix_high, mix_low, before_ref,
                 column_ref, after_ref, low_ref, basis_ref, slope_ref, unit_ref, sums_ref,
                 gate_ref):
    atoms = low_ref.shape[1]
    ids = ids_ref[...]
    frame = [before_ref, column_ref, after_ref]
    own = unfold_block(column_ref[1], atoms)
    own = jnp.concatenate([own, jnp.zeros_like(own)], axis=0)
    halves = []
    for a, b in OFFSETS:
        block = frame[a + 1][b + 1]
        for s in range(atoms // 128):
            rows = block[4 * s : 4 * s + 4]
            halves.append(
                jnp.concatenate(
                    [rows[0:1] + a * cell_width, rows[1:2] + b * cell_width, rows[2:4], rows],
                    axis=0,
                )
            )
    pieces = []
    for start in range(0, ids.shape[1], 128):
        part = jnp.broadcast_to(ids[:, start : start + 128], (8, 128))
        lane, half = part & 127, part >> 7
        found = jnp.zeros((8, 128), F32)
        for h, rows in enumerate(halves):
            found = jnp.where(half == h, jnp.take_along_axis(rows, lane, axis=1), found)
        pieces.append(found)
    found = jnp.concatenate(pieces, axis=1)
    relative = found - jnp.concatenate([own] * slots, axis=1)
    rel = [relative[i : i + 1] for i in range(3)]
    distance = jnp.sqrt(rel[0] * rel[0] + rel[1] * rel[1] + rel[2] * rel[2] + soften)
    inverse = 1.0 / distance
    order = (lax.broadcasted_iota(jnp.int32, (8, 1), 0) + 1).astype(F32)
    sine, cosine = sin_cos((order * (0.5 / cut_radius)) * distance)
    wave = sine / ((order * (math.pi / cut_radius)) * distance)
    count = count_ref[0]
    live = jnp.concatenate([jnp.where(count > n, 1.0, 0.0) for n in range(slots)], axis=1)
    basis = wave * live
    basis_ref[...] = basis
    slope_ref[...] = (cosine - wave) * (inverse * live)
    kinds = found[3:4]
    unit = jnp.concatenate(
        [r * inverse for r in rel] + [inverse, kinds] + [jnp.zeros_like(kinds)] * 3, axis=0
    )
    unit_ref[...] = unit
    stack = embed_ref[...]
    parts = edge_parts(basis, unit)
    sums = [None] * 4
    for n in range(slots):
        lanes = slice(n * atoms, (n + 1) * atoms)
        feature = embedded(stack, kinds[:, lanes])
        for part in range(4):
            term = weights_of(left_ref, 0, part, parts[part][:, lanes]) * feature
            sums[part] = term if sums[part] is None else sums[part] + term
    step, gate = mixed(sums, mix_high, mix_low, 0)
    low_ref[...] = (embedded(stack, own[3:4]) + step).astype(BF16)
    for part in range(3):
        sums_ref[part] = sums[part + 1]
    gate_ref[...] = gate


def hot_columns(ids, rows):
    place = lax.broadcasted_iota(jnp.int32, (rows, ids.shape[1]), 0)
    return jnp.where(ids == place, 1.0, 0.0).astype(BF16)


def second_near_kernel(slots, ids_ref, basis_ref, unit_ref, left_ref, column_ref, weight_ref,
                       near_ref):
    atoms = column_ref.shape[2]
    parts = edge_parts(basis_ref[...], unit_ref[...])
    source = jnp.concatenate([column_ref[b] for b in range(3)], axis=1)
    for n in range(slots):
        lanes = slice(n * atoms, (n + 1) * atoms)
        for part in range(4):
            weight_ref[part, :, lanes] = weights_of(left_ref, 1, part, parts[part][:, lanes])
        hot = hot_columns(ids_ref[:, lanes] - 3 * atoms, 3 * atoms)
        near_ref[:, lanes] = dot(source, hot)


def second_kernel(slots, ids_ref, weight_ref, near_ref, mix_high, mix_low, hidden_high, hidden_low,
                  turn_high, turn_low, out_ref, charge_ref, cell_ref, before_ref, column_ref,
                  after_ref, feature_ref, sums_ref, gate_ref, packed_ref, full_charge_ref,
                  energy_ref, slope_ref):
    atoms = column_ref.shape[2]
    source = jnp.concatenate(
        [before_ref[b] for b in range(3)] + [after_ref[b] for b in range(3)], axis=1
    )
    sums = [None] * 4
    for n in range(slots):
        lanes = slice(n * atoms, (n + 1) * atoms)
        ids = ids_ref[:, lanes]
        ids = jnp.where(ids >= 6 * atoms, ids - 3 * atoms, jnp.where(ids >= 3 * atoms, -1, ids))
        feature = near_ref[:, lanes] + dot(source, hot_columns(ids, 6 * atoms))
        feature_ref[:, lanes] = feature.astype(BF16)
        for part in range(4):
            term = weight_ref[part, :, lanes] * feature
            sums[part] = term if sums[part] is None else sums[part] + term
    step, gate = mixed(sums, mix_high, mix_low, 1)
    hidden = column_ref[1].astype(F32) + step
    for part in range(3):
        sums_ref[part] = sums[part + 1]
    gate_ref[...] = gate
    charge = dot_split((charge_ref[0], charge_ref[1]), hidden)
    full_charge_ref[...] = charge
    place = unfold_block(cell_ref[1], atoms)[:3]
    high = place.astype(BF16).astype(F32)
    rest = place - high
    middle = rest.astype(BF16).astype(F32)
    zero = jnp.zeros((packed_ref.shape[0] - charge.shape[0] - 9, atoms), F32)
    packed_ref[...] = jnp.concatenate([charge, high, middle, rest - middle, zero], axis=0).astype(
        BF16
    )
    value, slope = silu_pair(dot_split((hidden_high[...], hidden_low[...]), hidden))
    out = out_ref[...].T
    energy_ref[...] = jnp.sum(value * out, axis=0, keepdims=True)
    slope_ref[...] = dot_split((turn_high[...], turn_low[...]), slope * out)


def message_grads(cotangent, gate_ref, sums_ref, high_ref, low_ref, layer):
    pre = cotangent * gate_ref[...]
    both = dot_split((high_ref[layer], low_ref[layer]), pre)
    half = both.shape[0] // 2
    return [both[:half]] + [both[half:] * sums_ref[i] for i in range(3)]


def radial_grad(left, value):
    high, low = split(value)
    both = dot(left, jnp.concatenate([high, low], axis=0))
    half = both.shape[0] // 2
    return both[:half] + both[half:]


def second_back_kernel(slots, scale, grid_x, ids_ref, weight_ref, turn_high, turn_low, charge_ref,
                       sums_ref, gate_ref, full_charge_ref, energy_ref, slope_ref, *refs):
    folds, refs = refs[:grid_x], refs[grid_x:]
    site_ref, long_ref, cotangent_ref, grad_ref, term_ref, before_ref, after_ref = refs
    atoms = gate_ref.shape[1]
    total = folds[0][...].astype(F32)
    for part in folds[1:]:
        total = total + part[...].astype(F32)
    wide = full_charge_ref.shape[0]
    potential = total[:wide] * (2.0 * scale)
    slopes = total[wide : wide + 3] + total[wide + 3 : wide + 6] + total[wide + 6 : wide + 9]
    long_ref[...] = jnp.concatenate(
        [slopes * (2.0 * scale), jnp.zeros((5, atoms), F32)], axis=0
    )
    site_ref[0] = energy_ref[...] + 0.5 * jnp.sum(
        full_charge_ref[...] * potential, axis=0, keepdims=True
    )
    high, low = split(potential)
    turned = ((0,), (0,))
    cotangent = slope_ref[...] + (
        dot(charge_ref[0], high, turned)
        + (dot(charge_ref[0], low, turned) + dot(charge_ref[1], high, turned))
    )
    cotangent_ref[...] = cotangent
    grads = message_grads(cotangent, gate_ref, sums_ref, turn_high, turn_low, 1)
    for part in range(4):
        grad_ref[part] = grads[part]
    for n in range(slots):
        lanes = slice(n * atoms, (n + 1) * atoms)
        term = weight_ref[0, :, lanes] * grads[0]
        for part in range(1, 4):
            term = term + weight_ref[part, :, lanes] * grads[part]
        term_ref[:, lanes] = term.astype(BF16)
    ids = ids_ref[...]
    for side, out_ref in ((0, before_ref), (2, after_ref)):
        for b in range(3):
            hot = hot_columns(ids - (3 * side + b) * atoms, atoms)
            out_ref[b] = dot(term_ref[...], hot, ((1,), (1,))).astype(BF16)


def second_middle_kernel(ids_ref, term_ref, cotangent_ref, middle_ref):
    ids = ids_ref[...]
    atoms = cotangent_ref.shape[1]
    for b in range(3):
        hot = hot_columns(ids - (3 + b) * atoms, atoms)
        grad = dot(term_ref[...], hot, ((1,), (1,)))
        middle_ref[b] = grad + cotangent_ref[...] if b == 1 else grad


def second_edge_kernel(slots, back_ref, feature_ref, grad_ref, edge_ref):
    atoms = grad_ref.shape[2]
    for n in range(slots):
        lanes = slice(n * atoms, (n + 1) * atoms)
        feature = feature_ref[:, lanes].astype(F32)
        for part in range(4):
            edge_ref[8 * part : 8 * part + 8, lanes] = radial_grad(
                back_ref[1, 1 if part else 0], grad_ref[part] * feature
            )


def first_back_kernel(slots, ids_ref, basis_ref, slope_ref, unit_ref, embed_ref, back_ref,
                      turn_high, turn_low, sums_ref, gate_ref, edge_ref, long_ref, middle_ref,
                      *refs):
    from_x, from_y, outs = refs[:2], refs[2:4], refs[4:]
    atoms = gate_ref.shape[1]
    cotangent = middle_ref[1]
    for block in (from_x[0][1], from_x[1][1], from_y[0][...], from_y[1][...]):
        cotangent = cotangent + block.astype(F32)
    grads = message_grads(cotangent, gate_ref, sums_ref, turn_high, turn_low, 0)
    stack = embed_ref[...]
    unit = unit_ref[...]
    kinds = unit[4:5]
    edges = [[] for _ in range(4)]
    for n in range(slots):
        lanes = slice(n * atoms, (n + 1) * atoms)
        feature = embedded(stack, kinds[:, lanes])
        for part in range(4):
            edges[part].append(radial_grad(back_ref[0, 1 if part else 0], grads[part] * feature))
    edges = [
        edge_ref[8 * part : 8 * part + 8] + jnp.concatenate(edges[part], axis=1) for part in range(4)
    ]
    basis = basis_ref[...]
    units = [unit[i : i + 1] for i in range(3)]
    inverse = unit[3:4]
    by_basis = edges[0]
    for i in range(3):
        by_basis = by_basis + edges[i + 1] * units[i]
    by_unit = [jnp.sum(edges[i + 1] * basis, axis=0, keepdims=True) * inverse for i in range(3)]
    by_distance = jnp.sum(by_basis * slope_ref[...], axis=0, keepdims=True)
    for i in range(3):
        by_distance = by_distance - by_unit[i] * units[i]
    moves = [by_unit[i] + by_distance * units[i] for i in range(3)]
    zero = jnp.zeros_like(moves[0])
    move = jnp.concatenate(moves + [zero] * 5, axis=0)
    own = long_ref[...]
    for n in range(slots):
        own = own - move[:, n * atoms : (n + 1) * atoms]
    ids = ids_ref[...]
    lane_hot = hot_columns(ids & 127, 128)
    half = ids >> 7
    high = move.astype(BF16).astype(F32)
    both = jnp.concatenate([high, move - high], axis=0)
    per_cell = atoms // 128
    rows = jnp.concatenate(
        [jnp.where(half == h, both, 0.0).astype(BF16) for h in range(9 * per_cell)], axis=0
    )
    spread = dot(rows, lane_hot, ((1,), (1,)))
    for cell in range(9):
        found = []
        for h in range(cell * per_cell, (cell + 1) * per_cell):
            found.append(spread[16 * h : 16 * h + 8] + spread[16 * h + 8 : 16 * h + 16])
        grad = jnp.concatenate(found, axis=1)
        if cell == CENTRE:
            grad = own + grad
        outs[cell // 3][cell % 3] = grad


def pair_counts(parts):
    total = WAVE_REACH + WAVE_REACH * (2 * WAVE_REACH + 1)
    share = -(-total // parts)
    return total, share, -(-share // 16) * 16


def pair_vectors(slot, share, part):
    side = 2 * WAVE_REACH + 1
    total = WAVE_REACH + WAVE_REACH * side
    index = slot + part.astype(F32) * share
    later = index - WAVE_REACH
    row = jnp.floor((later + 0.5) * (1.0 / side))
    first = index < WAVE_REACH
    kx = jnp.where(first, 0.0, row + 1.0)
    ky = jnp.where(first, index + 1.0, later - row * side - WAVE_REACH)
    valid = jnp.where((slot < share) & (index < total), 1.0, 0.0)
    return kx, ky, valid


def count_up(rows):
    return lax.broadcasted_iota(jnp.int32, (rows, 1), 0).astype(F32)


def green_weights(share, padded, grid, place_ref, vec_ref, weight_ref):
    grid_x, grid_y = grid
    turn = 2.0 * math.pi
    side = 2 * WAVE_REACH + 1
    top = side * side * side - 1
    vec = vec_ref[...].astype(F32) + WAVE_REACH
    code = (vec[0:1] * side + vec[1:2]) * side + vec[2:3]
    code = jnp.maximum(code, top - code)
    span = 8 * share
    row = count_up(span)
    slot = jnp.floor(row * 0.125)
    height = row - 8.0 * slot + 1.0
    flat = count_up(padded)
    slot = jnp.concatenate([slot, slot, flat], axis=0)
    kz = jnp.concatenate([height, -height, jnp.zeros_like(flat)], axis=0)
    kx, ky, valid = pair_vectors(slot, share, place_ref[0])
    own = ((kx + WAVE_REACH) * side + ky + WAVE_REACH) * side + kz + WAVE_REACH
    seen = jnp.zeros((own.shape[0], 128), F32)
    for start in range(0, code.shape[1], 128):
        seen = seen + jnp.where(own == code[:, start : start + 128], 1.0, 0.0)
    count = jnp.sum(seen, axis=1, keepdims=True) * valid
    sq = (
        (kx * (turn / (grid_x * cell_width))) ** 2
        + (ky * (turn / (grid_y * cell_width))) ** 2
        + (kz * (turn / box_height)) ** 2
    )
    green = jnp.exp(-smear_width * sq) / (sq + screen * screen) * count
    weight_ref[...] = jnp.broadcast_to(green, weight_ref.shape)


def basis_rows(share, ca, sa, cb, sb):
    cc, ss, sc, cs = [], [], [], []
    for p in range(share):
        c, s = ca[p : p + 1], sa[p : p + 1]
        cc.append(c * cb)
        ss.append(s * sb)
        sc.append(s * cb)
        cs.append(c * sb)
    return cc, ss, sc, cs


def unpack_rows(block):
    half = block.shape[1] // 2
    return jnp.concatenate([block[:, :half], block[:, half:]], axis=0)


def pack_rows(block):
    half = block.shape[0] // 2
    return jnp.concatenate([block[:half], block[half:]], axis=1)


def structure_kernel(share, padded, grid, wide, place_ref, *refs):
    grid_x, grid_y = grid
    blocks, (ca_ref, sa_ref, cb_ref, sb_ref, out_ref) = refs[:grid_x], refs[grid_x:]
    col = place_ref[1].astype(F32) * (1.0 / grid_y)
    kx, ky, _ = pair_vectors(count_up(padded), share, place_ref[0])
    kz = count_up(8) + 1.0
    total = None
    for d in range(grid_x):
        block = blocks[d][...]
        charge = block[:wide]
        atoms = charge.shape[1]
        pieces = block[wide:].astype(F32)
        place = pieces[0:3] + (pieces[3:6] + pieces[6:9])
        row = lax.rem(place_ref[0] + d, grid_x).astype(F32) * (1.0 / grid_x)
        x = place[0:1] * (1.0 / (grid_x * cell_width)) + row
        y = place[1:2] * (1.0 / (grid_y * cell_width)) + col
        sa, ca = sin_cos(kx * x + ky * y)
        sb, cb = sin_cos(kz * (place[2:3] * (1.0 / box_height)))
        lanes = pl.ds(d * atoms, atoms)
        ca_ref[:, lanes] = ca
        sa_ref[:, lanes] = sa
        cb_ref[:, lanes] = cb
        sb_ref[:, lanes] = sb
        cc, ss, sc, cs = basis_rows(share, ca, sa, cb, sb)
        high, low = split(jnp.concatenate(cc + ss + sc + cs + [ca, sa], axis=0))
        term = dot(high, charge, ((1,), (1,))) + dot(low, charge, ((1,), (1,)))
        total = term if total is None else total + term
    out_ref[...] = pack_rows(total).astype(BF16)


def fold_kernel(share, padded, grid, wide, place_ref, ca_ref, sa_ref, cb_ref, sb_ref, weight_ref,
                *refs):
    grid_x, grid_y = grid
    blocks, parts, outs = refs[:grid_x], refs[grid_x : grid_x + grid_y], refs[grid_x + grid_y :]
    turn = 2.0 * math.pi
    packed = parts[0][...].astype(F32)
    for part in parts[1:]:
        packed = packed + part[...].astype(F32)
    struct = unpack_rows(packed)
    span = 8 * share
    cc, ss, sc, cs = (struct[i * span : (i + 1) * span] for i in range(4))
    weight = weight_ref[:, :wide]
    plus, minus, flat = weight[:span], weight[span : 2 * span], weight[2 * span :]
    re_plus, im_plus = plus * (cc - ss), plus * (sc + cs)
    re_minus, im_minus = minus * (cc + ss), minus * (sc - cs)
    rows = jnp.concatenate(
        [
            re_plus + re_minus,
            re_minus - re_plus,
            im_plus + im_minus,
            im_plus - im_minus,
            flat * struct[4 * span : 4 * span + padded],
            flat * struct[4 * span + padded :],
        ],
        axis=0,
    )
    row_high, row_low = split(rows)
    row_pair = jnp.concatenate([row_high, row_low], axis=1)
    turned = rows.T
    t_high, t_low = split(turned)
    t_both = jnp.concatenate([t_high, t_low], axis=0)
    kx, ky, _ = pair_vectors(count_up(padded), share, place_ref[0])
    kx = kx * (turn / (grid_x * cell_width))
    ky = ky * (turn / (grid_y * cell_width))
    kz = (count_up(8) + 1.0) * (turn / box_height)
    for d in range(grid_x):
        charge = blocks[d][:wide]
        atoms = charge.shape[1]
        lanes = pl.ds(d * atoms, atoms)
        ca, sa, cb, sb = ca_ref[:, lanes], sa_ref[:, lanes], cb_ref[:, lanes], sb_ref[:, lanes]
        bcc, bss, bsc, bcs = basis_rows(share, ca, sa, cb, sb)
        high, low = split(jnp.concatenate(bcc + bss + bsc + bcs + [ca, sa], axis=0))
        both = dot(t_both, high)
        pot = both[:wide] + both[wide:] + dot(t_high, low)
        proj = dot(row_pair, jnp.concatenate([charge, charge], axis=0))
        by_x = jnp.zeros((8, atoms), jnp.float32)
        by_y = jnp.zeros((8, atoms), jnp.float32)
        by_z = jnp.zeros((8, atoms), jnp.float32)
        for p in range(share):
            pcc, pss, psc, pcs = (
                proj[i * span + 8 * p : i * span + 8 * p + 8] for i in range(4)
            )
            slope = bcs[p] * pss - bsc[p] * pcc + bcc[p] * psc - bss[p] * pcs
            by_x = by_x + kx[p : p + 1] * slope
            by_y = by_y + ky[p : p + 1] * slope
            by_z = by_z + (bsc[p] * pss - bcs[p] * pcc - bss[p] * psc + bcc[p] * pcs)
        flat_slope = ca * proj[4 * span + padded :] - sa * proj[4 * span : 4 * span + padded]
        grad_x = jnp.sum(by_x, axis=0, keepdims=True) + jnp.sum(kx * flat_slope, axis=0, keepdims=True)
        grad_y = jnp.sum(by_y, axis=0, keepdims=True) + jnp.sum(ky * flat_slope, axis=0, keepdims=True)
        grad_z = jnp.sum(kz * by_z, axis=0, keepdims=True)
        slopes = jnp.concatenate([grad_x, grad_y, grad_z], axis=0)
        high = slopes.astype(BF16).astype(F32)
        rest = slopes - high
        middle = rest.astype(BF16).astype(F32)
        zero = jnp.zeros((outs[d].shape[0] - wide - 9, atoms), F32)
        outs[d][...] = jnp.concatenate([pot, high, middle, rest - middle, zero], axis=0).astype(
            BF16
        )


def per_device(
    positions,
    species,
    neighbours,
    counts,
    species_embed,
    radial,
    mixing,
    read_hidden,
    read_out,
    charge_map,
    wavevectors,
):
    atoms = positions.shape[3]
    slots = neighbours.shape[3]
    features, lat_width = charge_map.shape
    wave_count = wavevectors.shape[1]
    grid = lax.axis_size("gx"), lax.axis_size("gy")
    grid_x, grid_y = grid
    edges = slots * atoms
    scale = 1.0 / math.sqrt(wave_count * lat_width * atoms * grid_x * grid_y)
    place = jnp.stack([lax.axis_index("gx"), lax.axis_index("gy")]).astype(jnp.int32)
    _, share, padded = pair_counts(grid_x)
    ids = neighbours.transpose(0, 3, 1, 2).reshape(1, edges)
    dma = pltpu.SemaphoreType.DMA
    shown = positions.transpose(0, 2, 1, 3)

    (own,) = run(
        pack_kernel,
        [shape(4 * atoms // 128, 128)],
        [shown, species],
        scratch=[
            pltpu.VMEM(shown.shape, F32),
            pltpu.VMEM(species.shape, jnp.int32),
            dma((2,)),
        ],
        hbm=2,
        name="pack",
    )
    cells = around(own)

    pair = [shape(features, features, dtype=BF16)] * 2
    (ids, counts, read_out, embed, left, back, mix_high, mix_low, turn_high, turn_low, hidden_high,
     hidden_low, hidden_turn_high, hidden_turn_low, charge_pair, weight) = run(
        functools.partial(prep_kernel, share, padded, grid, 1.0 / math.sqrt(slots)),
        [
            shape(1, edges, dtype=jnp.int32),
            shape(*counts.shape, dtype=jnp.int32),
            shape(1, features),
            shape(features, 32, dtype=BF16),
            shape(2, 2, features, 32, dtype=BF16),
            shape(2, 2, 16, 2 * features, dtype=BF16),
            shape(2, features, 2 * features, dtype=BF16),
            shape(2, features, 2 * features, dtype=BF16),
            shape(2, 2 * features, features, dtype=BF16),
            shape(2, 2 * features, features, dtype=BF16),
        ]
        + pair + pair
        + [
            shape(2, lat_width, features, dtype=BF16),
            shape(16 * share + padded, 128),
        ],
        [place, ids, counts, read_out[None, :], species_embed, radial, mixing, read_hidden,
         charge_map.T, wavevectors],
        scratch=[
            pltpu.VMEM(species_embed.shape, F32),
            pltpu.VMEM(radial.shape, F32),
            pltpu.VMEM(mixing.shape, F32),
            pltpu.VMEM(read_hidden.shape, F32),
            pltpu.VMEM((lat_width, features), F32),
            pltpu.VMEM(wavevectors.shape, jnp.int32),
            dma((9,)),
        ],
        smem=1,
        hbm=9,
        name="prep",
    )
    low, basis, slope, unit, sums_one, gate_one = run(
        functools.partial(first_kernel, slots),
        [
            shape(features, atoms, dtype=BF16),
            shape(8, edges),
            shape(8, edges),
            shape(8, edges),
            shape(3, features, atoms),
            shape(features, atoms),
        ],
        [ids, counts, embed, left, mix_high, mix_low] + cells,
        name="first",
    )
    hidden = around(low)
    edge_weights, near = run(
        functools.partial(second_near_kernel, slots),
        [shape(4, features, edges), shape(features, edges)],
        [ids, basis, unit, left, hidden[1]],
        flops=2_000_000_000,
        name="second_near",
    )
    block_rows = -(-(lat_width + 9) // 16) * 16
    feature, sums_two, gate_two, packed, charge, energy, energy_slope = run(
        functools.partial(second_kernel, slots),
        [
            shape(features, edges, dtype=BF16),
            shape(3, features, atoms),
            shape(features, atoms),
            shape(block_rows, atoms, dtype=BF16),
            shape(lat_width, atoms),
            shape(1, atoms),
            shape(features, atoms),
        ],
        [ids, edge_weights, near, mix_high, mix_low, hidden_high, hidden_low, hidden_turn_high,
         hidden_turn_low, read_out, charge_pair, cells[1]] + hidden,
        name="second",
    )
    charges = [packed] + [shifted(packed, d, 0) for d in range(1, grid_x)]
    span = grid_x * atoms
    rows = 32 * share + 2 * padded
    *phases, part = run(
        functools.partial(structure_kernel, share, padded, grid, lat_width),
        [
            shape(padded, span),
            shape(padded, span),
            shape(8, span),
            shape(8, span),
            shape(rows // 2, 2 * lat_width, dtype=BF16),
        ],
        [place] + charges,
        smem=1,
        name="structure",
    )
    parts = [part] + [shifted(part, 0, d) for d in range(1, grid_y)]
    folds = run(
        functools.partial(fold_kernel, share, padded, grid, lat_width),
        [shape(block_rows, atoms, dtype=BF16)] * grid_x,
        [place] + phases + [weight] + charges + parts,
        smem=1,
        name="fold",
    )
    folds = [folds[0]] + [shifted(folds[d], -d, 0) for d in range(1, grid_x)]

    site, long, cotangent, grads, term, before, after = run(
        functools.partial(second_back_kernel, slots, scale, grid_x),
        [
            shape(1, 1, atoms),
            shape(8, atoms),
            shape(features, atoms),
            shape(4, features, atoms),
            shape(features, edges, dtype=BF16),
            shape(3, features, atoms, dtype=BF16),
            shape(3, features, atoms, dtype=BF16),
        ],
        [ids, edge_weights, turn_high, turn_low, charge_pair, sums_two, gate_two, charge, energy,
         energy_slope] + folds,
        name="second_back",
    )
    from_x = [shifted(after, -1, 0), shifted(before, 1, 0)]
    (middle,) = run(
        second_middle_kernel,
        [shape(3, features, atoms)],
        [ids, term, cotangent],
        flops=1_000_000_000,
        name="second_middle",
    )
    sides = [
        (middle[b] + from_x[0][b].astype(F32) + from_x[1][b].astype(F32)).astype(BF16)
        for b in (0, 2)
    ]
    from_y = [shifted(sides[1], 0, -1), shifted(sides[0], 0, 1)]
    (edge,) = run(
        functools.partial(second_edge_kernel, slots),
        [shape(32, edges)],
        [back, feature, grads],
        flops=1_000_000_000,
        name="second_edge",
    )
    before, middle, after = run(
        functools.partial(first_back_kernel, slots),
        [shape(3, 8, atoms)] * 3,
        [ids, basis, slope, unit, embed, back, turn_high, turn_low, sums_one, gate_one, edge, long,
         middle] + from_x + from_y,
        name="first_back",
    )
    total = middle + shifted(after, -1, 0) + shifted(before, 1, 0)
    total = total[1] + shifted(total[2], 0, -1) + shifted(total[0], 0, 1)
    forces = -total[None, :3, None, :]
    return (forces.transpose(0, 2, 1, 3), site)


def solution(mesh):
    in_specs = (
        P("gx", "gy", None, None),
        P("gx", "gy", None),
        P("gx", "gy", None, None),
        P("gx", "gy", None),
        P(),
        P(),
        P(),
        P(),
        P(),
        P(),
        P(),
    )
    out_specs = (P("gx", "gy", None, None), P("gx", "gy", None))
    return jax.shard_map(
        per_device, mesh=mesh, in_specs=in_specs, out_specs=out_specs, check_vma=False
    )
```

```python
import functools
import math

import jax
import jax.numpy as jnp
import numpy as np
from jax import lax
from jax.experimental import pallas as pl
from jax.experimental.pallas import tpu as pltpu
from jax.sharding import PartitionSpec as P

cell_width = 10.0
box_height = 30.0
cut_radius = 50.0
soften = 0.25
screen = 0.5
smear_width = 0.5
WAVE_REACH = 8
F32 = jnp.float32
BF16 = jnp.bfloat16
OFFSETS = [(a, b) for a in (-1, 0, 1) for b in (-1, 0, 1)]
CENTRE = 4


def shifted(block, along_x, along_y):
    count_x, count_y = lax.axis_size("gx"), lax.axis_size("gy")
    route = []
    for i in range(count_x):
        for j in range(count_y):
            source = ((i + along_x) % count_x) * count_y + (j + along_y) % count_y
            route.append((source, i * count_y + j))
    return lax.ppermute(block, ("gx", "gy"), route)


def around(block, beside):
    column = jnp.stack([shifted(block, 0, -1), block, shifted(block, 0, 1)])
    column, beside = lax.optimization_barrier((column, beside))
    return [shifted(column, -1, 0), column, shifted(column, 1, 0)], beside


def whole(space=pltpu.VMEM):
    return pl.BlockSpec(memory_space=space)


def run(kernel, outs, args, scratch=(), smem=0, hbm=0, flops=10_000_000, grant=16, name=None):
    specs = [whole(pltpu.SMEM)] * smem + [whole(pltpu.HBM)] * hbm
    specs += [whole()] * (len(args) - smem - hbm)
    return list(
        pl.pallas_call(
            kernel,
            out_shape=outs,
            in_specs=specs,
            out_specs=[whole() for _ in outs],
            scratch_shapes=list(scratch),
            compiler_params=pltpu.CompilerParams(vmem_limit_bytes=grant * 1024 * 1024),
            cost_estimate=pl.CostEstimate(
                flops=flops, bytes_accessed=1_000_000, transcendentals=0
            ),
            name=name,
        )(*args)
    )


def shape(*dims, dtype=F32):
    return jax.ShapeDtypeStruct(dims, dtype)


def split(value):
    high = value.astype(BF16)
    return high, (value - high.astype(F32)).astype(BF16)


def dot(left, right, contract=((1,), (0,))):
    return lax.dot_general(left, right, (contract, ((), ())), preferred_element_type=F32)


def dot3(left, right):
    left_high, left_low = split(left)
    right_high, right_low = split(right)
    return dot(left_high, right_high) + (dot(left_high, right_low) + dot(left_low, right_high))


def dot_split(left, right):
    right_high, right_low = split(right)
    return dot(left[0], right_high) + (dot(left[0], right_low) + dot(left[1], right_high))


def sin_cos(turns):
    quarter = jnp.round(turns * 4.0)
    x = (turns - quarter * 0.25) * (2.0 * math.pi)
    z = x * x
    sine = ((-1.9515295891e-4 * z + 8.3321608736e-3) * z - 1.6666654611e-1) * (z * x) + x
    cosine = (2.443315711809948e-5 * z - 1.388731625493765e-3) * z + 4.166664568298827e-2
    cosine = cosine * (z * z) - 0.5 * z + 1.0
    k = quarter.astype(jnp.int32) & 3
    odd = (k & 1) == 1
    by_sine = jnp.where(odd, cosine, sine)
    by_cosine = jnp.where(odd, sine, cosine)
    return (
        jnp.where(k >= 2, -by_sine, by_sine),
        jnp.where((k == 1) | (k == 2), -by_cosine, by_cosine),
    )


def stacked_left(value):
    high = value.astype(BF16).astype(F32)
    rows = jnp.concatenate([high, high, value - high, jnp.zeros_like(high)], axis=0)
    return rows.T.astype(BF16)


def stacked_right(value):
    high = value.astype(BF16).astype(F32)
    return jnp.concatenate([high, value - high, high, jnp.zeros_like(high)], axis=0).astype(BF16)


def silu_pair(value):
    gate = 1.0 / (1.0 + jnp.exp(-value))
    return value * gate, gate * (1.0 + value * (1.0 - gate))


def onehot_kinds(kinds, rows):
    levels = lax.broadcasted_iota(jnp.int32, (rows, kinds.shape[1]), 0).astype(F32)
    return jnp.where(kinds == levels, 1.0, 0.0)


def embedding_stack(embed):
    high = embed.astype(BF16).astype(F32)
    rest = embed - high
    middle = rest.astype(BF16).astype(F32)
    rows = jnp.concatenate([high, middle, rest - middle, jnp.zeros_like(high)], axis=0)
    return rows.T.astype(BF16)


def embedded(stack, kinds):
    hot = onehot_kinds(kinds, 8)
    return dot(stack, jnp.concatenate([hot, hot, hot, jnp.zeros_like(hot)], axis=0).astype(BF16))


def weights_of(stack_ref, part, rows):
    return dot(stack_ref[1 if part else 0], stacked_right(rows))


def mixed(sums, high_ref, low_ref, layer):
    squares = sums[1] * sums[1] + sums[2] * sums[2] + sums[3] * sums[3]
    both = jnp.concatenate([sums[0], squares], axis=0)
    return silu_pair(dot_split((high_ref[layer], low_ref[layer]), both))


def edge_parts(basis, unit):
    return [basis] + [basis * unit[i : i + 1] for i in range(3)]


def pack_kernel(position_ref, species_ref, out_ref, place, kind, sems):
    copies = [
        pltpu.make_async_copy(position_ref, place, sems.at[0]),
        pltpu.make_async_copy(species_ref, kind, sems.at[1]),
    ]
    for copy in copies:
        copy.start()
    for copy in copies:
        copy.wait()
    rows = [place[0, i] for i in range(3)] + [kind[0].astype(F32)]
    atoms = rows[0].shape[1]
    out_ref[...] = jnp.concatenate(
        [row[:, s : s + 128] for s in range(0, atoms, 128) for row in rows], axis=0
    )


def radial_left(radial):
    high = radial.astype(BF16).astype(F32)
    low = radial - high
    top = jnp.concatenate([high, high], axis=1)
    end = jnp.concatenate([low, jnp.zeros_like(low)], axis=1)
    return jnp.concatenate([top, end], axis=0).astype(BF16)


def put_split(value, high_ref, low_ref, *at):
    high, low = split(value)
    high_ref[at] = high
    low_ref[at] = low


def fetch(sources, targets, sems):
    copies = [
        pltpu.make_async_copy(source, target, sems.at[i])
        for i, (source, target) in enumerate(zip(sources, targets))
    ]
    for copy in copies:
        copy.start()
    for copy in copies:
        copy.wait()


def prep_first_kernel(norm, ids_in, count_in, embed_in, radial_in, mixing_in, id_ref, count_ref,
                      embed_out, kind_left, left_out, back_out, kind_high, kind_low, mix_high,
                      mix_low, turn_high, turn_low, embed_ref, radial_ref, mixing_ref, sems):
    fetch(
        [ids_in, count_in, embed_in, radial_in, mixing_in],
        [id_ref, count_ref, embed_ref, radial_ref, mixing_ref],
        sems,
    )
    embed = embed_ref[...]
    kinds = embed.shape[0]
    for path in range(2):
        radial = radial_ref[0, path] * norm
        rows = jnp.concatenate([radial * embed[s : s + 1] for s in range(kinds)], axis=0)
        kind_left[path] = stacked_left(rows)
        put_split(rows, kind_high, kind_low, path)
        radial = radial_ref[1, path] * norm
        left_out[path] = stacked_left(radial)
        back_out[path] = radial_left(radial)
    for layer in range(2):
        scalar, vector = mixing_ref[layer, 0], mixing_ref[layer, 1]
        put_split(jnp.concatenate([scalar.T, vector.T], axis=1), mix_high, mix_low, layer)
        put_split(jnp.concatenate([scalar, 2.0 * vector], axis=0), turn_high, turn_low, layer)
    embed = jnp.concatenate([embed, jnp.zeros((8 - kinds, embed.shape[1]), F32)], axis=0)
    embed_out[...] = embedding_stack(embed)


def prep_second_kernel(read_in, hidden_in, charge_in, read_ref, hidden_high, hidden_low,
                       hidden_turn_high, hidden_turn_low, charge_pair, hidden_ref, charge_ref, sems):
    fetch([read_in, hidden_in, charge_in], [read_ref, hidden_ref, charge_ref], sems)
    put_split(hidden_ref[...].T, hidden_high, hidden_low, Ellipsis)
    put_split(hidden_ref[...], hidden_turn_high, hidden_turn_low, Ellipsis)
    charge = charge_ref[...]
    high = charge.astype(BF16).astype(F32)
    charge_pair[0] = high.astype(BF16)
    charge_pair[1] = (charge - high).astype(BF16)


def hot_kernel(ids_ref, hot_ref):
    edges = ids_ref.shape[1]
    for start in range(0, edges, 256):
        lanes = slice(start, start + 256)
        hot_ref[:, lanes] = hot_columns(ids_ref[:, lanes], hot_ref.shape[0])


def unfold_block(block, atoms):
    parts = atoms // 128
    return jnp.concatenate([block[4 * s : 4 * s + 4] for s in range(parts)], axis=1)


def first_kernel(slots, ids_ref, count_ref, embed_ref, kind_left, mix_high, mix_low, before_ref,
                 column_ref, after_ref, low_ref, basis_ref, slope_ref, unit_ref, sums_ref,
                 gate_ref):
    atoms = low_ref.shape[1]
    ids = ids_ref[...]
    frame = [before_ref, column_ref, after_ref]
    own = unfold_block(column_ref[1], atoms)
    own = jnp.concatenate([own, jnp.zeros_like(own)], axis=0)
    halves = []
    for a, b in OFFSETS:
        block = frame[a + 1][b + 1]
        for s in range(atoms // 128):
            rows = block[4 * s : 4 * s + 4]
            halves.append(
                jnp.concatenate(
                    [rows[0:1] + a * cell_width, rows[1:2] + b * cell_width, rows[2:4], rows],
                    axis=0,
                )
            )
    pieces = []
    for start in range(0, ids.shape[1], 128):
        part = jnp.broadcast_to(ids[:, start : start + 128], (8, 128))
        lane, half = part & 127, part >> 7
        found = jnp.zeros((8, 128), F32)
        for h, rows in enumerate(halves):
            found = jnp.where(half == h, jnp.take_along_axis(rows, lane, axis=1), found)
        pieces.append(found)
    found = jnp.concatenate(pieces, axis=1)
    relative = found - jnp.concatenate([own] * slots, axis=1)
    rel = [relative[i : i + 1] for i in range(3)]
    distance = jnp.sqrt(rel[0] * rel[0] + rel[1] * rel[1] + rel[2] * rel[2] + soften)
    inverse = 1.0 / distance
    order = (lax.broadcasted_iota(jnp.int32, (8, 1), 0) + 1).astype(F32)
    sine, cosine = sin_cos((order * (0.5 / cut_radius)) * distance)
    wave = sine / ((order * (math.pi / cut_radius)) * distance)
    count = count_ref[0]
    live = jnp.concatenate([jnp.where(count > n, 1.0, 0.0) for n in range(slots)], axis=1)
    basis = wave * live
    basis_ref[...] = basis
    slope_ref[...] = (cosine - wave) * (inverse * live)
    kinds = found[3:4]
    unit = jnp.concatenate(
        [r * inverse for r in rel] + [inverse, kinds] + [jnp.zeros_like(kinds)] * 3, axis=0
    )
    unit_ref[...] = unit
    stack = embed_ref[...]
    parts = edge_parts(basis, unit)
    species = kind_left.shape[2] // 32
    by_kind = [[None] * species for _ in range(4)]
    for n in range(slots):
        lanes = slice(n * atoms, (n + 1) * atoms)
        kind = jnp.broadcast_to(kinds[:, lanes], (8, atoms))
        for k in range(species):
            match = kind == float(k)
            for part in range(4):
                term = jnp.where(match, parts[part][:, lanes], 0.0)
                old = by_kind[part][k]
                by_kind[part][k] = term if old is None else old + term
    stacks = [stacked_right(jnp.concatenate(rows, axis=0)) for rows in by_kind]
    vectors = dot(kind_left[1], jnp.concatenate(stacks[1:], axis=1))
    sums = [dot(kind_left[0], stacks[0])]
    sums += [vectors[:, i * atoms : (i + 1) * atoms] for i in range(3)]
    step, gate = mixed(sums, mix_high, mix_low, 0)
    low_ref[...] = (embedded(stack, own[3:4]) + step).astype(BF16)
    for part in range(3):
        sums_ref[part] = sums[part + 1]
    gate_ref[...] = gate


def hot_columns(ids, rows):
    place = lax.broadcasted_iota(jnp.int32, (rows, ids.shape[1]), 0)
    return jnp.where(ids == place, 1.0, 0.0).astype(BF16)


def second_near_kernel(slots, basis_ref, unit_ref, left_ref, hot_ref, column_ref, weight_ref,
                       near_ref):
    atoms = column_ref.shape[2]
    parts = edge_parts(basis_ref[...], unit_ref[...])
    source = jnp.concatenate([column_ref[b] for b in range(3)], axis=1)
    for n in range(slots):
        lanes = slice(n * atoms, (n + 1) * atoms)
        for part in range(4):
            weight_ref[part, :, lanes] = weights_of(left_ref, part, parts[part][:, lanes])
        near_ref[:, lanes] = dot(source, hot_ref[3 * atoms : 6 * atoms, lanes])


def second_side_kernel(slots, hot_ref, near_ref, after_ref, out_ref):
    atoms = after_ref.shape[2]
    source = jnp.concatenate([after_ref[b] for b in range(3)], axis=1)
    for n in range(slots):
        lanes = slice(n * atoms, (n + 1) * atoms)
        out_ref[:, lanes] = near_ref[:, lanes] + dot(source, hot_ref[6 * atoms :, lanes])


def second_kernel(slots, hot_ref, weight_ref, near_ref, mix_high, mix_low, hidden_high, hidden_low,
                  turn_high, turn_low, out_ref, charge_ref, cell_ref, column_ref, before_ref,
                  feature_ref, sums_ref, gate_ref, packed_ref, full_charge_ref, energy_ref,
                  slope_ref):
    atoms = column_ref.shape[2]
    source = jnp.concatenate([before_ref[b] for b in range(3)], axis=1)
    sums = [None] * 4
    for n in range(slots):
        lanes = slice(n * atoms, (n + 1) * atoms)
        feature = near_ref[:, lanes] + dot(source, hot_ref[: 3 * atoms, lanes])
        feature_ref[:, lanes] = feature.astype(BF16)
        for part in range(4):
            term = weight_ref[part, :, lanes] * feature
            sums[part] = term if sums[part] is None else sums[part] + term
    step, gate = mixed(sums, mix_high, mix_low, 1)
    hidden = column_ref[1].astype(F32) + step
    for part in range(3):
        sums_ref[part] = sums[part + 1]
    gate_ref[...] = gate
    charge = dot_split((charge_ref[0], charge_ref[1]), hidden)
    full_charge_ref[...] = charge
    place = unfold_block(cell_ref[1], atoms)[:3]
    high = place.astype(BF16).astype(F32)
    rest = place - high
    middle = rest.astype(BF16).astype(F32)
    zero = jnp.zeros((packed_ref.shape[0] - charge.shape[0] - 9, atoms), F32)
    packed_ref[...] = jnp.concatenate([charge, high, middle, rest - middle, zero], axis=0).astype(
        BF16
    )
    value, slope = silu_pair(dot_split((hidden_high[...], hidden_low[...]), hidden))
    out = out_ref[...].T
    energy_ref[...] = jnp.sum(value * out, axis=0, keepdims=True)
    slope_ref[...] = dot_split((turn_high[...], turn_low[...]), slope * out)


def message_grads(cotangent, gate_ref, sums_ref, high_ref, low_ref, layer):
    pre = cotangent * gate_ref[...]
    both = dot_split((high_ref[layer], low_ref[layer]), pre)
    half = both.shape[0] // 2
    return [both[:half]] + [both[half:] * sums_ref[i] for i in range(3)]


def radial_grad(left, value):
    high, low = split(value)
    both = dot(left, jnp.concatenate([high, low], axis=0))
    half = both.shape[0] // 2
    return both[:half] + both[half:]


def second_back_kernel(slots, scale, grid_x, hot_ref, weight_ref, turn_high, turn_low, charge_ref,
                       sums_ref, gate_ref, full_charge_ref, energy_ref, slope_ref, *refs):
    folds, refs = refs[:grid_x], refs[grid_x:]
    site_ref, long_ref, cotangent_ref, grad_ref, term_ref, before_ref, after_ref = refs
    atoms = gate_ref.shape[1]
    total = folds[0][...].astype(F32)
    for part in folds[1:]:
        total = total + part[...].astype(F32)
    wide = full_charge_ref.shape[0]
    potential = total[:wide] * (2.0 * scale)
    slopes = total[wide : wide + 3] + total[wide + 3 : wide + 6] + total[wide + 6 : wide + 9]
    long_ref[...] = jnp.concatenate(
        [slopes * (2.0 * scale), jnp.zeros((5, atoms), F32)], axis=0
    )
    site_ref[0] = energy_ref[...] + 0.5 * jnp.sum(
        full_charge_ref[...] * potential, axis=0, keepdims=True
    )
    high, low = split(potential)
    turned = ((0,), (0,))
    cotangent = slope_ref[...] + (
        dot(charge_ref[0], high, turned)
        + (dot(charge_ref[0], low, turned) + dot(charge_ref[1], high, turned))
    )
    cotangent_ref[...] = cotangent
    grads = message_grads(cotangent, gate_ref, sums_ref, turn_high, turn_low, 1)
    for part in range(4):
        grad_ref[part] = grads[part]
    for n in range(slots):
        lanes = slice(n * atoms, (n + 1) * atoms)
        term = weight_ref[0, :, lanes] * grads[0]
        for part in range(1, 4):
            term = term + weight_ref[part, :, lanes] * grads[part]
        term_ref[:, lanes] = term.astype(BF16)
    for side, out_ref in ((0, before_ref), (2, after_ref)):
        for b in range(3):
            start = (3 * side + b) * atoms
            hot = hot_ref[start : start + atoms]
            out_ref[b] = dot(term_ref[...], hot, ((1,), (1,))).astype(BF16)


def second_middle_kernel(hot_ref, term_ref, cotangent_ref, middle_ref):
    atoms = cotangent_ref.shape[1]
    for b in range(3):
        hot = hot_ref[(3 + b) * atoms : (4 + b) * atoms]
        grad = dot(term_ref[...], hot, ((1,), (1,)))
        middle_ref[b] = grad + cotangent_ref[...] if b == 1 else grad


def second_edge_kernel(slots, back_ref, feature_ref, grad_ref, edge_ref):
    atoms = grad_ref.shape[2]
    for n in range(slots):
        lanes = slice(n * atoms, (n + 1) * atoms)
        feature = feature_ref[:, lanes].astype(F32)
        for part in range(4):
            edge_ref[8 * part : 8 * part + 8, lanes] = radial_grad(
                back_ref[1 if part else 0], grad_ref[part] * feature
            )


def first_back_kernel(slots, ids_ref, basis_ref, slope_ref, unit_ref, kind_high, kind_low,
                      turn_high, turn_low, sums_ref, gate_ref, edge_ref, long_ref, middle_ref,
                      *refs):
    from_x, from_y, outs = refs[:2], refs[2:4], refs[4:]
    atoms = gate_ref.shape[1]
    cotangent = middle_ref[1]
    for block in (from_x[0][1], from_x[1][1], from_y[0][...], from_y[1][...]):
        cotangent = cotangent + block.astype(F32)
    grads = message_grads(cotangent, gate_ref, sums_ref, turn_high, turn_low, 0)
    unit = unit_ref[...]
    kinds = unit[4:5]
    by_kind = [dot_split((kind_high[0], kind_low[0]), grads[0])]
    by_kind += [dot_split((kind_high[1], kind_low[1]), grads[i]) for i in range(1, 4)]
    species = by_kind[0].shape[0] // 8
    edges = [[] for _ in range(4)]
    for n in range(slots):
        kind = jnp.broadcast_to(kinds[:, n * atoms : (n + 1) * atoms], (8, atoms))
        matches = [kind == float(k) for k in range(1, species)]
        for part in range(4):
            rows = by_kind[part]
            found = rows[:8]
            for k, match in enumerate(matches):
                found = jnp.where(match, rows[8 * k + 8 : 8 * k + 16], found)
            edges[part].append(found)
    edges = [
        edge_ref[8 * part : 8 * part + 8] + jnp.concatenate(edges[part], axis=1) for part in range(4)
    ]
    basis = basis_ref[...]
    units = [unit[i : i + 1] for i in range(3)]
    inverse = unit[3:4]
    by_basis = edges[0]
    for i in range(3):
        by_basis = by_basis + edges[i + 1] * units[i]
    by_unit = [jnp.sum(edges[i + 1] * basis, axis=0, keepdims=True) * inverse for i in range(3)]
    by_distance = jnp.sum(by_basis * slope_ref[...], axis=0, keepdims=True)
    for i in range(3):
        by_distance = by_distance - by_unit[i] * units[i]
    moves = [by_unit[i] + by_distance * units[i] for i in range(3)]
    zero = jnp.zeros_like(moves[0])
    move = jnp.concatenate(moves + [zero] * 5, axis=0)
    own = long_ref[...]
    for n in range(slots):
        own = own - move[:, n * atoms : (n + 1) * atoms]
    ids = ids_ref[...]
    lane_hot = hot_columns(ids & 127, 128)
    half = ids >> 7
    high = move.astype(BF16).astype(F32)
    both = jnp.concatenate([high, move - high], axis=0)
    per_cell = atoms // 128
    rows = jnp.concatenate(
        [jnp.where(half == h, both, 0.0).astype(BF16) for h in range(9 * per_cell)], axis=0
    )
    spread = dot(rows, lane_hot, ((1,), (1,)))
    for cell in range(9):
        found = []
        for h in range(cell * per_cell, (cell + 1) * per_cell):
            found.append(spread[16 * h : 16 * h + 8] + spread[16 * h + 8 : 16 * h + 16])
        grad = jnp.concatenate(found, axis=1)
        if cell == CENTRE:
            grad = own + grad
        outs[cell // 3][cell % 3] = grad


def pair_counts(parts):
    total = WAVE_REACH + WAVE_REACH * (2 * WAVE_REACH + 1)
    share = -(-total // parts)
    return total, share, -(-share // 16) * 16


def pair_vectors(slot, share, part):
    side = 2 * WAVE_REACH + 1
    total = WAVE_REACH + WAVE_REACH * side
    index = slot + part.astype(F32) * share
    later = index - WAVE_REACH
    row = jnp.floor((later + 0.5) * (1.0 / side))
    first = index < WAVE_REACH
    kx = jnp.where(first, 0.0, row + 1.0)
    ky = jnp.where(first, index + 1.0, later - row * side - WAVE_REACH)
    valid = jnp.where((slot < share) & (index < total), 1.0, 0.0)
    return kx, ky, valid


def count_up(rows):
    return lax.broadcasted_iota(jnp.int32, (rows, 1), 0).astype(F32)


def green_weights(share, padded, grid, place_ref, vec_ref, weight_ref):
    grid_x, grid_y = grid
    turn = 2.0 * math.pi
    side = 2 * WAVE_REACH + 1
    top = side * side * side - 1
    vec = vec_ref[...].astype(F32) + WAVE_REACH
    code = (vec[0:1] * side + vec[1:2]) * side + vec[2:3]
    code = jnp.maximum(code, top - code)
    span = 8 * share
    row = count_up(span)
    slot = jnp.floor(row * 0.125)
    height = row - 8.0 * slot + 1.0
    flat = count_up(padded)
    slot = jnp.concatenate([slot, slot, flat], axis=0)
    kz = jnp.concatenate([height, -height, jnp.zeros_like(flat)], axis=0)
    kx, ky, valid = pair_vectors(slot, share, place_ref[0])
    own = ((kx + WAVE_REACH) * side + ky + WAVE_REACH) * side + kz + WAVE_REACH
    seen = jnp.zeros((own.shape[0], 128), F32)
    for start in range(0, code.shape[1], 128):
        seen = seen + jnp.where(own == code[:, start : start + 128], 1.0, 0.0)
    count = jnp.sum(seen, axis=1, keepdims=True) * valid
    sq = (
        (kx * (turn / (grid_x * cell_width))) ** 2
        + (ky * (turn / (grid_y * cell_width))) ** 2
        + (kz * (turn / box_height)) ** 2
    )
    green = jnp.exp(-smear_width * sq) / (sq + screen * screen) * count
    weight_ref[...] = jnp.broadcast_to(green, weight_ref.shape)


def basis_rows(share, ca, sa, cb, sb):
    cc, ss, sc, cs = [], [], [], []
    for p in range(share):
        c, s = ca[p : p + 1], sa[p : p + 1]
        cc.append(c * cb)
        ss.append(s * sb)
        sc.append(s * cb)
        cs.append(c * sb)
    return cc, ss, sc, cs


def unpack_rows(block):
    half = block.shape[1] // 2
    return jnp.concatenate([block[:, :half], block[:, half:]], axis=0)


def pack_rows(block):
    half = block.shape[0] // 2
    return jnp.concatenate([block[:half], block[half:]], axis=1)


def structure_kernel(share, padded, grid, wide, place_ref, *refs):
    grid_x, grid_y = grid
    blocks, (ca_ref, sa_ref, cb_ref, sb_ref, own_ref, out_ref) = refs[:grid_x], refs[grid_x:]
    col = place_ref[1].astype(F32) * (1.0 / grid_y)
    kx, ky, _ = pair_vectors(count_up(padded), share, place_ref[0])
    kz = count_up(8) + 1.0
    total = None
    for d in range(grid_x):
        block = blocks[d][...]
        charge = block[:wide]
        atoms = charge.shape[1]
        pieces = block[wide:].astype(F32)
        place = pieces[0:3] + (pieces[3:6] + pieces[6:9])
        row = lax.rem(place_ref[0] + d, grid_x).astype(F32) * (1.0 / grid_x)
        x = place[0:1] * (1.0 / (grid_x * cell_width)) + row
        y = place[1:2] * (1.0 / (grid_y * cell_width)) + col
        sa, ca = sin_cos(kx * x + ky * y)
        sb, cb = sin_cos(kz * (place[2:3] * (1.0 / box_height)))
        lanes = pl.ds(d * atoms, atoms)
        ca_ref[:, lanes] = ca
        sa_ref[:, lanes] = sa
        cb_ref[:, lanes] = cb
        sb_ref[:, lanes] = sb
        cc, ss, sc, cs = basis_rows(share, ca, sa, cb, sb)
        high, low = split(jnp.concatenate(cc + ss + sc + cs + [ca, sa], axis=0))
        term = dot(high, charge, ((1,), (1,))) + dot(low, charge, ((1,), (1,)))
        total = term if total is None else total + term
    packed = pack_rows(total)
    own_ref[...] = packed
    out_ref[...] = packed.astype(BF16)


def fold_kernel(share, padded, grid, wide, place_ref, ca_ref, sa_ref, cb_ref, sb_ref, weight_ref,
                *refs):
    grid_x, grid_y = grid
    blocks, parts, outs = refs[:grid_x], refs[grid_x : grid_x + grid_y], refs[grid_x + grid_y :]
    turn = 2.0 * math.pi
    packed = parts[0][...].astype(F32)
    for part in parts[1:]:
        packed = packed + part[...].astype(F32)
    struct = unpack_rows(packed)
    span = 8 * share
    cc, ss, sc, cs = (struct[i * span : (i + 1) * span] for i in range(4))
    weight = weight_ref[:, :wide]
    plus, minus, flat = weight[:span], weight[span : 2 * span], weight[2 * span :]
    re_plus, im_plus = plus * (cc - ss), plus * (sc + cs)
    re_minus, im_minus = minus * (cc + ss), minus * (sc - cs)
    rows = jnp.concatenate(
        [
            re_plus + re_minus,
            re_minus - re_plus,
            im_plus + im_minus,
            im_plus - im_minus,
            flat * struct[4 * span : 4 * span + padded],
            flat * struct[4 * span + padded :],
        ],
        axis=0,
    )
    row_high, row_low = split(rows)
    row_pair = jnp.concatenate([row_high, row_low], axis=1)
    turned = rows.T
    t_high, t_low = split(turned)
    t_both = jnp.concatenate([t_high, t_low], axis=0)
    kx, ky, _ = pair_vectors(count_up(padded), share, place_ref[0])
    kx = kx * (turn / (grid_x * cell_width))
    ky = ky * (turn / (grid_y * cell_width))
    kz = (count_up(8) + 1.0) * (turn / box_height)
    for d in range(grid_x):
        charge = blocks[d][:wide]
        atoms = charge.shape[1]
        lanes = pl.ds(d * atoms, atoms)
        ca, sa, cb, sb = ca_ref[:, lanes], sa_ref[:, lanes], cb_ref[:, lanes], sb_ref[:, lanes]
        bcc, bss, bsc, bcs = basis_rows(share, ca, sa, cb, sb)
        high, low = split(jnp.concatenate(bcc + bss + bsc + bcs + [ca, sa], axis=0))
        both = dot(t_both, high)
        pot = both[:wide] + both[wide:] + dot(t_high, low)
        proj = dot(row_pair, jnp.concatenate([charge, charge], axis=0))
        by_x = jnp.zeros((8, atoms), jnp.float32)
        by_y = jnp.zeros((8, atoms), jnp.float32)
        by_z = jnp.zeros((8, atoms), jnp.float32)
        for p in range(share):
            pcc, pss, psc, pcs = (
                proj[i * span + 8 * p : i * span + 8 * p + 8] for i in range(4)
            )
            slope = bcs[p] * pss - bsc[p] * pcc + bcc[p] * psc - bss[p] * pcs
            by_x = by_x + kx[p : p + 1] * slope
            by_y = by_y + ky[p : p + 1] * slope
            by_z = by_z + (bsc[p] * pss - bcs[p] * pcc - bss[p] * psc + bcc[p] * pcs)
        flat_slope = ca * proj[4 * span + padded :] - sa * proj[4 * span : 4 * span + padded]
        grad_x = jnp.sum(by_x, axis=0, keepdims=True) + jnp.sum(kx * flat_slope, axis=0, keepdims=True)
        grad_y = jnp.sum(by_y, axis=0, keepdims=True) + jnp.sum(ky * flat_slope, axis=0, keepdims=True)
        grad_z = jnp.sum(kz * by_z, axis=0, keepdims=True)
        slopes = jnp.concatenate([grad_x, grad_y, grad_z], axis=0)
        high = slopes.astype(BF16).astype(F32)
        rest = slopes - high
        middle = rest.astype(BF16).astype(F32)
        zero = jnp.zeros((outs[d].shape[0] - wide - 9, atoms), F32)
        block = jnp.concatenate([pot, high, middle, rest - middle, zero], axis=0)
        outs[d][...] = block.astype(outs[d].dtype)


def per_device(
    positions,
    species,
    neighbours,
    counts,
    species_embed,
    radial,
    mixing,
    read_hidden,
    read_out,
    charge_map,
    wavevectors,
):
    atoms = positions.shape[3]
    slots = neighbours.shape[3]
    features, lat_width = charge_map.shape
    wave_count = wavevectors.shape[1]
    grid = lax.axis_size("gx"), lax.axis_size("gy")
    grid_x, grid_y = grid
    edges = slots * atoms
    scale = 1.0 / math.sqrt(wave_count * lat_width * atoms * grid_x * grid_y)
    place = jnp.stack([lax.axis_index("gx"), lax.axis_index("gy")]).astype(jnp.int32)
    _, share, padded = pair_counts(grid_x)
    ids = neighbours.transpose(0, 3, 1, 2).reshape(1, edges)
    dma = pltpu.SemaphoreType.DMA
    shown = positions.transpose(0, 2, 1, 3)

    (own,) = run(
        pack_kernel,
        [shape(4 * atoms // 128, 128)],
        [shown, species],
        scratch=[
            pltpu.VMEM(shown.shape, F32),
            pltpu.VMEM(species.shape, jnp.int32),
            dma((2,)),
        ],
        hbm=2,
        grant=60,
        name="pack",
    )
    norm = 1.0 / math.sqrt(slots)
    kind_rows = 8 * species_embed.shape[0]
    low_pair = lambda *dims: [shape(*dims, dtype=BF16)] * 2
    (ids, counts, embed, kind_left, left, back, kind_high, kind_low, mix_high, mix_low, turn_high,
     turn_low) = run(
        functools.partial(prep_first_kernel, norm),
        [
            shape(1, edges, dtype=jnp.int32),
            shape(*counts.shape, dtype=jnp.int32),
            shape(features, 32, dtype=BF16),
            shape(2, features, 4 * kind_rows, dtype=BF16),
            shape(2, features, 32, dtype=BF16),
            shape(2, 16, 2 * features, dtype=BF16),
        ]
        + low_pair(2, kind_rows, features)
        + low_pair(2, features, 2 * features)
        + low_pair(2, 2 * features, features),
        [ids, counts, species_embed, radial, mixing],
        scratch=[
            pltpu.VMEM(species_embed.shape, F32),
            pltpu.VMEM(radial.shape, F32),
            pltpu.VMEM(mixing.shape, F32),
            dma((5,)),
        ],
        hbm=5,
        name="prep_first",
    )
    cells, ids = around(own, ids)
    (hot,) = run(
        hot_kernel, [shape(9 * atoms, edges, dtype=BF16)], [ids], flops=2_000_000_000, name="hot"
    )
    read_out, hidden_high, hidden_low, hidden_turn_high, hidden_turn_low, charge_pair = run(
        prep_second_kernel,
        [shape(1, features)]
        + low_pair(features, features)
        + low_pair(features, features)
        + [shape(2, lat_width, features, dtype=BF16)],
        [read_out[None, :], read_hidden, charge_map.T],
        scratch=[
            pltpu.VMEM(read_hidden.shape, F32),
            pltpu.VMEM((lat_width, features), F32),
            dma((3,)),
        ],
        hbm=3,
        name="prep_second",
    )
    (weight,) = run(
        functools.partial(green_weights, share, padded, grid),
        [shape(16 * share + padded, 128)],
        [place, wavevectors],
        smem=1,
        name="green",
    )
    low, basis, slope, unit, sums_one, gate_one = run(
        functools.partial(first_kernel, slots),
        [
            shape(features, atoms, dtype=BF16),
            shape(8, edges),
            shape(8, edges),
            shape(8, edges),
            shape(3, features, atoms),
            shape(features, atoms),
        ],
        [ids, counts, embed, kind_left, mix_high, mix_low] + cells,
        name="first",
    )
    hidden, hot = around(low, hot)
    edge_weights, near = run(
        functools.partial(second_near_kernel, slots),
        [shape(4, features, edges), shape(features, edges)],
        [basis, unit, left, hot, hidden[1]],
        flops=2_000_000_000,
        name="second_near",
    )
    (near,) = run(
        functools.partial(second_side_kernel, slots),
        [shape(features, edges)],
        [hot, near, hidden[2]],
        flops=1_000_000_000,
        name="second_side",
    )
    block_rows = -(-(lat_width + 9) // 16) * 16
    feature, sums_two, gate_two, packed, charge, energy, energy_slope = run(
        functools.partial(second_kernel, slots),
        [
            shape(features, edges, dtype=BF16),
            shape(3, features, atoms),
            shape(features, atoms),
            shape(block_rows, atoms, dtype=BF16),
            shape(lat_width, atoms),
            shape(1, atoms),
            shape(features, atoms),
        ],
        [hot, edge_weights, near, mix_high, mix_low, hidden_high, hidden_low, hidden_turn_high,
         hidden_turn_low, read_out, charge_pair, cells[1], hidden[1], hidden[0]],
        name="second",
    )
    charges = [packed] + [shifted(packed, d, 0) for d in range(1, grid_x)]
    span = grid_x * atoms
    rows = 32 * share + 2 * padded
    *phases, own_part, part = run(
        functools.partial(structure_kernel, share, padded, grid, lat_width),
        [
            shape(padded, span),
            shape(padded, span),
            shape(8, span),
            shape(8, span),
            shape(rows // 2, 2 * lat_width),
            shape(rows // 2, 2 * lat_width, dtype=BF16),
        ],
        [place] + charges,
        smem=1,
        name="structure",
    )
    parts = [own_part] + [shifted(part, 0, d) for d in range(1, grid_y)]
    folds = run(
        functools.partial(fold_kernel, share, padded, grid, lat_width),
        [shape(block_rows, atoms)] + [shape(block_rows, atoms, dtype=BF16)] * (grid_x - 1),
        [place] + phases + [weight] + charges + parts,
        smem=1,
        name="fold",
    )
    folds = [folds[0]] + [shifted(folds[d], -d, 0) for d in range(1, grid_x)]

    site, long, cotangent, grads, term, before, after = run(
        functools.partial(second_back_kernel, slots, scale, grid_x),
        [
            shape(1, 1, atoms),
            shape(8, atoms),
            shape(features, atoms),
            shape(4, features, atoms),
            shape(features, edges, dtype=BF16),
            shape(3, features, atoms, dtype=BF16),
            shape(3, features, atoms, dtype=BF16),
        ],
        [hot, edge_weights, turn_high, turn_low, charge_pair, sums_two, gate_two, charge, energy,
         energy_slope] + folds,
        name="second_back",
    )
    from_x = [shifted(after, -1, 0), shifted(before, 1, 0)]
    (middle,) = run(
        second_middle_kernel,
        [shape(3, features, atoms)],
        [hot, term, cotangent],
        flops=1_000_000_000,
        name="second_middle",
    )
    sides = [
        (middle[b] + from_x[0][b].astype(F32) + from_x[1][b].astype(F32)).astype(BF16)
        for b in (0, 2)
    ]
    from_y = [shifted(sides[1], 0, -1), shifted(sides[0], 0, 1)]
    (edge,) = run(
        functools.partial(second_edge_kernel, slots),
        [shape(32, edges)],
        [back, feature, grads],
        flops=1_000_000_000,
        name="second_edge",
    )
    before, middle, after = run(
        functools.partial(first_back_kernel, slots),
        [shape(3, 8, atoms)] * 3,
        [ids, basis, slope, unit, kind_high, kind_low, turn_high, turn_low, sums_one, gate_one, edge,
         long, middle] + from_x + from_y,
        name="first_back",
    )
    total = middle + shifted(after, -1, 0) + shifted(before, 1, 0)
    total = total[1] + shifted(total[2], 0, -1) + shifted(total[0], 0, 1)
    forces = -total[None, :3, None, :]
    return (forces.transpose(0, 2, 1, 3), site)


def solution(mesh):
    in_specs = (
        P("gx", "gy", None, None),
        P("gx", "gy", None),
        P("gx", "gy", None, None),
        P("gx", "gy", None),
        P(),
        P(),
        P(),
        P(),
        P(),
        P(),
        P(),
    )
    out_specs = (P("gx", "gy", None, None), P("gx", "gy", None))
    return jax.shard_map(
        per_device, mesh=mesh, in_specs=in_specs, out_specs=out_specs, check_vma=False
    )
```

```python
import functools
import math

import jax
import jax.numpy as jnp
import numpy as np
from jax import lax
from jax.experimental import pallas as pl
from jax.experimental.pallas import tpu as pltpu
from jax.sharding import PartitionSpec as P

cell_width = 10.0
box_height = 30.0
cut_radius = 50.0
soften = 0.25
screen = 0.5
smear_width = 0.5
WAVE_REACH = 8
F32 = jnp.float32
BF16 = jnp.bfloat16
OFFSETS = [(a, b) for a in (-1, 0, 1) for b in (-1, 0, 1)]
CENTRE = 4


def shifted(block, along_x, along_y):
    count_x, count_y = lax.axis_size("gx"), lax.axis_size("gy")
    route = []
    for i in range(count_x):
        for j in range(count_y):
            source = ((i + along_x) % count_x) * count_y + (j + along_y) % count_y
            route.append((source, i * count_y + j))
    return lax.ppermute(block, ("gx", "gy"), route)


def around(block, beside):
    column = jnp.stack([shifted(block, 0, -1), block, shifted(block, 0, 1)])
    column, beside = lax.optimization_barrier((column, beside))
    return [shifted(column, -1, 0), column, shifted(column, 1, 0)], beside


def whole(space=pltpu.VMEM):
    return pl.BlockSpec(memory_space=space)


def run(kernel, outs, args, scratch=(), smem=0, hbm=0, flops=10_000_000, grant=16, name=None):
    specs = [whole(pltpu.SMEM)] * smem + [whole(pltpu.HBM)] * hbm
    specs += [whole()] * (len(args) - smem - hbm)
    return list(
        pl.pallas_call(
            kernel,
            out_shape=outs,
            in_specs=specs,
            out_specs=[whole() for _ in outs],
            scratch_shapes=list(scratch),
            compiler_params=pltpu.CompilerParams(vmem_limit_bytes=grant * 1024 * 1024),
            cost_estimate=pl.CostEstimate(
                flops=flops, bytes_accessed=1_000_000, transcendentals=0
            ),
            name=name,
        )(*args)
    )


def shape(*dims, dtype=F32):
    return jax.ShapeDtypeStruct(dims, dtype)


def split(value):
    high = value.astype(BF16)
    return high, (value - high.astype(F32)).astype(BF16)


def dot(left, right, contract=((1,), (0,))):
    return lax.dot_general(left, right, (contract, ((), ())), preferred_element_type=F32)


def dot3(left, right):
    left_high, left_low = split(left)
    right_high, right_low = split(right)
    return dot(left_high, right_high) + (dot(left_high, right_low) + dot(left_low, right_high))


def dot_split(left, right):
    right_high, right_low = split(right)
    return dot(left[0], right_high) + (dot(left[0], right_low) + dot(left[1], right_high))


def sin_cos(turns):
    quarter = jnp.round(turns * 4.0)
    x = (turns - quarter * 0.25) * (2.0 * math.pi)
    z = x * x
    sine = ((-1.9515295891e-4 * z + 8.3321608736e-3) * z - 1.6666654611e-1) * (z * x) + x
    cosine = (2.443315711809948e-5 * z - 1.388731625493765e-3) * z + 4.166664568298827e-2
    cosine = cosine * (z * z) - 0.5 * z + 1.0
    k = quarter.astype(jnp.int32) & 3
    odd = (k & 1) == 1
    by_sine = jnp.where(odd, cosine, sine)
    by_cosine = jnp.where(odd, sine, cosine)
    return (
        jnp.where(k >= 2, -by_sine, by_sine),
        jnp.where((k == 1) | (k == 2), -by_cosine, by_cosine),
    )


def stacked_left(value):
    high = value.astype(BF16).astype(F32)
    rows = jnp.concatenate([high, high, value - high, jnp.zeros_like(high)], axis=0)
    return rows.T.astype(BF16)


def stacked_right(value):
    high = value.astype(BF16).astype(F32)
    return jnp.concatenate([high, value - high, high, jnp.zeros_like(high)], axis=0).astype(BF16)


def silu_pair(value):
    gate = 1.0 / (1.0 + jnp.exp(-value))
    return value * gate, gate * (1.0 + value * (1.0 - gate))


def onehot_kinds(kinds, rows):
    levels = lax.broadcasted_iota(jnp.int32, (rows, kinds.shape[1]), 0).astype(F32)
    return jnp.where(kinds == levels, 1.0, 0.0)


def embedding_stack(embed):
    high = embed.astype(BF16).astype(F32)
    rest = embed - high
    middle = rest.astype(BF16).astype(F32)
    rows = jnp.concatenate([high, middle, rest - middle, jnp.zeros_like(high)], axis=0)
    return rows.T.astype(BF16)


def embedded(stack, kinds):
    hot = onehot_kinds(kinds, 8)
    return dot(stack, jnp.concatenate([hot, hot, hot, jnp.zeros_like(hot)], axis=0).astype(BF16))


def weights_of(stack_ref, part, rows):
    return dot(stack_ref[1 if part else 0], stacked_right(rows))


def mixed(sums, high_ref, low_ref, layer):
    squares = sums[1] * sums[1] + sums[2] * sums[2] + sums[3] * sums[3]
    both = jnp.concatenate([sums[0], squares], axis=0)
    return silu_pair(dot_split((high_ref[layer], low_ref[layer]), both))


def edge_parts(basis, unit):
    return [basis] + [basis * unit[i : i + 1] for i in range(3)]


def pack_kernel(position_ref, species_ref, out_ref, place, kind, sems):
    copies = [
        pltpu.make_async_copy(position_ref, place, sems.at[0]),
        pltpu.make_async_copy(species_ref, kind, sems.at[1]),
    ]
    for copy in copies:
        copy.start()
    for copy in copies:
        copy.wait()
    rows = [place[0, i] for i in range(3)] + [kind[0].astype(F32)]
    atoms = rows[0].shape[1]
    out_ref[...] = jnp.concatenate(
        [row[:, s : s + 128] for s in range(0, atoms, 128) for row in rows], axis=0
    )


def radial_left(radial):
    high = radial.astype(BF16).astype(F32)
    low = radial - high
    top = jnp.concatenate([high, high], axis=1)
    end = jnp.concatenate([low, jnp.zeros_like(low)], axis=1)
    return jnp.concatenate([top, end], axis=0).astype(BF16)


def put_split(value, high_ref, low_ref, *at):
    high, low = split(value)
    high_ref[at] = high
    low_ref[at] = low


def fetch(sources, targets, sems):
    copies = [
        pltpu.make_async_copy(source, target, sems.at[i])
        for i, (source, target) in enumerate(zip(sources, targets))
    ]
    for copy in copies:
        copy.start()
    for copy in copies:
        copy.wait()


def prep_first_kernel(norm, ids_in, count_in, embed_in, radial_in, mixing_in, id_ref, count_ref,
                      embed_out, kind_left, left_out, back_out, kind_high, kind_low, mix_high,
                      mix_low, turn_high, turn_low, embed_ref, radial_ref, mixing_ref, sems):
    fetch(
        [ids_in, count_in, embed_in, radial_in, mixing_in],
        [id_ref, count_ref, embed_ref, radial_ref, mixing_ref],
        sems,
    )
    embed = embed_ref[...]
    kinds = embed.shape[0]
    for path in range(2):
        radial = radial_ref[0, path] * norm
        rows = jnp.concatenate([radial * embed[s : s + 1] for s in range(kinds)], axis=0)
        kind_left[path] = stacked_left(rows)
        put_split(rows, kind_high, kind_low, path)
        radial = radial_ref[1, path] * norm
        left_out[path] = stacked_left(radial)
        back_out[path] = radial_left(radial)
    for layer in range(2):
        scalar, vector = mixing_ref[layer, 0], mixing_ref[layer, 1]
        put_split(jnp.concatenate([scalar.T, vector.T], axis=1), mix_high, mix_low, layer)
        put_split(jnp.concatenate([scalar, 2.0 * vector], axis=0), turn_high, turn_low, layer)
    embed = jnp.concatenate([embed, jnp.zeros((8 - kinds, embed.shape[1]), F32)], axis=0)
    embed_out[...] = embedding_stack(embed)


def prep_second_kernel(read_in, hidden_in, charge_in, read_ref, hidden_high, hidden_low,
                       hidden_turn_high, hidden_turn_low, charge_pair, hidden_ref, charge_ref, sems):
    fetch([read_in, hidden_in, charge_in], [read_ref, hidden_ref, charge_ref], sems)
    put_split(hidden_ref[...].T, hidden_high, hidden_low, Ellipsis)
    put_split(hidden_ref[...], hidden_turn_high, hidden_turn_low, Ellipsis)
    charge = charge_ref[...]
    high = charge.astype(BF16).astype(F32)
    charge_pair[0] = high.astype(BF16)
    charge_pair[1] = (charge - high).astype(BF16)


def hot_kernel(ids_ref, hot_ref):
    edges = ids_ref.shape[1]
    for start in range(0, edges, 256):
        lanes = slice(start, start + 256)
        hot_ref[:, lanes] = hot_columns(ids_ref[:, lanes], hot_ref.shape[0])


def hot_back_kernel(ids_ref, hot_ref):
    edges = ids_ref.shape[1]
    entry = lax.broadcasted_iota(jnp.int32, (128, hot_ref.shape[1]), 1).astype(F32)
    for start in range(0, edges, 128):
        row = jnp.broadcast_to(ids_ref[:, start : start + 128].astype(F32), (8, 128))
        column = row.T[:, 0:1]
        hot_ref[start : start + 128] = jnp.where(column == entry, 1.0, 0.0).astype(BF16)


def unfold_block(block, atoms):
    parts = atoms // 128
    return jnp.concatenate([block[4 * s : 4 * s + 4] for s in range(parts)], axis=1)


def first_kernel(slots, ids_ref, count_ref, embed_ref, kind_left, mix_high, mix_low, before_ref,
                 column_ref, after_ref, low_ref, basis_ref, slope_ref, unit_ref, sums_ref,
                 gate_ref):
    atoms = low_ref.shape[1]
    ids = ids_ref[...]
    frame = [before_ref, column_ref, after_ref]
    own = unfold_block(column_ref[1], atoms)
    own = jnp.concatenate([own, jnp.zeros_like(own)], axis=0)
    per_cell = atoms // 128
    places = lax.broadcasted_iota(jnp.int32, (4 * per_cell, 128), 0)
    upper = places >> 2
    kind_of_row = places & 3
    rows = []
    for a, b in OFFSETS:
        move = jnp.where(kind_of_row == 0, a * cell_width, 0.0)
        move = move + jnp.where(kind_of_row == 1, b * cell_width, 0.0)
        rows.append(frame[a + 1][b + 1] + move)
    pieces = []
    for start in range(0, ids.shape[1], 128):
        part = jnp.broadcast_to(ids[:, start : start + 128], places.shape)
        lane, half = part & 127, (part >> 7) - upper
        found = jnp.zeros(places.shape, F32)
        for cell, block in enumerate(rows):
            value = jnp.take_along_axis(block, lane, axis=1)
            found = jnp.where(half == per_cell * cell, value, found)
        total = found[:4]
        for s in range(1, per_cell):
            total = total + found[4 * s : 4 * s + 4]
        pieces.append(jnp.concatenate([total, total], axis=0))
    found = jnp.concatenate(pieces, axis=1)
    relative = found - jnp.concatenate([own] * slots, axis=1)
    rel = [relative[i : i + 1] for i in range(3)]
    distance = jnp.sqrt(rel[0] * rel[0] + rel[1] * rel[1] + rel[2] * rel[2] + soften)
    inverse = 1.0 / distance
    order = (lax.broadcasted_iota(jnp.int32, (8, 1), 0) + 1).astype(F32)
    sine, cosine = sin_cos((order * (0.5 / cut_radius)) * distance)
    wave = sine / ((order * (math.pi / cut_radius)) * distance)
    count = count_ref[0]
    live = jnp.concatenate([jnp.where(count > n, 1.0, 0.0) for n in range(slots)], axis=1)
    basis = wave * live
    basis_ref[...] = basis
    slope_ref[...] = (cosine - wave) * (inverse * live)
    kinds = found[3:4]
    unit = jnp.concatenate(
        [r * inverse for r in rel] + [inverse, kinds] + [jnp.zeros_like(kinds)] * 3, axis=0
    )
    unit_ref[...] = unit
    stack = embed_ref[...]
    parts = edge_parts(basis, unit)
    species = kind_left.shape[2] // 32
    by_kind = [[None] * species for _ in range(4)]
    for n in range(slots):
        lanes = slice(n * atoms, (n + 1) * atoms)
        kind = jnp.broadcast_to(kinds[:, lanes], (8, atoms))
        for k in range(species):
            match = kind == float(k)
            for part in range(4):
                term = jnp.where(match, parts[part][:, lanes], 0.0)
                old = by_kind[part][k]
                by_kind[part][k] = term if old is None else old + term
    stacks = [stacked_right(jnp.concatenate(rows, axis=0)) for rows in by_kind]
    vectors = dot(kind_left[1], jnp.concatenate(stacks[1:], axis=1))
    sums = [dot(kind_left[0], stacks[0])]
    sums += [vectors[:, i * atoms : (i + 1) * atoms] for i in range(3)]
    step, gate = mixed(sums, mix_high, mix_low, 0)
    low_ref[...] = (embedded(stack, own[3:4]) + step).astype(BF16)
    for part in range(3):
        sums_ref[part] = sums[part + 1]
    gate_ref[...] = gate


def hot_columns(ids, rows):
    place = lax.broadcasted_iota(jnp.int32, (rows, ids.shape[1]), 0)
    return jnp.where(ids == place, 1.0, 0.0).astype(BF16)


def second_near_kernel(slots, basis_ref, unit_ref, left_ref, hot_ref, column_ref, weight_ref,
                       near_ref):
    atoms = column_ref.shape[2]
    parts = edge_parts(basis_ref[...], unit_ref[...])
    source = jnp.concatenate([column_ref[b] for b in range(3)], axis=1)
    for n in range(slots):
        lanes = slice(n * atoms, (n + 1) * atoms)
        for part in range(4):
            weight_ref[part, :, lanes] = weights_of(left_ref, part, parts[part][:, lanes])
        near_ref[:, lanes] = dot(source, hot_ref[3 * atoms : 6 * atoms, lanes])


def second_side_kernel(slots, hot_ref, near_ref, after_ref, out_ref):
    atoms = after_ref.shape[2]
    source = jnp.concatenate([after_ref[b] for b in range(3)], axis=1)
    for n in range(slots):
        lanes = slice(n * atoms, (n + 1) * atoms)
        out_ref[:, lanes] = near_ref[:, lanes] + dot(source, hot_ref[6 * atoms :, lanes])


def second_kernel(slots, hot_ref, weight_ref, near_ref, mix_high, mix_low, hidden_high, hidden_low,
                  turn_high, turn_low, out_ref, charge_ref, cell_ref, column_ref, before_ref,
                  feature_ref, sums_ref, gate_ref, packed_ref, full_charge_ref, energy_ref,
                  slope_ref):
    atoms = column_ref.shape[2]
    source = jnp.concatenate([before_ref[b] for b in range(3)], axis=1)
    sums = [None] * 4
    for n in range(slots):
        lanes = slice(n * atoms, (n + 1) * atoms)
        feature = near_ref[:, lanes] + dot(source, hot_ref[: 3 * atoms, lanes])
        feature_ref[:, lanes] = feature.astype(BF16)
        for part in range(4):
            term = weight_ref[part, :, lanes] * feature
            sums[part] = term if sums[part] is None else sums[part] + term
    step, gate = mixed(sums, mix_high, mix_low, 1)
    hidden = column_ref[1].astype(F32) + step
    for part in range(3):
        sums_ref[part] = sums[part + 1]
    gate_ref[...] = gate
    charge = dot_split((charge_ref[0], charge_ref[1]), hidden)
    full_charge_ref[...] = charge
    place = unfold_block(cell_ref[1], atoms)[:3]
    high = place.astype(BF16).astype(F32)
    rest = place - high
    middle = rest.astype(BF16).astype(F32)
    zero = jnp.zeros((packed_ref.shape[0] - charge.shape[0] - 9, atoms), F32)
    packed_ref[...] = jnp.concatenate([charge, high, middle, rest - middle, zero], axis=0).astype(
        BF16
    )
    value, slope = silu_pair(dot_split((hidden_high[...], hidden_low[...]), hidden))
    out = out_ref[...].T
    energy_ref[...] = jnp.sum(value * out, axis=0, keepdims=True)
    slope_ref[...] = dot_split((turn_high[...], turn_low[...]), slope * out)


def message_grads(cotangent, gate_ref, sums_ref, high_ref, low_ref, layer):
    pre = cotangent * gate_ref[...]
    both = dot_split((high_ref[layer], low_ref[layer]), pre)
    half = both.shape[0] // 2
    return [both[:half]] + [both[half:] * sums_ref[i] for i in range(3)]


def radial_grad(left, value):
    high, low = split(value)
    both = dot(left, jnp.concatenate([high, low], axis=0))
    half = both.shape[0] // 2
    return both[:half] + both[half:]


def second_back_kernel(slots, scale, grid_x, hot_ref, weight_ref, turn_high, turn_low, charge_ref,
                       sums_ref, gate_ref, full_charge_ref, energy_ref, slope_ref, *refs):
    folds, refs = refs[:grid_x], refs[grid_x:]
    site_ref, long_ref, cotangent_ref, grad_ref, term_ref, before_ref, after_ref = refs
    atoms = gate_ref.shape[1]
    total = folds[0][...].astype(F32)
    for part in folds[1:]:
        total = total + part[...].astype(F32)
    wide = full_charge_ref.shape[0]
    potential = total[:wide] * (2.0 * scale)
    slopes = total[wide : wide + 3] + total[wide + 3 : wide + 6] + total[wide + 6 : wide + 9]
    long_ref[...] = jnp.concatenate(
        [slopes * (2.0 * scale), jnp.zeros((5, atoms), F32)], axis=0
    )
    site_ref[0] = energy_ref[...] + 0.5 * jnp.sum(
        full_charge_ref[...] * potential, axis=0, keepdims=True
    )
    high, low = split(potential)
    turned = ((0,), (0,))
    cotangent = slope_ref[...] + (
        dot(charge_ref[0], high, turned)
        + (dot(charge_ref[0], low, turned) + dot(charge_ref[1], high, turned))
    )
    cotangent_ref[...] = cotangent
    grads = message_grads(cotangent, gate_ref, sums_ref, turn_high, turn_low, 1)
    for part in range(4):
        grad_ref[part] = grads[part]
    for n in range(slots):
        lanes = slice(n * atoms, (n + 1) * atoms)
        term = weight_ref[0, :, lanes] * grads[0]
        for part in range(1, 4):
            term = term + weight_ref[part, :, lanes] * grads[part]
        term_ref[:, lanes] = term.astype(BF16)
    for side, out_ref in ((0, before_ref), (2, after_ref)):
        for b in range(3):
            start = (3 * side + b) * atoms
            out_ref[b] = dot(term_ref[...], hot_ref[:, start : start + atoms]).astype(BF16)


def second_middle_kernel(hot_ref, term_ref, cotangent_ref, middle_ref):
    atoms = cotangent_ref.shape[1]
    for b in range(3):
        grad = dot(term_ref[...], hot_ref[:, (3 + b) * atoms : (4 + b) * atoms])
        middle_ref[b] = grad + cotangent_ref[...] if b == 1 else grad


def second_edge_kernel(slots, back_ref, feature_ref, grad_ref, edge_ref):
    atoms = grad_ref.shape[2]
    for n in range(slots):
        lanes = slice(n * atoms, (n + 1) * atoms)
        feature = feature_ref[:, lanes].astype(F32)
        for part in range(4):
            edge_ref[8 * part : 8 * part + 8, lanes] = radial_grad(
                back_ref[1 if part else 0], grad_ref[part] * feature
            )


def first_back_kernel(slots, ids_ref, basis_ref, slope_ref, unit_ref, kind_high, kind_low,
                      turn_high, turn_low, sums_ref, gate_ref, edge_ref, long_ref, middle_ref,
                      *refs):
    from_x, from_y, outs = refs[:2], refs[2:4], refs[4:]
    atoms = gate_ref.shape[1]
    cotangent = middle_ref[1]
    for block in (from_x[0][1], from_x[1][1], from_y[0][...], from_y[1][...]):
        cotangent = cotangent + block.astype(F32)
    grads = message_grads(cotangent, gate_ref, sums_ref, turn_high, turn_low, 0)
    unit = unit_ref[...]
    kinds = unit[4:5]
    by_kind = [dot_split((kind_high[0], kind_low[0]), grads[0])]
    by_kind += [dot_split((kind_high[1], kind_low[1]), grads[i]) for i in range(1, 4)]
    species = by_kind[0].shape[0] // 8
    edges = [[] for _ in range(4)]
    for n in range(slots):
        kind = jnp.broadcast_to(kinds[:, n * atoms : (n + 1) * atoms], (8, atoms))
        matches = [kind == float(k) for k in range(1, species)]
        for part in range(4):
            rows = by_kind[part]
            found = rows[:8]
            for k, match in enumerate(matches):
                found = jnp.where(match, rows[8 * k + 8 : 8 * k + 16], found)
            edges[part].append(found)
    edges = [
        edge_ref[8 * part : 8 * part + 8] + jnp.concatenate(edges[part], axis=1) for part in range(4)
    ]
    basis = basis_ref[...]
    units = [unit[i : i + 1] for i in range(3)]
    inverse = unit[3:4]
    by_basis = edges[0]
    for i in range(3):
        by_basis = by_basis + edges[i + 1] * units[i]
    by_unit = [jnp.sum(edges[i + 1] * basis, axis=0, keepdims=True) * inverse for i in range(3)]
    by_distance = jnp.sum(by_basis * slope_ref[...], axis=0, keepdims=True)
    for i in range(3):
        by_distance = by_distance - by_unit[i] * units[i]
    moves = [by_unit[i] + by_distance * units[i] for i in range(3)]
    zero = jnp.zeros_like(moves[0])
    move = jnp.concatenate(moves + [zero] * 5, axis=0)
    own = long_ref[...]
    for n in range(slots):
        own = own - move[:, n * atoms : (n + 1) * atoms]
    ids = ids_ref[...]
    lane_hot = hot_columns(ids & 127, 128)
    half = ids >> 7
    high = move.astype(BF16).astype(F32)
    both = jnp.concatenate([high, move - high], axis=0)
    per_cell = atoms // 128
    rows = jnp.concatenate(
        [jnp.where(half == h, both, 0.0).astype(BF16) for h in range(9 * per_cell)], axis=0
    )
    spread = dot(rows, lane_hot, ((1,), (1,)))
    for cell in range(9):
        found = []
        for h in range(cell * per_cell, (cell + 1) * per_cell):
            found.append(spread[16 * h : 16 * h + 8] + spread[16 * h + 8 : 16 * h + 16])
        grad = jnp.concatenate(found, axis=1)
        if cell == CENTRE:
            grad = own + grad
        outs[cell // 3][cell % 3] = grad


def pair_counts(parts):
    total = WAVE_REACH + WAVE_REACH * (2 * WAVE_REACH + 1)
    share = -(-total // parts)
    return total, share, -(-share // 16) * 16


def pair_vectors(slot, share, part):
    side = 2 * WAVE_REACH + 1
    total = WAVE_REACH + WAVE_REACH * side
    index = slot + part.astype(F32) * share
    later = index - WAVE_REACH
    row = jnp.floor((later + 0.5) * (1.0 / side))
    first = index < WAVE_REACH
    kx = jnp.where(first, 0.0, row + 1.0)
    ky = jnp.where(first, index + 1.0, later - row * side - WAVE_REACH)
    valid = jnp.where((slot < share) & (index < total), 1.0, 0.0)
    return kx, ky, valid


def count_up(rows):
    return lax.broadcasted_iota(jnp.int32, (rows, 1), 0).astype(F32)


def green_weights(share, padded, grid, place_ref, vec_ref, weight_ref):
    grid_x, grid_y = grid
    turn = 2.0 * math.pi
    side = 2 * WAVE_REACH + 1
    top = side * side * side - 1
    vec = vec_ref[...].astype(F32) + WAVE_REACH
    code = (vec[0:1] * side + vec[1:2]) * side + vec[2:3]
    code = jnp.maximum(code, top - code)
    span = 8 * share
    row = count_up(span)
    slot = jnp.floor(row * 0.125)
    height = row - 8.0 * slot + 1.0
    flat = count_up(padded)
    slot = jnp.concatenate([slot, slot, flat], axis=0)
    kz = jnp.concatenate([height, -height, jnp.zeros_like(flat)], axis=0)
    kx, ky, valid = pair_vectors(slot, share, place_ref[0])
    own = ((kx + WAVE_REACH) * side + ky + WAVE_REACH) * side + kz + WAVE_REACH
    seen = jnp.zeros((own.shape[0], 128), F32)
    for start in range(0, code.shape[1], 128):
        seen = seen + jnp.where(own == code[:, start : start + 128], 1.0, 0.0)
    count = jnp.sum(seen, axis=1, keepdims=True) * valid
    sq = (
        (kx * (turn / (grid_x * cell_width))) ** 2
        + (ky * (turn / (grid_y * cell_width))) ** 2
        + (kz * (turn / box_height)) ** 2
    )
    green = jnp.exp(-smear_width * sq) / (sq + screen * screen) * count
    weight_ref[...] = jnp.broadcast_to(green, weight_ref.shape)


def basis_rows(share, ca, sa, cb, sb):
    cc, ss, sc, cs = [], [], [], []
    for p in range(share):
        c, s = ca[p : p + 1], sa[p : p + 1]
        cc.append(c * cb)
        ss.append(s * sb)
        sc.append(s * cb)
        cs.append(c * sb)
    return cc, ss, sc, cs


def unpack_rows(block):
    half = block.shape[1] // 2
    return jnp.concatenate([block[:, :half], block[:, half:]], axis=0)


def pack_rows(block):
    half = block.shape[0] // 2
    return jnp.concatenate([block[:half], block[half:]], axis=1)


def structure_kernel(share, padded, grid, wide, place_ref, *refs):
    grid_x, grid_y = grid
    blocks, (ca_ref, sa_ref, cb_ref, sb_ref, high_ref, low_ref, own_ref, out_ref) = (
        refs[:grid_x],
        refs[grid_x:],
    )
    col = place_ref[1].astype(F32) * (1.0 / grid_y)
    kx, ky, _ = pair_vectors(count_up(padded), share, place_ref[0])
    kz = count_up(8) + 1.0
    total = None
    for d in range(grid_x):
        block = blocks[d][...]
        charge = block[:wide]
        atoms = charge.shape[1]
        pieces = block[wide:].astype(F32)
        place = pieces[0:3] + (pieces[3:6] + pieces[6:9])
        row = lax.rem(place_ref[0] + d, grid_x).astype(F32) * (1.0 / grid_x)
        x = place[0:1] * (1.0 / (grid_x * cell_width)) + row
        y = place[1:2] * (1.0 / (grid_y * cell_width)) + col
        sa, ca = sin_cos(kx * x + ky * y)
        sb, cb = sin_cos(kz * (place[2:3] * (1.0 / box_height)))
        lanes = pl.ds(d * atoms, atoms)
        ca_ref[:, lanes] = ca
        sa_ref[:, lanes] = sa
        cb_ref[:, lanes] = cb
        sb_ref[:, lanes] = sb
        cc, ss, sc, cs = basis_rows(share, ca, sa, cb, sb)
        high, low = split(jnp.concatenate(cc + ss + sc + cs + [ca, sa], axis=0))
        high_ref[:, lanes] = high
        low_ref[:, lanes] = low
        term = dot(high, charge, ((1,), (1,))) + dot(low, charge, ((1,), (1,)))
        total = term if total is None else total + term
    packed = pack_rows(total)
    own_ref[...] = packed
    out_ref[...] = packed.astype(BF16)


def fold_kernel(share, padded, grid, wide, place_ref, ca_ref, sa_ref, cb_ref, sb_ref, high_ref,
                low_ref, weight_ref, *refs):
    grid_x, grid_y = grid
    blocks, parts, outs = refs[:grid_x], refs[grid_x : grid_x + grid_y], refs[grid_x + grid_y :]
    turn = 2.0 * math.pi
    packed = parts[0][...].astype(F32)
    for part in parts[1:]:
        packed = packed + part[...].astype(F32)
    struct = unpack_rows(packed)
    span = 8 * share
    cc, ss, sc, cs = (struct[i * span : (i + 1) * span] for i in range(4))
    weight = weight_ref[:, :wide]
    plus, minus, flat = weight[:span], weight[span : 2 * span], weight[2 * span :]
    re_plus, im_plus = plus * (cc - ss), plus * (sc + cs)
    re_minus, im_minus = minus * (cc + ss), minus * (sc - cs)
    rows = jnp.concatenate(
        [
            re_plus + re_minus,
            re_minus - re_plus,
            im_plus + im_minus,
            im_plus - im_minus,
            flat * struct[4 * span : 4 * span + padded],
            flat * struct[4 * span + padded :],
        ],
        axis=0,
    )
    row_high, row_low = split(rows)
    row_pair = jnp.concatenate([row_high, row_low], axis=1)
    turned = rows.T
    t_high, t_low = split(turned)
    t_both = jnp.concatenate([t_high, t_low], axis=0)
    kx, ky, _ = pair_vectors(count_up(padded), share, place_ref[0])
    kx = kx * (turn / (grid_x * cell_width))
    ky = ky * (turn / (grid_y * cell_width))
    kz = (count_up(8) + 1.0) * (turn / box_height)
    for d in range(grid_x):
        charge = blocks[d][:wide]
        atoms = charge.shape[1]
        lanes = pl.ds(d * atoms, atoms)
        ca, sa, cb, sb = ca_ref[:, lanes], sa_ref[:, lanes], cb_ref[:, lanes], sb_ref[:, lanes]
        bcc, bss, bsc, bcs = basis_rows(share, ca, sa, cb, sb)
        high, low = high_ref[:, lanes], low_ref[:, lanes]
        both = dot(t_both, high)
        pot = both[:wide] + both[wide:] + dot(t_high, low)
        proj = dot(row_pair, jnp.concatenate([charge, charge], axis=0))
        by_x = jnp.zeros((8, atoms), jnp.float32)
        by_y = jnp.zeros((8, atoms), jnp.float32)
        by_z = jnp.zeros((8, atoms), jnp.float32)
        for p in range(share):
            pcc, pss, psc, pcs = (
                proj[i * span + 8 * p : i * span + 8 * p + 8] for i in range(4)
            )
            slope = bcs[p] * pss - bsc[p] * pcc + bcc[p] * psc - bss[p] * pcs
            by_x = by_x + kx[p : p + 1] * slope
            by_y = by_y + ky[p : p + 1] * slope
            by_z = by_z + (bsc[p] * pss - bcs[p] * pcc - bss[p] * psc + bcc[p] * pcs)
        flat_slope = ca * proj[4 * span + padded :] - sa * proj[4 * span : 4 * span + padded]
        grad_x = jnp.sum(by_x, axis=0, keepdims=True) + jnp.sum(kx * flat_slope, axis=0, keepdims=True)
        grad_y = jnp.sum(by_y, axis=0, keepdims=True) + jnp.sum(ky * flat_slope, axis=0, keepdims=True)
        grad_z = jnp.sum(kz * by_z, axis=0, keepdims=True)
        slopes = jnp.concatenate([grad_x, grad_y, grad_z], axis=0)
        high = slopes.astype(BF16).astype(F32)
        rest = slopes - high
        middle = rest.astype(BF16).astype(F32)
        zero = jnp.zeros((outs[d].shape[0] - wide - 9, atoms), F32)
        block = jnp.concatenate([pot, high, middle, rest - middle, zero], axis=0)
        outs[d][...] = block.astype(outs[d].dtype)


def per_device(
    positions,
    species,
    neighbours,
    counts,
    species_embed,
    radial,
    mixing,
    read_hidden,
    read_out,
    charge_map,
    wavevectors,
):
    atoms = positions.shape[3]
    slots = neighbours.shape[3]
    features, lat_width = charge_map.shape
    wave_count = wavevectors.shape[1]
    grid = lax.axis_size("gx"), lax.axis_size("gy")
    grid_x, grid_y = grid
    edges = slots * atoms
    scale = 1.0 / math.sqrt(wave_count * lat_width * atoms * grid_x * grid_y)
    place = jnp.stack([lax.axis_index("gx"), lax.axis_index("gy")]).astype(jnp.int32)
    _, share, padded = pair_counts(grid_x)
    ids = neighbours.transpose(0, 3, 1, 2).reshape(1, edges)
    dma = pltpu.SemaphoreType.DMA
    shown = positions.transpose(0, 2, 1, 3)

    (own,) = run(
        pack_kernel,
        [shape(4 * atoms // 128, 128)],
        [shown, species],
        scratch=[
            pltpu.VMEM(shown.shape, F32),
            pltpu.VMEM(species.shape, jnp.int32),
            dma((2,)),
        ],
        hbm=2,
        grant=60,
        name="pack",
    )
    norm = 1.0 / math.sqrt(slots)
    kind_rows = 8 * species_embed.shape[0]
    low_pair = lambda *dims: [shape(*dims, dtype=BF16)] * 2
    (ids, counts, embed, kind_left, left, back, kind_high, kind_low, mix_high, mix_low, turn_high,
     turn_low) = run(
        functools.partial(prep_first_kernel, norm),
        [
            shape(1, edges, dtype=jnp.int32),
            shape(*counts.shape, dtype=jnp.int32),
            shape(features, 32, dtype=BF16),
            shape(2, features, 4 * kind_rows, dtype=BF16),
            shape(2, features, 32, dtype=BF16),
            shape(2, 16, 2 * features, dtype=BF16),
        ]
        + low_pair(2, kind_rows, features)
        + low_pair(2, features, 2 * features)
        + low_pair(2, 2 * features, features),
        [ids, counts, species_embed, radial, mixing],
        scratch=[
            pltpu.VMEM(species_embed.shape, F32),
            pltpu.VMEM(radial.shape, F32),
            pltpu.VMEM(mixing.shape, F32),
            dma((5,)),
        ],
        hbm=5,
        name="prep_first",
    )
    cells, (ids, place) = around(own, (ids, place))
    (hot,) = run(
        hot_kernel, [shape(9 * atoms, edges, dtype=BF16)], [ids], flops=2_000_000_000, name="hot"
    )
    read_out, hidden_high, hidden_low, hidden_turn_high, hidden_turn_low, charge_pair = run(
        prep_second_kernel,
        [shape(1, features)]
        + low_pair(features, features)
        + low_pair(features, features)
        + [shape(2, lat_width, features, dtype=BF16)],
        [read_out[None, :], read_hidden, charge_map.T],
        scratch=[
            pltpu.VMEM(read_hidden.shape, F32),
            pltpu.VMEM((lat_width, features), F32),
            dma((3,)),
        ],
        hbm=3,
        name="prep_second",
    )
    (weight,) = run(
        functools.partial(green_weights, share, padded, grid),
        [shape(16 * share + padded, 128)],
        [place, wavevectors],
        smem=1,
        name="green",
    )
    low, basis, slope, unit, sums_one, gate_one = run(
        functools.partial(first_kernel, slots),
        [
            shape(features, atoms, dtype=BF16),
            shape(8, edges),
            shape(8, edges),
            shape(8, edges),
            shape(3, features, atoms),
            shape(features, atoms),
        ],
        [ids, counts, embed, kind_left, mix_high, mix_low] + cells,
        name="first",
    )
    hidden, hot = around(low, hot)
    edge_weights, near = run(
        functools.partial(second_near_kernel, slots),
        [shape(4, features, edges), shape(features, edges)],
        [basis, unit, left, hot, hidden[1]],
        flops=2_000_000_000,
        name="second_near",
    )
    (near,) = run(
        functools.partial(second_side_kernel, slots),
        [shape(features, edges)],
        [hot, near, hidden[2]],
        flops=1_000_000_000,
        name="second_side",
    )
    block_rows = -(-(lat_width + 9) // 16) * 16
    feature, sums_two, gate_two, packed, charge, energy, energy_slope = run(
        functools.partial(second_kernel, slots),
        [
            shape(features, edges, dtype=BF16),
            shape(3, features, atoms),
            shape(features, atoms),
            shape(block_rows, atoms, dtype=BF16),
            shape(lat_width, atoms),
            shape(1, atoms),
            shape(features, atoms),
        ],
        [hot, edge_weights, near, mix_high, mix_low, hidden_high, hidden_low, hidden_turn_high,
         hidden_turn_low, read_out, charge_pair, cells[1], hidden[1], hidden[0]],
        name="second",
    )
    charges = [packed] + [shifted(packed, d, 0) for d in range(1, grid_x)]
    (hot_back,) = run(
        hot_back_kernel,
        [shape(edges, 9 * atoms, dtype=BF16)],
        [ids],
        flops=2_000_000_000,
        name="hot_back",
    )
    charges, hot_back = lax.optimization_barrier((charges, hot_back))
    span = grid_x * atoms
    rows = 32 * share + 2 * padded
    *phases, own_part, part = run(
        functools.partial(structure_kernel, share, padded, grid, lat_width),
        [
            shape(padded, span),
            shape(padded, span),
            shape(8, span),
            shape(8, span),
            shape(rows, span, dtype=BF16),
            shape(rows, span, dtype=BF16),
            shape(rows // 2, 2 * lat_width),
            shape(rows // 2, 2 * lat_width, dtype=BF16),
        ],
        [place] + charges,
        smem=1,
        name="structure",
    )
    parts = [own_part] + [shifted(part, 0, d) for d in range(1, grid_y)]
    folds = run(
        functools.partial(fold_kernel, share, padded, grid, lat_width),
        [shape(block_rows, atoms)] + [shape(block_rows, atoms, dtype=BF16)] * (grid_x - 1),
        [place] + phases + [weight] + charges + parts,
        smem=1,
        name="fold",
    )
    folds = [folds[0]] + [shifted(folds[d], -d, 0) for d in range(1, grid_x)]

    site, long, cotangent, grads, term, before, after = run(
        functools.partial(second_back_kernel, slots, scale, grid_x),
        [
            shape(1, 1, atoms),
            shape(8, atoms),
            shape(features, atoms),
            shape(4, features, atoms),
            shape(features, edges, dtype=BF16),
            shape(3, features, atoms, dtype=BF16),
            shape(3, features, atoms, dtype=BF16),
        ],
        [hot_back, edge_weights, turn_high, turn_low, charge_pair, sums_two, gate_two, charge, energy,
         energy_slope] + folds,
        name="second_back",
    )
    from_x = [shifted(after, -1, 0), shifted(before, 1, 0)]
    (middle,) = run(
        second_middle_kernel,
        [shape(3, features, atoms)],
        [hot_back, term, cotangent],
        flops=1_000_000_000,
        name="second_middle",
    )
    sides = [
        (middle[b] + from_x[0][b].astype(F32) + from_x[1][b].astype(F32)).astype(BF16)
        for b in (0, 2)
    ]
    from_y = [shifted(sides[1], 0, -1), shifted(sides[0], 0, 1)]
    (edge,) = run(
        functools.partial(second_edge_kernel, slots),
        [shape(32, edges)],
        [back, feature, grads],
        flops=1_000_000_000,
        name="second_edge",
    )
    before, middle, after = run(
        functools.partial(first_back_kernel, slots),
        [shape(3, 8, atoms)] * 3,
        [ids, basis, slope, unit, kind_high, kind_low, turn_high, turn_low, sums_one, gate_one, edge,
         long, middle] + from_x + from_y,
        name="first_back",
    )
    total = middle + shifted(after, -1, 0) + shifted(before, 1, 0)
    total = total[1] + shifted(total[2], 0, -1) + shifted(total[0], 0, 1)
    forces = -total[None, :3, None, :]
    return (forces.transpose(0, 2, 1, 3), site)


def solution(mesh):
    in_specs = (
        P("gx", "gy", None, None),
        P("gx", "gy", None),
        P("gx", "gy", None, None),
        P("gx", "gy", None),
        P(),
        P(),
        P(),
        P(),
        P(),
        P(),
        P(),
    )
    out_specs = (P("gx", "gy", None, None), P("gx", "gy", None))
    return jax.shard_map(
        per_device, mesh=mesh, in_specs=in_specs, out_specs=out_specs, check_vma=False
    )
```

```python
import functools
import math

import jax
import jax.numpy as jnp
import numpy as np
from jax import lax
from jax.experimental import pallas as pl
from jax.experimental.pallas import tpu as pltpu
from jax.sharding import PartitionSpec as P

cell_width = 10.0
box_height = 30.0
cut_radius = 50.0
soften = 0.25
screen = 0.5
smear_width = 0.5
WAVE_REACH = 8
F32 = jnp.float32
BF16 = jnp.bfloat16
OFFSETS = [(a, b) for a in (-1, 0, 1) for b in (-1, 0, 1)]
CENTRE = 4


def shifted(block, along_x, along_y):
    count_x, count_y = lax.axis_size("gx"), lax.axis_size("gy")
    route = []
    for i in range(count_x):
        for j in range(count_y):
            source = ((i + along_x) % count_x) * count_y + (j + along_y) % count_y
            route.append((source, i * count_y + j))
    return lax.ppermute(block, ("gx", "gy"), route)


def swapped(block):
    count = lax.axis_size("gx")
    return lax.ppermute(block, "gx", [(i ^ 1, i) for i in range(count)])


def around(block, beside):
    column = jnp.stack([shifted(block, 0, -1), block, shifted(block, 0, 1)])
    column, beside = lax.optimization_barrier((column, beside))
    return [shifted(column, -1, 0), column, shifted(column, 1, 0)], beside


def whole(space=pltpu.VMEM):
    return pl.BlockSpec(memory_space=space)


def run(kernel, outs, args, scratch=(), smem=0, hbm=0, flops=10_000_000, grant=16, name=None):
    specs = [whole(pltpu.SMEM)] * smem + [whole(pltpu.HBM)] * hbm
    specs += [whole()] * (len(args) - smem - hbm)
    return list(
        pl.pallas_call(
            kernel,
            out_shape=outs,
            in_specs=specs,
            out_specs=[whole() for _ in outs],
            scratch_shapes=list(scratch),
            compiler_params=pltpu.CompilerParams(vmem_limit_bytes=grant * 1024 * 1024),
            cost_estimate=pl.CostEstimate(
                flops=flops, bytes_accessed=1_000_000, transcendentals=0
            ),
            name=name,
        )(*args)
    )


def shape(*dims, dtype=F32):
    return jax.ShapeDtypeStruct(dims, dtype)


def split(value):
    high = value.astype(BF16)
    return high, (value - high.astype(F32)).astype(BF16)


def dot(left, right, contract=((1,), (0,))):
    return lax.dot_general(left, right, (contract, ((), ())), preferred_element_type=F32)


def dot3(left, right):
    left_high, left_low = split(left)
    right_high, right_low = split(right)
    return dot(left_high, right_high) + (dot(left_high, right_low) + dot(left_low, right_high))


def dot_split(left, right):
    right_high, right_low = split(right)
    return dot(left[0], right_high) + (dot(left[0], right_low) + dot(left[1], right_high))


def sin_cos(turns):
    quarter = jnp.round(turns * 4.0)
    x = (turns - quarter * 0.25) * (2.0 * math.pi)
    z = x * x
    sine = ((-1.9515295891e-4 * z + 8.3321608736e-3) * z - 1.6666654611e-1) * (z * x) + x
    cosine = (2.443315711809948e-5 * z - 1.388731625493765e-3) * z + 4.166664568298827e-2
    cosine = cosine * (z * z) - 0.5 * z + 1.0
    k = quarter.astype(jnp.int32) & 3
    odd = (k & 1) == 1
    by_sine = jnp.where(odd, cosine, sine)
    by_cosine = jnp.where(odd, sine, cosine)
    return (
        jnp.where(k >= 2, -by_sine, by_sine),
        jnp.where((k == 1) | (k == 2), -by_cosine, by_cosine),
    )


def stacked_left(value):
    high = value.astype(BF16).astype(F32)
    rows = jnp.concatenate([high, high, value - high, jnp.zeros_like(high)], axis=0)
    return rows.T.astype(BF16)


def stacked_right(value):
    high = value.astype(BF16).astype(F32)
    return jnp.concatenate([high, value - high, high, jnp.zeros_like(high)], axis=0).astype(BF16)


def silu_pair(value):
    gate = 1.0 / (1.0 + jnp.exp(-value))
    return value * gate, gate * (1.0 + value * (1.0 - gate))


def onehot_kinds(kinds, rows):
    levels = lax.broadcasted_iota(jnp.int32, (rows, kinds.shape[1]), 0).astype(F32)
    return jnp.where(kinds == levels, 1.0, 0.0)


def embedding_stack(embed):
    high = embed.astype(BF16).astype(F32)
    rest = embed - high
    middle = rest.astype(BF16).astype(F32)
    rows = jnp.concatenate([high, middle, rest - middle, jnp.zeros_like(high)], axis=0)
    return rows.T.astype(BF16)


def embedded(stack, kinds):
    hot = onehot_kinds(kinds, 8)
    return dot(stack, jnp.concatenate([hot, hot, hot, jnp.zeros_like(hot)], axis=0).astype(BF16))


def weights_of(stack_ref, part, rows):
    return dot(stack_ref[1 if part else 0], stacked_right(rows))


def mixed(sums, high_ref, low_ref, layer):
    squares = sums[1] * sums[1] + sums[2] * sums[2] + sums[3] * sums[3]
    both = jnp.concatenate([sums[0], squares], axis=0)
    return silu_pair(dot_split((high_ref[layer], low_ref[layer]), both))


def edge_parts(basis, unit):
    return [basis] + [basis * unit[i : i + 1] for i in range(3)]


def pack_kernel(place_ref, position_ref, species_ref, out_ref, place, kind, sems):
    copies = [
        pltpu.make_async_copy(position_ref, place, sems.at[0]),
        pltpu.make_async_copy(species_ref, kind, sems.at[1]),
    ]
    for copy in copies:
        copy.start()
    for copy in copies:
        copy.wait()
    rows = [place[0, i] for i in range(3)] + [kind[0].astype(F32)]
    atoms = rows[0].shape[1]
    out_ref[...] = jnp.concatenate(
        [row[:, s : s + 128] for s in range(0, atoms, 128) for row in rows], axis=0
    )


def radial_left(radial):
    high = radial.astype(BF16).astype(F32)
    low = radial - high
    top = jnp.concatenate([high, high], axis=1)
    end = jnp.concatenate([low, jnp.zeros_like(low)], axis=1)
    return jnp.concatenate([top, end], axis=0).astype(BF16)


def put_split(value, high_ref, low_ref, *at):
    high, low = split(value)
    high_ref[at] = high
    low_ref[at] = low


def fetch(sources, targets, sems):
    copies = [
        pltpu.make_async_copy(source, target, sems.at[i])
        for i, (source, target) in enumerate(zip(sources, targets))
    ]
    for copy in copies:
        copy.start()
    for copy in copies:
        copy.wait()


def prep_first_kernel(norm, ids_in, count_in, embed_in, radial_in, mixing_in, id_ref, count_ref,
                      embed_out, kind_left, left_out, back_out, kind_high, kind_low, mix_high,
                      mix_low, turn_high, turn_low, embed_ref, radial_ref, mixing_ref, sems):
    fetch(
        [ids_in, count_in, embed_in, radial_in, mixing_in],
        [id_ref, count_ref, embed_ref, radial_ref, mixing_ref],
        sems,
    )
    embed = embed_ref[...]
    kinds = embed.shape[0]
    for path in range(2):
        radial = radial_ref[0, path] * norm
        rows = jnp.concatenate([radial * embed[s : s + 1] for s in range(kinds)], axis=0)
        kind_left[path] = stacked_left(rows)
        put_split(rows, kind_high, kind_low, path)
        radial = radial_ref[1, path] * norm
        left_out[path] = stacked_left(radial)
        back_out[path] = radial_left(radial)
    for layer in range(2):
        scalar, vector = mixing_ref[layer, 0], mixing_ref[layer, 1]
        put_split(jnp.concatenate([scalar.T, vector.T], axis=1), mix_high, mix_low, layer)
        put_split(jnp.concatenate([scalar, 2.0 * vector], axis=0), turn_high, turn_low, layer)
    embed = jnp.concatenate([embed, jnp.zeros((8 - kinds, embed.shape[1]), F32)], axis=0)
    embed_out[...] = embedding_stack(embed)


def prep_second_kernel(read_in, hidden_in, charge_in, read_ref, hidden_high, hidden_low,
                       hidden_turn_high, hidden_turn_low, charge_pair, hidden_ref, charge_ref, sems):
    fetch([read_in, hidden_in, charge_in], [read_ref, hidden_ref, charge_ref], sems)
    put_split(hidden_ref[...].T, hidden_high, hidden_low, Ellipsis)
    put_split(hidden_ref[...], hidden_turn_high, hidden_turn_low, Ellipsis)
    charge = charge_ref[...]
    high = charge.astype(BF16).astype(F32)
    charge_pair[0] = high.astype(BF16)
    charge_pair[1] = (charge - high).astype(BF16)


def hot_kernel(ids_ref, hot_ref):
    edges = ids_ref.shape[1]
    for start in range(0, edges, 256):
        lanes = slice(start, start + 256)
        hot_ref[:, lanes] = hot_columns(ids_ref[:, lanes], hot_ref.shape[0])


def hot_back_kernel(ids_ref, hot_ref):
    edges = ids_ref.shape[1]
    entry = lax.broadcasted_iota(jnp.int32, (128, hot_ref.shape[1]), 1).astype(F32)
    for start in range(0, edges, 128):
        row = jnp.broadcast_to(ids_ref[:, start : start + 128].astype(F32), (8, 128))
        column = row.T[:, 0:1]
        hot_ref[start : start + 128] = jnp.where(column == entry, 1.0, 0.0).astype(BF16)


def unfold_block(block, atoms):
    parts = atoms // 128
    return jnp.concatenate([block[4 * s : 4 * s + 4] for s in range(parts)], axis=1)


def first_kernel(slots, ids_ref, count_ref, embed_ref, kind_left, mix_high, mix_low, before_ref,
                 column_ref, after_ref, low_ref, basis_ref, slope_ref, unit_ref, sums_ref,
                 gate_ref):
    atoms = low_ref.shape[1]
    ids = ids_ref[...]
    frame = [before_ref, column_ref, after_ref]
    own = unfold_block(column_ref[1], atoms)
    own = jnp.concatenate([own, jnp.zeros_like(own)], axis=0)
    per_cell = atoms // 128
    places = lax.broadcasted_iota(jnp.int32, (4 * per_cell, 128), 0)
    upper = places >> 2
    kind_of_row = places & 3
    rows = []
    for a, b in OFFSETS:
        move = jnp.where(kind_of_row == 0, a * cell_width, 0.0)
        move = move + jnp.where(kind_of_row == 1, b * cell_width, 0.0)
        rows.append(frame[a + 1][b + 1] + move)
    pieces = []
    for start in range(0, ids.shape[1], 128):
        part = jnp.broadcast_to(ids[:, start : start + 128], places.shape)
        lane, half = part & 127, (part >> 7) - upper
        found = jnp.zeros(places.shape, F32)
        for cell, block in enumerate(rows):
            value = jnp.take_along_axis(block, lane, axis=1)
            found = jnp.where(half == per_cell * cell, value, found)
        total = found[:4]
        for s in range(1, per_cell):
            total = total + found[4 * s : 4 * s + 4]
        pieces.append(jnp.concatenate([total, total], axis=0))
    found = jnp.concatenate(pieces, axis=1)
    relative = found - jnp.concatenate([own] * slots, axis=1)
    rel = [relative[i : i + 1] for i in range(3)]
    distance = jnp.sqrt(rel[0] * rel[0] + rel[1] * rel[1] + rel[2] * rel[2] + soften)
    inverse = 1.0 / distance
    order = (lax.broadcasted_iota(jnp.int32, (8, 1), 0) + 1).astype(F32)
    sine, cosine = sin_cos((order * (0.5 / cut_radius)) * distance)
    wave = sine / ((order * (math.pi / cut_radius)) * distance)
    count = count_ref[0]
    live = jnp.concatenate([jnp.where(count > n, 1.0, 0.0) for n in range(slots)], axis=1)
    basis = wave * live
    basis_ref[...] = basis
    slope_ref[...] = (cosine - wave) * (inverse * live)
    kinds = found[3:4]
    unit = jnp.concatenate(
        [r * inverse for r in rel] + [inverse, kinds] + [jnp.zeros_like(kinds)] * 3, axis=0
    )
    unit_ref[...] = unit
    stack = embed_ref[...]
    parts = edge_parts(basis, unit)
    species = kind_left.shape[2] // 32
    by_kind = [[None] * species for _ in range(4)]
    for n in range(slots):
        lanes = slice(n * atoms, (n + 1) * atoms)
        kind = jnp.broadcast_to(kinds[:, lanes], (8, atoms))
        for k in range(species):
            match = kind == float(k)
            for part in range(4):
                term = jnp.where(match, parts[part][:, lanes], 0.0)
                old = by_kind[part][k]
                by_kind[part][k] = term if old is None else old + term
    stacks = [stacked_right(jnp.concatenate(rows, axis=0)) for rows in by_kind]
    vectors = dot(kind_left[1], jnp.concatenate(stacks[1:], axis=1))
    sums = [dot(kind_left[0], stacks[0])]
    sums += [vectors[:, i * atoms : (i + 1) * atoms] for i in range(3)]
    step, gate = mixed(sums, mix_high, mix_low, 0)
    low_ref[...] = (embedded(stack, own[3:4]) + step).astype(BF16)
    for part in range(3):
        sums_ref[part] = sums[part + 1]
    gate_ref[...] = gate


def hot_columns(ids, rows):
    place = lax.broadcasted_iota(jnp.int32, (rows, ids.shape[1]), 0)
    return jnp.where(ids == place, 1.0, 0.0).astype(BF16)


def second_near_kernel(slots, basis_ref, unit_ref, left_ref, hot_ref, column_ref, weight_ref,
                       near_ref):
    atoms = column_ref.shape[2]
    parts = edge_parts(basis_ref[...], unit_ref[...])
    source = jnp.concatenate([column_ref[b] for b in range(3)], axis=1)
    for n in range(slots):
        lanes = slice(n * atoms, (n + 1) * atoms)
        for part in range(4):
            weight_ref[part, :, lanes] = weights_of(left_ref, part, parts[part][:, lanes])
        near_ref[:, lanes] = dot(source, hot_ref[3 * atoms : 6 * atoms, lanes])


def second_side_kernel(slots, hot_ref, near_ref, after_ref, out_ref):
    atoms = after_ref.shape[2]
    source = jnp.concatenate([after_ref[b] for b in range(3)], axis=1)
    for n in range(slots):
        lanes = slice(n * atoms, (n + 1) * atoms)
        out_ref[:, lanes] = near_ref[:, lanes] + dot(source, hot_ref[6 * atoms :, lanes])


def second_kernel(slots, hot_ref, weight_ref, near_ref, mix_high, mix_low, hidden_high, hidden_low,
                  turn_high, turn_low, out_ref, charge_ref, cell_ref, column_ref, before_ref,
                  feature_ref, sums_ref, gate_ref, packed_ref, full_charge_ref, energy_ref,
                  slope_ref):
    atoms = column_ref.shape[2]
    source = jnp.concatenate([before_ref[b] for b in range(3)], axis=1)
    sums = [None] * 4
    for n in range(slots):
        lanes = slice(n * atoms, (n + 1) * atoms)
        feature = near_ref[:, lanes] + dot(source, hot_ref[: 3 * atoms, lanes])
        feature_ref[:, lanes] = feature.astype(BF16)
        for part in range(4):
            term = weight_ref[part, :, lanes] * feature
            sums[part] = term if sums[part] is None else sums[part] + term
    step, gate = mixed(sums, mix_high, mix_low, 1)
    hidden = column_ref[1].astype(F32) + step
    for part in range(3):
        sums_ref[part] = sums[part + 1]
    gate_ref[...] = gate
    charge = dot_split((charge_ref[0], charge_ref[1]), hidden)
    full_charge_ref[...] = charge
    place = unfold_block(cell_ref[1], atoms)[:3]
    high = place.astype(BF16).astype(F32)
    rest = place - high
    middle = rest.astype(BF16).astype(F32)
    zero = jnp.zeros((packed_ref.shape[0] - charge.shape[0] - 9, atoms), F32)
    packed_ref[...] = jnp.concatenate([charge, high, middle, rest - middle, zero], axis=0).astype(
        BF16
    )
    value, slope = silu_pair(dot_split((hidden_high[...], hidden_low[...]), hidden))
    out = out_ref[...].T
    energy_ref[...] = jnp.sum(value * out, axis=0, keepdims=True)
    slope_ref[...] = dot_split((turn_high[...], turn_low[...]), slope * out)


def message_grads(cotangent, gate_ref, sums_ref, high_ref, low_ref, layer):
    pre = cotangent * gate_ref[...]
    both = dot_split((high_ref[layer], low_ref[layer]), pre)
    half = both.shape[0] // 2
    return [both[:half]] + [both[half:] * sums_ref[i] for i in range(3)]


def radial_grad(left, value):
    high, low = split(value)
    both = dot(left, jnp.concatenate([high, low], axis=0))
    half = both.shape[0] // 2
    return both[:half] + both[half:]


def second_back_kernel(slots, scale, count, hot_ref, weight_ref, turn_high, turn_low, charge_ref,
                       sums_ref, gate_ref, full_charge_ref, energy_ref, slope_ref, *refs):
    folds, refs = refs[:count], refs[count:]
    site_ref, long_ref, cotangent_ref, grad_ref, term_ref, before_ref, after_ref = refs
    atoms = gate_ref.shape[1]
    total = folds[0][...].astype(F32)
    for part in folds[1:]:
        total = total + part[...].astype(F32)
    wide = full_charge_ref.shape[0]
    potential = total[:wide] * (2.0 * scale)
    slopes = total[wide : wide + 3] + total[wide + 3 : wide + 6] + total[wide + 6 : wide + 9]
    long_ref[...] = jnp.concatenate(
        [slopes * (2.0 * scale), jnp.zeros((5, atoms), F32)], axis=0
    )
    site_ref[0] = energy_ref[...] + 0.5 * jnp.sum(
        full_charge_ref[...] * potential, axis=0, keepdims=True
    )
    high, low = split(potential)
    turned = ((0,), (0,))
    cotangent = slope_ref[...] + (
        dot(charge_ref[0], high, turned)
        + (dot(charge_ref[0], low, turned) + dot(charge_ref[1], high, turned))
    )
    cotangent_ref[...] = cotangent
    grads = message_grads(cotangent, gate_ref, sums_ref, turn_high, turn_low, 1)
    for part in range(4):
        grad_ref[part] = grads[part]
    for n in range(slots):
        lanes = slice(n * atoms, (n + 1) * atoms)
        term = weight_ref[0, :, lanes] * grads[0]
        for part in range(1, 4):
            term = term + weight_ref[part, :, lanes] * grads[part]
        term_ref[:, lanes] = term.astype(BF16)
    for side, out_ref in ((0, before_ref), (2, after_ref)):
        for b in range(3):
            start = (3 * side + b) * atoms
            out_ref[b] = dot(term_ref[...], hot_ref[:, start : start + atoms]).astype(BF16)


def second_middle_kernel(hot_ref, term_ref, cotangent_ref, middle_ref):
    atoms = cotangent_ref.shape[1]
    for b in range(3):
        grad = dot(term_ref[...], hot_ref[:, (3 + b) * atoms : (4 + b) * atoms])
        middle_ref[b] = grad + cotangent_ref[...] if b == 1 else grad


def second_edge_kernel(slots, back_ref, feature_ref, grad_ref, edge_ref):
    atoms = grad_ref.shape[2]
    for n in range(slots):
        lanes = slice(n * atoms, (n + 1) * atoms)
        feature = feature_ref[:, lanes].astype(F32)
        for part in range(4):
            edge_ref[8 * part : 8 * part + 8, lanes] = radial_grad(
                back_ref[1 if part else 0], grad_ref[part] * feature
            )


def first_back_kernel(slots, ids_ref, basis_ref, slope_ref, unit_ref, kind_high, kind_low,
                      turn_high, turn_low, sums_ref, gate_ref, edge_ref, long_ref, middle_ref,
                      *refs):
    from_x, from_y, outs = refs[:2], refs[2:4], refs[4:]
    atoms = gate_ref.shape[1]
    cotangent = middle_ref[1]
    for block in (from_x[0][1], from_x[1][1], from_y[0][...], from_y[1][...]):
        cotangent = cotangent + block.astype(F32)
    grads = message_grads(cotangent, gate_ref, sums_ref, turn_high, turn_low, 0)
    unit = unit_ref[...]
    kinds = unit[4:5]
    by_kind = [dot_split((kind_high[0], kind_low[0]), grads[0])]
    by_kind += [dot_split((kind_high[1], kind_low[1]), grads[i]) for i in range(1, 4)]
    species = by_kind[0].shape[0] // 8
    edges = [[] for _ in range(4)]
    for n in range(slots):
        kind = jnp.broadcast_to(kinds[:, n * atoms : (n + 1) * atoms], (8, atoms))
        matches = [kind == float(k) for k in range(1, species)]
        for part in range(4):
            rows = by_kind[part]
            found = rows[:8]
            for k, match in enumerate(matches):
                found = jnp.where(match, rows[8 * k + 8 : 8 * k + 16], found)
            edges[part].append(found)
    edges = [
        edge_ref[8 * part : 8 * part + 8] + jnp.concatenate(edges[part], axis=1) for part in range(4)
    ]
    basis = basis_ref[...]
    units = [unit[i : i + 1] for i in range(3)]
    inverse = unit[3:4]
    by_basis = edges[0]
    for i in range(3):
        by_basis = by_basis + edges[i + 1] * units[i]
    by_unit = [jnp.sum(edges[i + 1] * basis, axis=0, keepdims=True) * inverse for i in range(3)]
    by_distance = jnp.sum(by_basis * slope_ref[...], axis=0, keepdims=True)
    for i in range(3):
        by_distance = by_distance - by_unit[i] * units[i]
    moves = [by_unit[i] + by_distance * units[i] for i in range(3)]
    zero = jnp.zeros_like(moves[0])
    move = jnp.concatenate(moves + [zero] * 5, axis=0)
    own = long_ref[...]
    for n in range(slots):
        own = own - move[:, n * atoms : (n + 1) * atoms]
    ids = ids_ref[...]
    lane_hot = hot_columns(ids & 127, 128)
    half = ids >> 7
    high = move.astype(BF16).astype(F32)
    both = jnp.concatenate([high, move - high], axis=0)
    per_cell = atoms // 128
    rows = jnp.concatenate(
        [jnp.where(half == h, both, 0.0).astype(BF16) for h in range(9 * per_cell)], axis=0
    )
    spread = dot(rows, lane_hot, ((1,), (1,)))
    for cell in range(9):
        found = []
        for h in range(cell * per_cell, (cell + 1) * per_cell):
            found.append(spread[16 * h : 16 * h + 8] + spread[16 * h + 8 : 16 * h + 16])
        grad = jnp.concatenate(found, axis=1)
        if cell == CENTRE:
            grad = own + grad
        outs[cell // 3][cell % 3] = grad


def pair_counts(parts):
    total = WAVE_REACH + WAVE_REACH * (2 * WAVE_REACH + 1)
    share = -(-total // parts)
    return total, share, -(-share // 16) * 16


def pair_vectors(slot, share, part):
    side = 2 * WAVE_REACH + 1
    total = WAVE_REACH + WAVE_REACH * side
    index = slot + part.astype(F32) * share
    later = index - WAVE_REACH
    row = jnp.floor((later + 0.5) * (1.0 / side))
    first = index < WAVE_REACH
    kx = jnp.where(first, 0.0, row + 1.0)
    ky = jnp.where(first, index + 1.0, later - row * side - WAVE_REACH)
    valid = jnp.where((slot < share) & (index < total), 1.0, 0.0)
    return kx, ky, valid


def count_up(rows):
    return lax.broadcasted_iota(jnp.int32, (rows, 1), 0).astype(F32)


def green_weights(share, padded, grid, place_ref, vec_ref, weight_ref):
    grid_x, grid_y = grid
    turn = 2.0 * math.pi
    side = 2 * WAVE_REACH + 1
    top = side * side * side - 1
    vec = vec_ref[...].astype(F32) + WAVE_REACH
    code = (vec[0:1] * side + vec[1:2]) * side + vec[2:3]
    code = jnp.maximum(code, top - code)
    span = 8 * share
    row = count_up(span)
    slot = jnp.floor(row * 0.125)
    height = row - 8.0 * slot + 1.0
    flat = count_up(padded)
    slot = jnp.concatenate([slot, slot, flat], axis=0)
    kz = jnp.concatenate([height, -height, jnp.zeros_like(flat)], axis=0)
    kx, ky, valid = pair_vectors(slot, share, place_ref[0])
    own = ((kx + WAVE_REACH) * side + ky + WAVE_REACH) * side + kz + WAVE_REACH
    seen = jnp.zeros((own.shape[0], 128), F32)
    for start in range(0, code.shape[1], 128):
        seen = seen + jnp.where(own == code[:, start : start + 128], 1.0, 0.0)
    count = jnp.sum(seen, axis=1, keepdims=True) * valid
    sq = (
        (kx * (turn / (grid_x * cell_width))) ** 2
        + (ky * (turn / (grid_y * cell_width))) ** 2
        + (kz * (turn / box_height)) ** 2
    )
    green = jnp.exp(-smear_width * sq) / (sq + screen * screen) * count
    weight_ref[...] = jnp.broadcast_to(green, weight_ref.shape)


def basis_rows(share, ca, sa, cb, sb):
    cc, ss, sc, cs = [], [], [], []
    for p in range(share):
        c, s = ca[p : p + 1], sa[p : p + 1]
        cc.append(c * cb)
        ss.append(s * sb)
        sc.append(s * cb)
        cs.append(c * sb)
    return cc, ss, sc, cs


def unpack_rows(block):
    half = block.shape[1] // 2
    return jnp.concatenate([block[:, :half], block[:, half:]], axis=0)


def pack_rows(block):
    half = block.shape[0] // 2
    return jnp.concatenate([block[:half], block[half:]], axis=1)


def structure_kernel(share, padded, grid, wide, flip, place_ref, blocks, *refs):
    grid_x, grid_y = grid
    if flip:
        near_ref, (ca_ref, sa_ref, cb_ref, sb_ref, high_ref, low_ref, own_ref, out_ref) = (
            refs[0],
            refs[1:],
        )
        total = near_ref[...]
    else:
        ca_ref, sa_ref, cb_ref, sb_ref, high_ref, low_ref, total_ref = refs
        total = None
    col = place_ref[1].astype(F32) * (1.0 / grid_y)
    first = place_ref[0] ^ flip
    kx, ky, _ = pair_vectors(count_up(padded), share, place_ref[0])
    kz = count_up(8) + 1.0
    for d in range(grid_x // 2):
        block = blocks[d]
        charge = block[:wide]
        atoms = charge.shape[1]
        pieces = block[wide:].astype(F32)
        place = pieces[0:3] + (pieces[3:6] + pieces[6:9])
        row = lax.rem(first + 2 * d, grid_x).astype(F32) * (1.0 / grid_x)
        x = place[0:1] * (1.0 / (grid_x * cell_width)) + row
        y = place[1:2] * (1.0 / (grid_y * cell_width)) + col
        sa, ca = sin_cos(kx * x + ky * y)
        sb, cb = sin_cos(kz * (place[2:3] * (1.0 / box_height)))
        lanes = pl.ds(d * atoms, atoms)
        ca_ref[:, lanes] = ca
        sa_ref[:, lanes] = sa
        cb_ref[:, lanes] = cb
        sb_ref[:, lanes] = sb
        cc, ss, sc, cs = basis_rows(share, ca, sa, cb, sb)
        high, low = split(jnp.concatenate(cc + ss + sc + cs + [ca, sa], axis=0))
        high_ref[:, lanes] = high
        low_ref[:, lanes] = low
        term = dot(high, charge, ((1,), (1,))) + dot(low, charge, ((1,), (1,)))
        total = term if total is None else total + term
    if flip:
        packed = pack_rows(total)
        own_ref[...] = packed
        out_ref[...] = packed.astype(BF16)
    else:
        total_ref[...] = total


def weighted_rows(share, padded, wide, weight_ref, parts):
    packed = parts[0][...].astype(F32)
    for part in parts[1:]:
        packed = packed + part[...].astype(F32)
    struct = unpack_rows(packed)
    span = 8 * share
    cc, ss, sc, cs = (struct[i * span : (i + 1) * span] for i in range(4))
    weight = weight_ref[:, :wide]
    plus, minus, flat = weight[:span], weight[span : 2 * span], weight[2 * span :]
    re_plus, im_plus = plus * (cc - ss), plus * (sc + cs)
    re_minus, im_minus = minus * (cc + ss), minus * (sc - cs)
    rows = jnp.concatenate(
        [
            re_plus + re_minus,
            re_minus - re_plus,
            im_plus + im_minus,
            im_plus - im_minus,
            flat * struct[4 * span : 4 * span + padded],
            flat * struct[4 * span + padded :],
        ],
        axis=0,
    )
    return rows


def fold_kernel(share, padded, grid, wide, flip, place_ref, *refs):
    grid_x, grid_y = grid
    turn = 2.0 * math.pi
    if flip:
        weight_ref, parts, refs = refs[0], refs[1 : 1 + grid_y], refs[1 + grid_y :]
        rows = weighted_rows(share, padded, wide, weight_ref, parts)
        refs, rows_ref = refs[:-1], refs[-1]
        rows_ref[...] = rows
    else:
        rows, refs = refs[0][...], refs[1:]
    ca_ref, sa_ref, cb_ref, sb_ref, high_ref, low_ref, blocks, out_ref = refs
    row_high, row_low = split(rows)
    row_pair = jnp.concatenate([row_high, row_low], axis=1)
    turned = rows.T
    t_high, t_low = split(turned)
    t_both = jnp.concatenate([t_high, t_low], axis=0)
    span = 8 * share
    kx, ky, _ = pair_vectors(count_up(padded), share, place_ref[0])
    kx = kx * (turn / (grid_x * cell_width))
    ky = ky * (turn / (grid_y * cell_width))
    kz = (count_up(8) + 1.0) * (turn / box_height)
    for d in range(grid_x // 2):
        charge = blocks[d][:wide]
        atoms = charge.shape[1]
        lanes = pl.ds(d * atoms, atoms)
        ca, sa, cb, sb = ca_ref[:, lanes], sa_ref[:, lanes], cb_ref[:, lanes], sb_ref[:, lanes]
        bcc, bss, bsc, bcs = basis_rows(share, ca, sa, cb, sb)
        high, low = high_ref[:, lanes], low_ref[:, lanes]
        both = dot(t_both, high)
        pot = both[:wide] + both[wide:] + dot(t_high, low)
        proj = dot(row_pair, jnp.concatenate([charge, charge], axis=0))
        by_x = jnp.zeros((8, atoms), jnp.float32)
        by_y = jnp.zeros((8, atoms), jnp.float32)
        by_z = jnp.zeros((8, atoms), jnp.float32)
        for p in range(share):
            pcc, pss, psc, pcs = (
                proj[i * span + 8 * p : i * span + 8 * p + 8] for i in range(4)
            )
            slope = bcs[p] * pss - bsc[p] * pcc + bcc[p] * psc - bss[p] * pcs
            by_x = by_x + kx[p : p + 1] * slope
            by_y = by_y + ky[p : p + 1] * slope
            by_z = by_z + (bsc[p] * pss - bcs[p] * pcc - bss[p] * psc + bcc[p] * pcs)
        flat_slope = ca * proj[4 * span + padded :] - sa * proj[4 * span : 4 * span + padded]
        grad_x = jnp.sum(by_x, axis=0, keepdims=True) + jnp.sum(kx * flat_slope, axis=0, keepdims=True)
        grad_y = jnp.sum(by_y, axis=0, keepdims=True) + jnp.sum(ky * flat_slope, axis=0, keepdims=True)
        grad_z = jnp.sum(kz * by_z, axis=0, keepdims=True)
        slopes = jnp.concatenate([grad_x, grad_y, grad_z], axis=0)
        out_ref[d] = pieced(pot, slopes, out_ref.shape[1]).astype(out_ref.dtype)


def pieced(pot, slopes, rows):
    high = slopes.astype(BF16).astype(F32)
    rest = slopes - high
    middle = rest.astype(BF16).astype(F32)
    zero = jnp.zeros((rows - pot.shape[0] - 9, pot.shape[1]), F32)
    return jnp.concatenate([pot, high, middle, rest - middle, zero], axis=0)


def unpieced(block, wide):
    slopes = block[wide : wide + 3] + (block[wide + 3 : wide + 6] + block[wide + 6 : wide + 9])
    return block[:wide], slopes


def join_kernel(wide, near_ref, far_ref, own_ref, *outs):
    for d in range(near_ref.shape[0]):
        pot, slopes = unpieced(near_ref[d], wide)
        pot_far, slopes_far = unpieced(far_ref[d].astype(F32), wide)
        block = pieced(pot + pot_far, slopes + slopes_far, near_ref.shape[1])
        if d:
            outs[d - 1][...] = block.astype(BF16)
        else:
            own_ref[...] = block


def per_device(
    positions,
    species,
    neighbours,
    counts,
    species_embed,
    radial,
    mixing,
    read_hidden,
    read_out,
    charge_map,
    wavevectors,
):
    atoms = positions.shape[3]
    slots = neighbours.shape[3]
    features, lat_width = charge_map.shape
    wave_count = wavevectors.shape[1]
    grid = lax.axis_size("gx"), lax.axis_size("gy")
    grid_x, grid_y = grid
    edges = slots * atoms
    scale = 1.0 / math.sqrt(wave_count * lat_width * atoms * grid_x * grid_y)
    place = jnp.stack([lax.axis_index("gx"), lax.axis_index("gy")]).astype(jnp.int32)
    _, share, padded = pair_counts(grid_x)
    ids = neighbours.transpose(0, 3, 1, 2).reshape(1, edges)
    dma = pltpu.SemaphoreType.DMA
    shown = positions.transpose(0, 2, 1, 3)

    (own,) = run(
        pack_kernel,
        [shape(4 * atoms // 128, 128)],
        [place, shown, species],
        scratch=[
            pltpu.VMEM(shown.shape, F32),
            pltpu.VMEM(species.shape, jnp.int32),
            dma((2,)),
        ],
        smem=1,
        hbm=2,
        name="pack",
    )
    norm = 1.0 / math.sqrt(slots)
    kind_rows = 8 * species_embed.shape[0]
    low_pair = lambda *dims: [shape(*dims, dtype=BF16)] * 2
    (ids, counts, embed, kind_left, left, back, kind_high, kind_low, mix_high, mix_low, turn_high,
     turn_low) = run(
        functools.partial(prep_first_kernel, norm),
        [
            shape(1, edges, dtype=jnp.int32),
            shape(*counts.shape, dtype=jnp.int32),
            shape(features, 32, dtype=BF16),
            shape(2, features, 4 * kind_rows, dtype=BF16),
            shape(2, features, 32, dtype=BF16),
            shape(2, 16, 2 * features, dtype=BF16),
        ]
        + low_pair(2, kind_rows, features)
        + low_pair(2, features, 2 * features)
        + low_pair(2, 2 * features, features),
        [ids, counts, species_embed, radial, mixing],
        scratch=[
            pltpu.VMEM(species_embed.shape, F32),
            pltpu.VMEM(radial.shape, F32),
            pltpu.VMEM(mixing.shape, F32),
            dma((5,)),
        ],
        hbm=5,
        name="prep_first",
    )
    cells, ids = around(own, ids)
    (hot,) = run(
        hot_kernel, [shape(9 * atoms, edges, dtype=BF16)], [ids], flops=2_000_000_000, name="hot"
    )
    read_out, hidden_high, hidden_low, hidden_turn_high, hidden_turn_low, charge_pair = run(
        prep_second_kernel,
        [shape(1, features)]
        + low_pair(features, features)
        + low_pair(features, features)
        + [shape(2, lat_width, features, dtype=BF16)],
        [read_out[None, :], read_hidden, charge_map.T],
        scratch=[
            pltpu.VMEM(read_hidden.shape, F32),
            pltpu.VMEM((lat_width, features), F32),
            dma((3,)),
        ],
        hbm=3,
        name="prep_second",
    )
    (weight,) = run(
        functools.partial(green_weights, share, padded, grid),
        [shape(16 * share + padded, 128)],
        [place, wavevectors],
        smem=1,
        name="green",
    )
    low, basis, slope, unit, sums_one, gate_one = run(
        functools.partial(first_kernel, slots),
        [
            shape(features, atoms, dtype=BF16),
            shape(8, edges),
            shape(8, edges),
            shape(8, edges),
            shape(3, features, atoms),
            shape(features, atoms),
        ],
        [ids, counts, embed, kind_left, mix_high, mix_low] + cells,
        name="first",
    )
    hidden, hot = around(low, hot)
    edge_weights, near = run(
        functools.partial(second_near_kernel, slots),
        [shape(4, features, edges), shape(features, edges)],
        [basis, unit, left, hot, hidden[1]],
        flops=2_000_000_000,
        name="second_near",
    )
    (near,) = run(
        functools.partial(second_side_kernel, slots),
        [shape(features, edges)],
        [hot, near, hidden[2]],
        flops=1_000_000_000,
        name="second_side",
    )
    block_rows = -(-(lat_width + 9) // 16) * 16
    feature, sums_two, gate_two, packed, charge, energy, energy_slope = run(
        functools.partial(second_kernel, slots),
        [
            shape(features, edges, dtype=BF16),
            shape(3, features, atoms),
            shape(features, atoms),
            shape(block_rows, atoms, dtype=BF16),
            shape(lat_width, atoms),
            shape(1, atoms),
            shape(features, atoms),
        ],
        [hot, edge_weights, near, mix_high, mix_low, hidden_high, hidden_low, hidden_turn_high,
         hidden_turn_low, read_out, charge_pair, cells[1], hidden[1], hidden[0]],
        name="second",
    )
    half = grid_x // 2
    near_charges = jnp.stack([packed] + [shifted(packed, 2 * d, 0) for d in range(1, half)])
    (hot_back,) = run(
        hot_back_kernel,
        [shape(edges, 9 * atoms, dtype=BF16)],
        [ids],
        flops=2_000_000_000,
        name="hot_back",
    )
    near_charges, hot_back = lax.optimization_barrier((near_charges, hot_back))
    far_charges = swapped(near_charges)
    span = half * atoms
    rows = 32 * share + 2 * padded
    phase_shapes = [
        shape(padded, span),
        shape(padded, span),
        shape(8, span),
        shape(8, span),
        shape(rows, span, dtype=BF16),
        shape(rows, span, dtype=BF16),
    ]
    *near_phases, near_total = run(
        functools.partial(structure_kernel, share, padded, grid, lat_width, 0),
        phase_shapes + [shape(rows, lat_width)],
        [place, near_charges],
        smem=1,
        flops=1_000_000_000,
        name="structure_near",
    )
    *far_phases, own_part, part = run(
        functools.partial(structure_kernel, share, padded, grid, lat_width, 1),
        phase_shapes
        + [
            shape(rows // 2, 2 * lat_width),
            shape(rows // 2, 2 * lat_width, dtype=BF16),
        ],
        [place, far_charges, near_total],
        smem=1,
        name="structure_far",
    )
    parts = [own_part] + [shifted(part, 0, d) for d in range(1, grid_y)]
    far_folds, wave_rows = run(
        functools.partial(fold_kernel, share, padded, grid, lat_width, 1),
        [shape(half, block_rows, atoms, dtype=BF16), shape(rows, lat_width)],
        [place, weight] + parts + far_phases + [far_charges],
        smem=1,
        name="fold_far",
    )
    far_folds = swapped(far_folds)
    (near_folds,) = run(
        functools.partial(fold_kernel, share, padded, grid, lat_width, 0),
        [shape(half, block_rows, atoms)],
        [place, wave_rows] + near_phases + [near_charges],
        smem=1,
        flops=1_000_000_000,
        name="fold_near",
    )
    folds = run(
        functools.partial(join_kernel, lat_width),
        [shape(block_rows, atoms)] + [shape(block_rows, atoms, dtype=BF16)] * (half - 1),
        [near_folds, far_folds],
        name="fold_join",
    )
    folds = [folds[0]] + [shifted(folds[d], -2 * d, 0) for d in range(1, half)]

    site, long, cotangent, grads, term, before, after = run(
        functools.partial(second_back_kernel, slots, scale, half),
        [
            shape(1, 1, atoms),
            shape(8, atoms),
            shape(features, atoms),
            shape(4, features, atoms),
            shape(features, edges, dtype=BF16),
            shape(3, features, atoms, dtype=BF16),
            shape(3, features, atoms, dtype=BF16),
        ],
        [hot_back, edge_weights, turn_high, turn_low, charge_pair, sums_two, gate_two, charge, energy,
         energy_slope] + folds,
        name="second_back",
    )
    from_x = [shifted(after, -1, 0), shifted(before, 1, 0)]
    (middle,) = run(
        second_middle_kernel,
        [shape(3, features, atoms)],
        [hot_back, term, cotangent],
        flops=1_000_000_000,
        name="second_middle",
    )
    sides = [
        (middle[b] + from_x[0][b].astype(F32) + from_x[1][b].astype(F32)).astype(BF16)
        for b in (0, 2)
    ]
    from_y = [shifted(sides[1], 0, -1), shifted(sides[0], 0, 1)]
    (edge,) = run(
        functools.partial(second_edge_kernel, slots),
        [shape(32, edges)],
        [back, feature, grads],
        flops=1_000_000_000,
        name="second_edge",
    )
    before, middle, after = run(
        functools.partial(first_back_kernel, slots),
        [shape(3, 8, atoms)] * 3,
        [ids, basis, slope, unit, kind_high, kind_low, turn_high, turn_low, sums_one, gate_one, edge,
         long, middle] + from_x + from_y,
        name="first_back",
    )
    total = middle + shifted(after, -1, 0) + shifted(before, 1, 0)
    total = total[1] + shifted(total[2], 0, -1) + shifted(total[0], 0, 1)
    forces = -total[None, :3, None, :]
    return (forces.transpose(0, 2, 1, 3), site)


def solution(mesh):
    in_specs = (
        P("gx", "gy", None, None),
        P("gx", "gy", None),
        P("gx", "gy", None, None),
        P("gx", "gy", None),
        P(),
        P(),
        P(),
        P(),
        P(),
        P(),
        P(),
    )
    out_specs = (P("gx", "gy", None, None), P("gx", "gy", None))
    return jax.shard_map(
        per_device, mesh=mesh, in_specs=in_specs, out_specs=out_specs, check_vma=False
    )
```

```python
import functools
import math

import jax
import jax.numpy as jnp
import numpy as np
from jax import lax
from jax.experimental import pallas as pl
from jax.experimental.pallas import tpu as pltpu
from jax.sharding import PartitionSpec as P

cell_width = 10.0
box_height = 30.0
cut_radius = 50.0
soften = 0.25
screen = 0.5
smear_width = 0.5
WAVE_REACH = 8
F32 = jnp.float32
BF16 = jnp.bfloat16
CENTRE = 4


def paired(block, axis, mask):
    return lax.ppermute(block, axis, [(i ^ mask, i) for i in range(lax.axis_size(axis))])


def beyond(block, axis):
    count = lax.axis_size(axis)
    route = [((i + (1 if i % 2 else -1)) % count, i) for i in range(count)]
    return lax.ppermute(block, axis, route)


def around(block, beside):
    column = jnp.stack([paired(block, "gy", 1), block, beyond(block, "gy")])
    column, beside = lax.optimization_barrier((column, beside))
    return [paired(column, "gx", 1), column, beyond(column, "gx")], beside


def whole(space=pltpu.VMEM):
    return pl.BlockSpec(memory_space=space)


def run(kernel, outs, args, scratch=(), smem=0, hbm=0, flops=10_000_000, grant=16, name=None):
    specs = [whole(pltpu.SMEM)] * smem + [whole(pltpu.HBM)] * hbm
    specs += [whole()] * (len(args) - smem - hbm)
    return list(
        pl.pallas_call(
            kernel,
            out_shape=outs,
            in_specs=specs,
            out_specs=[whole() for _ in outs],
            scratch_shapes=list(scratch),
            compiler_params=pltpu.CompilerParams(vmem_limit_bytes=grant * 1024 * 1024),
            cost_estimate=pl.CostEstimate(
                flops=flops, bytes_accessed=1_000_000, transcendentals=0
            ),
            name=name,
        )(*args)
    )


def shape(*dims, dtype=F32):
    return jax.ShapeDtypeStruct(dims, dtype)


def split(value):
    high = value.astype(BF16)
    return high, (value - high.astype(F32)).astype(BF16)


def dot(left, right, contract=((1,), (0,))):
    return lax.dot_general(left, right, (contract, ((), ())), preferred_element_type=F32)


def dot3(left, right):
    left_high, left_low = split(left)
    right_high, right_low = split(right)
    return dot(left_high, right_high) + (dot(left_high, right_low) + dot(left_low, right_high))


def dot_split(left, right):
    right_high, right_low = split(right)
    return dot(left[0], right_high) + (dot(left[0], right_low) + dot(left[1], right_high))


def sin_cos(turns):
    quarter = jnp.round(turns * 4.0)
    x = (turns - quarter * 0.25) * (2.0 * math.pi)
    z = x * x
    sine = ((-1.9515295891e-4 * z + 8.3321608736e-3) * z - 1.6666654611e-1) * (z * x) + x
    cosine = (2.443315711809948e-5 * z - 1.388731625493765e-3) * z + 4.166664568298827e-2
    cosine = cosine * (z * z) - 0.5 * z + 1.0
    k = quarter.astype(jnp.int32) & 3
    odd = (k & 1) == 1
    by_sine = jnp.where(odd, cosine, sine)
    by_cosine = jnp.where(odd, sine, cosine)
    return (
        jnp.where(k >= 2, -by_sine, by_sine),
        jnp.where((k == 1) | (k == 2), -by_cosine, by_cosine),
    )


def stacked_left(value):
    high = value.astype(BF16).astype(F32)
    rows = jnp.concatenate([high, high, value - high, jnp.zeros_like(high)], axis=0)
    return rows.T.astype(BF16)


def stacked_right(value):
    high = value.astype(BF16).astype(F32)
    return jnp.concatenate([high, value - high, high, jnp.zeros_like(high)], axis=0).astype(BF16)


def silu_pair(value):
    gate = 1.0 / (1.0 + jnp.exp(-value))
    return value * gate, gate * (1.0 + value * (1.0 - gate))


def onehot_kinds(kinds, rows):
    levels = lax.broadcasted_iota(jnp.int32, (rows, kinds.shape[1]), 0).astype(F32)
    return jnp.where(kinds == levels, 1.0, 0.0)


def embedding_stack(embed):
    high = embed.astype(BF16).astype(F32)
    rest = embed - high
    middle = rest.astype(BF16).astype(F32)
    rows = jnp.concatenate([high, middle, rest - middle, jnp.zeros_like(high)], axis=0)
    return rows.T.astype(BF16)


def embedded(stack, kinds):
    hot = onehot_kinds(kinds, 8)
    return dot(stack, jnp.concatenate([hot, hot, hot, jnp.zeros_like(hot)], axis=0).astype(BF16))


def weights_of(stack_ref, part, rows):
    return dot(stack_ref[1 if part else 0], stacked_right(rows))


def mixed(sums, high_ref, low_ref, layer):
    squares = sums[1] * sums[1] + sums[2] * sums[2] + sums[3] * sums[3]
    both = jnp.concatenate([sums[0], squares], axis=0)
    return silu_pair(dot_split((high_ref[layer], low_ref[layer]), both))


def edge_parts(basis, unit):
    return [basis] + [basis * unit[i : i + 1] for i in range(3)]


def pack_kernel(place_ref, position_ref, species_ref, out_ref, place, kind, sems):
    copies = [
        pltpu.make_async_copy(position_ref, place, sems.at[0]),
        pltpu.make_async_copy(species_ref, kind, sems.at[1]),
    ]
    for copy in copies:
        copy.start()
    for copy in copies:
        copy.wait()
    rows = [place[0, i] for i in range(3)] + [kind[0].astype(F32)]
    atoms = rows[0].shape[1]
    out_ref[...] = jnp.concatenate(
        [row[:, s : s + 128] for s in range(0, atoms, 128) for row in rows], axis=0
    )


def radial_left(radial):
    high = radial.astype(BF16).astype(F32)
    low = radial - high
    top = jnp.concatenate([high, high], axis=1)
    end = jnp.concatenate([low, jnp.zeros_like(low)], axis=1)
    return jnp.concatenate([top, end], axis=0).astype(BF16)


def put_split(value, high_ref, low_ref, *at):
    high, low = split(value)
    high_ref[at] = high
    low_ref[at] = low


def slot_order(ids, place_ref, atoms):
    cell = ids // atoms
    a = (cell * 11) >> 5
    b = cell - 3 * a
    a = jnp.where((place_ref[0] & 1) == 0, 2 - a, a)
    b = jnp.where((place_ref[1] & 1) == 0, 2 - b, b)
    return ids + (3 * a + b - cell) * atoms


def fetch(sources, targets, sems):
    copies = [
        pltpu.make_async_copy(source, target, sems.at[i])
        for i, (source, target) in enumerate(zip(sources, targets))
    ]
    for copy in copies:
        copy.start()
    for copy in copies:
        copy.wait()


def prep_first_kernel(norm, place_ref, ids_in, count_in, embed_in, radial_in, mixing_in, id_ref, count_ref,
                      embed_out, kind_left, left_out, back_out, kind_high, kind_low, mix_high,
                      mix_low, turn_high, turn_low, embed_ref, radial_ref, mixing_ref, sems):
    fetch(
        [ids_in, count_in, embed_in, radial_in, mixing_in],
        [id_ref, count_ref, embed_ref, radial_ref, mixing_ref],
        sems,
    )
    id_ref[...] = slot_order(id_ref[...], place_ref, count_ref.shape[2])
    embed = embed_ref[...]
    kinds = embed.shape[0]
    for path in range(2):
        radial = radial_ref[0, path] * norm
        rows = jnp.concatenate([radial * embed[s : s + 1] for s in range(kinds)], axis=0)
        kind_left[path] = stacked_left(rows)
        put_split(rows, kind_high, kind_low, path)
        radial = radial_ref[1, path] * norm
        left_out[path] = stacked_left(radial)
        back_out[path] = radial_left(radial)
    for layer in range(2):
        scalar, vector = mixing_ref[layer, 0], mixing_ref[layer, 1]
        put_split(jnp.concatenate([scalar.T, vector.T], axis=1), mix_high, mix_low, layer)
        put_split(jnp.concatenate([scalar, 2.0 * vector], axis=0), turn_high, turn_low, layer)
    embed = jnp.concatenate([embed, jnp.zeros((8 - kinds, embed.shape[1]), F32)], axis=0)
    embed_out[...] = embedding_stack(embed)


def prep_second_kernel(read_in, hidden_in, charge_in, read_ref, hidden_high, hidden_low,
                       hidden_turn_high, hidden_turn_low, charge_pair, hidden_ref, charge_ref, sems):
    fetch([read_in, hidden_in, charge_in], [read_ref, hidden_ref, charge_ref], sems)
    put_split(hidden_ref[...].T, hidden_high, hidden_low, Ellipsis)
    put_split(hidden_ref[...], hidden_turn_high, hidden_turn_low, Ellipsis)
    charge = charge_ref[...]
    high = charge.astype(BF16).astype(F32)
    charge_pair[0] = high.astype(BF16)
    charge_pair[1] = (charge - high).astype(BF16)


def hot_kernel(ids_ref, hot_ref):
    edges = ids_ref.shape[1]
    for start in range(0, edges, 256):
        lanes = slice(start, start + 256)
        hot_ref[:, lanes] = hot_columns(ids_ref[:, lanes], hot_ref.shape[0])


def hot_back_kernel(ids_ref, hot_ref):
    edges = ids_ref.shape[1]
    entry = lax.broadcasted_iota(jnp.int32, (128, hot_ref.shape[1]), 1).astype(F32)
    for start in range(0, edges, 128):
        row = jnp.broadcast_to(ids_ref[:, start : start + 128].astype(F32), (8, 128))
        column = row.T[:, 0:1]
        hot_ref[start : start + 128] = jnp.where(column == entry, 1.0, 0.0).astype(BF16)


def unfold_block(block, atoms):
    parts = atoms // 128
    return jnp.concatenate([block[4 * s : 4 * s + 4] for s in range(parts)], axis=1)


def first_kernel(slots, place_ref, ids_ref, count_ref, embed_ref, kind_left, mix_high, mix_low,
                 pair_ref, column_ref, beyond_ref, low_ref, basis_ref, slope_ref, unit_ref, sums_ref,
                 gate_ref):
    atoms = low_ref.shape[1]
    ids = ids_ref[...]
    frame = [pair_ref, column_ref, beyond_ref]
    own = unfold_block(column_ref[1], atoms)
    own = jnp.concatenate([own, jnp.zeros_like(own)], axis=0)
    per_cell = atoms // 128
    places = lax.broadcasted_iota(jnp.int32, (4 * per_cell, 128), 0)
    upper = places >> 2
    kind_of_row = places & 3
    rows = []
    to_x = jnp.where(kind_of_row == 0, cell_width, 0.0)
    to_x = jnp.where((place_ref[0] & 1) == 0, to_x, -to_x)
    to_y = jnp.where(kind_of_row == 1, cell_width, 0.0)
    to_y = jnp.where((place_ref[1] & 1) == 0, to_y, -to_y)
    for a in range(3):
        for b in range(3):
            rows.append(frame[a][b] + ((1 - a) * to_x + (1 - b) * to_y))
    pieces = []
    for start in range(0, ids.shape[1], 128):
        part = jnp.broadcast_to(ids[:, start : start + 128], places.shape)
        lane, half = part & 127, (part >> 7) - upper
        found = jnp.zeros(places.shape, F32)
        for cell, block in enumerate(rows):
            value = jnp.take_along_axis(block, lane, axis=1)
            found = jnp.where(half == per_cell * cell, value, found)
        total = found[:4]
        for s in range(1, per_cell):
            total = total + found[4 * s : 4 * s + 4]
        pieces.append(jnp.concatenate([total, total], axis=0))
    found = jnp.concatenate(pieces, axis=1)
    relative = found - jnp.concatenate([own] * slots, axis=1)
    rel = [relative[i : i + 1] for i in range(3)]
    distance = jnp.sqrt(rel[0] * rel[0] + rel[1] * rel[1] + rel[2] * rel[2] + soften)
    inverse = 1.0 / distance
    order = (lax.broadcasted_iota(jnp.int32, (8, 1), 0) + 1).astype(F32)
    sine, cosine = sin_cos((order * (0.5 / cut_radius)) * distance)
    wave = sine / ((order * (math.pi / cut_radius)) * distance)
    count = count_ref[0]
    live = jnp.concatenate([jnp.where(count > n, 1.0, 0.0) for n in range(slots)], axis=1)
    basis = wave * live
    basis_ref[...] = basis
    slope_ref[...] = (cosine - wave) * (inverse * live)
    kinds = found[3:4]
    unit = jnp.concatenate(
        [r * inverse for r in rel] + [inverse, kinds] + [jnp.zeros_like(kinds)] * 3, axis=0
    )
    unit_ref[...] = unit
    stack = embed_ref[...]
    parts = edge_parts(basis, unit)
    species = kind_left.shape[2] // 32
    by_kind = [[None] * species for _ in range(4)]
    for n in range(slots):
        lanes = slice(n * atoms, (n + 1) * atoms)
        kind = jnp.broadcast_to(kinds[:, lanes], (8, atoms))
        for k in range(species):
            match = kind == float(k)
            for part in range(4):
                term = jnp.where(match, parts[part][:, lanes], 0.0)
                old = by_kind[part][k]
                by_kind[part][k] = term if old is None else old + term
    stacks = [stacked_right(jnp.concatenate(rows, axis=0)) for rows in by_kind]
    vectors = dot(kind_left[1], jnp.concatenate(stacks[1:], axis=1))
    sums = [dot(kind_left[0], stacks[0])]
    sums += [vectors[:, i * atoms : (i + 1) * atoms] for i in range(3)]
    step, gate = mixed(sums, mix_high, mix_low, 0)
    low_ref[...] = (embedded(stack, own[3:4]) + step).astype(BF16)
    for part in range(3):
        sums_ref[part] = sums[part + 1]
    gate_ref[...] = gate


def hot_columns(ids, rows):
    place = lax.broadcasted_iota(jnp.int32, (rows, ids.shape[1]), 0)
    return jnp.where(ids == place, 1.0, 0.0).astype(BF16)


def second_near_kernel(slots, basis_ref, unit_ref, left_ref, hot_ref, column_ref, weight_ref,
                       near_ref):
    atoms = column_ref.shape[2]
    parts = edge_parts(basis_ref[...], unit_ref[...])
    source = jnp.concatenate([column_ref[b] for b in range(3)], axis=1)
    for n in range(slots):
        lanes = slice(n * atoms, (n + 1) * atoms)
        for part in range(4):
            weight_ref[part, :, lanes] = weights_of(left_ref, part, parts[part][:, lanes])
        near_ref[:, lanes] = dot(source, hot_ref[3 * atoms : 6 * atoms, lanes])


def second_side_kernel(slots, hot_ref, near_ref, pair_ref, out_ref):
    atoms = pair_ref.shape[2]
    source = jnp.concatenate([pair_ref[b] for b in range(3)], axis=1)
    for n in range(slots):
        lanes = slice(n * atoms, (n + 1) * atoms)
        out_ref[:, lanes] = near_ref[:, lanes] + dot(source, hot_ref[: 3 * atoms, lanes])


def second_kernel(slots, hot_ref, weight_ref, near_ref, mix_high, mix_low, hidden_high, hidden_low,
                  turn_high, turn_low, out_ref, charge_ref, cell_ref, column_ref, beyond_ref,
                  feature_ref, sums_ref, gate_ref, packed_ref, full_charge_ref, energy_ref,
                  slope_ref):
    atoms = column_ref.shape[2]
    source = jnp.concatenate([beyond_ref[b] for b in range(3)], axis=1)
    sums = [None] * 4
    for n in range(slots):
        lanes = slice(n * atoms, (n + 1) * atoms)
        feature = near_ref[:, lanes] + dot(source, hot_ref[6 * atoms :, lanes])
        feature_ref[:, lanes] = feature.astype(BF16)
        for part in range(4):
            term = weight_ref[part, :, lanes] * feature
            sums[part] = term if sums[part] is None else sums[part] + term
    step, gate = mixed(sums, mix_high, mix_low, 1)
    hidden = column_ref[1].astype(F32) + step
    for part in range(3):
        sums_ref[part] = sums[part + 1]
    gate_ref[...] = gate
    charge = dot_split((charge_ref[0], charge_ref[1]), hidden)
    full_charge_ref[...] = charge
    place = unfold_block(cell_ref[1], atoms)[:3]
    high = place.astype(BF16).astype(F32)
    rest = place - high
    middle = rest.astype(BF16).astype(F32)
    zero = jnp.zeros((packed_ref.shape[0] - charge.shape[0] - 9, atoms), F32)
    packed_ref[...] = jnp.concatenate([charge, high, middle, rest - middle, zero], axis=0).astype(
        BF16
    )
    value, slope = silu_pair(dot_split((hidden_high[...], hidden_low[...]), hidden))
    out = out_ref[...].T
    energy_ref[...] = jnp.sum(value * out, axis=0, keepdims=True)
    slope_ref[...] = dot_split((turn_high[...], turn_low[...]), slope * out)


def message_grads(cotangent, gate_ref, sums_ref, high_ref, low_ref, layer):
    pre = cotangent * gate_ref[...]
    both = dot_split((high_ref[layer], low_ref[layer]), pre)
    half = both.shape[0] // 2
    return [both[:half]] + [both[half:] * sums_ref[i] for i in range(3)]


def radial_grad(left, value):
    high, low = split(value)
    both = dot(left, jnp.concatenate([high, low], axis=0))
    half = both.shape[0] // 2
    return both[:half] + both[half:]


def second_back_kernel(slots, scale, count, hot_ref, weight_ref, turn_high, turn_low, charge_ref,
                       sums_ref, gate_ref, full_charge_ref, energy_ref, slope_ref, *refs):
    folds, refs = refs[:count], refs[count:]
    site_ref, long_ref, cotangent_ref, grad_ref, term_ref, beyond_ref = refs
    atoms = gate_ref.shape[1]
    total = folds[0][...].astype(F32)
    for part in folds[1:]:
        total = total + part[...].astype(F32)
    wide = full_charge_ref.shape[0]
    potential = total[:wide] * (2.0 * scale)
    slopes = total[wide : wide + 3] + total[wide + 3 : wide + 6] + total[wide + 6 : wide + 9]
    long_ref[...] = jnp.concatenate(
        [slopes * (2.0 * scale), jnp.zeros((5, atoms), F32)], axis=0
    )
    site_ref[0] = energy_ref[...] + 0.5 * jnp.sum(
        full_charge_ref[...] * potential, axis=0, keepdims=True
    )
    high, low = split(potential)
    turned = ((0,), (0,))
    cotangent = slope_ref[...] + (
        dot(charge_ref[0], high, turned)
        + (dot(charge_ref[0], low, turned) + dot(charge_ref[1], high, turned))
    )
    cotangent_ref[...] = cotangent
    grads = message_grads(cotangent, gate_ref, sums_ref, turn_high, turn_low, 1)
    for part in range(4):
        grad_ref[part] = grads[part]
    for n in range(slots):
        lanes = slice(n * atoms, (n + 1) * atoms)
        term = weight_ref[0, :, lanes] * grads[0]
        for part in range(1, 4):
            term = term + weight_ref[part, :, lanes] * grads[part]
        term_ref[:, lanes] = term.astype(BF16)
    for b in range(3):
        start = (6 + b) * atoms
        beyond_ref[b] = dot(term_ref[...], hot_ref[:, start : start + atoms]).astype(BF16)


def second_middle_kernel(hot_ref, term_ref, cotangent_ref, pair_ref, middle_ref):
    atoms = cotangent_ref.shape[1]
    for b in range(3):
        grad = dot(term_ref[...], hot_ref[:, (3 + b) * atoms : (4 + b) * atoms])
        middle_ref[b] = grad + cotangent_ref[...] if b == 1 else grad
        pair_ref[b] = dot(term_ref[...], hot_ref[:, b * atoms : (b + 1) * atoms]).astype(BF16)


def second_edge_kernel(slots, back_ref, feature_ref, grad_ref, edge_ref):
    atoms = grad_ref.shape[2]
    for n in range(slots):
        lanes = slice(n * atoms, (n + 1) * atoms)
        feature = feature_ref[:, lanes].astype(F32)
        for part in range(4):
            edge_ref[8 * part : 8 * part + 8, lanes] = radial_grad(
                back_ref[1 if part else 0], grad_ref[part] * feature
            )


def first_back_kernel(slots, ids_ref, basis_ref, slope_ref, unit_ref, kind_high, kind_low,
                      turn_high, turn_low, sums_ref, gate_ref, edge_ref, long_ref, middle_ref,
                      *refs):
    from_x, from_y, outs = refs[:2], refs[2:4], refs[4:]
    atoms = gate_ref.shape[1]
    cotangent = middle_ref[1]
    for block in (from_x[0][1], from_x[1][1], from_y[0][...], from_y[1][...]):
        cotangent = cotangent + block.astype(F32)
    grads = message_grads(cotangent, gate_ref, sums_ref, turn_high, turn_low, 0)
    unit = unit_ref[...]
    kinds = unit[4:5]
    by_kind = [dot_split((kind_high[0], kind_low[0]), grads[0])]
    by_kind += [dot_split((kind_high[1], kind_low[1]), grads[i]) for i in range(1, 4)]
    species = by_kind[0].shape[0] // 8
    edges = [[] for _ in range(4)]
    for n in range(slots):
        kind = jnp.broadcast_to(kinds[:, n * atoms : (n + 1) * atoms], (8, atoms))
        matches = [kind == float(k) for k in range(1, species)]
        for part in range(4):
            rows = by_kind[part]
            found = rows[:8]
            for k, match in enumerate(matches):
                found = jnp.where(match, rows[8 * k + 8 : 8 * k + 16], found)
            edges[part].append(found)
    edges = [
        edge_ref[8 * part : 8 * part + 8] + jnp.concatenate(edges[part], axis=1) for part in range(4)
    ]
    basis = basis_ref[...]
    units = [unit[i : i + 1] for i in range(3)]
    inverse = unit[3:4]
    by_basis = edges[0]
    for i in range(3):
        by_basis = by_basis + edges[i + 1] * units[i]
    by_unit = [jnp.sum(edges[i + 1] * basis, axis=0, keepdims=True) * inverse for i in range(3)]
    by_distance = jnp.sum(by_basis * slope_ref[...], axis=0, keepdims=True)
    for i in range(3):
        by_distance = by_distance - by_unit[i] * units[i]
    moves = [by_unit[i] + by_distance * units[i] for i in range(3)]
    zero = jnp.zeros_like(moves[0])
    move = jnp.concatenate(moves + [zero] * 5, axis=0)
    own = long_ref[...]
    for n in range(slots):
        own = own - move[:, n * atoms : (n + 1) * atoms]
    ids = ids_ref[...]
    lane_hot = hot_columns(ids & 127, 128)
    half = ids >> 7
    high = move.astype(BF16).astype(F32)
    both = jnp.concatenate([high, move - high], axis=0)
    per_cell = atoms // 128
    rows = jnp.concatenate(
        [jnp.where(half == h, both, 0.0).astype(BF16) for h in range(9 * per_cell)], axis=0
    )
    spread = dot(rows, lane_hot, ((1,), (1,)))
    for cell in range(9):
        found = []
        for h in range(cell * per_cell, (cell + 1) * per_cell):
            found.append(spread[16 * h : 16 * h + 8] + spread[16 * h + 8 : 16 * h + 16])
        grad = jnp.concatenate(found, axis=1)
        if cell == CENTRE:
            grad = own + grad
        outs[cell // 3][cell % 3] = grad


def pair_counts(parts):
    total = WAVE_REACH + WAVE_REACH * (2 * WAVE_REACH + 1)
    share = -(-total // parts)
    return total, share, -(-share // 16) * 16


def pair_vectors(slot, share, part):
    side = 2 * WAVE_REACH + 1
    total = WAVE_REACH + WAVE_REACH * side
    index = slot + part.astype(F32) * share
    later = index - WAVE_REACH
    row = jnp.floor((later + 0.5) * (1.0 / side))
    first = index < WAVE_REACH
    kx = jnp.where(first, 0.0, row + 1.0)
    ky = jnp.where(first, index + 1.0, later - row * side - WAVE_REACH)
    valid = jnp.where((slot < share) & (index < total), 1.0, 0.0)
    return kx, ky, valid


def count_up(rows):
    return lax.broadcasted_iota(jnp.int32, (rows, 1), 0).astype(F32)


def green_weights(share, padded, grid, place_ref, vec_ref, weight_ref):
    grid_x, grid_y = grid
    turn = 2.0 * math.pi
    side = 2 * WAVE_REACH + 1
    top = side * side * side - 1
    vec = vec_ref[...].astype(F32) + WAVE_REACH
    code = (vec[0:1] * side + vec[1:2]) * side + vec[2:3]
    code = jnp.maximum(code, top - code)
    span = 8 * share
    row = count_up(span)
    slot = jnp.floor(row * 0.125)
    height = row - 8.0 * slot + 1.0
    flat = count_up(padded)
    slot = jnp.concatenate([slot, slot, flat], axis=0)
    kz = jnp.concatenate([height, -height, jnp.zeros_like(flat)], axis=0)
    kx, ky, valid = pair_vectors(slot, share, place_ref[0])
    own = ((kx + WAVE_REACH) * side + ky + WAVE_REACH) * side + kz + WAVE_REACH
    seen = jnp.zeros((own.shape[0], 128), F32)
    for start in range(0, code.shape[1], 128):
        seen = seen + jnp.where(own == code[:, start : start + 128], 1.0, 0.0)
    count = jnp.sum(seen, axis=1, keepdims=True) * valid
    sq = (
        (kx * (turn / (grid_x * cell_width))) ** 2
        + (ky * (turn / (grid_y * cell_width))) ** 2
        + (kz * (turn / box_height)) ** 2
    )
    green = jnp.exp(-smear_width * sq) / (sq + screen * screen) * count
    weight_ref[...] = jnp.broadcast_to(green, weight_ref.shape)


def basis_rows(share, ca, sa, cb, sb):
    cc, ss, sc, cs = [], [], [], []
    for p in range(share):
        c, s = ca[p : p + 1], sa[p : p + 1]
        cc.append(c * cb)
        ss.append(s * sb)
        sc.append(s * cb)
        cs.append(c * sb)
    return cc, ss, sc, cs


def unpack_rows(block):
    half = block.shape[1] // 2
    return jnp.concatenate([block[:, :half], block[:, half:]], axis=0)


def pack_rows(block):
    half = block.shape[0] // 2
    return jnp.concatenate([block[:half], block[half:]], axis=1)


def structure_kernel(share, padded, grid, wide, flip, place_ref, blocks, *refs):
    grid_x, grid_y = grid
    if flip:
        near_ref, (ca_ref, sa_ref, cb_ref, sb_ref, high_ref, low_ref, own_ref, out_ref) = (
            refs[0],
            refs[1:],
        )
        total = near_ref[...]
    else:
        ca_ref, sa_ref, cb_ref, sb_ref, high_ref, low_ref, total_ref = refs
        total = None
    col = place_ref[1].astype(F32) * (1.0 / grid_y)
    first = place_ref[0] ^ flip
    kx, ky, _ = pair_vectors(count_up(padded), share, place_ref[0])
    kz = count_up(8) + 1.0
    for d in range(grid_x // 2):
        block = blocks[d]
        charge = block[:wide]
        atoms = charge.shape[1]
        pieces = block[wide:].astype(F32)
        place = pieces[0:3] + (pieces[3:6] + pieces[6:9])
        row = (first ^ (2 * d)).astype(F32) * (1.0 / grid_x)
        x = place[0:1] * (1.0 / (grid_x * cell_width)) + row
        y = place[1:2] * (1.0 / (grid_y * cell_width)) + col
        sa, ca = sin_cos(kx * x + ky * y)
        sb, cb = sin_cos(kz * (place[2:3] * (1.0 / box_height)))
        lanes = pl.ds(d * atoms, atoms)
        ca_ref[:, lanes] = ca
        sa_ref[:, lanes] = sa
        cb_ref[:, lanes] = cb
        sb_ref[:, lanes] = sb
        cc, ss, sc, cs = basis_rows(share, ca, sa, cb, sb)
        high, low = split(jnp.concatenate(cc + ss + sc + cs + [ca, sa], axis=0))
        high_ref[:, lanes] = high
        low_ref[:, lanes] = low
        term = dot(high, charge, ((1,), (1,))) + dot(low, charge, ((1,), (1,)))
        total = term if total is None else total + term
    if flip:
        packed = pack_rows(total)
        own_ref[...] = packed
        out_ref[...] = packed.astype(BF16)
    else:
        total_ref[...] = total


def weighted_rows(share, padded, wide, weight_ref, parts):
    packed = parts[0][...].astype(F32)
    for part in parts[1:]:
        packed = packed + part[...].astype(F32)
    struct = unpack_rows(packed)
    span = 8 * share
    cc, ss, sc, cs = (struct[i * span : (i + 1) * span] for i in range(4))
    weight = weight_ref[:, :wide]
    plus, minus, flat = weight[:span], weight[span : 2 * span], weight[2 * span :]
    re_plus, im_plus = plus * (cc - ss), plus * (sc + cs)
    re_minus, im_minus = minus * (cc + ss), minus * (sc - cs)
    rows = jnp.concatenate(
        [
            re_plus + re_minus,
            re_minus - re_plus,
            im_plus + im_minus,
            im_plus - im_minus,
            flat * struct[4 * span : 4 * span + padded],
            flat * struct[4 * span + padded :],
        ],
        axis=0,
    )
    return rows


def fold_kernel(share, padded, grid, wide, flip, place_ref, *refs):
    grid_x, grid_y = grid
    turn = 2.0 * math.pi
    if flip:
        weight_ref, parts, refs = refs[0], refs[1 : 1 + grid_y], refs[1 + grid_y :]
        rows = weighted_rows(share, padded, wide, weight_ref, parts)
        refs, rows_ref = refs[:-1], refs[-1]
        rows_ref[...] = rows
    else:
        rows, refs = refs[0][...], refs[1:]
    ca_ref, sa_ref, cb_ref, sb_ref, high_ref, low_ref, blocks, out_ref = refs
    row_high, row_low = split(rows)
    row_pair = jnp.concatenate([row_high, row_low], axis=1)
    turned = rows.T
    t_high, t_low = split(turned)
    t_both = jnp.concatenate([t_high, t_low], axis=0)
    span = 8 * share
    kx, ky, _ = pair_vectors(count_up(padded), share, place_ref[0])
    kx = kx * (turn / (grid_x * cell_width))
    ky = ky * (turn / (grid_y * cell_width))
    kz = (count_up(8) + 1.0) * (turn / box_height)
    for d in range(grid_x // 2):
        charge = blocks[d][:wide]
        atoms = charge.shape[1]
        lanes = pl.ds(d * atoms, atoms)
        ca, sa, cb, sb = ca_ref[:, lanes], sa_ref[:, lanes], cb_ref[:, lanes], sb_ref[:, lanes]
        bcc, bss, bsc, bcs = basis_rows(share, ca, sa, cb, sb)
        high, low = high_ref[:, lanes], low_ref[:, lanes]
        both = dot(t_both, high)
        pot = both[:wide] + both[wide:] + dot(t_high, low)
        proj = dot(row_pair, jnp.concatenate([charge, charge], axis=0))
        by_x = jnp.zeros((8, atoms), jnp.float32)
        by_y = jnp.zeros((8, atoms), jnp.float32)
        by_z = jnp.zeros((8, atoms), jnp.float32)
        for p in range(share):
            pcc, pss, psc, pcs = (
                proj[i * span + 8 * p : i * span + 8 * p + 8] for i in range(4)
            )
            slope = bcs[p] * pss - bsc[p] * pcc + bcc[p] * psc - bss[p] * pcs
            by_x = by_x + kx[p : p + 1] * slope
            by_y = by_y + ky[p : p + 1] * slope
            by_z = by_z + (bsc[p] * pss - bcs[p] * pcc - bss[p] * psc + bcc[p] * pcs)
        flat_slope = ca * proj[4 * span + padded :] - sa * proj[4 * span : 4 * span + padded]
        grad_x = jnp.sum(by_x, axis=0, keepdims=True) + jnp.sum(kx * flat_slope, axis=0, keepdims=True)
        grad_y = jnp.sum(by_y, axis=0, keepdims=True) + jnp.sum(ky * flat_slope, axis=0, keepdims=True)
        grad_z = jnp.sum(kz * by_z, axis=0, keepdims=True)
        slopes = jnp.concatenate([grad_x, grad_y, grad_z], axis=0)
        out_ref[d] = pieced(pot, slopes, out_ref.shape[1]).astype(out_ref.dtype)


def pieced(pot, slopes, rows):
    high = slopes.astype(BF16).astype(F32)
    rest = slopes - high
    middle = rest.astype(BF16).astype(F32)
    zero = jnp.zeros((rows - pot.shape[0] - 9, pot.shape[1]), F32)
    return jnp.concatenate([pot, high, middle, rest - middle, zero], axis=0)


def unpieced(block, wide):
    slopes = block[wide : wide + 3] + (block[wide + 3 : wide + 6] + block[wide + 6 : wide + 9])
    return block[:wide], slopes


def join_kernel(wide, near_ref, far_ref, own_ref, *outs):
    for d in range(near_ref.shape[0]):
        pot, slopes = unpieced(near_ref[d], wide)
        pot_far, slopes_far = unpieced(far_ref[d].astype(F32), wide)
        block = pieced(pot + pot_far, slopes + slopes_far, near_ref.shape[1])
        if d:
            outs[d - 1][...] = block.astype(BF16)
        else:
            own_ref[...] = block


def per_device(
    positions,
    species,
    neighbours,
    counts,
    species_embed,
    radial,
    mixing,
    read_hidden,
    read_out,
    charge_map,
    wavevectors,
):
    atoms = positions.shape[3]
    slots = neighbours.shape[3]
    features, lat_width = charge_map.shape
    wave_count = wavevectors.shape[1]
    grid = lax.axis_size("gx"), lax.axis_size("gy")
    grid_x, grid_y = grid
    edges = slots * atoms
    scale = 1.0 / math.sqrt(wave_count * lat_width * atoms * grid_x * grid_y)
    place = jnp.stack([lax.axis_index("gx"), lax.axis_index("gy")]).astype(jnp.int32)
    _, share, padded = pair_counts(grid_x)
    ids = neighbours.transpose(0, 3, 1, 2).reshape(1, edges)
    dma = pltpu.SemaphoreType.DMA
    shown = positions.transpose(0, 2, 1, 3)

    (own,) = run(
        pack_kernel,
        [shape(4 * atoms // 128, 128)],
        [place, shown, species],
        scratch=[
            pltpu.VMEM(shown.shape, F32),
            pltpu.VMEM(species.shape, jnp.int32),
            dma((2,)),
        ],
        smem=1,
        hbm=2,
        name="pack",
    )
    norm = 1.0 / math.sqrt(slots)
    kind_rows = 8 * species_embed.shape[0]
    low_pair = lambda *dims: [shape(*dims, dtype=BF16)] * 2
    (ids, counts, embed, kind_left, left, back, kind_high, kind_low, mix_high, mix_low, turn_high,
     turn_low) = run(
        functools.partial(prep_first_kernel, norm),
        [
            shape(1, edges, dtype=jnp.int32),
            shape(*counts.shape, dtype=jnp.int32),
            shape(features, 32, dtype=BF16),
            shape(2, features, 4 * kind_rows, dtype=BF16),
            shape(2, features, 32, dtype=BF16),
            shape(2, 16, 2 * features, dtype=BF16),
        ]
        + low_pair(2, kind_rows, features)
        + low_pair(2, features, 2 * features)
        + low_pair(2, 2 * features, features),
        [place, ids, counts, species_embed, radial, mixing],
        scratch=[
            pltpu.VMEM(species_embed.shape, F32),
            pltpu.VMEM(radial.shape, F32),
            pltpu.VMEM(mixing.shape, F32),
            dma((5,)),
        ],
        smem=1,
        hbm=5,
        name="prep_first",
    )
    cells, ids = around(own, ids)
    (hot,) = run(
        hot_kernel, [shape(9 * atoms, edges, dtype=BF16)], [ids], flops=2_000_000_000, name="hot"
    )
    read_out, hidden_high, hidden_low, hidden_turn_high, hidden_turn_low, charge_pair = run(
        prep_second_kernel,
        [shape(1, features)]
        + low_pair(features, features)
        + low_pair(features, features)
        + [shape(2, lat_width, features, dtype=BF16)],
        [read_out[None, :], read_hidden, charge_map.T],
        scratch=[
            pltpu.VMEM(read_hidden.shape, F32),
            pltpu.VMEM((lat_width, features), F32),
            dma((3,)),
        ],
        hbm=3,
        name="prep_second",
    )
    low, basis, slope, unit, sums_one, gate_one = run(
        functools.partial(first_kernel, slots),
        [
            shape(features, atoms, dtype=BF16),
            shape(8, edges),
            shape(8, edges),
            shape(8, edges),
            shape(3, features, atoms),
            shape(features, atoms),
        ],
        [place, ids, counts, embed, kind_left, mix_high, mix_low] + cells,
        smem=1,
        name="first",
    )
    hidden, hot = around(low, hot)
    edge_weights, near = run(
        functools.partial(second_near_kernel, slots),
        [shape(4, features, edges), shape(features, edges)],
        [basis, unit, left, hot, hidden[1]],
        flops=2_000_000_000,
        name="second_near",
    )
    (near,) = run(
        functools.partial(second_side_kernel, slots),
        [shape(features, edges)],
        [hot, near, hidden[0]],
        flops=1_000_000_000,
        name="second_side",
    )
    block_rows = -(-(lat_width + 9) // 16) * 16
    feature, sums_two, gate_two, packed, charge, energy, energy_slope = run(
        functools.partial(second_kernel, slots),
        [
            shape(features, edges, dtype=BF16),
            shape(3, features, atoms),
            shape(features, atoms),
            shape(block_rows, atoms, dtype=BF16),
            shape(lat_width, atoms),
            shape(1, atoms),
            shape(features, atoms),
        ],
        [hot, edge_weights, near, mix_high, mix_low, hidden_high, hidden_low, hidden_turn_high,
         hidden_turn_low, read_out, charge_pair, cells[1], hidden[1], hidden[2]],
        name="second",
    )
    half = grid_x // 2
    near_charges = jnp.stack([packed] + [paired(packed, "gx", 2 * d) for d in range(1, half)])
    (weight,) = run(
        functools.partial(green_weights, share, padded, grid),
        [shape(16 * share + padded, 128)],
        [place, wavevectors],
        smem=1,
        name="green",
    )
    near_charges, weight = lax.optimization_barrier((near_charges, weight))
    far_charges = paired(near_charges, "gx", 1)
    span = half * atoms
    rows = 32 * share + 2 * padded
    phase_shapes = [
        shape(padded, span),
        shape(padded, span),
        shape(8, span),
        shape(8, span),
        shape(rows, span, dtype=BF16),
        shape(rows, span, dtype=BF16),
    ]
    *near_phases, near_total = run(
        functools.partial(structure_kernel, share, padded, grid, lat_width, 0),
        phase_shapes + [shape(rows, lat_width)],
        [place, near_charges],
        smem=1,
        flops=1_000_000_000,
        name="structure_near",
    )
    *far_phases, own_part, part = run(
        functools.partial(structure_kernel, share, padded, grid, lat_width, 1),
        phase_shapes
        + [
            shape(rows // 2, 2 * lat_width),
            shape(rows // 2, 2 * lat_width, dtype=BF16),
        ],
        [place, far_charges, near_total],
        smem=1,
        name="structure_far",
    )
    parts = [own_part] + [paired(part, "gy", d) for d in range(1, grid_y)]
    (hot_back,) = run(
        hot_back_kernel,
        [shape(edges, 9 * atoms, dtype=BF16)],
        [ids],
        flops=2_000_000_000,
        name="hot_back",
    )
    parts, hot_back = lax.optimization_barrier((parts, hot_back))
    far_folds, wave_rows = run(
        functools.partial(fold_kernel, share, padded, grid, lat_width, 1),
        [shape(half, block_rows, atoms, dtype=BF16), shape(rows, lat_width)],
        [place, weight] + parts + far_phases + [far_charges],
        smem=1,
        name="fold_far",
    )
    far_folds = paired(far_folds, "gx", 1)
    (near_folds,) = run(
        functools.partial(fold_kernel, share, padded, grid, lat_width, 0),
        [shape(half, block_rows, atoms)],
        [place, wave_rows] + near_phases + [near_charges],
        smem=1,
        flops=1_000_000_000,
        name="fold_near",
    )
    folds = run(
        functools.partial(join_kernel, lat_width),
        [shape(block_rows, atoms)] + [shape(block_rows, atoms, dtype=BF16)] * (half - 1),
        [near_folds, far_folds],
        name="fold_join",
    )
    folds = [folds[0]] + [paired(folds[d], "gx", 2 * d) for d in range(1, half)]

    site, long, cotangent, grads, term, to_beyond = run(
        functools.partial(second_back_kernel, slots, scale, half),
        [
            shape(1, 1, atoms),
            shape(8, atoms),
            shape(features, atoms),
            shape(4, features, atoms),
            shape(features, edges, dtype=BF16),
            shape(3, features, atoms, dtype=BF16),
        ],
        [hot_back, edge_weights, turn_high, turn_low, charge_pair, sums_two, gate_two, charge,
         energy, energy_slope] + folds,
        name="second_back",
    )
    from_beyond = beyond(to_beyond, "gx")
    to_pair, middle = run(
        second_middle_kernel,
        [shape(3, features, atoms, dtype=BF16), shape(3, features, atoms)],
        [hot_back, term, cotangent],
        flops=1_000_000_000,
        name="second_middle",
    )
    from_x = [paired(to_pair, "gx", 1), from_beyond]
    sides = [
        (middle[b] + from_x[0][b].astype(F32) + from_x[1][b].astype(F32)).astype(BF16)
        for b in (0, 2)
    ]
    from_y = [paired(sides[0], "gy", 1), beyond(sides[1], "gy")]
    (edge,) = run(
        functools.partial(second_edge_kernel, slots),
        [shape(32, edges)],
        [back, feature, grads],
        flops=1_000_000_000,
        name="second_edge",
    )
    to_pair, middle, to_beyond = run(
        functools.partial(first_back_kernel, slots),
        [shape(3, 8, atoms)] * 3,
        [ids, basis, slope, unit, kind_high, kind_low, turn_high, turn_low, sums_one, gate_one, edge,
         long, middle] + from_x + from_y,
        name="first_back",
    )
    total = middle + paired(to_pair, "gx", 1) + beyond(to_beyond, "gx")
    total = total[1] + paired(total[0], "gy", 1) + beyond(total[2], "gy")
    forces = -total[None, :3, None, :]
    return (forces.transpose(0, 2, 1, 3), site)


def solution(mesh):
    in_specs = (
        P("gx", "gy", None, None),
        P("gx", "gy", None),
        P("gx", "gy", None, None),
        P("gx", "gy", None),
        P(),
        P(),
        P(),
        P(),
        P(),
        P(),
        P(),
    )
    out_specs = (P("gx", "gy", None, None), P("gx", "gy", None))
    return jax.shard_map(
        per_device, mesh=mesh, in_specs=in_specs, out_specs=out_specs, check_vma=False
    )
```

```python
import functools
import math

import jax
import jax.numpy as jnp
import numpy as np
from jax import lax
from jax.experimental import pallas as pl
from jax.experimental.pallas import tpu as pltpu
from jax.sharding import PartitionSpec as P

cell_width = 10.0
box_height = 30.0
cut_radius = 50.0
soften = 0.25
screen = 0.5
smear_width = 0.5
WAVE_REACH = 8
F32 = jnp.float32
BF16 = jnp.bfloat16
CENTRE = 4


def paired(block, axis, mask):
    return lax.ppermute(block, axis, [(i ^ mask, i) for i in range(lax.axis_size(axis))])


def beyond(block, axis):
    count = lax.axis_size(axis)
    route = [((i + (1 if i % 2 else -1)) % count, i) for i in range(count)]
    return lax.ppermute(block, axis, route)


def around(block, beside):
    column = jnp.stack([paired(block, "gy", 1), block, beyond(block, "gy")])
    column, beside = lax.optimization_barrier((column, beside))
    return [paired(column, "gx", 1), column, beyond(column, "gx")], beside


def whole(space=pltpu.VMEM):
    return pl.BlockSpec(memory_space=space)


def run(kernel, outs, args, scratch=(), smem=0, hbm=0, flops=10_000_000, grant=16, name=None):
    specs = [whole(pltpu.SMEM)] * smem + [whole(pltpu.HBM)] * hbm
    specs += [whole()] * (len(args) - smem - hbm)
    return list(
        pl.pallas_call(
            kernel,
            out_shape=outs,
            in_specs=specs,
            out_specs=[whole() for _ in outs],
            scratch_shapes=list(scratch),
            compiler_params=pltpu.CompilerParams(vmem_limit_bytes=grant * 1024 * 1024),
            cost_estimate=pl.CostEstimate(
                flops=flops, bytes_accessed=1_000_000, transcendentals=0
            ),
            name=name,
        )(*args)
    )


def shape(*dims, dtype=F32):
    return jax.ShapeDtypeStruct(dims, dtype)


def split(value):
    high = value.astype(BF16)
    return high, (value - high.astype(F32)).astype(BF16)


def dot(left, right, contract=((1,), (0,))):
    return lax.dot_general(left, right, (contract, ((), ())), preferred_element_type=F32)


def dot3(left, right):
    left_high, left_low = split(left)
    right_high, right_low = split(right)
    return dot(left_high, right_high) + (dot(left_high, right_low) + dot(left_low, right_high))


def dot_split(left, right):
    right_high, right_low = split(right)
    return dot(left[0], right_high) + (dot(left[0], right_low) + dot(left[1], right_high))


def sin_cos(turns):
    quarter = jnp.round(turns * 4.0)
    x = (turns - quarter * 0.25) * (2.0 * math.pi)
    z = x * x
    sine = ((-1.9515295891e-4 * z + 8.3321608736e-3) * z - 1.6666654611e-1) * (z * x) + x
    cosine = (2.443315711809948e-5 * z - 1.388731625493765e-3) * z + 4.166664568298827e-2
    cosine = cosine * (z * z) - 0.5 * z + 1.0
    k = quarter.astype(jnp.int32) & 3
    odd = (k & 1) == 1
    by_sine = jnp.where(odd, cosine, sine)
    by_cosine = jnp.where(odd, sine, cosine)
    return (
        jnp.where(k >= 2, -by_sine, by_sine),
        jnp.where((k == 1) | (k == 2), -by_cosine, by_cosine),
    )


def stacked_left(value):
    high = value.astype(BF16).astype(F32)
    rows = jnp.concatenate([high, high, value - high, jnp.zeros_like(high)], axis=0)
    return rows.T.astype(BF16)


def stacked_right(value):
    high = value.astype(BF16).astype(F32)
    return jnp.concatenate([high, value - high, high, jnp.zeros_like(high)], axis=0).astype(BF16)


def silu_pair(value):
    gate = 1.0 / (1.0 + jnp.exp(-value))
    return value * gate, gate * (1.0 + value * (1.0 - gate))


def onehot_kinds(kinds, rows):
    levels = lax.broadcasted_iota(jnp.int32, (rows, kinds.shape[1]), 0).astype(F32)
    return jnp.where(kinds == levels, 1.0, 0.0)


def embedding_stack(embed):
    high = embed.astype(BF16).astype(F32)
    rest = embed - high
    middle = rest.astype(BF16).astype(F32)
    rows = jnp.concatenate([high, middle, rest - middle, jnp.zeros_like(high)], axis=0)
    return rows.T.astype(BF16)


def embedded(stack, kinds):
    hot = onehot_kinds(kinds, 8)
    return dot(stack, jnp.concatenate([hot, hot, hot, jnp.zeros_like(hot)], axis=0).astype(BF16))


def weights_of(stack_ref, part, rows):
    return dot(stack_ref[1 if part else 0], stacked_right(rows))


def mixed(sums, high_ref, low_ref, layer):
    squares = sums[1] * sums[1] + sums[2] * sums[2] + sums[3] * sums[3]
    both = jnp.concatenate([sums[0], squares], axis=0)
    return silu_pair(dot_split((high_ref[layer], low_ref[layer]), both))


def edge_parts(basis, unit):
    return [basis] + [basis * unit[i : i + 1] for i in range(3)]


def pack_kernel(place_ref, position_ref, species_ref, out_ref, place, kind, sems):
    copies = [
        pltpu.make_async_copy(position_ref, place, sems.at[0]),
        pltpu.make_async_copy(species_ref, kind, sems.at[1]),
    ]
    for copy in copies:
        copy.start()
    for copy in copies:
        copy.wait()
    rows = [place[0, i] for i in range(3)] + [kind[0].astype(F32)]
    atoms = rows[0].shape[1]
    out_ref[...] = jnp.concatenate(
        [row[:, s : s + 128] for s in range(0, atoms, 128) for row in rows], axis=0
    )


def radial_left(radial):
    high = radial.astype(BF16).astype(F32)
    low = radial - high
    top = jnp.concatenate([high, high], axis=1)
    end = jnp.concatenate([low, jnp.zeros_like(low)], axis=1)
    return jnp.concatenate([top, end], axis=0).astype(BF16)


def put_split(value, high_ref, low_ref, *at):
    high, low = split(value)
    high_ref[at] = high
    low_ref[at] = low


def slot_order(ids, place_ref, atoms):
    cell = ids >> (atoms.bit_length() - 1) if atoms & (atoms - 1) == 0 else ids // atoms
    a = (cell * 11) >> 5
    b = cell - 3 * a
    a = jnp.where((place_ref[0] & 1) == 0, 2 - a, a)
    b = jnp.where((place_ref[1] & 1) == 0, 2 - b, b)
    return ids + (3 * a + b - cell) * atoms


def fetch(sources, targets, sems):
    copies = [
        pltpu.make_async_copy(source, target, sems.at[i])
        for i, (source, target) in enumerate(zip(sources, targets))
    ]
    for copy in copies:
        copy.start()
    for copy in copies:
        copy.wait()


def prep_first_kernel(norm, place_ref, ids_in, count_in, embed_in, radial_in, mixing_in, id_ref, count_ref,
                      embed_out, kind_left, left_out, back_out, kind_high, kind_low, mix_high,
                      mix_low, turn_high, turn_low, embed_ref, radial_ref, mixing_ref, sems):
    fetch(
        [ids_in, count_in, embed_in, radial_in, mixing_in],
        [id_ref, count_ref, embed_ref, radial_ref, mixing_ref],
        sems,
    )
    id_ref[...] = slot_order(id_ref[...], place_ref, count_ref.shape[2])
    embed = embed_ref[...]
    kinds = embed.shape[0]
    for path in range(2):
        radial = radial_ref[0, path] * norm
        rows = jnp.concatenate([radial * embed[s : s + 1] for s in range(kinds)], axis=0)
        kind_left[path] = stacked_left(rows)
        put_split(rows, kind_high, kind_low, path)
        radial = radial_ref[1, path] * norm
        left_out[path] = stacked_left(radial)
        back_out[path] = radial_left(radial)
    for layer in range(2):
        scalar, vector = mixing_ref[layer, 0], mixing_ref[layer, 1]
        put_split(jnp.concatenate([scalar.T, vector.T], axis=1), mix_high, mix_low, layer)
        put_split(jnp.concatenate([scalar, 2.0 * vector], axis=0), turn_high, turn_low, layer)
    embed = jnp.concatenate([embed, jnp.zeros((8 - kinds, embed.shape[1]), F32)], axis=0)
    embed_out[...] = embedding_stack(embed)


def prep_second_kernel(read_in, hidden_in, charge_in, read_ref, hidden_high, hidden_low,
                       hidden_turn_high, hidden_turn_low, charge_pair, hidden_ref, charge_ref, sems):
    fetch([read_in, hidden_in, charge_in], [read_ref, hidden_ref, charge_ref], sems)
    put_split(hidden_ref[...].T, hidden_high, hidden_low, Ellipsis)
    put_split(hidden_ref[...], hidden_turn_high, hidden_turn_low, Ellipsis)
    charge = charge_ref[...]
    high = charge.astype(BF16).astype(F32)
    charge_pair[0] = high.astype(BF16)
    charge_pair[1] = (charge - high).astype(BF16)


def hot_kernel(first, ids_ref, hot_ref):
    edges = ids_ref.shape[1]
    for start in range(0, edges, 256):
        lanes = slice(start, start + 256)
        hot_ref[:, lanes] = hot_columns(ids_ref[:, lanes] - first, hot_ref.shape[0])


def hot_back_kernel(ids_ref, hot_ref):
    edges = ids_ref.shape[1]
    entry = lax.broadcasted_iota(jnp.int32, (128, hot_ref.shape[1]), 1).astype(F32)
    for start in range(0, edges, 128):
        row = jnp.broadcast_to(ids_ref[:, start : start + 128].astype(F32), (8, 128))
        column = row.T[:, 0:1]
        hot_ref[start : start + 128] = jnp.where(column == entry, 1.0, 0.0).astype(BF16)


def unfold_block(block, atoms):
    parts = atoms // 128
    return jnp.concatenate([block[4 * s : 4 * s + 4] for s in range(parts)], axis=1)


def first_kernel(slots, place_ref, ids_ref, count_ref, embed_ref, kind_left, mix_high, mix_low,
                 pair_ref, column_ref, beyond_ref, low_ref, basis_ref, slope_ref, unit_ref, sums_ref,
                 gate_ref):
    atoms = low_ref.shape[1]
    ids = ids_ref[...]
    frame = [pair_ref, column_ref, beyond_ref]
    own = unfold_block(column_ref[1], atoms)
    own = jnp.concatenate([own, jnp.zeros_like(own)], axis=0)
    per_cell = atoms // 128
    places = lax.broadcasted_iota(jnp.int32, (4 * per_cell, 128), 0)
    upper = places >> 2
    kind_of_row = places & 3
    rows = []
    to_x = jnp.where(kind_of_row == 0, cell_width, 0.0)
    to_x = jnp.where((place_ref[0] & 1) == 0, to_x, -to_x)
    to_y = jnp.where(kind_of_row == 1, cell_width, 0.0)
    to_y = jnp.where((place_ref[1] & 1) == 0, to_y, -to_y)
    for a in range(3):
        for b in range(3):
            rows.append(frame[a][b] + ((1 - a) * to_x + (1 - b) * to_y))
    pieces = []
    for start in range(0, ids.shape[1], 128):
        part = jnp.broadcast_to(ids[:, start : start + 128], places.shape)
        lane, half = part & 127, (part >> 7) - upper
        found = jnp.zeros(places.shape, F32)
        for cell, block in enumerate(rows):
            value = jnp.take_along_axis(block, lane, axis=1)
            found = jnp.where(half == per_cell * cell, value, found)
        total = found[:4]
        for s in range(1, per_cell):
            total = total + found[4 * s : 4 * s + 4]
        pieces.append(jnp.concatenate([total, total], axis=0))
    found = jnp.concatenate(pieces, axis=1)
    relative = found - jnp.concatenate([own] * slots, axis=1)
    rel = [relative[i : i + 1] for i in range(3)]
    distance = jnp.sqrt(rel[0] * rel[0] + rel[1] * rel[1] + rel[2] * rel[2] + soften)
    inverse = 1.0 / distance
    order = (lax.broadcasted_iota(jnp.int32, (8, 1), 0) + 1).astype(F32)
    sine, cosine = sin_cos((order * (0.5 / cut_radius)) * distance)
    wave = sine / ((order * (math.pi / cut_radius)) * distance)
    count = count_ref[0]
    live = jnp.concatenate([jnp.where(count > n, 1.0, 0.0) for n in range(slots)], axis=1)
    basis = wave * live
    basis_ref[...] = basis
    slope_ref[...] = (cosine - wave) * (inverse * live)
    kinds = found[3:4]
    unit = jnp.concatenate(
        [r * inverse for r in rel] + [inverse, kinds] + [jnp.zeros_like(kinds)] * 3, axis=0
    )
    unit_ref[...] = unit
    stack = embed_ref[...]
    parts = edge_parts(basis, unit)
    species = kind_left.shape[2] // 32
    by_kind = [[None] * species for _ in range(4)]
    for n in range(slots):
        lanes = slice(n * atoms, (n + 1) * atoms)
        kind = jnp.broadcast_to(kinds[:, lanes], (8, atoms))
        for k in range(species):
            match = kind == float(k)
            for part in range(4):
                term = jnp.where(match, parts[part][:, lanes], 0.0)
                old = by_kind[part][k]
                by_kind[part][k] = term if old is None else old + term
    stacks = [stacked_right(jnp.concatenate(rows, axis=0)) for rows in by_kind]
    vectors = dot(kind_left[1], jnp.concatenate(stacks[1:], axis=1))
    sums = [dot(kind_left[0], stacks[0])]
    sums += [vectors[:, i * atoms : (i + 1) * atoms] for i in range(3)]
    step, gate = mixed(sums, mix_high, mix_low, 0)
    low_ref[...] = (embedded(stack, own[3:4]) + step).astype(BF16)
    for part in range(3):
        sums_ref[part] = sums[part + 1]
    gate_ref[...] = gate


def hot_columns(ids, rows):
    place = lax.broadcasted_iota(jnp.int32, (rows, ids.shape[1]), 0)
    return jnp.where(ids == place, 1.0, 0.0).astype(BF16)


def second_near_kernel(slots, basis_ref, unit_ref, left_ref, hot_ref, column_ref, weight_ref,
                       near_ref):
    atoms = column_ref.shape[2]
    parts = edge_parts(basis_ref[...], unit_ref[...])
    source = jnp.concatenate([column_ref[b] for b in range(3)], axis=1)
    for n in range(slots):
        lanes = slice(n * atoms, (n + 1) * atoms)
        for part in range(4):
            weight_ref[part, :, lanes] = weights_of(left_ref, part, parts[part][:, lanes])
        near_ref[:, lanes] = dot(source, hot_ref[3 * atoms : 6 * atoms, lanes])


def second_side_kernel(slots, hot_ref, near_ref, pair_ref, out_ref):
    atoms = pair_ref.shape[2]
    source = jnp.concatenate([pair_ref[b] for b in range(3)], axis=1)
    for n in range(slots):
        lanes = slice(n * atoms, (n + 1) * atoms)
        out_ref[:, lanes] = near_ref[:, lanes] + dot(source, hot_ref[: 3 * atoms, lanes])


def second_kernel(slots, hot_ref, weight_ref, near_ref, mix_high, mix_low, hidden_high, hidden_low,
                  turn_high, turn_low, out_ref, charge_ref, cell_ref, column_ref, beyond_ref,
                  feature_ref, sums_ref, gate_ref, packed_ref, full_charge_ref, energy_ref,
                  slope_ref):
    atoms = column_ref.shape[2]
    source = jnp.concatenate([beyond_ref[b] for b in range(3)], axis=1)
    sums = [None] * 4
    for n in range(slots):
        lanes = slice(n * atoms, (n + 1) * atoms)
        feature = near_ref[:, lanes] + dot(source, hot_ref[:, lanes])
        feature_ref[:, lanes] = feature.astype(BF16)
        for part in range(4):
            term = weight_ref[part, :, lanes] * feature
            sums[part] = term if sums[part] is None else sums[part] + term
    step, gate = mixed(sums, mix_high, mix_low, 1)
    hidden = column_ref[1].astype(F32) + step
    for part in range(3):
        sums_ref[part] = sums[part + 1]
    gate_ref[...] = gate
    charge = dot_split((charge_ref[0], charge_ref[1]), hidden)
    full_charge_ref[...] = charge
    place = unfold_block(cell_ref[1], atoms)[:3]
    high = place.astype(BF16).astype(F32)
    rest = place - high
    middle = rest.astype(BF16).astype(F32)
    zero = jnp.zeros((packed_ref.shape[0] - charge.shape[0] - 9, atoms), F32)
    packed_ref[...] = jnp.concatenate([charge, high, middle, rest - middle, zero], axis=0).astype(
        BF16
    )
    value, slope = silu_pair(dot_split((hidden_high[...], hidden_low[...]), hidden))
    out = out_ref[...].T
    energy_ref[...] = jnp.sum(value * out, axis=0, keepdims=True)
    slope_ref[...] = dot_split((turn_high[...], turn_low[...]), slope * out)


def message_grads(cotangent, gate_ref, sums_ref, high_ref, low_ref, layer):
    pre = cotangent * gate_ref[...]
    both = dot_split((high_ref[layer], low_ref[layer]), pre)
    half = both.shape[0] // 2
    return [both[:half]] + [both[half:] * sums_ref[i] for i in range(3)]


def radial_grad(left, value):
    high, low = split(value)
    both = dot(left, jnp.concatenate([high, low], axis=0))
    half = both.shape[0] // 2
    return both[:half] + both[half:]


def second_back_kernel(slots, scale, count, hot_ref, weight_ref, turn_high, turn_low, charge_ref,
                       sums_ref, gate_ref, full_charge_ref, energy_ref, slope_ref, *refs):
    folds, refs = refs[:count], refs[count:]
    site_ref, long_ref, cotangent_ref, grad_ref, term_ref, sides_ref, beyond_ref, pair_ref = refs
    atoms = gate_ref.shape[1]
    total = folds[0][...].astype(F32)
    for part in folds[1:]:
        total = total + part[...].astype(F32)
    wide = full_charge_ref.shape[0]
    potential = total[:wide] * (2.0 * scale)
    slopes = total[wide : wide + 3] + total[wide + 3 : wide + 6] + total[wide + 6 : wide + 9]
    long_ref[...] = jnp.concatenate(
        [slopes * (2.0 * scale), jnp.zeros((5, atoms), F32)], axis=0
    )
    site_ref[0] = energy_ref[...] + 0.5 * jnp.sum(
        full_charge_ref[...] * potential, axis=0, keepdims=True
    )
    high, low = split(potential)
    turned = ((0,), (0,))
    cotangent = slope_ref[...] + (
        dot(charge_ref[0], high, turned)
        + (dot(charge_ref[0], low, turned) + dot(charge_ref[1], high, turned))
    )
    cotangent_ref[...] = cotangent
    grads = message_grads(cotangent, gate_ref, sums_ref, turn_high, turn_low, 1)
    for part in range(4):
        grad_ref[part] = grads[part]
    for n in range(slots):
        lanes = slice(n * atoms, (n + 1) * atoms)
        term = weight_ref[0, :, lanes] * grads[0]
        for part in range(1, 4):
            term = term + weight_ref[part, :, lanes] * grads[part]
        term_ref[:, lanes] = term.astype(BF16)
    for b in range(3):
        start = (6 + b) * atoms
        grad = dot(term_ref[...], hot_ref[:, start : start + atoms]).astype(BF16)
        if b == 1:
            beyond_ref[...] = grad
        else:
            sides_ref[b // 2] = grad
    for b in range(3):
        pair_ref[b] = dot(term_ref[...], hot_ref[:, b * atoms : (b + 1) * atoms]).astype(BF16)


def second_middle_kernel(hot_ref, term_ref, cotangent_ref, middle_ref):
    atoms = cotangent_ref.shape[1]
    for b in range(3):
        grad = dot(term_ref[...], hot_ref[:, (3 + b) * atoms : (4 + b) * atoms])
        middle_ref[b] = grad + cotangent_ref[...] if b == 1 else grad


def second_edge_kernel(slots, back_ref, feature_ref, grad_ref, edge_ref):
    atoms = grad_ref.shape[2]
    for n in range(slots):
        lanes = slice(n * atoms, (n + 1) * atoms)
        feature = feature_ref[:, lanes].astype(F32)
        for part in range(4):
            edge_ref[8 * part : 8 * part + 8, lanes] = radial_grad(
                back_ref[1 if part else 0], grad_ref[part] * feature
            )


def first_back_kernel(slots, ids_ref, basis_ref, slope_ref, unit_ref, kind_high, kind_low,
                      turn_high, turn_low, sums_ref, gate_ref, edge_ref, long_ref, middle_ref,
                      *refs):
    from_x, from_y, outs = refs[:2], refs[2:4], refs[4:]
    atoms = gate_ref.shape[1]
    cotangent = middle_ref[1]
    for block in (from_x[0][1], from_x[1][...], from_y[0][...], from_y[1][...]):
        cotangent = cotangent + block.astype(F32)
    grads = message_grads(cotangent, gate_ref, sums_ref, turn_high, turn_low, 0)
    unit = unit_ref[...]
    kinds = unit[4:5]
    by_kind = [dot_split((kind_high[0], kind_low[0]), grads[0])]
    by_kind += [dot_split((kind_high[1], kind_low[1]), grads[i]) for i in range(1, 4)]
    species = by_kind[0].shape[0] // 8
    edges = [[] for _ in range(4)]
    for n in range(slots):
        kind = jnp.broadcast_to(kinds[:, n * atoms : (n + 1) * atoms], (8, atoms))
        matches = [kind == float(k) for k in range(1, species)]
        for part in range(4):
            rows = by_kind[part]
            found = rows[:8]
            for k, match in enumerate(matches):
                found = jnp.where(match, rows[8 * k + 8 : 8 * k + 16], found)
            edges[part].append(found)
    edges = [
        edge_ref[8 * part : 8 * part + 8] + jnp.concatenate(edges[part], axis=1) for part in range(4)
    ]
    basis = basis_ref[...]
    units = [unit[i : i + 1] for i in range(3)]
    inverse = unit[3:4]
    by_basis = edges[0]
    for i in range(3):
        by_basis = by_basis + edges[i + 1] * units[i]
    by_unit = [jnp.sum(edges[i + 1] * basis, axis=0, keepdims=True) * inverse for i in range(3)]
    by_distance = jnp.sum(by_basis * slope_ref[...], axis=0, keepdims=True)
    for i in range(3):
        by_distance = by_distance - by_unit[i] * units[i]
    moves = [by_unit[i] + by_distance * units[i] for i in range(3)]
    zero = jnp.zeros_like(moves[0])
    move = jnp.concatenate(moves + [zero] * 5, axis=0)
    own = long_ref[...]
    for n in range(slots):
        own = own - move[:, n * atoms : (n + 1) * atoms]
    ids = ids_ref[...]
    lane_hot = hot_columns(ids & 127, 128)
    half = ids >> 7
    high = move.astype(BF16).astype(F32)
    both = jnp.concatenate([high, move - high], axis=0)
    per_cell = atoms // 128
    rows = jnp.concatenate(
        [jnp.where(half == h, both, 0.0).astype(BF16) for h in range(9 * per_cell)], axis=0
    )
    spread = dot(rows, lane_hot, ((1,), (1,)))
    for cell in range(9):
        found = []
        for h in range(cell * per_cell, (cell + 1) * per_cell):
            found.append(spread[16 * h : 16 * h + 8] + spread[16 * h + 8 : 16 * h + 16])
        grad = jnp.concatenate(found, axis=1)
        if cell == CENTRE:
            grad = own + grad
        outs[cell // 3][cell % 3] = grad


def pair_counts(parts):
    total = WAVE_REACH + WAVE_REACH * (2 * WAVE_REACH + 1)
    share = -(-total // parts)
    return total, share, -(-share // 16) * 16


def pair_vectors(slot, share, part):
    side = 2 * WAVE_REACH + 1
    total = WAVE_REACH + WAVE_REACH * side
    index = slot + part.astype(F32) * share
    later = index - WAVE_REACH
    row = jnp.floor((later + 0.5) * (1.0 / side))
    first = index < WAVE_REACH
    kx = jnp.where(first, 0.0, row + 1.0)
    ky = jnp.where(first, index + 1.0, later - row * side - WAVE_REACH)
    valid = jnp.where((slot < share) & (index < total), 1.0, 0.0)
    return kx, ky, valid


def count_up(rows):
    return lax.broadcasted_iota(jnp.int32, (rows, 1), 0).astype(F32)


def green_weights(share, padded, grid, place_ref, vec_ref, weight_ref):
    grid_x, grid_y = grid
    turn = 2.0 * math.pi
    side = 2 * WAVE_REACH + 1
    top = side * side * side - 1
    vec = vec_ref[...].astype(F32) + WAVE_REACH
    code = (vec[0:1] * side + vec[1:2]) * side + vec[2:3]
    code = jnp.maximum(code, top - code)
    span = 8 * share
    row = count_up(span)
    slot = jnp.floor(row * 0.125)
    height = row - 8.0 * slot + 1.0
    flat = count_up(padded)
    slot = jnp.concatenate([slot, slot, flat], axis=0)
    kz = jnp.concatenate([height, -height, jnp.zeros_like(flat)], axis=0)
    kx, ky, valid = pair_vectors(slot, share, place_ref[0])
    own = ((kx + WAVE_REACH) * side + ky + WAVE_REACH) * side + kz + WAVE_REACH
    seen = jnp.zeros((own.shape[0], 128), F32)
    for start in range(0, code.shape[1], 128):
        seen = seen + jnp.where(own == code[:, start : start + 128], 1.0, 0.0)
    count = jnp.sum(seen, axis=1, keepdims=True) * valid
    sq = (
        (kx * (turn / (grid_x * cell_width))) ** 2
        + (ky * (turn / (grid_y * cell_width))) ** 2
        + (kz * (turn / box_height)) ** 2
    )
    green = jnp.exp(-smear_width * sq) / (sq + screen * screen) * count
    weight_ref[...] = jnp.broadcast_to(green, weight_ref.shape)


def basis_rows(share, ca, sa, cb, sb):
    cc, ss, sc, cs = [], [], [], []
    for p in range(share):
        c, s = ca[p : p + 1], sa[p : p + 1]
        cc.append(c * cb)
        ss.append(s * sb)
        sc.append(s * cb)
        cs.append(c * sb)
    return cc, ss, sc, cs


def unpack_rows(block):
    half = block.shape[1] // 2
    return jnp.concatenate([block[:, :half], block[:, half:]], axis=0)


def pack_rows(block):
    half = block.shape[0] // 2
    return jnp.concatenate([block[:half], block[half:]], axis=1)


def structure_kernel(share, padded, grid, wide, flip, place_ref, blocks, *refs):
    grid_x, grid_y = grid
    if flip:
        near_ref, (ca_ref, sa_ref, cb_ref, sb_ref, high_ref, low_ref, own_ref, out_ref) = (
            refs[0],
            refs[1:],
        )
        total = near_ref[...]
    else:
        ca_ref, sa_ref, cb_ref, sb_ref, high_ref, low_ref, total_ref = refs
        total = None
    col = place_ref[1].astype(F32) * (1.0 / grid_y)
    first = place_ref[0] ^ flip
    kx, ky, _ = pair_vectors(count_up(padded), share, place_ref[0])
    kz = count_up(8) + 1.0
    for d in range(grid_x // 2):
        block = blocks[d]
        charge = block[:wide]
        atoms = charge.shape[1]
        pieces = block[wide:].astype(F32)
        place = pieces[0:3] + (pieces[3:6] + pieces[6:9])
        row = (first ^ (2 * d)).astype(F32) * (1.0 / grid_x)
        x = place[0:1] * (1.0 / (grid_x * cell_width)) + row
        y = place[1:2] * (1.0 / (grid_y * cell_width)) + col
        sa, ca = sin_cos(kx * x + ky * y)
        sb, cb = sin_cos(kz * (place[2:3] * (1.0 / box_height)))
        lanes = pl.ds(d * atoms, atoms)
        ca_ref[:, lanes] = ca
        sa_ref[:, lanes] = sa
        cb_ref[:, lanes] = cb
        sb_ref[:, lanes] = sb
        cc, ss, sc, cs = basis_rows(share, ca, sa, cb, sb)
        high, low = split(jnp.concatenate(cc + ss + sc + cs + [ca, sa], axis=0))
        high_ref[:, lanes] = high
        low_ref[:, lanes] = low
        term = dot(high, charge, ((1,), (1,))) + dot(low, charge, ((1,), (1,)))
        total = term if total is None else total + term
    if flip:
        packed = pack_rows(total)
        own_ref[...] = packed
        out_ref[...] = packed.astype(BF16)
    else:
        total_ref[...] = total


def weighted_rows(share, padded, wide, weight_ref, parts):
    packed = parts[0][...].astype(F32)
    for part in parts[1:]:
        packed = packed + part[...].astype(F32)
    struct = unpack_rows(packed)
    span = 8 * share
    cc, ss, sc, cs = (struct[i * span : (i + 1) * span] for i in range(4))
    weight = weight_ref[:, :wide]
    plus, minus, flat = weight[:span], weight[span : 2 * span], weight[2 * span :]
    re_plus, im_plus = plus * (cc - ss), plus * (sc + cs)
    re_minus, im_minus = minus * (cc + ss), minus * (sc - cs)
    rows = jnp.concatenate(
        [
            re_plus + re_minus,
            re_minus - re_plus,
            im_plus + im_minus,
            im_plus - im_minus,
            flat * struct[4 * span : 4 * span + padded],
            flat * struct[4 * span + padded :],
        ],
        axis=0,
    )
    return rows


def fold_kernel(share, padded, grid, wide, flip, place_ref, *refs):
    grid_x, grid_y = grid
    turn = 2.0 * math.pi
    if flip:
        weight_ref, parts, refs = refs[0], refs[1 : 1 + grid_y], refs[1 + grid_y :]
        rows = weighted_rows(share, padded, wide, weight_ref, parts)
        refs, rows_ref = refs[:-1], refs[-1]
        rows_ref[...] = rows
    else:
        rows, refs = refs[0][...], refs[1:]
    ca_ref, sa_ref, cb_ref, sb_ref, high_ref, low_ref, blocks, out_ref = refs
    row_high, row_low = split(rows)
    row_pair = jnp.concatenate([row_high, row_low], axis=1)
    turned = rows.T
    t_high, t_low = split(turned)
    t_both = jnp.concatenate([t_high, t_low], axis=0)
    span = 8 * share
    kx, ky, _ = pair_vectors(count_up(padded), share, place_ref[0])
    kx = kx * (turn / (grid_x * cell_width))
    ky = ky * (turn / (grid_y * cell_width))
    kz = (count_up(8) + 1.0) * (turn / box_height)
    for d in range(grid_x // 2):
        charge = blocks[d][:wide]
        atoms = charge.shape[1]
        lanes = pl.ds(d * atoms, atoms)
        ca, sa, cb, sb = ca_ref[:, lanes], sa_ref[:, lanes], cb_ref[:, lanes], sb_ref[:, lanes]
        bcc, bss, bsc, bcs = basis_rows(share, ca, sa, cb, sb)
        high, low = high_ref[:, lanes], low_ref[:, lanes]
        both = dot(t_both, high)
        pot = both[:wide] + both[wide:] + dot(t_high, low)
        proj = dot(row_pair, jnp.concatenate([charge, charge], axis=0))
        by_x = jnp.zeros((8, atoms), jnp.float32)
        by_y = jnp.zeros((8, atoms), jnp.float32)
        by_z = jnp.zeros((8, atoms), jnp.float32)
        for p in range(share):
            pcc, pss, psc, pcs = (
                proj[i * span + 8 * p : i * span + 8 * p + 8] for i in range(4)
            )
            slope = bcs[p] * pss - bsc[p] * pcc + bcc[p] * psc - bss[p] * pcs
            by_x = by_x + kx[p : p + 1] * slope
            by_y = by_y + ky[p : p + 1] * slope
            by_z = by_z + (bsc[p] * pss - bcs[p] * pcc - bss[p] * psc + bcc[p] * pcs)
        flat_slope = ca * proj[4 * span + padded :] - sa * proj[4 * span : 4 * span + padded]
        grad_x = jnp.sum(by_x, axis=0, keepdims=True) + jnp.sum(kx * flat_slope, axis=0, keepdims=True)
        grad_y = jnp.sum(by_y, axis=0, keepdims=True) + jnp.sum(ky * flat_slope, axis=0, keepdims=True)
        grad_z = jnp.sum(kz * by_z, axis=0, keepdims=True)
        slopes = jnp.concatenate([grad_x, grad_y, grad_z], axis=0)
        out_ref[d] = pieced(pot, slopes, out_ref.shape[1]).astype(out_ref.dtype)


def pieced(pot, slopes, rows):
    high = slopes.astype(BF16).astype(F32)
    rest = slopes - high
    middle = rest.astype(BF16).astype(F32)
    zero = jnp.zeros((rows - pot.shape[0] - 9, pot.shape[1]), F32)
    return jnp.concatenate([pot, high, middle, rest - middle, zero], axis=0)


def unpieced(block, wide):
    slopes = block[wide : wide + 3] + (block[wide + 3 : wide + 6] + block[wide + 6 : wide + 9])
    return block[:wide], slopes


def join_kernel(wide, near_ref, far_ref, own_ref, *outs):
    for d in range(near_ref.shape[0]):
        pot, slopes = unpieced(near_ref[d], wide)
        pot_far, slopes_far = unpieced(far_ref[d].astype(F32), wide)
        block = pieced(pot + pot_far, slopes + slopes_far, near_ref.shape[1])
        if d:
            outs[d - 1][...] = block.astype(BF16)
        else:
            own_ref[...] = block


def per_device(
    positions,
    species,
    neighbours,
    counts,
    species_embed,
    radial,
    mixing,
    read_hidden,
    read_out,
    charge_map,
    wavevectors,
):
    atoms = positions.shape[3]
    slots = neighbours.shape[3]
    features, lat_width = charge_map.shape
    wave_count = wavevectors.shape[1]
    grid = lax.axis_size("gx"), lax.axis_size("gy")
    grid_x, grid_y = grid
    edges = slots * atoms
    scale = 1.0 / math.sqrt(wave_count * lat_width * atoms * grid_x * grid_y)
    place = jnp.stack([lax.axis_index("gx"), lax.axis_index("gy")]).astype(jnp.int32)
    _, share, padded = pair_counts(grid_x)
    ids = neighbours.transpose(0, 3, 1, 2).reshape(1, edges)
    dma = pltpu.SemaphoreType.DMA
    shown = positions.transpose(0, 2, 1, 3)

    (own,) = run(
        pack_kernel,
        [shape(4 * atoms // 128, 128)],
        [place, shown, species],
        scratch=[
            pltpu.VMEM(shown.shape, F32),
            pltpu.VMEM(species.shape, jnp.int32),
            dma((2,)),
        ],
        smem=1,
        hbm=2,
        flops=10_000_000_000,
        name="pack",
    )
    norm = 1.0 / math.sqrt(slots)
    kind_rows = 8 * species_embed.shape[0]
    low_pair = lambda *dims: [shape(*dims, dtype=BF16)] * 2
    (ids, counts, embed, kind_left, left, back, kind_high, kind_low, mix_high, mix_low, turn_high,
     turn_low) = run(
        functools.partial(prep_first_kernel, norm),
        [
            shape(1, edges, dtype=jnp.int32),
            shape(*counts.shape, dtype=jnp.int32),
            shape(features, 32, dtype=BF16),
            shape(2, features, 4 * kind_rows, dtype=BF16),
            shape(2, features, 32, dtype=BF16),
            shape(2, 16, 2 * features, dtype=BF16),
        ]
        + low_pair(2, kind_rows, features)
        + low_pair(2, features, 2 * features)
        + low_pair(2, 2 * features, features),
        [place, ids, counts, species_embed, radial, mixing],
        scratch=[
            pltpu.VMEM(species_embed.shape, F32),
            pltpu.VMEM(radial.shape, F32),
            pltpu.VMEM(mixing.shape, F32),
            dma((5,)),
        ],
        smem=1,
        hbm=5,
        name="prep_first",
    )
    cells, ids = around(own, ids)
    (hot,) = run(
        functools.partial(hot_kernel, 0),
        [shape(6 * atoms, edges, dtype=BF16)],
        [ids],
        flops=1_000_000,
        name="hot",
    )
    (hot_beyond,) = run(
        functools.partial(hot_kernel, 6 * atoms),
        [shape(3 * atoms, edges, dtype=BF16)],
        [ids],
        flops=1_000_000_000,
        name="hot_beyond",
    )
    read_out, hidden_high, hidden_low, hidden_turn_high, hidden_turn_low, charge_pair = run(
        prep_second_kernel,
        [shape(1, features)]
        + low_pair(features, features)
        + low_pair(features, features)
        + [shape(2, lat_width, features, dtype=BF16)],
        [read_out[None, :], read_hidden, charge_map.T],
        scratch=[
            pltpu.VMEM(read_hidden.shape, F32),
            pltpu.VMEM((lat_width, features), F32),
            dma((3,)),
        ],
        hbm=3,
        name="prep_second",
    )
    low, basis, slope, unit, sums_one, gate_one = run(
        functools.partial(first_kernel, slots),
        [
            shape(features, atoms, dtype=BF16),
            shape(8, edges),
            shape(8, edges),
            shape(8, edges),
            shape(3, features, atoms),
            shape(features, atoms),
        ],
        [place, ids, counts, embed, kind_left, mix_high, mix_low] + cells,
        smem=1,
        name="first",
    )
    hidden, hot = around(low, hot)
    edge_weights, near = run(
        functools.partial(second_near_kernel, slots),
        [shape(4, features, edges), shape(features, edges)],
        [basis, unit, left, hot, hidden[1]],
        flops=2_000_000_000,
        name="second_near",
    )
    (near,) = run(
        functools.partial(second_side_kernel, slots),
        [shape(features, edges)],
        [hot, near, hidden[0]],
        flops=1_000_000_000,
        name="second_side",
    )
    block_rows = -(-(lat_width + 9) // 16) * 16
    feature, sums_two, gate_two, packed, charge, energy, energy_slope = run(
        functools.partial(second_kernel, slots),
        [
            shape(features, edges, dtype=BF16),
            shape(3, features, atoms),
            shape(features, atoms),
            shape(block_rows, atoms, dtype=BF16),
            shape(lat_width, atoms),
            shape(1, atoms),
            shape(features, atoms),
        ],
        [hot_beyond, edge_weights, near, mix_high, mix_low, hidden_high, hidden_low, hidden_turn_high,
         hidden_turn_low, read_out, charge_pair, cells[1], hidden[1], hidden[2]],
        name="second",
    )
    half = grid_x // 2
    near_charges = jnp.stack([packed] + [paired(packed, "gx", 2 * d) for d in range(1, half)])
    (weight,) = run(
        functools.partial(green_weights, share, padded, grid),
        [shape(16 * share + padded, 128)],
        [place, wavevectors],
        smem=1,
        name="green",
    )
    near_charges, weight = lax.optimization_barrier((near_charges, weight))
    far_charges = paired(near_charges, "gx", 1)
    span = half * atoms
    rows = 32 * share + 2 * padded
    phase_shapes = [
        shape(padded, span),
        shape(padded, span),
        shape(8, span),
        shape(8, span),
        shape(rows, span, dtype=BF16),
        shape(rows, span, dtype=BF16),
    ]
    *near_phases, near_total = run(
        functools.partial(structure_kernel, share, padded, grid, lat_width, 0),
        phase_shapes + [shape(rows, lat_width)],
        [place, near_charges],
        smem=1,
        flops=1_000_000_000,
        name="structure_near",
    )
    *far_phases, own_part, part = run(
        functools.partial(structure_kernel, share, padded, grid, lat_width, 1),
        phase_shapes
        + [
            shape(rows // 2, 2 * lat_width),
            shape(rows // 2, 2 * lat_width, dtype=BF16),
        ],
        [place, far_charges, near_total],
        smem=1,
        name="structure_far",
    )
    parts = [own_part] + [paired(part, "gy", d) for d in range(1, grid_y)]
    (hot_back,) = run(
        hot_back_kernel,
        [shape(edges, 9 * atoms, dtype=BF16)],
        [ids],
        flops=2_000_000_000,
        name="hot_back",
    )
    parts, hot_back = lax.optimization_barrier((parts, hot_back))
    far_folds, wave_rows = run(
        functools.partial(fold_kernel, share, padded, grid, lat_width, 1),
        [shape(half, block_rows, atoms, dtype=BF16), shape(rows, lat_width)],
        [place, weight] + parts + far_phases + [far_charges],
        smem=1,
        name="fold_far",
    )
    far_folds = paired(far_folds, "gx", 1)
    (near_folds,) = run(
        functools.partial(fold_kernel, share, padded, grid, lat_width, 0),
        [shape(half, block_rows, atoms)],
        [place, wave_rows] + near_phases + [near_charges],
        smem=1,
        flops=1_000_000_000,
        name="fold_near",
    )
    folds = run(
        functools.partial(join_kernel, lat_width),
        [shape(block_rows, atoms)] + [shape(block_rows, atoms, dtype=BF16)] * (half - 1),
        [near_folds, far_folds],
        name="fold_join",
    )
    folds = [folds[0]] + [paired(folds[d], "gx", 2 * d) for d in range(1, half)]

    site, long, cotangent, grads, term, to_sides, to_beyond, to_pair = run(
        functools.partial(second_back_kernel, slots, scale, half),
        [
            shape(1, 1, atoms),
            shape(8, atoms),
            shape(features, atoms),
            shape(4, features, atoms),
            shape(features, edges, dtype=BF16),
            shape(2, features, atoms, dtype=BF16),
            shape(features, atoms, dtype=BF16),
            shape(3, features, atoms, dtype=BF16),
        ],
        [hot_back, edge_weights, turn_high, turn_low, charge_pair, sums_two, gate_two, charge,
         energy, energy_slope] + folds,
        name="second_back",
    )
    from_pair, from_sides = paired(to_pair, "gx", 1), beyond(to_sides, "gx")
    (middle,) = run(
        second_middle_kernel,
        [shape(3, features, atoms)],
        [hot_back, term, cotangent],
        flops=1_000_000_000,
        name="second_middle",
    )
    sides = [
        (middle[2 * b] + from_pair[2 * b].astype(F32) + from_sides[b].astype(F32)).astype(BF16)
        for b in range(2)
    ]
    sides, to_beyond = lax.optimization_barrier((sides, to_beyond))
    from_beyond = beyond(to_beyond, "gx")
    from_y = [paired(sides[0], "gy", 1), beyond(sides[1], "gy")]
    (edge,) = run(
        functools.partial(second_edge_kernel, slots),
        [shape(32, edges)],
        [back, feature, grads],
        flops=1_000_000_000,
        name="second_edge",
    )
    to_pair, middle, to_beyond = run(
        functools.partial(first_back_kernel, slots),
        [shape(3, 8, atoms)] * 3,
        [ids, basis, slope, unit, kind_high, kind_low, turn_high, turn_low, sums_one, gate_one, edge,
         long, middle, from_pair, from_beyond] + from_y,
        name="first_back",
    )
    total = middle + paired(to_pair, "gx", 1) + beyond(to_beyond, "gx")
    total = total[1] + paired(total[0], "gy", 1) + beyond(total[2], "gy")
    forces = -total[None, :3, None, :]
    return (forces.transpose(0, 2, 1, 3), site)


def solution(mesh):
    in_specs = (
        P("gx", "gy", None, None),
        P("gx", "gy", None),
        P("gx", "gy", None, None),
        P("gx", "gy", None),
        P(),
        P(),
        P(),
        P(),
        P(),
        P(),
        P(),
    )
    out_specs = (P("gx", "gy", None, None), P("gx", "gy", None))
    return jax.shard_map(
        per_device, mesh=mesh, in_specs=in_specs, out_specs=out_specs, check_vma=False
    )
```

```python
import functools
import math

import jax
import jax.numpy as jnp
import numpy as np
from jax import lax
from jax.experimental import pallas as pl
from jax.experimental.pallas import tpu as pltpu
from jax.sharding import PartitionSpec as P

cell_width = 10.0
box_height = 30.0
cut_radius = 50.0
soften = 0.25
screen = 0.5
smear_width = 0.5
WAVE_REACH = 8
F32 = jnp.float32
BF16 = jnp.bfloat16
CENTRE = 4


def paired(block, axis, mask):
    return lax.ppermute(block, axis, [(i ^ mask, i) for i in range(lax.axis_size(axis))])


def beyond(block, axis):
    count = lax.axis_size(axis)
    route = [((i + (1 if i % 2 else -1)) % count, i) for i in range(count)]
    return lax.ppermute(block, axis, route)


def around(block, beside):
    column = jnp.stack([paired(block, "gy", 1), block, beyond(block, "gy")])
    column, beside = lax.optimization_barrier((column, beside))
    return [paired(column, "gx", 1), column, beyond(column, "gx")], beside


def whole(space=pltpu.VMEM):
    return pl.BlockSpec(memory_space=space)


def run(kernel, outs, args, scratch=(), hbm=0, flops=10_000_000, grant=16, name=None):
    specs = [whole()] * (len(args) - hbm) + [whole(pltpu.HBM)] * hbm
    return list(
        pl.pallas_call(
            kernel,
            out_shape=outs,
            in_specs=specs,
            out_specs=[whole() for _ in outs],
            scratch_shapes=list(scratch),
            compiler_params=pltpu.CompilerParams(vmem_limit_bytes=grant * 1024 * 1024),
            cost_estimate=pl.CostEstimate(
                flops=flops, bytes_accessed=1_000_000, transcendentals=0
            ),
            name=name,
        )(*args)
    )


def shape(*dims, dtype=F32):
    return jax.ShapeDtypeStruct(dims, dtype)


def split(value):
    high = value.astype(BF16)
    return high, (value - high.astype(F32)).astype(BF16)


def dot(left, right, contract=((1,), (0,))):
    return lax.dot_general(left, right, (contract, ((), ())), preferred_element_type=F32)


def dot3(left, right):
    left_high, left_low = split(left)
    right_high, right_low = split(right)
    return dot(left_high, right_high) + (dot(left_high, right_low) + dot(left_low, right_high))


def dot_split(left, right):
    right_high, right_low = split(right)
    return dot(left[0], right_high) + (dot(left[0], right_low) + dot(left[1], right_high))


def sin_cos(turns):
    quarter = jnp.round(turns * 4.0)
    x = (turns - quarter * 0.25) * (2.0 * math.pi)
    z = x * x
    sine = ((-1.9515295891e-4 * z + 8.3321608736e-3) * z - 1.6666654611e-1) * (z * x) + x
    cosine = (2.443315711809948e-5 * z - 1.388731625493765e-3) * z + 4.166664568298827e-2
    cosine = cosine * (z * z) - 0.5 * z + 1.0
    k = quarter.astype(jnp.int32) & 3
    odd = (k & 1) == 1
    by_sine = jnp.where(odd, cosine, sine)
    by_cosine = jnp.where(odd, sine, cosine)
    return (
        jnp.where(k >= 2, -by_sine, by_sine),
        jnp.where((k == 1) | (k == 2), -by_cosine, by_cosine),
    )


def stacked_left(value):
    high = value.astype(BF16).astype(F32)
    rows = jnp.concatenate([high, high, value - high, jnp.zeros_like(high)], axis=0)
    return rows.T.astype(BF16)


def stacked_right(value):
    high = value.astype(BF16).astype(F32)
    return jnp.concatenate([high, value - high, high, jnp.zeros_like(high)], axis=0).astype(BF16)


def silu_pair(value):
    gate = 1.0 / (1.0 + jnp.exp(-value))
    return value * gate, gate * (1.0 + value * (1.0 - gate))


def onehot_kinds(kinds, rows):
    levels = lax.broadcasted_iota(jnp.int32, (rows, kinds.shape[1]), 0).astype(F32)
    return jnp.where(kinds == levels, 1.0, 0.0)


def embedding_stack(embed):
    high = embed.astype(BF16).astype(F32)
    rest = embed - high
    middle = rest.astype(BF16).astype(F32)
    rows = jnp.concatenate([high, middle, rest - middle, jnp.zeros_like(high)], axis=0)
    return rows.T.astype(BF16)


def embedded(stack, kinds):
    hot = onehot_kinds(kinds, 8)
    return dot(stack, jnp.concatenate([hot, hot, hot, jnp.zeros_like(hot)], axis=0).astype(BF16))


def weights_of(stack_ref, part, rows):
    return dot(stack_ref[1 if part else 0], stacked_right(rows))


def mixed(sums, high_ref, low_ref, layer):
    squares = sums[1] * sums[1] + sums[2] * sums[2] + sums[3] * sums[3]
    both = jnp.concatenate([sums[0], squares], axis=0)
    return silu_pair(dot_split((high_ref[layer], low_ref[layer]), both))


def edge_parts(basis, unit):
    return [basis] + [basis * unit[i : i + 1] for i in range(3)]


def pack_kernel(place_ref, position_ref, species_ref, out_ref):
    rows = [position_ref[0, i] for i in range(3)] + [species_ref[0].astype(F32)]
    atoms = rows[0].shape[1]
    out_ref[...] = jnp.concatenate(
        [row[:, s : s + 128] for row in rows for s in range(0, atoms, 128)], axis=0
    )


def radial_left(radial):
    high = radial.astype(BF16).astype(F32)
    low = radial - high
    top = jnp.concatenate([high, high], axis=1)
    end = jnp.concatenate([low, jnp.zeros_like(low)], axis=1)
    return jnp.concatenate([top, end], axis=0).astype(BF16)


def put_split(value, high_ref, low_ref, *at):
    high, low = split(value)
    high_ref[at] = high
    low_ref[at] = low


def slot_order(ids, place_ref, atoms):
    cell = ids >> (atoms.bit_length() - 1) if atoms & (atoms - 1) == 0 else ids // atoms
    a = (cell * 11) >> 5
    b = cell - 3 * a
    a = jnp.where((place_ref[0, 0:1, 0:1] & 1) == 0, 2 - a, a)
    b = jnp.where((place_ref[1, 0:1, 0:1] & 1) == 0, 2 - b, b)
    return ids + (3 * a + b - cell) * atoms


def fetch(sources, targets, sems):
    copies = [
        pltpu.make_async_copy(source, target, sems.at[i])
        for i, (source, target) in enumerate(zip(sources, targets))
    ]
    for copy in copies:
        copy.start()
    for copy in copies:
        copy.wait()


def prep_first_kernel(norm, place_ref, ids_in, count_in, embed_in, radial_in, mixing_in, id_ref, count_ref,
                      embed_out, kind_left, left_out, back_out, kind_high, kind_low, mix_high,
                      mix_low, turn_high, turn_low, embed_ref, radial_ref, mixing_ref, sems):
    fetch(
        [ids_in, count_in, embed_in, radial_in, mixing_in],
        [id_ref, count_ref, embed_ref, radial_ref, mixing_ref],
        sems,
    )
    id_ref[...] = slot_order(id_ref[...], place_ref, count_ref.shape[2])
    embed = embed_ref[...]
    kinds = embed.shape[0]
    for path in range(2):
        radial = radial_ref[0, path] * norm
        rows = jnp.concatenate([radial * embed[s : s + 1] for s in range(kinds)], axis=0)
        kind_left[path] = stacked_left(rows)
        put_split(rows, kind_high, kind_low, path)
        radial = radial_ref[1, path] * norm
        left_out[path] = stacked_left(radial)
        back_out[path] = radial_left(radial)
    for layer in range(2):
        scalar, vector = mixing_ref[layer, 0], mixing_ref[layer, 1]
        put_split(jnp.concatenate([scalar.T, vector.T], axis=1), mix_high, mix_low, layer)
        put_split(jnp.concatenate([scalar, 2.0 * vector], axis=0), turn_high, turn_low, layer)
    embed = jnp.concatenate([embed, jnp.zeros((8 - kinds, embed.shape[1]), F32)], axis=0)
    embed_out[...] = embedding_stack(embed)


def prep_second_kernel(read_in, hidden_in, charge_in, read_ref, hidden_high, hidden_low,
                       hidden_turn_high, hidden_turn_low, charge_pair, hidden_ref, charge_ref, sems):
    fetch([read_in, hidden_in, charge_in], [read_ref, hidden_ref, charge_ref], sems)
    put_split(hidden_ref[...].T, hidden_high, hidden_low, Ellipsis)
    put_split(hidden_ref[...], hidden_turn_high, hidden_turn_low, Ellipsis)
    charge = charge_ref[...]
    high = charge.astype(BF16).astype(F32)
    charge_pair[0] = high.astype(BF16)
    charge_pair[1] = (charge - high).astype(BF16)


def hot_kernel(ids_ref, hot_ref):
    edges = ids_ref.shape[1]
    for start in range(0, edges, 256):
        lanes = slice(start, start + 256)
        hot_ref[:, lanes] = hot_columns(ids_ref[:, lanes], hot_ref.shape[0])


def hot_back_kernel(ids_ref, hot_ref):
    edges = ids_ref.shape[1]
    entry = lax.broadcasted_iota(jnp.int32, (128, hot_ref.shape[1]), 1).astype(F32)
    for start in range(0, edges, 128):
        row = jnp.broadcast_to(ids_ref[:, start : start + 128].astype(F32), (8, 128))
        column = row.T[:, 0:1]
        hot_ref[start : start + 128] = jnp.where(column == entry, 1.0, 0.0).astype(BF16)


def unfold_block(block, atoms):
    parts = atoms // 128
    rows = [block[r : r + 1] for r in range(4 * parts)]
    return [jnp.concatenate(rows[q * parts : (q + 1) * parts], axis=1) for q in range(4)]


def first_kernel(slots, place_ref, ids_ref, count_ref, embed_ref, kind_left, mix_high, mix_low,
                 pair_ref, column_ref, beyond_ref, low_ref, basis_ref, slope_ref, unit_ref, sums_ref,
                 gate_ref):
    atoms = low_ref.shape[1]
    ids = ids_ref[...]
    frame = [pair_ref, column_ref, beyond_ref]
    own = unfold_block(column_ref[1], atoms)
    per_cell = atoms // 128
    places = lax.broadcasted_iota(jnp.int32, (4 * per_cell, 128), 0)
    upper = places % per_cell
    kind_of_row = places // per_cell
    rows = []
    to_x = jnp.where(kind_of_row == 0, cell_width, 0.0)
    to_x = jnp.where((place_ref[0] & 1) == 0, to_x, -to_x)
    to_y = jnp.where(kind_of_row == 1, cell_width, 0.0)
    to_y = jnp.where((place_ref[1] & 1) == 0, to_y, -to_y)
    for a in range(3):
        for b in range(3):
            rows.append(frame[a][b] + ((1 - a) * to_x + (1 - b) * to_y))
    pieces = []
    for start in range(0, ids.shape[1], 128):
        part = jnp.broadcast_to(ids[:, start : start + 128], places.shape)
        lane, half = part & 127, (part >> 7) - upper
        found = jnp.zeros(places.shape, F32)
        for cell, block in enumerate(rows):
            value = jnp.take_along_axis(block, lane, axis=1)
            found = jnp.where(half == per_cell * cell, value, found)
        total = found
        for s in range(1, per_cell):
            total = total + pltpu.roll(found, 4 * per_cell - s, 0)
        pieces.append(total)
    found = jnp.concatenate(pieces, axis=1)
    found = [found[q * per_cell : q * per_cell + 1] for q in range(4)]
    rel = [found[q] - jnp.concatenate([own[q]] * slots, axis=1) for q in range(3)]
    distance = jnp.sqrt(rel[0] * rel[0] + rel[1] * rel[1] + rel[2] * rel[2] + soften)
    inverse = 1.0 / distance
    order = (lax.broadcasted_iota(jnp.int32, (8, 1), 0) + 1).astype(F32)
    sine, cosine = sin_cos((order * (0.5 / cut_radius)) * distance)
    wave = sine / ((order * (math.pi / cut_radius)) * distance)
    count = count_ref[0]
    live = jnp.concatenate([jnp.where(count > n, 1.0, 0.0) for n in range(slots)], axis=1)
    basis = wave * live
    basis_ref[...] = basis
    slope_ref[...] = (cosine - wave) * (inverse * live)
    kinds = found[3]
    unit = jnp.concatenate(
        [r * inverse for r in rel] + [inverse, kinds] + [jnp.zeros_like(kinds)] * 3, axis=0
    )
    unit_ref[...] = unit
    stack = embed_ref[...]
    parts = edge_parts(basis, unit)
    species = kind_left.shape[2] // 32
    by_kind = [[None] * species for _ in range(4)]
    for n in range(slots):
        lanes = slice(n * atoms, (n + 1) * atoms)
        kind = jnp.broadcast_to(kinds[:, lanes], (8, atoms))
        for k in range(species):
            match = kind == float(k)
            for part in range(4):
                term = jnp.where(match, parts[part][:, lanes], 0.0)
                old = by_kind[part][k]
                by_kind[part][k] = term if old is None else old + term
    stacks = [stacked_right(jnp.concatenate(rows, axis=0)) for rows in by_kind]
    vectors = dot(kind_left[1], jnp.concatenate(stacks[1:], axis=1))
    sums = [dot(kind_left[0], stacks[0])]
    sums += [vectors[:, i * atoms : (i + 1) * atoms] for i in range(3)]
    step, gate = mixed(sums, mix_high, mix_low, 0)
    low_ref[...] = (embedded(stack, own[3]) + step).astype(BF16)
    for part in range(3):
        sums_ref[part] = sums[part + 1]
    gate_ref[...] = gate


def hot_columns(ids, rows):
    place = lax.broadcasted_iota(jnp.int32, (rows, ids.shape[1]), 0)
    return jnp.where(ids == place, 1.0, 0.0).astype(BF16)


def second_near_kernel(slots, ids_ref, basis_ref, unit_ref, left_ref, hot_ref, column_ref,
                       weight_ref, near_ref, beyond_ref):
    atoms = column_ref.shape[2]
    parts = edge_parts(basis_ref[...], unit_ref[...])
    source = jnp.concatenate([column_ref[b] for b in range(3)], axis=1)
    for n in range(slots):
        lanes = slice(n * atoms, (n + 1) * atoms)
        for part in range(4):
            weight_ref[part, :, lanes] = weights_of(left_ref, part, parts[part][:, lanes])
        near_ref[:, lanes] = dot(source, hot_ref[3 * atoms : 6 * atoms, lanes])
        beyond_ref[:, lanes] = hot_columns(ids_ref[:, lanes] - 6 * atoms, 3 * atoms)


def second_side_kernel(slots, hot_ref, near_ref, pair_ref, out_ref):
    atoms = pair_ref.shape[2]
    source = jnp.concatenate([pair_ref[b] for b in range(3)], axis=1)
    for n in range(slots):
        lanes = slice(n * atoms, (n + 1) * atoms)
        out_ref[:, lanes] = near_ref[:, lanes] + dot(source, hot_ref[: 3 * atoms, lanes])


def second_kernel(slots, hot_ref, weight_ref, near_ref, mix_high, mix_low, charge_ref, cell_ref,
                  column_ref, beyond_ref, feature_ref, sums_ref, gate_ref, packed_ref,
                  full_charge_ref, hidden_ref):
    atoms = column_ref.shape[2]
    source = jnp.concatenate([beyond_ref[b] for b in range(3)], axis=1)
    sums = [None] * 4
    for n in range(slots):
        lanes = slice(n * atoms, (n + 1) * atoms)
        feature = near_ref[:, lanes] + dot(source, hot_ref[:, lanes])
        feature_ref[:, lanes] = feature.astype(BF16)
        for part in range(4):
            term = weight_ref[part, :, lanes] * feature
            sums[part] = term if sums[part] is None else sums[part] + term
    step, gate = mixed(sums, mix_high, mix_low, 1)
    hidden = column_ref[1].astype(F32) + step
    hidden_ref[...] = hidden
    for part in range(3):
        sums_ref[part] = sums[part + 1]
    gate_ref[...] = gate
    charge = dot_split((charge_ref[0], charge_ref[1]), hidden)
    full_charge_ref[...] = charge
    place = jnp.concatenate(unfold_block(cell_ref[1], atoms)[:3], axis=0)
    high = place.astype(BF16).astype(F32)
    rest = place - high
    middle = rest.astype(BF16).astype(F32)
    zero = jnp.zeros((packed_ref.shape[0] - charge.shape[0] - 9, atoms), F32)
    packed_ref[...] = jnp.concatenate([charge, high, middle, rest - middle, zero], axis=0).astype(
        BF16
    )


def readout_kernel(hidden_high, hidden_low, turn_high, turn_low, out_ref, hidden_ref, energy_ref,
                   slope_ref):
    hidden = hidden_ref[...]
    value, slope = silu_pair(dot_split((hidden_high[...], hidden_low[...]), hidden))
    out = out_ref[...].T
    energy_ref[...] = jnp.sum(value * out, axis=0, keepdims=True)
    slope_ref[...] = dot_split((turn_high[...], turn_low[...]), slope * out)


def message_grads(cotangent, gate_ref, sums_ref, high_ref, low_ref, layer):
    pre = cotangent * gate_ref[...]
    both = dot_split((high_ref[layer], low_ref[layer]), pre)
    half = both.shape[0] // 2
    return [both[:half]] + [both[half:] * sums_ref[i] for i in range(3)]


def radial_grad(left, value):
    high, low = split(value)
    both = dot(left, jnp.concatenate([high, low], axis=0))
    half = both.shape[0] // 2
    return both[:half] + both[half:]


def second_back_kernel(slots, scale, count, hot_ref, weight_ref, turn_high, turn_low, charge_ref,
                       sums_ref, gate_ref, full_charge_ref, energy_ref, slope_ref, *refs):
    folds, refs = refs[:count], refs[count:]
    site_ref, long_ref, cotangent_ref, grad_ref, term_ref, sides_ref, beyond_ref, pair_ref = refs
    atoms = gate_ref.shape[1]
    total = folds[0][...].astype(F32)
    for part in folds[1:]:
        total = total + part[...].astype(F32)
    wide = full_charge_ref.shape[0]
    potential = total[:wide] * (2.0 * scale)
    slopes = total[wide : wide + 3] + total[wide + 3 : wide + 6] + total[wide + 6 : wide + 9]
    long_ref[...] = jnp.concatenate(
        [slopes * (2.0 * scale), jnp.zeros((5, atoms), F32)], axis=0
    )
    site_ref[0] = energy_ref[...] + 0.5 * jnp.sum(
        full_charge_ref[...] * potential, axis=0, keepdims=True
    )
    high, low = split(potential)
    turned = ((0,), (0,))
    cotangent = slope_ref[...] + (
        dot(charge_ref[0], high, turned)
        + (dot(charge_ref[0], low, turned) + dot(charge_ref[1], high, turned))
    )
    cotangent_ref[...] = cotangent
    grads = message_grads(cotangent, gate_ref, sums_ref, turn_high, turn_low, 1)
    for part in range(4):
        grad_ref[part] = grads[part]
    for n in range(slots):
        lanes = slice(n * atoms, (n + 1) * atoms)
        term = weight_ref[0, :, lanes] * grads[0]
        for part in range(1, 4):
            term = term + weight_ref[part, :, lanes] * grads[part]
        term_ref[:, lanes] = term.astype(BF16)
    for b in range(3):
        start = (6 + b) * atoms
        grad = dot(term_ref[...], hot_ref[:, start : start + atoms]).astype(BF16)
        if b == 1:
            beyond_ref[...] = grad
        else:
            sides_ref[b // 2] = grad
    for b in range(3):
        pair_ref[b] = dot(term_ref[...], hot_ref[:, b * atoms : (b + 1) * atoms]).astype(BF16)


def second_middle_kernel(hot_ref, term_ref, cotangent_ref, middle_ref):
    atoms = cotangent_ref.shape[1]
    for b in range(3):
        grad = dot(term_ref[...], hot_ref[:, (3 + b) * atoms : (4 + b) * atoms])
        middle_ref[b] = grad + cotangent_ref[...] if b == 1 else grad


def second_edge_kernel(slots, back_ref, feature_ref, grad_ref, edge_ref):
    atoms = grad_ref.shape[2]
    for n in range(slots):
        lanes = slice(n * atoms, (n + 1) * atoms)
        feature = feature_ref[:, lanes].astype(F32)
        for part in range(4):
            edge_ref[8 * part : 8 * part + 8, lanes] = radial_grad(
                back_ref[1 if part else 0], grad_ref[part] * feature
            )


def first_back_kernel(slots, ids_ref, basis_ref, slope_ref, unit_ref, kind_high, kind_low,
                      turn_high, turn_low, sums_ref, gate_ref, edge_ref, long_ref, middle_ref,
                      *refs):
    from_x, from_y, outs = refs[:2], refs[2:4], refs[4:]
    atoms = gate_ref.shape[1]
    cotangent = middle_ref[1]
    for block in (from_x[0][1], from_x[1][...], from_y[0][...], from_y[1][...]):
        cotangent = cotangent + block.astype(F32)
    grads = message_grads(cotangent, gate_ref, sums_ref, turn_high, turn_low, 0)
    unit = unit_ref[...]
    kinds = unit[4:5]
    by_kind = [dot_split((kind_high[0], kind_low[0]), grads[0])]
    by_kind += [dot_split((kind_high[1], kind_low[1]), grads[i]) for i in range(1, 4)]
    species = by_kind[0].shape[0] // 8
    edges = [[] for _ in range(4)]
    for n in range(slots):
        kind = jnp.broadcast_to(kinds[:, n * atoms : (n + 1) * atoms], (8, atoms))
        matches = [kind == float(k) for k in range(1, species)]
        for part in range(4):
            rows = by_kind[part]
            found = rows[:8]
            for k, match in enumerate(matches):
                found = jnp.where(match, rows[8 * k + 8 : 8 * k + 16], found)
            edges[part].append(found)
    edges = [
        edge_ref[8 * part : 8 * part + 8] + jnp.concatenate(edges[part], axis=1) for part in range(4)
    ]
    basis = basis_ref[...]
    units = [unit[i : i + 1] for i in range(3)]
    inverse = unit[3:4]
    by_basis = edges[0]
    for i in range(3):
        by_basis = by_basis + edges[i + 1] * units[i]
    by_unit = [jnp.sum(edges[i + 1] * basis, axis=0, keepdims=True) * inverse for i in range(3)]
    by_distance = jnp.sum(by_basis * slope_ref[...], axis=0, keepdims=True)
    for i in range(3):
        by_distance = by_distance - by_unit[i] * units[i]
    moves = [by_unit[i] + by_distance * units[i] for i in range(3)]
    zero = jnp.zeros_like(moves[0])
    move = jnp.concatenate(moves + [zero] * 5, axis=0)
    own = long_ref[...]
    for n in range(slots):
        own = own - move[:, n * atoms : (n + 1) * atoms]
    ids = ids_ref[...]
    lane_hot = hot_columns(ids & 127, 128)
    half = ids >> 7
    high = move.astype(BF16).astype(F32)
    both = jnp.concatenate([high, move - high], axis=0)
    per_cell = atoms // 128
    rows = jnp.concatenate(
        [jnp.where(half == h, both, 0.0).astype(BF16) for h in range(9 * per_cell)], axis=0
    )
    spread = dot(rows, lane_hot, ((1,), (1,)))
    for cell in range(9):
        found = []
        for h in range(cell * per_cell, (cell + 1) * per_cell):
            found.append(spread[16 * h : 16 * h + 8] + spread[16 * h + 8 : 16 * h + 16])
        grad = jnp.concatenate(found, axis=1)
        if cell == CENTRE:
            grad = own + grad
        outs[cell // 3][cell % 3] = grad


def pair_counts(parts):
    total = WAVE_REACH + WAVE_REACH * (2 * WAVE_REACH + 1)
    share = -(-total // parts)
    return total, share, -(-share // 16) * 16


def pair_vectors(slot, share, part):
    side = 2 * WAVE_REACH + 1
    total = WAVE_REACH + WAVE_REACH * side
    index = slot + part.astype(F32) * share
    later = index - WAVE_REACH
    row = jnp.floor((later + 0.5) * (1.0 / side))
    first = index < WAVE_REACH
    kx = jnp.where(first, 0.0, row + 1.0)
    ky = jnp.where(first, index + 1.0, later - row * side - WAVE_REACH)
    valid = jnp.where((slot < share) & (index < total), 1.0, 0.0)
    return kx, ky, valid


def count_up(rows):
    return lax.broadcasted_iota(jnp.int32, (rows, 1), 0).astype(F32)


def green_weights(share, padded, grid, place_ref, vec_ref, weight_ref):
    grid_x, grid_y = grid
    turn = 2.0 * math.pi
    side = 2 * WAVE_REACH + 1
    top = side * side * side - 1
    vec = vec_ref[...].astype(F32) + WAVE_REACH
    code = (vec[0:1] * side + vec[1:2]) * side + vec[2:3]
    code = jnp.maximum(code, top - code)
    span = 8 * share
    row = count_up(span)
    slot = jnp.floor(row * 0.125)
    height = row - 8.0 * slot + 1.0
    flat = count_up(padded)
    slot = jnp.concatenate([slot, slot, flat], axis=0)
    kz = jnp.concatenate([height, -height, jnp.zeros_like(flat)], axis=0)
    kx, ky, valid = pair_vectors(slot, share, place_ref[0, 0:1, 0:1])
    own = ((kx + WAVE_REACH) * side + ky + WAVE_REACH) * side + kz + WAVE_REACH
    seen = jnp.zeros((own.shape[0], 128), F32)
    for start in range(0, code.shape[1], 128):
        seen = seen + jnp.where(own == code[:, start : start + 128], 1.0, 0.0)
    count = jnp.sum(seen, axis=1, keepdims=True) * valid
    sq = (
        (kx * (turn / (grid_x * cell_width))) ** 2
        + (ky * (turn / (grid_y * cell_width))) ** 2
        + (kz * (turn / box_height)) ** 2
    )
    green = jnp.exp(-smear_width * sq) / (sq + screen * screen) * count
    weight_ref[...] = jnp.broadcast_to(green, weight_ref.shape)


def basis_rows(share, ca, sa, cb, sb):
    cc, ss, sc, cs = [], [], [], []
    for p in range(share):
        c, s = ca[p : p + 1], sa[p : p + 1]
        cc.append(c * cb)
        ss.append(s * sb)
        sc.append(s * cb)
        cs.append(c * sb)
    return cc, ss, sc, cs


def unpack_rows(block):
    half = block.shape[1] // 2
    return jnp.concatenate([block[:, :half], block[:, half:]], axis=0)


def pack_rows(block):
    half = block.shape[0] // 2
    return jnp.concatenate([block[:half], block[half:]], axis=1)


def structure_kernel(share, padded, grid, wide, flip, place_ref, blocks, *refs):
    grid_x, grid_y = grid
    if flip:
        near_ref, (ca_ref, sa_ref, cb_ref, sb_ref, high_ref, low_ref, own_ref, out_ref) = (
            refs[0],
            refs[1:],
        )
        total = near_ref[...]
    else:
        ca_ref, sa_ref, cb_ref, sb_ref, high_ref, low_ref, total_ref = refs
        total = None
    col = place_ref[1, 0:1, 0:1].astype(F32) * (1.0 / grid_y)
    first = place_ref[0, 0:1, 0:1] ^ flip
    kx, ky, _ = pair_vectors(count_up(padded), share, place_ref[0, 0:1, 0:1])
    kz = count_up(8) + 1.0
    for d in range(grid_x // 2):
        block = blocks[d]
        charge = block[:wide]
        atoms = charge.shape[1]
        pieces = block[wide:].astype(F32)
        place = pieces[0:3] + (pieces[3:6] + pieces[6:9])
        row = (first ^ (2 * d)).astype(F32) * (1.0 / grid_x)
        x = place[0:1] * (1.0 / (grid_x * cell_width)) + row
        y = place[1:2] * (1.0 / (grid_y * cell_width)) + col
        sa, ca = sin_cos(kx * x + ky * y)
        sb, cb = sin_cos(kz * (place[2:3] * (1.0 / box_height)))
        lanes = pl.ds(d * atoms, atoms)
        ca_ref[:, lanes] = ca
        sa_ref[:, lanes] = sa
        cb_ref[:, lanes] = cb
        sb_ref[:, lanes] = sb
        cc, ss, sc, cs = basis_rows(share, ca, sa, cb, sb)
        high, low = split(jnp.concatenate(cc + ss + sc + cs + [ca, sa], axis=0))
        high_ref[:, lanes] = high
        low_ref[:, lanes] = low
        term = dot(high, charge, ((1,), (1,))) + dot(low, charge, ((1,), (1,)))
        total = term if total is None else total + term
    if flip:
        packed = pack_rows(total)
        own_ref[...] = packed
        out_ref[...] = packed.astype(BF16)
    else:
        total_ref[...] = total


def weighted_rows(share, padded, wide, weight_ref, parts):
    packed = parts[0][...].astype(F32)
    for part in parts[1:]:
        packed = packed + part[...].astype(F32)
    struct = unpack_rows(packed)
    span = 8 * share
    cc, ss, sc, cs = (struct[i * span : (i + 1) * span] for i in range(4))
    weight = weight_ref[:, :wide]
    plus, minus, flat = weight[:span], weight[span : 2 * span], weight[2 * span :]
    re_plus, im_plus = plus * (cc - ss), plus * (sc + cs)
    re_minus, im_minus = minus * (cc + ss), minus * (sc - cs)
    rows = jnp.concatenate(
        [
            re_plus + re_minus,
            re_minus - re_plus,
            im_plus + im_minus,
            im_plus - im_minus,
            flat * struct[4 * span : 4 * span + padded],
            flat * struct[4 * span + padded :],
        ],
        axis=0,
    )
    return rows


def fold_kernel(share, padded, grid, wide, flip, place_ref, *refs):
    grid_x, grid_y = grid
    turn = 2.0 * math.pi
    if flip:
        weight_ref, parts, refs = refs[0], refs[1 : 1 + grid_y], refs[1 + grid_y :]
        rows = weighted_rows(share, padded, wide, weight_ref, parts)
        refs, rows_ref = refs[:-1], refs[-1]
        rows_ref[...] = rows
    else:
        rows, refs = refs[0][...], refs[1:]
    ca_ref, sa_ref, cb_ref, sb_ref, high_ref, low_ref, blocks, out_ref = refs
    row_high, row_low = split(rows)
    row_pair = jnp.concatenate([row_high, row_low], axis=1)
    turned = rows.T
    t_high, t_low = split(turned)
    t_both = jnp.concatenate([t_high, t_low], axis=0)
    span = 8 * share
    kx, ky, _ = pair_vectors(count_up(padded), share, place_ref[0, 0:1, 0:1])
    kx = kx * (turn / (grid_x * cell_width))
    ky = ky * (turn / (grid_y * cell_width))
    kz = (count_up(8) + 1.0) * (turn / box_height)
    for d in range(grid_x // 2):
        charge = blocks[d][:wide]
        atoms = charge.shape[1]
        lanes = pl.ds(d * atoms, atoms)
        ca, sa, cb, sb = ca_ref[:, lanes], sa_ref[:, lanes], cb_ref[:, lanes], sb_ref[:, lanes]
        bcc, bss, bsc, bcs = basis_rows(share, ca, sa, cb, sb)
        high, low = high_ref[:, lanes], low_ref[:, lanes]
        both = dot(t_both, high)
        pot = both[:wide] + both[wide:] + dot(t_high, low)
        proj = dot(row_pair, jnp.concatenate([charge, charge], axis=0))
        by_x = jnp.zeros((8, atoms), jnp.float32)
        by_y = jnp.zeros((8, atoms), jnp.float32)
        by_z = jnp.zeros((8, atoms), jnp.float32)
        for p in range(share):
            pcc, pss, psc, pcs = (
                proj[i * span + 8 * p : i * span + 8 * p + 8] for i in range(4)
            )
            slope = bcs[p] * pss - bsc[p] * pcc + bcc[p] * psc - bss[p] * pcs
            by_x = by_x + kx[p : p + 1] * slope
            by_y = by_y + ky[p : p + 1] * slope
            by_z = by_z + (bsc[p] * pss - bcs[p] * pcc - bss[p] * psc + bcc[p] * pcs)
        flat_slope = ca * proj[4 * span + padded :] - sa * proj[4 * span : 4 * span + padded]
        grad_x = jnp.sum(by_x, axis=0, keepdims=True) + jnp.sum(kx * flat_slope, axis=0, keepdims=True)
        grad_y = jnp.sum(by_y, axis=0, keepdims=True) + jnp.sum(ky * flat_slope, axis=0, keepdims=True)
        grad_z = jnp.sum(kz * by_z, axis=0, keepdims=True)
        slopes = jnp.concatenate([grad_x, grad_y, grad_z], axis=0)
        out_ref[d] = pieced(pot, slopes, out_ref.shape[1]).astype(out_ref.dtype)


def pieced(pot, slopes, rows):
    high = slopes.astype(BF16).astype(F32)
    rest = slopes - high
    middle = rest.astype(BF16).astype(F32)
    zero = jnp.zeros((rows - pot.shape[0] - 9, pot.shape[1]), F32)
    return jnp.concatenate([pot, high, middle, rest - middle, zero], axis=0)


def unpieced(block, wide):
    slopes = block[wide : wide + 3] + (block[wide + 3 : wide + 6] + block[wide + 6 : wide + 9])
    return block[:wide], slopes


def join_kernel(wide, near_ref, far_ref, own_ref, *outs):
    for d in range(near_ref.shape[0]):
        pot, slopes = unpieced(near_ref[d], wide)
        pot_far, slopes_far = unpieced(far_ref[d].astype(F32), wide)
        block = pieced(pot + pot_far, slopes + slopes_far, near_ref.shape[1])
        if d:
            outs[d - 1][...] = block.astype(BF16)
        else:
            own_ref[...] = block


def per_device(
    positions,
    species,
    neighbours,
    counts,
    species_embed,
    radial,
    mixing,
    read_hidden,
    read_out,
    charge_map,
    wavevectors,
):
    atoms = positions.shape[3]
    slots = neighbours.shape[3]
    features, lat_width = charge_map.shape
    wave_count = wavevectors.shape[1]
    grid = lax.axis_size("gx"), lax.axis_size("gy")
    grid_x, grid_y = grid
    edges = slots * atoms
    scale = 1.0 / math.sqrt(wave_count * lat_width * atoms * grid_x * grid_y)
    place = jnp.stack([lax.axis_index("gx"), lax.axis_index("gy")]).astype(jnp.int32)
    place = jnp.broadcast_to(place[:, None, None], (2, 8, 128))
    _, share, padded = pair_counts(grid_x)
    ids = neighbours.transpose(0, 3, 1, 2).reshape(1, edges)
    dma = pltpu.SemaphoreType.DMA
    (own,) = run(
        pack_kernel,
        [shape(4 * atoms // 128, 128)],
        [place, positions.transpose(0, 2, 1, 3), species],
        flops=10_000_000_000,
        name="pack",
    )
    norm = 1.0 / math.sqrt(slots)
    kind_rows = 8 * species_embed.shape[0]
    low_pair = lambda *dims: [shape(*dims, dtype=BF16)] * 2
    (ids, counts, embed, kind_left, left, back, kind_high, kind_low, mix_high, mix_low, turn_high,
     turn_low) = run(
        functools.partial(prep_first_kernel, norm),
        [
            shape(1, edges, dtype=jnp.int32),
            shape(*counts.shape, dtype=jnp.int32),
            shape(features, 32, dtype=BF16),
            shape(2, features, 4 * kind_rows, dtype=BF16),
            shape(2, features, 32, dtype=BF16),
            shape(2, 16, 2 * features, dtype=BF16),
        ]
        + low_pair(2, kind_rows, features)
        + low_pair(2, features, 2 * features)
        + low_pair(2, 2 * features, features),
        [place, ids, counts, species_embed, radial, mixing],
        scratch=[
            pltpu.VMEM(species_embed.shape, F32),
            pltpu.VMEM(radial.shape, F32),
            pltpu.VMEM(mixing.shape, F32),
            dma((5,)),
        ],
        hbm=5,
        name="prep_first",
    )
    cells, ids = around(own, ids)
    (hot,) = run(
        hot_kernel,
        [shape(6 * atoms, edges, dtype=BF16)],
        [ids],
        flops=1_000_000,
        name="hot",
    )
    read_out, hidden_high, hidden_low, hidden_turn_high, hidden_turn_low, charge_pair = run(
        prep_second_kernel,
        [shape(1, features)]
        + low_pair(features, features)
        + low_pair(features, features)
        + [shape(2, lat_width, features, dtype=BF16)],
        [read_out[None, :], read_hidden, charge_map.T],
        scratch=[
            pltpu.VMEM(read_hidden.shape, F32),
            pltpu.VMEM((lat_width, features), F32),
            dma((3,)),
        ],
        hbm=3,
        name="prep_second",
    )
    low, basis, slope, unit, sums_one, gate_one = run(
        functools.partial(first_kernel, slots),
        [
            shape(features, atoms, dtype=BF16),
            shape(8, edges),
            shape(8, edges),
            shape(8, edges),
            shape(3, features, atoms),
            shape(features, atoms),
        ],
        [place, ids, counts, embed, kind_left, mix_high, mix_low] + cells,
        name="first",
    )
    hidden, hot = around(low, hot)
    edge_weights, near, hot_beyond = run(
        functools.partial(second_near_kernel, slots),
        [
            shape(4, features, edges),
            shape(features, edges),
            shape(3 * atoms, edges, dtype=BF16),
        ],
        [ids, basis, unit, left, hot, hidden[1]],
        flops=2_000_000_000,
        name="second_near",
    )
    (near,) = run(
        functools.partial(second_side_kernel, slots),
        [shape(features, edges)],
        [hot, near, hidden[0]],
        flops=1_000_000_000,
        name="second_side",
    )
    block_rows = -(-(lat_width + 9) // 16) * 16
    feature, sums_two, gate_two, packed, charge, hidden_two = run(
        functools.partial(second_kernel, slots),
        [
            shape(features, edges, dtype=BF16),
            shape(3, features, atoms),
            shape(features, atoms),
            shape(block_rows, atoms, dtype=BF16),
            shape(lat_width, atoms),
            shape(features, atoms),
        ],
        [hot_beyond, edge_weights, near, mix_high, mix_low, charge_pair, cells[1], hidden[1],
         hidden[2]],
        name="second",
    )
    energy, energy_slope = run(
        readout_kernel,
        [shape(1, atoms), shape(features, atoms)],
        [hidden_high, hidden_low, hidden_turn_high, hidden_turn_low, read_out, hidden_two],
        name="readout",
    )
    half = grid_x // 2
    near_charges = jnp.stack([packed] + [paired(packed, "gx", 2 * d) for d in range(1, half)])
    (weight,) = run(
        functools.partial(green_weights, share, padded, grid),
        [shape(16 * share + padded, 128)],
        [place, wavevectors],
        name="green",
    )
    near_charges, weight = lax.optimization_barrier((near_charges, weight))
    far_charges = paired(near_charges, "gx", 1)
    span = half * atoms
    rows = 32 * share + 2 * padded
    phase_shapes = [
        shape(padded, span),
        shape(padded, span),
        shape(8, span),
        shape(8, span),
        shape(rows, span, dtype=BF16),
        shape(rows, span, dtype=BF16),
    ]
    *near_phases, near_total = run(
        functools.partial(structure_kernel, share, padded, grid, lat_width, 0),
        phase_shapes + [shape(rows, lat_width)],
        [place, near_charges],
        flops=1_000_000_000,
        name="structure_near",
    )
    *far_phases, own_part, part = run(
        functools.partial(structure_kernel, share, padded, grid, lat_width, 1),
        phase_shapes
        + [
            shape(rows // 2, 2 * lat_width),
            shape(rows // 2, 2 * lat_width, dtype=BF16),
        ],
        [place, far_charges, near_total],
        name="structure_far",
    )
    parts = [own_part] + [paired(part, "gy", d) for d in range(1, grid_y)]
    (hot_back,) = run(
        hot_back_kernel,
        [shape(edges, 9 * atoms, dtype=BF16)],
        [ids],
        flops=2_000_000_000,
        name="hot_back",
    )
    parts, hot_back = lax.optimization_barrier((parts, hot_back))
    far_folds, wave_rows = run(
        functools.partial(fold_kernel, share, padded, grid, lat_width, 1),
        [shape(half, block_rows, atoms, dtype=BF16), shape(rows, lat_width)],
        [place, weight] + parts + far_phases + [far_charges],
        name="fold_far",
    )
    far_folds = paired(far_folds, "gx", 1)
    (near_folds,) = run(
        functools.partial(fold_kernel, share, padded, grid, lat_width, 0),
        [shape(half, block_rows, atoms)],
        [place, wave_rows] + near_phases + [near_charges],
        flops=1_000_000_000,
        name="fold_near",
    )
    folds = run(
        functools.partial(join_kernel, lat_width),
        [shape(block_rows, atoms)] + [shape(block_rows, atoms, dtype=BF16)] * (half - 1),
        [near_folds, far_folds],
        name="fold_join",
    )
    folds = [folds[0]] + [paired(folds[d], "gx", 2 * d) for d in range(1, half)]

    site, long, cotangent, grads, term, to_sides, to_beyond, to_pair = run(
        functools.partial(second_back_kernel, slots, scale, half),
        [
            shape(1, 1, atoms),
            shape(8, atoms),
            shape(features, atoms),
            shape(4, features, atoms),
            shape(features, edges, dtype=BF16),
            shape(2, features, atoms, dtype=BF16),
            shape(features, atoms, dtype=BF16),
            shape(3, features, atoms, dtype=BF16),
        ],
        [hot_back, edge_weights, turn_high, turn_low, charge_pair, sums_two, gate_two, charge,
         energy, energy_slope] + folds,
        name="second_back",
    )
    from_pair, from_sides = paired(to_pair, "gx", 1), beyond(to_sides, "gx")
    (middle,) = run(
        second_middle_kernel,
        [shape(3, features, atoms)],
        [hot_back, term, cotangent],
        flops=1_000_000_000,
        name="second_middle",
    )
    sides = [
        (middle[2 * b] + from_pair[2 * b].astype(F32) + from_sides[b].astype(F32)).astype(BF16)
        for b in range(2)
    ]
    sides, to_beyond = lax.optimization_barrier((sides, to_beyond))
    from_beyond = beyond(to_beyond, "gx")
    from_y = [paired(sides[0], "gy", 1), beyond(sides[1], "gy")]
    (edge,) = run(
        functools.partial(second_edge_kernel, slots),
        [shape(32, edges)],
        [back, feature, grads],
        flops=1_000_000_000,
        name="second_edge",
    )
    to_pair, middle, to_beyond = run(
        functools.partial(first_back_kernel, slots),
        [shape(3, 8, atoms)] * 3,
        [ids, basis, slope, unit, kind_high, kind_low, turn_high, turn_low, sums_one, gate_one, edge,
         long, middle, from_pair, from_beyond] + from_y,
        name="first_back",
    )
    total = middle + paired(to_pair, "gx", 1) + beyond(to_beyond, "gx")
    total = total[1] + paired(total[0], "gy", 1) + beyond(total[2], "gy")
    forces = -total[None, :3, None, :]
    return (forces.transpose(0, 2, 1, 3), site)


def solution(mesh):
    in_specs = (
        P("gx", "gy", None, None),
        P("gx", "gy", None),
        P("gx", "gy", None, None),
        P("gx", "gy", None),
        P(),
        P(),
        P(),
        P(),
        P(),
        P(),
        P(),
    )
    out_specs = (P("gx", "gy", None, None), P("gx", "gy", None))
    return jax.shard_map(
        per_device, mesh=mesh, in_specs=in_specs, out_specs=out_specs, check_vma=False
    )
```

```python
import functools
import math

import jax
import jax.numpy as jnp
import numpy as np
from jax import lax
from jax.experimental import pallas as pl
from jax.experimental.pallas import tpu as pltpu
from jax.sharding import PartitionSpec as P

cell_width = 10.0
box_height = 30.0
cut_radius = 50.0
soften = 0.25
screen = 0.5
smear_width = 0.5
WAVE_REACH = 8
F32 = jnp.float32
BF16 = jnp.bfloat16
CENTRE = 4


def paired(block, axis, mask):
    return lax.ppermute(block, axis, [(i ^ mask, i) for i in range(lax.axis_size(axis))])


def beyond(block, axis):
    count = lax.axis_size(axis)
    route = [((i + (1 if i % 2 else -1)) % count, i) for i in range(count)]
    return lax.ppermute(block, axis, route)


def around(block, beside):
    column = jnp.stack([paired(block, "gy", 1), block, beyond(block, "gy")])
    column, beside = lax.optimization_barrier((column, beside))
    return [paired(column, "gx", 1), column, beyond(column, "gx")], beside


def whole(space=pltpu.VMEM):
    return pl.BlockSpec(memory_space=space)


def run(kernel, outs, args, scratch=(), hbm=0, flops=10_000_000, grant=16, name=None):
    specs = [whole()] * (len(args) - hbm) + [whole(pltpu.HBM)] * hbm
    return list(
        pl.pallas_call(
            kernel,
            out_shape=outs,
            in_specs=specs,
            out_specs=[whole() for _ in outs],
            scratch_shapes=list(scratch),
            compiler_params=pltpu.CompilerParams(vmem_limit_bytes=grant * 1024 * 1024),
            cost_estimate=pl.CostEstimate(
                flops=flops, bytes_accessed=1_000_000, transcendentals=0
            ),
            name=name,
        )(*args)
    )


def shape(*dims, dtype=F32):
    return jax.ShapeDtypeStruct(dims, dtype)


def split(value):
    high = value.astype(BF16)
    return high, (value - high.astype(F32)).astype(BF16)


def dot(left, right, contract=((1,), (0,))):
    return lax.dot_general(left, right, (contract, ((), ())), preferred_element_type=F32)


def dot3(left, right):
    left_high, left_low = split(left)
    right_high, right_low = split(right)
    return dot(left_high, right_high) + (dot(left_high, right_low) + dot(left_low, right_high))


def dot_split(left, right):
    right_high, right_low = split(right)
    return dot(left[0], right_high) + (dot(left[0], right_low) + dot(left[1], right_high))


def sin_cos(turns):
    quarter = jnp.round(turns * 4.0)
    x = (turns - quarter * 0.25) * (2.0 * math.pi)
    z = x * x
    sine = ((-1.9515295891e-4 * z + 8.3321608736e-3) * z - 1.6666654611e-1) * (z * x) + x
    cosine = (2.443315711809948e-5 * z - 1.388731625493765e-3) * z + 4.166664568298827e-2
    cosine = cosine * (z * z) - 0.5 * z + 1.0
    k = quarter.astype(jnp.int32) & 3
    odd = (k & 1) == 1
    by_sine = jnp.where(odd, cosine, sine)
    by_cosine = jnp.where(odd, sine, cosine)
    return (
        jnp.where(k >= 2, -by_sine, by_sine),
        jnp.where((k == 1) | (k == 2), -by_cosine, by_cosine),
    )


def stacked_left(value):
    high = value.astype(BF16).astype(F32)
    rows = jnp.concatenate([high, high, value - high, jnp.zeros_like(high)], axis=0)
    return rows.T.astype(BF16)


def stacked_right(value):
    high = value.astype(BF16).astype(F32)
    return jnp.concatenate([high, value - high, high, jnp.zeros_like(high)], axis=0).astype(BF16)


def silu_pair(value):
    gate = 1.0 / (1.0 + jnp.exp(-value))
    return value * gate, gate * (1.0 + value * (1.0 - gate))


def onehot_kinds(kinds, rows):
    levels = lax.broadcasted_iota(jnp.int32, (rows, kinds.shape[1]), 0).astype(F32)
    return jnp.where(kinds == levels, 1.0, 0.0)


def embedding_stack(embed):
    high = embed.astype(BF16).astype(F32)
    rest = embed - high
    middle = rest.astype(BF16).astype(F32)
    rows = jnp.concatenate([high, middle, rest - middle, jnp.zeros_like(high)], axis=0)
    return rows.T.astype(BF16)


def embedded(stack, kinds):
    hot = onehot_kinds(kinds, 8)
    return dot(stack, jnp.concatenate([hot, hot, hot, jnp.zeros_like(hot)], axis=0).astype(BF16))


def weights_of(stack_ref, part, rows):
    return dot(stack_ref[1 if part else 0], stacked_right(rows))


def mixed(sums, high_ref, low_ref, layer):
    squares = sums[1] * sums[1] + sums[2] * sums[2] + sums[3] * sums[3]
    both = jnp.concatenate([sums[0], squares], axis=0)
    return silu_pair(dot_split((high_ref[layer], low_ref[layer]), both))


def edge_parts(basis, unit):
    return [basis] + [basis * unit[i : i + 1] for i in range(3)]


def pack_kernel(place_ref, position_ref, species_ref, out_ref):
    rows = [position_ref[0, i] for i in range(3)] + [species_ref[0].astype(F32)]
    atoms = rows[0].shape[1]
    out_ref[...] = jnp.concatenate(
        [row[:, s : s + 128] for row in rows for s in range(0, atoms, 128)], axis=0
    )


def radial_left(radial):
    high = radial.astype(BF16).astype(F32)
    low = radial - high
    top = jnp.concatenate([high, high], axis=1)
    end = jnp.concatenate([low, jnp.zeros_like(low)], axis=1)
    return jnp.concatenate([top, end], axis=0).astype(BF16)


def put_split(value, high_ref, low_ref, *at):
    high, low = split(value)
    high_ref[at] = high
    low_ref[at] = low


def slot_order(ids, place_ref, atoms):
    cell = ids >> (atoms.bit_length() - 1) if atoms & (atoms - 1) == 0 else ids // atoms
    a = (cell * 11) >> 5
    b = cell - 3 * a
    a = jnp.where((place_ref[0, 0:1, 0:1] & 1) == 0, 2 - a, a)
    b = jnp.where((place_ref[1, 0:1, 0:1] & 1) == 0, 2 - b, b)
    return ids + (3 * a + b - cell) * atoms


def fetch(sources, targets, sems):
    copies = [
        pltpu.make_async_copy(source, target, sems.at[i])
        for i, (source, target) in enumerate(zip(sources, targets))
    ]
    for copy in copies:
        copy.start()
    for copy in copies:
        copy.wait()


def prep_first_kernel(norm, place_ref, ids_in, count_in, embed_in, radial_in, mixing_in, id_ref, count_ref,
                      embed_out, kind_left, left_out, back_out, kind_high, kind_low, mix_high,
                      mix_low, turn_high, turn_low, embed_ref, radial_ref, mixing_ref, sems):
    fetch(
        [ids_in, count_in, embed_in, radial_in, mixing_in],
        [id_ref, count_ref, embed_ref, radial_ref, mixing_ref],
        sems,
    )
    id_ref[...] = slot_order(id_ref[...], place_ref, count_ref.shape[2])
    embed = embed_ref[...]
    kinds = embed.shape[0]
    for path in range(2):
        radial = radial_ref[0, path] * norm
        rows = jnp.concatenate([radial * embed[s : s + 1] for s in range(kinds)], axis=0)
        kind_left[path] = stacked_left(rows)
        put_split(rows, kind_high, kind_low, path)
        radial = radial_ref[1, path] * norm
        left_out[path] = stacked_left(radial)
        back_out[path] = radial_left(radial)
    for layer in range(2):
        scalar, vector = mixing_ref[layer, 0], mixing_ref[layer, 1]
        put_split(jnp.concatenate([scalar.T, vector.T], axis=1), mix_high, mix_low, layer)
        put_split(jnp.concatenate([scalar, 2.0 * vector], axis=0), turn_high, turn_low, layer)
    embed = jnp.concatenate([embed, jnp.zeros((8 - kinds, embed.shape[1]), F32)], axis=0)
    embed_out[...] = embedding_stack(embed)


def prep_second_kernel(read_in, hidden_in, charge_in, read_ref, hidden_high, hidden_low,
                       hidden_turn_high, hidden_turn_low, charge_pair, hidden_ref, charge_ref, sems):
    fetch([read_in, hidden_in, charge_in], [read_ref, hidden_ref, charge_ref], sems)
    put_split(hidden_ref[...].T, hidden_high, hidden_low, Ellipsis)
    put_split(hidden_ref[...], hidden_turn_high, hidden_turn_low, Ellipsis)
    charge = charge_ref[...]
    high = charge.astype(BF16).astype(F32)
    charge_pair[0] = high.astype(BF16)
    charge_pair[1] = (charge - high).astype(BF16)


def hot_kernel(ids_ref, hot_ref):
    edges = ids_ref.shape[1]
    for start in range(0, edges, 256):
        lanes = slice(start, start + 256)
        hot_ref[:, lanes] = hot_columns(ids_ref[:, lanes], hot_ref.shape[0])


def hot_back_kernel(ids_ref, hot_ref):
    edges = ids_ref.shape[1]
    entry = lax.broadcasted_iota(jnp.int32, (128, hot_ref.shape[1]), 1).astype(F32)
    for start in range(0, edges, 128):
        row = jnp.broadcast_to(ids_ref[:, start : start + 128].astype(F32), (8, 128))
        column = row.T[:, 0:1]
        hot_ref[start : start + 128] = jnp.where(column == entry, 1.0, 0.0).astype(BF16)


def unfold_block(block, atoms):
    parts = atoms // 128
    rows = [block[r : r + 1] for r in range(4 * parts)]
    return [jnp.concatenate(rows[q * parts : (q + 1) * parts], axis=1) for q in range(4)]


def first_kernel(slots, place_ref, ids_ref, count_ref, embed_ref, kind_left, mix_high, mix_low,
                 pair_ref, column_ref, beyond_ref, low_ref, basis_ref, slope_ref, unit_ref, sums_ref,
                 gate_ref):
    atoms = low_ref.shape[1]
    ids = ids_ref[...]
    frame = [pair_ref, column_ref, beyond_ref]
    own = unfold_block(column_ref[1], atoms)
    per_cell = atoms // 128
    places = lax.broadcasted_iota(jnp.int32, (4 * per_cell, 128), 0)
    upper = places % per_cell
    kind_of_row = places // per_cell
    rows = []
    to_x = jnp.where(kind_of_row == 0, cell_width, 0.0)
    to_x = jnp.where((place_ref[0] & 1) == 0, to_x, -to_x)
    to_y = jnp.where(kind_of_row == 1, cell_width, 0.0)
    to_y = jnp.where((place_ref[1] & 1) == 0, to_y, -to_y)
    for a in range(3):
        for b in range(3):
            rows.append(frame[a][b] + ((1 - a) * to_x + (1 - b) * to_y))
    pieces = []
    for start in range(0, ids.shape[1], 128):
        part = jnp.broadcast_to(ids[:, start : start + 128], places.shape)
        lane, half = part & 127, (part >> 7) - upper
        found = jnp.zeros(places.shape, F32)
        for cell, block in enumerate(rows):
            value = jnp.take_along_axis(block, lane, axis=1)
            found = jnp.where(half == per_cell * cell, value, found)
        total = found
        for s in range(1, per_cell):
            total = total + pltpu.roll(found, 4 * per_cell - s, 0)
        pieces.append(total)
    found = jnp.concatenate(pieces, axis=1)
    found = [found[q * per_cell : q * per_cell + 1] for q in range(4)]
    rel = [found[q] - jnp.concatenate([own[q]] * slots, axis=1) for q in range(3)]
    distance = jnp.sqrt(rel[0] * rel[0] + rel[1] * rel[1] + rel[2] * rel[2] + soften)
    inverse = 1.0 / distance
    order = (lax.broadcasted_iota(jnp.int32, (8, 1), 0) + 1).astype(F32)
    sine, cosine = sin_cos((order * (0.5 / cut_radius)) * distance)
    wave = sine / ((order * (math.pi / cut_radius)) * distance)
    count = count_ref[0]
    live = jnp.concatenate([jnp.where(count > n, 1.0, 0.0) for n in range(slots)], axis=1)
    basis = wave * live
    basis_ref[...] = basis
    slope_ref[...] = (cosine - wave) * (inverse * live)
    kinds = found[3]
    unit = jnp.concatenate(
        [r * inverse for r in rel] + [inverse, kinds] + [jnp.zeros_like(kinds)] * 3, axis=0
    )
    unit_ref[...] = unit
    stack = embed_ref[...]
    parts = edge_parts(basis, unit)
    species = kind_left.shape[2] // 32
    by_kind = [[None] * species for _ in range(4)]
    for n in range(slots):
        lanes = slice(n * atoms, (n + 1) * atoms)
        kind = jnp.broadcast_to(kinds[:, lanes], (8, atoms))
        for k in range(species):
            match = kind == float(k)
            for part in range(4):
                term = jnp.where(match, parts[part][:, lanes], 0.0)
                old = by_kind[part][k]
                by_kind[part][k] = term if old is None else old + term
    stacks = [stacked_right(jnp.concatenate(rows, axis=0)) for rows in by_kind]
    vectors = dot(kind_left[1], jnp.concatenate(stacks[1:], axis=1))
    sums = [dot(kind_left[0], stacks[0])]
    sums += [vectors[:, i * atoms : (i + 1) * atoms] for i in range(3)]
    step, gate = mixed(sums, mix_high, mix_low, 0)
    low_ref[...] = (embedded(stack, own[3]) + step).astype(BF16)
    for part in range(3):
        sums_ref[part] = sums[part + 1]
    gate_ref[...] = gate


def hot_columns(ids, rows):
    place = lax.broadcasted_iota(jnp.int32, (rows, ids.shape[1]), 0)
    return jnp.where(ids == place, 1.0, 0.0).astype(BF16)


def second_near_kernel(slots, ids_ref, basis_ref, unit_ref, left_ref, hot_ref, column_ref,
                       weight_ref, near_ref, beyond_ref):
    atoms = column_ref.shape[2]
    parts = edge_parts(basis_ref[...], unit_ref[...])
    source = jnp.concatenate([column_ref[b] for b in range(3)], axis=1)
    for n in range(slots):
        lanes = slice(n * atoms, (n + 1) * atoms)
        for part in range(4):
            weight_ref[part, :, lanes] = weights_of(left_ref, part, parts[part][:, lanes])
        near_ref[:, lanes] = dot(source, hot_ref[3 * atoms : 6 * atoms, lanes])
        beyond_ref[:, lanes] = hot_columns(ids_ref[:, lanes] - 6 * atoms, 3 * atoms)


def second_side_kernel(slots, hot_ref, near_ref, pair_ref, out_ref):
    atoms = pair_ref.shape[2]
    source = jnp.concatenate([pair_ref[b] for b in range(3)], axis=1)
    for n in range(slots):
        lanes = slice(n * atoms, (n + 1) * atoms)
        out_ref[:, lanes] = near_ref[:, lanes] + dot(source, hot_ref[: 3 * atoms, lanes])


def second_kernel(slots, hot_ref, weight_ref, near_ref, mix_high, mix_low, charge_ref, cell_ref,
                  column_ref, beyond_ref, corner_pair, corner_beyond, feature_ref, sums_ref, gate_ref,
                  packed_ref, full_charge_ref, hidden_ref):
    atoms = column_ref.shape[2]
    source = jnp.concatenate([corner_pair[...], beyond_ref[...], corner_beyond[...]], axis=1)
    sums = [None] * 4
    for n in range(slots):
        lanes = slice(n * atoms, (n + 1) * atoms)
        feature = near_ref[:, lanes] + dot(source, hot_ref[:, lanes])
        feature_ref[:, lanes] = feature.astype(BF16)
        for part in range(4):
            term = weight_ref[part, :, lanes] * feature
            sums[part] = term if sums[part] is None else sums[part] + term
    step, gate = mixed(sums, mix_high, mix_low, 1)
    hidden = column_ref[1].astype(F32) + step
    hidden_ref[...] = hidden
    for part in range(3):
        sums_ref[part] = sums[part + 1]
    gate_ref[...] = gate
    charge = dot_split((charge_ref[0], charge_ref[1]), hidden)
    full_charge_ref[...] = charge
    place = jnp.concatenate(unfold_block(cell_ref[1], atoms)[:3], axis=0)
    high = place.astype(BF16).astype(F32)
    rest = place - high
    middle = rest.astype(BF16).astype(F32)
    zero = jnp.zeros((packed_ref.shape[0] - charge.shape[0] - 9, atoms), F32)
    packed_ref[...] = jnp.concatenate([charge, high, middle, rest - middle, zero], axis=0).astype(
        BF16
    )


def readout_kernel(hidden_high, hidden_low, turn_high, turn_low, out_ref, hidden_ref, energy_ref,
                   slope_ref):
    hidden = hidden_ref[...]
    value, slope = silu_pair(dot_split((hidden_high[...], hidden_low[...]), hidden))
    out = out_ref[...].T
    energy_ref[...] = jnp.sum(value * out, axis=0, keepdims=True)
    slope_ref[...] = dot_split((turn_high[...], turn_low[...]), slope * out)


def message_grads(cotangent, gate_ref, sums_ref, high_ref, low_ref, layer):
    pre = cotangent * gate_ref[...]
    both = dot_split((high_ref[layer], low_ref[layer]), pre)
    half = both.shape[0] // 2
    return [both[:half]] + [both[half:] * sums_ref[i] for i in range(3)]


def radial_grad(left, value):
    high, low = split(value)
    both = dot(left, jnp.concatenate([high, low], axis=0))
    half = both.shape[0] // 2
    return both[:half] + both[half:]


def second_back_kernel(slots, scale, count, hot_ref, weight_ref, turn_high, turn_low, charge_ref,
                       sums_ref, gate_ref, full_charge_ref, energy_ref, slope_ref, *refs):
    folds, refs = refs[:count], refs[count:]
    site_ref, long_ref, cotangent_ref, grad_ref, term_ref, pair_ref, *beyond_refs = refs
    atoms = gate_ref.shape[1]
    total = folds[0][...].astype(F32)
    for part in folds[1:]:
        total = total + part[...].astype(F32)
    wide = full_charge_ref.shape[0]
    potential = total[:wide] * (2.0 * scale)
    slopes = total[wide : wide + 3] + total[wide + 3 : wide + 6] + total[wide + 6 : wide + 9]
    long_ref[...] = jnp.concatenate(
        [slopes * (2.0 * scale), jnp.zeros((5, atoms), F32)], axis=0
    )
    site_ref[0] = energy_ref[...] + 0.5 * jnp.sum(
        full_charge_ref[...] * potential, axis=0, keepdims=True
    )
    high, low = split(potential)
    turned = ((0,), (0,))
    cotangent = slope_ref[...] + (
        dot(charge_ref[0], high, turned)
        + (dot(charge_ref[0], low, turned) + dot(charge_ref[1], high, turned))
    )
    cotangent_ref[...] = cotangent
    grads = message_grads(cotangent, gate_ref, sums_ref, turn_high, turn_low, 1)
    for part in range(4):
        grad_ref[part] = grads[part]
    for n in range(slots):
        lanes = slice(n * atoms, (n + 1) * atoms)
        term = weight_ref[0, :, lanes] * grads[0]
        for part in range(1, 4):
            term = term + weight_ref[part, :, lanes] * grads[part]
        term_ref[:, lanes] = term.astype(BF16)
    for b in range(3):
        start = (6 + b) * atoms
        beyond_refs[b][...] = dot(term_ref[...], hot_ref[:, start : start + atoms]).astype(BF16)
    for b in range(3):
        pair_ref[b] = dot(term_ref[...], hot_ref[:, b * atoms : (b + 1) * atoms]).astype(BF16)


def second_middle_kernel(hot_ref, term_ref, cotangent_ref, middle_ref):
    atoms = cotangent_ref.shape[1]
    for b in range(3):
        grad = dot(term_ref[...], hot_ref[:, (3 + b) * atoms : (4 + b) * atoms])
        middle_ref[b] = grad + cotangent_ref[...] if b == 1 else grad


def second_edge_kernel(slots, back_ref, feature_ref, grad_ref, edge_ref):
    atoms = grad_ref.shape[2]
    for n in range(slots):
        lanes = slice(n * atoms, (n + 1) * atoms)
        feature = feature_ref[:, lanes].astype(F32)
        for part in range(4):
            edge_ref[8 * part : 8 * part + 8, lanes] = radial_grad(
                back_ref[1 if part else 0], grad_ref[part] * feature
            )


def first_back_kernel(slots, ids_ref, basis_ref, slope_ref, unit_ref, kind_high, kind_low,
                      turn_high, turn_low, sums_ref, gate_ref, edge_ref, long_ref, middle_ref,
                      *refs):
    from_x, from_y, outs = refs[:2], refs[2:4], refs[4:]
    atoms = gate_ref.shape[1]
    cotangent = middle_ref[1]
    for block in (from_x[0][1], from_x[1][...], from_y[0][...], from_y[1][...]):
        cotangent = cotangent + block.astype(F32)
    grads = message_grads(cotangent, gate_ref, sums_ref, turn_high, turn_low, 0)
    unit = unit_ref[...]
    kinds = unit[4:5]
    by_kind = [dot_split((kind_high[0], kind_low[0]), grads[0])]
    by_kind += [dot_split((kind_high[1], kind_low[1]), grads[i]) for i in range(1, 4)]
    species = by_kind[0].shape[0] // 8
    edges = [[] for _ in range(4)]
    for n in range(slots):
        kind = jnp.broadcast_to(kinds[:, n * atoms : (n + 1) * atoms], (8, atoms))
        matches = [kind == float(k) for k in range(1, species)]
        for part in range(4):
            rows = by_kind[part]
            found = rows[:8]
            for k, match in enumerate(matches):
                found = jnp.where(match, rows[8 * k + 8 : 8 * k + 16], found)
            edges[part].append(found)
    edges = [
        edge_ref[8 * part : 8 * part + 8] + jnp.concatenate(edges[part], axis=1) for part in range(4)
    ]
    basis = basis_ref[...]
    units = [unit[i : i + 1] for i in range(3)]
    inverse = unit[3:4]
    by_basis = edges[0]
    for i in range(3):
        by_basis = by_basis + edges[i + 1] * units[i]
    by_unit = [jnp.sum(edges[i + 1] * basis, axis=0, keepdims=True) * inverse for i in range(3)]
    by_distance = jnp.sum(by_basis * slope_ref[...], axis=0, keepdims=True)
    for i in range(3):
        by_distance = by_distance - by_unit[i] * units[i]
    moves = [by_unit[i] + by_distance * units[i] for i in range(3)]
    zero = jnp.zeros_like(moves[0])
    move = jnp.concatenate(moves + [zero] * 5, axis=0)
    own = long_ref[...]
    for n in range(slots):
        own = own - move[:, n * atoms : (n + 1) * atoms]
    ids = ids_ref[...]
    lane_hot = hot_columns(ids & 127, 128)
    half = ids >> 7
    high = move.astype(BF16).astype(F32)
    both = jnp.concatenate([high, move - high], axis=0)
    per_cell = atoms // 128
    rows = jnp.concatenate(
        [jnp.where(half == h, both, 0.0).astype(BF16) for h in range(9 * per_cell)], axis=0
    )
    spread = dot(rows, lane_hot, ((1,), (1,)))
    for cell in range(9):
        found = []
        for h in range(cell * per_cell, (cell + 1) * per_cell):
            found.append(spread[16 * h : 16 * h + 8] + spread[16 * h + 8 : 16 * h + 16])
        grad = jnp.concatenate(found, axis=1)
        if cell == CENTRE:
            grad = own + grad
        outs[cell // 3][cell % 3] = grad


def pair_counts(parts):
    total = WAVE_REACH + WAVE_REACH * (2 * WAVE_REACH + 1)
    share = -(-total // parts)
    return total, share, -(-share // 16) * 16


def pair_vectors(slot, share, part):
    side = 2 * WAVE_REACH + 1
    total = WAVE_REACH + WAVE_REACH * side
    index = slot + part.astype(F32) * share
    later = index - WAVE_REACH
    row = jnp.floor((later + 0.5) * (1.0 / side))
    first = index < WAVE_REACH
    kx = jnp.where(first, 0.0, row + 1.0)
    ky = jnp.where(first, index + 1.0, later - row * side - WAVE_REACH)
    valid = jnp.where((slot < share) & (index < total), 1.0, 0.0)
    return kx, ky, valid


def count_up(rows):
    return lax.broadcasted_iota(jnp.int32, (rows, 1), 0).astype(F32)


def green_weights(share, padded, grid, place_ref, vec_ref, weight_ref):
    grid_x, grid_y = grid
    turn = 2.0 * math.pi
    side = 2 * WAVE_REACH + 1
    top = side * side * side - 1
    vec = vec_ref[...].astype(F32) + WAVE_REACH
    code = (vec[0:1] * side + vec[1:2]) * side + vec[2:3]
    code = jnp.maximum(code, top - code)
    span = 8 * share
    row = count_up(span)
    slot = jnp.floor(row * 0.125)
    height = row - 8.0 * slot + 1.0
    flat = count_up(padded)
    slot = jnp.concatenate([slot, slot, flat], axis=0)
    kz = jnp.concatenate([height, -height, jnp.zeros_like(flat)], axis=0)
    kx, ky, valid = pair_vectors(slot, share, place_ref[0, 0:1, 0:1])
    own = ((kx + WAVE_REACH) * side + ky + WAVE_REACH) * side + kz + WAVE_REACH
    seen = jnp.zeros((own.shape[0], 128), F32)
    for start in range(0, code.shape[1], 128):
        seen = seen + jnp.where(own == code[:, start : start + 128], 1.0, 0.0)
    count = jnp.sum(seen, axis=1, keepdims=True) * valid
    sq = (
        (kx * (turn / (grid_x * cell_width))) ** 2
        + (ky * (turn / (grid_y * cell_width))) ** 2
        + (kz * (turn / box_height)) ** 2
    )
    green = jnp.exp(-smear_width * sq) / (sq + screen * screen) * count
    weight_ref[...] = jnp.broadcast_to(green, weight_ref.shape)


def basis_rows(share, ca, sa, cb, sb):
    cc, ss, sc, cs = [], [], [], []
    for p in range(share):
        c, s = ca[p : p + 1], sa[p : p + 1]
        cc.append(c * cb)
        ss.append(s * sb)
        sc.append(s * cb)
        cs.append(c * sb)
    return cc, ss, sc, cs


def unpack_rows(block):
    half = block.shape[1] // 2
    return jnp.concatenate([block[:, :half], block[:, half:]], axis=0)


def pack_rows(block):
    half = block.shape[0] // 2
    return jnp.concatenate([block[:half], block[half:]], axis=1)


def structure_kernel(share, padded, grid, wide, flip, place_ref, blocks, *refs):
    grid_x, grid_y = grid
    if flip:
        near_ref, (ca_ref, sa_ref, cb_ref, sb_ref, high_ref, low_ref, own_ref, out_ref) = (
            refs[0],
            refs[1:],
        )
        total = near_ref[...]
    else:
        ca_ref, sa_ref, cb_ref, sb_ref, high_ref, low_ref, total_ref = refs
        total = None
    col = place_ref[1, 0:1, 0:1].astype(F32) * (1.0 / grid_y)
    first = place_ref[0, 0:1, 0:1] ^ flip
    kx, ky, _ = pair_vectors(count_up(padded), share, place_ref[0, 0:1, 0:1])
    kz = count_up(8) + 1.0
    for d in range(grid_x // 2):
        block = blocks[d]
        charge = block[:wide]
        atoms = charge.shape[1]
        pieces = block[wide:].astype(F32)
        place = pieces[0:3] + (pieces[3:6] + pieces[6:9])
        row = (first ^ (2 * d)).astype(F32) * (1.0 / grid_x)
        x = place[0:1] * (1.0 / (grid_x * cell_width)) + row
        y = place[1:2] * (1.0 / (grid_y * cell_width)) + col
        sa, ca = sin_cos(kx * x + ky * y)
        sb, cb = sin_cos(kz * (place[2:3] * (1.0 / box_height)))
        lanes = pl.ds(d * atoms, atoms)
        ca_ref[:, lanes] = ca
        sa_ref[:, lanes] = sa
        cb_ref[:, lanes] = cb
        sb_ref[:, lanes] = sb
        cc, ss, sc, cs = basis_rows(share, ca, sa, cb, sb)
        high, low = split(jnp.concatenate(cc + ss + sc + cs + [ca, sa], axis=0))
        high_ref[:, lanes] = high
        low_ref[:, lanes] = low
        term = dot(high, charge, ((1,), (1,))) + dot(low, charge, ((1,), (1,)))
        total = term if total is None else total + term
    if flip:
        packed = pack_rows(total)
        own_ref[...] = packed
        out_ref[...] = packed.astype(BF16)
    else:
        total_ref[...] = total


def weighted_rows(share, padded, wide, weight_ref, parts):
    packed = parts[0][...].astype(F32)
    for part in parts[1:]:
        packed = packed + part[...].astype(F32)
    struct = unpack_rows(packed)
    span = 8 * share
    cc, ss, sc, cs = (struct[i * span : (i + 1) * span] for i in range(4))
    weight = weight_ref[:, :wide]
    plus, minus, flat = weight[:span], weight[span : 2 * span], weight[2 * span :]
    re_plus, im_plus = plus * (cc - ss), plus * (sc + cs)
    re_minus, im_minus = minus * (cc + ss), minus * (sc - cs)
    rows = jnp.concatenate(
        [
            re_plus + re_minus,
            re_minus - re_plus,
            im_plus + im_minus,
            im_plus - im_minus,
            flat * struct[4 * span : 4 * span + padded],
            flat * struct[4 * span + padded :],
        ],
        axis=0,
    )
    return rows


def fold_kernel(share, padded, grid, wide, flip, place_ref, *refs):
    grid_x, grid_y = grid
    turn = 2.0 * math.pi
    if flip:
        weight_ref, parts, refs = refs[0], refs[1 : 1 + grid_y], refs[1 + grid_y :]
        rows = weighted_rows(share, padded, wide, weight_ref, parts)
        refs, rows_ref = refs[:-1], refs[-1]
        rows_ref[...] = rows
    else:
        rows, refs = refs[0][...], refs[1:]
    ca_ref, sa_ref, cb_ref, sb_ref, high_ref, low_ref, blocks, out_ref = refs
    row_high, row_low = split(rows)
    row_pair = jnp.concatenate([row_high, row_low], axis=1)
    turned = rows.T
    t_high, t_low = split(turned)
    t_both = jnp.concatenate([t_high, t_low], axis=0)
    span = 8 * share
    kx, ky, _ = pair_vectors(count_up(padded), share, place_ref[0, 0:1, 0:1])
    kx = kx * (turn / (grid_x * cell_width))
    ky = ky * (turn / (grid_y * cell_width))
    kz = (count_up(8) + 1.0) * (turn / box_height)
    for d in range(grid_x // 2):
        charge = blocks[d][:wide]
        atoms = charge.shape[1]
        lanes = pl.ds(d * atoms, atoms)
        ca, sa, cb, sb = ca_ref[:, lanes], sa_ref[:, lanes], cb_ref[:, lanes], sb_ref[:, lanes]
        bcc, bss, bsc, bcs = basis_rows(share, ca, sa, cb, sb)
        high, low = high_ref[:, lanes], low_ref[:, lanes]
        both = dot(t_both, high)
        pot = both[:wide] + both[wide:] + dot(t_high, low)
        proj = dot(row_pair, jnp.concatenate([charge, charge], axis=0))
        by_x = jnp.zeros((8, atoms), jnp.float32)
        by_y = jnp.zeros((8, atoms), jnp.float32)
        by_z = jnp.zeros((8, atoms), jnp.float32)
        for p in range(share):
            pcc, pss, psc, pcs = (
                proj[i * span + 8 * p : i * span + 8 * p + 8] for i in range(4)
            )
            slope = bcs[p] * pss - bsc[p] * pcc + bcc[p] * psc - bss[p] * pcs
            by_x = by_x + kx[p : p + 1] * slope
            by_y = by_y + ky[p : p + 1] * slope
            by_z = by_z + (bsc[p] * pss - bcs[p] * pcc - bss[p] * psc + bcc[p] * pcs)
        flat_slope = ca * proj[4 * span + padded :] - sa * proj[4 * span : 4 * span + padded]
        grad_x = jnp.sum(by_x, axis=0, keepdims=True) + jnp.sum(kx * flat_slope, axis=0, keepdims=True)
        grad_y = jnp.sum(by_y, axis=0, keepdims=True) + jnp.sum(ky * flat_slope, axis=0, keepdims=True)
        grad_z = jnp.sum(kz * by_z, axis=0, keepdims=True)
        slopes = jnp.concatenate([grad_x, grad_y, grad_z], axis=0)
        out_ref[d] = pieced(pot, slopes, out_ref.shape[1]).astype(out_ref.dtype)


def pieced(pot, slopes, rows):
    high = slopes.astype(BF16).astype(F32)
    rest = slopes - high
    middle = rest.astype(BF16).astype(F32)
    zero = jnp.zeros((rows - pot.shape[0] - 9, pot.shape[1]), F32)
    return jnp.concatenate([pot, high, middle, rest - middle, zero], axis=0)


def unpieced(block, wide):
    slopes = block[wide : wide + 3] + (block[wide + 3 : wide + 6] + block[wide + 6 : wide + 9])
    return block[:wide], slopes


def join_kernel(wide, near_ref, far_ref, own_ref, *outs):
    for d in range(near_ref.shape[0]):
        pot, slopes = unpieced(near_ref[d], wide)
        pot_far, slopes_far = unpieced(far_ref[d].astype(F32), wide)
        block = pieced(pot + pot_far, slopes + slopes_far, near_ref.shape[1])
        if d:
            outs[d - 1][...] = block.astype(BF16)
        else:
            own_ref[...] = block


def per_device(
    positions,
    species,
    neighbours,
    counts,
    species_embed,
    radial,
    mixing,
    read_hidden,
    read_out,
    charge_map,
    wavevectors,
):
    atoms = positions.shape[3]
    slots = neighbours.shape[3]
    features, lat_width = charge_map.shape
    wave_count = wavevectors.shape[1]
    grid = lax.axis_size("gx"), lax.axis_size("gy")
    grid_x, grid_y = grid
    edges = slots * atoms
    scale = 1.0 / math.sqrt(wave_count * lat_width * atoms * grid_x * grid_y)
    place = jnp.stack([lax.axis_index("gx"), lax.axis_index("gy")]).astype(jnp.int32)
    place = jnp.broadcast_to(place[:, None, None], (2, 8, 128))
    _, share, padded = pair_counts(grid_x)
    ids = neighbours.transpose(0, 3, 1, 2).reshape(1, edges)
    dma = pltpu.SemaphoreType.DMA
    (own,) = run(
        pack_kernel,
        [shape(4 * atoms // 128, 128)],
        [place, positions.transpose(0, 2, 1, 3), species],
        flops=10_000_000_000,
        name="pack",
    )
    norm = 1.0 / math.sqrt(slots)
    kind_rows = 8 * species_embed.shape[0]
    low_pair = lambda *dims: [shape(*dims, dtype=BF16)] * 2
    (ids, counts, embed, kind_left, left, back, kind_high, kind_low, mix_high, mix_low, turn_high,
     turn_low) = run(
        functools.partial(prep_first_kernel, norm),
        [
            shape(1, edges, dtype=jnp.int32),
            shape(*counts.shape, dtype=jnp.int32),
            shape(features, 32, dtype=BF16),
            shape(2, features, 4 * kind_rows, dtype=BF16),
            shape(2, features, 32, dtype=BF16),
            shape(2, 16, 2 * features, dtype=BF16),
        ]
        + low_pair(2, kind_rows, features)
        + low_pair(2, features, 2 * features)
        + low_pair(2, 2 * features, features),
        [place, ids, counts, species_embed, radial, mixing],
        scratch=[
            pltpu.VMEM(species_embed.shape, F32),
            pltpu.VMEM(radial.shape, F32),
            pltpu.VMEM(mixing.shape, F32),
            dma((5,)),
        ],
        hbm=5,
        name="prep_first",
    )
    cells, ids = around(own, ids)
    (hot,) = run(
        hot_kernel,
        [shape(6 * atoms, edges, dtype=BF16)],
        [ids],
        flops=1_000_000,
        name="hot",
    )
    read_out, hidden_high, hidden_low, hidden_turn_high, hidden_turn_low, charge_pair = run(
        prep_second_kernel,
        [shape(1, features)]
        + low_pair(features, features)
        + low_pair(features, features)
        + [shape(2, lat_width, features, dtype=BF16)],
        [read_out[None, :], read_hidden, charge_map.T],
        scratch=[
            pltpu.VMEM(read_hidden.shape, F32),
            pltpu.VMEM((lat_width, features), F32),
            dma((3,)),
        ],
        hbm=3,
        name="prep_second",
    )
    low, basis, slope, unit, sums_one, gate_one = run(
        functools.partial(first_kernel, slots),
        [
            shape(features, atoms, dtype=BF16),
            shape(8, edges),
            shape(8, edges),
            shape(8, edges),
            shape(3, features, atoms),
            shape(features, atoms),
        ],
        [place, ids, counts, embed, kind_left, mix_high, mix_low] + cells,
        name="first",
    )
    y_pair, y_beyond = paired(low, "gy", 1), beyond(low, "gy")
    x_beyond = beyond(low, "gx")
    column = jnp.stack([y_pair, low, y_beyond])
    column, x_beyond, hot = lax.optimization_barrier((column, x_beyond, hot))
    hidden_pair = paired(column, "gx", 1)
    corners = [paired(x_beyond, "gy", 1), beyond(x_beyond, "gy")]
    edge_weights, near, hot_beyond = run(
        functools.partial(second_near_kernel, slots),
        [
            shape(4, features, edges),
            shape(features, edges),
            shape(3 * atoms, edges, dtype=BF16),
        ],
        [ids, basis, unit, left, hot, column],
        flops=2_000_000_000,
        name="second_near",
    )
    (near,) = run(
        functools.partial(second_side_kernel, slots),
        [shape(features, edges)],
        [hot, near, hidden_pair],
        flops=1_000_000_000,
        name="second_side",
    )
    block_rows = -(-(lat_width + 9) // 16) * 16
    feature, sums_two, gate_two, packed, charge, hidden_two = run(
        functools.partial(second_kernel, slots),
        [
            shape(features, edges, dtype=BF16),
            shape(3, features, atoms),
            shape(features, atoms),
            shape(block_rows, atoms, dtype=BF16),
            shape(lat_width, atoms),
            shape(features, atoms),
        ],
        [hot_beyond, edge_weights, near, mix_high, mix_low, charge_pair, cells[1], column, x_beyond]
        + corners,
        name="second",
    )
    energy, energy_slope = run(
        readout_kernel,
        [shape(1, atoms), shape(features, atoms)],
        [hidden_high, hidden_low, hidden_turn_high, hidden_turn_low, read_out, hidden_two],
        name="readout",
    )
    half = grid_x // 2
    near_charges = jnp.stack([packed] + [paired(packed, "gx", 2 * d) for d in range(1, half)])
    (weight,) = run(
        functools.partial(green_weights, share, padded, grid),
        [shape(16 * share + padded, 128)],
        [place, wavevectors],
        name="green",
    )
    near_charges, weight = lax.optimization_barrier((near_charges, weight))
    far_charges = paired(near_charges, "gx", 1)
    span = half * atoms
    rows = 32 * share + 2 * padded
    phase_shapes = [
        shape(padded, span),
        shape(padded, span),
        shape(8, span),
        shape(8, span),
        shape(rows, span, dtype=BF16),
        shape(rows, span, dtype=BF16),
    ]
    *near_phases, near_total = run(
        functools.partial(structure_kernel, share, padded, grid, lat_width, 0),
        phase_shapes + [shape(rows, lat_width)],
        [place, near_charges],
        flops=1_000_000_000,
        name="structure_near",
    )
    *far_phases, own_part, part = run(
        functools.partial(structure_kernel, share, padded, grid, lat_width, 1),
        phase_shapes
        + [
            shape(rows // 2, 2 * lat_width),
            shape(rows // 2, 2 * lat_width, dtype=BF16),
        ],
        [place, far_charges, near_total],
        name="structure_far",
    )
    parts = [own_part] + [paired(part, "gy", d) for d in range(1, grid_y)]
    (hot_back,) = run(
        hot_back_kernel,
        [shape(edges, 9 * atoms, dtype=BF16)],
        [ids],
        flops=2_000_000_000,
        name="hot_back",
    )
    parts, hot_back = lax.optimization_barrier((parts, hot_back))
    far_folds, wave_rows = run(
        functools.partial(fold_kernel, share, padded, grid, lat_width, 1),
        [shape(half, block_rows, atoms, dtype=BF16), shape(rows, lat_width)],
        [place, weight] + parts + far_phases + [far_charges],
        name="fold_far",
    )
    far_folds = paired(far_folds, "gx", 1)
    (near_folds,) = run(
        functools.partial(fold_kernel, share, padded, grid, lat_width, 0),
        [shape(half, block_rows, atoms)],
        [place, wave_rows] + near_phases + [near_charges],
        flops=1_000_000_000,
        name="fold_near",
    )
    folds = run(
        functools.partial(join_kernel, lat_width),
        [shape(block_rows, atoms)] + [shape(block_rows, atoms, dtype=BF16)] * (half - 1),
        [near_folds, far_folds],
        name="fold_join",
    )
    folds = [folds[0]] + [paired(folds[d], "gx", 2 * d) for d in range(1, half)]

    site, long, cotangent, grads, term, to_pair, *to_beyond = run(
        functools.partial(second_back_kernel, slots, scale, half),
        [
            shape(1, 1, atoms),
            shape(8, atoms),
            shape(features, atoms),
            shape(4, features, atoms),
            shape(features, edges, dtype=BF16),
            shape(3, features, atoms, dtype=BF16),
        ]
        + [shape(features, atoms, dtype=BF16)] * 3,
        [hot_back, edge_weights, turn_high, turn_low, charge_pair, sums_two, gate_two, charge,
         energy, energy_slope] + folds,
        name="second_back",
    )
    corners = [paired(to_beyond[0], "gy", 1), beyond(to_beyond[2], "gy")]
    from_pair = paired(to_pair, "gx", 1)
    (middle,) = run(
        second_middle_kernel,
        [shape(3, features, atoms)],
        [hot_back, term, cotangent],
        flops=1_000_000_000,
        name="second_middle",
    )
    sides = [(middle[b] + from_pair[b].astype(F32)).astype(BF16) for b in (0, 2)]
    to_beyond = (to_beyond[1].astype(F32) + corners[0].astype(F32) + corners[1].astype(F32)).astype(
        BF16
    )
    from_beyond = beyond(to_beyond, "gx")
    from_y = [paired(sides[0], "gy", 1), beyond(sides[1], "gy")]
    (edge,) = run(
        functools.partial(second_edge_kernel, slots),
        [shape(32, edges)],
        [back, feature, grads],
        flops=1_000_000_000,
        name="second_edge",
    )
    to_pair, middle, to_beyond = run(
        functools.partial(first_back_kernel, slots),
        [shape(3, 8, atoms)] * 3,
        [ids, basis, slope, unit, kind_high, kind_low, turn_high, turn_low, sums_one, gate_one, edge,
         long, middle, from_pair, from_beyond] + from_y,
        name="first_back",
    )
    total = middle + paired(to_pair, "gx", 1) + beyond(to_beyond, "gx")
    total = total[1] + paired(total[0], "gy", 1) + beyond(total[2], "gy")
    forces = -total[None, :3, None, :]
    return (forces.transpose(0, 2, 1, 3), site)


def solution(mesh):
    in_specs = (
        P("gx", "gy", None, None),
        P("gx", "gy", None),
        P("gx", "gy", None, None),
        P("gx", "gy", None),
        P(),
        P(),
        P(),
        P(),
        P(),
        P(),
        P(),
    )
    out_specs = (P("gx", "gy", None, None), P("gx", "gy", None))
    return jax.shard_map(
        per_device, mesh=mesh, in_specs=in_specs, out_specs=out_specs, check_vma=False
    )
```

```python
import functools
import math

import jax
import jax.numpy as jnp
import numpy as np
from jax import lax
from jax.experimental import pallas as pl
from jax.experimental.pallas import tpu as pltpu
from jax.sharding import PartitionSpec as P

cell_width = 10.0
box_height = 30.0
cut_radius = 50.0
soften = 0.25
screen = 0.5
smear_width = 0.5
WAVE_REACH = 8
F32 = jnp.float32
BF16 = jnp.bfloat16
CENTRE = 4


def paired(block, axis, mask):
    return lax.ppermute(block, axis, [(i ^ mask, i) for i in range(lax.axis_size(axis))])


def beyond(block, axis):
    count = lax.axis_size(axis)
    route = [((i + (1 if i % 2 else -1)) % count, i) for i in range(count)]
    return lax.ppermute(block, axis, route)


def around(block, beside):
    column = jnp.stack([paired(block, "gy", 1), block, beyond(block, "gy")])
    column, beside = lax.optimization_barrier((column, beside))
    return [paired(column, "gx", 1), column, beyond(column, "gx")], beside


def whole(space=pltpu.VMEM):
    return pl.BlockSpec(memory_space=space)


def run(kernel, outs, args, scratch=(), hbm=0, flops=10_000_000, grant=16, name=None):
    specs = [whole()] * (len(args) - hbm) + [whole(pltpu.HBM)] * hbm
    return list(
        pl.pallas_call(
            kernel,
            out_shape=outs,
            in_specs=specs,
            out_specs=[whole() for _ in outs],
            scratch_shapes=list(scratch),
            compiler_params=pltpu.CompilerParams(vmem_limit_bytes=grant * 1024 * 1024),
            cost_estimate=pl.CostEstimate(
                flops=flops, bytes_accessed=1_000_000, transcendentals=0
            ),
            name=name,
        )(*args)
    )


def shape(*dims, dtype=F32):
    return jax.ShapeDtypeStruct(dims, dtype)


def split(value):
    high = value.astype(BF16)
    return high, (value - high.astype(F32)).astype(BF16)


def dot(left, right, contract=((1,), (0,))):
    return lax.dot_general(left, right, (contract, ((), ())), preferred_element_type=F32)


def dot3(left, right):
    left_high, left_low = split(left)
    right_high, right_low = split(right)
    return dot(left_high, right_high) + (dot(left_high, right_low) + dot(left_low, right_high))


def dot_split(left, right):
    right_high, right_low = split(right)
    return dot(left[0], right_high) + (dot(left[0], right_low) + dot(left[1], right_high))


def sin_cos(turns):
    quarter = jnp.round(turns * 4.0)
    x = (turns - quarter * 0.25) * (2.0 * math.pi)
    z = x * x
    sine = ((-1.9515295891e-4 * z + 8.3321608736e-3) * z - 1.6666654611e-1) * (z * x) + x
    cosine = (2.443315711809948e-5 * z - 1.388731625493765e-3) * z + 4.166664568298827e-2
    cosine = cosine * (z * z) - 0.5 * z + 1.0
    k = quarter.astype(jnp.int32) & 3
    odd = (k & 1) == 1
    by_sine = jnp.where(odd, cosine, sine)
    by_cosine = jnp.where(odd, sine, cosine)
    return (
        jnp.where(k >= 2, -by_sine, by_sine),
        jnp.where((k == 1) | (k == 2), -by_cosine, by_cosine),
    )


def stacked_left(value):
    high = value.astype(BF16).astype(F32)
    rows = jnp.concatenate([high, high, value - high, jnp.zeros_like(high)], axis=0)
    return rows.T.astype(BF16)


def stacked_right(value):
    high = value.astype(BF16).astype(F32)
    return jnp.concatenate([high, value - high, high, jnp.zeros_like(high)], axis=0).astype(BF16)


def silu_pair(value):
    gate = 1.0 / (1.0 + jnp.exp(-value))
    return value * gate, gate * (1.0 + value * (1.0 - gate))


def onehot_kinds(kinds, rows):
    levels = lax.broadcasted_iota(jnp.int32, (rows, kinds.shape[1]), 0).astype(F32)
    return jnp.where(kinds == levels, 1.0, 0.0)


def embedding_stack(embed):
    high = embed.astype(BF16).astype(F32)
    rest = embed - high
    middle = rest.astype(BF16).astype(F32)
    rows = jnp.concatenate([high, middle, rest - middle, jnp.zeros_like(high)], axis=0)
    return rows.T.astype(BF16)


def embedded(stack, kinds):
    hot = onehot_kinds(kinds, 8)
    return dot(stack, jnp.concatenate([hot, hot, hot, jnp.zeros_like(hot)], axis=0).astype(BF16))


def weights_of(stack_ref, part, rows):
    return dot(stack_ref[1 if part else 0], stacked_right(rows))


def mixed(sums, high_ref, low_ref, layer):
    squares = sums[1] * sums[1] + sums[2] * sums[2] + sums[3] * sums[3]
    both = jnp.concatenate([sums[0], squares], axis=0)
    return silu_pair(dot_split((high_ref[layer], low_ref[layer]), both))


def edge_parts(basis, unit):
    return [basis] + [basis * unit[i : i + 1] for i in range(3)]


def pack_kernel(place_ref, position_ref, species_ref, out_ref):
    rows = [position_ref[0, i] for i in range(3)] + [species_ref[0].astype(F32)]
    atoms = rows[0].shape[1]
    out_ref[...] = jnp.concatenate(
        [row[:, s : s + 128] for row in rows for s in range(0, atoms, 128)], axis=0
    )


def radial_left(radial):
    high = radial.astype(BF16).astype(F32)
    low = radial - high
    top = jnp.concatenate([high, high], axis=1)
    end = jnp.concatenate([low, jnp.zeros_like(low)], axis=1)
    return jnp.concatenate([top, end], axis=0).astype(BF16)


def put_split(value, high_ref, low_ref, *at):
    high, low = split(value)
    high_ref[at] = high
    low_ref[at] = low


def slot_order(ids, place_ref, atoms):
    cell = ids >> (atoms.bit_length() - 1) if atoms & (atoms - 1) == 0 else ids // atoms
    a = (cell * 11) >> 5
    b = cell - 3 * a
    a = jnp.where((place_ref[0, 0:1, 0:1] & 1) == 0, 2 - a, a)
    b = jnp.where((place_ref[1, 0:1, 0:1] & 1) == 0, 2 - b, b)
    return ids + (3 * a + b - cell) * atoms


def fetch(sources, targets, sems):
    copies = [
        pltpu.make_async_copy(source, target, sems.at[i])
        for i, (source, target) in enumerate(zip(sources, targets))
    ]
    for copy in copies:
        copy.start()
    for copy in copies:
        copy.wait()


def prep_first_kernel(norm, place_ref, ids_in, count_in, embed_in, radial_in, mixing_in, id_ref, count_ref,
                      embed_out, kind_left, left_out, back_out, kind_high, kind_low, mix_high,
                      mix_low, turn_high, turn_low, embed_ref, radial_ref, mixing_ref, sems):
    fetch(
        [ids_in, count_in, embed_in, radial_in, mixing_in],
        [id_ref, count_ref, embed_ref, radial_ref, mixing_ref],
        sems,
    )
    id_ref[...] = slot_order(id_ref[...], place_ref, count_ref.shape[2])
    embed = embed_ref[...]
    kinds = embed.shape[0]
    for path in range(2):
        radial = radial_ref[0, path] * norm
        rows = jnp.concatenate([radial * embed[s : s + 1] for s in range(kinds)], axis=0)
        kind_left[path] = stacked_left(rows)
        put_split(rows, kind_high, kind_low, path)
        radial = radial_ref[1, path] * norm
        left_out[path] = stacked_left(radial)
        back_out[path] = radial_left(radial)
    for layer in range(2):
        scalar, vector = mixing_ref[layer, 0], mixing_ref[layer, 1]
        put_split(jnp.concatenate([scalar.T, vector.T], axis=1), mix_high, mix_low, layer)
        put_split(jnp.concatenate([scalar, 2.0 * vector], axis=0), turn_high, turn_low, layer)
    embed = jnp.concatenate([embed, jnp.zeros((8 - kinds, embed.shape[1]), F32)], axis=0)
    embed_out[...] = embedding_stack(embed)


def prep_second_kernel(read_in, hidden_in, charge_in, read_ref, hidden_high, hidden_low,
                       hidden_turn_high, hidden_turn_low, charge_pair, hidden_ref, charge_ref, sems):
    fetch([read_in, hidden_in, charge_in], [read_ref, hidden_ref, charge_ref], sems)
    put_split(hidden_ref[...].T, hidden_high, hidden_low, Ellipsis)
    put_split(hidden_ref[...], hidden_turn_high, hidden_turn_low, Ellipsis)
    charge = charge_ref[...]
    high = charge.astype(BF16).astype(F32)
    charge_pair[0] = high.astype(BF16)
    charge_pair[1] = (charge - high).astype(BF16)


def hot_kernel(ids_ref, hot_ref):
    edges = ids_ref.shape[1]
    for start in range(0, edges, 256):
        lanes = slice(start, start + 256)
        hot_ref[:, lanes] = hot_columns(ids_ref[:, lanes], hot_ref.shape[0])


def hot_back_kernel(ids_ref, hot_ref):
    edges = ids_ref.shape[1]
    entry = lax.broadcasted_iota(jnp.int32, (128, hot_ref.shape[1]), 1).astype(F32)
    for start in range(0, edges, 128):
        row = jnp.broadcast_to(ids_ref[:, start : start + 128].astype(F32), (8, 128))
        column = row.T[:, 0:1]
        hot_ref[start : start + 128] = jnp.where(column == entry, 1.0, 0.0).astype(BF16)


def unfold_block(block, atoms):
    parts = atoms // 128
    rows = [block[r : r + 1] for r in range(4 * parts)]
    return [jnp.concatenate(rows[q * parts : (q + 1) * parts], axis=1) for q in range(4)]


def first_kernel(slots, place_ref, ids_ref, count_ref, embed_ref, kind_left, mix_high, mix_low,
                 pair_ref, column_ref, beyond_ref, low_ref, basis_ref, slope_ref, unit_ref, sums_ref,
                 gate_ref):
    atoms = low_ref.shape[1]
    ids = ids_ref[...]
    frame = [pair_ref, column_ref, beyond_ref]
    own = unfold_block(column_ref[1], atoms)
    per_cell = atoms // 128
    places = lax.broadcasted_iota(jnp.int32, (4 * per_cell, 128), 0)
    upper = places % per_cell
    kind_of_row = places // per_cell
    rows = []
    to_x = jnp.where(kind_of_row == 0, cell_width, 0.0)
    to_x = jnp.where((place_ref[0] & 1) == 0, to_x, -to_x)
    to_y = jnp.where(kind_of_row == 1, cell_width, 0.0)
    to_y = jnp.where((place_ref[1] & 1) == 0, to_y, -to_y)
    for a in range(3):
        for b in range(3):
            rows.append(frame[a][b] + ((1 - a) * to_x + (1 - b) * to_y))
    pieces = []
    for start in range(0, ids.shape[1], 128):
        part = jnp.broadcast_to(ids[:, start : start + 128], places.shape)
        lane, half = part & 127, (part >> 7) - upper
        found = jnp.zeros(places.shape, F32)
        for cell, block in enumerate(rows):
            value = jnp.take_along_axis(block, lane, axis=1)
            found = jnp.where(half == per_cell * cell, value, found)
        total = found
        for s in range(1, per_cell):
            total = total + pltpu.roll(found, 4 * per_cell - s, 0)
        pieces.append(total)
    found = jnp.concatenate(pieces, axis=1)
    found = [found[q * per_cell : q * per_cell + 1] for q in range(4)]
    rel = [found[q] - jnp.concatenate([own[q]] * slots, axis=1) for q in range(3)]
    distance = jnp.sqrt(rel[0] * rel[0] + rel[1] * rel[1] + rel[2] * rel[2] + soften)
    inverse = 1.0 / distance
    order = (lax.broadcasted_iota(jnp.int32, (8, 1), 0) + 1).astype(F32)
    sine, cosine = sin_cos((order * (0.5 / cut_radius)) * distance)
    wave = sine / ((order * (math.pi / cut_radius)) * distance)
    count = count_ref[0]
    live = jnp.concatenate([jnp.where(count > n, 1.0, 0.0) for n in range(slots)], axis=1)
    basis = wave * live
    basis_ref[...] = basis
    slope_ref[...] = (cosine - wave) * (inverse * live)
    kinds = found[3]
    unit = jnp.concatenate(
        [r * inverse for r in rel] + [inverse, kinds] + [jnp.zeros_like(kinds)] * 3, axis=0
    )
    unit_ref[...] = unit
    stack = embed_ref[...]
    parts = edge_parts(basis, unit)
    species = kind_left.shape[2] // 32
    by_kind = [[None] * species for _ in range(4)]
    for n in range(slots):
        lanes = slice(n * atoms, (n + 1) * atoms)
        kind = jnp.broadcast_to(kinds[:, lanes], (8, atoms))
        for k in range(species):
            match = kind == float(k)
            for part in range(4):
                term = jnp.where(match, parts[part][:, lanes], 0.0)
                old = by_kind[part][k]
                by_kind[part][k] = term if old is None else old + term
    stacks = [stacked_right(jnp.concatenate(rows, axis=0)) for rows in by_kind]
    vectors = dot(kind_left[1], jnp.concatenate(stacks[1:], axis=1))
    sums = [dot(kind_left[0], stacks[0])]
    sums += [vectors[:, i * atoms : (i + 1) * atoms] for i in range(3)]
    step, gate = mixed(sums, mix_high, mix_low, 0)
    low_ref[...] = (embedded(stack, own[3]) + step).astype(BF16)
    for part in range(3):
        sums_ref[part] = sums[part + 1]
    gate_ref[...] = gate


def hot_columns(ids, rows):
    place = lax.broadcasted_iota(jnp.int32, (rows, ids.shape[1]), 0)
    return jnp.where(ids == place, 1.0, 0.0).astype(BF16)


def second_near_kernel(slots, ids_ref, basis_ref, unit_ref, left_ref, hot_ref, column_ref,
                       weight_ref, near_ref, beyond_ref):
    atoms = column_ref.shape[2]
    parts = edge_parts(basis_ref[...], unit_ref[...])
    source = jnp.concatenate([column_ref[b] for b in range(3)], axis=1)
    for n in range(slots):
        lanes = slice(n * atoms, (n + 1) * atoms)
        for part in range(4):
            weight_ref[part, :, lanes] = weights_of(left_ref, part, parts[part][:, lanes])
        near_ref[:, lanes] = dot(source, hot_ref[3 * atoms : 6 * atoms, lanes])
        beyond_ref[:, lanes] = hot_columns(ids_ref[:, lanes] - 6 * atoms, 3 * atoms)


def second_side_kernel(slots, hot_ref, near_ref, pair_ref, out_ref):
    atoms = pair_ref.shape[2]
    source = jnp.concatenate([pair_ref[b] for b in range(3)], axis=1)
    for n in range(slots):
        lanes = slice(n * atoms, (n + 1) * atoms)
        out_ref[:, lanes] = near_ref[:, lanes] + dot(source, hot_ref[: 3 * atoms, lanes])


def second_kernel(slots, hot_ref, weight_ref, near_ref, mix_high, mix_low, charge_ref, cell_ref,
                  column_ref, beyond_ref, feature_ref, sums_ref, gate_ref, packed_ref,
                  full_charge_ref, hidden_ref):
    atoms = column_ref.shape[2]
    source = jnp.concatenate([beyond_ref[b] for b in range(3)], axis=1)
    sums = [None] * 4
    for n in range(slots):
        lanes = slice(n * atoms, (n + 1) * atoms)
        feature = near_ref[:, lanes] + dot(source, hot_ref[:, lanes])
        feature_ref[:, lanes] = feature.astype(BF16)
        for part in range(4):
            term = weight_ref[part, :, lanes] * feature
            sums[part] = term if sums[part] is None else sums[part] + term
    step, gate = mixed(sums, mix_high, mix_low, 1)
    hidden = column_ref[1].astype(F32) + step
    hidden_ref[...] = hidden
    for part in range(3):
        sums_ref[part] = sums[part + 1]
    gate_ref[...] = gate
    charge = dot_split((charge_ref[0], charge_ref[1]), hidden)
    full_charge_ref[...] = charge
    place = jnp.concatenate(unfold_block(cell_ref[1], atoms)[:3], axis=0)
    high = place.astype(BF16).astype(F32)
    rest = place - high
    middle = rest.astype(BF16).astype(F32)
    zero = jnp.zeros((packed_ref.shape[0] - charge.shape[0] - 9, atoms), F32)
    packed_ref[...] = jnp.concatenate([charge, high, middle, rest - middle, zero], axis=0).astype(
        BF16
    )


def readout_kernel(hidden_high, hidden_low, turn_high, turn_low, out_ref, hidden_ref, energy_ref,
                   slope_ref):
    hidden = hidden_ref[...]
    value, slope = silu_pair(dot_split((hidden_high[...], hidden_low[...]), hidden))
    out = out_ref[...].T
    energy_ref[...] = jnp.sum(value * out, axis=0, keepdims=True)
    slope_ref[...] = dot_split((turn_high[...], turn_low[...]), slope * out)


def message_grads(cotangent, gate_ref, sums_ref, high_ref, low_ref, layer):
    pre = cotangent * gate_ref[...]
    both = dot_split((high_ref[layer], low_ref[layer]), pre)
    half = both.shape[0] // 2
    return [both[:half]] + [both[half:] * sums_ref[i] for i in range(3)]


def radial_grad(left, value):
    high, low = split(value)
    both = dot(left, jnp.concatenate([high, low], axis=0))
    half = both.shape[0] // 2
    return both[:half] + both[half:]


def second_back_kernel(slots, scale, count, hot_ref, weight_ref, turn_high, turn_low, charge_ref,
                       sums_ref, gate_ref, full_charge_ref, energy_ref, slope_ref, *refs):
    folds, refs = refs[:count], refs[count:]
    site_ref, long_ref, cotangent_ref, grad_ref, term_ref, sides_ref, beyond_ref, pair_ref = refs
    atoms = gate_ref.shape[1]
    total = folds[0][0].astype(F32)
    for part in folds[1:]:
        total = total + part[0].astype(F32)
    wide = full_charge_ref.shape[0]
    potential = total[:wide] * (2.0 * scale)
    slopes = total[wide : wide + 3] + total[wide + 3 : wide + 6] + total[wide + 6 : wide + 9]
    long_ref[...] = jnp.concatenate(
        [slopes * (2.0 * scale), jnp.zeros((5, atoms), F32)], axis=0
    )
    site_ref[0] = energy_ref[...] + 0.5 * jnp.sum(
        full_charge_ref[...] * potential, axis=0, keepdims=True
    )
    high, low = split(potential)
    turned = ((0,), (0,))
    cotangent = slope_ref[...] + (
        dot(charge_ref[0], high, turned)
        + (dot(charge_ref[0], low, turned) + dot(charge_ref[1], high, turned))
    )
    cotangent_ref[...] = cotangent
    grads = message_grads(cotangent, gate_ref, sums_ref, turn_high, turn_low, 1)
    for part in range(4):
        grad_ref[part] = grads[part]
    for n in range(slots):
        lanes = slice(n * atoms, (n + 1) * atoms)
        term = weight_ref[0, :, lanes] * grads[0]
        for part in range(1, 4):
            term = term + weight_ref[part, :, lanes] * grads[part]
        term_ref[:, lanes] = term.astype(BF16)
    for b in range(3):
        start = (6 + b) * atoms
        grad = dot(term_ref[...], hot_ref[:, start : start + atoms]).astype(BF16)
        if b == 1:
            beyond_ref[...] = grad
        else:
            sides_ref[b // 2] = grad
    for b in range(3):
        pair_ref[b] = dot(term_ref[...], hot_ref[:, b * atoms : (b + 1) * atoms]).astype(BF16)


def second_middle_kernel(hot_ref, term_ref, cotangent_ref, middle_ref):
    atoms = cotangent_ref.shape[1]
    for b in range(3):
        grad = dot(term_ref[...], hot_ref[:, (3 + b) * atoms : (4 + b) * atoms])
        middle_ref[b] = grad + cotangent_ref[...] if b == 1 else grad


def second_edge_kernel(slots, back_ref, feature_ref, grad_ref, edge_ref):
    atoms = grad_ref.shape[2]
    for n in range(slots):
        lanes = slice(n * atoms, (n + 1) * atoms)
        feature = feature_ref[:, lanes].astype(F32)
        for part in range(4):
            edge_ref[8 * part : 8 * part + 8, lanes] = radial_grad(
                back_ref[1 if part else 0], grad_ref[part] * feature
            )


def first_back_kernel(slots, ids_ref, basis_ref, slope_ref, unit_ref, kind_high, kind_low,
                      turn_high, turn_low, sums_ref, gate_ref, edge_ref, long_ref, middle_ref,
                      *refs):
    from_x, from_y, outs = refs[:2], refs[2:4], refs[4:]
    atoms = gate_ref.shape[1]
    cotangent = middle_ref[1]
    for block in (from_x[0][1], from_x[1][...], from_y[0][...], from_y[1][...]):
        cotangent = cotangent + block.astype(F32)
    grads = message_grads(cotangent, gate_ref, sums_ref, turn_high, turn_low, 0)
    unit = unit_ref[...]
    kinds = unit[4:5]
    by_kind = [dot_split((kind_high[0], kind_low[0]), grads[0])]
    by_kind += [dot_split((kind_high[1], kind_low[1]), grads[i]) for i in range(1, 4)]
    species = by_kind[0].shape[0] // 8
    edges = [[] for _ in range(4)]
    for n in range(slots):
        kind = jnp.broadcast_to(kinds[:, n * atoms : (n + 1) * atoms], (8, atoms))
        matches = [kind == float(k) for k in range(1, species)]
        for part in range(4):
            rows = by_kind[part]
            found = rows[:8]
            for k, match in enumerate(matches):
                found = jnp.where(match, rows[8 * k + 8 : 8 * k + 16], found)
            edges[part].append(found)
    edges = [
        edge_ref[8 * part : 8 * part + 8] + jnp.concatenate(edges[part], axis=1) for part in range(4)
    ]
    basis = basis_ref[...]
    units = [unit[i : i + 1] for i in range(3)]
    inverse = unit[3:4]
    by_basis = edges[0]
    for i in range(3):
        by_basis = by_basis + edges[i + 1] * units[i]
    by_unit = [jnp.sum(edges[i + 1] * basis, axis=0, keepdims=True) * inverse for i in range(3)]
    by_distance = jnp.sum(by_basis * slope_ref[...], axis=0, keepdims=True)
    for i in range(3):
        by_distance = by_distance - by_unit[i] * units[i]
    moves = [by_unit[i] + by_distance * units[i] for i in range(3)]
    zero = jnp.zeros_like(moves[0])
    move = jnp.concatenate(moves + [zero] * 5, axis=0)
    own = long_ref[...]
    for n in range(slots):
        own = own - move[:, n * atoms : (n + 1) * atoms]
    ids = ids_ref[...]
    lane_hot = hot_columns(ids & 127, 128)
    half = ids >> 7
    high = move.astype(BF16).astype(F32)
    both = jnp.concatenate([high, move - high], axis=0)
    per_cell = atoms // 128
    rows = jnp.concatenate(
        [jnp.where(half == h, both, 0.0).astype(BF16) for h in range(9 * per_cell)], axis=0
    )
    spread = dot(rows, lane_hot, ((1,), (1,)))
    for cell in range(9):
        found = []
        for h in range(cell * per_cell, (cell + 1) * per_cell):
            found.append(spread[16 * h : 16 * h + 8] + spread[16 * h + 8 : 16 * h + 16])
        grad = jnp.concatenate(found, axis=1)
        if cell == CENTRE:
            grad = own + grad
        outs[cell // 3][cell % 3] = grad


def pair_counts(parts):
    total = WAVE_REACH + WAVE_REACH * (2 * WAVE_REACH + 1)
    share = -(-total // parts)
    return total, share, -(-share // 16) * 16


def pair_vectors(slot, share, part):
    side = 2 * WAVE_REACH + 1
    total = WAVE_REACH + WAVE_REACH * side
    index = slot + part.astype(F32) * share
    later = index - WAVE_REACH
    row = jnp.floor((later + 0.5) * (1.0 / side))
    first = index < WAVE_REACH
    kx = jnp.where(first, 0.0, row + 1.0)
    ky = jnp.where(first, index + 1.0, later - row * side - WAVE_REACH)
    valid = jnp.where((slot < share) & (index < total), 1.0, 0.0)
    return kx, ky, valid


def count_up(rows):
    return lax.broadcasted_iota(jnp.int32, (rows, 1), 0).astype(F32)


def green_weights(share, padded, grid, place_ref, vec_ref, weight_ref):
    grid_x, grid_y = grid
    turn = 2.0 * math.pi
    side = 2 * WAVE_REACH + 1
    top = side * side * side - 1
    vec = vec_ref[...].astype(F32) + WAVE_REACH
    code = (vec[0:1] * side + vec[1:2]) * side + vec[2:3]
    code = jnp.maximum(code, top - code)
    span = 8 * share
    row = count_up(span)
    slot = jnp.floor(row * 0.125)
    height = row - 8.0 * slot + 1.0
    flat = count_up(padded)
    slot = jnp.concatenate([slot, slot, flat], axis=0)
    kz = jnp.concatenate([height, -height, jnp.zeros_like(flat)], axis=0)
    kx, ky, valid = pair_vectors(slot, share, place_ref[0, 0:1, 0:1])
    own = ((kx + WAVE_REACH) * side + ky + WAVE_REACH) * side + kz + WAVE_REACH
    seen = jnp.zeros((own.shape[0], 128), F32)
    for start in range(0, code.shape[1], 128):
        seen = seen + jnp.where(own == code[:, start : start + 128], 1.0, 0.0)
    count = jnp.sum(seen, axis=1, keepdims=True) * valid
    sq = (
        (kx * (turn / (grid_x * cell_width))) ** 2
        + (ky * (turn / (grid_y * cell_width))) ** 2
        + (kz * (turn / box_height)) ** 2
    )
    green = jnp.exp(-smear_width * sq) / (sq + screen * screen) * count
    weight_ref[...] = jnp.broadcast_to(green, weight_ref.shape)


def basis_rows(share, ca, sa, cb, sb):
    cc, ss, sc, cs = [], [], [], []
    for p in range(share):
        c, s = ca[p : p + 1], sa[p : p + 1]
        cc.append(c * cb)
        ss.append(s * sb)
        sc.append(s * cb)
        cs.append(c * sb)
    return cc, ss, sc, cs


def unpack_rows(block):
    half = block.shape[1] // 2
    return jnp.concatenate([block[:, :half], block[:, half:]], axis=0)


def pack_rows(block):
    half = block.shape[0] // 2
    return jnp.concatenate([block[:half], block[half:]], axis=1)


def structure_kernel(share, padded, grid, wide, flip, place_ref, blocks, *refs):
    grid_x, grid_y = grid
    if flip:
        near_ref, (ca_ref, sa_ref, cb_ref, sb_ref, high_ref, low_ref, own_ref, out_ref) = (
            refs[0],
            refs[1:],
        )
        total = near_ref[...]
    else:
        ca_ref, sa_ref, cb_ref, sb_ref, high_ref, low_ref, total_ref = refs
        total = None
    col = place_ref[1, 0:1, 0:1].astype(F32) * (1.0 / grid_y)
    first = place_ref[0, 0:1, 0:1] ^ flip
    kx, ky, _ = pair_vectors(count_up(padded), share, place_ref[0, 0:1, 0:1])
    kz = count_up(8) + 1.0
    for d in range(grid_x // 2):
        block = blocks[d]
        charge = block[:wide]
        atoms = charge.shape[1]
        pieces = block[wide:].astype(F32)
        place = pieces[0:3] + (pieces[3:6] + pieces[6:9])
        row = (first ^ (2 * d)).astype(F32) * (1.0 / grid_x)
        x = place[0:1] * (1.0 / (grid_x * cell_width)) + row
        y = place[1:2] * (1.0 / (grid_y * cell_width)) + col
        sa, ca = sin_cos(kx * x + ky * y)
        sb, cb = sin_cos(kz * (place[2:3] * (1.0 / box_height)))
        lanes = pl.ds(d * atoms, atoms)
        ca_ref[:, lanes] = ca
        sa_ref[:, lanes] = sa
        cb_ref[:, lanes] = cb
        sb_ref[:, lanes] = sb
        cc, ss, sc, cs = basis_rows(share, ca, sa, cb, sb)
        high, low = split(jnp.concatenate(cc + ss + sc + cs + [ca, sa], axis=0))
        high_ref[:, lanes] = high
        low_ref[:, lanes] = low
        term = dot(high, charge, ((1,), (1,))) + dot(low, charge, ((1,), (1,)))
        total = term if total is None else total + term
    if flip:
        packed = pack_rows(total)
        own_ref[...] = packed
        out_ref[...] = packed.astype(BF16)
    else:
        total_ref[...] = total


def weighted_rows(share, padded, wide, weight_ref, parts):
    packed = parts[0][...].astype(F32)
    for part in parts[1:]:
        packed = packed + part[...].astype(F32)
    struct = unpack_rows(packed)
    span = 8 * share
    cc, ss, sc, cs = (struct[i * span : (i + 1) * span] for i in range(4))
    weight = weight_ref[:, :wide]
    plus, minus, flat = weight[:span], weight[span : 2 * span], weight[2 * span :]
    re_plus, im_plus = plus * (cc - ss), plus * (sc + cs)
    re_minus, im_minus = minus * (cc + ss), minus * (sc - cs)
    rows = jnp.concatenate(
        [
            re_plus + re_minus,
            re_minus - re_plus,
            im_plus + im_minus,
            im_plus - im_minus,
            flat * struct[4 * span : 4 * span + padded],
            flat * struct[4 * span + padded :],
        ],
        axis=0,
    )
    return rows


def fold_kernel(share, padded, grid, wide, flip, place_ref, *refs):
    grid_x, grid_y = grid
    turn = 2.0 * math.pi
    if flip:
        weight_ref, parts, refs = refs[0], refs[1 : 1 + grid_y], refs[1 + grid_y :]
        rows = weighted_rows(share, padded, wide, weight_ref, parts)
        refs, rows_ref = refs[:-1], refs[-1]
        rows_ref[...] = rows
    else:
        rows, refs = refs[0][...], refs[1:]
    ca_ref, sa_ref, cb_ref, sb_ref, high_ref, low_ref, blocks, out_ref = refs
    row_high, row_low = split(rows)
    row_pair = jnp.concatenate([row_high, row_low], axis=1)
    turned = rows.T
    t_high, t_low = split(turned)
    t_both = jnp.concatenate([t_high, t_low], axis=0)
    span = 8 * share
    kx, ky, _ = pair_vectors(count_up(padded), share, place_ref[0, 0:1, 0:1])
    kx = kx * (turn / (grid_x * cell_width))
    ky = ky * (turn / (grid_y * cell_width))
    kz = (count_up(8) + 1.0) * (turn / box_height)
    for d in range(grid_x // 2):
        charge = blocks[d][:wide]
        atoms = charge.shape[1]
        lanes = pl.ds(d * atoms, atoms)
        ca, sa, cb, sb = ca_ref[:, lanes], sa_ref[:, lanes], cb_ref[:, lanes], sb_ref[:, lanes]
        bcc, bss, bsc, bcs = basis_rows(share, ca, sa, cb, sb)
        high, low = high_ref[:, lanes], low_ref[:, lanes]
        both = dot(t_both, high)
        pot = both[:wide] + both[wide:] + dot(t_high, low)
        proj = dot(row_pair, jnp.concatenate([charge, charge], axis=0))
        by_x = jnp.zeros((8, atoms), jnp.float32)
        by_y = jnp.zeros((8, atoms), jnp.float32)
        by_z = jnp.zeros((8, atoms), jnp.float32)
        for p in range(share):
            pcc, pss, psc, pcs = (
                proj[i * span + 8 * p : i * span + 8 * p + 8] for i in range(4)
            )
            slope = bcs[p] * pss - bsc[p] * pcc + bcc[p] * psc - bss[p] * pcs
            by_x = by_x + kx[p : p + 1] * slope
            by_y = by_y + ky[p : p + 1] * slope
            by_z = by_z + (bsc[p] * pss - bcs[p] * pcc - bss[p] * psc + bcc[p] * pcs)
        flat_slope = ca * proj[4 * span + padded :] - sa * proj[4 * span : 4 * span + padded]
        grad_x = jnp.sum(by_x, axis=0, keepdims=True) + jnp.sum(kx * flat_slope, axis=0, keepdims=True)
        grad_y = jnp.sum(by_y, axis=0, keepdims=True) + jnp.sum(ky * flat_slope, axis=0, keepdims=True)
        grad_z = jnp.sum(kz * by_z, axis=0, keepdims=True)
        slopes = jnp.concatenate([grad_x, grad_y, grad_z], axis=0)
        out_ref[d] = pieced(pot, slopes, out_ref.shape[1]).astype(out_ref.dtype)


def pieced(pot, slopes, rows):
    high = slopes.astype(BF16).astype(F32)
    rest = slopes - high
    middle = rest.astype(BF16).astype(F32)
    zero = jnp.zeros((rows - pot.shape[0] - 9, pot.shape[1]), F32)
    return jnp.concatenate([pot, high, middle, rest - middle, zero], axis=0)


def unpieced(block, wide):
    slopes = block[wide : wide + 3] + (block[wide + 3 : wide + 6] + block[wide + 6 : wide + 9])
    return block[:wide], slopes


def join_kernel(wide, kept_ref, come_ref, keep_ref, send_ref):
    for d in range(kept_ref.shape[0]):
        pot, slopes = unpieced(kept_ref[d], wide)
        pot_come, slopes_come = unpieced(come_ref[d].astype(F32), wide)
        block = pieced(pot + pot_come, slopes + slopes_come, kept_ref.shape[1])
        if d % 2:
            send_ref[d // 2] = block.astype(BF16)
        else:
            keep_ref[d // 2] = block


def per_device(
    positions,
    species,
    neighbours,
    counts,
    species_embed,
    radial,
    mixing,
    read_hidden,
    read_out,
    charge_map,
    wavevectors,
):
    atoms = positions.shape[3]
    slots = neighbours.shape[3]
    features, lat_width = charge_map.shape
    wave_count = wavevectors.shape[1]
    grid = lax.axis_size("gx"), lax.axis_size("gy")
    grid_x, grid_y = grid
    edges = slots * atoms
    scale = 1.0 / math.sqrt(wave_count * lat_width * atoms * grid_x * grid_y)
    place = jnp.stack([lax.axis_index("gx"), lax.axis_index("gy")]).astype(jnp.int32)
    place = jnp.broadcast_to(place[:, None, None], (2, 8, 128))
    _, share, padded = pair_counts(grid_x)
    ids = neighbours.transpose(0, 3, 1, 2).reshape(1, edges)
    dma = pltpu.SemaphoreType.DMA
    (own,) = run(
        pack_kernel,
        [shape(4 * atoms // 128, 128)],
        [place, positions.transpose(0, 2, 1, 3), species],
        flops=10_000_000_000,
        name="pack",
    )
    norm = 1.0 / math.sqrt(slots)
    kind_rows = 8 * species_embed.shape[0]
    low_pair = lambda *dims: [shape(*dims, dtype=BF16)] * 2
    (ids, counts, embed, kind_left, left, back, kind_high, kind_low, mix_high, mix_low, turn_high,
     turn_low) = run(
        functools.partial(prep_first_kernel, norm),
        [
            shape(1, edges, dtype=jnp.int32),
            shape(*counts.shape, dtype=jnp.int32),
            shape(features, 32, dtype=BF16),
            shape(2, features, 4 * kind_rows, dtype=BF16),
            shape(2, features, 32, dtype=BF16),
            shape(2, 16, 2 * features, dtype=BF16),
        ]
        + low_pair(2, kind_rows, features)
        + low_pair(2, features, 2 * features)
        + low_pair(2, 2 * features, features),
        [place, ids, counts, species_embed, radial, mixing],
        scratch=[
            pltpu.VMEM(species_embed.shape, F32),
            pltpu.VMEM(radial.shape, F32),
            pltpu.VMEM(mixing.shape, F32),
            dma((5,)),
        ],
        hbm=5,
        name="prep_first",
    )
    cells, ids = around(own, ids)
    (hot,) = run(
        hot_kernel,
        [shape(6 * atoms, edges, dtype=BF16)],
        [ids],
        flops=1_000_000,
        name="hot",
    )
    read_out, hidden_high, hidden_low, hidden_turn_high, hidden_turn_low, charge_pair = run(
        prep_second_kernel,
        [shape(1, features)]
        + low_pair(features, features)
        + low_pair(features, features)
        + [shape(2, lat_width, features, dtype=BF16)],
        [read_out[None, :], read_hidden, charge_map.T],
        scratch=[
            pltpu.VMEM(read_hidden.shape, F32),
            pltpu.VMEM((lat_width, features), F32),
            dma((3,)),
        ],
        hbm=3,
        name="prep_second",
    )
    low, basis, slope, unit, sums_one, gate_one = run(
        functools.partial(first_kernel, slots),
        [
            shape(features, atoms, dtype=BF16),
            shape(8, edges),
            shape(8, edges),
            shape(8, edges),
            shape(3, features, atoms),
            shape(features, atoms),
        ],
        [place, ids, counts, embed, kind_left, mix_high, mix_low] + cells,
        name="first",
    )
    hidden, hot = around(low, hot)
    edge_weights, near, hot_beyond = run(
        functools.partial(second_near_kernel, slots),
        [
            shape(4, features, edges),
            shape(features, edges),
            shape(3 * atoms, edges, dtype=BF16),
        ],
        [ids, basis, unit, left, hot, hidden[1]],
        flops=2_000_000_000,
        name="second_near",
    )
    (near,) = run(
        functools.partial(second_side_kernel, slots),
        [shape(features, edges)],
        [hot, near, hidden[0]],
        flops=1_000_000_000,
        name="second_side",
    )
    block_rows = -(-(lat_width + 9) // 16) * 16
    feature, sums_two, gate_two, packed, charge, hidden_two = run(
        functools.partial(second_kernel, slots),
        [
            shape(features, edges, dtype=BF16),
            shape(3, features, atoms),
            shape(features, atoms),
            shape(block_rows, atoms, dtype=BF16),
            shape(lat_width, atoms),
            shape(features, atoms),
        ],
        [hot_beyond, edge_weights, near, mix_high, mix_low, charge_pair, cells[1], hidden[1],
         hidden[2]],
        name="second",
    )
    energy, energy_slope = run(
        readout_kernel,
        [shape(1, atoms), shape(features, atoms)],
        [hidden_high, hidden_low, hidden_turn_high, hidden_turn_low, read_out, hidden_two],
        name="readout",
    )
    half = grid_x // 2
    near_charges = jnp.stack([packed] + [paired(packed, "gx", 2 * d) for d in range(1, half)])
    (weight,) = run(
        functools.partial(green_weights, share, padded, grid),
        [shape(16 * share + padded, 128)],
        [place, wavevectors],
        name="green",
    )
    near_charges, weight = lax.optimization_barrier((near_charges, weight))
    far_charges = paired(near_charges, "gx", 1)
    span = half * atoms
    rows = 32 * share + 2 * padded
    phase_shapes = [
        shape(padded, span),
        shape(padded, span),
        shape(8, span),
        shape(8, span),
        shape(rows, span, dtype=BF16),
        shape(rows, span, dtype=BF16),
    ]
    *near_phases, near_total = run(
        functools.partial(structure_kernel, share, padded, grid, lat_width, 0),
        phase_shapes + [shape(rows, lat_width)],
        [place, near_charges],
        flops=1_000_000_000,
        name="structure_near",
    )
    *far_phases, own_part, part = run(
        functools.partial(structure_kernel, share, padded, grid, lat_width, 1),
        phase_shapes
        + [
            shape(rows // 2, 2 * lat_width),
            shape(rows // 2, 2 * lat_width, dtype=BF16),
        ],
        [place, far_charges, near_total],
        name="structure_far",
    )
    parts = [own_part] + [paired(part, "gy", d) for d in range(1, grid_y)]
    (hot_back,) = run(
        hot_back_kernel,
        [shape(edges, 9 * atoms, dtype=BF16)],
        [ids],
        flops=2_000_000_000,
        name="hot_back",
    )
    parts, hot_back = lax.optimization_barrier((parts, hot_back))
    far_folds, wave_rows = run(
        functools.partial(fold_kernel, share, padded, grid, lat_width, 1),
        [shape(half, block_rows, atoms, dtype=BF16), shape(rows, lat_width)],
        [place, weight] + parts + far_phases + [far_charges],
        name="fold_far",
    )
    far_folds = paired(far_folds, "gx", 1)
    (near_folds,) = run(
        functools.partial(fold_kernel, share, padded, grid, lat_width, 0),
        [shape(half, block_rows, atoms)],
        [place, wave_rows] + near_phases + [near_charges],
        flops=1_000_000_000,
        name="fold_near",
    )
    kept, come, mask = near_folds, far_folds, 2
    while mask < grid_x:
        count = kept.shape[0] // 2
        kept, sent = run(
            functools.partial(join_kernel, lat_width),
            [
                shape(count, block_rows, atoms),
                shape(count, block_rows, atoms, dtype=BF16),
            ],
            [kept, come],
            name="fold_join",
        )
        come = paired(sent, "gx", mask)
        mask *= 2
    folds = [kept, come]

    site, long, cotangent, grads, term, to_sides, to_beyond, to_pair = run(
        functools.partial(second_back_kernel, slots, scale, len(folds)),
        [
            shape(1, 1, atoms),
            shape(8, atoms),
            shape(features, atoms),
            shape(4, features, atoms),
            shape(features, edges, dtype=BF16),
            shape(2, features, atoms, dtype=BF16),
            shape(features, atoms, dtype=BF16),
            shape(3, features, atoms, dtype=BF16),
        ],
        [hot_back, edge_weights, turn_high, turn_low, charge_pair, sums_two, gate_two, charge,
         energy, energy_slope] + folds,
        name="second_back",
    )
    from_pair, from_sides = paired(to_pair, "gx", 1), beyond(to_sides, "gx")
    (middle,) = run(
        second_middle_kernel,
        [shape(3, features, atoms)],
        [hot_back, term, cotangent],
        flops=1_000_000_000,
        name="second_middle",
    )
    sides = [
        (middle[2 * b] + from_pair[2 * b].astype(F32) + from_sides[b].astype(F32)).astype(BF16)
        for b in range(2)
    ]
    sides, to_beyond = lax.optimization_barrier((sides, to_beyond))
    from_beyond = beyond(to_beyond, "gx")
    from_y = [paired(sides[0], "gy", 1), beyond(sides[1], "gy")]
    (edge,) = run(
        functools.partial(second_edge_kernel, slots),
        [shape(32, edges)],
        [back, feature, grads],
        flops=1_000_000_000,
        name="second_edge",
    )
    to_pair, middle, to_beyond = run(
        functools.partial(first_back_kernel, slots),
        [shape(3, 8, atoms)] * 3,
        [ids, basis, slope, unit, kind_high, kind_low, turn_high, turn_low, sums_one, gate_one, edge,
         long, middle, from_pair, from_beyond] + from_y,
        name="first_back",
    )
    total = middle + paired(to_pair, "gx", 1) + beyond(to_beyond, "gx")
    total = total[1] + paired(total[0], "gy", 1) + beyond(total[2], "gy")
    forces = -total[None, :3, None, :]
    return (forces.transpose(0, 2, 1, 3), site)


def solution(mesh):
    in_specs = (
        P("gx", "gy", None, None),
        P("gx", "gy", None),
        P("gx", "gy", None, None),
        P("gx", "gy", None),
        P(),
        P(),
        P(),
        P(),
        P(),
        P(),
        P(),
    )
    out_specs = (P("gx", "gy", None, None), P("gx", "gy", None))
    return jax.shard_map(
        per_device, mesh=mesh, in_specs=in_specs, out_specs=out_specs, check_vma=False
    )
```

```python
import functools
import math

import jax
import jax.numpy as jnp
import numpy as np
from jax import lax
from jax.experimental import pallas as pl
from jax.experimental.pallas import tpu as pltpu
from jax.sharding import PartitionSpec as P

cell_width = 10.0
box_height = 30.0
cut_radius = 50.0
soften = 0.25
screen = 0.5
smear_width = 0.5
WAVE_REACH = 8
F32 = jnp.float32
BF16 = jnp.bfloat16


def paired(block, axis, mask):
    return lax.ppermute(block, axis, [(i ^ mask, i) for i in range(lax.axis_size(axis))])


def other_side(index, count):
    return (index + (1 if index % 2 else -1)) % count


def beyond(block, axis):
    count = lax.axis_size(axis)
    return lax.ppermute(block, axis, [(other_side(i, count), i) for i in range(count)])


def far(block, axis, over_pair):
    count = lax.axis_size(axis)
    if over_pair:
        route = [(other_side(i ^ 1, count), i) for i in range(count)]
    else:
        route = [(other_side(i, count) ^ 1, i) for i in range(count)]
    return lax.ppermute(block, axis, route)


SLOT_CELLS = ((2, 1, 0), (1, 2, 3), (4, 3, 2))


def whole(space=pltpu.VMEM):
    return pl.BlockSpec(memory_space=space)


def run(kernel, outs, args, scratch=(), hbm=0, flops=10_000_000, grant=16, name=None):
    specs = [whole()] * (len(args) - hbm) + [whole(pltpu.HBM)] * hbm
    return list(
        pl.pallas_call(
            kernel,
            out_shape=outs,
            in_specs=specs,
            out_specs=[whole() for _ in outs],
            scratch_shapes=list(scratch),
            compiler_params=pltpu.CompilerParams(vmem_limit_bytes=grant * 1024 * 1024),
            cost_estimate=pl.CostEstimate(
                flops=flops, bytes_accessed=1_000_000, transcendentals=0
            ),
            name=name,
        )(*args)
    )


def shape(*dims, dtype=F32):
    return jax.ShapeDtypeStruct(dims, dtype)


def split(value):
    high = value.astype(BF16)
    return high, (value - high.astype(F32)).astype(BF16)


def dot(left, right, contract=((1,), (0,))):
    return lax.dot_general(left, right, (contract, ((), ())), preferred_element_type=F32)


def dot3(left, right):
    left_high, left_low = split(left)
    right_high, right_low = split(right)
    return dot(left_high, right_high) + (dot(left_high, right_low) + dot(left_low, right_high))


def dot_split(left, right):
    right_high, right_low = split(right)
    return dot(left[0], right_high) + (dot(left[0], right_low) + dot(left[1], right_high))


def sin_cos(turns):
    quarter = jnp.round(turns * 4.0)
    x = (turns - quarter * 0.25) * (2.0 * math.pi)
    z = x * x
    sine = ((-1.9515295891e-4 * z + 8.3321608736e-3) * z - 1.6666654611e-1) * (z * x) + x
    cosine = (2.443315711809948e-5 * z - 1.388731625493765e-3) * z + 4.166664568298827e-2
    cosine = cosine * (z * z) - 0.5 * z + 1.0
    k = quarter.astype(jnp.int32) & 3
    odd = (k & 1) == 1
    by_sine = jnp.where(odd, cosine, sine)
    by_cosine = jnp.where(odd, sine, cosine)
    return (
        jnp.where(k >= 2, -by_sine, by_sine),
        jnp.where((k == 1) | (k == 2), -by_cosine, by_cosine),
    )


def stacked_left(value):
    high = value.astype(BF16).astype(F32)
    rows = jnp.concatenate([high, high, value - high, jnp.zeros_like(high)], axis=0)
    return rows.T.astype(BF16)


def stacked_right(value):
    high = value.astype(BF16).astype(F32)
    return jnp.concatenate([high, value - high, high, jnp.zeros_like(high)], axis=0).astype(BF16)


def silu_pair(value):
    gate = 1.0 / (1.0 + jnp.exp(-value))
    return value * gate, gate * (1.0 + value * (1.0 - gate))


def onehot_kinds(kinds, rows):
    levels = lax.broadcasted_iota(jnp.int32, (rows, kinds.shape[1]), 0).astype(F32)
    return jnp.where(kinds == levels, 1.0, 0.0)


def embedding_stack(embed):
    high = embed.astype(BF16).astype(F32)
    rest = embed - high
    middle = rest.astype(BF16).astype(F32)
    rows = jnp.concatenate([high, middle, rest - middle, jnp.zeros_like(high)], axis=0)
    return rows.T.astype(BF16)


def embedded(stack, kinds):
    hot = onehot_kinds(kinds, 8)
    return dot(stack, jnp.concatenate([hot, hot, hot, jnp.zeros_like(hot)], axis=0).astype(BF16))


def weights_of(stack_ref, part, rows):
    return dot(stack_ref[1 if part else 0], stacked_right(rows))


def mixed(sums, high_ref, low_ref, layer):
    squares = sums[1] * sums[1] + sums[2] * sums[2] + sums[3] * sums[3]
    both = jnp.concatenate([sums[0], squares], axis=0)
    return silu_pair(dot_split((high_ref[layer], low_ref[layer]), both))


def edge_parts(basis, unit):
    return [basis] + [basis * unit[i : i + 1] for i in range(3)]


def pack_kernel(place_ref, position_in, species_in, ids_in, count_in, place_out, block_out, position,
                species, ids, count, sems):
    fetch([position_in, species_in, ids_in, count_in], [position, species, ids, count], sems)
    rows = [position[0, i] for i in range(3)] + [species[0].astype(F32)]
    atoms = rows[0].shape[1]
    rows = [row[:, s : s + 128] for row in rows for s in range(0, atoms, 128)]
    place_out[...] = jnp.concatenate(rows, axis=0)
    order = slot_order(ids[...], place_ref, atoms).astype(F32)
    rows += [order[:, s : s + 128] for s in range(0, order.shape[1], 128)]
    rows += [count[0, :, s : s + 128].astype(F32) for s in range(0, atoms, 128)]
    rows += [jnp.zeros((block_out.shape[0] - len(rows), 128), F32)]
    block_out[...] = jnp.concatenate(rows, axis=0)


def block_ids(block, atoms, edges):
    start = 4 * atoms // 128
    middle, end = start + edges // 128, start + edges // 128 + atoms // 128
    rows = [block[r : r + 1] for r in range(start, end)]
    ids = jnp.concatenate(rows[: middle - start], axis=1).astype(jnp.int32)
    return ids, jnp.concatenate(rows[middle - start :], axis=1)


def radial_left(radial):
    high = radial.astype(BF16).astype(F32)
    low = radial - high
    top = jnp.concatenate([high, high], axis=1)
    end = jnp.concatenate([low, jnp.zeros_like(low)], axis=1)
    return jnp.concatenate([top, end], axis=0).astype(BF16)


def put_split(value, high_ref, low_ref, *at):
    high, low = split(value)
    high_ref[at] = high
    low_ref[at] = low


def slot_order(ids, place_ref, atoms):
    cell = ids >> (atoms.bit_length() - 1) if atoms & (atoms - 1) == 0 else ids // atoms
    a = (cell * 11) >> 5
    b = cell - 3 * a
    a = jnp.where((place_ref[0, 0:1, 0:1] & 1) == 0, 2 - a, a)
    b = jnp.where((place_ref[1, 0:1, 0:1] & 1) == 0, 2 - b, b)
    return ids + (3 * a + b - cell) * atoms


def fetch(sources, targets, sems):
    copies = [
        pltpu.make_async_copy(source, target, sems.at[i])
        for i, (source, target) in enumerate(zip(sources, targets))
    ]
    for copy in copies:
        copy.start()
    for copy in copies:
        copy.wait()


def prep_first_kernel(norm, embed_in, radial_in, mixing_in, embed_out, kind_left, left_out, back_out,
                      kind_high, kind_low, mix_high, mix_low, turn_high, turn_low, embed_ref,
                      radial_ref, mixing_ref, sems):
    fetch([embed_in, radial_in, mixing_in], [embed_ref, radial_ref, mixing_ref], sems)
    embed = embed_ref[...]
    kinds = embed.shape[0]
    for path in range(2):
        radial = radial_ref[0, path] * norm
        rows = jnp.concatenate([radial * embed[s : s + 1] for s in range(kinds)], axis=0)
        kind_left[path] = stacked_left(rows)
        put_split(rows, kind_high, kind_low, path)
        radial = radial_ref[1, path] * norm
        left_out[path] = stacked_left(radial)
        back_out[path] = radial_left(radial)
    for layer in range(2):
        scalar, vector = mixing_ref[layer, 0], mixing_ref[layer, 1]
        put_split(jnp.concatenate([scalar.T, vector.T], axis=1), mix_high, mix_low, layer)
        put_split(jnp.concatenate([scalar, 2.0 * vector], axis=0), turn_high, turn_low, layer)
    embed = jnp.concatenate([embed, jnp.zeros((8 - kinds, embed.shape[1]), F32)], axis=0)
    embed_out[...] = embedding_stack(embed)


def prep_second_kernel(read_in, hidden_in, charge_in, read_ref, hidden_high, hidden_low,
                       hidden_turn_high, hidden_turn_low, charge_pair, hidden_ref, charge_ref, sems):
    fetch([read_in, hidden_in, charge_in], [read_ref, hidden_ref, charge_ref], sems)
    put_split(hidden_ref[...].T, hidden_high, hidden_low, Ellipsis)
    put_split(hidden_ref[...], hidden_turn_high, hidden_turn_low, Ellipsis)
    charge = charge_ref[...]
    high = charge.astype(BF16).astype(F32)
    charge_pair[0] = high.astype(BF16)
    charge_pair[1] = (charge - high).astype(BF16)


def hot_kernel(atoms, block_ref, hot_ref):
    ids, _ = block_ids(block_ref[...], atoms, hot_ref.shape[1])
    for start in range(0, hot_ref.shape[1], 256):
        lanes = slice(start, start + 256)
        hot_ref[:, lanes] = hot_columns(ids[:, lanes], hot_ref.shape[0])


def hot_beyond_kernel(ids_ref, near_ref, hot_ref):
    ids = ids_ref[1:2, :] - 2 * hot_ref.shape[0]
    for start in range(0, hot_ref.shape[1], 256):
        lanes = slice(start, start + 256)
        hot_ref[:, lanes] = hot_columns(ids[:, lanes], hot_ref.shape[0])


def hot_back_kernel(ids_ref, hot_ref):
    edges = ids_ref.shape[1]
    entry = lax.broadcasted_iota(jnp.int32, (128, hot_ref.shape[1]), 1).astype(F32)
    for start in range(0, edges, 128):
        row = jnp.broadcast_to(ids_ref[1:2, start : start + 128].astype(F32), (8, 128))
        column = row.T[:, 0:1]
        hot_ref[start : start + 128] = jnp.where(column == entry, 1.0, 0.0).astype(BF16)


def unfold_block(block, atoms):
    parts = atoms // 128
    rows = [block[r : r + 1] for r in range(4 * parts)]
    return [jnp.concatenate(rows[q * parts : (q + 1) * parts], axis=1) for q in range(4)]


def first_kernel(slots, place_ref, embed_ref, kind_left, mix_high, mix_low, y_pair_ref, own_ref,
                 y_beyond_ref, pair_ref, column_ref, beyond_ref, low_ref, ids_ref, basis_ref, slope_ref,
                 unit_ref, sums_ref, gate_ref):
    atoms = low_ref.shape[2]
    frame = [pair_ref, column_ref, beyond_ref]
    per_cell = atoms // 128
    places = lax.broadcasted_iota(jnp.int32, (4 * per_cell, 128), 0)
    upper = places % per_cell
    kind_of_row = places // per_cell
    to_x = jnp.where(kind_of_row == 0, cell_width, 0.0)
    to_x = jnp.where((place_ref[0] & 1) == 0, to_x, -to_x)
    to_y = jnp.where(kind_of_row == 1, cell_width, 0.0)
    to_y = jnp.where((place_ref[1] & 1) == 0, to_y, -to_y)
    for cell, block_ref in enumerate((y_pair_ref, own_ref, y_beyond_ref)):
        ids, count = block_ids(block_ref[...], atoms, slots * atoms)
        ids_ref[cell : cell + 1, :] = ids
        own = unfold_block(column_ref[cell + 1], atoms)
        step_y = to_y if cell == 1 else -to_y
        rows = []
        for a in range(3):
            for b in range(3):
                block = frame[a][SLOT_CELLS[cell][b]]
                rows.append(block + ((1 - a) * to_x + (1 - b) * step_y))
        first_cell(
            slots, atoms, ids, count, rows, places, upper, own, embed_ref, kind_left, mix_high,
            mix_low, low_ref.at[cell], basis_ref.at[cell], slope_ref.at[cell], unit_ref.at[cell],
            sums_ref.at[cell], gate_ref.at[cell],
        )


def first_cell(slots, atoms, ids, count, rows, places, upper, own, embed_ref, kind_left, mix_high,
               mix_low, low_ref, basis_ref, slope_ref, unit_ref, sums_ref, gate_ref):
    per_cell = atoms // 128
    pieces = []
    for start in range(0, ids.shape[1], 128):
        part = jnp.broadcast_to(ids[:, start : start + 128], places.shape)
        lane, half = part & 127, (part >> 7) - upper
        found = jnp.zeros(places.shape, F32)
        for cell, block in enumerate(rows):
            value = jnp.take_along_axis(block, lane, axis=1)
            found = jnp.where(half == per_cell * cell, value, found)
        total = found
        for s in range(1, per_cell):
            total = total + pltpu.roll(found, 4 * per_cell - s, 0)
        pieces.append(total)
    found = jnp.concatenate(pieces, axis=1)
    found = [found[q * per_cell : q * per_cell + 1] for q in range(4)]
    rel = [found[q] - jnp.concatenate([own[q]] * slots, axis=1) for q in range(3)]
    distance = jnp.sqrt(rel[0] * rel[0] + rel[1] * rel[1] + rel[2] * rel[2] + soften)
    inverse = 1.0 / distance
    order = (lax.broadcasted_iota(jnp.int32, (8, 1), 0) + 1).astype(F32)
    sine, cosine = sin_cos((order * (0.5 / cut_radius)) * distance)
    wave = sine / ((order * (math.pi / cut_radius)) * distance)
    live = jnp.concatenate([jnp.where(count > n, 1.0, 0.0) for n in range(slots)], axis=1)
    basis = wave * live
    basis_ref[...] = basis
    slope_ref[...] = (cosine - wave) * (inverse * live)
    kinds = found[3]
    unit = jnp.concatenate(
        [r * inverse for r in rel] + [inverse, kinds] + [jnp.zeros_like(kinds)] * 3, axis=0
    )
    unit_ref[...] = unit
    stack = embed_ref[...]
    parts = edge_parts(basis, unit)
    species = kind_left.shape[2] // 32
    by_kind = [[None] * species for _ in range(4)]
    for n in range(slots):
        lanes = slice(n * atoms, (n + 1) * atoms)
        kind = jnp.broadcast_to(kinds[:, lanes], (8, atoms))
        for k in range(species):
            match = kind == float(k)
            for part in range(4):
                term = jnp.where(match, parts[part][:, lanes], 0.0)
                old = by_kind[part][k]
                by_kind[part][k] = term if old is None else old + term
    stacks = [stacked_right(jnp.concatenate(rows, axis=0)) for rows in by_kind]
    vectors = dot(kind_left[1], jnp.concatenate(stacks[1:], axis=1))
    sums = [dot(kind_left[0], stacks[0])]
    sums += [vectors[:, i * atoms : (i + 1) * atoms] for i in range(3)]
    step, gate = mixed(sums, mix_high, mix_low, 0)
    low_ref[...] = (embedded(stack, own[3]) + step).astype(BF16)
    for part in range(3):
        sums_ref[part] = sums[part + 1]
    gate_ref[...] = gate


def hot_columns(ids, rows):
    place = lax.broadcasted_iota(jnp.int32, (rows, ids.shape[1]), 0)
    return jnp.where(ids == place, 1.0, 0.0).astype(BF16)


def second_near_kernel(slots, basis_ref, unit_ref, left_ref, hot_ref, column_ref, weight_ref,
                       near_ref):
    atoms = column_ref.shape[2]
    parts = edge_parts(basis_ref[1], unit_ref[1])
    source = jnp.concatenate([column_ref[b] for b in range(3)], axis=1)
    for n in range(slots):
        lanes = slice(n * atoms, (n + 1) * atoms)
        for part in range(4):
            weight_ref[part, :, lanes] = weights_of(left_ref, part, parts[part][:, lanes])
        near_ref[:, lanes] = dot(source, hot_ref[3 * atoms : 6 * atoms, lanes])


def second_side_kernel(slots, hot_ref, near_ref, pair_ref, out_ref):
    atoms = pair_ref.shape[2]
    source = jnp.concatenate([pair_ref[b] for b in range(3)], axis=1)
    for n in range(slots):
        lanes = slice(n * atoms, (n + 1) * atoms)
        out_ref[:, lanes] = near_ref[:, lanes] + dot(source, hot_ref[: 3 * atoms, lanes])


def second_kernel(slots, hot_ref, weight_ref, near_ref, mix_high, mix_low, charge_ref, cell_ref,
                  column_ref, beyond_ref, feature_ref, sums_ref, gate_ref, packed_ref,
                  full_charge_ref, hidden_ref):
    atoms = column_ref.shape[2]
    source = jnp.concatenate([beyond_ref[b] for b in range(3)], axis=1)
    sums = [None] * 4
    for n in range(slots):
        lanes = slice(n * atoms, (n + 1) * atoms)
        feature = near_ref[:, lanes] + dot(source, hot_ref[:, lanes])
        feature_ref[:, lanes] = feature.astype(BF16)
        for part in range(4):
            term = weight_ref[part, :, lanes] * feature
            sums[part] = term if sums[part] is None else sums[part] + term
    step, gate = mixed(sums, mix_high, mix_low, 1)
    hidden = column_ref[1].astype(F32) + step
    hidden_ref[...] = hidden
    for part in range(3):
        sums_ref[part] = sums[part + 1]
    gate_ref[...] = gate
    charge = dot_split((charge_ref[0], charge_ref[1]), hidden)
    full_charge_ref[...] = charge
    place = jnp.concatenate(unfold_block(cell_ref[2], atoms)[:3], axis=0)
    high = place.astype(BF16).astype(F32)
    rest = place - high
    middle = rest.astype(BF16).astype(F32)
    zero = jnp.zeros((packed_ref.shape[0] - charge.shape[0] - 9, atoms), F32)
    packed_ref[...] = jnp.concatenate([charge, high, middle, rest - middle, zero], axis=0).astype(
        BF16
    )


def readout_kernel(hidden_high, hidden_low, turn_high, turn_low, out_ref, hidden_ref, energy_ref,
                   slope_ref):
    hidden = hidden_ref[...]
    value, slope = silu_pair(dot_split((hidden_high[...], hidden_low[...]), hidden))
    out = out_ref[...].T
    energy_ref[...] = jnp.sum(value * out, axis=0, keepdims=True)
    slope_ref[...] = dot_split((turn_high[...], turn_low[...]), slope * out)


def message_grads(cotangent, gate_ref, sums_ref, high_ref, low_ref, layer):
    pre = cotangent * gate_ref[...]
    both = dot_split((high_ref[layer], low_ref[layer]), pre)
    half = both.shape[0] // 2
    return [both[:half]] + [both[half:] * sums_ref[i] for i in range(3)]


def radial_grad(left, value):
    high, low = split(value)
    both = dot(left, jnp.concatenate([high, low], axis=0))
    half = both.shape[0] // 2
    return both[:half] + both[half:]


def second_back_kernel(slots, scale, count, hot_ref, weight_ref, turn_high, turn_low, charge_ref,
                       sums_ref, gate_ref, full_charge_ref, energy_ref, slope_ref, *refs):
    folds, refs = refs[:count], refs[count:]
    site_ref, long_ref, cotangent_ref, grad_ref, term_ref, beyond_ref, pair_ref = refs
    atoms = gate_ref.shape[1]
    total = folds[0][...].astype(F32)
    for part in folds[1:]:
        total = total + part[...].astype(F32)
    wide = full_charge_ref.shape[0]
    potential = total[:wide] * (2.0 * scale)
    slopes = total[wide : wide + 3] + total[wide + 3 : wide + 6] + total[wide + 6 : wide + 9]
    long_ref[...] = jnp.concatenate(
        [slopes * (2.0 * scale), jnp.zeros((5, atoms), F32)], axis=0
    )
    site_ref[0] = energy_ref[...] + 0.5 * jnp.sum(
        full_charge_ref[...] * potential, axis=0, keepdims=True
    )
    high, low = split(potential)
    turned = ((0,), (0,))
    cotangent = slope_ref[...] + (
        dot(charge_ref[0], high, turned)
        + (dot(charge_ref[0], low, turned) + dot(charge_ref[1], high, turned))
    )
    cotangent_ref[...] = cotangent
    grads = message_grads(cotangent, gate_ref, sums_ref, turn_high, turn_low, 1)
    for part in range(4):
        grad_ref[part] = grads[part]
    for n in range(slots):
        lanes = slice(n * atoms, (n + 1) * atoms)
        term = weight_ref[0, :, lanes] * grads[0]
        for part in range(1, 4):
            term = term + weight_ref[part, :, lanes] * grads[part]
        term_ref[:, lanes] = term.astype(BF16)
    for b in range(3):
        start = (6 + b) * atoms
        beyond_ref[b] = dot(term_ref[...], hot_ref[:, start : start + atoms]).astype(BF16)
    for b in range(3):
        pair_ref[b] = dot(term_ref[...], hot_ref[:, b * atoms : (b + 1) * atoms]).astype(BF16)


def second_middle_kernel(hot_ref, term_ref, cotangent_ref, middle_ref):
    atoms = cotangent_ref.shape[1]
    for b in range(3):
        grad = dot(term_ref[...], hot_ref[:, (3 + b) * atoms : (4 + b) * atoms])
        middle_ref[b] = grad + cotangent_ref[...] if b == 1 else grad


def second_edge_kernel(slots, back_ref, feature_ref, grad_ref, edge_ref):
    atoms = grad_ref.shape[2]
    for n in range(slots):
        lanes = slice(n * atoms, (n + 1) * atoms)
        feature = feature_ref[:, lanes].astype(F32)
        for part in range(4):
            edge_ref[8 * part : 8 * part + 8, lanes] = radial_grad(
                back_ref[1 if part else 0], grad_ref[part] * feature
            )


def first_back_kernel(slots, ids_ref, basis_ref, slope_ref, unit_ref, kind_high, kind_low, turn_high,
                      turn_low, sums_ref, gate_ref, edge_ref, long_ref, middle_ref, from_pair,
                      from_beyond, *outs):
    sums = {(1, 2): long_ref[...]}
    for cell in range(3):
        cotangent = middle_ref[cell] + (
            from_pair[cell].astype(F32) + from_beyond[cell].astype(F32)
        )
        own, found = first_back_cell(
            slots, ids_ref[cell : cell + 1, :], basis_ref.at[cell], slope_ref.at[cell],
            unit_ref.at[cell], kind_high, kind_low, turn_high, turn_low, sums_ref.at[cell],
            gate_ref.at[cell], edge_ref if cell == 1 else None, cotangent,
        )
        terms = [((1, cell + 1), own)]
        terms += [((n // 3, SLOT_CELLS[cell][n % 3]), found[n]) for n in range(9)]
        for key, term in terms:
            sums[key] = sums[key] + term if key in sums else term
    for (x, y), total in sums.items():
        outs[x][y] = total


def first_back_cell(slots, ids, basis_ref, slope_ref, unit_ref, kind_high, kind_low, turn_high,
                    turn_low, sums_ref, gate_ref, edge_ref, cotangent):
    atoms = gate_ref.shape[1]
    pre = cotangent * gate_ref[...]
    both = dot_split((turn_high[0], turn_low[0]), pre)
    wide = both.shape[0] // 2
    grads = [both[:wide]] + [both[wide:] * sums_ref[i] for i in range(3)]
    unit = unit_ref[...]
    kinds = unit[4:5]
    by_kind = [dot_split((kind_high[0], kind_low[0]), grads[0])]
    by_kind += [dot_split((kind_high[1], kind_low[1]), grads[i]) for i in range(1, 4)]
    species = by_kind[0].shape[0] // 8
    edges = [[] for _ in range(4)]
    for n in range(slots):
        kind = jnp.broadcast_to(kinds[:, n * atoms : (n + 1) * atoms], (8, atoms))
        matches = [kind == float(k) for k in range(1, species)]
        for part in range(4):
            rows = by_kind[part]
            found = rows[:8]
            for k, match in enumerate(matches):
                found = jnp.where(match, rows[8 * k + 8 : 8 * k + 16], found)
            edges[part].append(found)
    edges = [jnp.concatenate(rows, axis=1) for rows in edges]
    if edge_ref is not None:
        edges = [edge_ref[8 * part : 8 * part + 8] + edges[part] for part in range(4)]
    basis = basis_ref[...]
    units = [unit[i : i + 1] for i in range(3)]
    inverse = unit[3:4]
    by_basis = edges[0]
    for i in range(3):
        by_basis = by_basis + edges[i + 1] * units[i]
    by_unit = [jnp.sum(edges[i + 1] * basis, axis=0, keepdims=True) * inverse for i in range(3)]
    by_distance = jnp.sum(by_basis * slope_ref[...], axis=0, keepdims=True)
    for i in range(3):
        by_distance = by_distance - by_unit[i] * units[i]
    moves = [by_unit[i] + by_distance * units[i] for i in range(3)]
    zero = jnp.zeros_like(moves[0])
    move = jnp.concatenate(moves + [zero] * 5, axis=0)
    own = -move[:, :atoms]
    for n in range(1, slots):
        own = own - move[:, n * atoms : (n + 1) * atoms]
    lane_hot = hot_columns(ids & 127, 128)
    half = ids >> 7
    high = move.astype(BF16).astype(F32)
    both = jnp.concatenate([high, move - high], axis=0)
    per_cell = atoms // 128
    rows = jnp.concatenate(
        [jnp.where(half == h, both, 0.0).astype(BF16) for h in range(9 * per_cell)], axis=0
    )
    spread = dot(rows, lane_hot, ((1,), (1,)))
    grads = []
    for cell in range(9):
        found = []
        for h in range(cell * per_cell, (cell + 1) * per_cell):
            found.append(spread[16 * h : 16 * h + 8] + spread[16 * h + 8 : 16 * h + 16])
        grads.append(jnp.concatenate(found, axis=1))
    return own, grads


def pair_counts(parts):
    total = WAVE_REACH + WAVE_REACH * (2 * WAVE_REACH + 1)
    share = -(-total // parts)
    return total, share, -(-share // 16) * 16


def pair_vectors(slot, share, part):
    side = 2 * WAVE_REACH + 1
    total = WAVE_REACH + WAVE_REACH * side
    index = slot + part.astype(F32) * share
    later = index - WAVE_REACH
    row = jnp.floor((later + 0.5) * (1.0 / side))
    first = index < WAVE_REACH
    kx = jnp.where(first, 0.0, row + 1.0)
    ky = jnp.where(first, index + 1.0, later - row * side - WAVE_REACH)
    valid = jnp.where((slot < share) & (index < total), 1.0, 0.0)
    return kx, ky, valid


def count_up(rows):
    return lax.broadcasted_iota(jnp.int32, (rows, 1), 0).astype(F32)


def green_weights(share, padded, grid, place_ref, vec_ref, weight_ref):
    grid_x, grid_y = grid
    turn = 2.0 * math.pi
    side = 2 * WAVE_REACH + 1
    top = side * side * side - 1
    vec = vec_ref[...].astype(F32) + WAVE_REACH
    code = (vec[0:1] * side + vec[1:2]) * side + vec[2:3]
    code = jnp.maximum(code, top - code)
    span = 8 * share
    row = count_up(span)
    slot = jnp.floor(row * 0.125)
    height = row - 8.0 * slot + 1.0
    flat = count_up(padded)
    slot = jnp.concatenate([slot, slot, flat], axis=0)
    kz = jnp.concatenate([height, -height, jnp.zeros_like(flat)], axis=0)
    kx, ky, valid = pair_vectors(slot, share, place_ref[0, 0:1, 0:1])
    own = ((kx + WAVE_REACH) * side + ky + WAVE_REACH) * side + kz + WAVE_REACH
    seen = jnp.zeros((own.shape[0], 128), F32)
    for start in range(0, code.shape[1], 128):
        seen = seen + jnp.where(own == code[:, start : start + 128], 1.0, 0.0)
    count = jnp.sum(seen, axis=1, keepdims=True) * valid
    sq = (
        (kx * (turn / (grid_x * cell_width))) ** 2
        + (ky * (turn / (grid_y * cell_width))) ** 2
        + (kz * (turn / box_height)) ** 2
    )
    green = jnp.exp(-smear_width * sq) / (sq + screen * screen) * count
    weight_ref[...] = jnp.broadcast_to(green, weight_ref.shape)


def basis_rows(share, ca, sa, cb, sb):
    cc, ss, sc, cs = [], [], [], []
    for p in range(share):
        c, s = ca[p : p + 1], sa[p : p + 1]
        cc.append(c * cb)
        ss.append(s * sb)
        sc.append(s * cb)
        cs.append(c * sb)
    return cc, ss, sc, cs


def unpack_rows(block):
    half = block.shape[1] // 2
    return jnp.concatenate([block[:, :half], block[:, half:]], axis=0)


def pack_rows(block):
    half = block.shape[0] // 2
    return jnp.concatenate([block[:half], block[half:]], axis=1)


def structure_kernel(share, padded, grid, wide, flip, place_ref, blocks, *refs):
    grid_x, grid_y = grid
    if flip:
        near_ref, (ca_ref, sa_ref, cb_ref, sb_ref, high_ref, low_ref, own_ref, out_ref) = (
            refs[0],
            refs[1:],
        )
        total = near_ref[...]
    else:
        ca_ref, sa_ref, cb_ref, sb_ref, high_ref, low_ref, total_ref = refs
        total = None
    col = place_ref[1, 0:1, 0:1].astype(F32) * (1.0 / grid_y)
    first = place_ref[0, 0:1, 0:1] ^ flip
    kx, ky, _ = pair_vectors(count_up(padded), share, place_ref[0, 0:1, 0:1])
    kz = count_up(8) + 1.0
    for d in range(grid_x // 2):
        block = blocks[d]
        charge = block[:wide]
        atoms = charge.shape[1]
        pieces = block[wide:].astype(F32)
        place = pieces[0:3] + (pieces[3:6] + pieces[6:9])
        row = (first ^ (2 * d)).astype(F32) * (1.0 / grid_x)
        x = place[0:1] * (1.0 / (grid_x * cell_width)) + row
        y = place[1:2] * (1.0 / (grid_y * cell_width)) + col
        sa, ca = sin_cos(kx * x + ky * y)
        sb, cb = sin_cos(kz * (place[2:3] * (1.0 / box_height)))
        lanes = pl.ds(d * atoms, atoms)
        ca_ref[:, lanes] = ca
        sa_ref[:, lanes] = sa
        cb_ref[:, lanes] = cb
        sb_ref[:, lanes] = sb
        cc, ss, sc, cs = basis_rows(share, ca, sa, cb, sb)
        high, low = split(jnp.concatenate(cc + ss + sc + cs + [ca, sa], axis=0))
        high_ref[:, lanes] = high
        low_ref[:, lanes] = low
        term = dot(high, charge, ((1,), (1,))) + dot(low, charge, ((1,), (1,)))
        total = term if total is None else total + term
    if flip:
        packed = pack_rows(total)
        own_ref[...] = packed
        out_ref[...] = packed.astype(BF16)
    else:
        total_ref[...] = total


def weighted_rows(share, padded, wide, weight_ref, parts):
    packed = parts[0][...].astype(F32)
    for part in parts[1:]:
        packed = packed + part[...].astype(F32)
    struct = unpack_rows(packed)
    span = 8 * share
    cc, ss, sc, cs = (struct[i * span : (i + 1) * span] for i in range(4))
    weight = weight_ref[:, :wide]
    plus, minus, flat = weight[:span], weight[span : 2 * span], weight[2 * span :]
    re_plus, im_plus = plus * (cc - ss), plus * (sc + cs)
    re_minus, im_minus = minus * (cc + ss), minus * (sc - cs)
    rows = jnp.concatenate(
        [
            re_plus + re_minus,
            re_minus - re_plus,
            im_plus + im_minus,
            im_plus - im_minus,
            flat * struct[4 * span : 4 * span + padded],
            flat * struct[4 * span + padded :],
        ],
        axis=0,
    )
    return rows


def fold_kernel(share, padded, grid, wide, flip, place_ref, *refs):
    grid_x, grid_y = grid
    turn = 2.0 * math.pi
    if flip:
        weight_ref, parts, refs = refs[0], refs[1 : 1 + grid_y], refs[1 + grid_y :]
        rows = weighted_rows(share, padded, wide, weight_ref, parts)
        refs, rows_ref = refs[:-1], refs[-1]
        rows_ref[...] = rows
    else:
        rows, refs = refs[0][...], refs[1:]
    ca_ref, sa_ref, cb_ref, sb_ref, high_ref, low_ref, blocks, out_ref = refs
    row_high, row_low = split(rows)
    row_pair = jnp.concatenate([row_high, row_low], axis=1)
    turned = rows.T
    t_high, t_low = split(turned)
    t_both = jnp.concatenate([t_high, t_low], axis=0)
    span = 8 * share
    kx, ky, _ = pair_vectors(count_up(padded), share, place_ref[0, 0:1, 0:1])
    kx = kx * (turn / (grid_x * cell_width))
    ky = ky * (turn / (grid_y * cell_width))
    kz = (count_up(8) + 1.0) * (turn / box_height)
    for d in range(grid_x // 2):
        charge = blocks[d][:wide]
        atoms = charge.shape[1]
        lanes = pl.ds(d * atoms, atoms)
        ca, sa, cb, sb = ca_ref[:, lanes], sa_ref[:, lanes], cb_ref[:, lanes], sb_ref[:, lanes]
        bcc, bss, bsc, bcs = basis_rows(share, ca, sa, cb, sb)
        high, low = high_ref[:, lanes], low_ref[:, lanes]
        both = dot(t_both, high)
        pot = both[:wide] + both[wide:] + dot(t_high, low)
        proj = dot(row_pair, jnp.concatenate([charge, charge], axis=0))
        by_x = jnp.zeros((8, atoms), jnp.float32)
        by_y = jnp.zeros((8, atoms), jnp.float32)
        by_z = jnp.zeros((8, atoms), jnp.float32)
        for p in range(share):
            pcc, pss, psc, pcs = (
                proj[i * span + 8 * p : i * span + 8 * p + 8] for i in range(4)
            )
            slope = bcs[p] * pss - bsc[p] * pcc + bcc[p] * psc - bss[p] * pcs
            by_x = by_x + kx[p : p + 1] * slope
            by_y = by_y + ky[p : p + 1] * slope
            by_z = by_z + (bsc[p] * pss - bcs[p] * pcc - bss[p] * psc + bcc[p] * pcs)
        flat_slope = ca * proj[4 * span + padded :] - sa * proj[4 * span : 4 * span + padded]
        grad_x = jnp.sum(by_x, axis=0, keepdims=True) + jnp.sum(kx * flat_slope, axis=0, keepdims=True)
        grad_y = jnp.sum(by_y, axis=0, keepdims=True) + jnp.sum(ky * flat_slope, axis=0, keepdims=True)
        grad_z = jnp.sum(kz * by_z, axis=0, keepdims=True)
        slopes = jnp.concatenate([grad_x, grad_y, grad_z], axis=0)
        out_ref[d] = pieced(pot, slopes, out_ref.shape[1]).astype(out_ref.dtype)


def pieced(pot, slopes, rows):
    high = slopes.astype(BF16).astype(F32)
    rest = slopes - high
    middle = rest.astype(BF16).astype(F32)
    zero = jnp.zeros((rows - pot.shape[0] - 9, pot.shape[1]), F32)
    return jnp.concatenate([pot, high, middle, rest - middle, zero], axis=0)


def unpieced(block, wide):
    slopes = block[wide : wide + 3] + (block[wide + 3 : wide + 6] + block[wide + 6 : wide + 9])
    return block[:wide], slopes


def join_kernel(wide, near_ref, far_ref, own_ref, *outs):
    for d in range(near_ref.shape[0]):
        pot, slopes = unpieced(near_ref[d], wide)
        pot_far, slopes_far = unpieced(far_ref[d].astype(F32), wide)
        block = pieced(pot + pot_far, slopes + slopes_far, near_ref.shape[1])
        if d:
            outs[d - 1][...] = block.astype(BF16)
        else:
            own_ref[...] = block


def per_device(
    positions,
    species,
    neighbours,
    counts,
    species_embed,
    radial,
    mixing,
    read_hidden,
    read_out,
    charge_map,
    wavevectors,
):
    atoms = positions.shape[3]
    slots = neighbours.shape[3]
    features, lat_width = charge_map.shape
    wave_count = wavevectors.shape[1]
    grid = lax.axis_size("gx"), lax.axis_size("gy")
    grid_x, grid_y = grid
    edges = slots * atoms
    scale = 1.0 / math.sqrt(wave_count * lat_width * atoms * grid_x * grid_y)
    place = jnp.stack([lax.axis_index("gx"), lax.axis_index("gy")]).astype(jnp.int32)
    place = jnp.broadcast_to(place[:, None, None], (2, 8, 128))
    _, share, padded = pair_counts(grid_x)
    ids = neighbours.transpose(0, 3, 1, 2).reshape(1, edges)
    cell_rows = 4 * atoms // 128
    block_total = -(-(cell_rows + (edges + atoms) // 128) // 8) * 8
    dma = pltpu.SemaphoreType.DMA
    shown = positions.transpose(0, 2, 1, 3)
    own_place, own = run(
        pack_kernel,
        [shape(cell_rows, 128), shape(block_total, 128)],
        [place, shown, species, ids, counts],
        scratch=[
            pltpu.VMEM(shown.shape, F32),
            pltpu.VMEM(species.shape, jnp.int32),
            pltpu.VMEM(ids.shape, jnp.int32),
            pltpu.VMEM(counts.shape, jnp.int32),
            dma((4,)),
        ],
        hbm=4,
        grant=60,
        name="pack",
    )
    y_pair, y_beyond = paired(own, "gy", 1), beyond(own, "gy")
    over_pair = far(own_place, "gy", True)
    over_beyond = over_pair if grid_y == 4 else far(own_place, "gy", False)
    cells = jnp.stack(
        [over_pair, y_pair[:cell_rows], own_place, y_beyond[:cell_rows], over_beyond]
    )
    cells = [paired(cells, "gx", 1), cells, beyond(cells, "gx")]

    norm = 1.0 / math.sqrt(slots)
    kind_rows = 8 * species_embed.shape[0]
    low_pair = lambda *dims: [shape(*dims, dtype=BF16)] * 2
    embed, kind_left, left, back, kind_high, kind_low, mix_high, mix_low, turn_high, turn_low = run(
        functools.partial(prep_first_kernel, norm),
        [
            shape(features, 32, dtype=BF16),
            shape(2, features, 4 * kind_rows, dtype=BF16),
            shape(2, features, 32, dtype=BF16),
            shape(2, 16, 2 * features, dtype=BF16),
        ]
        + low_pair(2, kind_rows, features)
        + low_pair(2, features, 2 * features)
        + low_pair(2, 2 * features, features),
        [species_embed, radial, mixing],
        scratch=[
            pltpu.VMEM(species_embed.shape, F32),
            pltpu.VMEM(radial.shape, F32),
            pltpu.VMEM(mixing.shape, F32),
            dma((3,)),
        ],
        hbm=3,
        name="prep_first",
    )
    (hot,) = run(
        functools.partial(hot_kernel, atoms),
        [shape(6 * atoms, edges, dtype=BF16)],
        [own],
        flops=1_000_000,
        name="hot",
    )
    read_out, hidden_high, hidden_low, hidden_turn_high, hidden_turn_low, charge_pair = run(
        prep_second_kernel,
        [shape(1, features)]
        + low_pair(features, features)
        + low_pair(features, features)
        + [shape(2, lat_width, features, dtype=BF16)],
        [read_out[None, :], read_hidden, charge_map.T],
        scratch=[
            pltpu.VMEM(read_hidden.shape, F32),
            pltpu.VMEM((lat_width, features), F32),
            dma((3,)),
        ],
        hbm=3,
        name="prep_second",
    )
    low, ids, basis, slope, unit, sums_one, gate_one = run(
        functools.partial(first_kernel, slots),
        [
            shape(3, features, atoms, dtype=BF16),
            shape(3, edges, dtype=jnp.int32),
            shape(3, 8, edges),
            shape(3, 8, edges),
            shape(3, 8, edges),
            shape(3, 3, features, atoms),
            shape(3, features, atoms),
        ],
        [place, embed, kind_left, mix_high, mix_low, y_pair, own, y_beyond] + cells,
        name="first",
    )
    hidden = [paired(low, "gx", 1), low, beyond(low, "gx")]
    edge_weights, near = run(
        functools.partial(second_near_kernel, slots),
        [shape(4, features, edges), shape(features, edges)],
        [basis, unit, left, hot, low],
        flops=2_000_000_000,
        name="second_near",
    )
    (hot_beyond,) = run(
        hot_beyond_kernel,
        [shape(3 * atoms, edges, dtype=BF16)],
        [ids, near],
        flops=1_000_000,
        name="hot_beyond",
    )
    (near,) = run(
        functools.partial(second_side_kernel, slots),
        [shape(features, edges)],
        [hot, near, hidden[0]],
        flops=1_000_000_000,
        name="second_side",
    )
    block_rows = -(-(lat_width + 9) // 16) * 16
    feature, sums_two, gate_two, packed, charge, hidden_two = run(
        functools.partial(second_kernel, slots),
        [
            shape(features, edges, dtype=BF16),
            shape(3, features, atoms),
            shape(features, atoms),
            shape(block_rows, atoms, dtype=BF16),
            shape(lat_width, atoms),
            shape(features, atoms),
        ],
        [hot_beyond, edge_weights, near, mix_high, mix_low, charge_pair, cells[1], hidden[1],
         hidden[2]],
        name="second",
    )
    energy, energy_slope = run(
        readout_kernel,
        [shape(1, atoms), shape(features, atoms)],
        [hidden_high, hidden_low, hidden_turn_high, hidden_turn_low, read_out, hidden_two],
        name="readout",
    )
    half = grid_x // 2
    near_charges = jnp.stack([packed] + [paired(packed, "gx", 2 * d) for d in range(1, half)])
    (weight,) = run(
        functools.partial(green_weights, share, padded, grid),
        [shape(16 * share + padded, 128)],
        [place, wavevectors],
        name="green",
    )
    near_charges, weight = lax.optimization_barrier((near_charges, weight))
    far_charges = paired(near_charges, "gx", 1)
    span = half * atoms
    rows = 32 * share + 2 * padded
    phase_shapes = [
        shape(padded, span),
        shape(padded, span),
        shape(8, span),
        shape(8, span),
        shape(rows, span, dtype=BF16),
        shape(rows, span, dtype=BF16),
    ]
    *near_phases, near_total = run(
        functools.partial(structure_kernel, share, padded, grid, lat_width, 0),
        phase_shapes + [shape(rows, lat_width)],
        [place, near_charges],
        flops=1_000_000_000,
        name="structure_near",
    )
    *far_phases, own_part, part = run(
        functools.partial(structure_kernel, share, padded, grid, lat_width, 1),
        phase_shapes
        + [
            shape(rows // 2, 2 * lat_width),
            shape(rows // 2, 2 * lat_width, dtype=BF16),
        ],
        [place, far_charges, near_total],
        name="structure_far",
    )
    parts = [own_part] + [paired(part, "gy", d) for d in range(1, grid_y)]
    (hot_back,) = run(
        hot_back_kernel,
        [shape(edges, 9 * atoms, dtype=BF16)],
        [ids],
        flops=2_000_000_000,
        name="hot_back",
    )
    parts, hot_back = lax.optimization_barrier((parts, hot_back))
    far_folds, wave_rows = run(
        functools.partial(fold_kernel, share, padded, grid, lat_width, 1),
        [shape(half, block_rows, atoms, dtype=BF16), shape(rows, lat_width)],
        [place, weight] + parts + far_phases + [far_charges],
        name="fold_far",
    )
    far_folds = paired(far_folds, "gx", 1)
    (near_folds,) = run(
        functools.partial(fold_kernel, share, padded, grid, lat_width, 0),
        [shape(half, block_rows, atoms)],
        [place, wave_rows] + near_phases + [near_charges],
        flops=1_000_000_000,
        name="fold_near",
    )
    folds = run(
        functools.partial(join_kernel, lat_width),
        [shape(block_rows, atoms)] + [shape(block_rows, atoms, dtype=BF16)] * (half - 1),
        [near_folds, far_folds],
        name="fold_join",
    )
    folds = [folds[0]] + [paired(folds[d], "gx", 2 * d) for d in range(1, half)]

    site, long, cotangent, grads, term, to_beyond, to_pair = run(
        functools.partial(second_back_kernel, slots, scale, half),
        [
            shape(1, 1, atoms),
            shape(8, atoms),
            shape(features, atoms),
            shape(4, features, atoms),
            shape(features, edges, dtype=BF16),
            shape(3, features, atoms, dtype=BF16),
            shape(3, features, atoms, dtype=BF16),
        ],
        [hot_back, edge_weights, turn_high, turn_low, charge_pair, sums_two, gate_two, charge,
         energy, energy_slope] + folds,
        name="second_back",
    )
    from_pair, from_beyond = paired(to_pair, "gx", 1), beyond(to_beyond, "gx")
    (middle,) = run(
        second_middle_kernel,
        [shape(3, features, atoms)],
        [hot_back, term, cotangent],
        flops=1_000_000_000,
        name="second_middle",
    )
    (edge,) = run(
        functools.partial(second_edge_kernel, slots),
        [shape(32, edges)],
        [back, feature, grads],
        flops=1_000_000_000,
        name="second_edge",
    )
    to_pair, middle, to_beyond = run(
        functools.partial(first_back_kernel, slots),
        [shape(5, 8, atoms)] * 3,
        [ids, basis, slope, unit, kind_high, kind_low, turn_high, turn_low, sums_one, gate_one, edge,
         long, middle, from_pair, from_beyond],
        name="first_back",
    )
    total = middle + paired(to_pair, "gx", 1) + beyond(to_beyond, "gx")
    if grid_y == 4:
        distant = far(total[0] + total[4], "gy", True)
    else:
        distant = far(total[0], "gy", False) + far(total[4], "gy", True)
    total = total[2] + paired(total[1], "gy", 1) + beyond(total[3], "gy") + distant
    forces = -total[None, :3, None, :]
    return (forces.transpose(0, 2, 1, 3), site)


def solution(mesh):
    in_specs = (
        P("gx", "gy", None, None),
        P("gx", "gy", None),
        P("gx", "gy", None, None),
        P("gx", "gy", None),
        P(),
        P(),
        P(),
        P(),
        P(),
        P(),
        P(),
    )
    out_specs = (P("gx", "gy", None, None), P("gx", "gy", None))
    return jax.shard_map(
        per_device, mesh=mesh, in_specs=in_specs, out_specs=out_specs, check_vma=False
    )
```

```python
import functools
import math

import jax
import jax.numpy as jnp
import numpy as np
from jax import lax
from jax.experimental import pallas as pl
from jax.experimental.pallas import tpu as pltpu
from jax.sharding import PartitionSpec as P

cell_width = 10.0
box_height = 30.0
cut_radius = 50.0
soften = 0.25
screen = 0.5
smear_width = 0.5
WAVE_REACH = 8
F32 = jnp.float32
BF16 = jnp.bfloat16


def paired(block, axis, mask):
    return lax.ppermute(block, axis, [(i ^ mask, i) for i in range(lax.axis_size(axis))])


def other_side(index, count):
    return (index + (1 if index % 2 else -1)) % count


def beyond(block, axis):
    count = lax.axis_size(axis)
    return lax.ppermute(block, axis, [(other_side(i, count), i) for i in range(count)])


def far(block, axis, over_pair):
    count = lax.axis_size(axis)
    if over_pair:
        route = [(other_side(i ^ 1, count), i) for i in range(count)]
    else:
        route = [(other_side(i, count) ^ 1, i) for i in range(count)]
    return lax.ppermute(block, axis, route)


SLOT_CELLS = ((2, 1, 0), (1, 2, 3), (4, 3, 2))


def whole(space=pltpu.VMEM):
    return pl.BlockSpec(memory_space=space)


def run(kernel, outs, args, scratch=(), hbm=0, flops=10_000_000, grant=16, name=None):
    specs = [whole()] * (len(args) - hbm) + [whole(pltpu.HBM)] * hbm
    return list(
        pl.pallas_call(
            kernel,
            out_shape=outs,
            in_specs=specs,
            out_specs=[whole() for _ in outs],
            scratch_shapes=list(scratch),
            compiler_params=pltpu.CompilerParams(vmem_limit_bytes=grant * 1024 * 1024),
            cost_estimate=pl.CostEstimate(
                flops=flops, bytes_accessed=1_000_000, transcendentals=0
            ),
            name=name,
        )(*args)
    )


def shape(*dims, dtype=F32):
    return jax.ShapeDtypeStruct(dims, dtype)


def split(value):
    high = value.astype(BF16)
    return high, (value - high.astype(F32)).astype(BF16)


def dot(left, right, contract=((1,), (0,))):
    return lax.dot_general(left, right, (contract, ((), ())), preferred_element_type=F32)


def dot3(left, right):
    left_high, left_low = split(left)
    right_high, right_low = split(right)
    return dot(left_high, right_high) + (dot(left_high, right_low) + dot(left_low, right_high))


def dot_split(left, right):
    right_high, right_low = split(right)
    return dot(left[0], right_high) + (dot(left[0], right_low) + dot(left[1], right_high))


def sin_cos(turns):
    quarter = jnp.round(turns * 4.0)
    x = (turns - quarter * 0.25) * (2.0 * math.pi)
    z = x * x
    sine = ((-1.9515295891e-4 * z + 8.3321608736e-3) * z - 1.6666654611e-1) * (z * x) + x
    cosine = (2.443315711809948e-5 * z - 1.388731625493765e-3) * z + 4.166664568298827e-2
    cosine = cosine * (z * z) - 0.5 * z + 1.0
    k = quarter.astype(jnp.int32) & 3
    odd = (k & 1) == 1
    by_sine = jnp.where(odd, cosine, sine)
    by_cosine = jnp.where(odd, sine, cosine)
    return (
        jnp.where(k >= 2, -by_sine, by_sine),
        jnp.where((k == 1) | (k == 2), -by_cosine, by_cosine),
    )


def stacked_left(value):
    high = value.astype(BF16).astype(F32)
    rows = jnp.concatenate([high, high, value - high, jnp.zeros_like(high)], axis=0)
    return rows.T.astype(BF16)


def stacked_right(value):
    high = value.astype(BF16).astype(F32)
    return jnp.concatenate([high, value - high, high, jnp.zeros_like(high)], axis=0).astype(BF16)


def silu_pair(value):
    gate = 1.0 / (1.0 + jnp.exp(-value))
    return value * gate, gate * (1.0 + value * (1.0 - gate))


def onehot_kinds(kinds, rows):
    levels = lax.broadcasted_iota(jnp.int32, (rows, kinds.shape[1]), 0).astype(F32)
    return jnp.where(kinds == levels, 1.0, 0.0)


def embedding_stack(embed):
    high = embed.astype(BF16).astype(F32)
    rest = embed - high
    middle = rest.astype(BF16).astype(F32)
    rows = jnp.concatenate([high, middle, rest - middle, jnp.zeros_like(high)], axis=0)
    return rows.T.astype(BF16)


def embedded(stack, kinds):
    hot = onehot_kinds(kinds, 8)
    return dot(stack, jnp.concatenate([hot, hot, hot, jnp.zeros_like(hot)], axis=0).astype(BF16))


def weights_of(stack_ref, part, rows):
    return dot(stack_ref[1 if part else 0], stacked_right(rows))


def mixed(sums, high_ref, low_ref, layer):
    squares = sums[1] * sums[1] + sums[2] * sums[2] + sums[3] * sums[3]
    both = jnp.concatenate([sums[0], squares], axis=0)
    return silu_pair(dot_split((high_ref[layer], low_ref[layer]), both))


def edge_parts(basis, unit):
    return [basis] + [basis * unit[i : i + 1] for i in range(3)]


def pack_kernel(place_ref, position_ref, species_ref, out_ref):
    rows = [position_ref[0, i] for i in range(3)] + [species_ref[0].astype(F32)]
    atoms = rows[0].shape[1]
    out_ref[...] = jnp.concatenate(
        [row[:, s : s + 128] for row in rows for s in range(0, atoms, 128)], axis=0
    )


def pack_more_kernel(place_ref, ids_ref, count_ref, first_ref, out_ref):
    atoms = count_ref.shape[2]
    order = slot_order(ids_ref[...], place_ref, atoms).astype(F32)
    rows = [first_ref[...]]
    rows += [order[:, s : s + 128] for s in range(0, order.shape[1], 128)]
    rows += [count_ref[0, :, s : s + 128].astype(F32) for s in range(0, atoms, 128)]
    missing = out_ref.shape[0] - sum(row.shape[0] for row in rows)
    out_ref[...] = jnp.concatenate(rows + [jnp.zeros((missing, 128), F32)], axis=0)


def block_ids(block, atoms, edges):
    start = 4 * atoms // 128
    middle, end = start + edges // 128, start + edges // 128 + atoms // 128
    rows = [block[r : r + 1] for r in range(start, end)]
    ids = jnp.concatenate(rows[: middle - start], axis=1).astype(jnp.int32)
    return ids, jnp.concatenate(rows[middle - start :], axis=1)


def radial_left(radial):
    high = radial.astype(BF16).astype(F32)
    low = radial - high
    top = jnp.concatenate([high, high], axis=1)
    end = jnp.concatenate([low, jnp.zeros_like(low)], axis=1)
    return jnp.concatenate([top, end], axis=0).astype(BF16)


def put_split(value, high_ref, low_ref, *at):
    high, low = split(value)
    high_ref[at] = high
    low_ref[at] = low


def slot_order(ids, place_ref, atoms):
    cell = ids >> (atoms.bit_length() - 1) if atoms & (atoms - 1) == 0 else ids // atoms
    a = (cell * 11) >> 5
    b = cell - 3 * a
    a = jnp.where((place_ref[0, 0:1, 0:1] & 1) == 0, 2 - a, a)
    b = jnp.where((place_ref[1, 0:1, 0:1] & 1) == 0, 2 - b, b)
    return ids + (3 * a + b - cell) * atoms


def fetch(sources, targets, sems):
    copies = [
        pltpu.make_async_copy(source, target, sems.at[i])
        for i, (source, target) in enumerate(zip(sources, targets))
    ]
    for copy in copies:
        copy.start()
    for copy in copies:
        copy.wait()


def prep_first_kernel(norm, embed_in, radial_in, mixing_in, embed_out, kind_left, left_out, back_out,
                      kind_high, kind_low, mix_high, mix_low, turn_high, turn_low, embed_ref,
                      radial_ref, mixing_ref, sems):
    fetch([embed_in, radial_in, mixing_in], [embed_ref, radial_ref, mixing_ref], sems)
    embed = embed_ref[...]
    kinds = embed.shape[0]
    for path in range(2):
        radial = radial_ref[0, path] * norm
        rows = jnp.concatenate([radial * embed[s : s + 1] for s in range(kinds)], axis=0)
        kind_left[path] = stacked_left(rows)
        put_split(rows, kind_high, kind_low, path)
        radial = radial_ref[1, path] * norm
        left_out[path] = stacked_left(radial)
        back_out[path] = radial_left(radial)
    for layer in range(2):
        scalar, vector = mixing_ref[layer, 0], mixing_ref[layer, 1]
        put_split(jnp.concatenate([scalar.T, vector.T], axis=1), mix_high, mix_low, layer)
        put_split(jnp.concatenate([scalar, 2.0 * vector], axis=0), turn_high, turn_low, layer)
    embed = jnp.concatenate([embed, jnp.zeros((8 - kinds, embed.shape[1]), F32)], axis=0)
    embed_out[...] = embedding_stack(embed)


def prep_second_kernel(read_in, hidden_in, charge_in, read_ref, hidden_high, hidden_low,
                       hidden_turn_high, hidden_turn_low, charge_pair, hidden_ref, charge_ref, sems):
    fetch([read_in, hidden_in, charge_in], [read_ref, hidden_ref, charge_ref], sems)
    put_split(hidden_ref[...].T, hidden_high, hidden_low, Ellipsis)
    put_split(hidden_ref[...], hidden_turn_high, hidden_turn_low, Ellipsis)
    charge = charge_ref[...]
    high = charge.astype(BF16).astype(F32)
    charge_pair[0] = high.astype(BF16)
    charge_pair[1] = (charge - high).astype(BF16)


def hot_beyond_kernel(ids_ref, near_ref, hot_ref):
    ids = ids_ref[1:2, :] - 2 * hot_ref.shape[0]
    for start in range(0, hot_ref.shape[1], 256):
        lanes = slice(start, start + 256)
        hot_ref[:, lanes] = hot_columns(ids[:, lanes], hot_ref.shape[0])


def hot_back_kernel(ids_ref, hot_ref):
    edges = ids_ref.shape[1]
    entry = lax.broadcasted_iota(jnp.int32, (128, hot_ref.shape[1]), 1).astype(F32)
    for start in range(0, edges, 128):
        row = jnp.broadcast_to(ids_ref[1:2, start : start + 128].astype(F32), (8, 128))
        column = row.T[:, 0:1]
        hot_ref[start : start + 128] = jnp.where(column == entry, 1.0, 0.0).astype(BF16)


def unfold_block(block, atoms):
    parts = atoms // 128
    rows = [block[r : r + 1] for r in range(4 * parts)]
    return [jnp.concatenate(rows[q * parts : (q + 1) * parts], axis=1) for q in range(4)]


def first_kernel(slots, place_ref, embed_ref, kind_left, mix_high, mix_low, y_pair_ref, own_ref,
                 y_beyond_ref, pair_ref, column_ref, beyond_ref, low_ref, ids_ref, basis_ref, slope_ref,
                 unit_ref, sums_ref, gate_ref):
    atoms = low_ref.shape[2]
    frame = [pair_ref, column_ref, beyond_ref]
    per_cell = atoms // 128
    places = lax.broadcasted_iota(jnp.int32, (4 * per_cell, 128), 0)
    upper = places % per_cell
    kind_of_row = places // per_cell
    to_x = jnp.where(kind_of_row == 0, cell_width, 0.0)
    to_x = jnp.where((place_ref[0] & 1) == 0, to_x, -to_x)
    to_y = jnp.where(kind_of_row == 1, cell_width, 0.0)
    to_y = jnp.where((place_ref[1] & 1) == 0, to_y, -to_y)
    for cell, block_ref in enumerate((y_pair_ref, own_ref, y_beyond_ref)):
        ids, count = block_ids(block_ref[...], atoms, slots * atoms)
        ids_ref[cell : cell + 1, :] = ids
        own = unfold_block(column_ref[cell + 1], atoms)
        step_y = to_y if cell == 1 else -to_y
        rows = []
        for a in range(3):
            for b in range(3):
                block = frame[a][SLOT_CELLS[cell][b]]
                rows.append(block + ((1 - a) * to_x + (1 - b) * step_y))
        first_cell(
            slots, atoms, ids, count, rows, places, upper, own, embed_ref, kind_left, mix_high,
            mix_low, low_ref.at[cell], basis_ref.at[cell], slope_ref.at[cell], unit_ref.at[cell],
            sums_ref.at[cell], gate_ref.at[cell],
        )


def first_cell(slots, atoms, ids, count, rows, places, upper, own, embed_ref, kind_left, mix_high,
               mix_low, low_ref, basis_ref, slope_ref, unit_ref, sums_ref, gate_ref):
    per_cell = atoms // 128
    pieces = []
    for start in range(0, ids.shape[1], 128):
        part = jnp.broadcast_to(ids[:, start : start + 128], places.shape)
        lane, half = part & 127, (part >> 7) - upper
        found = jnp.zeros(places.shape, F32)
        for cell, block in enumerate(rows):
            value = jnp.take_along_axis(block, lane, axis=1)
            found = jnp.where(half == per_cell * cell, value, found)
        total = found
        for s in range(1, per_cell):
            total = total + pltpu.roll(found, 4 * per_cell - s, 0)
        pieces.append(total)
    found = jnp.concatenate(pieces, axis=1)
    found = [found[q * per_cell : q * per_cell + 1] for q in range(4)]
    rel = [found[q] - jnp.concatenate([own[q]] * slots, axis=1) for q in range(3)]
    distance = jnp.sqrt(rel[0] * rel[0] + rel[1] * rel[1] + rel[2] * rel[2] + soften)
    inverse = 1.0 / distance
    order = (lax.broadcasted_iota(jnp.int32, (8, 1), 0) + 1).astype(F32)
    sine, cosine = sin_cos((order * (0.5 / cut_radius)) * distance)
    wave = sine / ((order * (math.pi / cut_radius)) * distance)
    live = jnp.concatenate([jnp.where(count > n, 1.0, 0.0) for n in range(slots)], axis=1)
    basis = wave * live
    basis_ref[...] = basis
    slope_ref[...] = (cosine - wave) * (inverse * live)
    kinds = found[3]
    unit = jnp.concatenate(
        [r * inverse for r in rel] + [inverse, kinds] + [jnp.zeros_like(kinds)] * 3, axis=0
    )
    unit_ref[...] = unit
    stack = embed_ref[...]
    parts = edge_parts(basis, unit)
    species = kind_left.shape[2] // 32
    by_kind = [[None] * species for _ in range(4)]
    for n in range(slots):
        lanes = slice(n * atoms, (n + 1) * atoms)
        kind = jnp.broadcast_to(kinds[:, lanes], (8, atoms))
        for k in range(species):
            match = kind == float(k)
            for part in range(4):
                term = jnp.where(match, parts[part][:, lanes], 0.0)
                old = by_kind[part][k]
                by_kind[part][k] = term if old is None else old + term
    stacks = [stacked_right(jnp.concatenate(rows, axis=0)) for rows in by_kind]
    vectors = dot(kind_left[1], jnp.concatenate(stacks[1:], axis=1))
    sums = [dot(kind_left[0], stacks[0])]
    sums += [vectors[:, i * atoms : (i + 1) * atoms] for i in range(3)]
    step, gate = mixed(sums, mix_high, mix_low, 0)
    low_ref[...] = (embedded(stack, own[3]) + step).astype(BF16)
    for part in range(3):
        sums_ref[part] = sums[part + 1]
    gate_ref[...] = gate


def hot_columns(ids, rows):
    place = lax.broadcasted_iota(jnp.int32, (rows, ids.shape[1]), 0)
    return jnp.where(ids == place, 1.0, 0.0).astype(BF16)


def second_near_kernel(slots, ids_ref, basis_ref, unit_ref, left_ref, column_ref, weight_ref,
                       near_ref):
    atoms = column_ref.shape[2]
    parts = edge_parts(basis_ref[1], unit_ref[1])
    source = jnp.concatenate([column_ref[b] for b in range(3)], axis=1)
    for n in range(slots):
        lanes = slice(n * atoms, (n + 1) * atoms)
        for part in range(4):
            weight_ref[part, :, lanes] = weights_of(left_ref, part, parts[part][:, lanes])
        ids = ids_ref[1:2, lanes] - 3 * atoms
        near_ref[:, lanes] = dot(source, hot_columns(ids, 3 * atoms))


def second_side_kernel(slots, ids_ref, near_ref, pair_ref, out_ref):
    atoms = pair_ref.shape[2]
    source = jnp.concatenate([pair_ref[b] for b in range(3)], axis=1)
    for n in range(slots):
        lanes = slice(n * atoms, (n + 1) * atoms)
        hot = hot_columns(ids_ref[1:2, lanes], 3 * atoms)
        out_ref[:, lanes] = near_ref[:, lanes] + dot(source, hot)


def second_kernel(slots, hot_ref, weight_ref, near_ref, mix_high, mix_low, charge_ref, cell_ref,
                  column_ref, beyond_ref, feature_ref, sums_ref, gate_ref, packed_ref,
                  full_charge_ref, hidden_ref):
    atoms = column_ref.shape[2]
    source = jnp.concatenate([beyond_ref[b] for b in range(3)], axis=1)
    sums = [None] * 4
    for n in range(slots):
        lanes = slice(n * atoms, (n + 1) * atoms)
        feature = near_ref[:, lanes] + dot(source, hot_ref[:, lanes])
        feature_ref[:, lanes] = feature.astype(BF16)
        for part in range(4):
            term = weight_ref[part, :, lanes] * feature
            sums[part] = term if sums[part] is None else sums[part] + term
    step, gate = mixed(sums, mix_high, mix_low, 1)
    hidden = column_ref[1].astype(F32) + step
    hidden_ref[...] = hidden
    for part in range(3):
        sums_ref[part] = sums[part + 1]
    gate_ref[...] = gate
    charge = dot_split((charge_ref[0], charge_ref[1]), hidden)
    full_charge_ref[...] = charge
    place = jnp.concatenate(unfold_block(cell_ref[2], atoms)[:3], axis=0)
    high = place.astype(BF16).astype(F32)
    rest = place - high
    middle = rest.astype(BF16).astype(F32)
    zero = jnp.zeros((packed_ref.shape[0] - charge.shape[0] - 9, atoms), F32)
    packed_ref[...] = jnp.concatenate([charge, high, middle, rest - middle, zero], axis=0).astype(
        BF16
    )


def readout_kernel(hidden_high, hidden_low, turn_high, turn_low, out_ref, hidden_ref, energy_ref,
                   slope_ref):
    hidden = hidden_ref[...]
    value, slope = silu_pair(dot_split((hidden_high[...], hidden_low[...]), hidden))
    out = out_ref[...].T
    energy_ref[...] = jnp.sum(value * out, axis=0, keepdims=True)
    slope_ref[...] = dot_split((turn_high[...], turn_low[...]), slope * out)


def message_grads(cotangent, gate_ref, sums_ref, high_ref, low_ref, layer):
    pre = cotangent * gate_ref[...]
    both = dot_split((high_ref[layer], low_ref[layer]), pre)
    half = both.shape[0] // 2
    return [both[:half]] + [both[half:] * sums_ref[i] for i in range(3)]


def radial_grad(left, value):
    high, low = split(value)
    both = dot(left, jnp.concatenate([high, low], axis=0))
    half = both.shape[0] // 2
    return both[:half] + both[half:]


def second_back_kernel(slots, scale, count, hot_ref, weight_ref, turn_high, turn_low, charge_ref,
                       sums_ref, gate_ref, full_charge_ref, energy_ref, slope_ref, *refs):
    folds, refs = refs[:count], refs[count:]
    site_ref, long_ref, cotangent_ref, grad_ref, term_ref, beyond_ref, pair_ref = refs
    atoms = gate_ref.shape[1]
    total = folds[0][...].astype(F32)
    for part in folds[1:]:
        total = total + part[...].astype(F32)
    wide = full_charge_ref.shape[0]
    potential = total[:wide] * (2.0 * scale)
    slopes = total[wide : wide + 3] + total[wide + 3 : wide + 6] + total[wide + 6 : wide + 9]
    long_ref[...] = jnp.concatenate(
        [slopes * (2.0 * scale), jnp.zeros((5, atoms), F32)], axis=0
    )
    site_ref[0] = energy_ref[...] + 0.5 * jnp.sum(
        full_charge_ref[...] * potential, axis=0, keepdims=True
    )
    high, low = split(potential)
    turned = ((0,), (0,))
    cotangent = slope_ref[...] + (
        dot(charge_ref[0], high, turned)
        + (dot(charge_ref[0], low, turned) + dot(charge_ref[1], high, turned))
    )
    cotangent_ref[...] = cotangent
    grads = message_grads(cotangent, gate_ref, sums_ref, turn_high, turn_low, 1)
    for part in range(4):
        grad_ref[part] = grads[part]
    for n in range(slots):
        lanes = slice(n * atoms, (n + 1) * atoms)
        term = weight_ref[0, :, lanes] * grads[0]
        for part in range(1, 4):
            term = term + weight_ref[part, :, lanes] * grads[part]
        term_ref[:, lanes] = term.astype(BF16)
    for b in range(3):
        start = (6 + b) * atoms
        beyond_ref[b] = dot(term_ref[...], hot_ref[:, start : start + atoms]).astype(BF16)
    for b in range(3):
        pair_ref[b] = dot(term_ref[...], hot_ref[:, b * atoms : (b + 1) * atoms]).astype(BF16)


def second_middle_kernel(hot_ref, term_ref, cotangent_ref, middle_ref):
    atoms = cotangent_ref.shape[1]
    for b in range(3):
        grad = dot(term_ref[...], hot_ref[:, (3 + b) * atoms : (4 + b) * atoms])
        middle_ref[b] = grad + cotangent_ref[...] if b == 1 else grad


def second_edge_kernel(slots, back_ref, feature_ref, grad_ref, edge_ref):
    atoms = grad_ref.shape[2]
    for n in range(slots):
        lanes = slice(n * atoms, (n + 1) * atoms)
        feature = feature_ref[:, lanes].astype(F32)
        for part in range(4):
            edge_ref[8 * part : 8 * part + 8, lanes] = radial_grad(
                back_ref[1 if part else 0], grad_ref[part] * feature
            )


def first_back_kernel(slots, ids_ref, basis_ref, slope_ref, unit_ref, kind_high, kind_low, turn_high,
                      turn_low, sums_ref, gate_ref, edge_ref, long_ref, middle_ref, from_pair,
                      from_beyond, *outs):
    sums = {(1, 2): long_ref[...]}
    for cell in range(3):
        cotangent = middle_ref[cell] + (
            from_pair[cell].astype(F32) + from_beyond[cell].astype(F32)
        )
        own, found = first_back_cell(
            slots, ids_ref[cell : cell + 1, :], basis_ref.at[cell], slope_ref.at[cell],
            unit_ref.at[cell], kind_high, kind_low, turn_high, turn_low, sums_ref.at[cell],
            gate_ref.at[cell], edge_ref if cell == 1 else None, cotangent,
        )
        terms = [((1, cell + 1), own)]
        terms += [((n // 3, SLOT_CELLS[cell][n % 3]), found[n]) for n in range(9)]
        for key, term in terms:
            sums[key] = sums[key] + term if key in sums else term
    for (x, y), total in sums.items():
        outs[x][y] = total


def first_back_cell(slots, ids, basis_ref, slope_ref, unit_ref, kind_high, kind_low, turn_high,
                    turn_low, sums_ref, gate_ref, edge_ref, cotangent):
    atoms = gate_ref.shape[1]
    pre = cotangent * gate_ref[...]
    both = dot_split((turn_high[0], turn_low[0]), pre)
    wide = both.shape[0] // 2
    grads = [both[:wide]] + [both[wide:] * sums_ref[i] for i in range(3)]
    unit = unit_ref[...]
    kinds = unit[4:5]
    by_kind = [dot_split((kind_high[0], kind_low[0]), grads[0])]
    by_kind += [dot_split((kind_high[1], kind_low[1]), grads[i]) for i in range(1, 4)]
    species = by_kind[0].shape[0] // 8
    edges = [[] for _ in range(4)]
    for n in range(slots):
        kind = jnp.broadcast_to(kinds[:, n * atoms : (n + 1) * atoms], (8, atoms))
        matches = [kind == float(k) for k in range(1, species)]
        for part in range(4):
            rows = by_kind[part]
            found = rows[:8]
            for k, match in enumerate(matches):
                found = jnp.where(match, rows[8 * k + 8 : 8 * k + 16], found)
            edges[part].append(found)
    edges = [jnp.concatenate(rows, axis=1) for rows in edges]
    if edge_ref is not None:
        edges = [edge_ref[8 * part : 8 * part + 8] + edges[part] for part in range(4)]
    basis = basis_ref[...]
    units = [unit[i : i + 1] for i in range(3)]
    inverse = unit[3:4]
    by_basis = edges[0]
    for i in range(3):
        by_basis = by_basis + edges[i + 1] * units[i]
    by_unit = [jnp.sum(edges[i + 1] * basis, axis=0, keepdims=True) * inverse for i in range(3)]
    by_distance = jnp.sum(by_basis * slope_ref[...], axis=0, keepdims=True)
    for i in range(3):
        by_distance = by_distance - by_unit[i] * units[i]
    moves = [by_unit[i] + by_distance * units[i] for i in range(3)]
    zero = jnp.zeros_like(moves[0])
    move = jnp.concatenate(moves + [zero] * 5, axis=0)
    own = -move[:, :atoms]
    for n in range(1, slots):
        own = own - move[:, n * atoms : (n + 1) * atoms]
    lane_hot = hot_columns(ids & 127, 128)
    half = ids >> 7
    high = move.astype(BF16).astype(F32)
    both = jnp.concatenate([high, move - high], axis=0)
    per_cell = atoms // 128
    rows = jnp.concatenate(
        [jnp.where(half == h, both, 0.0).astype(BF16) for h in range(9 * per_cell)], axis=0
    )
    spread = dot(rows, lane_hot, ((1,), (1,)))
    grads = []
    for cell in range(9):
        found = []
        for h in range(cell * per_cell, (cell + 1) * per_cell):
            found.append(spread[16 * h : 16 * h + 8] + spread[16 * h + 8 : 16 * h + 16])
        grads.append(jnp.concatenate(found, axis=1))
    return own, grads


def pair_counts(parts):
    total = WAVE_REACH + WAVE_REACH * (2 * WAVE_REACH + 1)
    share = -(-total // parts)
    return total, share, -(-share // 16) * 16


def pair_vectors(slot, share, part):
    side = 2 * WAVE_REACH + 1
    total = WAVE_REACH + WAVE_REACH * side
    index = slot + part.astype(F32) * share
    later = index - WAVE_REACH
    row = jnp.floor((later + 0.5) * (1.0 / side))
    first = index < WAVE_REACH
    kx = jnp.where(first, 0.0, row + 1.0)
    ky = jnp.where(first, index + 1.0, later - row * side - WAVE_REACH)
    valid = jnp.where((slot < share) & (index < total), 1.0, 0.0)
    return kx, ky, valid


def count_up(rows):
    return lax.broadcasted_iota(jnp.int32, (rows, 1), 0).astype(F32)


def green_weights(share, padded, grid, place_ref, vec_ref, weight_ref):
    grid_x, grid_y = grid
    turn = 2.0 * math.pi
    side = 2 * WAVE_REACH + 1
    top = side * side * side - 1
    vec = vec_ref[...].astype(F32) + WAVE_REACH
    code = (vec[0:1] * side + vec[1:2]) * side + vec[2:3]
    code = jnp.maximum(code, top - code)
    span = 8 * share
    row = count_up(span)
    slot = jnp.floor(row * 0.125)
    height = row - 8.0 * slot + 1.0
    flat = count_up(padded)
    slot = jnp.concatenate([slot, slot, flat], axis=0)
    kz = jnp.concatenate([height, -height, jnp.zeros_like(flat)], axis=0)
    kx, ky, valid = pair_vectors(slot, share, place_ref[0, 0:1, 0:1])
    own = ((kx + WAVE_REACH) * side + ky + WAVE_REACH) * side + kz + WAVE_REACH
    seen = jnp.zeros((own.shape[0], 128), F32)
    for start in range(0, code.shape[1], 128):
        seen = seen + jnp.where(own == code[:, start : start + 128], 1.0, 0.0)
    count = jnp.sum(seen, axis=1, keepdims=True) * valid
    sq = (
        (kx * (turn / (grid_x * cell_width))) ** 2
        + (ky * (turn / (grid_y * cell_width))) ** 2
        + (kz * (turn / box_height)) ** 2
    )
    green = jnp.exp(-smear_width * sq) / (sq + screen * screen) * count
    weight_ref[...] = jnp.broadcast_to(green, weight_ref.shape)


def basis_rows(share, ca, sa, cb, sb):
    cc, ss, sc, cs = [], [], [], []
    for p in range(share):
        c, s = ca[p : p + 1], sa[p : p + 1]
        cc.append(c * cb)
        ss.append(s * sb)
        sc.append(s * cb)
        cs.append(c * sb)
    return cc, ss, sc, cs


def unpack_rows(block):
    half = block.shape[1] // 2
    return jnp.concatenate([block[:, :half], block[:, half:]], axis=0)


def pack_rows(block):
    half = block.shape[0] // 2
    return jnp.concatenate([block[:half], block[half:]], axis=1)


def structure_kernel(share, padded, grid, wide, flip, place_ref, blocks, *refs):
    grid_x, grid_y = grid
    if flip:
        near_ref, (ca_ref, sa_ref, cb_ref, sb_ref, high_ref, low_ref, own_ref, out_ref) = (
            refs[0],
            refs[1:],
        )
        total = near_ref[...]
    else:
        ca_ref, sa_ref, cb_ref, sb_ref, high_ref, low_ref, total_ref = refs
        total = None
    col = place_ref[1, 0:1, 0:1].astype(F32) * (1.0 / grid_y)
    first = place_ref[0, 0:1, 0:1] ^ flip
    kx, ky, _ = pair_vectors(count_up(padded), share, place_ref[0, 0:1, 0:1])
    kz = count_up(8) + 1.0
    for d in range(grid_x // 2):
        block = blocks[d]
        charge = block[:wide]
        atoms = charge.shape[1]
        pieces = block[wide:].astype(F32)
        place = pieces[0:3] + (pieces[3:6] + pieces[6:9])
        row = (first ^ (2 * d)).astype(F32) * (1.0 / grid_x)
        x = place[0:1] * (1.0 / (grid_x * cell_width)) + row
        y = place[1:2] * (1.0 / (grid_y * cell_width)) + col
        sa, ca = sin_cos(kx * x + ky * y)
        sb, cb = sin_cos(kz * (place[2:3] * (1.0 / box_height)))
        lanes = pl.ds(d * atoms, atoms)
        ca_ref[:, lanes] = ca
        sa_ref[:, lanes] = sa
        cb_ref[:, lanes] = cb
        sb_ref[:, lanes] = sb
        cc, ss, sc, cs = basis_rows(share, ca, sa, cb, sb)
        high, low = split(jnp.concatenate(cc + ss + sc + cs + [ca, sa], axis=0))
        high_ref[:, lanes] = high
        low_ref[:, lanes] = low
        term = dot(high, charge, ((1,), (1,))) + dot(low, charge, ((1,), (1,)))
        total = term if total is None else total + term
    if flip:
        packed = pack_rows(total)
        own_ref[...] = packed
        out_ref[...] = packed.astype(BF16)
    else:
        total_ref[...] = total


def weighted_rows(share, padded, wide, weight_ref, parts):
    packed = parts[0][...].astype(F32)
    for part in parts[1:]:
        packed = packed + part[...].astype(F32)
    struct = unpack_rows(packed)
    span = 8 * share
    cc, ss, sc, cs = (struct[i * span : (i + 1) * span] for i in range(4))
    weight = weight_ref[:, :wide]
    plus, minus, flat = weight[:span], weight[span : 2 * span], weight[2 * span :]
    re_plus, im_plus = plus * (cc - ss), plus * (sc + cs)
    re_minus, im_minus = minus * (cc + ss), minus * (sc - cs)
    rows = jnp.concatenate(
        [
            re_plus + re_minus,
            re_minus - re_plus,
            im_plus + im_minus,
            im_plus - im_minus,
            flat * struct[4 * span : 4 * span + padded],
            flat * struct[4 * span + padded :],
        ],
        axis=0,
    )
    return rows


def fold_kernel(share, padded, grid, wide, flip, place_ref, *refs):
    grid_x, grid_y = grid
    turn = 2.0 * math.pi
    if flip:
        weight_ref, parts, refs = refs[0], refs[1 : 1 + grid_y], refs[1 + grid_y :]
        rows = weighted_rows(share, padded, wide, weight_ref, parts)
        refs, rows_ref = refs[:-1], refs[-1]
        rows_ref[...] = rows
    else:
        rows, refs = refs[0][...], refs[1:]
    ca_ref, sa_ref, cb_ref, sb_ref, high_ref, low_ref, blocks, out_ref = refs
    row_high, row_low = split(rows)
    row_pair = jnp.concatenate([row_high, row_low], axis=1)
    turned = rows.T
    t_high, t_low = split(turned)
    t_both = jnp.concatenate([t_high, t_low], axis=0)
    span = 8 * share
    kx, ky, _ = pair_vectors(count_up(padded), share, place_ref[0, 0:1, 0:1])
    kx = kx * (turn / (grid_x * cell_width))
    ky = ky * (turn / (grid_y * cell_width))
    kz = (count_up(8) + 1.0) * (turn / box_height)
    for d in range(grid_x // 2):
        charge = blocks[d][:wide]
        atoms = charge.shape[1]
        lanes = pl.ds(d * atoms, atoms)
        ca, sa, cb, sb = ca_ref[:, lanes], sa_ref[:, lanes], cb_ref[:, lanes], sb_ref[:, lanes]
        bcc, bss, bsc, bcs = basis_rows(share, ca, sa, cb, sb)
        high, low = high_ref[:, lanes], low_ref[:, lanes]
        both = dot(t_both, high)
        pot = both[:wide] + both[wide:] + dot(t_high, low)
        proj = dot(row_pair, jnp.concatenate([charge, charge], axis=0))
        by_x = jnp.zeros((8, atoms), jnp.float32)
        by_y = jnp.zeros((8, atoms), jnp.float32)
        by_z = jnp.zeros((8, atoms), jnp.float32)
        for p in range(share):
            pcc, pss, psc, pcs = (
                proj[i * span + 8 * p : i * span + 8 * p + 8] for i in range(4)
            )
            slope = bcs[p] * pss - bsc[p] * pcc + bcc[p] * psc - bss[p] * pcs
            by_x = by_x + kx[p : p + 1] * slope
            by_y = by_y + ky[p : p + 1] * slope
            by_z = by_z + (bsc[p] * pss - bcs[p] * pcc - bss[p] * psc + bcc[p] * pcs)
        flat_slope = ca * proj[4 * span + padded :] - sa * proj[4 * span : 4 * span + padded]
        grad_x = jnp.sum(by_x, axis=0, keepdims=True) + jnp.sum(kx * flat_slope, axis=0, keepdims=True)
        grad_y = jnp.sum(by_y, axis=0, keepdims=True) + jnp.sum(ky * flat_slope, axis=0, keepdims=True)
        grad_z = jnp.sum(kz * by_z, axis=0, keepdims=True)
        slopes = jnp.concatenate([grad_x, grad_y, grad_z], axis=0)
        out_ref[d] = pieced(pot, slopes, out_ref.shape[1]).astype(out_ref.dtype)


def pieced(pot, slopes, rows):
    high = slopes.astype(BF16).astype(F32)
    rest = slopes - high
    middle = rest.astype(BF16).astype(F32)
    zero = jnp.zeros((rows - pot.shape[0] - 9, pot.shape[1]), F32)
    return jnp.concatenate([pot, high, middle, rest - middle, zero], axis=0)


def unpieced(block, wide):
    slopes = block[wide : wide + 3] + (block[wide + 3 : wide + 6] + block[wide + 6 : wide + 9])
    return block[:wide], slopes


def join_kernel(wide, near_ref, far_ref, own_ref, *outs):
    for d in range(near_ref.shape[0]):
        pot, slopes = unpieced(near_ref[d], wide)
        pot_far, slopes_far = unpieced(far_ref[d].astype(F32), wide)
        block = pieced(pot + pot_far, slopes + slopes_far, near_ref.shape[1])
        if d:
            outs[d - 1][...] = block.astype(BF16)
        else:
            own_ref[...] = block


def per_device(
    positions,
    species,
    neighbours,
    counts,
    species_embed,
    radial,
    mixing,
    read_hidden,
    read_out,
    charge_map,
    wavevectors,
):
    atoms = positions.shape[3]
    slots = neighbours.shape[3]
    features, lat_width = charge_map.shape
    wave_count = wavevectors.shape[1]
    grid = lax.axis_size("gx"), lax.axis_size("gy")
    grid_x, grid_y = grid
    edges = slots * atoms
    scale = 1.0 / math.sqrt(wave_count * lat_width * atoms * grid_x * grid_y)
    place = jnp.stack([lax.axis_index("gx"), lax.axis_index("gy")]).astype(jnp.int32)
    place = jnp.broadcast_to(place[:, None, None], (2, 8, 128))
    _, share, padded = pair_counts(grid_x)
    ids = neighbours.transpose(0, 3, 1, 2).reshape(1, edges)
    cell_rows = 4 * atoms // 128
    block_total = -(-(cell_rows + (edges + atoms) // 128) // 8) * 8
    dma = pltpu.SemaphoreType.DMA
    shown = positions.transpose(0, 2, 1, 3)
    (own_place,) = run(
        pack_kernel,
        [shape(cell_rows, 128)],
        [place, shown, species],
        flops=10_000_000_000,
        name="pack",
    )
    (own,) = run(
        pack_more_kernel,
        [shape(block_total, 128)],
        [place, ids, counts, own_place],
        name="pack_more",
    )
    y_pair, y_beyond = paired(own, "gy", 1), beyond(own, "gy")
    over_pair = far(own_place, "gy", True)
    over_beyond = over_pair if grid_y == 4 else far(own_place, "gy", False)
    cells = jnp.stack(
        [over_pair, y_pair[:cell_rows], own_place, y_beyond[:cell_rows], over_beyond]
    )
    cells = [paired(cells, "gx", 1), cells, beyond(cells, "gx")]

    norm = 1.0 / math.sqrt(slots)
    kind_rows = 8 * species_embed.shape[0]
    low_pair = lambda *dims: [shape(*dims, dtype=BF16)] * 2
    embed, kind_left, left, back, kind_high, kind_low, mix_high, mix_low, turn_high, turn_low = run(
        functools.partial(prep_first_kernel, norm),
        [
            shape(features, 32, dtype=BF16),
            shape(2, features, 4 * kind_rows, dtype=BF16),
            shape(2, features, 32, dtype=BF16),
            shape(2, 16, 2 * features, dtype=BF16),
        ]
        + low_pair(2, kind_rows, features)
        + low_pair(2, features, 2 * features)
        + low_pair(2, 2 * features, features),
        [species_embed, radial, mixing],
        scratch=[
            pltpu.VMEM(species_embed.shape, F32),
            pltpu.VMEM(radial.shape, F32),
            pltpu.VMEM(mixing.shape, F32),
            dma((3,)),
        ],
        hbm=3,
        name="prep_first",
    )
    read_out, hidden_high, hidden_low, hidden_turn_high, hidden_turn_low, charge_pair = run(
        prep_second_kernel,
        [shape(1, features)]
        + low_pair(features, features)
        + low_pair(features, features)
        + [shape(2, lat_width, features, dtype=BF16)],
        [read_out[None, :], read_hidden, charge_map.T],
        scratch=[
            pltpu.VMEM(read_hidden.shape, F32),
            pltpu.VMEM((lat_width, features), F32),
            dma((3,)),
        ],
        hbm=3,
        name="prep_second",
    )
    cells, hidden_high = lax.optimization_barrier((cells, hidden_high))
    low, ids, basis, slope, unit, sums_one, gate_one = run(
        functools.partial(first_kernel, slots),
        [
            shape(3, features, atoms, dtype=BF16),
            shape(3, edges, dtype=jnp.int32),
            shape(3, 8, edges),
            shape(3, 8, edges),
            shape(3, 8, edges),
            shape(3, 3, features, atoms),
            shape(3, features, atoms),
        ],
        [place, embed, kind_left, mix_high, mix_low, y_pair, own, y_beyond] + cells,
        name="first",
    )
    hidden = [paired(low, "gx", 1), low, beyond(low, "gx")]
    edge_weights, near = run(
        functools.partial(second_near_kernel, slots),
        [shape(4, features, edges), shape(features, edges)],
        [ids, basis, unit, left, low],
        flops=2_000_000_000,
        name="second_near",
    )
    (hot_beyond,) = run(
        hot_beyond_kernel,
        [shape(3 * atoms, edges, dtype=BF16)],
        [ids, near],
        flops=1_000_000,
        name="hot_beyond",
    )
    (near,) = run(
        functools.partial(second_side_kernel, slots),
        [shape(features, edges)],
        [ids, near, hidden[0]],
        flops=1_000_000_000,
        name="second_side",
    )
    block_rows = -(-(lat_width + 9) // 16) * 16
    feature, sums_two, gate_two, packed, charge, hidden_two = run(
        functools.partial(second_kernel, slots),
        [
            shape(features, edges, dtype=BF16),
            shape(3, features, atoms),
            shape(features, atoms),
            shape(block_rows, atoms, dtype=BF16),
            shape(lat_width, atoms),
            shape(features, atoms),
        ],
        [hot_beyond, edge_weights, near, mix_high, mix_low, charge_pair, cells[1], hidden[1],
         hidden[2]],
        name="second",
    )
    energy, energy_slope = run(
        readout_kernel,
        [shape(1, atoms), shape(features, atoms)],
        [hidden_high, hidden_low, hidden_turn_high, hidden_turn_low, read_out, hidden_two],
        name="readout",
    )
    half = grid_x // 2
    near_charges = jnp.stack([packed] + [paired(packed, "gx", 2 * d) for d in range(1, half)])
    (weight,) = run(
        functools.partial(green_weights, share, padded, grid),
        [shape(16 * share + padded, 128)],
        [place, wavevectors],
        name="green",
    )
    near_charges, weight = lax.optimization_barrier((near_charges, weight))
    far_charges = paired(near_charges, "gx", 1)
    span = half * atoms
    rows = 32 * share + 2 * padded
    phase_shapes = [
        shape(padded, span),
        shape(padded, span),
        shape(8, span),
        shape(8, span),
        shape(rows, span, dtype=BF16),
        shape(rows, span, dtype=BF16),
    ]
    *near_phases, near_total = run(
        functools.partial(structure_kernel, share, padded, grid, lat_width, 0),
        phase_shapes + [shape(rows, lat_width)],
        [place, near_charges],
        flops=1_000_000_000,
        name="structure_near",
    )
    *far_phases, own_part, part = run(
        functools.partial(structure_kernel, share, padded, grid, lat_width, 1),
        phase_shapes
        + [
            shape(rows // 2, 2 * lat_width),
            shape(rows // 2, 2 * lat_width, dtype=BF16),
        ],
        [place, far_charges, near_total],
        name="structure_far",
    )
    parts = [own_part] + [paired(part, "gy", d) for d in range(1, grid_y)]
    (hot_back,) = run(
        hot_back_kernel,
        [shape(edges, 9 * atoms, dtype=BF16)],
        [ids],
        flops=2_000_000_000,
        name="hot_back",
    )
    parts, hot_back = lax.optimization_barrier((parts, hot_back))
    far_folds, wave_rows = run(
        functools.partial(fold_kernel, share, padded, grid, lat_width, 1),
        [shape(half, block_rows, atoms, dtype=BF16), shape(rows, lat_width)],
        [place, weight] + parts + far_phases + [far_charges],
        name="fold_far",
    )
    far_folds = paired(far_folds, "gx", 1)
    (near_folds,) = run(
        functools.partial(fold_kernel, share, padded, grid, lat_width, 0),
        [shape(half, block_rows, atoms)],
        [place, wave_rows] + near_phases + [near_charges],
        flops=1_000_000_000,
        name="fold_near",
    )
    folds = run(
        functools.partial(join_kernel, lat_width),
        [shape(block_rows, atoms)] + [shape(block_rows, atoms, dtype=BF16)] * (half - 1),
        [near_folds, far_folds],
        name="fold_join",
    )
    folds = [folds[0]] + [paired(folds[d], "gx", 2 * d) for d in range(1, half)]

    site, long, cotangent, grads, term, to_beyond, to_pair = run(
        functools.partial(second_back_kernel, slots, scale, half),
        [
            shape(1, 1, atoms),
            shape(8, atoms),
            shape(features, atoms),
            shape(4, features, atoms),
            shape(features, edges, dtype=BF16),
            shape(3, features, atoms, dtype=BF16),
            shape(3, features, atoms, dtype=BF16),
        ],
        [hot_back, edge_weights, turn_high, turn_low, charge_pair, sums_two, gate_two, charge,
         energy, energy_slope] + folds,
        name="second_back",
    )
    from_pair, from_beyond = paired(to_pair, "gx", 1), beyond(to_beyond, "gx")
    (middle,) = run(
        second_middle_kernel,
        [shape(3, features, atoms)],
        [hot_back, term, cotangent],
        flops=1_000_000_000,
        name="second_middle",
    )
    (edge,) = run(
        functools.partial(second_edge_kernel, slots),
        [shape(32, edges)],
        [back, feature, grads],
        flops=1_000_000_000,
        name="second_edge",
    )
    to_pair, middle, to_beyond = run(
        functools.partial(first_back_kernel, slots),
        [shape(5, 8, atoms)] * 3,
        [ids, basis, slope, unit, kind_high, kind_low, turn_high, turn_low, sums_one, gate_one, edge,
         long, middle, from_pair, from_beyond],
        name="first_back",
    )
    total = middle + paired(to_pair, "gx", 1) + beyond(to_beyond, "gx")
    if grid_y == 4:
        distant = far(total[0] + total[4], "gy", True)
    else:
        distant = far(total[0], "gy", False) + far(total[4], "gy", True)
    total = total[2] + paired(total[1], "gy", 1) + beyond(total[3], "gy") + distant
    forces = -total[None, :3, None, :]
    return (forces.transpose(0, 2, 1, 3), site)


def solution(mesh):
    in_specs = (
        P("gx", "gy", None, None),
        P("gx", "gy", None),
        P("gx", "gy", None, None),
        P("gx", "gy", None),
        P(),
        P(),
        P(),
        P(),
        P(),
        P(),
        P(),
    )
    out_specs = (P("gx", "gy", None, None), P("gx", "gy", None))
    return jax.shard_map(
        per_device, mesh=mesh, in_specs=in_specs, out_specs=out_specs, check_vma=False
    )
```

```python
import functools
import math

import jax
import jax.numpy as jnp
import numpy as np
from jax import lax
from jax.experimental import pallas as pl
from jax.experimental.pallas import tpu as pltpu
from jax.sharding import PartitionSpec as P

cell_width = 10.0
box_height = 30.0
cut_radius = 50.0
soften = 0.25
screen = 0.5
smear_width = 0.5
WAVE_REACH = 8
F32 = jnp.float32
BF16 = jnp.bfloat16


def paired(block, axis, mask):
    return lax.ppermute(block, axis, [(i ^ mask, i) for i in range(lax.axis_size(axis))])


def other_side(index, count):
    return (index + (1 if index % 2 else -1)) % count


def beyond(block, axis):
    count = lax.axis_size(axis)
    return lax.ppermute(block, axis, [(other_side(i, count), i) for i in range(count)])


def far(block, axis, over_pair):
    count = lax.axis_size(axis)
    if over_pair:
        route = [(other_side(i ^ 1, count), i) for i in range(count)]
    else:
        route = [(other_side(i, count) ^ 1, i) for i in range(count)]
    return lax.ppermute(block, axis, route)


SLOT_CELLS = ((2, 1, 0), (1, 2, 3), (4, 3, 2))


def whole(space=pltpu.VMEM):
    return pl.BlockSpec(memory_space=space)


def run(kernel, outs, args, scratch=(), hbm=0, flops=10_000_000, grant=16, name=None):
    specs = [whole()] * (len(args) - hbm) + [whole(pltpu.HBM)] * hbm
    return list(
        pl.pallas_call(
            kernel,
            out_shape=outs,
            in_specs=specs,
            out_specs=[whole() for _ in outs],
            scratch_shapes=list(scratch),
            compiler_params=pltpu.CompilerParams(vmem_limit_bytes=grant * 1024 * 1024),
            cost_estimate=pl.CostEstimate(
                flops=flops, bytes_accessed=1_000_000, transcendentals=0
            ),
            name=name,
        )(*args)
    )


def shape(*dims, dtype=F32):
    return jax.ShapeDtypeStruct(dims, dtype)


def split(value):
    high = value.astype(BF16)
    return high, (value - high.astype(F32)).astype(BF16)


def dot(left, right, contract=((1,), (0,))):
    return lax.dot_general(left, right, (contract, ((), ())), preferred_element_type=F32)


def dot3(left, right):
    left_high, left_low = split(left)
    right_high, right_low = split(right)
    return dot(left_high, right_high) + (dot(left_high, right_low) + dot(left_low, right_high))


def dot_split(left, right):
    right_high, right_low = split(right)
    return dot(left[0], right_high) + (dot(left[0], right_low) + dot(left[1], right_high))


def sin_cos(turns):
    quarter = jnp.round(turns * 4.0)
    x = (turns - quarter * 0.25) * (2.0 * math.pi)
    z = x * x
    sine = ((-1.9515295891e-4 * z + 8.3321608736e-3) * z - 1.6666654611e-1) * (z * x) + x
    cosine = (2.443315711809948e-5 * z - 1.388731625493765e-3) * z + 4.166664568298827e-2
    cosine = cosine * (z * z) - 0.5 * z + 1.0
    k = quarter.astype(jnp.int32) & 3
    odd = (k & 1) == 1
    by_sine = jnp.where(odd, cosine, sine)
    by_cosine = jnp.where(odd, sine, cosine)
    return (
        jnp.where(k >= 2, -by_sine, by_sine),
        jnp.where((k == 1) | (k == 2), -by_cosine, by_cosine),
    )


def stacked_left(value):
    high = value.astype(BF16).astype(F32)
    rows = jnp.concatenate([high, high, value - high, jnp.zeros_like(high)], axis=0)
    return rows.T.astype(BF16)


def stacked_right(value):
    high = value.astype(BF16).astype(F32)
    return jnp.concatenate([high, value - high, high, jnp.zeros_like(high)], axis=0).astype(BF16)


def silu_pair(value):
    gate = 1.0 / (1.0 + jnp.exp(-value))
    return value * gate, gate * (1.0 + value * (1.0 - gate))


def onehot_kinds(kinds, rows):
    levels = lax.broadcasted_iota(jnp.int32, (rows, kinds.shape[1]), 0).astype(F32)
    return jnp.where(kinds == levels, 1.0, 0.0)


def embedding_stack(embed):
    high = embed.astype(BF16).astype(F32)
    rest = embed - high
    middle = rest.astype(BF16).astype(F32)
    rows = jnp.concatenate([high, middle, rest - middle, jnp.zeros_like(high)], axis=0)
    return rows.T.astype(BF16)


def embedded(stack, kinds):
    hot = onehot_kinds(kinds, 8)
    return dot(stack, jnp.concatenate([hot, hot, hot, jnp.zeros_like(hot)], axis=0).astype(BF16))


def weights_of(stack_ref, part, rows):
    return dot(stack_ref[1 if part else 0], stacked_right(rows))


def mixed(sums, high_ref, low_ref, layer):
    squares = sums[1] * sums[1] + sums[2] * sums[2] + sums[3] * sums[3]
    both = jnp.concatenate([sums[0], squares], axis=0)
    return silu_pair(dot_split((high_ref[layer], low_ref[layer]), both))


def edge_parts(basis, unit):
    return [basis] + [basis * unit[i : i + 1] for i in range(3)]


def pack_kernel(place_ref, position_ref, species_ref, out_ref):
    rows = [position_ref[0, i] for i in range(3)] + [species_ref[0].astype(F32)]
    atoms = rows[0].shape[1]
    out_ref[...] = jnp.concatenate(
        [row[:, s : s + 128] for row in rows for s in range(0, atoms, 128)], axis=0
    )


def pack_more_kernel(place_ref, ids_ref, count_ref, first_ref, out_ref):
    atoms = count_ref.shape[2]
    order = slot_order(ids_ref[...], place_ref, atoms).astype(F32)
    rows = [first_ref[...]]
    rows += [order[:, s : s + 128] for s in range(0, order.shape[1], 128)]
    rows += [count_ref[0, :, s : s + 128].astype(F32) for s in range(0, atoms, 128)]
    missing = out_ref.shape[0] - sum(row.shape[0] for row in rows)
    out_ref[...] = jnp.concatenate(rows + [jnp.zeros((missing, 128), F32)], axis=0)


def block_ids(block, atoms, edges):
    start = 4 * atoms // 128
    middle, end = start + edges // 128, start + edges // 128 + atoms // 128
    rows = [block[r : r + 1] for r in range(start, end)]
    ids = jnp.concatenate(rows[: middle - start], axis=1).astype(jnp.int32)
    return ids, jnp.concatenate(rows[middle - start :], axis=1)


def radial_left(radial):
    high = radial.astype(BF16).astype(F32)
    low = radial - high
    top = jnp.concatenate([high, high], axis=1)
    end = jnp.concatenate([low, jnp.zeros_like(low)], axis=1)
    return jnp.concatenate([top, end], axis=0).astype(BF16)


def put_split(value, high_ref, low_ref, *at):
    high, low = split(value)
    high_ref[at] = high
    low_ref[at] = low


def slot_order(ids, place_ref, atoms):
    cell = ids >> (atoms.bit_length() - 1) if atoms & (atoms - 1) == 0 else ids // atoms
    a = (cell * 11) >> 5
    b = cell - 3 * a
    a = jnp.where((place_ref[0, 0:1, 0:1] & 1) == 0, 2 - a, a)
    b = jnp.where((place_ref[1, 0:1, 0:1] & 1) == 0, 2 - b, b)
    return ids + (3 * a + b - cell) * atoms


def fetch(sources, targets, sems):
    copies = [
        pltpu.make_async_copy(source, target, sems.at[i])
        for i, (source, target) in enumerate(zip(sources, targets))
    ]
    for copy in copies:
        copy.start()
    for copy in copies:
        copy.wait()


def prep_first_kernel(norm, embed_in, radial_in, mixing_in, embed_out, kind_left, left_out, back_out,
                      kind_high, kind_low, mix_high, mix_low, turn_high, turn_low, embed_ref,
                      radial_ref, mixing_ref, sems):
    fetch([embed_in, radial_in, mixing_in], [embed_ref, radial_ref, mixing_ref], sems)
    embed = embed_ref[...]
    kinds = embed.shape[0]
    for path in range(2):
        radial = radial_ref[0, path] * norm
        rows = jnp.concatenate([radial * embed[s : s + 1] for s in range(kinds)], axis=0)
        kind_left[path] = stacked_left(rows)
        put_split(rows, kind_high, kind_low, path)
        radial = radial_ref[1, path] * norm
        left_out[path] = stacked_left(radial)
        back_out[path] = radial_left(radial)
    for layer in range(2):
        scalar, vector = mixing_ref[layer, 0], mixing_ref[layer, 1]
        put_split(jnp.concatenate([scalar.T, vector.T], axis=1), mix_high, mix_low, layer)
        put_split(jnp.concatenate([scalar, 2.0 * vector], axis=0), turn_high, turn_low, layer)
    embed = jnp.concatenate([embed, jnp.zeros((8 - kinds, embed.shape[1]), F32)], axis=0)
    embed_out[...] = embedding_stack(embed)


def prep_second_kernel(read_in, hidden_in, charge_in, read_ref, hidden_high, hidden_low,
                       hidden_turn_high, hidden_turn_low, charge_pair, hidden_ref, charge_ref, sems):
    fetch([read_in, hidden_in, charge_in], [read_ref, hidden_ref, charge_ref], sems)
    put_split(hidden_ref[...].T, hidden_high, hidden_low, Ellipsis)
    put_split(hidden_ref[...], hidden_turn_high, hidden_turn_low, Ellipsis)
    charge = charge_ref[...]
    high = charge.astype(BF16).astype(F32)
    charge_pair[0] = high.astype(BF16)
    charge_pair[1] = (charge - high).astype(BF16)


def hot_beyond_kernel(ids_ref, near_ref, hot_ref):
    ids = ids_ref[1:2, :] - 2 * hot_ref.shape[0]
    for start in range(0, hot_ref.shape[1], 256):
        lanes = slice(start, start + 256)
        hot_ref[:, lanes] = hot_columns(ids[:, lanes], hot_ref.shape[0])


def hot_back_kernel(ids_ref, hot_ref):
    edges = ids_ref.shape[1]
    entry = lax.broadcasted_iota(jnp.int32, (128, hot_ref.shape[1]), 1).astype(F32)
    for start in range(0, edges, 128):
        row = jnp.broadcast_to(ids_ref[1:2, start : start + 128].astype(F32), (8, 128))
        column = row.T[:, 0:1]
        hot_ref[start : start + 128] = jnp.where(column == entry, 1.0, 0.0).astype(BF16)


def lane_hot_kernel(ids_ref, hot_ref):
    edges = ids_ref.shape[1]
    lane = lax.broadcasted_iota(jnp.int32, (128, 128), 1).astype(F32)
    for cell in range(3):
        for start in range(0, edges, 128):
            row = (ids_ref[cell : cell + 1, start : start + 128] & 127).astype(F32)
            column = jnp.broadcast_to(row, (8, 128)).T[:, 0:1]
            hot_ref[cell, start : start + 128] = jnp.where(column == lane, 1.0, 0.0).astype(BF16)


def unfold_block(block, atoms):
    parts = atoms // 128
    rows = [block[r : r + 1] for r in range(4 * parts)]
    return [jnp.concatenate(rows[q * parts : (q + 1) * parts], axis=1) for q in range(4)]


def first_kernel(slots, place_ref, embed_ref, kind_left, mix_high, mix_low, y_pair_ref, own_ref,
                 y_beyond_ref, pair_ref, column_ref, beyond_ref, low_ref, ids_ref, basis_ref, slope_ref,
                 unit_ref, sums_ref, gate_ref):
    atoms = low_ref.shape[2]
    frame = [pair_ref, column_ref, beyond_ref]
    per_cell = atoms // 128
    places = lax.broadcasted_iota(jnp.int32, (4 * per_cell, 128), 0)
    upper = places % per_cell
    kind_of_row = places // per_cell
    to_x = jnp.where(kind_of_row == 0, cell_width, 0.0)
    to_x = jnp.where((place_ref[0] & 1) == 0, to_x, -to_x)
    to_y = jnp.where(kind_of_row == 1, cell_width, 0.0)
    to_y = jnp.where((place_ref[1] & 1) == 0, to_y, -to_y)
    cells = []
    for cell, block_ref in enumerate((y_pair_ref, own_ref, y_beyond_ref)):
        ids, count = block_ids(block_ref[...], atoms, slots * atoms)
        ids_ref[cell : cell + 1, :] = ids
        own = unfold_block(column_ref[cell + 1], atoms)
        step_y = to_y if cell == 1 else -to_y
        rows = []
        for a in range(3):
            for b in range(3):
                block = frame[a][SLOT_CELLS[cell][b]]
                rows.append(block + ((1 - a) * to_x + (1 - b) * step_y))
        cells.append((count, own, gathered_rows(ids, rows, places, upper)))
    rel = []
    for q in range(3):
        found = jnp.concatenate([found[q] for _, _, found in cells], axis=0)
        own = jnp.concatenate([own[q] for _, own, _ in cells], axis=0)
        rel.append(found - jnp.concatenate([own] * slots, axis=1))
    distance = jnp.sqrt(rel[0] * rel[0] + rel[1] * rel[1] + rel[2] * rel[2] + soften)
    inverse = 1.0 / distance
    units = [r * inverse for r in rel]
    for cell, (count, own, found) in enumerate(cells):
        one = slice(cell, cell + 1)
        first_cell(
            slots, atoms, count, [u[one] for u in units], distance[one], inverse[one], found[3],
            own[3], embed_ref, kind_left, mix_high, mix_low, low_ref.at[cell], basis_ref.at[cell],
            slope_ref.at[cell], unit_ref.at[cell], sums_ref.at[cell], gate_ref.at[cell],
        )


def gathered_rows(ids, rows, places, upper):
    per_cell = places.shape[0] // 4
    pieces = []
    for start in range(0, ids.shape[1], 128):
        part = jnp.broadcast_to(ids[:, start : start + 128], places.shape)
        lane, half = part & 127, (part >> 7) - upper
        found = jnp.zeros(places.shape, F32)
        for cell, block in enumerate(rows):
            value = jnp.take_along_axis(block, lane, axis=1)
            found = jnp.where(half == per_cell * cell, value, found)
        total = found
        for s in range(1, per_cell):
            total = total + pltpu.roll(found, 4 * per_cell - s, 0)
        pieces.append(total)
    found = jnp.concatenate(pieces, axis=1)
    found = [found[q * per_cell : q * per_cell + 1] for q in range(4)]
    return found


def first_cell(slots, atoms, count, units, distance, inverse, kinds, own_kinds, embed_ref, kind_left,
               mix_high, mix_low, low_ref, basis_ref, slope_ref, unit_ref, sums_ref, gate_ref):
    order = (lax.broadcasted_iota(jnp.int32, (8, 1), 0) + 1).astype(F32)
    sine, cosine = sin_cos((order * (0.5 / cut_radius)) * distance)
    wave = sine / ((order * (math.pi / cut_radius)) * distance)
    live = jnp.concatenate([jnp.where(count > n, 1.0, 0.0) for n in range(slots)], axis=1)
    basis = wave * live
    basis_ref[...] = basis
    slope_ref[...] = (cosine - wave) * (inverse * live)
    unit = jnp.concatenate(
        units + [inverse, kinds] + [jnp.zeros_like(kinds)] * 3, axis=0
    )
    unit_ref[...] = unit
    stack = embed_ref[...]
    parts = edge_parts(basis, unit)
    species = kind_left.shape[2] // 32
    by_kind = [[None] * species for _ in range(4)]
    for n in range(slots):
        lanes = slice(n * atoms, (n + 1) * atoms)
        kind = jnp.broadcast_to(kinds[:, lanes], (8, atoms))
        for k in range(species):
            match = kind == float(k)
            for part in range(4):
                term = jnp.where(match, parts[part][:, lanes], 0.0)
                old = by_kind[part][k]
                by_kind[part][k] = term if old is None else old + term
    stacks = [stacked_right(jnp.concatenate(rows, axis=0)) for rows in by_kind]
    vectors = dot(kind_left[1], jnp.concatenate(stacks[1:], axis=1))
    sums = [dot(kind_left[0], stacks[0])]
    sums += [vectors[:, i * atoms : (i + 1) * atoms] for i in range(3)]
    step, gate = mixed(sums, mix_high, mix_low, 0)
    low_ref[...] = (embedded(stack, own_kinds) + step).astype(BF16)
    for part in range(3):
        sums_ref[part] = sums[part + 1]
    gate_ref[...] = gate


def hot_columns(ids, rows):
    place = lax.broadcasted_iota(jnp.int32, (rows, ids.shape[1]), 0)
    return jnp.where(ids == place, 1.0, 0.0).astype(BF16)


def second_near_kernel(slots, ids_ref, basis_ref, unit_ref, left_ref, column_ref, weight_ref,
                       near_ref):
    atoms = column_ref.shape[2]
    parts = edge_parts(basis_ref[1], unit_ref[1])
    source = jnp.concatenate([column_ref[b] for b in range(3)], axis=1)
    for n in range(slots):
        lanes = slice(n * atoms, (n + 1) * atoms)
        for part in range(4):
            weight_ref[part, :, lanes] = weights_of(left_ref, part, parts[part][:, lanes])
        ids = ids_ref[1:2, lanes] - 3 * atoms
        near_ref[:, lanes] = dot(source, hot_columns(ids, 3 * atoms))


def second_side_kernel(slots, ids_ref, near_ref, pair_ref, out_ref):
    atoms = pair_ref.shape[2]
    source = jnp.concatenate([pair_ref[b] for b in range(3)], axis=1)
    for n in range(slots):
        lanes = slice(n * atoms, (n + 1) * atoms)
        hot = hot_columns(ids_ref[1:2, lanes], 3 * atoms)
        out_ref[:, lanes] = near_ref[:, lanes] + dot(source, hot)


def second_kernel(slots, hot_ref, weight_ref, near_ref, mix_high, mix_low, charge_ref, cell_ref,
                  column_ref, beyond_ref, feature_ref, sums_ref, gate_ref, packed_ref,
                  full_charge_ref, hidden_ref):
    atoms = column_ref.shape[2]
    source = jnp.concatenate([beyond_ref[b] for b in range(3)], axis=1)
    sums = [None] * 4
    for n in range(slots):
        lanes = slice(n * atoms, (n + 1) * atoms)
        feature = near_ref[:, lanes] + dot(source, hot_ref[:, lanes])
        feature_ref[:, lanes] = feature.astype(BF16)
        for part in range(4):
            term = weight_ref[part, :, lanes] * feature
            sums[part] = term if sums[part] is None else sums[part] + term
    step, gate = mixed(sums, mix_high, mix_low, 1)
    hidden = column_ref[1].astype(F32) + step
    hidden_ref[...] = hidden
    for part in range(3):
        sums_ref[part] = sums[part + 1]
    gate_ref[...] = gate
    charge = dot_split((charge_ref[0], charge_ref[1]), hidden)
    full_charge_ref[...] = charge
    place = jnp.concatenate(unfold_block(cell_ref[2], atoms)[:3], axis=0)
    high = place.astype(BF16).astype(F32)
    rest = place - high
    middle = rest.astype(BF16).astype(F32)
    zero = jnp.zeros((packed_ref.shape[0] - charge.shape[0] - 9, atoms), F32)
    packed_ref[...] = jnp.concatenate([charge, high, middle, rest - middle, zero], axis=0).astype(
        BF16
    )


def readout_kernel(hidden_high, hidden_low, turn_high, turn_low, out_ref, hidden_ref, energy_ref,
                   slope_ref):
    hidden = hidden_ref[...]
    value, slope = silu_pair(dot_split((hidden_high[...], hidden_low[...]), hidden))
    out = out_ref[...].T
    energy_ref[...] = jnp.sum(value * out, axis=0, keepdims=True)
    slope_ref[...] = dot_split((turn_high[...], turn_low[...]), slope * out)


def message_grads(cotangent, gate_ref, sums_ref, high_ref, low_ref, layer):
    pre = cotangent * gate_ref[...]
    both = dot_split((high_ref[layer], low_ref[layer]), pre)
    half = both.shape[0] // 2
    return [both[:half]] + [both[half:] * sums_ref[i] for i in range(3)]


def radial_grad(left, value):
    high, low = split(value)
    both = dot(left, jnp.concatenate([high, low], axis=0))
    half = both.shape[0] // 2
    return both[:half] + both[half:]


def second_back_kernel(slots, scale, count, hot_ref, weight_ref, turn_high, turn_low, charge_ref,
                       sums_ref, gate_ref, full_charge_ref, energy_ref, slope_ref, *refs):
    folds, refs = refs[:count], refs[count:]
    site_ref, long_ref, cotangent_ref, grad_ref, term_ref, beyond_ref, pair_ref = refs
    atoms = gate_ref.shape[1]
    total = folds[0][...].astype(F32)
    for part in folds[1:]:
        total = total + part[...].astype(F32)
    wide = full_charge_ref.shape[0]
    potential = total[:wide] * (2.0 * scale)
    slopes = total[wide : wide + 3] + total[wide + 3 : wide + 6] + total[wide + 6 : wide + 9]
    long_ref[...] = jnp.concatenate(
        [slopes * (2.0 * scale), jnp.zeros((5, atoms), F32)], axis=0
    )
    site_ref[0] = energy_ref[...] + 0.5 * jnp.sum(
        full_charge_ref[...] * potential, axis=0, keepdims=True
    )
    high, low = split(potential)
    turned = ((0,), (0,))
    cotangent = slope_ref[...] + (
        dot(charge_ref[0], high, turned)
        + (dot(charge_ref[0], low, turned) + dot(charge_ref[1], high, turned))
    )
    cotangent_ref[...] = cotangent
    grads = message_grads(cotangent, gate_ref, sums_ref, turn_high, turn_low, 1)
    for part in range(4):
        grad_ref[part] = grads[part]
    for n in range(slots):
        lanes = slice(n * atoms, (n + 1) * atoms)
        term = weight_ref[0, :, lanes] * grads[0]
        for part in range(1, 4):
            term = term + weight_ref[part, :, lanes] * grads[part]
        term_ref[:, lanes] = term.astype(BF16)
    for b in range(3):
        start = (6 + b) * atoms
        beyond_ref[b] = dot(term_ref[...], hot_ref[:, start : start + atoms]).astype(BF16)
    for b in range(3):
        pair_ref[b] = dot(term_ref[...], hot_ref[:, b * atoms : (b + 1) * atoms]).astype(BF16)


def second_middle_kernel(hot_ref, term_ref, cotangent_ref, middle_ref):
    atoms = cotangent_ref.shape[1]
    for b in range(3):
        grad = dot(term_ref[...], hot_ref[:, (3 + b) * atoms : (4 + b) * atoms])
        middle_ref[b] = grad + cotangent_ref[...] if b == 1 else grad


def second_edge_kernel(slots, back_ref, feature_ref, grad_ref, edge_ref):
    atoms = grad_ref.shape[2]
    for n in range(slots):
        lanes = slice(n * atoms, (n + 1) * atoms)
        feature = feature_ref[:, lanes].astype(F32)
        for part in range(4):
            edge_ref[8 * part : 8 * part + 8, lanes] = radial_grad(
                back_ref[1 if part else 0], grad_ref[part] * feature
            )


def first_back_kernel(slots, ids_ref, lane_ref, basis_ref, slope_ref, unit_ref, kind_high, kind_low, turn_high,
                      turn_low, sums_ref, gate_ref, edge_ref, long_ref, middle_ref, from_pair,
                      from_beyond, *outs):
    sums = {(1, 2): long_ref[...]}
    for cell in range(3):
        cotangent = middle_ref[cell] + (
            from_pair[cell].astype(F32) + from_beyond[cell].astype(F32)
        )
        own, found = first_back_cell(
            slots, ids_ref[cell : cell + 1, :], lane_ref.at[cell], basis_ref.at[cell], slope_ref.at[cell],
            unit_ref.at[cell], kind_high, kind_low, turn_high, turn_low, sums_ref.at[cell],
            gate_ref.at[cell], edge_ref if cell == 1 else None, cotangent,
        )
        terms = [((1, cell + 1), own)]
        terms += [((n // 3, SLOT_CELLS[cell][n % 3]), found[n]) for n in range(9)]
        for key, term in terms:
            sums[key] = sums[key] + term if key in sums else term
    for (x, y), total in sums.items():
        outs[x][y] = total


def first_back_cell(slots, ids, lane_ref, basis_ref, slope_ref, unit_ref, kind_high, kind_low, turn_high,
                    turn_low, sums_ref, gate_ref, edge_ref, cotangent):
    atoms = gate_ref.shape[1]
    pre = cotangent * gate_ref[...]
    both = dot_split((turn_high[0], turn_low[0]), pre)
    wide = both.shape[0] // 2
    grads = [both[:wide]] + [both[wide:] * sums_ref[i] for i in range(3)]
    unit = unit_ref[...]
    kinds = unit[4:5]
    by_kind = [dot_split((kind_high[0], kind_low[0]), grads[0])]
    by_kind += [dot_split((kind_high[1], kind_low[1]), grads[i]) for i in range(1, 4)]
    species = by_kind[0].shape[0] // 8
    edges = [[] for _ in range(4)]
    for n in range(slots):
        kind = jnp.broadcast_to(kinds[:, n * atoms : (n + 1) * atoms], (8, atoms))
        matches = [kind == float(k) for k in range(1, species)]
        for part in range(4):
            rows = by_kind[part]
            found = rows[:8]
            for k, match in enumerate(matches):
                found = jnp.where(match, rows[8 * k + 8 : 8 * k + 16], found)
            edges[part].append(found)
    edges = [jnp.concatenate(rows, axis=1) for rows in edges]
    if edge_ref is not None:
        edges = [edge_ref[8 * part : 8 * part + 8] + edges[part] for part in range(4)]
    basis = basis_ref[...]
    units = [unit[i : i + 1] for i in range(3)]
    inverse = unit[3:4]
    by_basis = edges[0]
    for i in range(3):
        by_basis = by_basis + edges[i + 1] * units[i]
    by_unit = [jnp.sum(edges[i + 1] * basis, axis=0, keepdims=True) * inverse for i in range(3)]
    by_distance = jnp.sum(by_basis * slope_ref[...], axis=0, keepdims=True)
    for i in range(3):
        by_distance = by_distance - by_unit[i] * units[i]
    moves = [by_unit[i] + by_distance * units[i] for i in range(3)]
    zero = jnp.zeros_like(moves[0])
    move = jnp.concatenate(moves + [zero] * 5, axis=0)
    own = -move[:, :atoms]
    for n in range(1, slots):
        own = own - move[:, n * atoms : (n + 1) * atoms]
    half = ids >> 7
    high = move.astype(BF16).astype(F32)
    both = jnp.concatenate([high, move - high], axis=0)
    per_cell = atoms // 128
    rows = jnp.concatenate(
        [jnp.where(half == h, both, 0.0).astype(BF16) for h in range(9 * per_cell)], axis=0
    )
    spread = dot(rows, lane_ref[...])
    grads = []
    for cell in range(9):
        found = []
        for h in range(cell * per_cell, (cell + 1) * per_cell):
            found.append(spread[16 * h : 16 * h + 8] + spread[16 * h + 8 : 16 * h + 16])
        grads.append(jnp.concatenate(found, axis=1))
    return own, grads


def pair_counts(parts):
    total = WAVE_REACH + WAVE_REACH * (2 * WAVE_REACH + 1)
    share = -(-total // parts)
    return total, share, -(-share // 16) * 16


def pair_vectors(slot, share, part):
    side = 2 * WAVE_REACH + 1
    total = WAVE_REACH + WAVE_REACH * side
    index = slot + part.astype(F32) * share
    later = index - WAVE_REACH
    row = jnp.floor((later + 0.5) * (1.0 / side))
    first = index < WAVE_REACH
    kx = jnp.where(first, 0.0, row + 1.0)
    ky = jnp.where(first, index + 1.0, later - row * side - WAVE_REACH)
    valid = jnp.where((slot < share) & (index < total), 1.0, 0.0)
    return kx, ky, valid


def count_up(rows):
    return lax.broadcasted_iota(jnp.int32, (rows, 1), 0).astype(F32)


def green_weights(share, padded, grid, place_ref, vec_ref, weight_ref):
    grid_x, grid_y = grid
    turn = 2.0 * math.pi
    side = 2 * WAVE_REACH + 1
    top = side * side * side - 1
    vec = vec_ref[...].astype(F32) + WAVE_REACH
    code = (vec[0:1] * side + vec[1:2]) * side + vec[2:3]
    code = jnp.maximum(code, top - code)
    span = 8 * share
    row = count_up(span)
    slot = jnp.floor(row * 0.125)
    height = row - 8.0 * slot + 1.0
    flat = count_up(padded)
    slot = jnp.concatenate([slot, slot, flat], axis=0)
    kz = jnp.concatenate([height, -height, jnp.zeros_like(flat)], axis=0)
    kx, ky, valid = pair_vectors(slot, share, place_ref[0, 0:1, 0:1])
    own = ((kx + WAVE_REACH) * side + ky + WAVE_REACH) * side + kz + WAVE_REACH
    seen = jnp.zeros((own.shape[0], 128), F32)
    for start in range(0, code.shape[1], 128):
        seen = seen + jnp.where(own == code[:, start : start + 128], 1.0, 0.0)
    count = jnp.sum(seen, axis=1, keepdims=True) * valid
    sq = (
        (kx * (turn / (grid_x * cell_width))) ** 2
        + (ky * (turn / (grid_y * cell_width))) ** 2
        + (kz * (turn / box_height)) ** 2
    )
    green = jnp.exp(-smear_width * sq) / (sq + screen * screen) * count
    weight_ref[...] = jnp.broadcast_to(green, weight_ref.shape)


def basis_rows(share, ca, sa, cb, sb):
    cc, ss, sc, cs = [], [], [], []
    for p in range(share):
        c, s = ca[p : p + 1], sa[p : p + 1]
        cc.append(c * cb)
        ss.append(s * sb)
        sc.append(s * cb)
        cs.append(c * sb)
    return cc, ss, sc, cs


def unpack_rows(block):
    half = block.shape[1] // 2
    return jnp.concatenate([block[:, :half], block[:, half:]], axis=0)


def pack_rows(block):
    half = block.shape[0] // 2
    return jnp.concatenate([block[:half], block[half:]], axis=1)


def structure_kernel(share, padded, grid, wide, flip, place_ref, blocks, *refs):
    grid_x, grid_y = grid
    if flip:
        near_ref, (ca_ref, sa_ref, cb_ref, sb_ref, high_ref, low_ref, own_ref, out_ref) = (
            refs[0],
            refs[1:],
        )
        total = near_ref[...]
    else:
        ca_ref, sa_ref, cb_ref, sb_ref, high_ref, low_ref, total_ref = refs
        total = None
    col = place_ref[1, 0:1, 0:1].astype(F32) * (1.0 / grid_y)
    first = place_ref[0, 0:1, 0:1] ^ flip
    kx, ky, _ = pair_vectors(count_up(padded), share, place_ref[0, 0:1, 0:1])
    kz = count_up(8) + 1.0
    for d in range(grid_x // 2):
        block = blocks[d]
        charge = block[:wide]
        atoms = charge.shape[1]
        pieces = block[wide:].astype(F32)
        place = pieces[0:3] + (pieces[3:6] + pieces[6:9])
        row = (first ^ (2 * d)).astype(F32) * (1.0 / grid_x)
        x = place[0:1] * (1.0 / (grid_x * cell_width)) + row
        y = place[1:2] * (1.0 / (grid_y * cell_width)) + col
        sa, ca = sin_cos(kx * x + ky * y)
        sb, cb = sin_cos(kz * (place[2:3] * (1.0 / box_height)))
        lanes = pl.ds(d * atoms, atoms)
        ca_ref[:, lanes] = ca
        sa_ref[:, lanes] = sa
        cb_ref[:, lanes] = cb
        sb_ref[:, lanes] = sb
        cc, ss, sc, cs = basis_rows(share, ca, sa, cb, sb)
        high, low = split(jnp.concatenate(cc + ss + sc + cs + [ca, sa], axis=0))
        high_ref[:, lanes] = high
        low_ref[:, lanes] = low
        term = dot(high, charge, ((1,), (1,))) + dot(low, charge, ((1,), (1,)))
        total = term if total is None else total + term
    if flip:
        packed = pack_rows(total)
        own_ref[...] = packed
        out_ref[...] = packed.astype(BF16)
    else:
        total_ref[...] = total


def weighted_rows(share, padded, wide, weight_ref, parts):
    packed = parts[0][...].astype(F32)
    for part in parts[1:]:
        packed = packed + part[...].astype(F32)
    struct = unpack_rows(packed)
    span = 8 * share
    cc, ss, sc, cs = (struct[i * span : (i + 1) * span] for i in range(4))
    weight = weight_ref[:, :wide]
    plus, minus, flat = weight[:span], weight[span : 2 * span], weight[2 * span :]
    re_plus, im_plus = plus * (cc - ss), plus * (sc + cs)
    re_minus, im_minus = minus * (cc + ss), minus * (sc - cs)
    rows = jnp.concatenate(
        [
            re_plus + re_minus,
            re_minus - re_plus,
            im_plus + im_minus,
            im_plus - im_minus,
            flat * struct[4 * span : 4 * span + padded],
            flat * struct[4 * span + padded :],
        ],
        axis=0,
    )
    return rows


def fold_kernel(share, padded, grid, wide, flip, place_ref, *refs):
    grid_x, grid_y = grid
    turn = 2.0 * math.pi
    if flip:
        weight_ref, parts, refs = refs[0], refs[1 : 1 + grid_y], refs[1 + grid_y :]
        rows = weighted_rows(share, padded, wide, weight_ref, parts)
        refs, rows_ref = refs[:-1], refs[-1]
        rows_ref[...] = rows
    else:
        rows, refs = refs[0][...], refs[1:]
    ca_ref, sa_ref, cb_ref, sb_ref, high_ref, low_ref, blocks, out_ref = refs
    row_high, row_low = split(rows)
    row_pair = jnp.concatenate([row_high, row_low], axis=1)
    turned = rows.T
    t_high, t_low = split(turned)
    t_both = jnp.concatenate([t_high, t_low], axis=0)
    span = 8 * share
    kx, ky, _ = pair_vectors(count_up(padded), share, place_ref[0, 0:1, 0:1])
    kx = kx * (turn / (grid_x * cell_width))
    ky = ky * (turn / (grid_y * cell_width))
    kz = (count_up(8) + 1.0) * (turn / box_height)
    for d in range(grid_x // 2):
        charge = blocks[d][:wide]
        atoms = charge.shape[1]
        lanes = pl.ds(d * atoms, atoms)
        ca, sa, cb, sb = ca_ref[:, lanes], sa_ref[:, lanes], cb_ref[:, lanes], sb_ref[:, lanes]
        bcc, bss, bsc, bcs = basis_rows(share, ca, sa, cb, sb)
        high, low = high_ref[:, lanes], low_ref[:, lanes]
        both = dot(t_both, high)
        pot = both[:wide] + both[wide:] + dot(t_high, low)
        proj = dot(row_pair, jnp.concatenate([charge, charge], axis=0))
        by_x = jnp.zeros((8, atoms), jnp.float32)
        by_y = jnp.zeros((8, atoms), jnp.float32)
        by_z = jnp.zeros((8, atoms), jnp.float32)
        for p in range(share):
            pcc, pss, psc, pcs = (
                proj[i * span + 8 * p : i * span + 8 * p + 8] for i in range(4)
            )
            slope = bcs[p] * pss - bsc[p] * pcc + bcc[p] * psc - bss[p] * pcs
            by_x = by_x + kx[p : p + 1] * slope
            by_y = by_y + ky[p : p + 1] * slope
            by_z = by_z + (bsc[p] * pss - bcs[p] * pcc - bss[p] * psc + bcc[p] * pcs)
        flat_slope = ca * proj[4 * span + padded :] - sa * proj[4 * span : 4 * span + padded]
        grad_x = jnp.sum(by_x, axis=0, keepdims=True) + jnp.sum(kx * flat_slope, axis=0, keepdims=True)
        grad_y = jnp.sum(by_y, axis=0, keepdims=True) + jnp.sum(ky * flat_slope, axis=0, keepdims=True)
        grad_z = jnp.sum(kz * by_z, axis=0, keepdims=True)
        slopes = jnp.concatenate([grad_x, grad_y, grad_z], axis=0)
        out_ref[d] = pieced(pot, slopes, out_ref.shape[1]).astype(out_ref.dtype)


def pieced(pot, slopes, rows):
    high = slopes.astype(BF16).astype(F32)
    rest = slopes - high
    middle = rest.astype(BF16).astype(F32)
    zero = jnp.zeros((rows - pot.shape[0] - 9, pot.shape[1]), F32)
    return jnp.concatenate([pot, high, middle, rest - middle, zero], axis=0)


def unpieced(block, wide):
    slopes = block[wide : wide + 3] + (block[wide + 3 : wide + 6] + block[wide + 6 : wide + 9])
    return block[:wide], slopes


def join_kernel(wide, near_ref, far_ref, own_ref, *outs):
    for d in range(near_ref.shape[0]):
        pot, slopes = unpieced(near_ref[d], wide)
        pot_far, slopes_far = unpieced(far_ref[d].astype(F32), wide)
        block = pieced(pot + pot_far, slopes + slopes_far, near_ref.shape[1])
        if d:
            outs[d - 1][...] = block.astype(BF16)
        else:
            own_ref[...] = block


def per_device(
    positions,
    species,
    neighbours,
    counts,
    species_embed,
    radial,
    mixing,
    read_hidden,
    read_out,
    charge_map,
    wavevectors,
):
    atoms = positions.shape[3]
    slots = neighbours.shape[3]
    features, lat_width = charge_map.shape
    wave_count = wavevectors.shape[1]
    grid = lax.axis_size("gx"), lax.axis_size("gy")
    grid_x, grid_y = grid
    edges = slots * atoms
    scale = 1.0 / math.sqrt(wave_count * lat_width * atoms * grid_x * grid_y)
    place = jnp.stack([lax.axis_index("gx"), lax.axis_index("gy")]).astype(jnp.int32)
    place = jnp.broadcast_to(place[:, None, None], (2, 8, 128))
    _, share, padded = pair_counts(grid_x)
    ids = neighbours.transpose(0, 3, 1, 2).reshape(1, edges)
    cell_rows = 4 * atoms // 128
    block_total = -(-(cell_rows + (edges + atoms) // 128) // 8) * 8
    dma = pltpu.SemaphoreType.DMA
    shown = positions.transpose(0, 2, 1, 3)
    (own_place,) = run(
        pack_kernel,
        [shape(cell_rows, 128)],
        [place, shown, species],
        flops=10_000_000_000,
        name="pack",
    )
    (own,) = run(
        pack_more_kernel,
        [shape(block_total, 128)],
        [place, ids, counts, own_place],
        name="pack_more",
    )
    y_pair, y_beyond = paired(own, "gy", 1), beyond(own, "gy")
    over_pair = far(own_place, "gy", True)
    over_beyond = over_pair if grid_y == 4 else far(own_place, "gy", False)
    cells = jnp.stack(
        [over_pair, y_pair[:cell_rows], own_place, y_beyond[:cell_rows], over_beyond]
    )
    cells = [paired(cells, "gx", 1), cells, beyond(cells, "gx")]

    norm = 1.0 / math.sqrt(slots)
    kind_rows = 8 * species_embed.shape[0]
    low_pair = lambda *dims: [shape(*dims, dtype=BF16)] * 2
    embed, kind_left, left, back, kind_high, kind_low, mix_high, mix_low, turn_high, turn_low = run(
        functools.partial(prep_first_kernel, norm),
        [
            shape(features, 32, dtype=BF16),
            shape(2, features, 4 * kind_rows, dtype=BF16),
            shape(2, features, 32, dtype=BF16),
            shape(2, 16, 2 * features, dtype=BF16),
        ]
        + low_pair(2, kind_rows, features)
        + low_pair(2, features, 2 * features)
        + low_pair(2, 2 * features, features),
        [species_embed, radial, mixing],
        scratch=[
            pltpu.VMEM(species_embed.shape, F32),
            pltpu.VMEM(radial.shape, F32),
            pltpu.VMEM(mixing.shape, F32),
            dma((3,)),
        ],
        hbm=3,
        name="prep_first",
    )
    read_out, hidden_high, hidden_low, hidden_turn_high, hidden_turn_low, charge_pair = run(
        prep_second_kernel,
        [shape(1, features)]
        + low_pair(features, features)
        + low_pair(features, features)
        + [shape(2, lat_width, features, dtype=BF16)],
        [read_out[None, :], read_hidden, charge_map.T],
        scratch=[
            pltpu.VMEM(read_hidden.shape, F32),
            pltpu.VMEM((lat_width, features), F32),
            dma((3,)),
        ],
        hbm=3,
        name="prep_second",
    )
    cells, hidden_high = lax.optimization_barrier((cells, hidden_high))
    low, ids, basis, slope, unit, sums_one, gate_one = run(
        functools.partial(first_kernel, slots),
        [
            shape(3, features, atoms, dtype=BF16),
            shape(3, edges, dtype=jnp.int32),
            shape(3, 8, edges),
            shape(3, 8, edges),
            shape(3, 8, edges),
            shape(3, 3, features, atoms),
            shape(3, features, atoms),
        ],
        [place, embed, kind_left, mix_high, mix_low, y_pair, own, y_beyond] + cells,
        name="first",
    )
    hidden = [paired(low, "gx", 1), low, beyond(low, "gx")]
    edge_weights, near = run(
        functools.partial(second_near_kernel, slots),
        [shape(4, features, edges), shape(features, edges)],
        [ids, basis, unit, left, low],
        flops=2_000_000_000,
        name="second_near",
    )
    (hot_beyond,) = run(
        hot_beyond_kernel,
        [shape(3 * atoms, edges, dtype=BF16)],
        [ids, near],
        flops=1_000_000,
        name="hot_beyond",
    )
    (near,) = run(
        functools.partial(second_side_kernel, slots),
        [shape(features, edges)],
        [ids, near, hidden[0]],
        flops=1_000_000_000,
        name="second_side",
    )
    block_rows = -(-(lat_width + 9) // 16) * 16
    feature, sums_two, gate_two, packed, charge, hidden_two = run(
        functools.partial(second_kernel, slots),
        [
            shape(features, edges, dtype=BF16),
            shape(3, features, atoms),
            shape(features, atoms),
            shape(block_rows, atoms, dtype=BF16),
            shape(lat_width, atoms),
            shape(features, atoms),
        ],
        [hot_beyond, edge_weights, near, mix_high, mix_low, charge_pair, cells[1], hidden[1],
         hidden[2]],
        name="second",
    )
    energy, energy_slope = run(
        readout_kernel,
        [shape(1, atoms), shape(features, atoms)],
        [hidden_high, hidden_low, hidden_turn_high, hidden_turn_low, read_out, hidden_two],
        name="readout",
    )
    half = grid_x // 2
    near_charges = jnp.stack([packed] + [paired(packed, "gx", 2 * d) for d in range(1, half)])
    (weight,) = run(
        functools.partial(green_weights, share, padded, grid),
        [shape(16 * share + padded, 128)],
        [place, wavevectors],
        name="green",
    )
    near_charges, weight = lax.optimization_barrier((near_charges, weight))
    far_charges = paired(near_charges, "gx", 1)
    span = half * atoms
    rows = 32 * share + 2 * padded
    phase_shapes = [
        shape(padded, span),
        shape(padded, span),
        shape(8, span),
        shape(8, span),
        shape(rows, span, dtype=BF16),
        shape(rows, span, dtype=BF16),
    ]
    *near_phases, near_total = run(
        functools.partial(structure_kernel, share, padded, grid, lat_width, 0),
        phase_shapes + [shape(rows, lat_width)],
        [place, near_charges],
        flops=1_000_000_000,
        name="structure_near",
    )
    *far_phases, own_part, part = run(
        functools.partial(structure_kernel, share, padded, grid, lat_width, 1),
        phase_shapes
        + [
            shape(rows // 2, 2 * lat_width),
            shape(rows // 2, 2 * lat_width, dtype=BF16),
        ],
        [place, far_charges, near_total],
        name="structure_far",
    )
    parts = [own_part] + [paired(part, "gy", d) for d in range(1, grid_y)]
    (hot_back,) = run(
        hot_back_kernel,
        [shape(edges, 9 * atoms, dtype=BF16)],
        [ids],
        flops=2_000_000_000,
        name="hot_back",
    )
    parts, hot_back = lax.optimization_barrier((parts, hot_back))
    far_folds, wave_rows = run(
        functools.partial(fold_kernel, share, padded, grid, lat_width, 1),
        [shape(half, block_rows, atoms, dtype=BF16), shape(rows, lat_width)],
        [place, weight] + parts + far_phases + [far_charges],
        name="fold_far",
    )
    far_folds = paired(far_folds, "gx", 1)
    (near_folds,) = run(
        functools.partial(fold_kernel, share, padded, grid, lat_width, 0),
        [shape(half, block_rows, atoms)],
        [place, wave_rows] + near_phases + [near_charges],
        flops=1_000_000_000,
        name="fold_near",
    )
    folds = run(
        functools.partial(join_kernel, lat_width),
        [shape(block_rows, atoms)] + [shape(block_rows, atoms, dtype=BF16)] * (half - 1),
        [near_folds, far_folds],
        name="fold_join",
    )
    folds = [folds[0]] + [paired(folds[d], "gx", 2 * d) for d in reversed(range(1, half))]

    site, long, cotangent, grads, term, to_beyond, to_pair = run(
        functools.partial(second_back_kernel, slots, scale, half),
        [
            shape(1, 1, atoms),
            shape(8, atoms),
            shape(features, atoms),
            shape(4, features, atoms),
            shape(features, edges, dtype=BF16),
            shape(3, features, atoms, dtype=BF16),
            shape(3, features, atoms, dtype=BF16),
        ],
        [hot_back, edge_weights, turn_high, turn_low, charge_pair, sums_two, gate_two, charge,
         energy, energy_slope] + folds,
        name="second_back",
    )
    from_pair, from_beyond = paired(to_pair, "gx", 1), beyond(to_beyond, "gx")
    (middle,) = run(
        second_middle_kernel,
        [shape(3, features, atoms)],
        [hot_back, term, cotangent],
        flops=1_000_000_000,
        name="second_middle",
    )
    (edge,) = run(
        functools.partial(second_edge_kernel, slots),
        [shape(32, edges)],
        [back, feature, grads],
        flops=1_000_000_000,
        name="second_edge",
    )
    (lane_hot,) = run(
        lane_hot_kernel,
        [shape(3, edges, 128, dtype=BF16)],
        [ids],
        flops=1_000_000_000,
        name="lane_hot",
    )
    to_pair, middle, to_beyond = run(
        functools.partial(first_back_kernel, slots),
        [shape(5, 8, atoms)] * 3,
        [ids, lane_hot, basis, slope, unit, kind_high, kind_low, turn_high, turn_low, sums_one,
         gate_one, edge, long, middle, from_pair, from_beyond],
        name="first_back",
    )
    total = middle + paired(to_pair, "gx", 1) + beyond(to_beyond, "gx")
    if grid_y == 4:
        distant = far(total[0] + total[4], "gy", True)
    else:
        distant = far(total[0], "gy", False) + far(total[4], "gy", True)
    total = total[2] + paired(total[1], "gy", 1) + beyond(total[3], "gy") + distant
    forces = -total[None, :3, None, :]
    return (forces.transpose(0, 2, 1, 3), site)


def solution(mesh):
    in_specs = (
        P("gx", "gy", None, None),
        P("gx", "gy", None),
        P("gx", "gy", None, None),
        P("gx", "gy", None),
        P(),
        P(),
        P(),
        P(),
        P(),
        P(),
        P(),
    )
    out_specs = (P("gx", "gy", None, None), P("gx", "gy", None))
    return jax.shard_map(
        per_device, mesh=mesh, in_specs=in_specs, out_specs=out_specs, check_vma=False
    )
```

```python
import functools
import math

import jax
import jax.numpy as jnp
import numpy as np
from jax import lax
from jax.experimental import pallas as pl
from jax.experimental.pallas import tpu as pltpu
from jax.sharding import PartitionSpec as P

cell_width = 10.0
box_height = 30.0
cut_radius = 50.0
soften = 0.25
screen = 0.5
smear_width = 0.5
WAVE_REACH = 8
F32 = jnp.float32
BF16 = jnp.bfloat16


def paired(block, axis, mask):
    return lax.ppermute(block, axis, [(i ^ mask, i) for i in range(lax.axis_size(axis))])


def other_side(index, count):
    return (index + (1 if index % 2 else -1)) % count


def beyond(block, axis):
    count = lax.axis_size(axis)
    return lax.ppermute(block, axis, [(other_side(i, count), i) for i in range(count)])


def far(block, axis, over_pair):
    count = lax.axis_size(axis)
    if over_pair:
        route = [(other_side(i ^ 1, count), i) for i in range(count)]
    else:
        route = [(other_side(i, count) ^ 1, i) for i in range(count)]
    return lax.ppermute(block, axis, route)


SLOT_CELLS = ((2, 1, 0), (1, 2, 3), (4, 3, 2))


def whole(space=pltpu.VMEM):
    return pl.BlockSpec(memory_space=space)


def run(kernel, outs, args, scratch=(), hbm=0, flops=10_000_000, grant=16, name=None):
    specs = [whole()] * (len(args) - hbm) + [whole(pltpu.HBM)] * hbm
    return list(
        pl.pallas_call(
            kernel,
            out_shape=outs,
            in_specs=specs,
            out_specs=[whole() for _ in outs],
            scratch_shapes=list(scratch),
            compiler_params=pltpu.CompilerParams(vmem_limit_bytes=grant * 1024 * 1024),
            cost_estimate=pl.CostEstimate(
                flops=flops, bytes_accessed=1_000_000, transcendentals=0
            ),
            name=name,
        )(*args)
    )


def shape(*dims, dtype=F32):
    return jax.ShapeDtypeStruct(dims, dtype)


def split(value):
    high = value.astype(BF16)
    return high, (value - high.astype(F32)).astype(BF16)


def dot(left, right, contract=((1,), (0,))):
    return lax.dot_general(left, right, (contract, ((), ())), preferred_element_type=F32)


def dot3(left, right):
    left_high, left_low = split(left)
    right_high, right_low = split(right)
    return dot(left_high, right_high) + (dot(left_high, right_low) + dot(left_low, right_high))


def dot_split(left, right):
    right_high, right_low = split(right)
    return dot(left[0], right_high) + (dot(left[0], right_low) + dot(left[1], right_high))


def sin_cos(turns):
    quarter = jnp.round(turns * 4.0)
    x = (turns - quarter * 0.25) * (2.0 * math.pi)
    z = x * x
    sine = ((-1.9515295891e-4 * z + 8.3321608736e-3) * z - 1.6666654611e-1) * (z * x) + x
    cosine = (2.443315711809948e-5 * z - 1.388731625493765e-3) * z + 4.166664568298827e-2
    cosine = cosine * (z * z) - 0.5 * z + 1.0
    k = quarter.astype(jnp.int32) & 3
    odd = (k & 1) == 1
    by_sine = jnp.where(odd, cosine, sine)
    by_cosine = jnp.where(odd, sine, cosine)
    return (
        jnp.where(k >= 2, -by_sine, by_sine),
        jnp.where((k == 1) | (k == 2), -by_cosine, by_cosine),
    )


def stacked_left(value):
    high = value.astype(BF16).astype(F32)
    rows = jnp.concatenate([high, high, value - high, jnp.zeros_like(high)], axis=0)
    return rows.T.astype(BF16)


def stacked_right(value):
    high = value.astype(BF16).astype(F32)
    return jnp.concatenate([high, value - high, high, jnp.zeros_like(high)], axis=0).astype(BF16)


def silu_pair(value):
    gate = 1.0 / (1.0 + jnp.exp(-value))
    return value * gate, gate * (1.0 + value * (1.0 - gate))


def onehot_kinds(kinds, rows):
    levels = lax.broadcasted_iota(jnp.int32, (rows, kinds.shape[1]), 0).astype(F32)
    return jnp.where(kinds == levels, 1.0, 0.0)


def embedding_stack(embed):
    high = embed.astype(BF16).astype(F32)
    rest = embed - high
    middle = rest.astype(BF16).astype(F32)
    rows = jnp.concatenate([high, middle, rest - middle, jnp.zeros_like(high)], axis=0)
    return rows.T.astype(BF16)


def embedded(stack, kinds):
    hot = onehot_kinds(kinds, 8)
    return dot(stack, jnp.concatenate([hot, hot, hot, jnp.zeros_like(hot)], axis=0).astype(BF16))


def weights_of(stack_ref, part, rows):
    return dot(stack_ref[1 if part else 0], stacked_right(rows))


def mixed(sums, high_ref, low_ref, layer):
    squares = sums[1] * sums[1] + sums[2] * sums[2] + sums[3] * sums[3]
    both = jnp.concatenate([sums[0], squares], axis=0)
    return silu_pair(dot_split((high_ref[layer], low_ref[layer]), both))


def edge_parts(basis, unit):
    return [basis] + [basis * unit[i : i + 1] for i in range(3)]


def pack_kernel(place_ref, position_ref, species_ref, out_ref):
    rows = [position_ref[0, i] for i in range(3)] + [species_ref[0].astype(F32)]
    atoms = rows[0].shape[1]
    out_ref[...] = jnp.concatenate(
        [row[:, s : s + 128] for row in rows for s in range(0, atoms, 128)], axis=0
    )


def pack_more_kernel(place_ref, ids_ref, count_ref, first_ref, out_ref):
    atoms = count_ref.shape[2]
    order = slot_order(ids_ref[...], place_ref, atoms).astype(F32)
    rows = [first_ref[...]]
    rows += [order[:, s : s + 128] for s in range(0, order.shape[1], 128)]
    rows += [count_ref[0, :, s : s + 128].astype(F32) for s in range(0, atoms, 128)]
    missing = out_ref.shape[0] - sum(row.shape[0] for row in rows)
    out_ref[...] = jnp.concatenate(rows + [jnp.zeros((missing, 128), F32)], axis=0)


def block_ids(block, atoms, edges):
    start = 4 * atoms // 128
    middle, end = start + edges // 128, start + edges // 128 + atoms // 128
    rows = [block[r : r + 1] for r in range(start, end)]
    ids = jnp.concatenate(rows[: middle - start], axis=1).astype(jnp.int32)
    return ids, jnp.concatenate(rows[middle - start :], axis=1)


def radial_left(radial):
    high = radial.astype(BF16).astype(F32)
    low = radial - high
    top = jnp.concatenate([high, high], axis=1)
    end = jnp.concatenate([low, jnp.zeros_like(low)], axis=1)
    return jnp.concatenate([top, end], axis=0).astype(BF16)


def put_split(value, high_ref, low_ref, *at):
    high, low = split(value)
    high_ref[at] = high
    low_ref[at] = low


def slot_order(ids, place_ref, atoms):
    cell = ids >> (atoms.bit_length() - 1) if atoms & (atoms - 1) == 0 else ids // atoms
    a = (cell * 11) >> 5
    b = cell - 3 * a
    a = jnp.where((place_ref[0, 0:1, 0:1] & 1) == 0, 2 - a, a)
    b = jnp.where((place_ref[1, 0:1, 0:1] & 1) == 0, 2 - b, b)
    return ids + (3 * a + b - cell) * atoms


def fetch(sources, targets, sems):
    copies = [
        pltpu.make_async_copy(source, target, sems.at[i])
        for i, (source, target) in enumerate(zip(sources, targets))
    ]
    for copy in copies:
        copy.start()
    for copy in copies:
        copy.wait()


def prep_first_kernel(norm, embed_in, radial_in, mixing_in, embed_out, kind_left, left_out, back_out,
                      kind_high, kind_low, mix_high, mix_low, turn_high, turn_low, embed_ref,
                      radial_ref, mixing_ref, sems):
    fetch([embed_in, radial_in, mixing_in], [embed_ref, radial_ref, mixing_ref], sems)
    embed = embed_ref[...]
    kinds = embed.shape[0]
    for path in range(2):
        radial = radial_ref[0, path] * norm
        rows = jnp.concatenate([radial * embed[s : s + 1] for s in range(kinds)], axis=0)
        kind_left[path] = stacked_left(rows)
        put_split(rows, kind_high, kind_low, path)
        radial = radial_ref[1, path] * norm
        left_out[path] = stacked_left(radial)
        back_out[path] = radial_left(radial)
    for layer in range(2):
        scalar, vector = mixing_ref[layer, 0], mixing_ref[layer, 1]
        put_split(jnp.concatenate([scalar.T, vector.T], axis=1), mix_high, mix_low, layer)
        put_split(jnp.concatenate([scalar, 2.0 * vector], axis=0), turn_high, turn_low, layer)
    embed = jnp.concatenate([embed, jnp.zeros((8 - kinds, embed.shape[1]), F32)], axis=0)
    embed_out[...] = embedding_stack(embed)


def prep_second_kernel(read_in, hidden_in, charge_in, read_ref, hidden_high, hidden_low,
                       hidden_turn_high, hidden_turn_low, charge_pair, hidden_ref, charge_ref, sems):
    fetch([read_in, hidden_in, charge_in], [read_ref, hidden_ref, charge_ref], sems)
    put_split(hidden_ref[...].T, hidden_high, hidden_low, Ellipsis)
    put_split(hidden_ref[...], hidden_turn_high, hidden_turn_low, Ellipsis)
    charge = charge_ref[...]
    high = charge.astype(BF16).astype(F32)
    charge_pair[0] = high.astype(BF16)
    charge_pair[1] = (charge - high).astype(BF16)


def hot_beyond_kernel(ids_ref, near_ref, hot_ref):
    ids = ids_ref[1:2, :] - 2 * hot_ref.shape[0]
    for start in range(0, hot_ref.shape[1], 256):
        lanes = slice(start, start + 256)
        hot_ref[:, lanes] = hot_columns(ids[:, lanes], hot_ref.shape[0])


def hot_back_kernel(slots_x, ids_ref, hot_ref):
    edges = ids_ref.shape[1]
    width = hot_ref.shape[1] // len(slots_x)
    entry = lax.broadcasted_iota(jnp.int32, (128, width), 1).astype(F32)
    for start in range(0, edges, 128):
        row = jnp.broadcast_to(ids_ref[1:2, start : start + 128].astype(F32), (8, 128))
        column = row.T[:, 0:1]
        for n, slot in enumerate(slots_x):
            hot_ref[start : start + 128, n * width : (n + 1) * width] = jnp.where(
                column - float(slot * width) == entry, 1.0, 0.0
            ).astype(BF16)


def unfold_block(block, atoms):
    parts = atoms // 128
    rows = [block[r : r + 1] for r in range(4 * parts)]
    return [jnp.concatenate(rows[q * parts : (q + 1) * parts], axis=1) for q in range(4)]


def first_kernel(slots, place_ref, embed_ref, kind_left, mix_high, mix_low, y_beyond_ref, own_ref,
                 y_pair_ref, beyond_ref, column_ref, pair_ref, low_ref, ids_ref, basis_ref, slope_ref,
                 unit_ref, sums_ref, gate_ref):
    atoms = low_ref.shape[2]
    frame = [pair_ref, column_ref, beyond_ref]
    per_cell = atoms // 128
    places = lax.broadcasted_iota(jnp.int32, (4 * per_cell, 128), 0)
    upper = places % per_cell
    kind_of_row = places // per_cell
    to_x = jnp.where(kind_of_row == 0, cell_width, 0.0)
    to_x = jnp.where((place_ref[0] & 1) == 0, to_x, -to_x)
    to_y = jnp.where(kind_of_row == 1, cell_width, 0.0)
    to_y = jnp.where((place_ref[1] & 1) == 0, to_y, -to_y)
    for cell, block_ref in enumerate((y_pair_ref, own_ref, y_beyond_ref)):
        ids, count = block_ids(block_ref[...], atoms, slots * atoms)
        ids_ref[cell : cell + 1, :] = ids
        own = unfold_block(column_ref[cell + 1], atoms)
        step_y = to_y if cell == 1 else -to_y
        rows = []
        for a in range(3):
            for b in range(3):
                block = frame[a][SLOT_CELLS[cell][b]]
                rows.append(block + ((1 - a) * to_x + (1 - b) * step_y))
        first_cell(
            slots, atoms, ids, count, rows, places, upper, own, embed_ref, kind_left, mix_high,
            mix_low, low_ref.at[cell], basis_ref.at[cell], slope_ref.at[cell], unit_ref.at[cell],
            sums_ref.at[cell], gate_ref.at[cell],
        )


def first_cell(slots, atoms, ids, count, rows, places, upper, own, embed_ref, kind_left, mix_high,
               mix_low, low_ref, basis_ref, slope_ref, unit_ref, sums_ref, gate_ref):
    per_cell = atoms // 128
    pieces = []
    for start in range(0, ids.shape[1], 128):
        part = jnp.broadcast_to(ids[:, start : start + 128], places.shape)
        lane, half = part & 127, (part >> 7) - upper
        found = jnp.zeros(places.shape, F32)
        for cell, block in enumerate(rows):
            value = jnp.take_along_axis(block, lane, axis=1)
            found = jnp.where(half == per_cell * cell, value, found)
        total = found
        for s in range(1, per_cell):
            total = total + pltpu.roll(found, 4 * per_cell - s, 0)
        pieces.append(total)
    found = jnp.concatenate(pieces, axis=1)
    found = [found[q * per_cell : q * per_cell + 1] for q in range(4)]
    rel = [found[q] - jnp.concatenate([own[q]] * slots, axis=1) for q in range(3)]
    distance = jnp.sqrt(rel[0] * rel[0] + rel[1] * rel[1] + rel[2] * rel[2] + soften)
    inverse = 1.0 / distance
    order = (lax.broadcasted_iota(jnp.int32, (8, 1), 0) + 1).astype(F32)
    sine, cosine = sin_cos((order * (0.5 / cut_radius)) * distance)
    wave = sine / ((order * (math.pi / cut_radius)) * distance)
    live = jnp.concatenate([jnp.where(count > n, 1.0, 0.0) for n in range(slots)], axis=1)
    basis = wave * live
    basis_ref[...] = basis
    slope_ref[...] = (cosine - wave) * (inverse * live)
    kinds = found[3]
    unit = jnp.concatenate(
        [r * inverse for r in rel] + [inverse, kinds] + [jnp.zeros_like(kinds)] * 3, axis=0
    )
    unit_ref[...] = unit
    stack = embed_ref[...]
    parts = edge_parts(basis, unit)
    species = kind_left.shape[2] // 32
    by_kind = [[None] * species for _ in range(4)]
    for n in range(slots):
        lanes = slice(n * atoms, (n + 1) * atoms)
        kind = jnp.broadcast_to(kinds[:, lanes], (8, atoms))
        for k in range(species):
            match = kind == float(k)
            for part in range(4):
                term = jnp.where(match, parts[part][:, lanes], 0.0)
                old = by_kind[part][k]
                by_kind[part][k] = term if old is None else old + term
    stacks = [stacked_right(jnp.concatenate(rows, axis=0)) for rows in by_kind]
    vectors = dot(kind_left[1], jnp.concatenate(stacks[1:], axis=1))
    sums = [dot(kind_left[0], stacks[0])]
    sums += [vectors[:, i * atoms : (i + 1) * atoms] for i in range(3)]
    step, gate = mixed(sums, mix_high, mix_low, 0)
    low_ref[...] = (embedded(stack, own[3]) + step).astype(BF16)
    for part in range(3):
        sums_ref[part] = sums[part + 1]
    gate_ref[...] = gate


def hot_columns(ids, rows):
    place = lax.broadcasted_iota(jnp.int32, (rows, ids.shape[1]), 0)
    return jnp.where(ids == place, 1.0, 0.0).astype(BF16)


def second_near_kernel(slots, ids_ref, basis_ref, unit_ref, left_ref, column_ref, weight_ref,
                       near_ref):
    atoms = column_ref.shape[2]
    parts = edge_parts(basis_ref[1], unit_ref[1])
    source = jnp.concatenate([column_ref[b] for b in range(3)], axis=1)
    for n in range(slots):
        lanes = slice(n * atoms, (n + 1) * atoms)
        for part in range(4):
            weight_ref[part, :, lanes] = weights_of(left_ref, part, parts[part][:, lanes])
        ids = ids_ref[1:2, lanes] - 3 * atoms
        near_ref[:, lanes] = dot(source, hot_columns(ids, 3 * atoms))


def second_side_kernel(slots, ids_ref, near_ref, pair_ref, out_ref):
    atoms = pair_ref.shape[2]
    source = jnp.concatenate([pair_ref[b] for b in range(3)], axis=1)
    for n in range(slots):
        lanes = slice(n * atoms, (n + 1) * atoms)
        hot = hot_columns(ids_ref[1:2, lanes], 3 * atoms)
        out_ref[:, lanes] = near_ref[:, lanes] + dot(source, hot)


def second_kernel(slots, hot_ref, weight_ref, near_ref, mix_high, mix_low, charge_ref, cell_ref,
                  column_ref, beyond_ref, feature_ref, sums_ref, gate_ref, packed_ref,
                  full_charge_ref, hidden_ref):
    atoms = column_ref.shape[2]
    source = jnp.concatenate([beyond_ref[b] for b in range(3)], axis=1)
    sums = [None] * 4
    for n in range(slots):
        lanes = slice(n * atoms, (n + 1) * atoms)
        feature = near_ref[:, lanes] + dot(source, hot_ref[:, lanes])
        feature_ref[:, lanes] = feature.astype(BF16)
        for part in range(4):
            term = weight_ref[part, :, lanes] * feature
            sums[part] = term if sums[part] is None else sums[part] + term
    step, gate = mixed(sums, mix_high, mix_low, 1)
    hidden = column_ref[1].astype(F32) + step
    hidden_ref[...] = hidden
    for part in range(3):
        sums_ref[part] = sums[part + 1]
    gate_ref[...] = gate
    charge = dot_split((charge_ref[0], charge_ref[1]), hidden)
    full_charge_ref[...] = charge
    place = jnp.concatenate(unfold_block(cell_ref[2], atoms)[:3], axis=0)
    high = place.astype(BF16).astype(F32)
    rest = place - high
    middle = rest.astype(BF16).astype(F32)
    zero = jnp.zeros((packed_ref.shape[0] - charge.shape[0] - 9, atoms), F32)
    packed_ref[...] = jnp.concatenate([charge, high, middle, rest - middle, zero], axis=0).astype(
        BF16
    )


def readout_kernel(hidden_high, hidden_low, turn_high, turn_low, out_ref, hidden_ref, energy_ref,
                   slope_ref):
    hidden = hidden_ref[...]
    value, slope = silu_pair(dot_split((hidden_high[...], hidden_low[...]), hidden))
    out = out_ref[...].T
    energy_ref[...] = jnp.sum(value * out, axis=0, keepdims=True)
    slope_ref[...] = dot_split((turn_high[...], turn_low[...]), slope * out)


def message_grads(cotangent, gate_ref, sums_ref, high_ref, low_ref, layer):
    pre = cotangent * gate_ref[...]
    both = dot_split((high_ref[layer], low_ref[layer]), pre)
    half = both.shape[0] // 2
    return [both[:half]] + [both[half:] * sums_ref[i] for i in range(3)]


def radial_grad(left, value):
    high, low = split(value)
    both = dot(left, jnp.concatenate([high, low], axis=0))
    half = both.shape[0] // 2
    return both[:half] + both[half:]


def second_back_kernel(slots, scale, count, hot_ref, weight_ref, turn_high, turn_low, charge_ref,
                       sums_ref, gate_ref, full_charge_ref, energy_ref, slope_ref, *refs):
    folds, refs = refs[:count], refs[count:]
    site_ref, long_ref, cotangent_ref, grad_ref, term_ref, beyond_ref, pair_ref = refs
    atoms = gate_ref.shape[1]
    total = folds[0][...].astype(F32)
    for part in folds[1:]:
        total = total + part[...].astype(F32)
    wide = full_charge_ref.shape[0]
    potential = total[:wide] * (2.0 * scale)
    slopes = total[wide : wide + 3] + total[wide + 3 : wide + 6] + total[wide + 6 : wide + 9]
    long_ref[...] = jnp.concatenate(
        [slopes * (2.0 * scale), jnp.zeros((5, atoms), F32)], axis=0
    )
    site_ref[0] = energy_ref[...] + 0.5 * jnp.sum(
        full_charge_ref[...] * potential, axis=0, keepdims=True
    )
    high, low = split(potential)
    turned = ((0,), (0,))
    cotangent = slope_ref[...] + (
        dot(charge_ref[0], high, turned)
        + (dot(charge_ref[0], low, turned) + dot(charge_ref[1], high, turned))
    )
    cotangent_ref[...] = cotangent
    grads = message_grads(cotangent, gate_ref, sums_ref, turn_high, turn_low, 1)
    for part in range(4):
        grad_ref[part] = grads[part]
    for n in range(slots):
        lanes = slice(n * atoms, (n + 1) * atoms)
        term = weight_ref[0, :, lanes] * grads[0]
        for part in range(1, 4):
            term = term + weight_ref[part, :, lanes] * grads[part]
        term_ref[:, lanes] = term.astype(BF16)
    for b in range(3):
        start = (3 + b) * atoms
        beyond_ref[b] = dot(term_ref[...], hot_ref[:, start : start + atoms]).astype(BF16)
    for b in range(3):
        pair_ref[b] = dot(term_ref[...], hot_ref[:, b * atoms : (b + 1) * atoms]).astype(BF16)


def second_middle_kernel(hot_ref, term_ref, cotangent_ref, middle_ref):
    atoms = cotangent_ref.shape[1]
    for b in range(3):
        grad = dot(term_ref[...], hot_ref[:, b * atoms : (b + 1) * atoms])
        middle_ref[b] = grad + cotangent_ref[...] if b == 1 else grad


def second_edge_kernel(slots, back_ref, feature_ref, grad_ref, edge_ref):
    atoms = grad_ref.shape[2]
    for n in range(slots):
        lanes = slice(n * atoms, (n + 1) * atoms)
        feature = feature_ref[:, lanes].astype(F32)
        for part in range(4):
            edge_ref[8 * part : 8 * part + 8, lanes] = radial_grad(
                back_ref[1 if part else 0], grad_ref[part] * feature
            )


def first_back_kernel(slots, ids_ref, basis_ref, slope_ref, unit_ref, kind_high, kind_low, turn_high,
                      turn_low, sums_ref, gate_ref, edge_ref, long_ref, middle_ref, from_pair,
                      from_beyond, *outs):
    sums = {(1, 2): long_ref[...]}
    for cell in range(3):
        cotangent = middle_ref[cell] + (
            from_pair[cell].astype(F32) + from_beyond[cell].astype(F32)
        )
        own, found = first_back_cell(
            slots, ids_ref[cell : cell + 1, :], basis_ref.at[cell], slope_ref.at[cell],
            unit_ref.at[cell], kind_high, kind_low, turn_high, turn_low, sums_ref.at[cell],
            gate_ref.at[cell], edge_ref if cell == 1 else None, cotangent,
        )
        terms = [((1, cell + 1), own)]
        terms += [((n // 3, SLOT_CELLS[cell][n % 3]), found[n]) for n in range(9)]
        for key, term in terms:
            sums[key] = sums[key] + term if key in sums else term
    for x in range(3):
        rows = [sums[(x, y)][:3] for y in range(5)]
        outs[x][...] = jnp.concatenate(rows + [jnp.zeros((1, rows[0].shape[1]), F32)], axis=0)


def first_back_cell(slots, ids, basis_ref, slope_ref, unit_ref, kind_high, kind_low, turn_high,
                    turn_low, sums_ref, gate_ref, edge_ref, cotangent):
    atoms = gate_ref.shape[1]
    pre = cotangent * gate_ref[...]
    both = dot_split((turn_high[0], turn_low[0]), pre)
    wide = both.shape[0] // 2
    grads = [both[:wide]] + [both[wide:] * sums_ref[i] for i in range(3)]
    unit = unit_ref[...]
    kinds = unit[4:5]
    by_kind = [dot_split((kind_high[0], kind_low[0]), grads[0])]
    by_kind += [dot_split((kind_high[1], kind_low[1]), grads[i]) for i in range(1, 4)]
    species = by_kind[0].shape[0] // 8
    edges = [[] for _ in range(4)]
    for n in range(slots):
        kind = jnp.broadcast_to(kinds[:, n * atoms : (n + 1) * atoms], (8, atoms))
        matches = [kind == float(k) for k in range(1, species)]
        for part in range(4):
            rows = by_kind[part]
            found = rows[:8]
            for k, match in enumerate(matches):
                found = jnp.where(match, rows[8 * k + 8 : 8 * k + 16], found)
            edges[part].append(found)
    edges = [jnp.concatenate(rows, axis=1) for rows in edges]
    if edge_ref is not None:
        edges = [edge_ref[8 * part : 8 * part + 8] + edges[part] for part in range(4)]
    basis = basis_ref[...]
    units = [unit[i : i + 1] for i in range(3)]
    inverse = unit[3:4]
    by_basis = edges[0]
    for i in range(3):
        by_basis = by_basis + edges[i + 1] * units[i]
    by_unit = [jnp.sum(edges[i + 1] * basis, axis=0, keepdims=True) * inverse for i in range(3)]
    by_distance = jnp.sum(by_basis * slope_ref[...], axis=0, keepdims=True)
    for i in range(3):
        by_distance = by_distance - by_unit[i] * units[i]
    moves = [by_unit[i] + by_distance * units[i] for i in range(3)]
    zero = jnp.zeros_like(moves[0])
    move = jnp.concatenate(moves + [zero] * 5, axis=0)
    own = -move[:, :atoms]
    for n in range(1, slots):
        own = own - move[:, n * atoms : (n + 1) * atoms]
    lane_hot = hot_columns(ids & 127, 128)
    half = ids >> 7
    high = move.astype(BF16).astype(F32)
    both = jnp.concatenate([high, move - high], axis=0)
    per_cell = atoms // 128
    rows = jnp.concatenate(
        [jnp.where(half == h, both, 0.0).astype(BF16) for h in range(9 * per_cell)], axis=0
    )
    spread = dot(rows, lane_hot, ((1,), (1,)))
    grads = []
    for cell in range(9):
        found = []
        for h in range(cell * per_cell, (cell + 1) * per_cell):
            found.append(spread[16 * h : 16 * h + 8] + spread[16 * h + 8 : 16 * h + 16])
        grads.append(jnp.concatenate(found, axis=1))
    return own, grads


def pair_counts(parts):
    total = WAVE_REACH + WAVE_REACH * (2 * WAVE_REACH + 1)
    share = -(-total // parts)
    return total, share, -(-share // 16) * 16


def pair_vectors(slot, share, part):
    side = 2 * WAVE_REACH + 1
    total = WAVE_REACH + WAVE_REACH * side
    index = slot + part.astype(F32) * share
    later = index - WAVE_REACH
    row = jnp.floor((later + 0.5) * (1.0 / side))
    first = index < WAVE_REACH
    kx = jnp.where(first, 0.0, row + 1.0)
    ky = jnp.where(first, index + 1.0, later - row * side - WAVE_REACH)
    valid = jnp.where((slot < share) & (index < total), 1.0, 0.0)
    return kx, ky, valid


def count_up(rows):
    return lax.broadcasted_iota(jnp.int32, (rows, 1), 0).astype(F32)


def green_weights(share, padded, grid, place_ref, vec_ref, weight_ref):
    grid_x, grid_y = grid
    turn = 2.0 * math.pi
    side = 2 * WAVE_REACH + 1
    top = side * side * side - 1
    vec = vec_ref[...].astype(F32) + WAVE_REACH
    code = (vec[0:1] * side + vec[1:2]) * side + vec[2:3]
    code = jnp.maximum(code, top - code)
    span = 8 * share
    row = count_up(span)
    slot = jnp.floor(row * 0.125)
    height = row - 8.0 * slot + 1.0
    flat = count_up(padded)
    slot = jnp.concatenate([slot, slot, flat], axis=0)
    kz = jnp.concatenate([height, -height, jnp.zeros_like(flat)], axis=0)
    kx, ky, valid = pair_vectors(slot, share, place_ref[0, 0:1, 0:1])
    own = ((kx + WAVE_REACH) * side + ky + WAVE_REACH) * side + kz + WAVE_REACH
    seen = jnp.zeros((own.shape[0], 128), F32)
    for start in range(0, code.shape[1], 128):
        seen = seen + jnp.where(own == code[:, start : start + 128], 1.0, 0.0)
    count = jnp.sum(seen, axis=1, keepdims=True) * valid
    sq = (
        (kx * (turn / (grid_x * cell_width))) ** 2
        + (ky * (turn / (grid_y * cell_width))) ** 2
        + (kz * (turn / box_height)) ** 2
    )
    green = jnp.exp(-smear_width * sq) / (sq + screen * screen) * count
    weight_ref[...] = jnp.broadcast_to(green, weight_ref.shape)


def basis_rows(share, ca, sa, cb, sb):
    cc, ss, sc, cs = [], [], [], []
    for p in range(share):
        c, s = ca[p : p + 1], sa[p : p + 1]
        cc.append(c * cb)
        ss.append(s * sb)
        sc.append(s * cb)
        cs.append(c * sb)
    return cc, ss, sc, cs


def unpack_rows(block):
    half = block.shape[1] // 2
    return jnp.concatenate([block[:, :half], block[:, half:]], axis=0)


def pack_rows(block):
    half = block.shape[0] // 2
    return jnp.concatenate([block[:half], block[half:]], axis=1)


def structure_kernel(share, padded, grid, wide, flip, place_ref, blocks, *refs):
    grid_x, grid_y = grid
    if flip:
        near_ref, (ca_ref, sa_ref, cb_ref, sb_ref, high_ref, low_ref, own_ref, out_ref) = (
            refs[0],
            refs[1:],
        )
        total = near_ref[...]
    else:
        ca_ref, sa_ref, cb_ref, sb_ref, high_ref, low_ref, total_ref = refs
        total = None
    col = place_ref[1, 0:1, 0:1].astype(F32) * (1.0 / grid_y)
    first = place_ref[0, 0:1, 0:1] ^ flip
    kx, ky, _ = pair_vectors(count_up(padded), share, place_ref[0, 0:1, 0:1])
    kz = count_up(8) + 1.0
    for d in range(grid_x // 2):
        block = blocks[d]
        charge = block[:wide]
        atoms = charge.shape[1]
        pieces = block[wide:].astype(F32)
        place = pieces[0:3] + (pieces[3:6] + pieces[6:9])
        row = (first ^ (2 * d)).astype(F32) * (1.0 / grid_x)
        x = place[0:1] * (1.0 / (grid_x * cell_width)) + row
        y = place[1:2] * (1.0 / (grid_y * cell_width)) + col
        sa, ca = sin_cos(kx * x + ky * y)
        sb, cb = sin_cos(kz * (place[2:3] * (1.0 / box_height)))
        lanes = pl.ds(d * atoms, atoms)
        ca_ref[:, lanes] = ca
        sa_ref[:, lanes] = sa
        cb_ref[:, lanes] = cb
        sb_ref[:, lanes] = sb
        cc, ss, sc, cs = basis_rows(share, ca, sa, cb, sb)
        high, low = split(jnp.concatenate(cc + ss + sc + cs + [ca, sa], axis=0))
        high_ref[:, lanes] = high
        low_ref[:, lanes] = low
        term = dot(high, charge, ((1,), (1,))) + dot(low, charge, ((1,), (1,)))
        total = term if total is None else total + term
    if flip:
        packed = pack_rows(total)
        own_ref[...] = packed
        out_ref[...] = packed.astype(BF16)
    else:
        total_ref[...] = total


def weighted_rows(share, padded, wide, weight_ref, parts):
    packed = parts[0][...].astype(F32)
    for part in parts[1:]:
        packed = packed + part[...].astype(F32)
    struct = unpack_rows(packed)
    span = 8 * share
    cc, ss, sc, cs = (struct[i * span : (i + 1) * span] for i in range(4))
    weight = weight_ref[:, :wide]
    plus, minus, flat = weight[:span], weight[span : 2 * span], weight[2 * span :]
    re_plus, im_plus = plus * (cc - ss), plus * (sc + cs)
    re_minus, im_minus = minus * (cc + ss), minus * (sc - cs)
    rows = jnp.concatenate(
        [
            re_plus + re_minus,
            re_minus - re_plus,
            im_plus + im_minus,
            im_plus - im_minus,
            flat * struct[4 * span : 4 * span + padded],
            flat * struct[4 * span + padded :],
        ],
        axis=0,
    )
    return rows


def fold_kernel(share, padded, grid, wide, flip, place_ref, *refs):
    grid_x, grid_y = grid
    turn = 2.0 * math.pi
    if flip:
        weight_ref, parts, refs = refs[0], refs[1 : 1 + grid_y], refs[1 + grid_y :]
        rows = weighted_rows(share, padded, wide, weight_ref, parts)
        refs, rows_ref = refs[:-1], refs[-1]
        rows_ref[...] = rows
    else:
        rows, refs = refs[0][...], refs[1:]
    ca_ref, sa_ref, cb_ref, sb_ref, high_ref, low_ref, blocks, out_ref = refs
    row_high, row_low = split(rows)
    row_pair = jnp.concatenate([row_high, row_low], axis=1)
    turned = rows.T
    t_high, t_low = split(turned)
    t_both = jnp.concatenate([t_high, t_low], axis=0)
    span = 8 * share
    kx, ky, _ = pair_vectors(count_up(padded), share, place_ref[0, 0:1, 0:1])
    kx = kx * (turn / (grid_x * cell_width))
    ky = ky * (turn / (grid_y * cell_width))
    kz = (count_up(8) + 1.0) * (turn / box_height)
    for d in range(grid_x // 2):
        charge = blocks[d][:wide]
        atoms = charge.shape[1]
        lanes = pl.ds(d * atoms, atoms)
        ca, sa, cb, sb = ca_ref[:, lanes], sa_ref[:, lanes], cb_ref[:, lanes], sb_ref[:, lanes]
        bcc, bss, bsc, bcs = basis_rows(share, ca, sa, cb, sb)
        high, low = high_ref[:, lanes], low_ref[:, lanes]
        both = dot(t_both, high)
        pot = both[:wide] + both[wide:] + dot(t_high, low)
        proj = dot(row_pair, jnp.concatenate([charge, charge], axis=0))
        by_x = jnp.zeros((8, atoms), jnp.float32)
        by_y = jnp.zeros((8, atoms), jnp.float32)
        by_z = jnp.zeros((8, atoms), jnp.float32)
        for p in range(share):
            pcc, pss, psc, pcs = (
                proj[i * span + 8 * p : i * span + 8 * p + 8] for i in range(4)
            )
            slope = bcs[p] * pss - bsc[p] * pcc + bcc[p] * psc - bss[p] * pcs
            by_x = by_x + kx[p : p + 1] * slope
            by_y = by_y + ky[p : p + 1] * slope
            by_z = by_z + (bsc[p] * pss - bcs[p] * pcc - bss[p] * psc + bcc[p] * pcs)
        flat_slope = ca * proj[4 * span + padded :] - sa * proj[4 * span : 4 * span + padded]
        grad_x = jnp.sum(by_x, axis=0, keepdims=True) + jnp.sum(kx * flat_slope, axis=0, keepdims=True)
        grad_y = jnp.sum(by_y, axis=0, keepdims=True) + jnp.sum(ky * flat_slope, axis=0, keepdims=True)
        grad_z = jnp.sum(kz * by_z, axis=0, keepdims=True)
        slopes = jnp.concatenate([grad_x, grad_y, grad_z], axis=0)
        out_ref[d] = pieced(pot, slopes, out_ref.shape[1]).astype(out_ref.dtype)


def pieced(pot, slopes, rows):
    high = slopes.astype(BF16).astype(F32)
    rest = slopes - high
    middle = rest.astype(BF16).astype(F32)
    zero = jnp.zeros((rows - pot.shape[0] - 9, pot.shape[1]), F32)
    return jnp.concatenate([pot, high, middle, rest - middle, zero], axis=0)


def unpieced(block, wide):
    slopes = block[wide : wide + 3] + (block[wide + 3 : wide + 6] + block[wide + 6 : wide + 9])
    return block[:wide], slopes


def join_kernel(wide, near_ref, far_ref, own_ref, *outs):
    for d in range(near_ref.shape[0]):
        pot, slopes = unpieced(near_ref[d], wide)
        pot_far, slopes_far = unpieced(far_ref[d].astype(F32), wide)
        block = pieced(pot + pot_far, slopes + slopes_far, near_ref.shape[1])
        if d:
            outs[d - 1][...] = block.astype(BF16)
        else:
            own_ref[...] = block


def per_device(
    positions,
    species,
    neighbours,
    counts,
    species_embed,
    radial,
    mixing,
    read_hidden,
    read_out,
    charge_map,
    wavevectors,
):
    atoms = positions.shape[3]
    slots = neighbours.shape[3]
    features, lat_width = charge_map.shape
    wave_count = wavevectors.shape[1]
    grid = lax.axis_size("gx"), lax.axis_size("gy")
    grid_x, grid_y = grid
    edges = slots * atoms
    scale = 1.0 / math.sqrt(wave_count * lat_width * atoms * grid_x * grid_y)
    place = jnp.stack([lax.axis_index("gx"), lax.axis_index("gy")]).astype(jnp.int32)
    place = jnp.broadcast_to(place[:, None, None], (2, 8, 128))
    _, share, padded = pair_counts(grid_x)
    ids = neighbours.transpose(0, 3, 1, 2).reshape(1, edges)
    cell_rows = 4 * atoms // 128
    block_total = -(-(cell_rows + (edges + atoms) // 128) // 8) * 8
    dma = pltpu.SemaphoreType.DMA
    shown = positions.transpose(0, 2, 1, 3)
    (own_place,) = run(
        pack_kernel,
        [shape(cell_rows, 128)],
        [place, shown, species],
        flops=10_000_000_000,
        name="pack",
    )
    (own,) = run(
        pack_more_kernel,
        [shape(block_total, 128)],
        [place, ids, counts, own_place],
        name="pack_more",
    )
    y_beyond, y_pair = beyond(own, "gy"), paired(own, "gy", 1)
    over_pair = far(own_place, "gy", True)
    over_beyond = over_pair if grid_y == 4 else far(own_place, "gy", False)
    cells = jnp.stack(
        [over_pair, y_pair[:cell_rows], own_place, y_beyond[:cell_rows], over_beyond]
    )
    x_beyond, x_pair = beyond(cells, "gx"), paired(cells, "gx", 1)
    cells = [x_pair, cells, x_beyond]

    norm = 1.0 / math.sqrt(slots)
    kind_rows = 8 * species_embed.shape[0]
    low_pair = lambda *dims: [shape(*dims, dtype=BF16)] * 2
    embed, kind_left, left, back, kind_high, kind_low, mix_high, mix_low, turn_high, turn_low = run(
        functools.partial(prep_first_kernel, norm),
        [
            shape(features, 32, dtype=BF16),
            shape(2, features, 4 * kind_rows, dtype=BF16),
            shape(2, features, 32, dtype=BF16),
            shape(2, 16, 2 * features, dtype=BF16),
        ]
        + low_pair(2, kind_rows, features)
        + low_pair(2, features, 2 * features)
        + low_pair(2, 2 * features, features),
        [species_embed, radial, mixing],
        scratch=[
            pltpu.VMEM(species_embed.shape, F32),
            pltpu.VMEM(radial.shape, F32),
            pltpu.VMEM(mixing.shape, F32),
            dma((3,)),
        ],
        hbm=3,
        name="prep_first",
    )
    read_out, hidden_high, hidden_low, hidden_turn_high, hidden_turn_low, charge_pair = run(
        prep_second_kernel,
        [shape(1, features)]
        + low_pair(features, features)
        + low_pair(features, features)
        + [shape(2, lat_width, features, dtype=BF16)],
        [read_out[None, :], read_hidden, charge_map.T],
        scratch=[
            pltpu.VMEM(read_hidden.shape, F32),
            pltpu.VMEM((lat_width, features), F32),
            dma((3,)),
        ],
        hbm=3,
        name="prep_second",
    )
    cells, hidden_high = lax.optimization_barrier((cells, hidden_high))
    low, ids, basis, slope, unit, sums_one, gate_one = run(
        functools.partial(first_kernel, slots),
        [
            shape(3, features, atoms, dtype=BF16),
            shape(3, edges, dtype=jnp.int32),
            shape(3, 8, edges),
            shape(3, 8, edges),
            shape(3, 8, edges),
            shape(3, 3, features, atoms),
            shape(3, features, atoms),
        ],
        [place, embed, kind_left, mix_high, mix_low, y_beyond, own, y_pair] + cells[::-1],
        name="first",
    )
    hidden = [paired(low, "gx", 1), low, beyond(low, "gx")]
    edge_weights, near = run(
        functools.partial(second_near_kernel, slots),
        [shape(4, features, edges), shape(features, edges)],
        [ids, basis, unit, left, low],
        flops=2_000_000_000,
        name="second_near",
    )
    (hot_beyond,) = run(
        hot_beyond_kernel,
        [shape(3 * atoms, edges, dtype=BF16)],
        [ids, near],
        flops=1_000_000,
        name="hot_beyond",
    )
    (near,) = run(
        functools.partial(second_side_kernel, slots),
        [shape(features, edges)],
        [ids, near, hidden[0]],
        flops=1_000_000_000,
        name="second_side",
    )
    block_rows = -(-(lat_width + 9) // 16) * 16
    feature, sums_two, gate_two, packed, charge, hidden_two = run(
        functools.partial(second_kernel, slots),
        [
            shape(features, edges, dtype=BF16),
            shape(3, features, atoms),
            shape(features, atoms),
            shape(block_rows, atoms, dtype=BF16),
            shape(lat_width, atoms),
            shape(features, atoms),
        ],
        [hot_beyond, edge_weights, near, mix_high, mix_low, charge_pair, cells[1], hidden[1],
         hidden[2]],
        name="second",
    )
    energy, energy_slope = run(
        readout_kernel,
        [shape(1, atoms), shape(features, atoms)],
        [hidden_high, hidden_low, hidden_turn_high, hidden_turn_low, read_out, hidden_two],
        name="readout",
    )
    half = grid_x // 2
    near_charges = jnp.stack([packed] + [paired(packed, "gx", 2 * d) for d in range(1, half)])
    (weight,) = run(
        functools.partial(green_weights, share, padded, grid),
        [shape(16 * share + padded, 128)],
        [place, wavevectors],
        name="green",
    )
    near_charges, weight = lax.optimization_barrier((near_charges, weight))
    far_charges = paired(near_charges, "gx", 1)
    span = half * atoms
    rows = 32 * share + 2 * padded
    phase_shapes = [
        shape(padded, span),
        shape(padded, span),
        shape(8, span),
        shape(8, span),
        shape(rows, span, dtype=BF16),
        shape(rows, span, dtype=BF16),
    ]
    *near_phases, near_total = run(
        functools.partial(structure_kernel, share, padded, grid, lat_width, 0),
        phase_shapes + [shape(rows, lat_width)],
        [place, near_charges],
        flops=1_000_000_000,
        name="structure_near",
    )
    *far_phases, own_part, part = run(
        functools.partial(structure_kernel, share, padded, grid, lat_width, 1),
        phase_shapes
        + [
            shape(rows // 2, 2 * lat_width),
            shape(rows // 2, 2 * lat_width, dtype=BF16),
        ],
        [place, far_charges, near_total],
        name="structure_far",
    )
    parts = [own_part] + [paired(part, "gy", d) for d in range(1, grid_y)]
    (hot_back,) = run(
        functools.partial(hot_back_kernel, (0, 2)),
        [shape(edges, 6 * atoms, dtype=BF16)],
        [ids],
        flops=2_000_000_000,
        name="hot_back",
    )
    parts, hot_back = lax.optimization_barrier((parts, hot_back))
    far_folds, wave_rows = run(
        functools.partial(fold_kernel, share, padded, grid, lat_width, 1),
        [shape(half, block_rows, atoms, dtype=BF16), shape(rows, lat_width)],
        [place, weight] + parts + far_phases + [far_charges],
        name="fold_far",
    )
    far_folds = paired(far_folds, "gx", 1)
    (near_folds,) = run(
        functools.partial(fold_kernel, share, padded, grid, lat_width, 0),
        [shape(half, block_rows, atoms)],
        [place, wave_rows] + near_phases + [near_charges],
        flops=1_000_000_000,
        name="fold_near",
    )
    folds = run(
        functools.partial(join_kernel, lat_width),
        [shape(block_rows, atoms)] + [shape(block_rows, atoms, dtype=BF16)] * (half - 1),
        [near_folds, far_folds],
        name="fold_join",
    )
    folds = [folds[0]] + [paired(folds[d], "gx", 2 * d) for d in range(1, half)]

    site, long, cotangent, grads, term, to_beyond, to_pair = run(
        functools.partial(second_back_kernel, slots, scale, half),
        [
            shape(1, 1, atoms),
            shape(8, atoms),
            shape(features, atoms),
            shape(4, features, atoms),
            shape(features, edges, dtype=BF16),
            shape(3, features, atoms, dtype=BF16),
            shape(3, features, atoms, dtype=BF16),
        ],
        [hot_back, edge_weights, turn_high, turn_low, charge_pair, sums_two, gate_two, charge,
         energy, energy_slope] + folds,
        name="second_back",
    )
    from_pair, from_beyond = paired(to_pair, "gx", 1), beyond(to_beyond, "gx")
    (hot_middle,) = run(
        functools.partial(hot_back_kernel, (1,)),
        [shape(edges, 3 * atoms, dtype=BF16)],
        [ids],
        flops=1_000_000_000,
        name="hot_middle",
    )
    (middle,) = run(
        second_middle_kernel,
        [shape(3, features, atoms)],
        [hot_middle, term, cotangent],
        flops=1_000_000_000,
        name="second_middle",
    )
    (edge,) = run(
        functools.partial(second_edge_kernel, slots),
        [shape(32, edges)],
        [back, feature, grads],
        flops=1_000_000_000,
        name="second_edge",
    )
    to_pair, middle, to_beyond = run(
        functools.partial(first_back_kernel, slots),
        [shape(16, atoms)] * 3,
        [ids, basis, slope, unit, kind_high, kind_low, turn_high, turn_low, sums_one, gate_one, edge,
         long, middle, from_pair, from_beyond],
        name="first_back",
    )
    total = middle + paired(to_pair, "gx", 1) + beyond(to_beyond, "gx")
    total = [total[3 * y : 3 * y + 3] for y in range(5)]
    if grid_y == 4:
        distant = far(total[0] + total[4], "gy", True)
    else:
        distant = far(total[0], "gy", False) + far(total[4], "gy", True)
    total = total[2] + paired(total[1], "gy", 1) + beyond(total[3], "gy") + distant
    forces = -total[None, :, None, :]
    return (forces.transpose(0, 2, 1, 3), site)


def solution(mesh):
    in_specs = (
        P("gx", "gy", None, None),
        P("gx", "gy", None),
        P("gx", "gy", None, None),
        P("gx", "gy", None),
        P(),
        P(),
        P(),
        P(),
        P(),
        P(),
        P(),
    )
    out_specs = (P("gx", "gy", None, None), P("gx", "gy", None))
    return jax.shard_map(
        per_device, mesh=mesh, in_specs=in_specs, out_specs=out_specs, check_vma=False
    )
```

```python
import functools
import math

import jax
import jax.numpy as jnp
import numpy as np
from jax import lax
from jax.experimental import pallas as pl
from jax.experimental.pallas import tpu as pltpu
from jax.sharding import PartitionSpec as P

cell_width = 10.0
box_height = 30.0
cut_radius = 50.0
soften = 0.25
screen = 0.5
smear_width = 0.5
WAVE_REACH = 8
F32 = jnp.float32
BF16 = jnp.bfloat16


def paired(block, axis, mask):
    return lax.ppermute(block, axis, [(i ^ mask, i) for i in range(lax.axis_size(axis))])


def other_side(index, count):
    return (index + (1 if index % 2 else -1)) % count


def beyond(block, axis):
    count = lax.axis_size(axis)
    return lax.ppermute(block, axis, [(other_side(i, count), i) for i in range(count)])


def far(block, axis, over_pair):
    count = lax.axis_size(axis)
    if over_pair:
        route = [(other_side(i ^ 1, count), i) for i in range(count)]
    else:
        route = [(other_side(i, count) ^ 1, i) for i in range(count)]
    return lax.ppermute(block, axis, route)


SLOT_CELLS = ((2, 1, 0), (1, 2, 3), (4, 3, 2))


def whole(space=pltpu.VMEM):
    return pl.BlockSpec(memory_space=space)


def run(kernel, outs, args, scratch=(), hbm=0, flops=10_000_000, grant=16, name=None):
    specs = [whole()] * (len(args) - hbm) + [whole(pltpu.HBM)] * hbm
    return list(
        pl.pallas_call(
            kernel,
            out_shape=outs,
            in_specs=specs,
            out_specs=[whole() for _ in outs],
            scratch_shapes=list(scratch),
            compiler_params=pltpu.CompilerParams(vmem_limit_bytes=grant * 1024 * 1024),
            cost_estimate=pl.CostEstimate(
                flops=flops, bytes_accessed=1_000_000, transcendentals=0
            ),
            name=name,
        )(*args)
    )


def shape(*dims, dtype=F32):
    return jax.ShapeDtypeStruct(dims, dtype)


def split(value):
    high = value.astype(BF16)
    return high, (value - high.astype(F32)).astype(BF16)


def dot(left, right, contract=((1,), (0,))):
    return lax.dot_general(left, right, (contract, ((), ())), preferred_element_type=F32)


def dot3(left, right):
    left_high, left_low = split(left)
    right_high, right_low = split(right)
    return dot(left_high, right_high) + (dot(left_high, right_low) + dot(left_low, right_high))


def dot_split(left, right):
    right_high, right_low = split(right)
    return dot(left[0], right_high) + (dot(left[0], right_low) + dot(left[1], right_high))


def sin_cos(turns):
    quarter = jnp.round(turns * 4.0)
    x = (turns - quarter * 0.25) * (2.0 * math.pi)
    z = x * x
    sine = ((-1.9515295891e-4 * z + 8.3321608736e-3) * z - 1.6666654611e-1) * (z * x) + x
    cosine = (2.443315711809948e-5 * z - 1.388731625493765e-3) * z + 4.166664568298827e-2
    cosine = cosine * (z * z) - 0.5 * z + 1.0
    k = quarter.astype(jnp.int32) & 3
    odd = (k & 1) == 1
    by_sine = jnp.where(odd, cosine, sine)
    by_cosine = jnp.where(odd, sine, cosine)
    return (
        jnp.where(k >= 2, -by_sine, by_sine),
        jnp.where((k == 1) | (k == 2), -by_cosine, by_cosine),
    )


def stacked_left(value):
    high = value.astype(BF16).astype(F32)
    rows = jnp.concatenate([high, high, value - high, jnp.zeros_like(high)], axis=0)
    return rows.T.astype(BF16)


def stacked_right(value):
    high = value.astype(BF16).astype(F32)
    return jnp.concatenate([high, value - high, high, jnp.zeros_like(high)], axis=0).astype(BF16)


def silu_pair(value):
    gate = 1.0 / (1.0 + jnp.exp(-value))
    return value * gate, gate * (1.0 + value * (1.0 - gate))


def onehot_kinds(kinds, rows):
    levels = lax.broadcasted_iota(jnp.int32, (rows, kinds.shape[1]), 0).astype(F32)
    return jnp.where(kinds == levels, 1.0, 0.0)


def embedding_stack(embed):
    high = embed.astype(BF16).astype(F32)
    rest = embed - high
    middle = rest.astype(BF16).astype(F32)
    rows = jnp.concatenate([high, middle, rest - middle, jnp.zeros_like(high)], axis=0)
    return rows.T.astype(BF16)


def embedded(stack, kinds):
    hot = onehot_kinds(kinds, 8)
    return dot(stack, jnp.concatenate([hot, hot, hot, jnp.zeros_like(hot)], axis=0).astype(BF16))


def weights_of(stack_ref, part, rows):
    return dot(stack_ref[1 if part else 0], stacked_right(rows))


def mixed(sums, high_ref, low_ref, layer):
    squares = sums[1] * sums[1] + sums[2] * sums[2] + sums[3] * sums[3]
    both = jnp.concatenate([sums[0], squares], axis=0)
    return silu_pair(dot_split((high_ref[layer], low_ref[layer]), both))


def edge_parts(basis, unit):
    return [basis] + [basis * unit[i : i + 1] for i in range(3)]


def pack_kernel(place_ref, position_ref, species_ref, out_ref):
    rows = [position_ref[0, i] for i in range(3)] + [species_ref[0].astype(F32)]
    atoms = rows[0].shape[1]
    out_ref[...] = jnp.concatenate(
        [row[:, s : s + 128] for row in rows for s in range(0, atoms, 128)], axis=0
    )


def pack_more_kernel(place_ref, ids_ref, count_ref, first_ref, out_ref):
    atoms = count_ref.shape[2]
    order = slot_order(ids_ref[...], place_ref, atoms).astype(F32)
    rows = [first_ref[...]]
    rows += [order[:, s : s + 128] for s in range(0, order.shape[1], 128)]
    rows += [count_ref[0, :, s : s + 128].astype(F32) for s in range(0, atoms, 128)]
    missing = out_ref.shape[0] - sum(row.shape[0] for row in rows)
    out_ref[...] = jnp.concatenate(rows + [jnp.zeros((missing, 128), F32)], axis=0)


def block_ids(block, atoms, edges):
    start = 4 * atoms // 128
    middle, end = start + edges // 128, start + edges // 128 + atoms // 128
    rows = [block[r : r + 1] for r in range(start, end)]
    ids = jnp.concatenate(rows[: middle - start], axis=1).astype(jnp.int32)
    return ids, jnp.concatenate(rows[middle - start :], axis=1)


def radial_left(radial):
    high = radial.astype(BF16).astype(F32)
    low = radial - high
    top = jnp.concatenate([high, high], axis=1)
    end = jnp.concatenate([low, jnp.zeros_like(low)], axis=1)
    return jnp.concatenate([top, end], axis=0).astype(BF16)


def put_split(value, high_ref, low_ref, *at):
    high, low = split(value)
    high_ref[at] = high
    low_ref[at] = low


def slot_order(ids, place_ref, atoms):
    cell = ids >> (atoms.bit_length() - 1) if atoms & (atoms - 1) == 0 else ids // atoms
    a = (cell * 11) >> 5
    b = cell - 3 * a
    a = jnp.where((place_ref[0, 0:1, 0:1] & 1) == 0, 2 - a, a)
    b = jnp.where((place_ref[1, 0:1, 0:1] & 1) == 0, 2 - b, b)
    return ids + (3 * a + b - cell) * atoms


def fetch(sources, targets, sems):
    copies = [
        pltpu.make_async_copy(source, target, sems.at[i])
        for i, (source, target) in enumerate(zip(sources, targets))
    ]
    for copy in copies:
        copy.start()
    for copy in copies:
        copy.wait()


def prep_first_kernel(norm, embed_in, radial_in, mixing_in, embed_out, kind_left, left_out, back_out,
                      kind_high, kind_low, mix_high, mix_low, turn_high, turn_low, embed_ref,
                      radial_ref, mixing_ref, sems):
    fetch([embed_in, radial_in, mixing_in], [embed_ref, radial_ref, mixing_ref], sems)
    embed = embed_ref[...]
    kinds = embed.shape[0]
    for path in range(2):
        radial = radial_ref[0, path] * norm
        rows = jnp.concatenate([radial * embed[s : s + 1] for s in range(kinds)], axis=0)
        kind_left[path] = stacked_left(rows)
        put_split(rows, kind_high, kind_low, path)
        radial = radial_ref[1, path] * norm
        left_out[path] = stacked_left(radial)
        back_out[path] = radial_left(radial)
    for layer in range(2):
        scalar, vector = mixing_ref[layer, 0], mixing_ref[layer, 1]
        put_split(jnp.concatenate([scalar.T, vector.T], axis=1), mix_high, mix_low, layer)
        put_split(jnp.concatenate([scalar, 2.0 * vector], axis=0), turn_high, turn_low, layer)
    embed = jnp.concatenate([embed, jnp.zeros((8 - kinds, embed.shape[1]), F32)], axis=0)
    embed_out[...] = embedding_stack(embed)


def prep_second_kernel(read_in, hidden_in, charge_in, read_ref, hidden_high, hidden_low,
                       hidden_turn_high, hidden_turn_low, charge_pair, hidden_ref, charge_ref, sems):
    fetch([read_in, hidden_in, charge_in], [read_ref, hidden_ref, charge_ref], sems)
    put_split(hidden_ref[...].T, hidden_high, hidden_low, Ellipsis)
    put_split(hidden_ref[...], hidden_turn_high, hidden_turn_low, Ellipsis)
    charge = charge_ref[...]
    high = charge.astype(BF16).astype(F32)
    charge_pair[0] = high.astype(BF16)
    charge_pair[1] = (charge - high).astype(BF16)


def hot_beyond_kernel(ids_ref, near_ref, hot_ref):
    ids = ids_ref[1:2, :] - 2 * hot_ref.shape[0]
    for start in range(0, hot_ref.shape[1], 256):
        lanes = slice(start, start + 256)
        hot_ref[:, lanes] = hot_columns(ids[:, lanes], hot_ref.shape[0])


def hot_back_kernel(slots_x, ids_ref, hot_ref):
    edges = ids_ref.shape[1]
    width = hot_ref.shape[1] // len(slots_x)
    entry = lax.broadcasted_iota(jnp.int32, (128, width), 1).astype(F32)
    for start in range(0, edges, 128):
        row = jnp.broadcast_to(ids_ref[1:2, start : start + 128].astype(F32), (8, 128))
        column = row.T[:, 0:1]
        for n, slot in enumerate(slots_x):
            hot_ref[start : start + 128, n * width : (n + 1) * width] = jnp.where(
                column - float(slot * width) == entry, 1.0, 0.0
            ).astype(BF16)


def unfold_block(block, atoms):
    parts = atoms // 128
    rows = [block[r : r + 1] for r in range(4 * parts)]
    return [jnp.concatenate(rows[q * parts : (q + 1) * parts], axis=1) for q in range(4)]


def first_kernel(slots, place_ref, embed_ref, kind_left, mix_high, mix_low, y_beyond_ref, own_ref,
                 y_pair_ref, beyond_ref, column_ref, pair_ref, low_ref, ids_ref, basis_ref, slope_ref,
                 unit_ref, sums_ref, gate_ref):
    atoms = low_ref.shape[2]
    frame = [pair_ref, column_ref, beyond_ref]
    per_cell = atoms // 128
    places = lax.broadcasted_iota(jnp.int32, (4 * per_cell, 128), 0)
    upper = places % per_cell
    kind_of_row = places // per_cell
    to_x = jnp.where(kind_of_row == 0, cell_width, 0.0)
    to_x = jnp.where((place_ref[0] & 1) == 0, to_x, -to_x)
    to_y = jnp.where(kind_of_row == 1, cell_width, 0.0)
    to_y = jnp.where((place_ref[1] & 1) == 0, to_y, -to_y)
    for cell, block_ref in enumerate((y_pair_ref, own_ref, y_beyond_ref)):
        ids, count = block_ids(block_ref[...], atoms, slots * atoms)
        ids_ref[cell : cell + 1, :] = ids
        own = unfold_block(column_ref[cell + 1], atoms)
        step_y = to_y if cell == 1 else -to_y
        rows = []
        for a in range(3):
            for b in range(3):
                block = frame[a][SLOT_CELLS[cell][b]]
                rows.append(block + ((1 - a) * to_x + (1 - b) * step_y))
        first_cell(
            slots, atoms, ids, count, rows, places, upper, own, embed_ref, kind_left, mix_high,
            mix_low, low_ref.at[cell], basis_ref.at[cell], slope_ref.at[cell], unit_ref.at[cell],
            sums_ref.at[cell], gate_ref.at[cell],
        )


def first_cell(slots, atoms, ids, count, rows, places, upper, own, embed_ref, kind_left, mix_high,
               mix_low, low_ref, basis_ref, slope_ref, unit_ref, sums_ref, gate_ref):
    per_cell = atoms // 128
    pieces = []
    for start in range(0, ids.shape[1], 128):
        part = jnp.broadcast_to(ids[:, start : start + 128], places.shape)
        lane, half = part & 127, (part >> 7) - upper
        found = jnp.zeros(places.shape, F32)
        for cell, block in enumerate(rows):
            value = jnp.take_along_axis(block, lane, axis=1)
            found = jnp.where(half == per_cell * cell, value, found)
        total = found
        for s in range(1, per_cell):
            total = total + pltpu.roll(found, 4 * per_cell - s, 0)
        pieces.append(total)
    found = jnp.concatenate(pieces, axis=1)
    found = [found[q * per_cell : q * per_cell + 1] for q in range(4)]
    rel = [found[q] - jnp.concatenate([own[q]] * slots, axis=1) for q in range(3)]
    distance = jnp.sqrt(rel[0] * rel[0] + rel[1] * rel[1] + rel[2] * rel[2] + soften)
    inverse = 1.0 / distance
    order = (lax.broadcasted_iota(jnp.int32, (8, 1), 0) + 1).astype(F32)
    sine, cosine = sin_cos((order * (0.5 / cut_radius)) * distance)
    wave = sine / ((order * (math.pi / cut_radius)) * distance)
    live = jnp.concatenate([jnp.where(count > n, 1.0, 0.0) for n in range(slots)], axis=1)
    basis = wave * live
    basis_ref[...] = basis
    slope_ref[...] = (cosine - wave) * (inverse * live)
    kinds = found[3]
    unit = jnp.concatenate(
        [r * inverse for r in rel] + [inverse, kinds] + [jnp.zeros_like(kinds)] * 3, axis=0
    )
    unit_ref[...] = unit
    stack = embed_ref[...]
    parts = edge_parts(basis, unit)
    species = kind_left.shape[2] // 32
    by_kind = [[None] * species for _ in range(4)]
    for n in range(slots):
        lanes = slice(n * atoms, (n + 1) * atoms)
        kind = jnp.broadcast_to(kinds[:, lanes], (8, atoms))
        for k in range(species):
            match = kind == float(k)
            for part in range(4):
                term = jnp.where(match, parts[part][:, lanes], 0.0)
                old = by_kind[part][k]
                by_kind[part][k] = term if old is None else old + term
    stacks = [stacked_right(jnp.concatenate(rows, axis=0)) for rows in by_kind]
    vectors = dot(kind_left[1], jnp.concatenate(stacks[1:], axis=1))
    sums = [dot(kind_left[0], stacks[0])]
    sums += [vectors[:, i * atoms : (i + 1) * atoms] for i in range(3)]
    step, gate = mixed(sums, mix_high, mix_low, 0)
    low_ref[...] = (embedded(stack, own[3]) + step).astype(BF16)
    for part in range(3):
        sums_ref[part] = sums[part + 1]
    gate_ref[...] = gate


def hot_columns(ids, rows):
    place = lax.broadcasted_iota(jnp.int32, (rows, ids.shape[1]), 0)
    return jnp.where(ids == place, 1.0, 0.0).astype(BF16)


def second_near_kernel(slots, ids_ref, basis_ref, unit_ref, left_ref, column_ref, weight_ref,
                       near_ref):
    atoms = column_ref.shape[2]
    parts = edge_parts(basis_ref[1], unit_ref[1])
    source = jnp.concatenate([column_ref[b] for b in range(3)], axis=1)
    for n in range(slots):
        lanes = slice(n * atoms, (n + 1) * atoms)
        for part in range(4):
            weight_ref[part, :, lanes] = weights_of(left_ref, part, parts[part][:, lanes])
        ids = ids_ref[1:2, lanes] - 3 * atoms
        near_ref[:, lanes] = dot(source, hot_columns(ids, 3 * atoms))


def second_side_kernel(slots, ids_ref, near_ref, pair_ref, out_ref):
    atoms = pair_ref.shape[2]
    source = jnp.concatenate([pair_ref[b] for b in range(3)], axis=1)
    for n in range(slots):
        lanes = slice(n * atoms, (n + 1) * atoms)
        hot = hot_columns(ids_ref[1:2, lanes], 3 * atoms)
        out_ref[:, lanes] = near_ref[:, lanes] + dot(source, hot)


def second_kernel(slots, hot_ref, weight_ref, near_ref, mix_high, mix_low, charge_ref, cell_ref,
                  column_ref, beyond_ref, feature_ref, sums_ref, gate_ref, packed_ref,
                  full_charge_ref, hidden_ref):
    atoms = column_ref.shape[2]
    source = jnp.concatenate([beyond_ref[b] for b in range(3)], axis=1)
    sums = [None] * 4
    for n in range(slots):
        lanes = slice(n * atoms, (n + 1) * atoms)
        feature = near_ref[:, lanes] + dot(source, hot_ref[:, lanes])
        feature_ref[:, lanes] = feature.astype(BF16)
        for part in range(4):
            term = weight_ref[part, :, lanes] * feature
            sums[part] = term if sums[part] is None else sums[part] + term
    step, gate = mixed(sums, mix_high, mix_low, 1)
    hidden = column_ref[1].astype(F32) + step
    hidden_ref[...] = hidden
    for part in range(3):
        sums_ref[part] = sums[part + 1]
    gate_ref[...] = gate
    charge = dot_split((charge_ref[0], charge_ref[1]), hidden)
    full_charge_ref[...] = charge
    place = jnp.concatenate(unfold_block(cell_ref[2], atoms)[:3], axis=0)
    high = place.astype(BF16).astype(F32)
    rest = place - high
    middle = rest.astype(BF16).astype(F32)
    zero = jnp.zeros((packed_ref.shape[0] - charge.shape[0] - 9, atoms), F32)
    packed_ref[...] = jnp.concatenate([charge, high, middle, rest - middle, zero], axis=0).astype(
        BF16
    )


def readout_kernel(hidden_high, hidden_low, turn_high, turn_low, out_ref, hidden_ref, energy_ref,
                   slope_ref):
    hidden = hidden_ref[...]
    value, slope = silu_pair(dot_split((hidden_high[...], hidden_low[...]), hidden))
    out = out_ref[...].T
    energy_ref[...] = jnp.sum(value * out, axis=0, keepdims=True)
    slope_ref[...] = dot_split((turn_high[...], turn_low[...]), slope * out)


def message_grads(cotangent, gate_ref, sums_ref, high_ref, low_ref, layer):
    pre = cotangent * gate_ref[...]
    both = dot_split((high_ref[layer], low_ref[layer]), pre)
    half = both.shape[0] // 2
    return [both[:half]] + [both[half:] * sums_ref[i] for i in range(3)]


def radial_grad(left, value):
    high, low = split(value)
    both = dot(left, jnp.concatenate([high, low], axis=0))
    half = both.shape[0] // 2
    return both[:half] + both[half:]


def second_back_kernel(slots, scale, count, hot_ref, weight_ref, turn_high, turn_low, charge_ref,
                       sums_ref, gate_ref, full_charge_ref, energy_ref, slope_ref, *refs):
    folds, refs = refs[:count], refs[count:]
    site_ref, long_ref, cotangent_ref, grad_ref, term_ref, beyond_ref, pair_ref = refs
    atoms = gate_ref.shape[1]
    total = folds[0][...].astype(F32)
    for part in folds[1:]:
        total = total + part[...].astype(F32)
    wide = full_charge_ref.shape[0]
    potential = total[:wide] * (2.0 * scale)
    slopes = total[wide : wide + 3] + total[wide + 3 : wide + 6] + total[wide + 6 : wide + 9]
    long_ref[...] = jnp.concatenate(
        [slopes * (2.0 * scale), jnp.zeros((5, atoms), F32)], axis=0
    )
    site_ref[0] = energy_ref[...] + 0.5 * jnp.sum(
        full_charge_ref[...] * potential, axis=0, keepdims=True
    )
    high, low = split(potential)
    turned = ((0,), (0,))
    cotangent = slope_ref[...] + (
        dot(charge_ref[0], high, turned)
        + (dot(charge_ref[0], low, turned) + dot(charge_ref[1], high, turned))
    )
    cotangent_ref[...] = cotangent
    grads = message_grads(cotangent, gate_ref, sums_ref, turn_high, turn_low, 1)
    for part in range(4):
        grad_ref[part] = grads[part]
    for n in range(slots):
        lanes = slice(n * atoms, (n + 1) * atoms)
        term = weight_ref[0, :, lanes] * grads[0]
        for part in range(1, 4):
            term = term + weight_ref[part, :, lanes] * grads[part]
        term_ref[:, lanes] = term.astype(BF16)
    for b in range(3):
        start = (3 + b) * atoms
        beyond_ref[b] = dot(term_ref[...], hot_ref[:, start : start + atoms]).astype(BF16)
    for b in range(3):
        pair_ref[b] = dot(term_ref[...], hot_ref[:, b * atoms : (b + 1) * atoms]).astype(BF16)


def second_middle_kernel(hot_ref, term_ref, cotangent_ref, middle_ref):
    atoms = cotangent_ref.shape[1]
    for b in range(3):
        grad = dot(term_ref[...], hot_ref[:, b * atoms : (b + 1) * atoms])
        middle_ref[b] = grad + cotangent_ref[...] if b == 1 else grad


def second_edge_kernel(slots, back_ref, feature_ref, grad_ref, edge_ref):
    atoms = grad_ref.shape[2]
    for n in range(slots):
        lanes = slice(n * atoms, (n + 1) * atoms)
        feature = feature_ref[:, lanes].astype(F32)
        for part in range(4):
            edge_ref[8 * part : 8 * part + 8, lanes] = radial_grad(
                back_ref[1 if part else 0], grad_ref[part] * feature
            )


def first_back_kernel(slots, ids_ref, basis_ref, slope_ref, unit_ref, kind_high, kind_low, turn_high,
                      turn_low, sums_ref, gate_ref, edge_ref, long_ref, middle_ref, from_pair,
                      from_beyond, *outs):
    sums = {(1, 2): long_ref[...]}
    for cell in range(3):
        cotangent = middle_ref[cell] + (
            from_pair[cell].astype(F32) + from_beyond[cell].astype(F32)
        )
        own, found = first_back_cell(
            slots, ids_ref[cell : cell + 1, :], basis_ref.at[cell], slope_ref.at[cell],
            unit_ref.at[cell], kind_high, kind_low, turn_high, turn_low, sums_ref.at[cell],
            gate_ref.at[cell], edge_ref if cell == 1 else None, cotangent,
        )
        terms = [((1, cell + 1), own)]
        terms += [((n // 3, SLOT_CELLS[cell][n % 3]), found[n]) for n in range(9)]
        for key, term in terms:
            sums[key] = sums[key] + term if key in sums else term
    for x in range(3):
        rows = [sums[(x, y)][:3] for y in range(5)]
        outs[x][...] = jnp.concatenate(rows + [jnp.zeros((1, rows[0].shape[1]), F32)], axis=0)


def first_back_cell(slots, ids, basis_ref, slope_ref, unit_ref, kind_high, kind_low, turn_high,
                    turn_low, sums_ref, gate_ref, edge_ref, cotangent):
    atoms = gate_ref.shape[1]
    pre = cotangent * gate_ref[...]
    both = dot_split((turn_high[0], turn_low[0]), pre)
    wide = both.shape[0] // 2
    grads = [both[:wide]] + [both[wide:] * sums_ref[i] for i in range(3)]
    unit = unit_ref[...]
    kinds = unit[4:5]
    by_kind = [dot_split((kind_high[0], kind_low[0]), grads[0])]
    by_kind += [dot_split((kind_high[1], kind_low[1]), grads[i]) for i in range(1, 4)]
    species = by_kind[0].shape[0] // 8
    edges = [[] for _ in range(4)]
    for n in range(slots):
        kind = jnp.broadcast_to(kinds[:, n * atoms : (n + 1) * atoms], (8, atoms))
        matches = [kind == float(k) for k in range(1, species)]
        for part in range(4):
            rows = by_kind[part]
            found = rows[:8]
            for k, match in enumerate(matches):
                found = jnp.where(match, rows[8 * k + 8 : 8 * k + 16], found)
            edges[part].append(found)
    edges = [jnp.concatenate(rows, axis=1) for rows in edges]
    if edge_ref is not None:
        edges = [edge_ref[8 * part : 8 * part + 8] + edges[part] for part in range(4)]
    basis = basis_ref[...]
    units = [unit[i : i + 1] for i in range(3)]
    inverse = unit[3:4]
    by_basis = edges[0]
    for i in range(3):
        by_basis = by_basis + edges[i + 1] * units[i]
    by_unit = [jnp.sum(edges[i + 1] * basis, axis=0, keepdims=True) * inverse for i in range(3)]
    by_distance = jnp.sum(by_basis * slope_ref[...], axis=0, keepdims=True)
    for i in range(3):
        by_distance = by_distance - by_unit[i] * units[i]
    moves = [by_unit[i] + by_distance * units[i] for i in range(3)]
    zero = jnp.zeros_like(moves[0])
    move = jnp.concatenate(moves + [zero] * 5, axis=0)
    own = -move[:, :atoms]
    for n in range(1, slots):
        own = own - move[:, n * atoms : (n + 1) * atoms]
    lane_hot = hot_columns(ids & 127, 128)
    half = ids >> 7
    high = move.astype(BF16).astype(F32)
    both = jnp.concatenate([high, move - high], axis=0)
    per_cell = atoms // 128
    rows = jnp.concatenate(
        [jnp.where(half == h, both, 0.0).astype(BF16) for h in range(9 * per_cell)], axis=0
    )
    spread = dot(rows, lane_hot, ((1,), (1,)))
    grads = []
    for cell in range(9):
        found = []
        for h in range(cell * per_cell, (cell + 1) * per_cell):
            found.append(spread[16 * h : 16 * h + 8] + spread[16 * h + 8 : 16 * h + 16])
        grads.append(jnp.concatenate(found, axis=1))
    return own, grads


def pair_counts(parts):
    total = WAVE_REACH + WAVE_REACH * (2 * WAVE_REACH + 1)
    share = -(-total // parts)
    return total, share, -(-share // 16) * 16


def pair_vectors(slot, share, part):
    side = 2 * WAVE_REACH + 1
    total = WAVE_REACH + WAVE_REACH * side
    index = slot + part.astype(F32) * share
    later = index - WAVE_REACH
    row = jnp.floor((later + 0.5) * (1.0 / side))
    first = index < WAVE_REACH
    kx = jnp.where(first, 0.0, row + 1.0)
    ky = jnp.where(first, index + 1.0, later - row * side - WAVE_REACH)
    valid = jnp.where((slot < share) & (index < total), 1.0, 0.0)
    return kx, ky, valid


def count_up(rows):
    return lax.broadcasted_iota(jnp.int32, (rows, 1), 0).astype(F32)


def green_weights(share, padded, grid, place_ref, vec_ref, weight_ref):
    grid_x, grid_y = grid
    turn = 2.0 * math.pi
    side = 2 * WAVE_REACH + 1
    top = side * side * side - 1
    vec = vec_ref[...].astype(F32) + WAVE_REACH
    code = (vec[0:1] * side + vec[1:2]) * side + vec[2:3]
    code = jnp.maximum(code, top - code)
    span = 8 * share
    row = count_up(span)
    slot = jnp.floor(row * 0.125)
    height = row - 8.0 * slot + 1.0
    flat = count_up(padded)
    slot = jnp.concatenate([slot, slot, flat], axis=0)
    kz = jnp.concatenate([height, -height, jnp.zeros_like(flat)], axis=0)
    kx, ky, valid = pair_vectors(slot, share, place_ref[0, 0:1, 0:1])
    own = ((kx + WAVE_REACH) * side + ky + WAVE_REACH) * side + kz + WAVE_REACH
    seen = jnp.zeros((own.shape[0], 128), F32)
    for start in range(0, code.shape[1], 128):
        seen = seen + jnp.where(own == code[:, start : start + 128], 1.0, 0.0)
    count = jnp.sum(seen, axis=1, keepdims=True) * valid
    sq = (
        (kx * (turn / (grid_x * cell_width))) ** 2
        + (ky * (turn / (grid_y * cell_width))) ** 2
        + (kz * (turn / box_height)) ** 2
    )
    green = jnp.exp(-smear_width * sq) / (sq + screen * screen) * count
    weight_ref[...] = jnp.broadcast_to(green, weight_ref.shape)


def basis_rows(share, ca, sa, cb, sb):
    cc, ss, sc, cs = [], [], [], []
    for p in range(share):
        c, s = ca[p : p + 1], sa[p : p + 1]
        cc.append(c * cb)
        ss.append(s * sb)
        sc.append(s * cb)
        cs.append(c * sb)
    return cc, ss, sc, cs


def unpack_rows(block):
    half = block.shape[1] // 2
    return jnp.concatenate([block[:, :half], block[:, half:]], axis=0)


def pack_rows(block):
    half = block.shape[0] // 2
    return jnp.concatenate([block[:half], block[half:]], axis=1)


def structure_kernel(share, padded, grid, wide, flip, place_ref, blocks, *refs):
    grid_x, grid_y = grid
    if flip:
        near_ref, (ca_ref, sa_ref, cb_ref, sb_ref, high_ref, low_ref, own_ref, out_ref) = (
            refs[0],
            refs[1:],
        )
        total = near_ref[...]
    else:
        ca_ref, sa_ref, cb_ref, sb_ref, high_ref, low_ref, total_ref = refs
        total = None
    col = place_ref[1, 0:1, 0:1].astype(F32) * (1.0 / grid_y)
    first = place_ref[0, 0:1, 0:1] ^ flip
    kx, ky, _ = pair_vectors(count_up(padded), share, place_ref[0, 0:1, 0:1])
    kz = count_up(8) + 1.0
    for d in range(grid_x // 2):
        block = blocks[d]
        charge = block[:wide]
        atoms = charge.shape[1]
        pieces = block[wide:].astype(F32)
        place = pieces[0:3] + (pieces[3:6] + pieces[6:9])
        row = (first ^ (2 * d)).astype(F32) * (1.0 / grid_x)
        x = place[0:1] * (1.0 / (grid_x * cell_width)) + row
        y = place[1:2] * (1.0 / (grid_y * cell_width)) + col
        sa, ca = sin_cos(kx * x + ky * y)
        sb, cb = sin_cos(kz * (place[2:3] * (1.0 / box_height)))
        lanes = pl.ds(d * atoms, atoms)
        ca_ref[:, lanes] = ca
        sa_ref[:, lanes] = sa
        cb_ref[:, lanes] = cb
        sb_ref[:, lanes] = sb
        cc, ss, sc, cs = basis_rows(share, ca, sa, cb, sb)
        high, low = split(jnp.concatenate(cc + ss + sc + cs + [ca, sa], axis=0))
        high_ref[:, lanes] = high
        low_ref[:, lanes] = low
        term = dot(high, charge, ((1,), (1,))) + dot(low, charge, ((1,), (1,)))
        total = term if total is None else total + term
    if flip:
        packed = pack_rows(total)
        own_ref[...] = packed
        out_ref[...] = packed.astype(BF16)
    else:
        total_ref[...] = total


def weighted_rows(share, padded, wide, weight_ref, parts):
    packed = parts[0][...].astype(F32)
    for part in parts[1:]:
        packed = packed + part[...].astype(F32)
    struct = unpack_rows(packed)
    span = 8 * share
    cc, ss, sc, cs = (struct[i * span : (i + 1) * span] for i in range(4))
    weight = weight_ref[:, :wide]
    plus, minus, flat = weight[:span], weight[span : 2 * span], weight[2 * span :]
    re_plus, im_plus = plus * (cc - ss), plus * (sc + cs)
    re_minus, im_minus = minus * (cc + ss), minus * (sc - cs)
    rows = jnp.concatenate(
        [
            re_plus + re_minus,
            re_minus - re_plus,
            im_plus + im_minus,
            im_plus - im_minus,
            flat * struct[4 * span : 4 * span + padded],
            flat * struct[4 * span + padded :],
        ],
        axis=0,
    )
    return rows


def fold_kernel(share, padded, grid, wide, flip, place_ref, *refs):
    grid_x, grid_y = grid
    turn = 2.0 * math.pi
    if flip:
        weight_ref, parts, refs = refs[0], refs[1 : 1 + grid_y], refs[1 + grid_y :]
        rows = weighted_rows(share, padded, wide, weight_ref, parts)
        refs, rows_ref = refs[:-1], refs[-1]
        rows_ref[...] = rows
    else:
        rows, refs = refs[0][...], refs[1:]
    ca_ref, sa_ref, cb_ref, sb_ref, high_ref, low_ref, blocks, out_ref = refs
    row_high, row_low = split(rows)
    row_pair = jnp.concatenate([row_high, row_low], axis=1)
    turned = rows.T
    t_high, t_low = split(turned)
    t_both = jnp.concatenate([t_high, t_low], axis=0)
    span = 8 * share
    kx, ky, _ = pair_vectors(count_up(padded), share, place_ref[0, 0:1, 0:1])
    kx = kx * (turn / (grid_x * cell_width))
    ky = ky * (turn / (grid_y * cell_width))
    kz = (count_up(8) + 1.0) * (turn / box_height)
    for d in range(grid_x // 2):
        charge = blocks[d][:wide]
        atoms = charge.shape[1]
        lanes = pl.ds(d * atoms, atoms)
        ca, sa, cb, sb = ca_ref[:, lanes], sa_ref[:, lanes], cb_ref[:, lanes], sb_ref[:, lanes]
        bcc, bss, bsc, bcs = basis_rows(share, ca, sa, cb, sb)
        high, low = high_ref[:, lanes], low_ref[:, lanes]
        both = dot(t_both, high)
        pot = both[:wide] + both[wide:] + dot(t_high, low)
        proj = dot(row_pair, jnp.concatenate([charge, charge], axis=0))
        by_x = jnp.zeros((8, atoms), jnp.float32)
        by_y = jnp.zeros((8, atoms), jnp.float32)
        by_z = jnp.zeros((8, atoms), jnp.float32)
        for p in range(share):
            pcc, pss, psc, pcs = (
                proj[i * span + 8 * p : i * span + 8 * p + 8] for i in range(4)
            )
            slope = bcs[p] * pss - bsc[p] * pcc + bcc[p] * psc - bss[p] * pcs
            by_x = by_x + kx[p : p + 1] * slope
            by_y = by_y + ky[p : p + 1] * slope
            by_z = by_z + (bsc[p] * pss - bcs[p] * pcc - bss[p] * psc + bcc[p] * pcs)
        flat_slope = ca * proj[4 * span + padded :] - sa * proj[4 * span : 4 * span + padded]
        grad_x = jnp.sum(by_x, axis=0, keepdims=True) + jnp.sum(kx * flat_slope, axis=0, keepdims=True)
        grad_y = jnp.sum(by_y, axis=0, keepdims=True) + jnp.sum(ky * flat_slope, axis=0, keepdims=True)
        grad_z = jnp.sum(kz * by_z, axis=0, keepdims=True)
        slopes = jnp.concatenate([grad_x, grad_y, grad_z], axis=0)
        out_ref[d] = pieced(pot, slopes, out_ref.shape[1]).astype(out_ref.dtype)


def pieced(pot, slopes, rows):
    high = slopes.astype(BF16).astype(F32)
    rest = slopes - high
    middle = rest.astype(BF16).astype(F32)
    zero = jnp.zeros((rows - pot.shape[0] - 9, pot.shape[1]), F32)
    return jnp.concatenate([pot, high, middle, rest - middle, zero], axis=0)


def unpieced(block, wide):
    slopes = block[wide : wide + 3] + (block[wide + 3 : wide + 6] + block[wide + 6 : wide + 9])
    return block[:wide], slopes


def join_kernel(wide, near_ref, far_ref, own_ref, *outs):
    for d in range(near_ref.shape[0]):
        pot, slopes = unpieced(near_ref[d], wide)
        pot_far, slopes_far = unpieced(far_ref[d].astype(F32), wide)
        block = pieced(pot + pot_far, slopes + slopes_far, near_ref.shape[1])
        if d:
            outs[d - 1][...] = block.astype(BF16)
        else:
            own_ref[...] = block


def per_device(
    positions,
    species,
    neighbours,
    counts,
    species_embed,
    radial,
    mixing,
    read_hidden,
    read_out,
    charge_map,
    wavevectors,
):
    atoms = positions.shape[3]
    slots = neighbours.shape[3]
    features, lat_width = charge_map.shape
    wave_count = wavevectors.shape[1]
    grid = lax.axis_size("gx"), lax.axis_size("gy")
    grid_x, grid_y = grid
    edges = slots * atoms
    scale = 1.0 / math.sqrt(wave_count * lat_width * atoms * grid_x * grid_y)
    place = jnp.stack([lax.axis_index("gx"), lax.axis_index("gy")]).astype(jnp.int32)
    place = jnp.broadcast_to(place[:, None, None], (2, 8, 128))
    _, share, padded = pair_counts(grid_x)
    ids = neighbours.transpose(0, 3, 1, 2).reshape(1, edges)
    cell_rows = 4 * atoms // 128
    block_total = -(-(cell_rows + (edges + atoms) // 128) // 8) * 8
    dma = pltpu.SemaphoreType.DMA
    shown = positions.transpose(0, 2, 1, 3)
    (own_place,) = run(
        pack_kernel,
        [shape(cell_rows, 128)],
        [place, shown, species],
        flops=10_000_000_000,
        name="pack",
    )
    (own,) = run(
        pack_more_kernel,
        [shape(block_total, 128)],
        [place, ids, counts, own_place],
        name="pack_more",
    )
    y_beyond, y_pair = beyond(own, "gy"), paired(own, "gy", 1)
    over_pair = far(own_place, "gy", True)
    over_beyond = over_pair if grid_y == 4 else far(own_place, "gy", False)
    cells = jnp.stack(
        [over_pair, y_pair[:cell_rows], own_place, y_beyond[:cell_rows], over_beyond]
    )
    x_beyond, x_pair = beyond(cells, "gx"), paired(cells, "gx", 1)
    cells = [x_pair, cells, x_beyond]

    norm = 1.0 / math.sqrt(slots)
    kind_rows = 8 * species_embed.shape[0]
    low_pair = lambda *dims: [shape(*dims, dtype=BF16)] * 2
    embed, kind_left, left, back, kind_high, kind_low, mix_high, mix_low, turn_high, turn_low = run(
        functools.partial(prep_first_kernel, norm),
        [
            shape(features, 32, dtype=BF16),
            shape(2, features, 4 * kind_rows, dtype=BF16),
            shape(2, features, 32, dtype=BF16),
            shape(2, 16, 2 * features, dtype=BF16),
        ]
        + low_pair(2, kind_rows, features)
        + low_pair(2, features, 2 * features)
        + low_pair(2, 2 * features, features),
        [species_embed, radial, mixing],
        scratch=[
            pltpu.VMEM(species_embed.shape, F32),
            pltpu.VMEM(radial.shape, F32),
            pltpu.VMEM(mixing.shape, F32),
            dma((3,)),
        ],
        hbm=3,
        name="prep_first",
    )
    read_out, hidden_high, hidden_low, hidden_turn_high, hidden_turn_low, charge_pair = run(
        prep_second_kernel,
        [shape(1, features)]
        + low_pair(features, features)
        + low_pair(features, features)
        + [shape(2, lat_width, features, dtype=BF16)],
        [read_out[None, :], read_hidden, charge_map.T],
        scratch=[
            pltpu.VMEM(read_hidden.shape, F32),
            pltpu.VMEM((lat_width, features), F32),
            dma((3,)),
        ],
        hbm=3,
        name="prep_second",
    )
    cells[2], hidden_high = lax.optimization_barrier((cells[2], hidden_high))
    low, ids, basis, slope, unit, sums_one, gate_one = run(
        functools.partial(first_kernel, slots),
        [
            shape(3, features, atoms, dtype=BF16),
            shape(3, edges, dtype=jnp.int32),
            shape(3, 8, edges),
            shape(3, 8, edges),
            shape(3, 8, edges),
            shape(3, 3, features, atoms),
            shape(3, features, atoms),
        ],
        [place, embed, kind_left, mix_high, mix_low, y_beyond, own, y_pair] + cells[::-1],
        name="first",
    )
    hidden = [paired(low, "gx", 1), low, beyond(low, "gx")]
    edge_weights, near = run(
        functools.partial(second_near_kernel, slots),
        [shape(4, features, edges), shape(features, edges)],
        [ids, basis, unit, left, low],
        flops=2_000_000_000,
        name="second_near",
    )
    (hot_beyond,) = run(
        hot_beyond_kernel,
        [shape(3 * atoms, edges, dtype=BF16)],
        [ids, near],
        flops=1_000_000,
        name="hot_beyond",
    )
    (near,) = run(
        functools.partial(second_side_kernel, slots),
        [shape(features, edges)],
        [ids, near, hidden[0]],
        flops=1_000_000_000,
        name="second_side",
    )
    block_rows = -(-(lat_width + 9) // 16) * 16
    feature, sums_two, gate_two, packed, charge, hidden_two = run(
        functools.partial(second_kernel, slots),
        [
            shape(features, edges, dtype=BF16),
            shape(3, features, atoms),
            shape(features, atoms),
            shape(block_rows, atoms, dtype=BF16),
            shape(lat_width, atoms),
            shape(features, atoms),
        ],
        [hot_beyond, edge_weights, near, mix_high, mix_low, charge_pair, cells[1], hidden[1],
         hidden[2]],
        name="second",
    )
    energy, energy_slope = run(
        readout_kernel,
        [shape(1, atoms), shape(features, atoms)],
        [hidden_high, hidden_low, hidden_turn_high, hidden_turn_low, read_out, hidden_two],
        name="readout",
    )
    half = grid_x // 2
    near_charges = jnp.stack([packed] + [paired(packed, "gx", 2 * d) for d in range(1, half)])
    (weight,) = run(
        functools.partial(green_weights, share, padded, grid),
        [shape(16 * share + padded, 128)],
        [place, wavevectors],
        name="green",
    )
    near_charges, weight = lax.optimization_barrier((near_charges, weight))
    far_charges = paired(near_charges, "gx", 1)
    span = half * atoms
    rows = 32 * share + 2 * padded
    phase_shapes = [
        shape(padded, span),
        shape(padded, span),
        shape(8, span),
        shape(8, span),
        shape(rows, span, dtype=BF16),
        shape(rows, span, dtype=BF16),
    ]
    *near_phases, near_total = run(
        functools.partial(structure_kernel, share, padded, grid, lat_width, 0),
        phase_shapes + [shape(rows, lat_width)],
        [place, near_charges],
        flops=1_000_000_000,
        name="structure_near",
    )
    *far_phases, own_part, part = run(
        functools.partial(structure_kernel, share, padded, grid, lat_width, 1),
        phase_shapes
        + [
            shape(rows // 2, 2 * lat_width),
            shape(rows // 2, 2 * lat_width, dtype=BF16),
        ],
        [place, far_charges, near_total],
        name="structure_far",
    )
    parts = [own_part] + [paired(part, "gy", d) for d in range(1, grid_y)]
    (hot_back,) = run(
        functools.partial(hot_back_kernel, (0, 2)),
        [shape(edges, 6 * atoms, dtype=BF16)],
        [ids],
        flops=2_000_000_000,
        name="hot_back",
    )
    parts, hot_back = lax.optimization_barrier((parts, hot_back))
    far_folds, wave_rows = run(
        functools.partial(fold_kernel, share, padded, grid, lat_width, 1),
        [shape(half, block_rows, atoms, dtype=BF16), shape(rows, lat_width)],
        [place, weight] + parts + far_phases + [far_charges],
        name="fold_far",
    )
    far_folds = paired(far_folds, "gx", 1)
    (near_folds,) = run(
        functools.partial(fold_kernel, share, padded, grid, lat_width, 0),
        [shape(half, block_rows, atoms)],
        [place, wave_rows] + near_phases + [near_charges],
        flops=1_000_000_000,
        name="fold_near",
    )
    folds = run(
        functools.partial(join_kernel, lat_width),
        [shape(block_rows, atoms)] + [shape(block_rows, atoms, dtype=BF16)] * (half - 1),
        [near_folds, far_folds],
        name="fold_join",
    )
    folds = [folds[0]] + [paired(folds[d], "gx", 2 * d) for d in range(1, half)]

    site, long, cotangent, grads, term, to_beyond, to_pair = run(
        functools.partial(second_back_kernel, slots, scale, half),
        [
            shape(1, 1, atoms),
            shape(8, atoms),
            shape(features, atoms),
            shape(4, features, atoms),
            shape(features, edges, dtype=BF16),
            shape(3, features, atoms, dtype=BF16),
            shape(3, features, atoms, dtype=BF16),
        ],
        [hot_back, edge_weights, turn_high, turn_low, charge_pair, sums_two, gate_two, charge,
         energy, energy_slope] + folds,
        name="second_back",
    )
    from_pair, from_beyond = paired(to_pair, "gx", 1), beyond(to_beyond, "gx")
    (hot_middle,) = run(
        functools.partial(hot_back_kernel, (1,)),
        [shape(edges, 3 * atoms, dtype=BF16)],
        [ids],
        flops=1_000_000_000,
        name="hot_middle",
    )
    (middle,) = run(
        second_middle_kernel,
        [shape(3, features, atoms)],
        [hot_middle, term, cotangent],
        flops=1_000_000_000,
        name="second_middle",
    )
    (edge,) = run(
        functools.partial(second_edge_kernel, slots),
        [shape(32, edges)],
        [back, feature, grads],
        flops=1_000_000_000,
        name="second_edge",
    )
    to_pair, middle, to_beyond = run(
        functools.partial(first_back_kernel, slots),
        [shape(16, atoms)] * 3,
        [ids, basis, slope, unit, kind_high, kind_low, turn_high, turn_low, sums_one, gate_one, edge,
         long, middle, from_pair, from_beyond],
        name="first_back",
    )
    total = middle + paired(to_pair, "gx", 1) + beyond(to_beyond, "gx")
    total = [total[3 * y : 3 * y + 3] for y in range(5)]
    if grid_y == 4:
        distant = far(total[0] + total[4], "gy", True)
    else:
        distant = far(total[0], "gy", False) + far(total[4], "gy", True)
    total = total[2] + paired(total[1], "gy", 1) + beyond(total[3], "gy") + distant
    forces = -total[None, :, None, :]
    return (forces.transpose(0, 2, 1, 3), site)


def solution(mesh):
    in_specs = (
        P("gx", "gy", None, None),
        P("gx", "gy", None),
        P("gx", "gy", None, None),
        P("gx", "gy", None),
        P(),
        P(),
        P(),
        P(),
        P(),
        P(),
        P(),
    )
    out_specs = (P("gx", "gy", None, None), P("gx", "gy", None))
    return jax.shard_map(
        per_device, mesh=mesh, in_specs=in_specs, out_specs=out_specs, check_vma=False
    )
```

```python
import functools
import math

import jax
import jax.numpy as jnp
import numpy as np
from jax import lax
from jax.experimental import pallas as pl
from jax.experimental.pallas import tpu as pltpu
from jax.sharding import PartitionSpec as P

cell_width = 10.0
box_height = 30.0
cut_radius = 50.0
soften = 0.25
screen = 0.5
smear_width = 0.5
WAVE_REACH = 8
F32 = jnp.float32
BF16 = jnp.bfloat16


def paired(block, axis, mask):
    return lax.ppermute(block, axis, [(i ^ mask, i) for i in range(lax.axis_size(axis))])


def other_side(index, count):
    return (index + (1 if index % 2 else -1)) % count


def beyond(block, axis):
    count = lax.axis_size(axis)
    return lax.ppermute(block, axis, [(other_side(i, count), i) for i in range(count)])


def far(block, axis, over_pair):
    count = lax.axis_size(axis)
    if over_pair:
        route = [(other_side(i ^ 1, count), i) for i in range(count)]
    else:
        route = [(other_side(i, count) ^ 1, i) for i in range(count)]
    return lax.ppermute(block, axis, route)


SLOT_CELLS = ((2, 1, 0), (1, 2, 3), (4, 3, 2))


def whole(space=pltpu.VMEM):
    return pl.BlockSpec(memory_space=space)


def run(kernel, outs, args, scratch=(), hbm=0, flops=10_000_000, grant=16, name=None):
    specs = [whole()] * (len(args) - hbm) + [whole(pltpu.HBM)] * hbm
    return list(
        pl.pallas_call(
            kernel,
            out_shape=outs,
            in_specs=specs,
            out_specs=[whole() for _ in outs],
            scratch_shapes=list(scratch),
            compiler_params=pltpu.CompilerParams(vmem_limit_bytes=grant * 1024 * 1024),
            cost_estimate=pl.CostEstimate(
                flops=flops, bytes_accessed=1_000_000, transcendentals=0
            ),
            name=name,
        )(*args)
    )


def shape(*dims, dtype=F32):
    return jax.ShapeDtypeStruct(dims, dtype)


def split(value):
    high = value.astype(BF16)
    return high, (value - high.astype(F32)).astype(BF16)


def dot(left, right, contract=((1,), (0,))):
    return lax.dot_general(left, right, (contract, ((), ())), preferred_element_type=F32)


def dot3(left, right):
    left_high, left_low = split(left)
    right_high, right_low = split(right)
    return dot(left_high, right_high) + (dot(left_high, right_low) + dot(left_low, right_high))


def dot_split(left, right):
    right_high, right_low = split(right)
    return dot(left[0], right_high) + (dot(left[0], right_low) + dot(left[1], right_high))


def sin_cos(turns):
    quarter = jnp.round(turns * 4.0)
    x = (turns - quarter * 0.25) * (2.0 * math.pi)
    z = x * x
    sine = ((-1.9515295891e-4 * z + 8.3321608736e-3) * z - 1.6666654611e-1) * (z * x) + x
    cosine = (2.443315711809948e-5 * z - 1.388731625493765e-3) * z + 4.166664568298827e-2
    cosine = cosine * (z * z) - 0.5 * z + 1.0
    k = quarter.astype(jnp.int32) & 3
    odd = (k & 1) == 1
    by_sine = jnp.where(odd, cosine, sine)
    by_cosine = jnp.where(odd, sine, cosine)
    return (
        jnp.where(k >= 2, -by_sine, by_sine),
        jnp.where((k == 1) | (k == 2), -by_cosine, by_cosine),
    )


def stacked_left(value):
    high = value.astype(BF16).astype(F32)
    rows = jnp.concatenate([high, high, value - high, jnp.zeros_like(high)], axis=0)
    return rows.T.astype(BF16)


def stacked_right(value):
    high = value.astype(BF16).astype(F32)
    return jnp.concatenate([high, value - high, high, jnp.zeros_like(high)], axis=0).astype(BF16)


def silu_pair(value):
    gate = 1.0 / (1.0 + jnp.exp(-value))
    return value * gate, gate * (1.0 + value * (1.0 - gate))


def onehot_kinds(kinds, rows):
    levels = lax.broadcasted_iota(jnp.int32, (rows, kinds.shape[1]), 0).astype(F32)
    return jnp.where(kinds == levels, 1.0, 0.0)


def embedding_stack(embed):
    high = embed.astype(BF16).astype(F32)
    rest = embed - high
    middle = rest.astype(BF16).astype(F32)
    rows = jnp.concatenate([high, middle, rest - middle, jnp.zeros_like(high)], axis=0)
    return rows.T.astype(BF16)


def embedded(stack, kinds):
    hot = onehot_kinds(kinds, 8)
    return dot(stack, jnp.concatenate([hot, hot, hot, jnp.zeros_like(hot)], axis=0).astype(BF16))


def weights_of(stack_ref, part, rows):
    return dot(stack_ref[1 if part else 0], stacked_right(rows))


def mixed(sums, high_ref, low_ref, layer):
    squares = sums[1] * sums[1] + sums[2] * sums[2] + sums[3] * sums[3]
    both = jnp.concatenate([sums[0], squares], axis=0)
    return silu_pair(dot_split((high_ref[layer], low_ref[layer]), both))


def edge_parts(basis, unit):
    return [basis] + [basis * unit[i : i + 1] for i in range(3)]


def pack_kernel(place_ref, position_ref, species_ref, out_ref):
    rows = [position_ref[0, i] for i in range(3)] + [species_ref[0].astype(F32)]
    atoms = rows[0].shape[1]
    out_ref[...] = jnp.concatenate(
        [row[:, s : s + 128] for row in rows for s in range(0, atoms, 128)], axis=0
    )


def pack_more_kernel(place_ref, ids_ref, count_ref, first_ref, out_ref):
    atoms = count_ref.shape[2]
    order = slot_order(ids_ref[...], place_ref, atoms).astype(F32)
    rows = [first_ref[...]]
    rows += [order[:, s : s + 128] for s in range(0, order.shape[1], 128)]
    rows += [count_ref[0, :, s : s + 128].astype(F32) for s in range(0, atoms, 128)]
    missing = out_ref.shape[0] - sum(row.shape[0] for row in rows)
    out_ref[...] = jnp.concatenate(rows + [jnp.zeros((missing, 128), F32)], axis=0)


def block_ids(block, atoms, edges):
    start = 4 * atoms // 128
    middle, end = start + edges // 128, start + edges // 128 + atoms // 128
    rows = [block[r : r + 1] for r in range(start, end)]
    ids = jnp.concatenate(rows[: middle - start], axis=1).astype(jnp.int32)
    return ids, jnp.concatenate(rows[middle - start :], axis=1)


def radial_left(radial):
    high = radial.astype(BF16).astype(F32)
    low = radial - high
    top = jnp.concatenate([high, high], axis=1)
    end = jnp.concatenate([low, jnp.zeros_like(low)], axis=1)
    return jnp.concatenate([top, end], axis=0).astype(BF16)


def put_split(value, high_ref, low_ref, *at):
    high, low = split(value)
    high_ref[at] = high
    low_ref[at] = low


def slot_order(ids, place_ref, atoms):
    cell = ids >> (atoms.bit_length() - 1) if atoms & (atoms - 1) == 0 else ids // atoms
    a = (cell * 11) >> 5
    b = cell - 3 * a
    a = jnp.where((place_ref[0, 0:1, 0:1] & 1) == 0, 2 - a, a)
    b = jnp.where((place_ref[1, 0:1, 0:1] & 1) == 0, 2 - b, b)
    return ids + (3 * a + b - cell) * atoms


def fetch(sources, targets, sems):
    copies = [
        pltpu.make_async_copy(source, target, sems.at[i])
        for i, (source, target) in enumerate(zip(sources, targets))
    ]
    for copy in copies:
        copy.start()
    for copy in copies:
        copy.wait()


def prep_first_kernel(norm, embed_in, radial_in, mixing_in, embed_out, kind_left, left_out, back_out,
                      kind_high, kind_low, mix_high, mix_low, turn_high, turn_low, embed_ref,
                      radial_ref, mixing_ref, sems):
    fetch([embed_in, radial_in, mixing_in], [embed_ref, radial_ref, mixing_ref], sems)
    embed = embed_ref[...]
    kinds = embed.shape[0]
    for path in range(2):
        radial = radial_ref[0, path] * norm
        rows = jnp.concatenate([radial * embed[s : s + 1] for s in range(kinds)], axis=0)
        kind_left[path] = stacked_left(rows)
        put_split(rows, kind_high, kind_low, path)
        radial = radial_ref[1, path] * norm
        left_out[path] = stacked_left(radial)
        back_out[path] = radial_left(radial)
    for layer in range(2):
        scalar, vector = mixing_ref[layer, 0], mixing_ref[layer, 1]
        put_split(jnp.concatenate([scalar.T, vector.T], axis=1), mix_high, mix_low, layer)
        put_split(jnp.concatenate([scalar, 2.0 * vector], axis=0), turn_high, turn_low, layer)
    embed = jnp.concatenate([embed, jnp.zeros((8 - kinds, embed.shape[1]), F32)], axis=0)
    embed_out[...] = embedding_stack(embed)


def prep_second_kernel(read_in, hidden_in, charge_in, read_ref, hidden_high, hidden_low,
                       hidden_turn_high, hidden_turn_low, charge_pair, hidden_ref, charge_ref, sems):
    fetch([read_in, hidden_in, charge_in], [read_ref, hidden_ref, charge_ref], sems)
    put_split(hidden_ref[...].T, hidden_high, hidden_low, Ellipsis)
    put_split(hidden_ref[...], hidden_turn_high, hidden_turn_low, Ellipsis)
    charge = charge_ref[...]
    high = charge.astype(BF16).astype(F32)
    charge_pair[0] = high.astype(BF16)
    charge_pair[1] = (charge - high).astype(BF16)


def hot_beyond_kernel(ids_ref, near_ref, hot_ref):
    ids = ids_ref[1:2, :] - 2 * hot_ref.shape[0]
    for start in range(0, hot_ref.shape[1], 256):
        lanes = slice(start, start + 256)
        hot_ref[:, lanes] = hot_columns(ids[:, lanes], hot_ref.shape[0])


def hot_back_kernel(slots_x, ids_ref, hot_ref):
    edges = ids_ref.shape[1]
    width = hot_ref.shape[1] // len(slots_x)
    entry = lax.broadcasted_iota(jnp.int32, (128, width), 1).astype(F32)
    for start in range(0, edges, 128):
        row = jnp.broadcast_to(ids_ref[1:2, start : start + 128].astype(F32), (8, 128))
        column = row.T[:, 0:1]
        for n, slot in enumerate(slots_x):
            hot_ref[start : start + 128, n * width : (n + 1) * width] = jnp.where(
                column - float(slot * width) == entry, 1.0, 0.0
            ).astype(BF16)


def unfold_block(block, atoms):
    parts = atoms // 128
    rows = [block[r : r + 1] for r in range(4 * parts)]
    return [jnp.concatenate(rows[q * parts : (q + 1) * parts], axis=1) for q in range(4)]


def first_kernel(slots, place_ref, embed_ref, kind_left, mix_high, mix_low, y_beyond_ref, own_ref,
                 y_pair_ref, beyond_ref, column_ref, pair_ref, low_ref, ids_ref, basis_ref, slope_ref,
                 unit_ref, sums_ref, gate_ref):
    atoms = low_ref.shape[2]
    frame = [pair_ref, column_ref, beyond_ref]
    per_cell = atoms // 128
    places = lax.broadcasted_iota(jnp.int32, (4 * per_cell, 128), 0)
    upper = places % per_cell
    kind_of_row = places // per_cell
    to_x = jnp.where(kind_of_row == 0, cell_width, 0.0)
    to_x = jnp.where((place_ref[0] & 1) == 0, to_x, -to_x)
    to_y = jnp.where(kind_of_row == 1, cell_width, 0.0)
    to_y = jnp.where((place_ref[1] & 1) == 0, to_y, -to_y)
    for cell, block_ref in enumerate((y_pair_ref, own_ref, y_beyond_ref)):
        ids, count = block_ids(block_ref[...], atoms, slots * atoms)
        ids_ref[cell : cell + 1, :] = ids
        own = unfold_block(column_ref[cell + 1], atoms)
        step_y = to_y if cell == 1 else -to_y
        rows = []
        for a in range(3):
            for b in range(3):
                block = frame[a][SLOT_CELLS[cell][b]]
                rows.append(block + ((1 - a) * to_x + (1 - b) * step_y))
        first_cell(
            slots, atoms, ids, count, rows, places, upper, own, embed_ref, kind_left, mix_high,
            mix_low, low_ref.at[cell], basis_ref.at[cell], slope_ref.at[cell], unit_ref.at[cell],
            sums_ref.at[cell], gate_ref.at[cell],
        )


def first_cell(slots, atoms, ids, count, rows, places, upper, own, embed_ref, kind_left, mix_high,
               mix_low, low_ref, basis_ref, slope_ref, unit_ref, sums_ref, gate_ref):
    per_cell = atoms // 128
    pieces = []
    for start in range(0, ids.shape[1], 128):
        part = jnp.broadcast_to(ids[:, start : start + 128], places.shape)
        lane, half = part & 127, (part >> 7) - upper
        found = jnp.zeros(places.shape, F32)
        for cell, block in enumerate(rows):
            value = jnp.take_along_axis(block, lane, axis=1)
            found = jnp.where(half == per_cell * cell, value, found)
        total = found
        for s in range(1, per_cell):
            total = total + pltpu.roll(found, 4 * per_cell - s, 0)
        pieces.append(total)
    found = jnp.concatenate(pieces, axis=1)
    found = [found[q * per_cell : q * per_cell + 1] for q in range(4)]
    rel = [found[q] - jnp.concatenate([own[q]] * slots, axis=1) for q in range(3)]
    distance = jnp.sqrt(rel[0] * rel[0] + rel[1] * rel[1] + rel[2] * rel[2] + soften)
    inverse = 1.0 / distance
    order = (lax.broadcasted_iota(jnp.int32, (8, 1), 0) + 1).astype(F32)
    sine, cosine = sin_cos((order * (0.5 / cut_radius)) * distance)
    wave = sine / ((order * (math.pi / cut_radius)) * distance)
    live = jnp.concatenate([jnp.where(count > n, 1.0, 0.0) for n in range(slots)], axis=1)
    basis = wave * live
    basis_ref[...] = basis
    slope_ref[...] = (cosine - wave) * (inverse * live)
    kinds = found[3]
    unit = jnp.concatenate(
        [r * inverse for r in rel] + [inverse, kinds] + [jnp.zeros_like(kinds)] * 3, axis=0
    )
    unit_ref[...] = unit
    stack = embed_ref[...]
    parts = edge_parts(basis, unit)
    species = kind_left.shape[2] // 32
    by_kind = [[None] * species for _ in range(4)]
    for n in range(slots):
        lanes = slice(n * atoms, (n + 1) * atoms)
        kind = jnp.broadcast_to(kinds[:, lanes], (8, atoms))
        for k in range(species):
            match = kind == float(k)
            for part in range(4):
                term = jnp.where(match, parts[part][:, lanes], 0.0)
                old = by_kind[part][k]
                by_kind[part][k] = term if old is None else old + term
    stacks = [stacked_right(jnp.concatenate(rows, axis=0)) for rows in by_kind]
    vectors = dot(kind_left[1], jnp.concatenate(stacks[1:], axis=1))
    sums = [dot(kind_left[0], stacks[0])]
    sums += [vectors[:, i * atoms : (i + 1) * atoms] for i in range(3)]
    step, gate = mixed(sums, mix_high, mix_low, 0)
    low_ref[...] = (embedded(stack, own[3]) + step).astype(BF16)
    for part in range(3):
        sums_ref[part] = sums[part + 1]
    gate_ref[...] = gate


def hot_columns(ids, rows):
    place = lax.broadcasted_iota(jnp.int32, (rows, ids.shape[1]), 0)
    return jnp.where(ids == place, 1.0, 0.0).astype(BF16)


def second_near_kernel(slots, ids_ref, basis_ref, unit_ref, left_ref, column_ref, weight_ref,
                       near_ref):
    atoms = column_ref.shape[2]
    parts = edge_parts(basis_ref[1], unit_ref[1])
    source = jnp.concatenate([column_ref[b] for b in range(3)], axis=1)
    for n in range(slots):
        lanes = slice(n * atoms, (n + 1) * atoms)
        for part in range(4):
            weight_ref[part, :, lanes] = weights_of(left_ref, part, parts[part][:, lanes])
        ids = ids_ref[1:2, lanes] - 3 * atoms
        near_ref[:, lanes] = dot(source, hot_columns(ids, 3 * atoms))


def second_side_kernel(slots, ids_ref, near_ref, pair_ref, out_ref):
    atoms = pair_ref.shape[2]
    source = jnp.concatenate([pair_ref[b] for b in range(3)], axis=1)
    for n in range(slots):
        lanes = slice(n * atoms, (n + 1) * atoms)
        hot = hot_columns(ids_ref[1:2, lanes], 3 * atoms)
        out_ref[:, lanes] = near_ref[:, lanes] + dot(source, hot)


def second_kernel(slots, hot_ref, weight_ref, near_ref, mix_high, mix_low, charge_ref, cell_ref,
                  column_ref, beyond_ref, feature_ref, sums_ref, gate_ref, packed_ref,
                  full_charge_ref, hidden_ref):
    atoms = column_ref.shape[2]
    source = jnp.concatenate([beyond_ref[b] for b in range(3)], axis=1)
    sums = [None] * 4
    for n in range(slots):
        lanes = slice(n * atoms, (n + 1) * atoms)
        feature = near_ref[:, lanes] + dot(source, hot_ref[:, lanes])
        feature_ref[:, lanes] = feature.astype(BF16)
        for part in range(4):
            term = weight_ref[part, :, lanes] * feature
            sums[part] = term if sums[part] is None else sums[part] + term
    step, gate = mixed(sums, mix_high, mix_low, 1)
    hidden = column_ref[1].astype(F32) + step
    hidden_ref[...] = hidden
    for part in range(3):
        sums_ref[part] = sums[part + 1]
    gate_ref[...] = gate
    charge = dot_split((charge_ref[0], charge_ref[1]), hidden)
    full_charge_ref[...] = charge
    place = jnp.concatenate(unfold_block(cell_ref[2], atoms)[:3], axis=0)
    high = place.astype(BF16).astype(F32)
    rest = place - high
    middle = rest.astype(BF16).astype(F32)
    zero = jnp.zeros((packed_ref.shape[0] - charge.shape[0] - 9, atoms), F32)
    packed_ref[...] = jnp.concatenate([charge, high, middle, rest - middle, zero], axis=0).astype(
        BF16
    )


def readout_kernel(hidden_high, hidden_low, turn_high, turn_low, out_ref, hidden_ref, energy_ref,
                   slope_ref):
    hidden = hidden_ref[...]
    value, slope = silu_pair(dot_split((hidden_high[...], hidden_low[...]), hidden))
    out = out_ref[...].T
    energy_ref[...] = jnp.sum(value * out, axis=0, keepdims=True)
    slope_ref[...] = dot_split((turn_high[...], turn_low[...]), slope * out)


def message_grads(cotangent, gate_ref, sums_ref, high_ref, low_ref, layer):
    pre = cotangent * gate_ref[...]
    both = dot_split((high_ref[layer], low_ref[layer]), pre)
    half = both.shape[0] // 2
    return [both[:half]] + [both[half:] * sums_ref[i] for i in range(3)]


def radial_grad(left, value):
    high, low = split(value)
    both = dot(left, jnp.concatenate([high, low], axis=0))
    half = both.shape[0] // 2
    return both[:half] + both[half:]


def second_back_kernel(slots, scale, count, hot_ref, weight_ref, turn_high, turn_low, charge_ref,
                       sums_ref, gate_ref, full_charge_ref, energy_ref, slope_ref, *refs):
    folds, refs = refs[:count], refs[count:]
    site_ref, long_ref, cotangent_ref, grad_ref, term_ref, beyond_ref, pair_ref = refs
    atoms = gate_ref.shape[1]
    total = folds[0][...].astype(F32)
    for part in folds[1:]:
        total = total + part[...].astype(F32)
    wide = full_charge_ref.shape[0]
    potential = total[:wide] * (2.0 * scale)
    slopes = total[wide : wide + 3] + total[wide + 3 : wide + 6] + total[wide + 6 : wide + 9]
    long_ref[...] = jnp.concatenate(
        [slopes * (2.0 * scale), jnp.zeros((5, atoms), F32)], axis=0
    )
    site_ref[0] = energy_ref[...] + 0.5 * jnp.sum(
        full_charge_ref[...] * potential, axis=0, keepdims=True
    )
    high, low = split(potential)
    turned = ((0,), (0,))
    cotangent = slope_ref[...] + (
        dot(charge_ref[0], high, turned)
        + (dot(charge_ref[0], low, turned) + dot(charge_ref[1], high, turned))
    )
    cotangent_ref[...] = cotangent
    grads = message_grads(cotangent, gate_ref, sums_ref, turn_high, turn_low, 1)
    for part in range(4):
        grad_ref[part] = grads[part]
    for n in range(slots):
        lanes = slice(n * atoms, (n + 1) * atoms)
        term = weight_ref[0, :, lanes] * grads[0]
        for part in range(1, 4):
            term = term + weight_ref[part, :, lanes] * grads[part]
        term_ref[:, lanes] = term.astype(BF16)
    for b in range(3):
        start = (3 + b) * atoms
        beyond_ref[b] = dot(term_ref[...], hot_ref[:, start : start + atoms]).astype(BF16)
    for b in range(3):
        pair_ref[b] = dot(term_ref[...], hot_ref[:, b * atoms : (b + 1) * atoms]).astype(BF16)


def second_middle_kernel(hot_ref, term_ref, cotangent_ref, middle_ref):
    atoms = cotangent_ref.shape[1]
    for b in range(3):
        grad = dot(term_ref[...], hot_ref[:, b * atoms : (b + 1) * atoms])
        middle_ref[b] = grad + cotangent_ref[...] if b == 1 else grad


def second_edge_kernel(slots, back_ref, feature_ref, grad_ref, edge_ref):
    atoms = grad_ref.shape[2]
    for n in range(slots):
        lanes = slice(n * atoms, (n + 1) * atoms)
        feature = feature_ref[:, lanes].astype(F32)
        for part in range(4):
            edge_ref[8 * part : 8 * part + 8, lanes] = radial_grad(
                back_ref[1 if part else 0], grad_ref[part] * feature
            )


def first_back_kernel(slots, ids_ref, basis_ref, slope_ref, unit_ref, kind_high, kind_low, turn_high,
                      turn_low, sums_ref, gate_ref, edge_ref, from_beyond, long_ref, middle_ref,
                      from_pair, *outs):
    sums = {(1, 2): long_ref[...]}
    for cell in range(3):
        cotangent = middle_ref[cell] + (
            from_pair[cell].astype(F32) + from_beyond[cell].astype(F32)
        )
        own, found = first_back_cell(
            slots, ids_ref[cell : cell + 1, :], basis_ref.at[cell], slope_ref.at[cell],
            unit_ref.at[cell], kind_high, kind_low, turn_high, turn_low, sums_ref.at[cell],
            gate_ref.at[cell], edge_ref if cell == 1 else None, cotangent,
        )
        terms = [((1, cell + 1), own)]
        terms += [((n // 3, SLOT_CELLS[cell][n % 3]), found[n]) for n in range(9)]
        for key, term in terms:
            sums[key] = sums[key] + term if key in sums else term
    for x in range(3):
        rows = [sums[(x, y)][:3] for y in range(5)]
        outs[x][...] = jnp.concatenate(rows + [jnp.zeros((1, rows[0].shape[1]), F32)], axis=0)


def first_back_cell(slots, ids, basis_ref, slope_ref, unit_ref, kind_high, kind_low, turn_high,
                    turn_low, sums_ref, gate_ref, edge_ref, cotangent):
    atoms = gate_ref.shape[1]
    pre = cotangent * gate_ref[...]
    both = dot_split((turn_high[0], turn_low[0]), pre)
    wide = both.shape[0] // 2
    grads = [both[:wide]] + [both[wide:] * sums_ref[i] for i in range(3)]
    unit = unit_ref[...]
    kinds = unit[4:5]
    by_kind = [dot_split((kind_high[0], kind_low[0]), grads[0])]
    by_kind += [dot_split((kind_high[1], kind_low[1]), grads[i]) for i in range(1, 4)]
    species = by_kind[0].shape[0] // 8
    edges = [[] for _ in range(4)]
    for n in range(slots):
        kind = jnp.broadcast_to(kinds[:, n * atoms : (n + 1) * atoms], (8, atoms))
        matches = [kind == float(k) for k in range(1, species)]
        for part in range(4):
            rows = by_kind[part]
            found = rows[:8]
            for k, match in enumerate(matches):
                found = jnp.where(match, rows[8 * k + 8 : 8 * k + 16], found)
            edges[part].append(found)
    edges = [jnp.concatenate(rows, axis=1) for rows in edges]
    if edge_ref is not None:
        edges = [edge_ref[8 * part : 8 * part + 8] + edges[part] for part in range(4)]
    basis = basis_ref[...]
    units = [unit[i : i + 1] for i in range(3)]
    inverse = unit[3:4]
    by_basis = edges[0]
    for i in range(3):
        by_basis = by_basis + edges[i + 1] * units[i]
    by_unit = [jnp.sum(edges[i + 1] * basis, axis=0, keepdims=True) * inverse for i in range(3)]
    by_distance = jnp.sum(by_basis * slope_ref[...], axis=0, keepdims=True)
    for i in range(3):
        by_distance = by_distance - by_unit[i] * units[i]
    moves = [by_unit[i] + by_distance * units[i] for i in range(3)]
    zero = jnp.zeros_like(moves[0])
    move = jnp.concatenate(moves + [zero] * 5, axis=0)
    own = -move[:, :atoms]
    for n in range(1, slots):
        own = own - move[:, n * atoms : (n + 1) * atoms]
    lane_hot = hot_columns(ids & 127, 128)
    half = ids >> 7
    high = move.astype(BF16).astype(F32)
    both = jnp.concatenate([high, move - high], axis=0)
    per_cell = atoms // 128
    rows = jnp.concatenate(
        [jnp.where(half == h, both, 0.0).astype(BF16) for h in range(9 * per_cell)], axis=0
    )
    spread = dot(rows, lane_hot, ((1,), (1,)))
    grads = []
    for cell in range(9):
        found = []
        for h in range(cell * per_cell, (cell + 1) * per_cell):
            found.append(spread[16 * h : 16 * h + 8] + spread[16 * h + 8 : 16 * h + 16])
        grads.append(jnp.concatenate(found, axis=1))
    return own, grads


def pair_counts(parts):
    total = WAVE_REACH + WAVE_REACH * (2 * WAVE_REACH + 1)
    share = -(-total // parts)
    return total, share, -(-share // 16) * 16


def pair_vectors(slot, share, part):
    side = 2 * WAVE_REACH + 1
    total = WAVE_REACH + WAVE_REACH * side
    index = slot + part.astype(F32) * share
    later = index - WAVE_REACH
    row = jnp.floor((later + 0.5) * (1.0 / side))
    first = index < WAVE_REACH
    kx = jnp.where(first, 0.0, row + 1.0)
    ky = jnp.where(first, index + 1.0, later - row * side - WAVE_REACH)
    valid = jnp.where((slot < share) & (index < total), 1.0, 0.0)
    return kx, ky, valid


def count_up(rows):
    return lax.broadcasted_iota(jnp.int32, (rows, 1), 0).astype(F32)


def green_weights(share, padded, grid, place_ref, vec_ref, weight_ref):
    grid_x, grid_y = grid
    turn = 2.0 * math.pi
    side = 2 * WAVE_REACH + 1
    top = side * side * side - 1
    vec = vec_ref[...].astype(F32) + WAVE_REACH
    code = (vec[0:1] * side + vec[1:2]) * side + vec[2:3]
    code = jnp.maximum(code, top - code)
    span = 8 * share
    row = count_up(span)
    slot = jnp.floor(row * 0.125)
    height = row - 8.0 * slot + 1.0
    flat = count_up(padded)
    slot = jnp.concatenate([slot, slot, flat], axis=0)
    kz = jnp.concatenate([height, -height, jnp.zeros_like(flat)], axis=0)
    kx, ky, valid = pair_vectors(slot, share, place_ref[0, 0:1, 0:1])
    own = ((kx + WAVE_REACH) * side + ky + WAVE_REACH) * side + kz + WAVE_REACH
    seen = jnp.zeros((own.shape[0], 128), F32)
    for start in range(0, code.shape[1], 128):
        seen = seen + jnp.where(own == code[:, start : start + 128], 1.0, 0.0)
    count = jnp.sum(seen, axis=1, keepdims=True) * valid
    sq = (
        (kx * (turn / (grid_x * cell_width))) ** 2
        + (ky * (turn / (grid_y * cell_width))) ** 2
        + (kz * (turn / box_height)) ** 2
    )
    green = jnp.exp(-smear_width * sq) / (sq + screen * screen) * count
    weight_ref[...] = jnp.broadcast_to(green, weight_ref.shape)


def basis_rows(share, ca, sa, cb, sb):
    cc, ss, sc, cs = [], [], [], []
    for p in range(share):
        c, s = ca[p : p + 1], sa[p : p + 1]
        cc.append(c * cb)
        ss.append(s * sb)
        sc.append(s * cb)
        cs.append(c * sb)
    return cc, ss, sc, cs


def unpack_rows(block):
    half = block.shape[1] // 2
    return jnp.concatenate([block[:, :half], block[:, half:]], axis=0)


def pack_rows(block):
    half = block.shape[0] // 2
    return jnp.concatenate([block[:half], block[half:]], axis=1)


def structure_kernel(share, padded, grid, wide, flip, place_ref, blocks, *refs):
    grid_x, grid_y = grid
    if flip:
        near_ref, (ca_ref, sa_ref, cb_ref, sb_ref, high_ref, low_ref, own_ref, out_ref) = (
            refs[0],
            refs[1:],
        )
        total = near_ref[...]
    else:
        ca_ref, sa_ref, cb_ref, sb_ref, high_ref, low_ref, total_ref = refs
        total = None
    col = place_ref[1, 0:1, 0:1].astype(F32) * (1.0 / grid_y)
    first = place_ref[0, 0:1, 0:1] ^ flip
    kx, ky, _ = pair_vectors(count_up(padded), share, place_ref[0, 0:1, 0:1])
    kz = count_up(8) + 1.0
    for d in range(grid_x // 2):
        block = blocks[d]
        charge = block[:wide]
        atoms = charge.shape[1]
        pieces = block[wide:].astype(F32)
        place = pieces[0:3] + (pieces[3:6] + pieces[6:9])
        row = (first ^ (2 * d)).astype(F32) * (1.0 / grid_x)
        x = place[0:1] * (1.0 / (grid_x * cell_width)) + row
        y = place[1:2] * (1.0 / (grid_y * cell_width)) + col
        sa, ca = sin_cos(kx * x + ky * y)
        sb, cb = sin_cos(kz * (place[2:3] * (1.0 / box_height)))
        lanes = pl.ds(d * atoms, atoms)
        ca_ref[:, lanes] = ca
        sa_ref[:, lanes] = sa
        cb_ref[:, lanes] = cb
        sb_ref[:, lanes] = sb
        cc, ss, sc, cs = basis_rows(share, ca, sa, cb, sb)
        high, low = split(jnp.concatenate(cc + ss + sc + cs + [ca, sa], axis=0))
        high_ref[:, lanes] = high
        low_ref[:, lanes] = low
        term = dot(high, charge, ((1,), (1,))) + dot(low, charge, ((1,), (1,)))
        total = term if total is None else total + term
    if flip:
        packed = pack_rows(total)
        own_ref[...] = packed
        out_ref[...] = packed.astype(BF16)
    else:
        total_ref[...] = total


def weighted_rows(share, padded, wide, weight_ref, parts):
    packed = parts[0][...].astype(F32)
    for part in parts[1:]:
        packed = packed + part[...].astype(F32)
    struct = unpack_rows(packed)
    span = 8 * share
    cc, ss, sc, cs = (struct[i * span : (i + 1) * span] for i in range(4))
    weight = weight_ref[:, :wide]
    plus, minus, flat = weight[:span], weight[span : 2 * span], weight[2 * span :]
    re_plus, im_plus = plus * (cc - ss), plus * (sc + cs)
    re_minus, im_minus = minus * (cc + ss), minus * (sc - cs)
    rows = jnp.concatenate(
        [
            re_plus + re_minus,
            re_minus - re_plus,
            im_plus + im_minus,
            im_plus - im_minus,
            flat * struct[4 * span : 4 * span + padded],
            flat * struct[4 * span + padded :],
        ],
        axis=0,
    )
    return rows


def fold_kernel(share, padded, grid, wide, flip, place_ref, *refs):
    grid_x, grid_y = grid
    turn = 2.0 * math.pi
    if flip:
        weight_ref, parts, refs = refs[0], refs[1 : 1 + grid_y], refs[1 + grid_y :]
        rows = weighted_rows(share, padded, wide, weight_ref, parts)
        refs, rows_ref = refs[:-1], refs[-1]
        rows_ref[...] = rows
    else:
        rows, refs = refs[0][...], refs[1:]
    ca_ref, sa_ref, cb_ref, sb_ref, high_ref, low_ref, blocks, out_ref = refs
    row_high, row_low = split(rows)
    row_pair = jnp.concatenate([row_high, row_low], axis=1)
    turned = rows.T
    t_high, t_low = split(turned)
    t_both = jnp.concatenate([t_high, t_low], axis=0)
    span = 8 * share
    kx, ky, _ = pair_vectors(count_up(padded), share, place_ref[0, 0:1, 0:1])
    kx = kx * (turn / (grid_x * cell_width))
    ky = ky * (turn / (grid_y * cell_width))
    kz = (count_up(8) + 1.0) * (turn / box_height)
    for d in range(grid_x // 2):
        charge = blocks[d][:wide]
        atoms = charge.shape[1]
        lanes = pl.ds(d * atoms, atoms)
        ca, sa, cb, sb = ca_ref[:, lanes], sa_ref[:, lanes], cb_ref[:, lanes], sb_ref[:, lanes]
        bcc, bss, bsc, bcs = basis_rows(share, ca, sa, cb, sb)
        high, low = high_ref[:, lanes], low_ref[:, lanes]
        both = dot(t_both, high)
        pot = both[:wide] + both[wide:] + dot(t_high, low)
        proj = dot(row_pair, jnp.concatenate([charge, charge], axis=0))
        by_x = jnp.zeros((8, atoms), jnp.float32)
        by_y = jnp.zeros((8, atoms), jnp.float32)
        by_z = jnp.zeros((8, atoms), jnp.float32)
        for p in range(share):
            pcc, pss, psc, pcs = (
                proj[i * span + 8 * p : i * span + 8 * p + 8] for i in range(4)
            )
            slope = bcs[p] * pss - bsc[p] * pcc + bcc[p] * psc - bss[p] * pcs
            by_x = by_x + kx[p : p + 1] * slope
            by_y = by_y + ky[p : p + 1] * slope
            by_z = by_z + (bsc[p] * pss - bcs[p] * pcc - bss[p] * psc + bcc[p] * pcs)
        flat_slope = ca * proj[4 * span + padded :] - sa * proj[4 * span : 4 * span + padded]
        grad_x = jnp.sum(by_x, axis=0, keepdims=True) + jnp.sum(kx * flat_slope, axis=0, keepdims=True)
        grad_y = jnp.sum(by_y, axis=0, keepdims=True) + jnp.sum(ky * flat_slope, axis=0, keepdims=True)
        grad_z = jnp.sum(kz * by_z, axis=0, keepdims=True)
        slopes = jnp.concatenate([grad_x, grad_y, grad_z], axis=0)
        out_ref[d] = pieced(pot, slopes, out_ref.shape[1]).astype(out_ref.dtype)


def pieced(pot, slopes, rows):
    high = slopes.astype(BF16).astype(F32)
    rest = slopes - high
    middle = rest.astype(BF16).astype(F32)
    zero = jnp.zeros((rows - pot.shape[0] - 9, pot.shape[1]), F32)
    return jnp.concatenate([pot, high, middle, rest - middle, zero], axis=0)


def unpieced(block, wide):
    slopes = block[wide : wide + 3] + (block[wide + 3 : wide + 6] + block[wide + 6 : wide + 9])
    return block[:wide], slopes


def join_kernel(wide, near_ref, far_ref, own_ref, *outs):
    for d in range(near_ref.shape[0]):
        pot, slopes = unpieced(near_ref[d], wide)
        pot_far, slopes_far = unpieced(far_ref[d].astype(F32), wide)
        block = pieced(pot + pot_far, slopes + slopes_far, near_ref.shape[1])
        if d:
            outs[d - 1][...] = block.astype(BF16)
        else:
            own_ref[...] = block


def per_device(
    positions,
    species,
    neighbours,
    counts,
    species_embed,
    radial,
    mixing,
    read_hidden,
    read_out,
    charge_map,
    wavevectors,
):
    atoms = positions.shape[3]
    slots = neighbours.shape[3]
    features, lat_width = charge_map.shape
    wave_count = wavevectors.shape[1]
    grid = lax.axis_size("gx"), lax.axis_size("gy")
    grid_x, grid_y = grid
    edges = slots * atoms
    scale = 1.0 / math.sqrt(wave_count * lat_width * atoms * grid_x * grid_y)
    place = jnp.stack([lax.axis_index("gx"), lax.axis_index("gy")]).astype(jnp.int32)
    place = jnp.broadcast_to(place[:, None, None], (2, 8, 128))
    _, share, padded = pair_counts(grid_x)
    ids = neighbours.transpose(0, 3, 1, 2).reshape(1, edges)
    cell_rows = 4 * atoms // 128
    block_total = -(-(cell_rows + (edges + atoms) // 128) // 8) * 8
    dma = pltpu.SemaphoreType.DMA
    shown = positions.transpose(0, 2, 1, 3)
    (own_place,) = run(
        pack_kernel,
        [shape(cell_rows, 128)],
        [place, shown, species],
        flops=10_000_000_000,
        name="pack",
    )
    (own,) = run(
        pack_more_kernel,
        [shape(block_total, 128)],
        [place, ids, counts, own_place],
        name="pack_more",
    )
    y_beyond, y_pair = beyond(own, "gy"), paired(own, "gy", 1)
    over_pair = far(own_place, "gy", True)
    over_beyond = over_pair if grid_y == 4 else far(own_place, "gy", False)
    cells = jnp.stack(
        [over_pair, y_pair[:cell_rows], own_place, y_beyond[:cell_rows], over_beyond]
    )
    x_beyond, x_pair = beyond(cells, "gx"), paired(cells, "gx", 1)
    cells = [x_pair, cells, x_beyond]

    norm = 1.0 / math.sqrt(slots)
    kind_rows = 8 * species_embed.shape[0]
    low_pair = lambda *dims: [shape(*dims, dtype=BF16)] * 2
    embed, kind_left, left, back, kind_high, kind_low, mix_high, mix_low, turn_high, turn_low = run(
        functools.partial(prep_first_kernel, norm),
        [
            shape(features, 32, dtype=BF16),
            shape(2, features, 4 * kind_rows, dtype=BF16),
            shape(2, features, 32, dtype=BF16),
            shape(2, 16, 2 * features, dtype=BF16),
        ]
        + low_pair(2, kind_rows, features)
        + low_pair(2, features, 2 * features)
        + low_pair(2, 2 * features, features),
        [species_embed, radial, mixing],
        scratch=[
            pltpu.VMEM(species_embed.shape, F32),
            pltpu.VMEM(radial.shape, F32),
            pltpu.VMEM(mixing.shape, F32),
            dma((3,)),
        ],
        hbm=3,
        name="prep_first",
    )
    read_out, hidden_high, hidden_low, hidden_turn_high, hidden_turn_low, charge_pair = run(
        prep_second_kernel,
        [shape(1, features)]
        + low_pair(features, features)
        + low_pair(features, features)
        + [shape(2, lat_width, features, dtype=BF16)],
        [read_out[None, :], read_hidden, charge_map.T],
        scratch=[
            pltpu.VMEM(read_hidden.shape, F32),
            pltpu.VMEM((lat_width, features), F32),
            dma((3,)),
        ],
        hbm=3,
        name="prep_second",
    )
    cells[2], hidden_high = lax.optimization_barrier((cells[2], hidden_high))
    low, ids, basis, slope, unit, sums_one, gate_one = run(
        functools.partial(first_kernel, slots),
        [
            shape(3, features, atoms, dtype=BF16),
            shape(3, edges, dtype=jnp.int32),
            shape(3, 8, edges),
            shape(3, 8, edges),
            shape(3, 8, edges),
            shape(3, 3, features, atoms),
            shape(3, features, atoms),
        ],
        [place, embed, kind_left, mix_high, mix_low, y_beyond, own, y_pair] + cells[::-1],
        name="first",
    )
    hidden = [paired(low, "gx", 1), low, beyond(low, "gx")]
    edge_weights, near = run(
        functools.partial(second_near_kernel, slots),
        [shape(4, features, edges), shape(features, edges)],
        [ids, basis, unit, left, low],
        flops=2_000_000_000,
        name="second_near",
    )
    (hot_beyond,) = run(
        hot_beyond_kernel,
        [shape(3 * atoms, edges, dtype=BF16)],
        [ids, near],
        flops=1_000_000,
        name="hot_beyond",
    )
    (near,) = run(
        functools.partial(second_side_kernel, slots),
        [shape(features, edges)],
        [ids, near, hidden[0]],
        flops=1_000_000_000,
        name="second_side",
    )
    block_rows = -(-(lat_width + 9) // 16) * 16
    feature, sums_two, gate_two, packed, charge, hidden_two = run(
        functools.partial(second_kernel, slots),
        [
            shape(features, edges, dtype=BF16),
            shape(3, features, atoms),
            shape(features, atoms),
            shape(block_rows, atoms, dtype=BF16),
            shape(lat_width, atoms),
            shape(features, atoms),
        ],
        [hot_beyond, edge_weights, near, mix_high, mix_low, charge_pair, cells[1], hidden[1],
         hidden[2]],
        name="second",
    )
    energy, energy_slope = run(
        readout_kernel,
        [shape(1, atoms), shape(features, atoms)],
        [hidden_high, hidden_low, hidden_turn_high, hidden_turn_low, read_out, hidden_two],
        name="readout",
    )
    half = grid_x // 2
    near_charges = jnp.stack([packed] + [paired(packed, "gx", 2 * d) for d in range(1, half)])
    (weight,) = run(
        functools.partial(green_weights, share, padded, grid),
        [shape(16 * share + padded, 128)],
        [place, wavevectors],
        name="green",
    )
    near_charges, weight = lax.optimization_barrier((near_charges, weight))
    far_charges = paired(near_charges, "gx", 1)
    span = half * atoms
    rows = 32 * share + 2 * padded
    phase_shapes = [
        shape(padded, span),
        shape(padded, span),
        shape(8, span),
        shape(8, span),
        shape(rows, span, dtype=BF16),
        shape(rows, span, dtype=BF16),
    ]
    *near_phases, near_total = run(
        functools.partial(structure_kernel, share, padded, grid, lat_width, 0),
        phase_shapes + [shape(rows, lat_width)],
        [place, near_charges],
        flops=1_000_000_000,
        name="structure_near",
    )
    *far_phases, own_part, part = run(
        functools.partial(structure_kernel, share, padded, grid, lat_width, 1),
        phase_shapes
        + [
            shape(rows // 2, 2 * lat_width),
            shape(rows // 2, 2 * lat_width, dtype=BF16),
        ],
        [place, far_charges, near_total],
        name="structure_far",
    )
    parts = [own_part] + [paired(part, "gy", d) for d in range(1, grid_y)]
    (hot_back,) = run(
        functools.partial(hot_back_kernel, (0, 2)),
        [shape(edges, 6 * atoms, dtype=BF16)],
        [ids],
        flops=2_000_000_000,
        name="hot_back",
    )
    parts, hot_back = lax.optimization_barrier((parts, hot_back))
    far_folds, wave_rows = run(
        functools.partial(fold_kernel, share, padded, grid, lat_width, 1),
        [shape(half, block_rows, atoms, dtype=BF16), shape(rows, lat_width)],
        [place, weight] + parts + far_phases + [far_charges],
        name="fold_far",
    )
    far_folds = paired(far_folds, "gx", 1)
    (near_folds,) = run(
        functools.partial(fold_kernel, share, padded, grid, lat_width, 0),
        [shape(half, block_rows, atoms)],
        [place, wave_rows] + near_phases + [near_charges],
        flops=1_000_000_000,
        name="fold_near",
    )
    folds = run(
        functools.partial(join_kernel, lat_width),
        [shape(block_rows, atoms)] + [shape(block_rows, atoms, dtype=BF16)] * (half - 1),
        [near_folds, far_folds],
        name="fold_join",
    )
    folds = [folds[0]] + [paired(folds[d], "gx", 2 * d) for d in range(1, half)]

    site, long, cotangent, grads, term, to_beyond, to_pair = run(
        functools.partial(second_back_kernel, slots, scale, half),
        [
            shape(1, 1, atoms),
            shape(8, atoms),
            shape(features, atoms),
            shape(4, features, atoms),
            shape(features, edges, dtype=BF16),
            shape(3, features, atoms, dtype=BF16),
            shape(3, features, atoms, dtype=BF16),
        ],
        [hot_back, edge_weights, turn_high, turn_low, charge_pair, sums_two, gate_two, charge,
         energy, energy_slope] + folds,
        name="second_back",
    )
    from_pair, from_beyond = paired(to_pair, "gx", 1), beyond(to_beyond, "gx")
    (hot_middle,) = run(
        functools.partial(hot_back_kernel, (1,)),
        [shape(edges, 3 * atoms, dtype=BF16)],
        [ids],
        flops=1_000_000_000,
        name="hot_middle",
    )
    (middle,) = run(
        second_middle_kernel,
        [shape(3, features, atoms)],
        [hot_middle, term, cotangent],
        flops=1_000_000_000,
        name="second_middle",
    )
    (edge,) = run(
        functools.partial(second_edge_kernel, slots),
        [shape(32, edges)],
        [back, feature, grads],
        flops=1_000_000_000,
        name="second_edge",
    )
    to_pair, middle, to_beyond = run(
        functools.partial(first_back_kernel, slots),
        [shape(16, atoms)] * 3,
        [ids, basis, slope, unit, kind_high, kind_low, turn_high, turn_low, sums_one, gate_one, edge,
         from_beyond, long, middle, from_pair],
        name="first_back",
    )
    total = middle + paired(to_pair, "gx", 1) + beyond(to_beyond, "gx")
    total = [total[3 * y : 3 * y + 3] for y in range(5)]
    if grid_y == 4:
        distant = far(total[0] + total[4], "gy", True)
    else:
        distant = far(total[0], "gy", False) + far(total[4], "gy", True)
    total = total[2] + paired(total[1], "gy", 1) + beyond(total[3], "gy") + distant
    forces = -total[None, :, None, :]
    return (forces.transpose(0, 2, 1, 3), site)


def solution(mesh):
    in_specs = (
        P("gx", "gy", None, None),
        P("gx", "gy", None),
        P("gx", "gy", None, None),
        P("gx", "gy", None),
        P(),
        P(),
        P(),
        P(),
        P(),
        P(),
        P(),
    )
    out_specs = (P("gx", "gy", None, None), P("gx", "gy", None))
    return jax.shard_map(
        per_device, mesh=mesh, in_specs=in_specs, out_specs=out_specs, check_vma=False
    )
```

```python
import functools
import math

import jax
import jax.numpy as jnp
import numpy as np
from jax import lax
from jax.experimental import pallas as pl
from jax.experimental.pallas import tpu as pltpu
from jax.sharding import PartitionSpec as P

cell_width = 10.0
box_height = 30.0
cut_radius = 50.0
soften = 0.25
screen = 0.5
smear_width = 0.5
WAVE_REACH = 8
F32 = jnp.float32
BF16 = jnp.bfloat16


def paired(block, axis, mask):
    return lax.ppermute(block, axis, [(i ^ mask, i) for i in range(lax.axis_size(axis))])


def other_side(index, count):
    return (index + (1 if index % 2 else -1)) % count


def beyond(block, axis):
    count = lax.axis_size(axis)
    return lax.ppermute(block, axis, [(other_side(i, count), i) for i in range(count)])


def far(block, axis, over_pair):
    count = lax.axis_size(axis)
    if over_pair:
        route = [(other_side(i ^ 1, count), i) for i in range(count)]
    else:
        route = [(other_side(i, count) ^ 1, i) for i in range(count)]
    return lax.ppermute(block, axis, route)


SLOT_CELLS = ((2, 1, 0), (1, 2, 3), (4, 3, 2))


def whole(space=pltpu.VMEM):
    return pl.BlockSpec(memory_space=space)


def run(kernel, outs, args, scratch=(), hbm=0, flops=10_000_000, grant=16, name=None):
    specs = [whole()] * (len(args) - hbm) + [whole(pltpu.HBM)] * hbm
    return list(
        pl.pallas_call(
            kernel,
            out_shape=outs,
            in_specs=specs,
            out_specs=[whole() for _ in outs],
            scratch_shapes=list(scratch),
            compiler_params=pltpu.CompilerParams(vmem_limit_bytes=grant * 1024 * 1024),
            cost_estimate=pl.CostEstimate(
                flops=flops, bytes_accessed=1_000_000, transcendentals=0
            ),
            name=name,
        )(*args)
    )


def shape(*dims, dtype=F32):
    return jax.ShapeDtypeStruct(dims, dtype)


def split(value):
    high = value.astype(BF16)
    return high, (value - high.astype(F32)).astype(BF16)


def dot(left, right, contract=((1,), (0,))):
    return lax.dot_general(left, right, (contract, ((), ())), preferred_element_type=F32)


def dot3(left, right):
    left_high, left_low = split(left)
    right_high, right_low = split(right)
    return dot(left_high, right_high) + (dot(left_high, right_low) + dot(left_low, right_high))


def dot_split(left, right):
    right_high, right_low = split(right)
    return dot(left[0], right_high) + (dot(left[0], right_low) + dot(left[1], right_high))


def sin_cos(turns):
    quarter = jnp.round(turns * 4.0)
    x = (turns - quarter * 0.25) * (2.0 * math.pi)
    z = x * x
    sine = ((-1.9515295891e-4 * z + 8.3321608736e-3) * z - 1.6666654611e-1) * (z * x) + x
    cosine = (2.443315711809948e-5 * z - 1.388731625493765e-3) * z + 4.166664568298827e-2
    cosine = cosine * (z * z) - 0.5 * z + 1.0
    k = quarter.astype(jnp.int32) & 3
    odd = (k & 1) == 1
    by_sine = jnp.where(odd, cosine, sine)
    by_cosine = jnp.where(odd, sine, cosine)
    return (
        jnp.where(k >= 2, -by_sine, by_sine),
        jnp.where((k == 1) | (k == 2), -by_cosine, by_cosine),
    )


def stacked_left(value):
    high = value.astype(BF16).astype(F32)
    rows = jnp.concatenate([high, high, value - high, jnp.zeros_like(high)], axis=0)
    return rows.T.astype(BF16)


def stacked_right(value):
    high = value.astype(BF16).astype(F32)
    return jnp.concatenate([high, value - high, high, jnp.zeros_like(high)], axis=0).astype(BF16)


def silu_pair(value):
    gate = 1.0 / (1.0 + jnp.exp(-value))
    return value * gate, gate * (1.0 + value * (1.0 - gate))


def onehot_kinds(kinds, rows):
    levels = lax.broadcasted_iota(jnp.int32, (rows, kinds.shape[1]), 0).astype(F32)
    return jnp.where(kinds == levels, 1.0, 0.0)


def embedding_stack(embed):
    high = embed.astype(BF16).astype(F32)
    rest = embed - high
    middle = rest.astype(BF16).astype(F32)
    rows = jnp.concatenate([high, middle, rest - middle, jnp.zeros_like(high)], axis=0)
    return rows.T.astype(BF16)


def embedded(stack, kinds):
    hot = onehot_kinds(kinds, 8)
    return dot(stack, jnp.concatenate([hot, hot, hot, jnp.zeros_like(hot)], axis=0).astype(BF16))


def weights_of(stack_ref, part, rows):
    return dot(stack_ref[1 if part else 0], stacked_right(rows))


def mixed(sums, high_ref, low_ref, layer):
    squares = sums[1] * sums[1] + sums[2] * sums[2] + sums[3] * sums[3]
    both = jnp.concatenate([sums[0], squares], axis=0)
    return silu_pair(dot_split((high_ref[layer], low_ref[layer]), both))


def edge_parts(basis, unit):
    return [basis] + [basis * unit[i : i + 1] for i in range(3)]


def pack_kernel(place_ref, position_ref, species_ref, out_ref):
    rows = [position_ref[0, i] for i in range(3)] + [species_ref[0].astype(F32)]
    atoms = rows[0].shape[1]
    out_ref[...] = jnp.concatenate(
        [row[:, s : s + 128] for row in rows for s in range(0, atoms, 128)], axis=0
    )


def pack_more_kernel(place_ref, ids_ref, count_ref, first_ref, out_ref):
    atoms = count_ref.shape[2]
    order = slot_order(ids_ref[...], place_ref, atoms).astype(F32)
    rows = [first_ref[...]]
    rows += [order[:, s : s + 128] for s in range(0, order.shape[1], 128)]
    rows += [count_ref[0, :, s : s + 128].astype(F32) for s in range(0, atoms, 128)]
    missing = out_ref.shape[0] - sum(row.shape[0] for row in rows)
    out_ref[...] = jnp.concatenate(rows + [jnp.zeros((missing, 128), F32)], axis=0)


def block_ids(block, atoms, edges):
    start = 4 * atoms // 128
    middle, end = start + edges // 128, start + edges // 128 + atoms // 128
    rows = [block[r : r + 1] for r in range(start, end)]
    ids = jnp.concatenate(rows[: middle - start], axis=1).astype(jnp.int32)
    return ids, jnp.concatenate(rows[middle - start :], axis=1)


def radial_left(radial):
    high = radial.astype(BF16).astype(F32)
    low = radial - high
    top = jnp.concatenate([high, high], axis=1)
    end = jnp.concatenate([low, jnp.zeros_like(low)], axis=1)
    return jnp.concatenate([top, end], axis=0).astype(BF16)


def put_split(value, high_ref, low_ref, *at):
    high, low = split(value)
    high_ref[at] = high
    low_ref[at] = low


def slot_order(ids, place_ref, atoms):
    cell = ids >> (atoms.bit_length() - 1) if atoms & (atoms - 1) == 0 else ids // atoms
    a = (cell * 11) >> 5
    b = cell - 3 * a
    a = jnp.where((place_ref[0, 0:1, 0:1] & 1) == 0, 2 - a, a)
    b = jnp.where((place_ref[1, 0:1, 0:1] & 1) == 0, 2 - b, b)
    return ids + (3 * a + b - cell) * atoms


def fetch(sources, targets, sems):
    copies = [
        pltpu.make_async_copy(source, target, sems.at[i])
        for i, (source, target) in enumerate(zip(sources, targets))
    ]
    for copy in copies:
        copy.start()
    for copy in copies:
        copy.wait()


def prep_first_kernel(norm, embed_in, radial_in, mixing_in, embed_out, kind_left, left_out, back_out,
                      kind_high, kind_low, mix_high, mix_low, turn_high, turn_low, embed_ref,
                      radial_ref, mixing_ref, sems):
    fetch([embed_in, radial_in, mixing_in], [embed_ref, radial_ref, mixing_ref], sems)
    embed = embed_ref[...]
    kinds = embed.shape[0]
    for path in range(2):
        radial = radial_ref[0, path] * norm
        rows = jnp.concatenate([radial * embed[s : s + 1] for s in range(kinds)], axis=0)
        kind_left[path] = stacked_left(rows)
        put_split(rows, kind_high, kind_low, path)
        radial = radial_ref[1, path] * norm
        left_out[path] = stacked_left(radial)
        back_out[path] = radial_left(radial)
    for layer in range(2):
        scalar, vector = mixing_ref[layer, 0], mixing_ref[layer, 1]
        put_split(jnp.concatenate([scalar.T, vector.T], axis=1), mix_high, mix_low, layer)
        put_split(jnp.concatenate([scalar, 2.0 * vector], axis=0), turn_high, turn_low, layer)
    embed = jnp.concatenate([embed, jnp.zeros((8 - kinds, embed.shape[1]), F32)], axis=0)
    embed_out[...] = embedding_stack(embed)


def prep_second_kernel(read_in, hidden_in, charge_in, read_ref, hidden_high, hidden_low,
                       hidden_turn_high, hidden_turn_low, charge_pair, hidden_ref, charge_ref, sems):
    fetch([read_in, hidden_in, charge_in], [read_ref, hidden_ref, charge_ref], sems)
    put_split(hidden_ref[...].T, hidden_high, hidden_low, Ellipsis)
    put_split(hidden_ref[...], hidden_turn_high, hidden_turn_low, Ellipsis)
    charge = charge_ref[...]
    high = charge.astype(BF16).astype(F32)
    charge_pair[0] = high.astype(BF16)
    charge_pair[1] = (charge - high).astype(BF16)


def hot_beyond_kernel(ids_ref, near_ref, hot_ref):
    ids = ids_ref[1:2, :] - 2 * hot_ref.shape[0]
    for start in range(0, hot_ref.shape[1], 256):
        lanes = slice(start, start + 256)
        hot_ref[:, lanes] = hot_columns(ids[:, lanes], hot_ref.shape[0])


def hot_back_kernel(slots_x, ids_ref, hot_ref):
    edges = ids_ref.shape[1]
    width = hot_ref.shape[1] // len(slots_x)
    entry = lax.broadcasted_iota(jnp.int32, (128, width), 1).astype(F32)
    for start in range(0, edges, 128):
        row = jnp.broadcast_to(ids_ref[1:2, start : start + 128].astype(F32), (8, 128))
        column = row.T[:, 0:1]
        for n, slot in enumerate(slots_x):
            hot_ref[start : start + 128, n * width : (n + 1) * width] = jnp.where(
                column - float(slot * width) == entry, 1.0, 0.0
            ).astype(BF16)


def unfold_block(block, atoms):
    parts = atoms // 128
    rows = [block[r : r + 1] for r in range(4 * parts)]
    return [jnp.concatenate(rows[q * parts : (q + 1) * parts], axis=1) for q in range(4)]


def first_kernel(slots, place_ref, embed_ref, kind_left, mix_high, mix_low, y_beyond_ref, own_ref,
                 y_pair_ref, beyond_ref, column_ref, pair_ref, low_ref, ids_ref, basis_ref, slope_ref,
                 unit_ref, sums_ref, gate_ref):
    atoms = low_ref.shape[2]
    frame = [pair_ref, column_ref, beyond_ref]
    per_cell = atoms // 128
    places = lax.broadcasted_iota(jnp.int32, (4 * per_cell, 128), 0)
    upper = places % per_cell
    kind_of_row = places // per_cell
    to_x = jnp.where(kind_of_row == 0, cell_width, 0.0)
    to_x = jnp.where((place_ref[0] & 1) == 0, to_x, -to_x)
    to_y = jnp.where(kind_of_row == 1, cell_width, 0.0)
    to_y = jnp.where((place_ref[1] & 1) == 0, to_y, -to_y)
    for cell, block_ref in enumerate((y_pair_ref, own_ref, y_beyond_ref)):
        ids, count = block_ids(block_ref[...], atoms, slots * atoms)
        ids_ref[cell : cell + 1, :] = ids
        own = unfold_block(column_ref[cell + 1], atoms)
        step_y = to_y if cell == 1 else -to_y
        rows = []
        for a in range(3):
            for b in range(3):
                block = frame[a][SLOT_CELLS[cell][b]]
                rows.append(block + ((1 - a) * to_x + (1 - b) * step_y))
        first_cell(
            slots, atoms, ids, count, rows, places, upper, own, embed_ref, kind_left, mix_high,
            mix_low, low_ref.at[cell], basis_ref.at[cell], slope_ref.at[cell], unit_ref.at[cell],
            sums_ref.at[cell], gate_ref.at[cell],
        )


def first_cell(slots, atoms, ids, count, rows, places, upper, own, embed_ref, kind_left, mix_high,
               mix_low, low_ref, basis_ref, slope_ref, unit_ref, sums_ref, gate_ref):
    per_cell = atoms // 128
    pieces = []
    for start in range(0, ids.shape[1], 128):
        part = jnp.broadcast_to(ids[:, start : start + 128], places.shape)
        lane, half = part & 127, (part >> 7) - upper
        found = jnp.zeros(places.shape, F32)
        for cell, block in enumerate(rows):
            value = jnp.take_along_axis(block, lane, axis=1)
            found = jnp.where(half == per_cell * cell, value, found)
        total = found
        for s in range(1, per_cell):
            total = total + pltpu.roll(found, 4 * per_cell - s, 0)
        pieces.append(total)
    found = jnp.concatenate(pieces, axis=1)
    found = [found[q * per_cell : q * per_cell + 1] for q in range(4)]
    rel = [found[q] - jnp.concatenate([own[q]] * slots, axis=1) for q in range(3)]
    distance = jnp.sqrt(rel[0] * rel[0] + rel[1] * rel[1] + rel[2] * rel[2] + soften)
    inverse = 1.0 / distance
    order = (lax.broadcasted_iota(jnp.int32, (8, 1), 0) + 1).astype(F32)
    sine, cosine = sin_cos((order * (0.5 / cut_radius)) * distance)
    wave = sine / ((order * (math.pi / cut_radius)) * distance)
    live = jnp.concatenate([jnp.where(count > n, 1.0, 0.0) for n in range(slots)], axis=1)
    basis = wave * live
    basis_ref[...] = basis
    slope_ref[...] = (cosine - wave) * (inverse * live)
    kinds = found[3]
    unit = jnp.concatenate(
        [r * inverse for r in rel] + [inverse, kinds] + [jnp.zeros_like(kinds)] * 3, axis=0
    )
    unit_ref[...] = unit
    stack = embed_ref[...]
    parts = edge_parts(basis, unit)
    species = kind_left.shape[2] // 32
    by_kind = [[None] * species for _ in range(4)]
    for n in range(slots):
        lanes = slice(n * atoms, (n + 1) * atoms)
        kind = jnp.broadcast_to(kinds[:, lanes], (8, atoms))
        for k in range(species):
            match = kind == float(k)
            for part in range(4):
                term = jnp.where(match, parts[part][:, lanes], 0.0)
                old = by_kind[part][k]
                by_kind[part][k] = term if old is None else old + term
    stacks = [stacked_right(jnp.concatenate(rows, axis=0)) for rows in by_kind]
    vectors = dot(kind_left[1], jnp.concatenate(stacks[1:], axis=1))
    sums = [dot(kind_left[0], stacks[0])]
    sums += [vectors[:, i * atoms : (i + 1) * atoms] for i in range(3)]
    step, gate = mixed(sums, mix_high, mix_low, 0)
    low_ref[...] = (embedded(stack, own[3]) + step).astype(BF16)
    for part in range(3):
        sums_ref[part] = sums[part + 1]
    gate_ref[...] = gate


def hot_columns(ids, rows):
    place = lax.broadcasted_iota(jnp.int32, (rows, ids.shape[1]), 0)
    return jnp.where(ids == place, 1.0, 0.0).astype(BF16)


def second_near_kernel(slots, ids_ref, basis_ref, unit_ref, left_ref, column_ref, weight_ref,
                       near_ref):
    atoms = column_ref.shape[2]
    parts = edge_parts(basis_ref[1], unit_ref[1])
    source = jnp.concatenate([column_ref[b] for b in range(3)], axis=1)
    for n in range(slots):
        lanes = slice(n * atoms, (n + 1) * atoms)
        for part in range(4):
            weight_ref[part, :, lanes] = weights_of(left_ref, part, parts[part][:, lanes])
        ids = ids_ref[1:2, lanes] - 3 * atoms
        near_ref[:, lanes] = dot(source, hot_columns(ids, 3 * atoms))


def second_side_kernel(slots, ids_ref, near_ref, pair_ref, out_ref):
    atoms = pair_ref.shape[2]
    source = jnp.concatenate([pair_ref[b] for b in range(3)], axis=1)
    for n in range(slots):
        lanes = slice(n * atoms, (n + 1) * atoms)
        hot = hot_columns(ids_ref[1:2, lanes], 3 * atoms)
        out_ref[:, lanes] = near_ref[:, lanes] + dot(source, hot)


def second_kernel(slots, hot_ref, weight_ref, near_ref, mix_high, mix_low, charge_ref, cell_ref,
                  column_ref, beyond_ref, feature_ref, sums_ref, gate_ref, packed_ref,
                  full_charge_ref, hidden_ref):
    atoms = column_ref.shape[2]
    source = jnp.concatenate([beyond_ref[b] for b in range(3)], axis=1)
    sums = [None] * 4
    for n in range(slots):
        lanes = slice(n * atoms, (n + 1) * atoms)
        feature = near_ref[:, lanes] + dot(source, hot_ref[:, lanes])
        feature_ref[:, lanes] = feature.astype(BF16)
        for part in range(4):
            term = weight_ref[part, :, lanes] * feature
            sums[part] = term if sums[part] is None else sums[part] + term
    step, gate = mixed(sums, mix_high, mix_low, 1)
    hidden = column_ref[1].astype(F32) + step
    hidden_ref[...] = hidden
    for part in range(3):
        sums_ref[part] = sums[part + 1]
    gate_ref[...] = gate
    charge = dot_split((charge_ref[0], charge_ref[1]), hidden)
    full_charge_ref[...] = charge
    place = jnp.concatenate(unfold_block(cell_ref[2], atoms)[:3], axis=0)
    high = place.astype(BF16).astype(F32)
    rest = place - high
    middle = rest.astype(BF16).astype(F32)
    zero = jnp.zeros((packed_ref.shape[0] - charge.shape[0] - 9, atoms), F32)
    packed_ref[...] = jnp.concatenate([charge, high, middle, rest - middle, zero], axis=0).astype(
        BF16
    )


def readout_kernel(hidden_high, hidden_low, turn_high, turn_low, out_ref, hidden_ref, energy_ref,
                   slope_ref):
    hidden = hidden_ref[...]
    value, slope = silu_pair(dot_split((hidden_high[...], hidden_low[...]), hidden))
    out = out_ref[...].T
    energy_ref[...] = jnp.sum(value * out, axis=0, keepdims=True)
    slope_ref[...] = dot_split((turn_high[...], turn_low[...]), slope * out)


def message_grads(cotangent, gate_ref, sums_ref, high_ref, low_ref, layer):
    pre = cotangent * gate_ref[...]
    both = dot_split((high_ref[layer], low_ref[layer]), pre)
    half = both.shape[0] // 2
    return [both[:half]] + [both[half:] * sums_ref[i] for i in range(3)]


def radial_grad(left, value):
    high, low = split(value)
    both = dot(left, jnp.concatenate([high, low], axis=0))
    half = both.shape[0] // 2
    return both[:half] + both[half:]


def second_back_kernel(slots, scale, count, hot_ref, weight_ref, turn_high, turn_low, charge_ref,
                       sums_ref, gate_ref, full_charge_ref, energy_ref, slope_ref, *refs):
    folds, refs = refs[:count], refs[count:]
    site_ref, long_ref, cotangent_ref, grad_ref, term_ref, beyond_ref = refs
    atoms = gate_ref.shape[1]
    total = folds[0][...].astype(F32)
    for part in folds[1:]:
        total = total + part[...].astype(F32)
    wide = full_charge_ref.shape[0]
    potential = total[:wide] * (2.0 * scale)
    slopes = total[wide : wide + 3] + total[wide + 3 : wide + 6] + total[wide + 6 : wide + 9]
    long_ref[...] = jnp.concatenate(
        [slopes * (2.0 * scale), jnp.zeros((5, atoms), F32)], axis=0
    )
    site_ref[0] = energy_ref[...] + 0.5 * jnp.sum(
        full_charge_ref[...] * potential, axis=0, keepdims=True
    )
    high, low = split(potential)
    turned = ((0,), (0,))
    cotangent = slope_ref[...] + (
        dot(charge_ref[0], high, turned)
        + (dot(charge_ref[0], low, turned) + dot(charge_ref[1], high, turned))
    )
    cotangent_ref[...] = cotangent
    grads = message_grads(cotangent, gate_ref, sums_ref, turn_high, turn_low, 1)
    for part in range(4):
        grad_ref[part] = grads[part]
    for n in range(slots):
        lanes = slice(n * atoms, (n + 1) * atoms)
        term = weight_ref[0, :, lanes] * grads[0]
        for part in range(1, 4):
            term = term + weight_ref[part, :, lanes] * grads[part]
        term_ref[:, lanes] = term.astype(BF16)
    for b in range(3):
        start = (3 + b) * atoms
        beyond_ref[b] = dot(term_ref[...], hot_ref[:, start : start + atoms]).astype(BF16)


def second_pair_kernel(hot_ref, term_ref, pair_ref):
    atoms = pair_ref.shape[2]
    for b in range(3):
        pair_ref[b] = dot(term_ref[...], hot_ref[:, b * atoms : (b + 1) * atoms]).astype(BF16)


def second_middle_kernel(hot_ref, term_ref, cotangent_ref, middle_ref):
    atoms = cotangent_ref.shape[1]
    for b in range(3):
        grad = dot(term_ref[...], hot_ref[:, b * atoms : (b + 1) * atoms])
        middle_ref[b] = grad + cotangent_ref[...] if b == 1 else grad


def second_edge_kernel(slots, back_ref, feature_ref, grad_ref, edge_ref):
    atoms = grad_ref.shape[2]
    for n in range(slots):
        lanes = slice(n * atoms, (n + 1) * atoms)
        feature = feature_ref[:, lanes].astype(F32)
        for part in range(4):
            edge_ref[8 * part : 8 * part + 8, lanes] = radial_grad(
                back_ref[1 if part else 0], grad_ref[part] * feature
            )


def first_back_kernel(slots, ids_ref, basis_ref, slope_ref, unit_ref, kind_high, kind_low, turn_high,
                      turn_low, sums_ref, gate_ref, edge_ref, from_beyond, long_ref, middle_ref,
                      from_pair, *outs):
    sums = {(1, 2): long_ref[...]}
    for cell in range(3):
        cotangent = middle_ref[cell] + (
            from_pair[cell].astype(F32) + from_beyond[cell].astype(F32)
        )
        own, found = first_back_cell(
            slots, ids_ref[cell : cell + 1, :], basis_ref.at[cell], slope_ref.at[cell],
            unit_ref.at[cell], kind_high, kind_low, turn_high, turn_low, sums_ref.at[cell],
            gate_ref.at[cell], edge_ref if cell == 1 else None, cotangent,
        )
        terms = [((1, cell + 1), own)]
        terms += [((n // 3, SLOT_CELLS[cell][n % 3]), found[n]) for n in range(9)]
        for key, term in terms:
            sums[key] = sums[key] + term if key in sums else term
    for x in range(3):
        rows = [sums[(x, y)][:3] for y in range(5)]
        outs[x][...] = jnp.concatenate(rows + [jnp.zeros((1, rows[0].shape[1]), F32)], axis=0)


def first_back_cell(slots, ids, basis_ref, slope_ref, unit_ref, kind_high, kind_low, turn_high,
                    turn_low, sums_ref, gate_ref, edge_ref, cotangent):
    atoms = gate_ref.shape[1]
    pre = cotangent * gate_ref[...]
    both = dot_split((turn_high[0], turn_low[0]), pre)
    wide = both.shape[0] // 2
    grads = [both[:wide]] + [both[wide:] * sums_ref[i] for i in range(3)]
    unit = unit_ref[...]
    kinds = unit[4:5]
    by_kind = [dot_split((kind_high[0], kind_low[0]), grads[0])]
    by_kind += [dot_split((kind_high[1], kind_low[1]), grads[i]) for i in range(1, 4)]
    species = by_kind[0].shape[0] // 8
    edges = [[] for _ in range(4)]
    for n in range(slots):
        kind = jnp.broadcast_to(kinds[:, n * atoms : (n + 1) * atoms], (8, atoms))
        matches = [kind == float(k) for k in range(1, species)]
        for part in range(4):
            rows = by_kind[part]
            found = rows[:8]
            for k, match in enumerate(matches):
                found = jnp.where(match, rows[8 * k + 8 : 8 * k + 16], found)
            edges[part].append(found)
    edges = [jnp.concatenate(rows, axis=1) for rows in edges]
    if edge_ref is not None:
        edges = [edge_ref[8 * part : 8 * part + 8] + edges[part] for part in range(4)]
    basis = basis_ref[...]
    units = [unit[i : i + 1] for i in range(3)]
    inverse = unit[3:4]
    by_basis = edges[0]
    for i in range(3):
        by_basis = by_basis + edges[i + 1] * units[i]
    by_unit = [jnp.sum(edges[i + 1] * basis, axis=0, keepdims=True) * inverse for i in range(3)]
    by_distance = jnp.sum(by_basis * slope_ref[...], axis=0, keepdims=True)
    for i in range(3):
        by_distance = by_distance - by_unit[i] * units[i]
    moves = [by_unit[i] + by_distance * units[i] for i in range(3)]
    zero = jnp.zeros_like(moves[0])
    move = jnp.concatenate(moves + [zero] * 5, axis=0)
    own = -move[:, :atoms]
    for n in range(1, slots):
        own = own - move[:, n * atoms : (n + 1) * atoms]
    lane_hot = hot_columns(ids & 127, 128)
    half = ids >> 7
    high = move.astype(BF16).astype(F32)
    both = jnp.concatenate([high, move - high], axis=0)
    per_cell = atoms // 128
    rows = jnp.concatenate(
        [jnp.where(half == h, both, 0.0).astype(BF16) for h in range(9 * per_cell)], axis=0
    )
    spread = dot(rows, lane_hot, ((1,), (1,)))
    grads = []
    for cell in range(9):
        found = []
        for h in range(cell * per_cell, (cell + 1) * per_cell):
            found.append(spread[16 * h : 16 * h + 8] + spread[16 * h + 8 : 16 * h + 16])
        grads.append(jnp.concatenate(found, axis=1))
    return own, grads


def pair_counts(parts):
    total = WAVE_REACH + WAVE_REACH * (2 * WAVE_REACH + 1)
    share = -(-total // parts)
    return total, share, -(-share // 16) * 16


def pair_vectors(slot, share, part):
    side = 2 * WAVE_REACH + 1
    total = WAVE_REACH + WAVE_REACH * side
    index = slot + part.astype(F32) * share
    later = index - WAVE_REACH
    row = jnp.floor((later + 0.5) * (1.0 / side))
    first = index < WAVE_REACH
    kx = jnp.where(first, 0.0, row + 1.0)
    ky = jnp.where(first, index + 1.0, later - row * side - WAVE_REACH)
    valid = jnp.where((slot < share) & (index < total), 1.0, 0.0)
    return kx, ky, valid


def count_up(rows):
    return lax.broadcasted_iota(jnp.int32, (rows, 1), 0).astype(F32)


def green_weights(share, padded, grid, place_ref, vec_ref, weight_ref):
    grid_x, grid_y = grid
    turn = 2.0 * math.pi
    side = 2 * WAVE_REACH + 1
    top = side * side * side - 1
    vec = vec_ref[...].astype(F32) + WAVE_REACH
    code = (vec[0:1] * side + vec[1:2]) * side + vec[2:3]
    code = jnp.maximum(code, top - code)
    span = 8 * share
    row = count_up(span)
    slot = jnp.floor(row * 0.125)
    height = row - 8.0 * slot + 1.0
    flat = count_up(padded)
    slot = jnp.concatenate([slot, slot, flat], axis=0)
    kz = jnp.concatenate([height, -height, jnp.zeros_like(flat)], axis=0)
    kx, ky, valid = pair_vectors(slot, share, place_ref[0, 0:1, 0:1])
    own = ((kx + WAVE_REACH) * side + ky + WAVE_REACH) * side + kz + WAVE_REACH
    seen = jnp.zeros((own.shape[0], 128), F32)
    for start in range(0, code.shape[1], 128):
        seen = seen + jnp.where(own == code[:, start : start + 128], 1.0, 0.0)
    count = jnp.sum(seen, axis=1, keepdims=True) * valid
    sq = (
        (kx * (turn / (grid_x * cell_width))) ** 2
        + (ky * (turn / (grid_y * cell_width))) ** 2
        + (kz * (turn / box_height)) ** 2
    )
    green = jnp.exp(-smear_width * sq) / (sq + screen * screen) * count
    weight_ref[...] = jnp.broadcast_to(green, weight_ref.shape)


def basis_rows(share, ca, sa, cb, sb):
    cc, ss, sc, cs = [], [], [], []
    for p in range(share):
        c, s = ca[p : p + 1], sa[p : p + 1]
        cc.append(c * cb)
        ss.append(s * sb)
        sc.append(s * cb)
        cs.append(c * sb)
    return cc, ss, sc, cs


def unpack_rows(block):
    half = block.shape[1] // 2
    return jnp.concatenate([block[:, :half], block[:, half:]], axis=0)


def pack_rows(block):
    half = block.shape[0] // 2
    return jnp.concatenate([block[:half], block[half:]], axis=1)


def structure_kernel(share, padded, grid, wide, flip, place_ref, blocks, *refs):
    grid_x, grid_y = grid
    if flip:
        near_ref, (ca_ref, sa_ref, cb_ref, sb_ref, high_ref, low_ref, own_ref, out_ref) = (
            refs[0],
            refs[1:],
        )
        total = near_ref[...]
    else:
        ca_ref, sa_ref, cb_ref, sb_ref, high_ref, low_ref, total_ref = refs
        total = None
    col = place_ref[1, 0:1, 0:1].astype(F32) * (1.0 / grid_y)
    first = place_ref[0, 0:1, 0:1] ^ flip
    kx, ky, _ = pair_vectors(count_up(padded), share, place_ref[0, 0:1, 0:1])
    kz = count_up(8) + 1.0
    for d in range(grid_x // 2):
        block = blocks[d]
        charge = block[:wide]
        atoms = charge.shape[1]
        pieces = block[wide:].astype(F32)
        place = pieces[0:3] + (pieces[3:6] + pieces[6:9])
        row = (first ^ (2 * d)).astype(F32) * (1.0 / grid_x)
        x = place[0:1] * (1.0 / (grid_x * cell_width)) + row
        y = place[1:2] * (1.0 / (grid_y * cell_width)) + col
        sa, ca = sin_cos(kx * x + ky * y)
        sb, cb = sin_cos(kz * (place[2:3] * (1.0 / box_height)))
        lanes = pl.ds(d * atoms, atoms)
        ca_ref[:, lanes] = ca
        sa_ref[:, lanes] = sa
        cb_ref[:, lanes] = cb
        sb_ref[:, lanes] = sb
        cc, ss, sc, cs = basis_rows(share, ca, sa, cb, sb)
        high, low = split(jnp.concatenate(cc + ss + sc + cs + [ca, sa], axis=0))
        high_ref[:, lanes] = high
        low_ref[:, lanes] = low
        term = dot(high, charge, ((1,), (1,))) + dot(low, charge, ((1,), (1,)))
        total = term if total is None else total + term
    if flip:
        packed = pack_rows(total)
        own_ref[...] = packed
        out_ref[...] = packed.astype(BF16)
    else:
        total_ref[...] = total


def weighted_rows(share, padded, wide, weight_ref, parts):
    packed = parts[0][...].astype(F32)
    for part in parts[1:]:
        packed = packed + part[...].astype(F32)
    struct = unpack_rows(packed)
    span = 8 * share
    cc, ss, sc, cs = (struct[i * span : (i + 1) * span] for i in range(4))
    weight = weight_ref[:, :wide]
    plus, minus, flat = weight[:span], weight[span : 2 * span], weight[2 * span :]
    re_plus, im_plus = plus * (cc - ss), plus * (sc + cs)
    re_minus, im_minus = minus * (cc + ss), minus * (sc - cs)
    rows = jnp.concatenate(
        [
            re_plus + re_minus,
            re_minus - re_plus,
            im_plus + im_minus,
            im_plus - im_minus,
            flat * struct[4 * span : 4 * span + padded],
            flat * struct[4 * span + padded :],
        ],
        axis=0,
    )
    return rows


def fold_kernel(share, padded, grid, wide, flip, place_ref, *refs):
    grid_x, grid_y = grid
    turn = 2.0 * math.pi
    if flip:
        weight_ref, parts, refs = refs[0], refs[1 : 1 + grid_y], refs[1 + grid_y :]
        rows = weighted_rows(share, padded, wide, weight_ref, parts)
        refs, rows_ref = refs[:-1], refs[-1]
        rows_ref[...] = rows
    else:
        rows, refs = refs[0][...], refs[1:]
    ca_ref, sa_ref, cb_ref, sb_ref, high_ref, low_ref, blocks, out_ref = refs
    row_high, row_low = split(rows)
    row_pair = jnp.concatenate([row_high, row_low], axis=1)
    turned = rows.T
    t_high, t_low = split(turned)
    t_both = jnp.concatenate([t_high, t_low], axis=0)
    span = 8 * share
    kx, ky, _ = pair_vectors(count_up(padded), share, place_ref[0, 0:1, 0:1])
    kx = kx * (turn / (grid_x * cell_width))
    ky = ky * (turn / (grid_y * cell_width))
    kz = (count_up(8) + 1.0) * (turn / box_height)
    for d in range(grid_x // 2):
        charge = blocks[d][:wide]
        atoms = charge.shape[1]
        lanes = pl.ds(d * atoms, atoms)
        ca, sa, cb, sb = ca_ref[:, lanes], sa_ref[:, lanes], cb_ref[:, lanes], sb_ref[:, lanes]
        bcc, bss, bsc, bcs = basis_rows(share, ca, sa, cb, sb)
        high, low = high_ref[:, lanes], low_ref[:, lanes]
        both = dot(t_both, high)
        pot = both[:wide] + both[wide:] + dot(t_high, low)
        proj = dot(row_pair, jnp.concatenate([charge, charge], axis=0))
        by_x = jnp.zeros((8, atoms), jnp.float32)
        by_y = jnp.zeros((8, atoms), jnp.float32)
        by_z = jnp.zeros((8, atoms), jnp.float32)
        for p in range(share):
            pcc, pss, psc, pcs = (
                proj[i * span + 8 * p : i * span + 8 * p + 8] for i in range(4)
            )
            slope = bcs[p] * pss - bsc[p] * pcc + bcc[p] * psc - bss[p] * pcs
            by_x = by_x + kx[p : p + 1] * slope
            by_y = by_y + ky[p : p + 1] * slope
            by_z = by_z + (bsc[p] * pss - bcs[p] * pcc - bss[p] * psc + bcc[p] * pcs)
        flat_slope = ca * proj[4 * span + padded :] - sa * proj[4 * span : 4 * span + padded]
        grad_x = jnp.sum(by_x, axis=0, keepdims=True) + jnp.sum(kx * flat_slope, axis=0, keepdims=True)
        grad_y = jnp.sum(by_y, axis=0, keepdims=True) + jnp.sum(ky * flat_slope, axis=0, keepdims=True)
        grad_z = jnp.sum(kz * by_z, axis=0, keepdims=True)
        slopes = jnp.concatenate([grad_x, grad_y, grad_z], axis=0)
        out_ref[d] = pieced(pot, slopes, out_ref.shape[1]).astype(out_ref.dtype)


def pieced(pot, slopes, rows):
    high = slopes.astype(BF16).astype(F32)
    rest = slopes - high
    middle = rest.astype(BF16).astype(F32)
    zero = jnp.zeros((rows - pot.shape[0] - 9, pot.shape[1]), F32)
    return jnp.concatenate([pot, high, middle, rest - middle, zero], axis=0)


def unpieced(block, wide):
    slopes = block[wide : wide + 3] + (block[wide + 3 : wide + 6] + block[wide + 6 : wide + 9])
    return block[:wide], slopes


def join_kernel(wide, near_ref, far_ref, own_ref, *outs):
    for d in range(near_ref.shape[0]):
        pot, slopes = unpieced(near_ref[d], wide)
        pot_far, slopes_far = unpieced(far_ref[d].astype(F32), wide)
        block = pieced(pot + pot_far, slopes + slopes_far, near_ref.shape[1])
        if d:
            outs[d - 1][...] = block.astype(BF16)
        else:
            own_ref[...] = block


def per_device(
    positions,
    species,
    neighbours,
    counts,
    species_embed,
    radial,
    mixing,
    read_hidden,
    read_out,
    charge_map,
    wavevectors,
):
    atoms = positions.shape[3]
    slots = neighbours.shape[3]
    features, lat_width = charge_map.shape
    wave_count = wavevectors.shape[1]
    grid = lax.axis_size("gx"), lax.axis_size("gy")
    grid_x, grid_y = grid
    edges = slots * atoms
    scale = 1.0 / math.sqrt(wave_count * lat_width * atoms * grid_x * grid_y)
    place = jnp.stack([lax.axis_index("gx"), lax.axis_index("gy")]).astype(jnp.int32)
    place = jnp.broadcast_to(place[:, None, None], (2, 8, 128))
    _, share, padded = pair_counts(grid_x)
    ids = neighbours.transpose(0, 3, 1, 2).reshape(1, edges)
    cell_rows = 4 * atoms // 128
    block_total = -(-(cell_rows + (edges + atoms) // 128) // 8) * 8
    dma = pltpu.SemaphoreType.DMA
    shown = positions.transpose(0, 2, 1, 3)
    (own_place,) = run(
        pack_kernel,
        [shape(cell_rows, 128)],
        [place, shown, species],
        flops=10_000_000_000,
        name="pack",
    )
    (own,) = run(
        pack_more_kernel,
        [shape(block_total, 128)],
        [place, ids, counts, own_place],
        name="pack_more",
    )
    y_beyond, y_pair = beyond(own, "gy"), paired(own, "gy", 1)
    over_pair = far(own_place, "gy", True)
    over_beyond = over_pair if grid_y == 4 else far(own_place, "gy", False)
    cells = jnp.stack(
        [over_pair, y_pair[:cell_rows], own_place, y_beyond[:cell_rows], over_beyond]
    )
    x_beyond, x_pair = beyond(cells, "gx"), paired(cells, "gx", 1)
    cells = [x_pair, cells, x_beyond]

    norm = 1.0 / math.sqrt(slots)
    kind_rows = 8 * species_embed.shape[0]
    low_pair = lambda *dims: [shape(*dims, dtype=BF16)] * 2
    embed, kind_left, left, back, kind_high, kind_low, mix_high, mix_low, turn_high, turn_low = run(
        functools.partial(prep_first_kernel, norm),
        [
            shape(features, 32, dtype=BF16),
            shape(2, features, 4 * kind_rows, dtype=BF16),
            shape(2, features, 32, dtype=BF16),
            shape(2, 16, 2 * features, dtype=BF16),
        ]
        + low_pair(2, kind_rows, features)
        + low_pair(2, features, 2 * features)
        + low_pair(2, 2 * features, features),
        [species_embed, radial, mixing],
        scratch=[
            pltpu.VMEM(species_embed.shape, F32),
            pltpu.VMEM(radial.shape, F32),
            pltpu.VMEM(mixing.shape, F32),
            dma((3,)),
        ],
        hbm=3,
        name="prep_first",
    )
    read_out, hidden_high, hidden_low, hidden_turn_high, hidden_turn_low, charge_pair = run(
        prep_second_kernel,
        [shape(1, features)]
        + low_pair(features, features)
        + low_pair(features, features)
        + [shape(2, lat_width, features, dtype=BF16)],
        [read_out[None, :], read_hidden, charge_map.T],
        scratch=[
            pltpu.VMEM(read_hidden.shape, F32),
            pltpu.VMEM((lat_width, features), F32),
            dma((3,)),
        ],
        hbm=3,
        name="prep_second",
    )
    cells[2], hidden_high = lax.optimization_barrier((cells[2], hidden_high))
    low, ids, basis, slope, unit, sums_one, gate_one = run(
        functools.partial(first_kernel, slots),
        [
            shape(3, features, atoms, dtype=BF16),
            shape(3, edges, dtype=jnp.int32),
            shape(3, 8, edges),
            shape(3, 8, edges),
            shape(3, 8, edges),
            shape(3, 3, features, atoms),
            shape(3, features, atoms),
        ],
        [place, embed, kind_left, mix_high, mix_low, y_beyond, own, y_pair] + cells[::-1],
        name="first",
    )
    hidden = [paired(low, "gx", 1), low, beyond(low, "gx")]
    edge_weights, near = run(
        functools.partial(second_near_kernel, slots),
        [shape(4, features, edges), shape(features, edges)],
        [ids, basis, unit, left, low],
        flops=2_000_000_000,
        name="second_near",
    )
    (hot_beyond,) = run(
        hot_beyond_kernel,
        [shape(3 * atoms, edges, dtype=BF16)],
        [ids, near],
        flops=1_000_000,
        name="hot_beyond",
    )
    (near,) = run(
        functools.partial(second_side_kernel, slots),
        [shape(features, edges)],
        [ids, near, hidden[0]],
        flops=1_000_000_000,
        name="second_side",
    )
    block_rows = -(-(lat_width + 9) // 16) * 16
    feature, sums_two, gate_two, packed, charge, hidden_two = run(
        functools.partial(second_kernel, slots),
        [
            shape(features, edges, dtype=BF16),
            shape(3, features, atoms),
            shape(features, atoms),
            shape(block_rows, atoms, dtype=BF16),
            shape(lat_width, atoms),
            shape(features, atoms),
        ],
        [hot_beyond, edge_weights, near, mix_high, mix_low, charge_pair, cells[1], hidden[1],
         hidden[2]],
        name="second",
    )
    energy, energy_slope = run(
        readout_kernel,
        [shape(1, atoms), shape(features, atoms)],
        [hidden_high, hidden_low, hidden_turn_high, hidden_turn_low, read_out, hidden_two],
        name="readout",
    )
    half = grid_x // 2
    near_charges = jnp.stack([packed] + [paired(packed, "gx", 2 * d) for d in range(1, half)])
    (weight,) = run(
        functools.partial(green_weights, share, padded, grid),
        [shape(16 * share + padded, 128)],
        [place, wavevectors],
        name="green",
    )
    near_charges, weight = lax.optimization_barrier((near_charges, weight))
    far_charges = paired(near_charges, "gx", 1)
    span = half * atoms
    rows = 32 * share + 2 * padded
    phase_shapes = [
        shape(padded, span),
        shape(padded, span),
        shape(8, span),
        shape(8, span),
        shape(rows, span, dtype=BF16),
        shape(rows, span, dtype=BF16),
    ]
    *near_phases, near_total = run(
        functools.partial(structure_kernel, share, padded, grid, lat_width, 0),
        phase_shapes + [shape(rows, lat_width)],
        [place, near_charges],
        flops=1_000_000_000,
        name="structure_near",
    )
    *far_phases, own_part, part = run(
        functools.partial(structure_kernel, share, padded, grid, lat_width, 1),
        phase_shapes
        + [
            shape(rows // 2, 2 * lat_width),
            shape(rows // 2, 2 * lat_width, dtype=BF16),
        ],
        [place, far_charges, near_total],
        name="structure_far",
    )
    parts = [own_part] + [paired(part, "gy", d) for d in range(1, grid_y)]
    (hot_back,) = run(
        functools.partial(hot_back_kernel, (0, 2)),
        [shape(edges, 6 * atoms, dtype=BF16)],
        [ids],
        flops=2_000_000_000,
        name="hot_back",
    )
    parts, hot_back = lax.optimization_barrier((parts, hot_back))
    far_folds, wave_rows = run(
        functools.partial(fold_kernel, share, padded, grid, lat_width, 1),
        [shape(half, block_rows, atoms, dtype=BF16), shape(rows, lat_width)],
        [place, weight] + parts + far_phases + [far_charges],
        name="fold_far",
    )
    far_folds = paired(far_folds, "gx", 1)
    (near_folds,) = run(
        functools.partial(fold_kernel, share, padded, grid, lat_width, 0),
        [shape(half, block_rows, atoms)],
        [place, wave_rows] + near_phases + [near_charges],
        flops=1_000_000_000,
        name="fold_near",
    )
    folds = run(
        functools.partial(join_kernel, lat_width),
        [shape(block_rows, atoms)] + [shape(block_rows, atoms, dtype=BF16)] * (half - 1),
        [near_folds, far_folds],
        name="fold_join",
    )
    folds = [folds[0]] + [paired(folds[d], "gx", 2 * d) for d in range(1, half)]

    site, long, cotangent, grads, term, to_beyond = run(
        functools.partial(second_back_kernel, slots, scale, half),
        [
            shape(1, 1, atoms),
            shape(8, atoms),
            shape(features, atoms),
            shape(4, features, atoms),
            shape(features, edges, dtype=BF16),
            shape(3, features, atoms, dtype=BF16),
        ],
        [hot_back, edge_weights, turn_high, turn_low, charge_pair, sums_two, gate_two, charge,
         energy, energy_slope] + folds,
        name="second_back",
    )
    (to_pair,) = run(
        second_pair_kernel,
        [shape(3, features, atoms, dtype=BF16)],
        [hot_back, term],
        flops=1_000_000,
        name="second_pair",
    )
    from_pair, from_beyond = paired(to_pair, "gx", 1), beyond(to_beyond, "gx")
    (hot_middle,) = run(
        functools.partial(hot_back_kernel, (1,)),
        [shape(edges, 3 * atoms, dtype=BF16)],
        [ids],
        flops=1_000_000_000,
        name="hot_middle",
    )
    (middle,) = run(
        second_middle_kernel,
        [shape(3, features, atoms)],
        [hot_middle, term, cotangent],
        flops=1_000_000_000,
        name="second_middle",
    )
    (edge,) = run(
        functools.partial(second_edge_kernel, slots),
        [shape(32, edges)],
        [back, feature, grads],
        flops=1_000_000_000,
        name="second_edge",
    )
    to_pair, middle, to_beyond = run(
        functools.partial(first_back_kernel, slots),
        [shape(16, atoms)] * 3,
        [ids, basis, slope, unit, kind_high, kind_low, turn_high, turn_low, sums_one, gate_one, edge,
         from_beyond, long, middle, from_pair],
        name="first_back",
    )
    total = middle + paired(to_pair, "gx", 1) + beyond(to_beyond, "gx")
    total = [total[3 * y : 3 * y + 3] for y in range(5)]
    if grid_y == 4:
        distant = far(total[0] + total[4], "gy", True)
    else:
        distant = far(total[0], "gy", False) + far(total[4], "gy", True)
    total = total[2] + paired(total[1], "gy", 1) + beyond(total[3], "gy") + distant
    forces = -total[None, :, None, :]
    return (forces.transpose(0, 2, 1, 3), site)


def solution(mesh):
    in_specs = (
        P("gx", "gy", None, None),
        P("gx", "gy", None),
        P("gx", "gy", None, None),
        P("gx", "gy", None),
        P(),
        P(),
        P(),
        P(),
        P(),
        P(),
        P(),
    )
    out_specs = (P("gx", "gy", None, None), P("gx", "gy", None))
    return jax.shard_map(
        per_device, mesh=mesh, in_specs=in_specs, out_specs=out_specs, check_vma=False
    )
```

```python
import functools
import math

import jax
import jax.numpy as jnp
import numpy as np
from jax import lax
from jax.experimental import pallas as pl
from jax.experimental.pallas import tpu as pltpu
from jax.sharding import PartitionSpec as P

cell_width = 10.0
box_height = 30.0
cut_radius = 50.0
soften = 0.25
screen = 0.5
smear_width = 0.5
WAVE_REACH = 8
F32 = jnp.float32
BF16 = jnp.bfloat16


def paired(block, axis, mask):
    return lax.ppermute(block, axis, [(i ^ mask, i) for i in range(lax.axis_size(axis))])


def other_side(index, count):
    return (index + (1 if index % 2 else -1)) % count


def beyond(block, axis):
    count = lax.axis_size(axis)
    return lax.ppermute(block, axis, [(other_side(i, count), i) for i in range(count)])


def far(block, axis, over_pair):
    count = lax.axis_size(axis)
    if over_pair:
        route = [(other_side(i ^ 1, count), i) for i in range(count)]
    else:
        route = [(other_side(i, count) ^ 1, i) for i in range(count)]
    return lax.ppermute(block, axis, route)


SLOT_CELLS = ((2, 1, 0), (1, 2, 3), (4, 3, 2))


def whole(space=pltpu.VMEM):
    return pl.BlockSpec(memory_space=space)


def run(kernel, outs, args, scratch=(), hbm=0, flops=10_000_000, grant=16, name=None):
    specs = [whole()] * (len(args) - hbm) + [whole(pltpu.HBM)] * hbm
    return list(
        pl.pallas_call(
            kernel,
            out_shape=outs,
            in_specs=specs,
            out_specs=[whole() for _ in outs],
            scratch_shapes=list(scratch),
            compiler_params=pltpu.CompilerParams(vmem_limit_bytes=grant * 1024 * 1024),
            cost_estimate=pl.CostEstimate(
                flops=flops, bytes_accessed=1_000_000, transcendentals=0
            ),
            name=name,
        )(*args)
    )


def shape(*dims, dtype=F32):
    return jax.ShapeDtypeStruct(dims, dtype)


def split(value):
    high = value.astype(BF16)
    return high, (value - high.astype(F32)).astype(BF16)


def dot(left, right, contract=((1,), (0,))):
    return lax.dot_general(left, right, (contract, ((), ())), preferred_element_type=F32)


def dot3(left, right):
    left_high, left_low = split(left)
    right_high, right_low = split(right)
    return dot(left_high, right_high) + (dot(left_high, right_low) + dot(left_low, right_high))


def dot_split(left, right):
    right_high, right_low = split(right)
    return dot(left[0], right_high) + (dot(left[0], right_low) + dot(left[1], right_high))


def sin_cos(turns):
    quarter = jnp.round(turns * 4.0)
    x = (turns - quarter * 0.25) * (2.0 * math.pi)
    z = x * x
    sine = ((-1.9515295891e-4 * z + 8.3321608736e-3) * z - 1.6666654611e-1) * (z * x) + x
    cosine = (2.443315711809948e-5 * z - 1.388731625493765e-3) * z + 4.166664568298827e-2
    cosine = cosine * (z * z) - 0.5 * z + 1.0
    k = quarter.astype(jnp.int32) & 3
    odd = (k & 1) == 1
    by_sine = jnp.where(odd, cosine, sine)
    by_cosine = jnp.where(odd, sine, cosine)
    return (
        jnp.where(k >= 2, -by_sine, by_sine),
        jnp.where((k == 1) | (k == 2), -by_cosine, by_cosine),
    )


def stacked_left(value):
    high = value.astype(BF16).astype(F32)
    rows = jnp.concatenate([high, high, value - high, jnp.zeros_like(high)], axis=0)
    return rows.T.astype(BF16)


def stacked_right(value):
    high = value.astype(BF16).astype(F32)
    return jnp.concatenate([high, value - high, high, jnp.zeros_like(high)], axis=0).astype(BF16)


def silu_pair(value):
    gate = 1.0 / (1.0 + jnp.exp(-value))
    return value * gate, gate * (1.0 + value * (1.0 - gate))


def onehot_kinds(kinds, rows):
    levels = lax.broadcasted_iota(jnp.int32, (rows, kinds.shape[1]), 0).astype(F32)
    return jnp.where(kinds == levels, 1.0, 0.0)


def embedding_stack(embed):
    high = embed.astype(BF16).astype(F32)
    rest = embed - high
    middle = rest.astype(BF16).astype(F32)
    rows = jnp.concatenate([high, middle, rest - middle, jnp.zeros_like(high)], axis=0)
    return rows.T.astype(BF16)


def embedded(stack, kinds):
    hot = onehot_kinds(kinds, 8)
    return dot(stack, jnp.concatenate([hot, hot, hot, jnp.zeros_like(hot)], axis=0).astype(BF16))


def weights_of(stack_ref, part, rows):
    return dot(stack_ref[1 if part else 0], stacked_right(rows))


def mixed(sums, high_ref, low_ref, layer):
    squares = sums[1] * sums[1] + sums[2] * sums[2] + sums[3] * sums[3]
    both = jnp.concatenate([sums[0], squares], axis=0)
    return silu_pair(dot_split((high_ref[layer], low_ref[layer]), both))


def edge_parts(basis, unit):
    return [basis] + [basis * unit[i : i + 1] for i in range(3)]


def pack_kernel(place_ref, position_ref, species_ref, out_ref):
    rows = [position_ref[0, i] for i in range(3)] + [species_ref[0].astype(F32)]
    atoms = rows[0].shape[1]
    out_ref[...] = jnp.concatenate(
        [row[:, s : s + 128] for row in rows for s in range(0, atoms, 128)], axis=0
    )


def pack_more_kernel(place_ref, ids_ref, count_ref, first_ref, out_ref):
    atoms = count_ref.shape[2]
    order = slot_order(ids_ref[...], place_ref, atoms).astype(F32)
    rows = [first_ref[...]]
    rows += [order[:, s : s + 128] for s in range(0, order.shape[1], 128)]
    rows += [count_ref[0, :, s : s + 128].astype(F32) for s in range(0, atoms, 128)]
    missing = out_ref.shape[0] - sum(row.shape[0] for row in rows)
    out_ref[...] = jnp.concatenate(rows + [jnp.zeros((missing, 128), F32)], axis=0)


def block_ids(block, atoms, edges):
    start = 4 * atoms // 128
    middle, end = start + edges // 128, start + edges // 128 + atoms // 128
    rows = [block[r : r + 1] for r in range(start, end)]
    ids = jnp.concatenate(rows[: middle - start], axis=1).astype(jnp.int32)
    return ids, jnp.concatenate(rows[middle - start :], axis=1)


def radial_left(radial):
    high = radial.astype(BF16).astype(F32)
    low = radial - high
    top = jnp.concatenate([high, high], axis=1)
    end = jnp.concatenate([low, jnp.zeros_like(low)], axis=1)
    return jnp.concatenate([top, end], axis=0).astype(BF16)


def put_split(value, high_ref, low_ref, *at):
    high, low = split(value)
    high_ref[at] = high
    low_ref[at] = low


def cell_of(ids, atoms):
    return ids >> (atoms.bit_length() - 1) if atoms & (atoms - 1) == 0 else ids // atoms


def slot_order(ids, place_ref, atoms):
    cell = cell_of(ids, atoms)
    a = (cell * 11) >> 5
    b = cell - 3 * a
    a = jnp.where((place_ref[0, 0:1, 0:1] & 1) == 0, 2 - a, a)
    b = jnp.where((place_ref[1, 0:1, 0:1] & 1) == 0, 2 - b, b)
    return ids + (3 * a + b - cell) * atoms


def fetch(sources, targets, sems):
    copies = [
        pltpu.make_async_copy(source, target, sems.at[i])
        for i, (source, target) in enumerate(zip(sources, targets))
    ]
    for copy in copies:
        copy.start()
    for copy in copies:
        copy.wait()


def prep_first_kernel(norm, embed_in, radial_in, mixing_in, embed_out, kind_left, left_out, back_out,
                      kind_high, kind_low, mix_high, mix_low, turn_high, turn_low, embed_ref,
                      radial_ref, mixing_ref, sems):
    fetch([embed_in, radial_in, mixing_in], [embed_ref, radial_ref, mixing_ref], sems)
    embed = embed_ref[...]
    kinds = embed.shape[0]
    for path in range(2):
        radial = radial_ref[0, path] * norm
        rows = jnp.concatenate([radial * embed[s : s + 1] for s in range(kinds)], axis=0)
        kind_left[path] = stacked_left(rows)
        put_split(rows, kind_high, kind_low, path)
        radial = radial_ref[1, path] * norm
        left_out[path] = stacked_left(radial)
        back_out[path] = radial_left(radial)
    for layer in range(2):
        scalar, vector = mixing_ref[layer, 0], mixing_ref[layer, 1]
        put_split(jnp.concatenate([scalar.T, vector.T], axis=1), mix_high, mix_low, layer)
        put_split(jnp.concatenate([scalar, 2.0 * vector], axis=0), turn_high, turn_low, layer)
    embed = jnp.concatenate([embed, jnp.zeros((8 - kinds, embed.shape[1]), F32)], axis=0)
    embed_out[...] = embedding_stack(embed)


def prep_second_kernel(read_in, hidden_in, charge_in, read_ref, hidden_high, hidden_low,
                       hidden_turn_high, hidden_turn_low, charge_pair, hidden_ref, charge_ref, sems):
    fetch([read_in, hidden_in, charge_in], [read_ref, hidden_ref, charge_ref], sems)
    put_split(hidden_ref[...].T, hidden_high, hidden_low, Ellipsis)
    put_split(hidden_ref[...], hidden_turn_high, hidden_turn_low, Ellipsis)
    charge = charge_ref[...]
    high = charge.astype(BF16).astype(F32)
    charge_pair[0] = high.astype(BF16)
    charge_pair[1] = (charge - high).astype(BF16)


def hot_beyond_kernel(ids_ref, near_ref, hot_ref):
    ids = ids_ref[1:2, :] - 2 * hot_ref.shape[0]
    for start in range(0, hot_ref.shape[1], 256):
        lanes = slice(start, start + 256)
        hot_ref[:, lanes] = hot_columns(ids[:, lanes], hot_ref.shape[0])


def hot_back_kernel(slots_x, ids_ref, hot_ref):
    edges = ids_ref.shape[1]
    width = hot_ref.shape[1] // len(slots_x)
    entry = lax.broadcasted_iota(jnp.int32, (128, width), 1).astype(F32)
    for start in range(0, edges, 128):
        row = jnp.broadcast_to(ids_ref[1:2, start : start + 128].astype(F32), (8, 128))
        column = row.T[:, 0:1]
        for n, slot in enumerate(slots_x):
            hot_ref[start : start + 128, n * width : (n + 1) * width] = jnp.where(
                column - float(slot * width) == entry, 1.0, 0.0
            ).astype(BF16)


def unfold_block(block, atoms):
    parts = atoms // 128
    rows = [block[r : r + 1] for r in range(4 * parts)]
    return [jnp.concatenate(rows[q * parts : (q + 1) * parts], axis=1) for q in range(4)]


def first_kernel(slots, place_ref, embed_ref, kind_left, mix_high, mix_low, y_beyond_ref, own_ref,
                 y_pair_ref, beyond_ref, column_ref, pair_ref, low_ref, ids_ref, basis_ref, slope_ref,
                 unit_ref, sums_ref, gate_ref):
    atoms = low_ref.shape[2]
    frame = [pair_ref, column_ref, beyond_ref]
    per_cell = atoms // 128
    places = lax.broadcasted_iota(jnp.int32, (4 * per_cell, 128), 0)
    upper = places % per_cell
    kind_of_row = places // per_cell
    to_x = jnp.where(kind_of_row == 0, cell_width, 0.0)
    to_x = jnp.where((place_ref[0] & 1) == 0, to_x, -to_x)
    to_y = jnp.where(kind_of_row == 1, cell_width, 0.0)
    to_y = jnp.where((place_ref[1] & 1) == 0, to_y, -to_y)
    for cell, block_ref in enumerate((y_pair_ref, own_ref, y_beyond_ref)):
        ids, count = block_ids(block_ref[...], atoms, slots * atoms)
        ids_ref[cell : cell + 1, :] = ids
        own = unfold_block(column_ref[cell + 1], atoms)
        step_y = to_y if cell == 1 else -to_y
        rows = []
        for a in range(3):
            for b in range(3):
                block = frame[a][SLOT_CELLS[cell][b]]
                rows.append(block + ((1 - a) * to_x + (1 - b) * step_y))
        first_cell(
            slots, atoms, ids, count, rows, places, upper, own, embed_ref, kind_left, mix_high,
            mix_low, low_ref.at[cell], basis_ref.at[cell], slope_ref.at[cell], unit_ref.at[cell],
            sums_ref.at[cell], gate_ref.at[cell],
        )


def first_cell(slots, atoms, ids, count, rows, places, upper, own, embed_ref, kind_left, mix_high,
               mix_low, low_ref, basis_ref, slope_ref, unit_ref, sums_ref, gate_ref):
    per_cell = atoms // 128
    pieces = []
    for start in range(0, ids.shape[1], 128):
        part = jnp.broadcast_to(ids[:, start : start + 128], places.shape)
        lane, half = part & 127, (part >> 7) - upper
        found = jnp.zeros(places.shape, F32)
        for cell, block in enumerate(rows):
            value = jnp.take_along_axis(block, lane, axis=1)
            found = jnp.where(half == per_cell * cell, value, found)
        total = found
        for s in range(1, per_cell):
            total = total + pltpu.roll(found, 4 * per_cell - s, 0)
        pieces.append(total)
    found = jnp.concatenate(pieces, axis=1)
    found = [found[q * per_cell : q * per_cell + 1] for q in range(4)]
    rel = [found[q] - jnp.concatenate([own[q]] * slots, axis=1) for q in range(3)]
    distance = jnp.sqrt(rel[0] * rel[0] + rel[1] * rel[1] + rel[2] * rel[2] + soften)
    inverse = 1.0 / distance
    order = (lax.broadcasted_iota(jnp.int32, (8, 1), 0) + 1).astype(F32)
    sine, cosine = sin_cos((order * (0.5 / cut_radius)) * distance)
    wave = sine / ((order * (math.pi / cut_radius)) * distance)
    live = jnp.concatenate([jnp.where(count > n, 1.0, 0.0) for n in range(slots)], axis=1)
    basis = wave * live
    basis_ref[...] = basis
    slope_ref[...] = (cosine - wave) * (inverse * live)
    kinds = found[3]
    unit = jnp.concatenate(
        [r * inverse for r in rel] + [inverse, kinds] + [jnp.zeros_like(kinds)] * 3, axis=0
    )
    unit_ref[...] = unit
    stack = embed_ref[...]
    parts = edge_parts(basis, unit)
    species = kind_left.shape[2] // 32
    by_kind = [[None] * species for _ in range(4)]
    for n in range(slots):
        lanes = slice(n * atoms, (n + 1) * atoms)
        kind = jnp.broadcast_to(kinds[:, lanes], (8, atoms))
        for k in range(species):
            match = kind == float(k)
            for part in range(4):
                term = jnp.where(match, parts[part][:, lanes], 0.0)
                old = by_kind[part][k]
                by_kind[part][k] = term if old is None else old + term
    stacks = [stacked_right(jnp.concatenate(rows, axis=0)) for rows in by_kind]
    vectors = dot(kind_left[1], jnp.concatenate(stacks[1:], axis=1))
    sums = [dot(kind_left[0], stacks[0])]
    sums += [vectors[:, i * atoms : (i + 1) * atoms] for i in range(3)]
    step, gate = mixed(sums, mix_high, mix_low, 0)
    low_ref[...] = (embedded(stack, own[3]) + step).astype(BF16)
    for part in range(3):
        sums_ref[part] = sums[part + 1]
    gate_ref[...] = gate


def hot_columns(ids, rows):
    place = lax.broadcasted_iota(jnp.int32, (rows, ids.shape[1]), 0)
    return jnp.where(ids == place, 1.0, 0.0).astype(BF16)


def second_near_kernel(slots, ids_ref, basis_ref, unit_ref, left_ref, column_ref, weight_ref,
                       near_ref):
    atoms = column_ref.shape[2]
    parts = edge_parts(basis_ref[1], unit_ref[1])
    source = jnp.concatenate([column_ref[b] for b in range(3)], axis=1)
    for n in range(slots):
        lanes = slice(n * atoms, (n + 1) * atoms)
        for part in range(4):
            weight_ref[part, :, lanes] = weights_of(left_ref, part, parts[part][:, lanes])
        ids = ids_ref[1:2, lanes] - 3 * atoms
        near_ref[:, lanes] = dot(source, hot_columns(ids, 3 * atoms))


def second_side_kernel(slots, ids_ref, near_ref, pair_ref, out_ref):
    atoms = pair_ref.shape[2]
    source = jnp.concatenate([pair_ref[b] for b in range(3)], axis=1)
    for n in range(slots):
        lanes = slice(n * atoms, (n + 1) * atoms)
        hot = hot_columns(ids_ref[1:2, lanes], 3 * atoms)
        out_ref[:, lanes] = near_ref[:, lanes] + dot(source, hot)


def second_kernel(slots, hot_ref, weight_ref, near_ref, mix_high, mix_low, charge_ref, cell_ref,
                  column_ref, beyond_ref, feature_ref, sums_ref, gate_ref, packed_ref,
                  full_charge_ref, hidden_ref):
    atoms = column_ref.shape[2]
    source = jnp.concatenate([beyond_ref[b] for b in range(3)], axis=1)
    sums = [None] * 4
    for n in range(slots):
        lanes = slice(n * atoms, (n + 1) * atoms)
        feature = near_ref[:, lanes] + dot(source, hot_ref[:, lanes])
        feature_ref[:, lanes] = feature.astype(BF16)
        for part in range(4):
            term = weight_ref[part, :, lanes] * feature
            sums[part] = term if sums[part] is None else sums[part] + term
    step, gate = mixed(sums, mix_high, mix_low, 1)
    hidden = column_ref[1].astype(F32) + step
    hidden_ref[...] = hidden
    for part in range(3):
        sums_ref[part] = sums[part + 1]
    gate_ref[...] = gate
    charge = dot_split((charge_ref[0], charge_ref[1]), hidden)
    full_charge_ref[...] = charge
    place = jnp.concatenate(unfold_block(cell_ref[2], atoms)[:3], axis=0)
    high = place.astype(BF16).astype(F32)
    rest = place - high
    middle = rest.astype(BF16).astype(F32)
    zero = jnp.zeros((packed_ref.shape[0] - charge.shape[0] - 9, atoms), F32)
    packed_ref[...] = jnp.concatenate([charge, high, middle, rest - middle, zero], axis=0).astype(
        BF16
    )


def readout_kernel(hidden_high, hidden_low, turn_high, turn_low, out_ref, hidden_ref, energy_ref,
                   slope_ref):
    hidden = hidden_ref[...]
    value, slope = silu_pair(dot_split((hidden_high[...], hidden_low[...]), hidden))
    out = out_ref[...].T
    energy_ref[...] = jnp.sum(value * out, axis=0, keepdims=True)
    slope_ref[...] = dot_split((turn_high[...], turn_low[...]), slope * out)


def message_grads(cotangent, gate_ref, sums_ref, high_ref, low_ref, layer):
    pre = cotangent * gate_ref[...]
    both = dot_split((high_ref[layer], low_ref[layer]), pre)
    half = both.shape[0] // 2
    return [both[:half]] + [both[half:] * sums_ref[i] for i in range(3)]


def radial_grad(left, value):
    high, low = split(value)
    both = dot(left, jnp.concatenate([high, low], axis=0))
    half = both.shape[0] // 2
    return both[:half] + both[half:]


def second_back_kernel(slots, scale, count, hot_ref, weight_ref, turn_high, turn_low, charge_ref,
                       sums_ref, gate_ref, full_charge_ref, energy_ref, slope_ref, *refs):
    folds, refs = refs[:count], refs[count:]
    site_ref, long_ref, cotangent_ref, grad_ref, term_ref, beyond_ref = refs
    atoms = gate_ref.shape[1]
    total = folds[0][...].astype(F32)
    for part in folds[1:]:
        total = total + part[...].astype(F32)
    wide = full_charge_ref.shape[0]
    potential = total[:wide] * (2.0 * scale)
    slopes = total[wide : wide + 3] + total[wide + 3 : wide + 6] + total[wide + 6 : wide + 9]
    long_ref[...] = jnp.concatenate(
        [slopes * (2.0 * scale), jnp.zeros((5, atoms), F32)], axis=0
    )
    site_ref[0] = energy_ref[...] + 0.5 * jnp.sum(
        full_charge_ref[...] * potential, axis=0, keepdims=True
    )
    high, low = split(potential)
    turned = ((0,), (0,))
    cotangent = slope_ref[...] + (
        dot(charge_ref[0], high, turned)
        + (dot(charge_ref[0], low, turned) + dot(charge_ref[1], high, turned))
    )
    cotangent_ref[...] = cotangent
    grads = message_grads(cotangent, gate_ref, sums_ref, turn_high, turn_low, 1)
    for part in range(4):
        grad_ref[part] = grads[part]
    for n in range(slots):
        lanes = slice(n * atoms, (n + 1) * atoms)
        term = weight_ref[0, :, lanes] * grads[0]
        for part in range(1, 4):
            term = term + weight_ref[part, :, lanes] * grads[part]
        term_ref[:, lanes] = term.astype(BF16)
    for b in range(3):
        start = (3 + b) * atoms
        beyond_ref[b] = dot(term_ref[...], hot_ref[:, start : start + atoms]).astype(BF16)


def second_pair_kernel(hot_ref, term_ref, pair_ref):
    atoms = pair_ref.shape[2]
    for b in range(3):
        pair_ref[b] = dot(term_ref[...], hot_ref[:, b * atoms : (b + 1) * atoms]).astype(BF16)


def second_middle_kernel(hot_ref, term_ref, cotangent_ref, middle_ref):
    atoms = cotangent_ref.shape[1]
    for b in range(3):
        grad = dot(term_ref[...], hot_ref[:, b * atoms : (b + 1) * atoms])
        middle_ref[b] = grad + cotangent_ref[...] if b == 1 else grad


def second_edge_kernel(slots, back_ref, feature_ref, grad_ref, edge_ref):
    atoms = grad_ref.shape[2]
    for n in range(slots):
        lanes = slice(n * atoms, (n + 1) * atoms)
        feature = feature_ref[:, lanes].astype(F32)
        for part in range(4):
            edge_ref[8 * part : 8 * part + 8, lanes] = radial_grad(
                back_ref[1 if part else 0], grad_ref[part] * feature
            )


def first_back_kernel(slots, ids_ref, basis_ref, slope_ref, unit_ref, kind_high, kind_low, turn_high,
                      turn_low, sums_ref, gate_ref, edge_ref, from_beyond, long_ref, middle_ref,
                      from_pair, *outs):
    sums = {(1, 2): long_ref[...]}
    for cell in range(3):
        cotangent = middle_ref[cell] + (
            from_pair[cell].astype(F32) + from_beyond[cell].astype(F32)
        )
        own, found = first_back_cell(
            slots, ids_ref[cell : cell + 1, :], basis_ref.at[cell], slope_ref.at[cell],
            unit_ref.at[cell], kind_high, kind_low, turn_high, turn_low, sums_ref.at[cell],
            gate_ref.at[cell], edge_ref if cell == 1 else None, cotangent,
        )
        terms = [((1, cell + 1), own)]
        terms += [((n // 3, SLOT_CELLS[cell][n % 3]), found[n]) for n in range(9)]
        for key, term in terms:
            sums[key] = sums[key] + term if key in sums else term
    for x in range(3):
        rows = [sums[(x, y)][:3] for y in range(5)]
        outs[x][...] = jnp.concatenate(rows + [jnp.zeros((1, rows[0].shape[1]), F32)], axis=0)


def first_back_cell(slots, ids, basis_ref, slope_ref, unit_ref, kind_high, kind_low, turn_high,
                    turn_low, sums_ref, gate_ref, edge_ref, cotangent):
    atoms = gate_ref.shape[1]
    pre = cotangent * gate_ref[...]
    both = dot_split((turn_high[0], turn_low[0]), pre)
    wide = both.shape[0] // 2
    grads = [both[:wide]] + [both[wide:] * sums_ref[i] for i in range(3)]
    unit = unit_ref[...]
    kinds = unit[4:5]
    by_kind = [dot_split((kind_high[0], kind_low[0]), grads[0])]
    by_kind += [dot_split((kind_high[1], kind_low[1]), grads[i]) for i in range(1, 4)]
    species = by_kind[0].shape[0] // 8
    edges = [[] for _ in range(4)]
    for n in range(slots):
        kind = jnp.broadcast_to(kinds[:, n * atoms : (n + 1) * atoms], (8, atoms))
        matches = [kind == float(k) for k in range(1, species)]
        for part in range(4):
            rows = by_kind[part]
            found = rows[:8]
            for k, match in enumerate(matches):
                found = jnp.where(match, rows[8 * k + 8 : 8 * k + 16], found)
            edges[part].append(found)
    edges = [jnp.concatenate(rows, axis=1) for rows in edges]
    if edge_ref is not None:
        edges = [edge_ref[8 * part : 8 * part + 8] + edges[part] for part in range(4)]
    basis = basis_ref[...]
    units = [unit[i : i + 1] for i in range(3)]
    inverse = unit[3:4]
    by_basis = edges[0]
    for i in range(3):
        by_basis = by_basis + edges[i + 1] * units[i]
    by_unit = [jnp.sum(edges[i + 1] * basis, axis=0, keepdims=True) * inverse for i in range(3)]
    by_distance = jnp.sum(by_basis * slope_ref[...], axis=0, keepdims=True)
    for i in range(3):
        by_distance = by_distance - by_unit[i] * units[i]
    moves = [by_unit[i] + by_distance * units[i] for i in range(3)]
    zero = jnp.zeros_like(moves[0])
    move = jnp.concatenate(moves + [zero] * 5, axis=0)
    own = -move[:, :atoms]
    for n in range(1, slots):
        own = own - move[:, n * atoms : (n + 1) * atoms]
    source = cell_of(ids, atoms)
    atom_hot = hot_columns(ids - source * atoms, atoms)
    high = move.astype(BF16).astype(F32)
    both = jnp.concatenate([high, move - high], axis=0)
    rows = jnp.concatenate(
        [jnp.where(source == cell, both, 0.0).astype(BF16) for cell in range(9)], axis=0
    )
    spread = dot(rows, atom_hot, ((1,), (1,)))
    grads = [
        spread[16 * cell : 16 * cell + 8] + spread[16 * cell + 8 : 16 * cell + 16]
        for cell in range(9)
    ]
    return own, grads


def pair_counts(parts):
    total = WAVE_REACH + WAVE_REACH * (2 * WAVE_REACH + 1)
    share = -(-total // parts)
    return total, share, -(-share // 16) * 16


def pair_vectors(slot, share, part):
    side = 2 * WAVE_REACH + 1
    total = WAVE_REACH + WAVE_REACH * side
    index = slot + part.astype(F32) * share
    later = index - WAVE_REACH
    row = jnp.floor((later + 0.5) * (1.0 / side))
    first = index < WAVE_REACH
    kx = jnp.where(first, 0.0, row + 1.0)
    ky = jnp.where(first, index + 1.0, later - row * side - WAVE_REACH)
    valid = jnp.where((slot < share) & (index < total), 1.0, 0.0)
    return kx, ky, valid


def count_up(rows):
    return lax.broadcasted_iota(jnp.int32, (rows, 1), 0).astype(F32)


def green_weights(share, padded, grid, place_ref, vec_ref, weight_ref):
    grid_x, grid_y = grid
    turn = 2.0 * math.pi
    side = 2 * WAVE_REACH + 1
    top = side * side * side - 1
    vec = vec_ref[...].astype(F32) + WAVE_REACH
    code = (vec[0:1] * side + vec[1:2]) * side + vec[2:3]
    code = jnp.maximum(code, top - code)
    span = 8 * share
    row = count_up(span)
    slot = jnp.floor(row * 0.125)
    height = row - 8.0 * slot + 1.0
    flat = count_up(padded)
    slot = jnp.concatenate([slot, slot, flat], axis=0)
    kz = jnp.concatenate([height, -height, jnp.zeros_like(flat)], axis=0)
    kx, ky, valid = pair_vectors(slot, share, place_ref[0, 0:1, 0:1])
    own = ((kx + WAVE_REACH) * side + ky + WAVE_REACH) * side + kz + WAVE_REACH
    seen = jnp.zeros((own.shape[0], 128), F32)
    for start in range(0, code.shape[1], 128):
        seen = seen + jnp.where(own == code[:, start : start + 128], 1.0, 0.0)
    count = jnp.sum(seen, axis=1, keepdims=True) * valid
    sq = (
        (kx * (turn / (grid_x * cell_width))) ** 2
        + (ky * (turn / (grid_y * cell_width))) ** 2
        + (kz * (turn / box_height)) ** 2
    )
    green = jnp.exp(-smear_width * sq) / (sq + screen * screen) * count
    weight_ref[...] = jnp.broadcast_to(green, weight_ref.shape)


def basis_rows(share, ca, sa, cb, sb):
    cc, ss, sc, cs = [], [], [], []
    for p in range(share):
        c, s = ca[p : p + 1], sa[p : p + 1]
        cc.append(c * cb)
        ss.append(s * sb)
        sc.append(s * cb)
        cs.append(c * sb)
    return cc, ss, sc, cs


def unpack_rows(block):
    half = block.shape[1] // 2
    return jnp.concatenate([block[:, :half], block[:, half:]], axis=0)


def pack_rows(block):
    half = block.shape[0] // 2
    return jnp.concatenate([block[:half], block[half:]], axis=1)


def structure_kernel(share, padded, grid, wide, flip, place_ref, blocks, *refs):
    grid_x, grid_y = grid
    if flip:
        near_ref, (ca_ref, sa_ref, cb_ref, sb_ref, high_ref, low_ref, own_ref, out_ref) = (
            refs[0],
            refs[1:],
        )
        total = near_ref[...]
    else:
        ca_ref, sa_ref, cb_ref, sb_ref, high_ref, low_ref, total_ref = refs
        total = None
    col = place_ref[1, 0:1, 0:1].astype(F32) * (1.0 / grid_y)
    first = place_ref[0, 0:1, 0:1] ^ flip
    kx, ky, _ = pair_vectors(count_up(padded), share, place_ref[0, 0:1, 0:1])
    kz = count_up(8) + 1.0
    for d in range(grid_x // 2):
        block = blocks[d]
        charge = block[:wide]
        atoms = charge.shape[1]
        pieces = block[wide:].astype(F32)
        place = pieces[0:3] + (pieces[3:6] + pieces[6:9])
        row = (first ^ (2 * d)).astype(F32) * (1.0 / grid_x)
        x = place[0:1] * (1.0 / (grid_x * cell_width)) + row
        y = place[1:2] * (1.0 / (grid_y * cell_width)) + col
        sa, ca = sin_cos(kx * x + ky * y)
        sb, cb = sin_cos(kz * (place[2:3] * (1.0 / box_height)))
        lanes = pl.ds(d * atoms, atoms)
        ca_ref[:, lanes] = ca
        sa_ref[:, lanes] = sa
        cb_ref[:, lanes] = cb
        sb_ref[:, lanes] = sb
        cc, ss, sc, cs = basis_rows(share, ca, sa, cb, sb)
        high, low = split(jnp.concatenate(cc + ss + sc + cs + [ca, sa], axis=0))
        high_ref[:, lanes] = high
        low_ref[:, lanes] = low
        term = dot(high, charge, ((1,), (1,))) + dot(low, charge, ((1,), (1,)))
        total = term if total is None else total + term
    if flip:
        packed = pack_rows(total)
        own_ref[...] = packed
        out_ref[...] = packed.astype(BF16)
    else:
        total_ref[...] = total


def weighted_rows(share, padded, wide, weight_ref, parts):
    packed = parts[0][...].astype(F32)
    for part in parts[1:]:
        packed = packed + part[...].astype(F32)
    struct = unpack_rows(packed)
    span = 8 * share
    cc, ss, sc, cs = (struct[i * span : (i + 1) * span] for i in range(4))
    weight = weight_ref[:, :wide]
    plus, minus, flat = weight[:span], weight[span : 2 * span], weight[2 * span :]
    re_plus, im_plus = plus * (cc - ss), plus * (sc + cs)
    re_minus, im_minus = minus * (cc + ss), minus * (sc - cs)
    rows = jnp.concatenate(
        [
            re_plus + re_minus,
            re_minus - re_plus,
            im_plus + im_minus,
            im_plus - im_minus,
            flat * struct[4 * span : 4 * span + padded],
            flat * struct[4 * span + padded :],
        ],
        axis=0,
    )
    return rows


def fold_kernel(share, padded, grid, wide, flip, place_ref, *refs):
    grid_x, grid_y = grid
    turn = 2.0 * math.pi
    if flip:
        weight_ref, parts, refs = refs[0], refs[1 : 1 + grid_y], refs[1 + grid_y :]
        rows = weighted_rows(share, padded, wide, weight_ref, parts)
        refs, rows_ref = refs[:-1], refs[-1]
        rows_ref[...] = rows
    else:
        rows, refs = refs[0][...], refs[1:]
    ca_ref, sa_ref, cb_ref, sb_ref, high_ref, low_ref, blocks, out_ref = refs
    row_high, row_low = split(rows)
    row_pair = jnp.concatenate([row_high, row_low], axis=1)
    turned = rows.T
    t_high, t_low = split(turned)
    t_both = jnp.concatenate([t_high, t_low], axis=0)
    span = 8 * share
    kx, ky, _ = pair_vectors(count_up(padded), share, place_ref[0, 0:1, 0:1])
    kx = kx * (turn / (grid_x * cell_width))
    ky = ky * (turn / (grid_y * cell_width))
    kz = (count_up(8) + 1.0) * (turn / box_height)
    for d in range(grid_x // 2):
        charge = blocks[d][:wide]
        atoms = charge.shape[1]
        lanes = pl.ds(d * atoms, atoms)
        ca, sa, cb, sb = ca_ref[:, lanes], sa_ref[:, lanes], cb_ref[:, lanes], sb_ref[:, lanes]
        bcc, bss, bsc, bcs = basis_rows(share, ca, sa, cb, sb)
        high, low = high_ref[:, lanes], low_ref[:, lanes]
        both = dot(t_both, high)
        pot = both[:wide] + both[wide:] + dot(t_high, low)
        proj = dot(row_pair, jnp.concatenate([charge, charge], axis=0))
        by_x = jnp.zeros((8, atoms), jnp.float32)
        by_y = jnp.zeros((8, atoms), jnp.float32)
        by_z = jnp.zeros((8, atoms), jnp.float32)
        for p in range(share):
            pcc, pss, psc, pcs = (
                proj[i * span + 8 * p : i * span + 8 * p + 8] for i in range(4)
            )
            slope = bcs[p] * pss - bsc[p] * pcc + bcc[p] * psc - bss[p] * pcs
            by_x = by_x + kx[p : p + 1] * slope
            by_y = by_y + ky[p : p + 1] * slope
            by_z = by_z + (bsc[p] * pss - bcs[p] * pcc - bss[p] * psc + bcc[p] * pcs)
        flat_slope = ca * proj[4 * span + padded :] - sa * proj[4 * span : 4 * span + padded]
        grad_x = jnp.sum(by_x, axis=0, keepdims=True) + jnp.sum(kx * flat_slope, axis=0, keepdims=True)
        grad_y = jnp.sum(by_y, axis=0, keepdims=True) + jnp.sum(ky * flat_slope, axis=0, keepdims=True)
        grad_z = jnp.sum(kz * by_z, axis=0, keepdims=True)
        slopes = jnp.concatenate([grad_x, grad_y, grad_z], axis=0)
        out_ref[d] = pieced(pot, slopes, out_ref.shape[1]).astype(out_ref.dtype)


def pieced(pot, slopes, rows):
    high = slopes.astype(BF16).astype(F32)
    rest = slopes - high
    middle = rest.astype(BF16).astype(F32)
    zero = jnp.zeros((rows - pot.shape[0] - 9, pot.shape[1]), F32)
    return jnp.concatenate([pot, high, middle, rest - middle, zero], axis=0)


def unpieced(block, wide):
    slopes = block[wide : wide + 3] + (block[wide + 3 : wide + 6] + block[wide + 6 : wide + 9])
    return block[:wide], slopes


def join_kernel(wide, near_ref, far_ref, own_ref, *outs):
    for d in range(near_ref.shape[0]):
        pot, slopes = unpieced(near_ref[d], wide)
        pot_far, slopes_far = unpieced(far_ref[d].astype(F32), wide)
        block = pieced(pot + pot_far, slopes + slopes_far, near_ref.shape[1])
        if d:
            outs[d - 1][...] = block.astype(BF16)
        else:
            own_ref[...] = block


def per_device(
    positions,
    species,
    neighbours,
    counts,
    species_embed,
    radial,
    mixing,
    read_hidden,
    read_out,
    charge_map,
    wavevectors,
):
    atoms = positions.shape[3]
    slots = neighbours.shape[3]
    features, lat_width = charge_map.shape
    wave_count = wavevectors.shape[1]
    grid = lax.axis_size("gx"), lax.axis_size("gy")
    grid_x, grid_y = grid
    edges = slots * atoms
    scale = 1.0 / math.sqrt(wave_count * lat_width * atoms * grid_x * grid_y)
    place = jnp.stack([lax.axis_index("gx"), lax.axis_index("gy")]).astype(jnp.int32)
    place = jnp.broadcast_to(place[:, None, None], (2, 8, 128))
    _, share, padded = pair_counts(grid_x)
    ids = neighbours.transpose(0, 3, 1, 2).reshape(1, edges)
    cell_rows = 4 * atoms // 128
    block_total = -(-(cell_rows + (edges + atoms) // 128) // 8) * 8
    dma = pltpu.SemaphoreType.DMA
    shown = positions.transpose(0, 2, 1, 3)
    (own_place,) = run(
        pack_kernel,
        [shape(cell_rows, 128)],
        [place, shown, species],
        flops=10_000_000_000,
        name="pack",
    )
    (own,) = run(
        pack_more_kernel,
        [shape(block_total, 128)],
        [place, ids, counts, own_place],
        name="pack_more",
    )
    y_beyond, y_pair = beyond(own, "gy"), paired(own, "gy", 1)
    over_pair = far(own_place, "gy", True)
    over_beyond = over_pair if grid_y == 4 else far(own_place, "gy", False)
    cells = jnp.stack(
        [over_pair, y_pair[:cell_rows], own_place, y_beyond[:cell_rows], over_beyond]
    )
    x_beyond, x_pair = beyond(cells, "gx"), paired(cells, "gx", 1)
    cells = [x_pair, cells, x_beyond]

    norm = 1.0 / math.sqrt(slots)
    kind_rows = 8 * species_embed.shape[0]
    low_pair = lambda *dims: [shape(*dims, dtype=BF16)] * 2
    embed, kind_left, left, back, kind_high, kind_low, mix_high, mix_low, turn_high, turn_low = run(
        functools.partial(prep_first_kernel, norm),
        [
            shape(features, 32, dtype=BF16),
            shape(2, features, 4 * kind_rows, dtype=BF16),
            shape(2, features, 32, dtype=BF16),
            shape(2, 16, 2 * features, dtype=BF16),
        ]
        + low_pair(2, kind_rows, features)
        + low_pair(2, features, 2 * features)
        + low_pair(2, 2 * features, features),
        [species_embed, radial, mixing],
        scratch=[
            pltpu.VMEM(species_embed.shape, F32),
            pltpu.VMEM(radial.shape, F32),
            pltpu.VMEM(mixing.shape, F32),
            dma((3,)),
        ],
        hbm=3,
        name="prep_first",
    )
    read_out, hidden_high, hidden_low, hidden_turn_high, hidden_turn_low, charge_pair = run(
        prep_second_kernel,
        [shape(1, features)]
        + low_pair(features, features)
        + low_pair(features, features)
        + [shape(2, lat_width, features, dtype=BF16)],
        [read_out[None, :], read_hidden, charge_map.T],
        scratch=[
            pltpu.VMEM(read_hidden.shape, F32),
            pltpu.VMEM((lat_width, features), F32),
            dma((3,)),
        ],
        hbm=3,
        name="prep_second",
    )
    cells[2], hidden_high = lax.optimization_barrier((cells[2], hidden_high))
    low, ids, basis, slope, unit, sums_one, gate_one = run(
        functools.partial(first_kernel, slots),
        [
            shape(3, features, atoms, dtype=BF16),
            shape(3, edges, dtype=jnp.int32),
            shape(3, 8, edges),
            shape(3, 8, edges),
            shape(3, 8, edges),
            shape(3, 3, features, atoms),
            shape(3, features, atoms),
        ],
        [place, embed, kind_left, mix_high, mix_low, y_beyond, own, y_pair] + cells[::-1],
        name="first",
    )
    hidden = [paired(low, "gx", 1), low, beyond(low, "gx")]
    edge_weights, near = run(
        functools.partial(second_near_kernel, slots),
        [shape(4, features, edges), shape(features, edges)],
        [ids, basis, unit, left, low],
        flops=2_000_000_000,
        name="second_near",
    )
    (hot_beyond,) = run(
        hot_beyond_kernel,
        [shape(3 * atoms, edges, dtype=BF16)],
        [ids, near],
        flops=1_000_000,
        name="hot_beyond",
    )
    (near,) = run(
        functools.partial(second_side_kernel, slots),
        [shape(features, edges)],
        [ids, near, hidden[0]],
        flops=1_000_000_000,
        name="second_side",
    )
    block_rows = -(-(lat_width + 9) // 16) * 16
    feature, sums_two, gate_two, packed, charge, hidden_two = run(
        functools.partial(second_kernel, slots),
        [
            shape(features, edges, dtype=BF16),
            shape(3, features, atoms),
            shape(features, atoms),
            shape(block_rows, atoms, dtype=BF16),
            shape(lat_width, atoms),
            shape(features, atoms),
        ],
        [hot_beyond, edge_weights, near, mix_high, mix_low, charge_pair, cells[1], hidden[1],
         hidden[2]],
        name="second",
    )
    energy, energy_slope = run(
        readout_kernel,
        [shape(1, atoms), shape(features, atoms)],
        [hidden_high, hidden_low, hidden_turn_high, hidden_turn_low, read_out, hidden_two],
        name="readout",
    )
    half = grid_x // 2
    near_charges = jnp.stack([packed] + [paired(packed, "gx", 2 * d) for d in range(1, half)])
    (weight,) = run(
        functools.partial(green_weights, share, padded, grid),
        [shape(16 * share + padded, 128)],
        [place, wavevectors],
        name="green",
    )
    near_charges, weight = lax.optimization_barrier((near_charges, weight))
    far_charges = paired(near_charges, "gx", 1)
    span = half * atoms
    rows = 32 * share + 2 * padded
    phase_shapes = [
        shape(padded, span),
        shape(padded, span),
        shape(8, span),
        shape(8, span),
        shape(rows, span, dtype=BF16),
        shape(rows, span, dtype=BF16),
    ]
    *near_phases, near_total = run(
        functools.partial(structure_kernel, share, padded, grid, lat_width, 0),
        phase_shapes + [shape(rows, lat_width)],
        [place, near_charges],
        flops=1_000_000_000,
        name="structure_near",
    )
    *far_phases, own_part, part = run(
        functools.partial(structure_kernel, share, padded, grid, lat_width, 1),
        phase_shapes
        + [
            shape(rows // 2, 2 * lat_width),
            shape(rows // 2, 2 * lat_width, dtype=BF16),
        ],
        [place, far_charges, near_total],
        name="structure_far",
    )
    parts = [own_part] + [paired(part, "gy", d) for d in range(1, grid_y)]
    (hot_back,) = run(
        functools.partial(hot_back_kernel, (0, 2)),
        [shape(edges, 6 * atoms, dtype=BF16)],
        [ids],
        flops=2_000_000_000,
        name="hot_back",
    )
    parts, hot_back = lax.optimization_barrier((parts, hot_back))
    far_folds, wave_rows = run(
        functools.partial(fold_kernel, share, padded, grid, lat_width, 1),
        [shape(half, block_rows, atoms, dtype=BF16), shape(rows, lat_width)],
        [place, weight] + parts + far_phases + [far_charges],
        name="fold_far",
    )
    far_folds = paired(far_folds, "gx", 1)
    (near_folds,) = run(
        functools.partial(fold_kernel, share, padded, grid, lat_width, 0),
        [shape(half, block_rows, atoms)],
        [place, wave_rows] + near_phases + [near_charges],
        flops=1_000_000_000,
        name="fold_near",
    )
    folds = run(
        functools.partial(join_kernel, lat_width),
        [shape(block_rows, atoms)] + [shape(block_rows, atoms, dtype=BF16)] * (half - 1),
        [near_folds, far_folds],
        name="fold_join",
    )
    folds = [folds[0]] + [paired(folds[d], "gx", 2 * d) for d in range(1, half)]

    site, long, cotangent, grads, term, to_beyond = run(
        functools.partial(second_back_kernel, slots, scale, half),
        [
            shape(1, 1, atoms),
            shape(8, atoms),
            shape(features, atoms),
            shape(4, features, atoms),
            shape(features, edges, dtype=BF16),
            shape(3, features, atoms, dtype=BF16),
        ],
        [hot_back, edge_weights, turn_high, turn_low, charge_pair, sums_two, gate_two, charge,
         energy, energy_slope] + folds,
        name="second_back",
    )
    (to_pair,) = run(
        second_pair_kernel,
        [shape(3, features, atoms, dtype=BF16)],
        [hot_back, term],
        flops=1_000_000,
        name="second_pair",
    )
    from_pair, from_beyond = paired(to_pair, "gx", 1), beyond(to_beyond, "gx")
    (hot_middle,) = run(
        functools.partial(hot_back_kernel, (1,)),
        [shape(edges, 3 * atoms, dtype=BF16)],
        [ids],
        flops=1_000_000_000,
        name="hot_middle",
    )
    (middle,) = run(
        second_middle_kernel,
        [shape(3, features, atoms)],
        [hot_middle, term, cotangent],
        flops=1_000_000_000,
        name="second_middle",
    )
    (edge,) = run(
        functools.partial(second_edge_kernel, slots),
        [shape(32, edges)],
        [back, feature, grads],
        flops=1_000_000_000,
        name="second_edge",
    )
    to_pair, middle, to_beyond = run(
        functools.partial(first_back_kernel, slots),
        [shape(16, atoms)] * 3,
        [ids, basis, slope, unit, kind_high, kind_low, turn_high, turn_low, sums_one, gate_one, edge,
         from_beyond, long, middle, from_pair],
        name="first_back",
    )
    total = middle + paired(to_pair, "gx", 1) + beyond(to_beyond, "gx")
    total = [total[3 * y : 3 * y + 3] for y in range(5)]
    if grid_y == 4:
        distant = far(total[0] + total[4], "gy", True)
    else:
        distant = far(total[0], "gy", False) + far(total[4], "gy", True)
    total = total[2] + paired(total[1], "gy", 1) + beyond(total[3], "gy") + distant
    forces = -total[None, :, None, :]
    return (forces.transpose(0, 2, 1, 3), site)


def solution(mesh):
    in_specs = (
        P("gx", "gy", None, None),
        P("gx", "gy", None),
        P("gx", "gy", None, None),
        P("gx", "gy", None),
        P(),
        P(),
        P(),
        P(),
        P(),
        P(),
        P(),
    )
    out_specs = (P("gx", "gy", None, None), P("gx", "gy", None))
    return jax.shard_map(
        per_device, mesh=mesh, in_specs=in_specs, out_specs=out_specs, check_vma=False
    )
```

```python
import functools
import math

import jax
import jax.numpy as jnp
import numpy as np
from jax import lax
from jax.experimental import pallas as pl
from jax.experimental.pallas import tpu as pltpu
from jax.sharding import PartitionSpec as P

cell_width = 10.0
box_height = 30.0
cut_radius = 50.0
soften = 0.25
screen = 0.5
smear_width = 0.5
WAVE_REACH = 8
F32 = jnp.float32
BF16 = jnp.bfloat16


def paired(block, axis, mask):
    return lax.ppermute(block, axis, [(i ^ mask, i) for i in range(lax.axis_size(axis))])


def other_side(index, count):
    return (index + (1 if index % 2 else -1)) % count


def beyond(block, axis):
    count = lax.axis_size(axis)
    return lax.ppermute(block, axis, [(other_side(i, count), i) for i in range(count)])


def far(block, axis, over_pair):
    count = lax.axis_size(axis)
    if over_pair:
        route = [(other_side(i ^ 1, count), i) for i in range(count)]
    else:
        route = [(other_side(i, count) ^ 1, i) for i in range(count)]
    return lax.ppermute(block, axis, route)


SLOT_CELLS = ((2, 1, 0), (1, 2, 3), (4, 3, 2))


def whole(space=pltpu.VMEM):
    return pl.BlockSpec(memory_space=space)


def run(kernel, outs, args, scratch=(), hbm=0, flops=10_000_000, grant=16, name=None):
    specs = [whole()] * (len(args) - hbm) + [whole(pltpu.HBM)] * hbm
    return list(
        pl.pallas_call(
            kernel,
            out_shape=outs,
            in_specs=specs,
            out_specs=[whole() for _ in outs],
            scratch_shapes=list(scratch),
            compiler_params=pltpu.CompilerParams(vmem_limit_bytes=grant * 1024 * 1024),
            cost_estimate=pl.CostEstimate(
                flops=flops, bytes_accessed=1_000_000, transcendentals=0
            ),
            name=name,
        )(*args)
    )


def shape(*dims, dtype=F32):
    return jax.ShapeDtypeStruct(dims, dtype)


def split(value):
    high = value.astype(BF16)
    return high, (value - high.astype(F32)).astype(BF16)


def dot(left, right, contract=((1,), (0,))):
    return lax.dot_general(left, right, (contract, ((), ())), preferred_element_type=F32)


def dot3(left, right):
    left_high, left_low = split(left)
    right_high, right_low = split(right)
    return dot(left_high, right_high) + (dot(left_high, right_low) + dot(left_low, right_high))


def dot_split(left, right):
    right_high, right_low = split(right)
    return dot(left[0], right_high) + (dot(left[0], right_low) + dot(left[1], right_high))


def sin_cos(turns):
    quarter = jnp.round(turns * 4.0)
    x = (turns - quarter * 0.25) * (2.0 * math.pi)
    z = x * x
    sine = ((-1.9515295891e-4 * z + 8.3321608736e-3) * z - 1.6666654611e-1) * (z * x) + x
    cosine = (2.443315711809948e-5 * z - 1.388731625493765e-3) * z + 4.166664568298827e-2
    cosine = cosine * (z * z) - 0.5 * z + 1.0
    k = quarter.astype(jnp.int32) & 3
    odd = (k & 1) == 1
    by_sine = jnp.where(odd, cosine, sine)
    by_cosine = jnp.where(odd, sine, cosine)
    return (
        jnp.where(k >= 2, -by_sine, by_sine),
        jnp.where((k == 1) | (k == 2), -by_cosine, by_cosine),
    )


def stacked_left(value):
    high = value.astype(BF16).astype(F32)
    rows = jnp.concatenate([high, high, value - high, jnp.zeros_like(high)], axis=0)
    return rows.T.astype(BF16)


def stacked_right(value):
    high = value.astype(BF16).astype(F32)
    return jnp.concatenate([high, value - high, high, jnp.zeros_like(high)], axis=0).astype(BF16)


def silu_pair(value):
    gate = 1.0 / (1.0 + jnp.exp(-value))
    return value * gate, gate * (1.0 + value * (1.0 - gate))


def onehot_kinds(kinds, rows):
    levels = lax.broadcasted_iota(jnp.int32, (rows, kinds.shape[1]), 0).astype(F32)
    return jnp.where(kinds == levels, 1.0, 0.0)


def embedding_stack(embed):
    high = embed.astype(BF16).astype(F32)
    rest = embed - high
    middle = rest.astype(BF16).astype(F32)
    rows = jnp.concatenate([high, middle, rest - middle, jnp.zeros_like(high)], axis=0)
    return rows.T.astype(BF16)


def embedded(stack, kinds):
    hot = onehot_kinds(kinds, 8)
    return dot(stack, jnp.concatenate([hot, hot, hot, jnp.zeros_like(hot)], axis=0).astype(BF16))


def weights_of(stack_ref, part, rows):
    return dot(stack_ref[1 if part else 0], stacked_right(rows))


def mixed(sums, high_ref, low_ref, layer):
    squares = sums[1] * sums[1] + sums[2] * sums[2] + sums[3] * sums[3]
    both = jnp.concatenate([sums[0], squares], axis=0)
    return silu_pair(dot_split((high_ref[layer], low_ref[layer]), both))


def edge_parts(basis, unit):
    return [basis] + [basis * unit[i : i + 1] for i in range(3)]


def pack_kernel(place_ref, position_ref, species_ref, out_ref):
    rows = [position_ref[0, i] for i in range(3)] + [species_ref[0].astype(F32)]
    atoms = rows[0].shape[1]
    out_ref[...] = jnp.concatenate(
        [row[:, s : s + 128] for row in rows for s in range(0, atoms, 128)], axis=0
    )


def pack_more_kernel(place_ref, ids_ref, count_ref, first_ref, out_ref):
    atoms = count_ref.shape[2]
    order = slot_order(ids_ref[...], place_ref, atoms).astype(F32)
    rows = [first_ref[...]]
    rows += [order[:, s : s + 128] for s in range(0, order.shape[1], 128)]
    rows += [count_ref[0, :, s : s + 128].astype(F32) for s in range(0, atoms, 128)]
    missing = out_ref.shape[0] - sum(row.shape[0] for row in rows)
    out_ref[...] = jnp.concatenate(rows + [jnp.zeros((missing, 128), F32)], axis=0)


def block_ids(block, atoms, edges):
    start = 4 * atoms // 128
    middle, end = start + edges // 128, start + edges // 128 + atoms // 128
    rows = [block[r : r + 1] for r in range(start, end)]
    ids = jnp.concatenate(rows[: middle - start], axis=1).astype(jnp.int32)
    return ids, jnp.concatenate(rows[middle - start :], axis=1)


def radial_left(radial):
    high = radial.astype(BF16).astype(F32)
    low = radial - high
    top = jnp.concatenate([high, high], axis=1)
    end = jnp.concatenate([low, jnp.zeros_like(low)], axis=1)
    return jnp.concatenate([top, end], axis=0).astype(BF16)


def put_split(value, high_ref, low_ref, *at):
    high, low = split(value)
    high_ref[at] = high
    low_ref[at] = low


def cell_of(ids, atoms):
    return ids >> (atoms.bit_length() - 1) if atoms & (atoms - 1) == 0 else ids // atoms


def slot_order(ids, place_ref, atoms):
    cell = cell_of(ids, atoms)
    a = (cell * 11) >> 5
    b = cell - 3 * a
    a = jnp.where((place_ref[0, 0:1, 0:1] & 1) == 0, 2 - a, a)
    b = jnp.where((place_ref[1, 0:1, 0:1] & 1) == 0, 2 - b, b)
    return ids + (3 * a + b - cell) * atoms


def fetch(sources, targets, sems):
    copies = [
        pltpu.make_async_copy(source, target, sems.at[i])
        for i, (source, target) in enumerate(zip(sources, targets))
    ]
    for copy in copies:
        copy.start()
    for copy in copies:
        copy.wait()


def prep_first_kernel(norm, embed_in, radial_in, mixing_in, embed_out, kind_left, left_out, back_out,
                      kind_high, kind_low, mix_high, mix_low, turn_high, turn_low, embed_ref,
                      radial_ref, mixing_ref, sems):
    fetch([embed_in, radial_in, mixing_in], [embed_ref, radial_ref, mixing_ref], sems)
    embed = embed_ref[...]
    kinds = embed.shape[0]
    for path in range(2):
        radial = radial_ref[0, path] * norm
        rows = jnp.concatenate([radial * embed[s : s + 1] for s in range(kinds)], axis=0)
        kind_left[path] = stacked_left(rows)
        put_split(rows, kind_high, kind_low, path)
        radial = radial_ref[1, path] * norm
        left_out[path] = stacked_left(radial)
        back_out[path] = radial_left(radial)
    for layer in range(2):
        scalar, vector = mixing_ref[layer, 0], mixing_ref[layer, 1]
        put_split(jnp.concatenate([scalar.T, vector.T], axis=1), mix_high, mix_low, layer)
        put_split(jnp.concatenate([scalar, 2.0 * vector], axis=0), turn_high, turn_low, layer)
    embed = jnp.concatenate([embed, jnp.zeros((8 - kinds, embed.shape[1]), F32)], axis=0)
    embed_out[...] = embedding_stack(embed)


def prep_second_kernel(read_in, hidden_in, charge_in, read_ref, hidden_high, hidden_low,
                       hidden_turn_high, hidden_turn_low, charge_pair, hidden_ref, charge_ref, sems):
    fetch([read_in, hidden_in, charge_in], [read_ref, hidden_ref, charge_ref], sems)
    put_split(hidden_ref[...].T, hidden_high, hidden_low, Ellipsis)
    put_split(hidden_ref[...], hidden_turn_high, hidden_turn_low, Ellipsis)
    charge = charge_ref[...]
    high = charge.astype(BF16).astype(F32)
    charge_pair[0] = high.astype(BF16)
    charge_pair[1] = (charge - high).astype(BF16)


def hot_beyond_kernel(ids_ref, near_ref, hot_ref):
    ids = ids_ref[1:2, :] - 2 * hot_ref.shape[0]
    for start in range(0, hot_ref.shape[1], 256):
        lanes = slice(start, start + 256)
        hot_ref[:, lanes] = hot_columns(ids[:, lanes], hot_ref.shape[0])


def hot_back_kernel(slots_x, ids_ref, hot_ref):
    edges = ids_ref.shape[1]
    width = hot_ref.shape[1] // len(slots_x)
    entry = lax.broadcasted_iota(jnp.int32, (128, width), 1).astype(F32)
    for start in range(0, edges, 128):
        row = jnp.broadcast_to(ids_ref[1:2, start : start + 128].astype(F32), (8, 128))
        column = row.T[:, 0:1]
        for n, slot in enumerate(slots_x):
            hot_ref[start : start + 128, n * width : (n + 1) * width] = jnp.where(
                column - float(slot * width) == entry, 1.0, 0.0
            ).astype(BF16)


def atom_hot_kernel(ids_ref, hot_ref):
    atoms = hot_ref.shape[1]
    for cell in range(3):
        ids = ids_ref[cell : cell + 1, :]
        hot_ref[cell] = hot_columns(ids - cell_of(ids, atoms) * atoms, atoms)


def unfold_block(block, atoms):
    parts = atoms // 128
    rows = [block[r : r + 1] for r in range(4 * parts)]
    return [jnp.concatenate(rows[q * parts : (q + 1) * parts], axis=1) for q in range(4)]


def first_kernel(slots, place_ref, embed_ref, kind_left, mix_high, mix_low, y_beyond_ref, own_ref,
                 y_pair_ref, beyond_ref, column_ref, pair_ref, low_ref, ids_ref, basis_ref, slope_ref,
                 unit_ref, sums_ref, gate_ref):
    atoms = low_ref.shape[2]
    frame = [pair_ref, column_ref, beyond_ref]
    per_cell = atoms // 128
    places = lax.broadcasted_iota(jnp.int32, (4 * per_cell, 128), 0)
    upper = places % per_cell
    kind_of_row = places // per_cell
    to_x = jnp.where(kind_of_row == 0, cell_width, 0.0)
    to_x = jnp.where((place_ref[0] & 1) == 0, to_x, -to_x)
    to_y = jnp.where(kind_of_row == 1, cell_width, 0.0)
    to_y = jnp.where((place_ref[1] & 1) == 0, to_y, -to_y)
    for cell, block_ref in enumerate((y_pair_ref, own_ref, y_beyond_ref)):
        ids, count = block_ids(block_ref[...], atoms, slots * atoms)
        ids_ref[cell : cell + 1, :] = ids
        own = unfold_block(column_ref[cell + 1], atoms)
        step_y = to_y if cell == 1 else -to_y
        rows = []
        for a in range(3):
            for b in range(3):
                block = frame[a][SLOT_CELLS[cell][b]]
                rows.append(block + ((1 - a) * to_x + (1 - b) * step_y))
        first_cell(
            slots, atoms, ids, count, rows, places, upper, own, embed_ref, kind_left, mix_high,
            mix_low, low_ref.at[cell], basis_ref.at[cell], slope_ref.at[cell], unit_ref.at[cell],
            sums_ref.at[cell], gate_ref.at[cell],
        )


def first_cell(slots, atoms, ids, count, rows, places, upper, own, embed_ref, kind_left, mix_high,
               mix_low, low_ref, basis_ref, slope_ref, unit_ref, sums_ref, gate_ref):
    per_cell = atoms // 128
    pieces = []
    for start in range(0, ids.shape[1], 128):
        part = jnp.broadcast_to(ids[:, start : start + 128], places.shape)
        lane, half = part & 127, (part >> 7) - upper
        found = jnp.zeros(places.shape, F32)
        for cell, block in enumerate(rows):
            value = jnp.take_along_axis(block, lane, axis=1)
            found = jnp.where(half == per_cell * cell, value, found)
        total = found
        for s in range(1, per_cell):
            total = total + pltpu.roll(found, 4 * per_cell - s, 0)
        pieces.append(total)
    found = jnp.concatenate(pieces, axis=1)
    found = [found[q * per_cell : q * per_cell + 1] for q in range(4)]
    rel = [found[q] - jnp.concatenate([own[q]] * slots, axis=1) for q in range(3)]
    distance = jnp.sqrt(rel[0] * rel[0] + rel[1] * rel[1] + rel[2] * rel[2] + soften)
    inverse = 1.0 / distance
    order = (lax.broadcasted_iota(jnp.int32, (8, 1), 0) + 1).astype(F32)
    sine, cosine = sin_cos((order * (0.5 / cut_radius)) * distance)
    wave = sine / ((order * (math.pi / cut_radius)) * distance)
    live = jnp.concatenate([jnp.where(count > n, 1.0, 0.0) for n in range(slots)], axis=1)
    basis = wave * live
    basis_ref[...] = basis
    slope_ref[...] = (cosine - wave) * (inverse * live)
    kinds = found[3]
    unit = jnp.concatenate(
        [r * inverse for r in rel] + [inverse, kinds] + [jnp.zeros_like(kinds)] * 3, axis=0
    )
    unit_ref[...] = unit
    stack = embed_ref[...]
    parts = edge_parts(basis, unit)
    species = kind_left.shape[2] // 32
    by_kind = [[None] * species for _ in range(4)]
    for n in range(slots):
        lanes = slice(n * atoms, (n + 1) * atoms)
        kind = jnp.broadcast_to(kinds[:, lanes], (8, atoms))
        for k in range(species):
            match = kind == float(k)
            for part in range(4):
                term = jnp.where(match, parts[part][:, lanes], 0.0)
                old = by_kind[part][k]
                by_kind[part][k] = term if old is None else old + term
    stacks = [stacked_right(jnp.concatenate(rows, axis=0)) for rows in by_kind]
    vectors = dot(kind_left[1], jnp.concatenate(stacks[1:], axis=1))
    sums = [dot(kind_left[0], stacks[0])]
    sums += [vectors[:, i * atoms : (i + 1) * atoms] for i in range(3)]
    step, gate = mixed(sums, mix_high, mix_low, 0)
    low_ref[...] = (embedded(stack, own[3]) + step).astype(BF16)
    for part in range(3):
        sums_ref[part] = sums[part + 1]
    gate_ref[...] = gate


def hot_columns(ids, rows):
    place = lax.broadcasted_iota(jnp.int32, (rows, ids.shape[1]), 0)
    return jnp.where(ids == place, 1.0, 0.0).astype(BF16)


def second_near_kernel(slots, ids_ref, basis_ref, unit_ref, left_ref, column_ref, weight_ref,
                       near_ref):
    atoms = column_ref.shape[2]
    parts = edge_parts(basis_ref[1], unit_ref[1])
    source = jnp.concatenate([column_ref[b] for b in range(3)], axis=1)
    for n in range(slots):
        lanes = slice(n * atoms, (n + 1) * atoms)
        for part in range(4):
            weight_ref[part, :, lanes] = weights_of(left_ref, part, parts[part][:, lanes])
        ids = ids_ref[1:2, lanes] - 3 * atoms
        near_ref[:, lanes] = dot(source, hot_columns(ids, 3 * atoms))


def second_side_kernel(slots, ids_ref, near_ref, pair_ref, out_ref):
    atoms = pair_ref.shape[2]
    source = jnp.concatenate([pair_ref[b] for b in range(3)], axis=1)
    for n in range(slots):
        lanes = slice(n * atoms, (n + 1) * atoms)
        hot = hot_columns(ids_ref[1:2, lanes], 3 * atoms)
        out_ref[:, lanes] = near_ref[:, lanes] + dot(source, hot)


def second_kernel(slots, hot_ref, weight_ref, near_ref, mix_high, mix_low, charge_ref, cell_ref,
                  column_ref, beyond_ref, feature_ref, sums_ref, gate_ref, packed_ref,
                  full_charge_ref, hidden_ref):
    atoms = column_ref.shape[2]
    source = jnp.concatenate([beyond_ref[b] for b in range(3)], axis=1)
    sums = [None] * 4
    for n in range(slots):
        lanes = slice(n * atoms, (n + 1) * atoms)
        feature = near_ref[:, lanes] + dot(source, hot_ref[:, lanes])
        feature_ref[:, lanes] = feature.astype(BF16)
        for part in range(4):
            term = weight_ref[part, :, lanes] * feature
            sums[part] = term if sums[part] is None else sums[part] + term
    step, gate = mixed(sums, mix_high, mix_low, 1)
    hidden = column_ref[1].astype(F32) + step
    hidden_ref[...] = hidden
    for part in range(3):
        sums_ref[part] = sums[part + 1]
    gate_ref[...] = gate
    charge = dot_split((charge_ref[0], charge_ref[1]), hidden)
    full_charge_ref[...] = charge
    place = jnp.concatenate(unfold_block(cell_ref[2], atoms)[:3], axis=0)
    high = place.astype(BF16).astype(F32)
    rest = place - high
    middle = rest.astype(BF16).astype(F32)
    zero = jnp.zeros((packed_ref.shape[0] - charge.shape[0] - 9, atoms), F32)
    packed_ref[...] = jnp.concatenate([charge, high, middle, rest - middle, zero], axis=0).astype(
        BF16
    )


def readout_kernel(hidden_high, hidden_low, turn_high, turn_low, out_ref, hidden_ref, energy_ref,
                   slope_ref):
    hidden = hidden_ref[...]
    value, slope = silu_pair(dot_split((hidden_high[...], hidden_low[...]), hidden))
    out = out_ref[...].T
    energy_ref[...] = jnp.sum(value * out, axis=0, keepdims=True)
    slope_ref[...] = dot_split((turn_high[...], turn_low[...]), slope * out)


def message_grads(cotangent, gate_ref, sums_ref, high_ref, low_ref, layer):
    pre = cotangent * gate_ref[...]
    both = dot_split((high_ref[layer], low_ref[layer]), pre)
    half = both.shape[0] // 2
    return [both[:half]] + [both[half:] * sums_ref[i] for i in range(3)]


def radial_grad(left, value):
    high, low = split(value)
    both = dot(left, jnp.concatenate([high, low], axis=0))
    half = both.shape[0] // 2
    return both[:half] + both[half:]


def second_back_kernel(slots, scale, count, hot_ref, weight_ref, turn_high, turn_low, charge_ref,
                       sums_ref, gate_ref, full_charge_ref, energy_ref, slope_ref, *refs):
    folds, refs = refs[:count], refs[count:]
    site_ref, long_ref, cotangent_ref, grad_ref, term_ref, beyond_ref = refs
    atoms = gate_ref.shape[1]
    total = folds[0][...].astype(F32)
    for part in folds[1:]:
        total = total + part[...].astype(F32)
    wide = full_charge_ref.shape[0]
    potential = total[:wide] * (2.0 * scale)
    slopes = total[wide : wide + 3] + total[wide + 3 : wide + 6] + total[wide + 6 : wide + 9]
    long_ref[...] = jnp.concatenate(
        [slopes * (2.0 * scale), jnp.zeros((5, atoms), F32)], axis=0
    )
    site_ref[0] = energy_ref[...] + 0.5 * jnp.sum(
        full_charge_ref[...] * potential, axis=0, keepdims=True
    )
    high, low = split(potential)
    turned = ((0,), (0,))
    cotangent = slope_ref[...] + (
        dot(charge_ref[0], high, turned)
        + (dot(charge_ref[0], low, turned) + dot(charge_ref[1], high, turned))
    )
    cotangent_ref[...] = cotangent
    grads = message_grads(cotangent, gate_ref, sums_ref, turn_high, turn_low, 1)
    for part in range(4):
        grad_ref[part] = grads[part]
    for n in range(slots):
        lanes = slice(n * atoms, (n + 1) * atoms)
        term = weight_ref[0, :, lanes] * grads[0]
        for part in range(1, 4):
            term = term + weight_ref[part, :, lanes] * grads[part]
        term_ref[:, lanes] = term.astype(BF16)
    for b in range(3):
        start = (3 + b) * atoms
        beyond_ref[b] = dot(term_ref[...], hot_ref[:, start : start + atoms]).astype(BF16)


def second_pair_kernel(hot_ref, term_ref, pair_ref):
    atoms = pair_ref.shape[2]
    for b in range(3):
        pair_ref[b] = dot(term_ref[...], hot_ref[:, b * atoms : (b + 1) * atoms]).astype(BF16)


def second_middle_kernel(hot_ref, term_ref, cotangent_ref, middle_ref):
    atoms = cotangent_ref.shape[1]
    for b in range(3):
        grad = dot(term_ref[...], hot_ref[:, b * atoms : (b + 1) * atoms])
        middle_ref[b] = grad + cotangent_ref[...] if b == 1 else grad


def second_edge_kernel(slots, back_ref, feature_ref, grad_ref, edge_ref):
    atoms = grad_ref.shape[2]
    for n in range(slots):
        lanes = slice(n * atoms, (n + 1) * atoms)
        feature = feature_ref[:, lanes].astype(F32)
        for part in range(4):
            edge_ref[8 * part : 8 * part + 8, lanes] = radial_grad(
                back_ref[1 if part else 0], grad_ref[part] * feature
            )


def first_back_kernel(slots, ids_ref, hot_ref, basis_ref, slope_ref, unit_ref, kind_high, kind_low, turn_high,
                      turn_low, sums_ref, gate_ref, edge_ref, from_beyond, long_ref, middle_ref,
                      from_pair, *outs):
    sums = {(1, 2): long_ref[...]}
    for cell in range(3):
        cotangent = middle_ref[cell] + (
            from_pair[cell].astype(F32) + from_beyond[cell].astype(F32)
        )
        own, found = first_back_cell(
            slots, ids_ref[cell : cell + 1, :], hot_ref.at[cell], basis_ref.at[cell], slope_ref.at[cell],
            unit_ref.at[cell], kind_high, kind_low, turn_high, turn_low, sums_ref.at[cell],
            gate_ref.at[cell], edge_ref if cell == 1 else None, cotangent,
        )
        terms = [((1, cell + 1), own)]
        terms += [((n // 3, SLOT_CELLS[cell][n % 3]), found[n]) for n in range(9)]
        for key, term in terms:
            sums[key] = sums[key] + term if key in sums else term
    for x in range(3):
        rows = [sums[(x, y)][:3] for y in range(5)]
        outs[x][...] = jnp.concatenate(rows + [jnp.zeros((1, rows[0].shape[1]), F32)], axis=0)


def first_back_cell(slots, ids, hot_ref, basis_ref, slope_ref, unit_ref, kind_high, kind_low, turn_high,
                    turn_low, sums_ref, gate_ref, edge_ref, cotangent):
    atoms = gate_ref.shape[1]
    pre = cotangent * gate_ref[...]
    both = dot_split((turn_high[0], turn_low[0]), pre)
    wide = both.shape[0] // 2
    grads = [both[:wide]] + [both[wide:] * sums_ref[i] for i in range(3)]
    unit = unit_ref[...]
    kinds = unit[4:5]
    by_kind = [dot_split((kind_high[0], kind_low[0]), grads[0])]
    by_kind += [dot_split((kind_high[1], kind_low[1]), grads[i]) for i in range(1, 4)]
    species = by_kind[0].shape[0] // 8
    edges = [[] for _ in range(4)]
    for n in range(slots):
        kind = jnp.broadcast_to(kinds[:, n * atoms : (n + 1) * atoms], (8, atoms))
        matches = [kind == float(k) for k in range(1, species)]
        for part in range(4):
            rows = by_kind[part]
            found = rows[:8]
            for k, match in enumerate(matches):
                found = jnp.where(match, rows[8 * k + 8 : 8 * k + 16], found)
            edges[part].append(found)
    edges = [jnp.concatenate(rows, axis=1) for rows in edges]
    if edge_ref is not None:
        edges = [edge_ref[8 * part : 8 * part + 8] + edges[part] for part in range(4)]
    basis = basis_ref[...]
    units = [unit[i : i + 1] for i in range(3)]
    inverse = unit[3:4]
    by_basis = edges[0]
    for i in range(3):
        by_basis = by_basis + edges[i + 1] * units[i]
    by_unit = [jnp.sum(edges[i + 1] * basis, axis=0, keepdims=True) * inverse for i in range(3)]
    by_distance = jnp.sum(by_basis * slope_ref[...], axis=0, keepdims=True)
    for i in range(3):
        by_distance = by_distance - by_unit[i] * units[i]
    moves = [by_unit[i] + by_distance * units[i] for i in range(3)]
    zero = jnp.zeros_like(moves[0])
    move = jnp.concatenate(moves + [zero] * 5, axis=0)
    own = -move[:, :atoms]
    for n in range(1, slots):
        own = own - move[:, n * atoms : (n + 1) * atoms]
    source = cell_of(ids, atoms)
    high = move.astype(BF16).astype(F32)
    both = jnp.concatenate([high, move - high], axis=0)
    rows = jnp.concatenate(
        [jnp.where(source == cell, both, 0.0).astype(BF16) for cell in range(9)], axis=0
    )
    spread = dot(rows, hot_ref[...], ((1,), (1,)))
    grads = [
        spread[16 * cell : 16 * cell + 8] + spread[16 * cell + 8 : 16 * cell + 16]
        for cell in range(9)
    ]
    return own, grads


def pair_counts(parts):
    total = WAVE_REACH + WAVE_REACH * (2 * WAVE_REACH + 1)
    share = -(-total // parts)
    return total, share, -(-share // 16) * 16


def pair_vectors(slot, share, part):
    side = 2 * WAVE_REACH + 1
    total = WAVE_REACH + WAVE_REACH * side
    index = slot + part.astype(F32) * share
    later = index - WAVE_REACH
    row = jnp.floor((later + 0.5) * (1.0 / side))
    first = index < WAVE_REACH
    kx = jnp.where(first, 0.0, row + 1.0)
    ky = jnp.where(first, index + 1.0, later - row * side - WAVE_REACH)
    valid = jnp.where((slot < share) & (index < total), 1.0, 0.0)
    return kx, ky, valid


def count_up(rows):
    return lax.broadcasted_iota(jnp.int32, (rows, 1), 0).astype(F32)


def green_weights(share, padded, grid, place_ref, vec_ref, weight_ref):
    grid_x, grid_y = grid
    turn = 2.0 * math.pi
    side = 2 * WAVE_REACH + 1
    top = side * side * side - 1
    vec = vec_ref[...].astype(F32) + WAVE_REACH
    code = (vec[0:1] * side + vec[1:2]) * side + vec[2:3]
    code = jnp.maximum(code, top - code)
    span = 8 * share
    row = count_up(span)
    slot = jnp.floor(row * 0.125)
    height = row - 8.0 * slot + 1.0
    flat = count_up(padded)
    slot = jnp.concatenate([slot, slot, flat], axis=0)
    kz = jnp.concatenate([height, -height, jnp.zeros_like(flat)], axis=0)
    kx, ky, valid = pair_vectors(slot, share, place_ref[0, 0:1, 0:1])
    own = ((kx + WAVE_REACH) * side + ky + WAVE_REACH) * side + kz + WAVE_REACH
    seen = jnp.zeros((own.shape[0], 128), F32)
    for start in range(0, code.shape[1], 128):
        seen = seen + jnp.where(own == code[:, start : start + 128], 1.0, 0.0)
    count = jnp.sum(seen, axis=1, keepdims=True) * valid
    sq = (
        (kx * (turn / (grid_x * cell_width))) ** 2
        + (ky * (turn / (grid_y * cell_width))) ** 2
        + (kz * (turn / box_height)) ** 2
    )
    green = jnp.exp(-smear_width * sq) / (sq + screen * screen) * count
    weight_ref[...] = jnp.broadcast_to(green, weight_ref.shape)


def basis_rows(share, ca, sa, cb, sb):
    cc, ss, sc, cs = [], [], [], []
    for p in range(share):
        c, s = ca[p : p + 1], sa[p : p + 1]
        cc.append(c * cb)
        ss.append(s * sb)
        sc.append(s * cb)
        cs.append(c * sb)
    return cc, ss, sc, cs


def unpack_rows(block):
    half = block.shape[1] // 2
    return jnp.concatenate([block[:, :half], block[:, half:]], axis=0)


def pack_rows(block):
    half = block.shape[0] // 2
    return jnp.concatenate([block[:half], block[half:]], axis=1)


def structure_kernel(share, padded, grid, wide, flip, place_ref, blocks, *refs):
    grid_x, grid_y = grid
    if flip:
        near_ref, (ca_ref, sa_ref, cb_ref, sb_ref, high_ref, low_ref, own_ref, out_ref) = (
            refs[0],
            refs[1:],
        )
        total = near_ref[...]
    else:
        ca_ref, sa_ref, cb_ref, sb_ref, high_ref, low_ref, total_ref = refs
        total = None
    col = place_ref[1, 0:1, 0:1].astype(F32) * (1.0 / grid_y)
    first = place_ref[0, 0:1, 0:1] ^ flip
    kx, ky, _ = pair_vectors(count_up(padded), share, place_ref[0, 0:1, 0:1])
    kz = count_up(8) + 1.0
    for d in range(grid_x // 2):
        block = blocks[d]
        charge = block[:wide]
        atoms = charge.shape[1]
        pieces = block[wide:].astype(F32)
        place = pieces[0:3] + (pieces[3:6] + pieces[6:9])
        row = (first ^ (2 * d)).astype(F32) * (1.0 / grid_x)
        x = place[0:1] * (1.0 / (grid_x * cell_width)) + row
        y = place[1:2] * (1.0 / (grid_y * cell_width)) + col
        sa, ca = sin_cos(kx * x + ky * y)
        sb, cb = sin_cos(kz * (place[2:3] * (1.0 / box_height)))
        lanes = pl.ds(d * atoms, atoms)
        ca_ref[:, lanes] = ca
        sa_ref[:, lanes] = sa
        cb_ref[:, lanes] = cb
        sb_ref[:, lanes] = sb
        cc, ss, sc, cs = basis_rows(share, ca, sa, cb, sb)
        high, low = split(jnp.concatenate(cc + ss + sc + cs + [ca, sa], axis=0))
        high_ref[:, lanes] = high
        low_ref[:, lanes] = low
        term = dot(high, charge, ((1,), (1,))) + dot(low, charge, ((1,), (1,)))
        total = term if total is None else total + term
    if flip:
        packed = pack_rows(total)
        own_ref[...] = packed
        out_ref[...] = packed.astype(BF16)
    else:
        total_ref[...] = total


def weighted_rows(share, padded, wide, weight_ref, parts):
    packed = parts[0][...].astype(F32)
    for part in parts[1:]:
        packed = packed + part[...].astype(F32)
    struct = unpack_rows(packed)
    span = 8 * share
    cc, ss, sc, cs = (struct[i * span : (i + 1) * span] for i in range(4))
    weight = weight_ref[:, :wide]
    plus, minus, flat = weight[:span], weight[span : 2 * span], weight[2 * span :]
    re_plus, im_plus = plus * (cc - ss), plus * (sc + cs)
    re_minus, im_minus = minus * (cc + ss), minus * (sc - cs)
    rows = jnp.concatenate(
        [
            re_plus + re_minus,
            re_minus - re_plus,
            im_plus + im_minus,
            im_plus - im_minus,
            flat * struct[4 * span : 4 * span + padded],
            flat * struct[4 * span + padded :],
        ],
        axis=0,
    )
    return rows


def fold_kernel(share, padded, grid, wide, flip, place_ref, *refs):
    grid_x, grid_y = grid
    turn = 2.0 * math.pi
    if flip:
        weight_ref, parts, refs = refs[0], refs[1 : 1 + grid_y], refs[1 + grid_y :]
        rows = weighted_rows(share, padded, wide, weight_ref, parts)
        refs, rows_ref = refs[:-1], refs[-1]
        rows_ref[...] = rows
    else:
        rows, refs = refs[0][...], refs[1:]
    ca_ref, sa_ref, cb_ref, sb_ref, high_ref, low_ref, blocks, out_ref = refs
    row_high, row_low = split(rows)
    row_pair = jnp.concatenate([row_high, row_low], axis=1)
    turned = rows.T
    t_high, t_low = split(turned)
    t_both = jnp.concatenate([t_high, t_low], axis=0)
    span = 8 * share
    kx, ky, _ = pair_vectors(count_up(padded), share, place_ref[0, 0:1, 0:1])
    kx = kx * (turn / (grid_x * cell_width))
    ky = ky * (turn / (grid_y * cell_width))
    kz = (count_up(8) + 1.0) * (turn / box_height)
    for d in range(grid_x // 2):
        charge = blocks[d][:wide]
        atoms = charge.shape[1]
        lanes = pl.ds(d * atoms, atoms)
        ca, sa, cb, sb = ca_ref[:, lanes], sa_ref[:, lanes], cb_ref[:, lanes], sb_ref[:, lanes]
        bcc, bss, bsc, bcs = basis_rows(share, ca, sa, cb, sb)
        high, low = high_ref[:, lanes], low_ref[:, lanes]
        both = dot(t_both, high)
        pot = both[:wide] + both[wide:] + dot(t_high, low)
        proj = dot(row_pair, jnp.concatenate([charge, charge], axis=0))
        by_x = jnp.zeros((8, atoms), jnp.float32)
        by_y = jnp.zeros((8, atoms), jnp.float32)
        by_z = jnp.zeros((8, atoms), jnp.float32)
        for p in range(share):
            pcc, pss, psc, pcs = (
                proj[i * span + 8 * p : i * span + 8 * p + 8] for i in range(4)
            )
            slope = bcs[p] * pss - bsc[p] * pcc + bcc[p] * psc - bss[p] * pcs
            by_x = by_x + kx[p : p + 1] * slope
            by_y = by_y + ky[p : p + 1] * slope
            by_z = by_z + (bsc[p] * pss - bcs[p] * pcc - bss[p] * psc + bcc[p] * pcs)
        flat_slope = ca * proj[4 * span + padded :] - sa * proj[4 * span : 4 * span + padded]
        grad_x = jnp.sum(by_x, axis=0, keepdims=True) + jnp.sum(kx * flat_slope, axis=0, keepdims=True)
        grad_y = jnp.sum(by_y, axis=0, keepdims=True) + jnp.sum(ky * flat_slope, axis=0, keepdims=True)
        grad_z = jnp.sum(kz * by_z, axis=0, keepdims=True)
        slopes = jnp.concatenate([grad_x, grad_y, grad_z], axis=0)
        out_ref[d] = pieced(pot, slopes, out_ref.shape[1]).astype(out_ref.dtype)


def pieced(pot, slopes, rows):
    high = slopes.astype(BF16).astype(F32)
    rest = slopes - high
    middle = rest.astype(BF16).astype(F32)
    zero = jnp.zeros((rows - pot.shape[0] - 9, pot.shape[1]), F32)
    return jnp.concatenate([pot, high, middle, rest - middle, zero], axis=0)


def unpieced(block, wide):
    slopes = block[wide : wide + 3] + (block[wide + 3 : wide + 6] + block[wide + 6 : wide + 9])
    return block[:wide], slopes


def join_kernel(wide, near_ref, far_ref, own_ref, *outs):
    for d in range(near_ref.shape[0]):
        pot, slopes = unpieced(near_ref[d], wide)
        pot_far, slopes_far = unpieced(far_ref[d].astype(F32), wide)
        block = pieced(pot + pot_far, slopes + slopes_far, near_ref.shape[1])
        if d:
            outs[d - 1][...] = block.astype(BF16)
        else:
            own_ref[...] = block


def per_device(
    positions,
    species,
    neighbours,
    counts,
    species_embed,
    radial,
    mixing,
    read_hidden,
    read_out,
    charge_map,
    wavevectors,
):
    atoms = positions.shape[3]
    slots = neighbours.shape[3]
    features, lat_width = charge_map.shape
    wave_count = wavevectors.shape[1]
    grid = lax.axis_size("gx"), lax.axis_size("gy")
    grid_x, grid_y = grid
    edges = slots * atoms
    scale = 1.0 / math.sqrt(wave_count * lat_width * atoms * grid_x * grid_y)
    place = jnp.stack([lax.axis_index("gx"), lax.axis_index("gy")]).astype(jnp.int32)
    place = jnp.broadcast_to(place[:, None, None], (2, 8, 128))
    _, share, padded = pair_counts(grid_x)
    ids = neighbours.transpose(0, 3, 1, 2).reshape(1, edges)
    cell_rows = 4 * atoms // 128
    block_total = -(-(cell_rows + (edges + atoms) // 128) // 8) * 8
    dma = pltpu.SemaphoreType.DMA
    shown = positions.transpose(0, 2, 1, 3)
    (own_place,) = run(
        pack_kernel,
        [shape(cell_rows, 128)],
        [place, shown, species],
        flops=10_000_000_000,
        name="pack",
    )
    (own,) = run(
        pack_more_kernel,
        [shape(block_total, 128)],
        [place, ids, counts, own_place],
        name="pack_more",
    )
    y_beyond, y_pair = beyond(own, "gy"), paired(own, "gy", 1)
    over_pair = far(own_place, "gy", True)
    over_beyond = over_pair if grid_y == 4 else far(own_place, "gy", False)
    cells = jnp.stack(
        [over_pair, y_pair[:cell_rows], own_place, y_beyond[:cell_rows], over_beyond]
    )
    x_beyond, x_pair = beyond(cells, "gx"), paired(cells, "gx", 1)
    cells = [x_pair, cells, x_beyond]

    norm = 1.0 / math.sqrt(slots)
    kind_rows = 8 * species_embed.shape[0]
    low_pair = lambda *dims: [shape(*dims, dtype=BF16)] * 2
    embed, kind_left, left, back, kind_high, kind_low, mix_high, mix_low, turn_high, turn_low = run(
        functools.partial(prep_first_kernel, norm),
        [
            shape(features, 32, dtype=BF16),
            shape(2, features, 4 * kind_rows, dtype=BF16),
            shape(2, features, 32, dtype=BF16),
            shape(2, 16, 2 * features, dtype=BF16),
        ]
        + low_pair(2, kind_rows, features)
        + low_pair(2, features, 2 * features)
        + low_pair(2, 2 * features, features),
        [species_embed, radial, mixing],
        scratch=[
            pltpu.VMEM(species_embed.shape, F32),
            pltpu.VMEM(radial.shape, F32),
            pltpu.VMEM(mixing.shape, F32),
            dma((3,)),
        ],
        hbm=3,
        name="prep_first",
    )
    read_out, hidden_high, hidden_low, hidden_turn_high, hidden_turn_low, charge_pair = run(
        prep_second_kernel,
        [shape(1, features)]
        + low_pair(features, features)
        + low_pair(features, features)
        + [shape(2, lat_width, features, dtype=BF16)],
        [read_out[None, :], read_hidden, charge_map.T],
        scratch=[
            pltpu.VMEM(read_hidden.shape, F32),
            pltpu.VMEM((lat_width, features), F32),
            dma((3,)),
        ],
        hbm=3,
        name="prep_second",
    )
    cells[2], hidden_high = lax.optimization_barrier((cells[2], hidden_high))
    low, ids, basis, slope, unit, sums_one, gate_one = run(
        functools.partial(first_kernel, slots),
        [
            shape(3, features, atoms, dtype=BF16),
            shape(3, edges, dtype=jnp.int32),
            shape(3, 8, edges),
            shape(3, 8, edges),
            shape(3, 8, edges),
            shape(3, 3, features, atoms),
            shape(3, features, atoms),
        ],
        [place, embed, kind_left, mix_high, mix_low, y_beyond, own, y_pair] + cells[::-1],
        name="first",
    )
    hidden = [paired(low, "gx", 1), low, beyond(low, "gx")]
    edge_weights, near = run(
        functools.partial(second_near_kernel, slots),
        [shape(4, features, edges), shape(features, edges)],
        [ids, basis, unit, left, low],
        flops=2_000_000_000,
        name="second_near",
    )
    (hot_beyond,) = run(
        hot_beyond_kernel,
        [shape(3 * atoms, edges, dtype=BF16)],
        [ids, near],
        flops=1_000_000,
        name="hot_beyond",
    )
    (near,) = run(
        functools.partial(second_side_kernel, slots),
        [shape(features, edges)],
        [ids, near, hidden[0]],
        flops=1_000_000_000,
        name="second_side",
    )
    block_rows = -(-(lat_width + 9) // 16) * 16
    feature, sums_two, gate_two, packed, charge, hidden_two = run(
        functools.partial(second_kernel, slots),
        [
            shape(features, edges, dtype=BF16),
            shape(3, features, atoms),
            shape(features, atoms),
            shape(block_rows, atoms, dtype=BF16),
            shape(lat_width, atoms),
            shape(features, atoms),
        ],
        [hot_beyond, edge_weights, near, mix_high, mix_low, charge_pair, cells[1], hidden[1],
         hidden[2]],
        name="second",
    )
    energy, energy_slope = run(
        readout_kernel,
        [shape(1, atoms), shape(features, atoms)],
        [hidden_high, hidden_low, hidden_turn_high, hidden_turn_low, read_out, hidden_two],
        name="readout",
    )
    half = grid_x // 2
    near_charges = jnp.stack([packed] + [paired(packed, "gx", 2 * d) for d in range(1, half)])
    (weight,) = run(
        functools.partial(green_weights, share, padded, grid),
        [shape(16 * share + padded, 128)],
        [place, wavevectors],
        name="green",
    )
    near_charges, weight = lax.optimization_barrier((near_charges, weight))
    far_charges = paired(near_charges, "gx", 1)
    span = half * atoms
    rows = 32 * share + 2 * padded
    phase_shapes = [
        shape(padded, span),
        shape(padded, span),
        shape(8, span),
        shape(8, span),
        shape(rows, span, dtype=BF16),
        shape(rows, span, dtype=BF16),
    ]
    *near_phases, near_total = run(
        functools.partial(structure_kernel, share, padded, grid, lat_width, 0),
        phase_shapes + [shape(rows, lat_width)],
        [place, near_charges],
        flops=1_000_000_000,
        name="structure_near",
    )
    *far_phases, own_part, part = run(
        functools.partial(structure_kernel, share, padded, grid, lat_width, 1),
        phase_shapes
        + [
            shape(rows // 2, 2 * lat_width),
            shape(rows // 2, 2 * lat_width, dtype=BF16),
        ],
        [place, far_charges, near_total],
        name="structure_far",
    )
    parts = [own_part] + [paired(part, "gy", d) for d in range(1, grid_y)]
    (hot_back,) = run(
        functools.partial(hot_back_kernel, (0, 2)),
        [shape(edges, 6 * atoms, dtype=BF16)],
        [ids],
        flops=2_000_000_000,
        name="hot_back",
    )
    parts, hot_back = lax.optimization_barrier((parts, hot_back))
    far_folds, wave_rows = run(
        functools.partial(fold_kernel, share, padded, grid, lat_width, 1),
        [shape(half, block_rows, atoms, dtype=BF16), shape(rows, lat_width)],
        [place, weight] + parts + far_phases + [far_charges],
        name="fold_far",
    )
    far_folds = paired(far_folds, "gx", 1)
    (near_folds,) = run(
        functools.partial(fold_kernel, share, padded, grid, lat_width, 0),
        [shape(half, block_rows, atoms)],
        [place, wave_rows] + near_phases + [near_charges],
        flops=1_000_000_000,
        name="fold_near",
    )
    folds = run(
        functools.partial(join_kernel, lat_width),
        [shape(block_rows, atoms)] + [shape(block_rows, atoms, dtype=BF16)] * (half - 1),
        [near_folds, far_folds],
        name="fold_join",
    )
    folds = [folds[0]] + [paired(folds[d], "gx", 2 * d) for d in range(1, half)]

    (atom_hot,) = run(
        atom_hot_kernel,
        [shape(3, atoms, edges, dtype=BF16)],
        [ids],
        flops=1_000_000_000,
        name="atom_hot",
    )
    folds[1], atom_hot = lax.optimization_barrier((folds[1], atom_hot))
    site, long, cotangent, grads, term, to_beyond = run(
        functools.partial(second_back_kernel, slots, scale, half),
        [
            shape(1, 1, atoms),
            shape(8, atoms),
            shape(features, atoms),
            shape(4, features, atoms),
            shape(features, edges, dtype=BF16),
            shape(3, features, atoms, dtype=BF16),
        ],
        [hot_back, edge_weights, turn_high, turn_low, charge_pair, sums_two, gate_two, charge,
         energy, energy_slope] + folds,
        name="second_back",
    )
    (to_pair,) = run(
        second_pair_kernel,
        [shape(3, features, atoms, dtype=BF16)],
        [hot_back, term],
        flops=1_000_000,
        name="second_pair",
    )
    from_pair, from_beyond = paired(to_pair, "gx", 1), beyond(to_beyond, "gx")
    (hot_middle,) = run(
        functools.partial(hot_back_kernel, (1,)),
        [shape(edges, 3 * atoms, dtype=BF16)],
        [ids],
        flops=1_000_000_000,
        name="hot_middle",
    )
    (middle,) = run(
        second_middle_kernel,
        [shape(3, features, atoms)],
        [hot_middle, term, cotangent],
        flops=1_000_000_000,
        name="second_middle",
    )
    (edge,) = run(
        functools.partial(second_edge_kernel, slots),
        [shape(32, edges)],
        [back, feature, grads],
        flops=1_000_000_000,
        name="second_edge",
    )
    to_pair, middle, to_beyond = run(
        functools.partial(first_back_kernel, slots),
        [shape(16, atoms)] * 3,
        [ids, atom_hot, basis, slope, unit, kind_high, kind_low, turn_high, turn_low, sums_one, gate_one, edge,
         from_beyond, long, middle, from_pair],
        name="first_back",
    )
    total = middle + paired(to_pair, "gx", 1) + beyond(to_beyond, "gx")
    total = [total[3 * y : 3 * y + 3] for y in range(5)]
    if grid_y == 4:
        distant = far(total[0] + total[4], "gy", True)
    else:
        distant = far(total[0], "gy", False) + far(total[4], "gy", True)
    total = total[2] + paired(total[1], "gy", 1) + beyond(total[3], "gy") + distant
    forces = -total[None, :, None, :]
    return (forces.transpose(0, 2, 1, 3), site)


def solution(mesh):
    in_specs = (
        P("gx", "gy", None, None),
        P("gx", "gy", None),
        P("gx", "gy", None, None),
        P("gx", "gy", None),
        P(),
        P(),
        P(),
        P(),
        P(),
        P(),
        P(),
    )
    out_specs = (P("gx", "gy", None, None), P("gx", "gy", None))
    return jax.shard_map(
        per_device, mesh=mesh, in_specs=in_specs, out_specs=out_specs, check_vma=False
    )
```
